32 devices in a mesh: rows: 2 (over core), canvas: 16 (over z, y, x).
Axes of the slice: x: 2, y: 2, z: 4, core: 2. Of those that a mesh axis runs over, the one named last changes fastest.
Arguments:
- patch_embeddings: float32 [16, 64, 32, 384], P('canvas', 'rows'), may hold values from -12 to 12
- loss_sensitivity: float32 [16, 64, 32, 384], P('canvas', 'rows'), may hold values from -6 to 6
- patch_tallness: int32 [16, 4], P('canvas'), may hold values from 2 to 24, as said below
- triple_linear_map: float32 [384, 1152], replicated, may hold values from -0.3125 to 0.3125
- mixing_linear_map: float32 [384, 384], replicated, may hold values from -0.625 to 0.625
- expanding_linear: float32 [384, 1536], replicated, may hold values from -0.3125 to 0.3125
- contracting_linear: float32 [1536, 384], replicated, may hold values from -0.15625 to 0.15625
- triple_momentum: float32 [384, 1152], replicated, may hold values from -320 to 320
- mixing_momentum: float32 [384, 384], replicated, may hold values from -448 to 448
- expanding_momentum: float32 [384, 1536], replicated, may hold values from -320 to 320
- contracting_momentum: float32 [1536, 384], replicated, may hold values from -640 to 640
- auxiliary_entry_table: float32 [40, 384], replicated, may hold values from -3 to 3
- auxiliary_first_moment: float32 [40, 384], replicated, may hold values from -32 to 32
- auxiliary_second_moment: float32 [40, 384], replicated, may hold values from 157.2864 to 622.592
- logit_scaling: float32 [8], replicated, may hold values from 2 to 6
- temper_first_moment: float32 [8], replicated, may hold values from -128 to 128
- temper_second_moment: float32 [8], replicated, may hold values from 1736.704 to 6881.28
Outputs:
- block_result: float32 [16, 64, 32, 384], P('canvas', 'rows')
- gradient_input_tokens: float32 [16, 64, 32, 384], P('canvas', 'rows')
- gradient_query_key_value: float32 [384, 1152], replicated
- gradient_output_weight: float32 [384, 384], replicated
- gradient_up_weight: float32 [384, 1536], replicated
- gradient_down_weight: float32 [1536, 384], replicated
- momentum_qkv: float32 [384, 1152], replicated
- momentum_proj: float32 [384, 384], replicated
- momentum_fc1: float32 [384, 1536], replicated
- momentum_fc2: float32 [1536, 384], replicated
- new_qkv: float32 [384, 1152], replicated
- new_proj: float32 [384, 384], replicated
- new_fc1: float32 [384, 1536], replicated
- new_fc2: float32 [1536, 384], replicated
- copy_qkv: bfloat16 [384, 1152], replicated
- copy_proj: bfloat16 [384, 384], replicated
- copy_fc1: bfloat16 [384, 1536], replicated
- copy_fc2: bfloat16 [1536, 384], replicated
- small_first_new: float32 [40, 384], replicated
- small_second_new: float32 [40, 384], replicated
- small_new: float32 [40, 384], replicated
- temper_first_moment_fresh: float32 [8], replicated
- temper_second_moment_fresh: float32 [8], replicated
- temper_revised: float32 [8], replicated
- stream_rms: float32 [4], replicated
The draws below stay inside these ranges and needn't reach their ends.
Inputs may be any that keep to these rules, and one draw needn't show every extreme that they name: `patch_tallness`: each row lists the 4 images of one canvas from top to bottom, each 32 columns wide; the heights sum to 64, and the third image has exactly 24 rows and holds rows 31 and 32.
All inputs are finite; a program needn't handle non-finite values.
Results may differ from the reference program's by a relative error of at most 0.001.
Values sent between devices are 32-bit elements; how exact they have to be, the bound alone decides.
A program may use at most 192 MiB of HBM per device.

```python
import math
import jax
import jax.numpy as jnp
from jax import lax

D = 384
HEAD_COUNT = 8
MLP = 1536
COLS = 32
CANV_ROWS = 64
NS_STEPS = 5
STEP = 10
CANVASES = 16
TOKENS = 32768
NSMALL = 40


def draw_patch_embeddings(key, part):
    key = jax.random.fold_in(key, 5)
    full_shape = (CANVASES, CANV_ROWS, COLS, D)
    canvas_ramp = jnp.arange(CANVASES, dtype=jnp.float32) / max(CANVASES - 1, 1)
    base_draw = jnp.clip(jax.random.normal(key, full_shape, jnp.float32), -4.0, 4.0)
    canvas_ramp = 1.0 + 2.0 * canvas_ramp
    return base_draw * canvas_ramp[:, None, None, None]


def draw_patch_tallness(key, part):
    key = jax.random.fold_in(key, 11)
    largest = 3 * CANV_ROWS // 8
    lowest = max(1, CANV_ROWS // 32)
    middle = CANV_ROWS // 2
    start_low = max(middle + 1 - largest, 2 * lowest, CANV_ROWS - 2 * largest)
    start_high = min(middle - 1, CANV_ROWS - largest - lowest, 2 * largest)
    key_start, key_first = jax.random.split(key)
    start_row = jax.random.randint(key_start, (CANVASES,), start_low, start_high + 1)
    first_low = jnp.maximum(lowest, start_row - largest)
    first_high = jnp.minimum(largest, start_row - lowest)
    spread_draw = jax.random.randint(key_first, (CANVASES,), 0, 1 << 20)
    first_height = first_low + spread_draw % (first_high - first_low + 1)
    stacked = jnp.stack([first_height, start_row - first_height, jnp.full((CANVASES,), largest, jnp.int32), CANV_ROWS - largest - start_row], axis=1)
    return stacked.astype(jnp.int32)


def draw_auxiliary_entry_table(key, part):
    key = jax.random.fold_in(key, 7)
    expand = MLP // D
    base_draw = jnp.clip(jax.random.normal(key, (NSMALL, D), jnp.float32), -3.0, 3.0)
    row_ids = jnp.arange(NSMALL)[:, None]
    gain_rows = (row_ids == 0) | (row_ids == 2) | (row_ids == 4) | (row_ids == 6) | (row_ids == 7) | (row_ids == 8) | (row_ids == 14)
    bias_rows = (row_ids >= 9) & (row_ids <= 11)
    kernel_rows = row_ids >= 18 + expand
    return jnp.where(gain_rows, 1.0 + 0.25 * base_draw, jnp.where(bias_rows, base_draw, jnp.where(kernel_rows, base_draw / 3.0, 0.3 * base_draw)))


def levels(own_key, extent, cuts, low, high):
    def one(dim, blocks):
        draws = jax.random.uniform(jax.random.fold_in(jax.random.fold_in(own_key, 6), dim), (blocks,), jnp.float32, low / len(cuts), high / len(cuts))
        return jnp.repeat(jnp.exp(draws), extent[dim] // blocks).reshape((-1,) + (1,) * (len(extent) - dim - 1))

    gain = one(*cuts[0])
    for cut in cuts[1:]:
        gain = gain * one(*cut)
    return gain


def noise(own_key, shape, deviation, reach, cuts=(), held_as=jnp.bfloat16):
    level = levels(own_key, shape, cuts, -0.22, 0.18) if cuts else 1.0
    drawn = jax.random.normal(own_key, shape, jnp.float32) * deviation * level
    return jnp.minimum(jnp.maximum(drawn, -reach), reach).astype(held_as)


def setup_inputs(seed: int = 0) -> dict:
    keys = jax.random.split(jax.random.key(seed), 18)
    return {
        "patch_embeddings": draw_patch_embeddings(jax.random.fold_in(keys[17], 71), 0),
        "loss_sensitivity": noise(keys[1], (CANVASES, CANV_ROWS, COLS, D), 1.0, 6.0, ((0, 16), (1, 2)), jnp.float32),
        "patch_tallness": draw_patch_tallness(jax.random.fold_in(keys[17], 71), 0),
        "triple_linear_map": noise(keys[3], (D, 3 * D), D ** -0.5, 0.3125, (), jnp.float32),
        "mixing_linear_map": noise(keys[4], (D, D), (D // 4) ** -0.5, 0.625, (), jnp.float32),
        "expanding_linear": noise(keys[5], (D, MLP), D ** -0.5, 0.3125, (), jnp.float32),
        "contracting_linear": noise(keys[6], (MLP, D), MLP ** -0.5, 0.15625, (), jnp.float32),
        "triple_momentum": noise(keys[7], (D, 3 * D), (0.3 * TOKENS ** 0.5), 320.0, (), jnp.float32),
        "mixing_momentum": noise(keys[8], (D, D), (0.4 * TOKENS ** 0.5), 448.0, (), jnp.float32),
        "expanding_momentum": noise(keys[9], (D, MLP), (0.3 * TOKENS ** 0.5), 320.0, (), jnp.float32),
        "contracting_momentum": noise(keys[10], (MLP, D), (0.6 * TOKENS ** 0.5), 640.0, (), jnp.float32),
        "auxiliary_entry_table": draw_auxiliary_entry_table(jax.random.fold_in(keys[17], 71), 0),
        "auxiliary_first_moment": noise(keys[12], (NSMALL, D), (0.033 * TOKENS ** 0.5), 32.0, (), jnp.float32),
        "auxiliary_second_moment": jnp.clip(jnp.exp(jax.random.uniform(keys[13], (NSMALL, D), jnp.float32, math.log(157.2864), math.log(622.592))), 157.2864, 622.592),
        "logit_scaling": jnp.clip(jnp.exp(jax.random.uniform(keys[14], (HEAD_COUNT,), jnp.float32, math.log(2.0), math.log(6.0))), 2.0, 6.0),
        "temper_first_moment": noise(keys[15], (HEAD_COUNT,), (0.11 * TOKENS ** 0.5), 128.0, (), jnp.float32),
        "temper_second_moment": jnp.clip(jnp.exp(jax.random.uniform(keys[16], (HEAD_COUNT,), jnp.float32, math.log(1736.704), math.log(6881.28))), 1736.704, 6881.28),
    }


exact_mode = lax.Precision.HIGHEST
eps_norm = 1e-06
root_half = 1.0 / math.sqrt(2.0)
ns_first = 3.4445
ns_second = -4.775
ns_third = 2.0315
muon_rate = 0.2
muon_keep = 0.95
decay_rate = 0.01
adam_rate = 0.2
beta_first = 0.9
beta_second = 0.95
adam_floor = 1e-08

@jax.custom_vjp
def low(v):
    return lax.optimization_barrier(v.astype(jnp.bfloat16)).astype(jnp.float32)

@jax.custom_vjp
def low_back(v):
    return v

def low_keep(v):
    return (low(v), None)

def low_pass(kept, grad):
    return (grad,)

def back_keep(v):
    return (v, None)

def back_low(kept, grad):
    return (low(grad),)
low.defvjp(low_keep, low_pass)
low_back.defvjp(back_keep, back_low)

def layer_norm(inputs, norm_gain, norm_shift):
    average = lax.optimization_barrier(jnp.mean(inputs, axis=-1, keepdims=True))
    centered = inputs - average
    spread = lax.optimization_barrier(jnp.mean(centered * centered, axis=-1, keepdims=True))
    return centered * lax.rsqrt(spread + eps_norm) * norm_gain + norm_shift

def gelu_exact(inputs):
    return 0.5 * inputs * (1.0 + lax.erf(inputs * root_half))

def row_labels():
    return ['norm1_gain', 'norm1_shift', 'norm3_gain', 'norm3_shift', 'norm2_gain', 'norm2_shift', 'scale_attn', 'scale_local', 'scale_mlp', 'query_bias', 'key_bias', 'value_bias', 'proj_bias', 'conv1_bias', 'batch_gain', 'batch_shift', 'conv2_bias', 'fc2_bias']

def unpack(auxiliary_entry_table):
    expand = auxiliary_entry_table.shape[0] - 36
    pieces = {}
    for position, row_label in enumerate(row_labels()):
        pieces[row_label] = auxiliary_entry_table[position]
    pieces['fc1_bias'] = auxiliary_entry_table[18:18 + expand].reshape(-1)
    pieces['conv1_kernel'] = auxiliary_entry_table[18 + expand:27 + expand]
    pieces['conv2_kernel'] = auxiliary_entry_table[27 + expand:36 + expand]
    return pieces

def segment_rows(canvas_heights, row_ids, total_rows):
    row_ends = jnp.cumsum(canvas_heights).astype(jnp.int32)
    segment = lax.optimization_barrier(jnp.sum((row_ids[:, None] >= row_ends[None, :]).astype(jnp.int32), axis=1))
    inside = (row_ids >= 0) & (row_ids < total_rows)
    return jnp.where(inside, segment, -1).astype(jnp.int32)

def tap_views(extended, segment_ext, out_first, out_count):
    width_cols = extended.shape[2]
    padded = jnp.pad(extended, ((0, 0), (0, 0), (1, 1), (0, 0)))
    target = lax.slice_in_dim(segment_ext, out_first, out_first + out_count, axis=1)
    tap_list = []
    for row_step in (-1, 0, 1):
        source = lax.slice_in_dim(padded, out_first + row_step, out_first + row_step + out_count, axis=1)
        source_segment = lax.slice_in_dim(segment_ext, out_first + row_step, out_first + row_step + out_count, axis=1)
        allowed = ((source_segment == target) & (source_segment >= 0)).astype(jnp.float32)
        for col_step in (-1, 0, 1):
            tap_list.append(source[:, :, 1 + col_step:1 + col_step + width_cols] * allowed[:, :, None, None])
    return tap_list

def depthwise(tap_list, kernel):
    result = tap_list[0] * kernel[0]
    for tap_index in range(1, 9):
        result = result + tap_list[tap_index] * kernel[tap_index]
    return result

def orthogonalize(matrix):
    scale_now = jnp.sqrt(lax.optimization_barrier(jnp.sum(matrix * matrix, axis=(-2, -1), keepdims=True)))
    iterate = matrix / (scale_now + 1e-07)
    for step_index in range(NS_STEPS):
        gram_matrix = jnp.einsum('...ij,...kj->...ik', iterate, iterate, precision=exact_mode)
        polynomial = ns_second * gram_matrix + ns_third * jnp.einsum('...ij,...jk->...ik', gram_matrix, gram_matrix, precision=exact_mode)
        iterate = ns_first * iterate + jnp.einsum('...ij,...jk->...ik', polynomial, iterate, precision=exact_mode)
    return iterate

def slot_result(slot_id, momenta):
    momentum_qkv, momentum_proj, momentum_fc1, momentum_fc2 = momenta
    if slot_id == 0:
        features = momentum_proj.shape[0]
        blocks = jnp.stack([momentum_qkv[:, :features], momentum_qkv[:, features:2 * features], momentum_qkv[:, 2 * features:], momentum_proj])
        orthogonal = orthogonalize(blocks)
        return jnp.concatenate([orthogonal[0], orthogonal[1], orthogonal[2], orthogonal[3]], axis=1)
    if slot_id == 1:
        return orthogonalize(momentum_fc1)
    return orthogonalize(momentum_fc2.T)

def muon_step(weight, orthogonal, factor):
    return weight * (1.0 - muon_rate * decay_rate) - muon_rate * 0.2 * factor * orthogonal

def decoupled_moment_step(current, moment_one, moment_two, gradient):
    first_new = beta_first * moment_one + (1.0 - beta_first) * gradient
    second_new = beta_second * moment_two + (1.0 - beta_second) * gradient * gradient
    fix_first = 1.0 - beta_first ** STEP
    fix_second = 1.0 - beta_second ** STEP
    updated = current - adam_rate * (first_new / fix_first) / (jnp.sqrt(second_new / fix_second) + adam_floor)
    return (first_new, second_new, updated)

def canvas_forward(inputs, canvas_heights, linear_map_group):
    triple_linear_map, mixing_linear_map, expanding_linear, contracting_linear, auxiliary_entry_table, logit_scaling = linear_map_group
    pieces = unpack(auxiliary_entry_table)
    total_rows, col_count, features = inputs.shape
    head_tally = logit_scaling.shape[0]
    head_dim = features // head_tally
    images = canvas_heights.shape[0]
    token_count = total_rows * col_count
    row_ids = jnp.arange(-1, total_rows + 1).astype(jnp.int32)
    segment_ext = segment_rows(canvas_heights, row_ids, total_rows)[None]
    row_hot = (segment_ext[0, 1:-1][:, None] == jnp.arange(images).astype(jnp.int32)[None, :]).astype(jnp.float32)
    token_hot = jnp.repeat(row_hot, col_count, axis=0)
    image_mask = token_hot.T[:, :, None, None]
    flat_tokens = inputs.reshape(token_count, features)
    normed = layer_norm(flat_tokens, pieces['norm1_gain'], pieces['norm1_shift'])
    qkv_bias = jnp.concatenate([pieces['query_bias'], pieces['key_bias'], pieces['value_bias']])
    qkv_rows = jnp.dot(normed, triple_linear_map, precision=exact_mode) + qkv_bias
    query_proj, key_proj, value_proj = jnp.split(qkv_rows, 3, axis=-1)
    head_shape = (token_count, head_tally, head_dim)
    query_heads = query_proj.reshape(head_shape)
    key_heads = key_proj.reshape(head_shape)
    value_heads = value_proj.reshape(head_shape)
    masked_query = image_mask * query_heads[None]
    masked_value = image_mask * value_heads[None]
    cross_sum = jnp.einsum('mthi,thj->mhij', masked_query, key_heads, precision=exact_mode)
    query_squares = jnp.dot(token_hot.T, query_proj * query_proj, precision=exact_mode)
    key_squares = jnp.dot(token_hot.T, key_proj * key_proj, precision=exact_mode)
    query_norm = jnp.sqrt(query_squares + eps_norm).reshape(images, head_tally, head_dim)
    key_norm = jnp.sqrt(key_squares + eps_norm).reshape(images, head_tally, head_dim)
    normalized_channel_gram = cross_sum / (query_norm[..., :, None] * key_norm[..., None, :])
    softmax_weights = jax.nn.softmax(logit_scaling[None, :, None, None] * normalized_channel_gram, axis=-1)
    mixed_heads = jnp.einsum('mhij,mthj->thi', softmax_weights, masked_value, precision=exact_mode).reshape(token_count, features)
    branch_attn = pieces['scale_attn'] * (jnp.dot(mixed_heads, mixing_linear_map, precision=exact_mode) + pieces['proj_bias'])
    stream_one = flat_tokens + branch_attn
    local_in = layer_norm(stream_one, pieces['norm3_gain'], pieces['norm3_shift']).reshape(1, total_rows, col_count, features)
    padded_in = jnp.pad(local_in, ((0, 0), (1, 1), (0, 0), (0, 0)))
    pre_act = depthwise(tap_views(padded_in, segment_ext, 1, total_rows), pieces['conv1_kernel']) + pieces['conv1_bias']
    middle = gelu_exact(pre_act) * pieces['batch_gain'] + pieces['batch_shift']
    padded_middle = jnp.pad(middle, ((0, 0), (1, 1), (0, 0), (0, 0)))
    local_out = depthwise(tap_views(padded_middle, segment_ext, 1, total_rows), pieces['conv2_kernel']) + pieces['conv2_bias']
    branch_local = pieces['scale_local'] * local_out.reshape(token_count, features)
    stream_two = stream_one + branch_local
    normed_two = layer_norm(stream_two, pieces['norm2_gain'], pieces['norm2_shift'])
    hidden = gelu_exact(jnp.dot(normed_two, expanding_linear, precision=exact_mode) + pieces['fc1_bias'])
    branch_mlp = pieces['scale_mlp'] * (jnp.dot(hidden, contracting_linear, precision=exact_mode) + pieces['fc2_bias'])
    block_result = stream_two + branch_mlp
    elementwise_squares = jnp.stack([jnp.sum(block_result * block_result), jnp.sum(branch_attn * branch_attn), jnp.sum(branch_local * branch_local), jnp.sum(branch_mlp * branch_mlp)])
    return (block_result.reshape(total_rows, col_count, features), elementwise_squares)

def reference(patch_embeddings, loss_sensitivity, patch_tallness, triple_linear_map, mixing_linear_map, expanding_linear, contracting_linear, triple_momentum, mixing_momentum, expanding_momentum, contracting_momentum, auxiliary_entry_table, auxiliary_first_moment, auxiliary_second_moment, logit_scaling, temper_first_moment, temper_second_moment):

    def evaluate_block(inputs_all, weight_qkv, weight_proj, weight_fc1, weight_fc2, small_all, temper_all):
        linear_map_group = (weight_qkv, weight_proj, weight_fc1, weight_fc2, small_all, temper_all)

        def one_canvas(canvas_pair):
            return canvas_forward(canvas_pair[0], canvas_pair[1], linear_map_group)
        outputs, elementwise_squares = lax.map(jax.checkpoint(one_canvas), (inputs_all, patch_tallness))
        return (outputs, lax.optimization_barrier(jnp.sum(elementwise_squares, axis=0)))
    block_result, evaluate_with_derivative, elementwise_squares = jax.vjp(evaluate_block, patch_embeddings, triple_linear_map, mixing_linear_map, expanding_linear, contracting_linear, auxiliary_entry_table, logit_scaling, has_aux=True)
    gradient_list = evaluate_with_derivative(loss_sensitivity)
    gradient_input_tokens, gradient_query_key_value, gradient_output_weight, gradient_up_weight, gradient_down_weight, gradient_small_params, derivative_temper = gradient_list
    stream_rms = jnp.sqrt(elementwise_squares / patch_embeddings.size)
    momenta = (muon_keep * triple_momentum + gradient_query_key_value, muon_keep * mixing_momentum + gradient_output_weight, muon_keep * expanding_momentum + gradient_up_weight, muon_keep * contracting_momentum + gradient_down_weight)
    results = [slot_result(slot_id, momenta) for slot_id in range(3)]
    features = mixing_linear_map.shape[0]
    root_small = math.sqrt(features)
    root_large = math.sqrt(expanding_linear.shape[1])
    new_qkv = muon_step(triple_linear_map, results[0][:, :3 * features], root_small)
    new_proj = muon_step(mixing_linear_map, results[0][:, 3 * features:], root_small)
    new_fc1 = muon_step(expanding_linear, results[1], root_large)
    new_fc2 = muon_step(contracting_linear, results[2].T, root_large)
    small_first_new, small_second_new, small_new = decoupled_moment_step(auxiliary_entry_table, auxiliary_first_moment, auxiliary_second_moment, gradient_small_params)
    temper_first_moment_fresh, temper_second_moment_fresh, temper_revised = decoupled_moment_step(logit_scaling, temper_first_moment, temper_second_moment, derivative_temper)
    return (block_result, gradient_input_tokens, gradient_query_key_value, gradient_output_weight, gradient_up_weight, gradient_down_weight, momenta[0], momenta[1], momenta[2], momenta[3], new_qkv, new_proj, new_fc1, new_fc2, new_qkv.astype(jnp.bfloat16), new_proj.astype(jnp.bfloat16), new_fc1.astype(jnp.bfloat16), new_fc2.astype(jnp.bfloat16), small_first_new, small_second_new, small_new, temper_first_moment_fresh, temper_second_moment_fresh, temper_revised, stream_rms)
```

```python
import math

import jax
import jax.numpy as jnp
from jax import lax
from jax.experimental import pallas as pl
from jax.experimental.pallas import tpu as pltpu
from jax.sharding import PartitionSpec as P

BF = jnp.bfloat16
F32 = jnp.float32
MESH_ID = pl.DeviceIdType.MESH

EPS = 1e-06
ROOT_HALF = 1.0 / math.sqrt(2.0)
ROOT_TWOPI = 1.0 / math.sqrt(2.0 * math.pi)
STEP = 10
MUON_RATE = 0.2
MUON_KEEP = 0.95
DECAY = 0.01
ADAM_RATE = 0.2
BETA1 = 0.9
BETA2 = 0.95
ADAM_FLOOR = 1e-08

HEADS = 8
HD = 48
D = HEADS * HD
COLS = 32
HALO = 4 * COLS
TILE = 256

N1G, N1S, N3G, N3S, N2G, N2S, SA, SL, SM, QB, KB, VB, PB, C1B, BG, BS, C2B, F2B = range(18)
F1B, K1R, K2R = 18, 22, 31
SMALL = 40
TABLE = 48


def halves(v):
    hi = v.astype(BF)
    return hi, (v - hi.astype(F32)).astype(BF)


def side(v):
    h, l = halves(v)
    return jnp.concatenate([h, l, h], axis=1)


def dot_nn(a, b):
    return lax.dot_general(a, b, (((1,), (0,)), ((), ())), preferred_element_type=F32)


def dot_nt(a, b):
    return lax.dot_general(a, b, (((1,), (1,)), ((), ())), preferred_element_type=F32)


def normalize(v):
    mean = jnp.mean(v, axis=1, keepdims=True)
    c = v - mean
    r = lax.rsqrt(jnp.mean(c * c, axis=1, keepdims=True) + EPS)
    return c * r, r


def normalize_back(e, xhat, r):
    return r * (
        e - jnp.mean(e, axis=1, keepdims=True) - xhat * jnp.mean(e * xhat, axis=1, keepdims=True)
    )


def gelu_parts(v):
    phi = 0.5 * (1.0 + lax.erf(v * ROOT_HALF))
    return v * phi, phi + v * jnp.exp(-0.5 * v * v) * ROOT_TWOPI


def eights(v):
    total = v[0:8]
    for i in range(8, v.shape[0], 8):
        total = total + v[i : i + 8]
    return total


def sweep(count, size, body):
    def one(i, carry):
        body(pl.multiple_of(i * size, size))
        return carry

    lax.fori_loop(0, count // size, one, 0)


def image_ends(tall_ref):
    e0 = tall_ref[0, 0]
    e1 = e0 + tall_ref[0, 1]
    return e0, e1, e1 + tall_ref[0, 2]


def slots(tall_ref, core, first_row, rows_all):
    e0, e1, e2 = image_ends(tall_ref)
    low = (jnp.where(core == 0, 0, e2), jnp.where(core == 0, e0, 0), e1)
    high = (jnp.where(core == 0, e0, rows_all), jnp.where(core == 0, e1, 0), e2)
    return [((a - first_row) * COLS, (b - first_row) * COLS) for a, b in zip(low, high)]


def span_mask(start, rows, lo, hi):
    token = start + lax.broadcasted_iota(jnp.int32, (rows, D), 0)
    return (token >= lo) & (token < hi)


def lane_head():
    return lax.broadcasted_iota(jnp.int32, (HD, D), 1) // HD


def lane_slot():
    return lax.broadcasted_iota(jnp.int32, (HD, D), 1) % HD


def fold(full):
    head = lane_head()
    total = jnp.where(head == 0, full[0:HD], 0.0)
    for h in range(1, HEADS):
        total = total + jnp.where(head == h, full[h * HD : h * HD + HD], 0.0)
    return total


def unfold(small):
    head = lane_head()
    return jnp.concatenate([jnp.where(head == h, small, 0.0) for h in range(HEADS)], axis=0)


def group_ones():
    a = lax.broadcasted_iota(jnp.int32, (D, D), 0) // HD
    b = lax.broadcasted_iota(jnp.int32, (D, D), 1) // HD
    return jnp.where(a == b, 1.0, 0.0).astype(BF)


def group_sum(v, ones):
    h = v.astype(BF)
    rest = v - h.astype(F32)
    m = rest.astype(BF)
    l = (rest - m.astype(F32)).astype(BF)
    return dot_nn(h, ones) + (dot_nn(m, ones) + dot_nn(l, ones))


def row_to_fold(row, ones):
    slot = lax.broadcasted_iota(jnp.int32, (HD, D), 0)
    return group_sum(jnp.where(lane_slot() == slot, jnp.broadcast_to(row, (HD, D)), 0.0), ones)


def fold_to_row(small):
    slot = lax.broadcasted_iota(jnp.int32, (HD, D), 0)
    return jnp.sum(jnp.where(lane_slot() == slot, small, 0.0), axis=0, keepdims=True)


def head_row(temp_ref):
    head = lax.broadcasted_iota(jnp.int32, (1, D), 1) // HD
    row = jnp.where(head == 0, temp_ref[0], 0.0)
    for h in range(1, HEADS):
        row = row + jnp.where(head == h, temp_ref[h], 0.0)
    return row


def project_kernel(tall_ref, x_ref, w_ref, tab_ref, q_ref, k_ref, v_ref, sums_ref, wcat, cross):
    step = pl.program_id(0)
    core = lax.axis_index("rows")
    rows_all = 2 * pl.num_programs(0) * TILE // COLS
    spans = slots(tall_ref, core, core * (rows_all // 2), rows_all)
    start = step * TILE

    @pl.when(step == 0)
    def _():
        def part(o):
            h, l = halves(w_ref[pl.ds(o, 16)])
            wcat[pl.ds(o, 16)] = h
            wcat[pl.ds(D + o, 16)] = h
            wcat[pl.ds(2 * D + o, 16)] = l

        sweep(D, 16, part)
        cross[...] = jnp.zeros_like(cross)
        sums_ref[...] = jnp.zeros_like(sums_ref)

    xhat, _ = normalize(x_ref[...])
    lhs = side(xhat * tab_ref[N1G : N1G + 1] + tab_ref[N1S : N1S + 1])
    q = dot_nn(lhs, wcat[:, 0:D]) + tab_ref[QB : QB + 1]
    q_ref[...] = q
    k = dot_nn(lhs, wcat[:, D : 2 * D]) + tab_ref[KB : KB + 1]
    k_ref[...] = k
    v_ref[...] = dot_nn(lhs, wcat[:, 2 * D : 3 * D]) + tab_ref[VB : VB + 1]
    qt = side(q.T)
    for s, (lo, hi) in enumerate(spans):

        @pl.when((lo < start + TILE) & (hi > start))
        def _():
            mask = span_mask(start, TILE, lo, hi)
            kh, kl = halves(jnp.where(mask, k_ref[...], 0.0))
            cross[s] += dot_nn(qt, jnp.concatenate([kh, kh, kl], axis=0))
            qm = jnp.where(mask, q_ref[...], 0.0)
            km = jnp.where(mask, k_ref[...], 0.0)
            sums_ref[s, HD : HD + 1] += jnp.sum(qm * qm, axis=0, keepdims=True)
            sums_ref[s, HD + 1 : HD + 2] += jnp.sum(km * km, axis=0, keepdims=True)

    @pl.when(step == pl.num_programs(0) - 1)
    def _():
        for s in range(3):
            sums_ref[s, 0:HD] = fold(cross[s])


def project(tall, x, w, tab):
    tokens = x.shape[0]
    row = pl.BlockSpec((TILE, D), lambda i: (i, 0))
    return pl.pallas_call(
        project_kernel,
        grid=(tokens // TILE,),
        out_shape=[jax.ShapeDtypeStruct((tokens, D), F32)] * 3
        + [jax.ShapeDtypeStruct((3, HD + 8, D), F32)],
        in_specs=[
            pl.BlockSpec(memory_space=pltpu.SMEM),
            row,
            pl.BlockSpec((D, 3 * D), lambda i: (0, 0)),
            pl.BlockSpec((SMALL, D), lambda i: (0, 0)),
        ],
        out_specs=[row, row, row, pl.BlockSpec((3, HD + 8, D), lambda i: (0, 0, 0))],
        scratch_shapes=[pltpu.VMEM((3 * D, 3 * D), BF), pltpu.VMEM((3, D, D), F32)],
        compiler_params=pltpu.CompilerParams(vmem_limit_bytes=40 << 20),
    )(tall, x, w, tab)


def widen_kernel(x_ref, dy_ref, v_ref, sums_ref, xe, dye, ve, peer, own_sem, send_sem, recv_sem):
    core = lax.axis_index("rows")
    tokens = x_ref.shape[0]
    barrier = pltpu.get_barrier_semaphore()
    pl.semaphore_signal(barrier, inc=1, device_id={"rows": 1 - core}, device_id_type=MESH_ID)
    local = []
    for i, (src, dst) in enumerate(((x_ref, xe), (dy_ref, dye), (v_ref, ve))):
        at = pl.multiple_of(core * HALO, HALO)
        local.append(pltpu.make_async_copy(src, dst.at[pl.ds(at, tokens)], own_sem.at[i]))
        local[-1].start()
    pl.semaphore_wait(barrier, 1)
    away = []
    pairs = [
        (
            src.at[pl.ds(pl.multiple_of((1 - core) * (tokens - HALO), HALO), HALO)],
            dst.at[pl.ds(pl.multiple_of(core * tokens, HALO), HALO)],
        )
        for src, dst in ((x_ref, xe), (dy_ref, dye), (v_ref, ve))
    ]
    pairs.append((sums_ref.at[2], peer))
    for i, (src, dst) in enumerate(pairs):
        away.append(
            pltpu.make_async_remote_copy(
                src_ref=src,
                dst_ref=dst,
                send_sem=send_sem.at[i],
                recv_sem=recv_sem.at[i],
                device_id={"rows": 1 - core},
                device_id_type=MESH_ID,
            )
        )
        away[-1].start()
    for copy in local + away:
        copy.wait()


def widen(x, dy, v, sums):
    tokens = x.shape[0]
    wide = jax.ShapeDtypeStruct((tokens + HALO, D), F32)
    anywhere = pl.BlockSpec(memory_space=pl.ANY)
    return pl.pallas_call(
        widen_kernel,
        out_shape=[wide, wide, wide, jax.ShapeDtypeStruct(sums.shape[1:], F32)],
        in_specs=[anywhere] * 4,
        out_specs=[anywhere] * 4,
        scratch_shapes=[
            pltpu.SemaphoreType.DMA((3,)),
            pltpu.SemaphoreType.DMA((4,)),
            pltpu.SemaphoreType.DMA((4,)),
        ],
        compiler_params=pltpu.CompilerParams(collective_id=0, has_side_effects=True),
    )(x, dy, v, sums)


def swap_kernel(src, dst, send_sem, recv_sem):
    core = lax.axis_index("rows")
    barrier = pltpu.get_barrier_semaphore()
    pl.semaphore_signal(barrier, inc=1, device_id={"rows": 1 - core}, device_id_type=MESH_ID)
    pl.semaphore_wait(barrier, 1)
    copy = pltpu.make_async_remote_copy(
        src_ref=src,
        dst_ref=dst,
        send_sem=send_sem,
        recv_sem=recv_sem,
        device_id={"rows": 1 - core},
        device_id_type=MESH_ID,
    )
    copy.start()
    copy.wait()


def swap(v, number):
    return pl.pallas_call(
        swap_kernel,
        out_shape=jax.ShapeDtypeStruct(v.shape, F32),
        in_specs=[pl.BlockSpec(memory_space=pl.ANY)],
        out_specs=pl.BlockSpec(memory_space=pl.ANY),
        scratch_shapes=[pltpu.SemaphoreType.DMA, pltpu.SemaphoreType.DMA],
        compiler_params=pltpu.CompilerParams(collective_id=number, has_side_effects=True),
    )(v)


def shifted(u, col):
    left = jnp.where(col == 0, 0.0, pltpu.roll(u, 1, 0))
    right = jnp.where(col == COLS - 1, 0.0, pltpu.roll(u, COLS - 1, 0))
    return left, u, right


def row_flags(tall_ref, rows_all):
    ends = image_ends(tall_ref)

    def above(row):
        first = (row == 0) | (row == ends[0]) | (row == ends[1]) | (row == ends[2])
        return jnp.where(first, 0.0, 1.0)

    def below(row):
        return jnp.where(row + 1 == rows_all, 0.0, above(row + 1))

    return above, below


def middle_kernel(
    tall_ref,
    temp_ref,
    x_ref,
    dy_ref,
    v_ref,
    sums_ref,
    peer_ref,
    wp_ref,
    w1_ref,
    w2_ref,
    tab_ref,
    out_ref,
    ds1_ref,
    dmx_ref,
    dwp_ref,
    dw1_ref,
    dw2_ref,
    gtab_ref,
    probs_ref,
    unit_ref,
    gprob_ref,
    wpv,
    wph,
    w1c,
    w2c,
    pcat,
    mixed,
    s1,
    li,
    act,
    slope,
    mid,
    lo_,
    s2,
    ds2,
    gp,
    z,
    n2c,
    dzc,
    hid_h,
    hid_l,
    hslope,
    b1_ref,
    b1g_ref,
    acc,
    cross,
):
    core = lax.axis_index("rows")
    wide = x_ref.shape[0]
    tokens = wide - HALO
    own_rows = tokens // COLS
    rows_wide = wide // COLS
    rows_all = 2 * own_rows
    first_row = core * (own_rows - HALO // COLS)
    own_off = pl.multiple_of(core * HALO, HALO)
    mlp = w1_ref.shape[1]
    spans = slots(tall_ref, core, first_row, rows_all)
    above, below = row_flags(tall_ref, rows_all)

    def tab(r):
        return tab_ref[r : r + 1]

    def part_p(o):
        h, l = halves(wp_ref[pl.ds(o, 16)])
        wpv[pl.ds(o, 16)] = h
        wpv[pl.ds(D + o, 16)] = h
        wpv[pl.ds(2 * D + o, 16)] = l
        wph[pl.ds(o, 16), 0:D] = h
        wph[pl.ds(o, 16), D : 2 * D] = h
        wph[pl.ds(o, 16), 2 * D : 3 * D] = l

    sweep(D, 16, part_p)

    def part_1(o):
        h, l = halves(w1_ref[pl.ds(o, 16)])
        w1c[pl.ds(o, 16)] = h
        w1c[pl.ds(D + o, 16)] = h
        w1c[pl.ds(2 * D + o, 16)] = l

    sweep(D, 16, part_1)

    def part_2(o):
        h, l = halves(w2_ref[pl.ds(o, 32)])
        w2c[pl.ds(o, 32), 0:D] = h
        w2c[pl.ds(o, 32), D : 2 * D] = h
        w2c[pl.ds(o, 32), 2 * D : 3 * D] = l

    sweep(mlp, 32, part_2)

    ones = group_ones()
    temp = head_row(temp_ref)
    for s in range(3):
        sums = sums_ref[s]
        if s == 2:
            sums = sums + peer_ref[...]
        inv_q = lax.rsqrt(sums[HD : HD + 1] + EPS)
        inv_k = lax.rsqrt(sums[HD + 1 : HD + 2] + EPS)
        unit = sums[0:HD] * row_to_fold(inv_q, ones) * inv_k
        unit_ref[s] = unit
        weight = jnp.exp(temp * unit)
        probs = weight / group_sum(weight, ones)
        probs_ref[s] = probs
        h, l = halves(unfold(probs))
        pcat[s, :, 0:D] = h
        pcat[s, :, D : 2 * D] = h
        pcat[s, :, 2 * D : 3 * D] = l

    acc[...] = jnp.zeros_like(acc)
    gtab_ref[...] = jnp.zeros_like(gtab_ref)

    def add(r, v):
        acc[8 * r : 8 * r + 8] += v

    def attend(o):
        size = wide // 3
        mixed[pl.ds(o, size)] = jnp.zeros((size, D), F32)
        for s, (lo, hi) in enumerate(spans):

            @pl.when((lo < o + size) & (hi > o))
            def _():
                vm = jnp.where(span_mask(o, size, lo, hi), v_ref[pl.ds(o, size)], 0.0)
                mixed[pl.ds(o, size)] += dot_nt(side(vm), pcat[s])

        z[...] = dot_nn(side(mixed[pl.ds(o, size)]), wpv[...]) + tab(PB)

        def finish(i):
            branch = tab(SA) * z[pl.ds(i, COLS)]
            at = pl.multiple_of(o + i, COLS)
            stream = x_ref[pl.ds(at, COLS)] + branch
            s1[pl.ds(at, COLS)] = stream
            xhat, _ = normalize(stream)
            li[pl.ds(at + COLS, COLS)] = xhat * tab(N3G) + tab(N3S)
            mine = jnp.where((at >= own_off) & (at < own_off + tokens), 1.0, 0.0)
            add(41, mine * eights(branch * branch))

        sweep(size, COLS, finish)

    sweep(wide, wide // 3, attend)

    pad = jnp.zeros((COLS, D), F32)
    for buf in (li, mid, gp, ds2):
        buf[0:COLS] = pad
        buf[wide + COLS : wide + 2 * COLS] = pad

    def convolve(src, base, flip, scale_row, lane, visit, source=None):
        lanes = pl.ds(lane, 128)
        taps = [tab_ref[base + t : base + t + 1, lanes] for t in range(9)]
        if flip:
            taps = taps[::-1]
        if scale_row is not None:
            taps = [t * scale_row for t in taps]
        taps = [jnp.broadcast_to(t, (COLS, 128)) for t in taps]
        col = lax.broadcasted_iota(jnp.int32, (COLS, 128), 0)
        zero = jnp.zeros((COLS, 128), F32)

        def one(r, carry):
            partial, from_above = carry
            at = pl.multiple_of(r * COLS + COLS, COLS)
            views = shifted(src[pl.ds(at, COLS), lanes], col)
            rows = [
                views[0] * taps[3 * a] + views[1] * taps[3 * a + 1] + views[2] * taps[3 * a + 2]
                for a in range(3)
            ]
            visit(r - 1, partial + below(first_row + r - 1) * rows[2])
            if source is not None:
                source(r, views)
            return rows[1] + above(first_row + r) * from_above, rows[0]

        lax.fori_loop(0, rows_wide + 1, one, (zero, zero))

    for lane in range(0, D, 128):
        lanes = pl.ds(lane, 128)

        def first(r, value):
            at = pl.multiple_of(r * COLS + COLS, COLS)
            a, s = gelu_parts(value + tab_ref[C1B : C1B + 1, lanes])
            act[pl.ds(at, COLS), lanes] = a
            slope[pl.ds(at, COLS), lanes] = s
            mid[pl.ds(at, COLS), lanes] = a * tab_ref[BG : BG + 1, lanes] + tab_ref[BS : BS + 1, lanes]

        convolve(li, K1R, False, None, lane, first)

    for lane in range(0, D, 128):
        lanes = pl.ds(lane, 128)

        def second(r, value):
            at = pl.multiple_of(r * COLS + COLS, COLS)
            value = value + tab_ref[C2B : C2B + 1, lanes]
            lo_[pl.ds(at, COLS), lanes] = value

        convolve(mid, K2R, False, None, lane, second)

    def join(o):
        branch = tab(SL) * lo_[pl.ds(o + COLS, COLS)]
        s2[pl.ds(o, COLS)] = s1[pl.ds(o, COLS)] + branch
        mine = jnp.where((o >= own_off) & (o < own_off + tokens), 1.0, 0.0)
        add(42, mine * eights(branch * branch))

    sweep(wide, COLS, join)

    dw1_ref[...] = jnp.zeros_like(dw1_ref)
    dw2_ref[...] = jnp.zeros_like(dw2_ref)
    b1g_ref[...] = jnp.zeros_like(b1g_ref)
    for i in range(mlp // D):
        b1_ref[0:1, i * D : i * D + D] = tab(F1B + i)

    def feed(o, size, own):
        rows = pl.ds(0, size)
        chunk = 16

        def enter(i):
            xhat, _ = normalize(s2[pl.ds(pl.multiple_of(o + i, chunk), chunk)])
            n2 = xhat * tab(N2G) + tab(N2S)
            h, l = halves(n2)
            n2c[pl.ds(i, chunk), 0:D] = h
            n2c[pl.ds(i, chunk), D : 2 * D] = l
            n2c[pl.ds(i, chunk), 2 * D : 3 * D] = h

        sweep(size, chunk, enter)

        def up(j):
            lanes = pl.ds(j, 256)
            pre = dot_nn(n2c[rows], w1c[:, lanes]) + b1_ref[0:1, lanes]
            a, s = gelu_parts(pre)
            h, l = halves(a)
            hid_h[rows, lanes] = h
            hid_l[rows, lanes] = l
            hslope[rows, lanes] = s

        sweep(mlp, 256, up)
        w2h, w2l = w2c[:, 0:D], w2c[:, 2 * D : 3 * D]
        z[rows] = (
            dot_nn(hid_h[rows], w2h) + (dot_nn(hid_l[rows], w2h) + dot_nn(hid_h[rows], w2l))
        ) + tab(F2B)

        def turn(i):
            at = pl.multiple_of(o + i, chunk)
            dy = dy_ref[pl.ds(at, chunk)]
            dz = tab(SM) * dy
            h, l = halves(dz)
            dzc[pl.ds(i, chunk), 0:D] = h
            dzc[pl.ds(i, chunk), D : 2 * D] = l
            dzc[pl.ds(i, chunk), 2 * D : 3 * D] = h
            if own:
                raw = z[pl.ds(i, chunk)]
                branch = tab(SM) * raw
                result = s2[pl.ds(at, chunk)] + branch
                out_ref[pl.ds(pl.multiple_of(at - own_off, chunk), chunk)] = result
                add(40, eights(result * result))
                add(43, eights(branch * branch))
                add(SM, eights(dy * raw))
                add(F2B, eights(dz))

        sweep(size, chunk, turn)
        if own:
            nt = n2c[rows, 0:D].T, n2c[rows, D : 2 * D].T
            dt = dzc[rows, 0:D].T, dzc[rows, D : 2 * D].T

        def down(j):
            lanes = pl.ds(j, 256)
            dpre = dot_nt(dzc[rows], w2c[lanes, :]) * hslope[rows, lanes]
            h, l = halves(dpre)
            if own:
                b1g_ref[:, lanes] += eights(dpre)
                dw1_ref[:, lanes] += dot_nn(nt[0], h) + (dot_nn(nt[1], h) + dot_nn(nt[0], l))
                hh, hl = hid_h[rows, lanes], hid_l[rows, lanes]
                dw2_ref[:, lanes] += dot_nn(dt[0], hh) + (dot_nn(dt[1], hh) + dot_nn(dt[0], hl))
            hid_h[rows, lanes] = h
            hid_l[rows, lanes] = l

        sweep(mlp, 256, down)
        w1h, w1l = w1c[0:D], w1c[2 * D : 3 * D]
        z[rows] = dot_nt(hid_h[rows], w1h) + (
            dot_nt(hid_l[rows], w1h) + dot_nt(hid_h[rows], w1l)
        )

        def leave(i):
            at = pl.multiple_of(o + i, chunk)
            xhat, r = normalize(s2[pl.ds(at, chunk)])
            dn = z[pl.ds(i, chunk)]
            ds2[pl.ds(at + COLS, chunk)] = dy_ref[pl.ds(at, chunk)] + normalize_back(dn * tab(N2G), xhat, r)
            if own:
                add(N2G, eights(dn * xhat))
                add(N2S, eights(dn))

        sweep(size, chunk, leave)

    def feed_one(i, carry):
        feed(pl.multiple_of(own_off + i * TILE, 128), TILE, True)
        return carry

    lax.fori_loop(0, tokens // TILE, feed_one, 0)
    edge = HALO // 2
    feed(pl.multiple_of(tokens - core * (tokens - edge), edge), edge, False)
    rest = pl.multiple_of(COLS + (1 - core) * (tokens + edge), COLS)
    ds2[pl.ds(rest, edge)] = jnp.zeros((edge, D), F32)

    def is_own(row):
        return (row >= core * (HALO // COLS)) & (row < core * (HALO // COLS) + own_rows)

    def tap_sums(base, other, lanes):
        def source(r, views):
            mine = jnp.where(is_own(r), 1.0, 0.0)
            flags = (mine * above(first_row + r), mine, mine * below(first_row + r))
            for a in range(3):
                near = jnp.minimum(r + a, rows_wide + 1)
                held = other[pl.ds(pl.multiple_of(near * COLS, COLS), COLS), lanes]
                for b in range(3):
                    t = 8 * (base + 3 * a + b)
                    acc[t : t + 8, lanes] += flags[a] * eights(views[2 - b] * held)

        return source

    for lane in range(0, D, 128):
        lanes = pl.ds(lane, 128)

        def third(r, value):
            at = pl.multiple_of(r * COLS + COLS, COLS)
            mine = jnp.where(is_own(r), 1.0, 0.0)
            grad = value * tab_ref[BG : BG + 1, lanes] * slope[pl.ds(at, COLS), lanes]
            gp[pl.ds(at, COLS), lanes] = grad
            acc[8 * BG : 8 * BG + 8, lanes] += mine * eights(value * act[pl.ds(at, COLS), lanes])
            acc[8 * BS : 8 * BS + 8, lanes] += mine * eights(value)
            acc[8 * C1B : 8 * C1B + 8, lanes] += mine * eights(grad)

        convolve(
            ds2, K2R, True, tab_ref[SL : SL + 1, lanes], lane, third, tap_sums(K2R, mid, lanes)
        )

    for lane in range(0, D, 128):
        lanes = pl.ds(lane, 128)

        def fourth(r, value):
            slope[pl.ds(pl.multiple_of(r * COLS + COLS, COLS), COLS), lanes] = value

        convolve(gp, K1R, True, None, lane, fourth, tap_sums(K1R, li, lanes))

    dwp_ref[...] = jnp.zeros_like(dwp_ref)
    cross[...] = jnp.zeros_like(cross)

    def back(step, carry):
        here = pl.multiple_of(step * TILE, TILE)
        o = pl.multiple_of(own_off + here, 128)

        def chunk(i):
            at = pl.multiple_of(o + i, COLS)
            xhat, r = normalize(s1[pl.ds(at, COLS)])
            grad = slope[pl.ds(at + COLS, COLS)]
            above_grad = ds2[pl.ds(at + COLS, COLS)]
            result = above_grad + normalize_back(grad * tab(N3G), xhat, r)
            ds1_ref[pl.ds(pl.multiple_of(here + i, COLS), COLS)] = result
            z[pl.ds(i, COLS)] = result
            h, l = halves(tab(SA) * result)
            dzc[pl.ds(i, COLS), 0:D] = h
            dzc[pl.ds(i, COLS), D : 2 * D] = l
            dzc[pl.ds(i, COLS), 2 * D : 3 * D] = h
            add(N3G, eights(grad * xhat))
            add(N3S, eights(grad))
            add(SL, eights(above_grad * lo_[pl.ds(at + COLS, COLS)]))
            add(C2B, eights(above_grad))
            add(PB, eights(result))

        sweep(TILE, COLS, chunk)
        rows = pl.ds(0, TILE)
        dmx = dot_nt(dzc[rows], wph[...])
        dmx_ref[pl.ds(here, TILE)] = dmx
        h, l = halves(z[rows])
        dwp_ref[...] += dot_nn(side(mixed[pl.ds(o, TILE)].T), jnp.concatenate([h, h, l], axis=0))
        dmxt = side(dmx.T)
        for s, (lo, hi) in enumerate(spans):

            @pl.when((lo < o + TILE) & (hi > o))
            def _():
                vm = jnp.where(span_mask(o, TILE, lo, hi), v_ref[pl.ds(o, TILE)], 0.0)
                vh, vl = halves(vm)
                cross[s] += dot_nn(dmxt, jnp.concatenate([vh, vh, vl], axis=0))

        return carry

    lax.fori_loop(0, tokens // TILE, back, 0)
    for s in range(3):
        gprob_ref[s] = fold(cross[s])

    def total(r):
        return jnp.sum(acc[8 * r : 8 * r + 8], axis=0, keepdims=True)

    for r in (N3G, N3S, N2G, N2S, SL, SM, C1B, BG, BS, F2B, 40, 41, 42, 43):
        gtab_ref[r : r + 1] = total(r)
    for t in range(9):
        gtab_ref[K1R + t : K1R + t + 1] = total(K1R + t)
        gtab_ref[K2R + t : K2R + t + 1] = total(K2R + t) * tab(SL)
    gtab_ref[C2B : C2B + 1] = total(C2B) * tab(SL)
    gtab_ref[PB : PB + 1] = total(PB) * tab(SA)
    raw = dwp_ref[...]
    gtab_ref[SA : SA + 1] = jnp.sum(raw * wp_ref[...], axis=0, keepdims=True) + total(PB) * tab(PB)
    dwp_ref[...] = raw * tab(SA)
    for i in range(mlp // D):
        gtab_ref[F1B + i : F1B + i + 1] = jnp.sum(b1g_ref[:, i * D : i * D + D], axis=0, keepdims=True)


def middle(tall, temp, xe, dye, ve, sums, peer, wp, w1, w2, tab):
    wide = xe.shape[0]
    tokens = wide - HALO
    mlp = w1.shape[1]
    smem = pl.BlockSpec(memory_space=pltpu.SMEM)
    vmem = pl.BlockSpec(memory_space=pltpu.VMEM)

    def f(*shape):
        return jax.ShapeDtypeStruct(shape, F32)

    def s(*shape):
        return pltpu.VMEM(shape, F32)

    def b(*shape):
        return pltpu.VMEM(shape, BF)

    padded = s(wide + 2 * COLS, D)
    return pl.pallas_call(
        middle_kernel,
        out_shape=[
            f(tokens, D),
            f(tokens, D),
            f(tokens, D),
            f(D, D),
            f(D, mlp),
            f(D, mlp),
            f(TABLE, D),
            f(3, HD, D),
            f(3, HD, D),
            f(3, HD, D),
        ],
        in_specs=[smem, smem] + [vmem] * 9,
        out_specs=[vmem] * 10,
        scratch_shapes=[
            b(3 * D, D),
            b(D, 3 * D),
            b(3 * D, mlp),
            b(mlp, 3 * D),
            b(3, D, 3 * D),
            s(wide, D),
            s(wide, D),
            padded,
            padded,
            padded,
            padded,
            padded,
            s(wide, D),
            padded,
            padded,
            s(wide // 3, D),
            b(TILE, 3 * D),
            b(TILE, 3 * D),
            b(TILE, mlp),
            b(TILE, mlp),
            s(TILE, mlp),
            s(8, mlp),
            s(8, mlp),
            s(8 * TABLE, D),
            s(3, D, D),
        ],
        compiler_params=pltpu.CompilerParams(vmem_limit_bytes=60 << 20),
    )(tall, temp, xe, dye, ve, sums, peer, wp, w1, w2, tab)


def finish_kernel(
    tall_ref,
    temp_ref,
    x_ref,
    q_ref,
    k_ref,
    ds1_ref,
    dmx_ref,
    sums_ref,
    peer_ref,
    probs_ref,
    unit_ref,
    gprob_ref,
    gpeer_ref,
    w_ref,
    tab_ref,
    gtab_ref,
    dx_ref,
    dw_ref,
    otab_ref,
    wh,
    wl,
    pv,
    cv,
    ch,
    side_rows,
    acc,
    dqkv,
):
    step = pl.program_id(0)
    last = pl.num_programs(0) - 1
    core = lax.axis_index("rows")
    rows_all = 2 * pl.num_programs(0) * TILE // COLS
    spans = slots(tall_ref, core, core * (rows_all // 2), rows_all)
    start = step * TILE

    def tab(r):
        return tab_ref[r : r + 1]

    @pl.when(step == 0)
    def _():
        def part(o):
            h, l = halves(w_ref[pl.ds(o, 16)])
            wh[pl.ds(o, 16)] = h
            wl[pl.ds(o, 16)] = l

        sweep(D, 16, part)
        dw_ref[...] = jnp.zeros_like(dw_ref)
        acc[...] = jnp.zeros_like(acc)
        ones = group_ones()
        temp = head_row(temp_ref)
        heat = jnp.zeros((1, D), F32)
        for s in range(3):
            sums = sums_ref[s]
            grad = gprob_ref[s]
            if s == 2:
                sums = sums + peer_ref[...]
                grad = grad + gpeer_ref[...]
            inv_q = lax.rsqrt(sums[HD : HD + 1] + EPS)
            inv_k = lax.rsqrt(sums[HD + 1 : HD + 2] + EPS)
            probs = probs_ref[s]
            unit = unit_ref[s]
            scores = probs * (grad - group_sum(probs * grad, ones))
            part_heat = jnp.sum(scores * unit, axis=0, keepdims=True)
            heat = heat + (part_heat if s < 2 else jnp.where(core == 0, part_heat, 0.0))
            pull = temp * scores
            both = pull * unit
            side_rows[8 * s : 8 * s + 1] = fold_to_row(group_sum(both, ones)) * inv_q * inv_q
            side_rows[8 * s + 1 : 8 * s + 2] = jnp.sum(both, axis=0, keepdims=True) * inv_k * inv_k
            h, l = halves(unfold(pull * row_to_fold(inv_q, ones) * inv_k))
            cv[s, 0:D] = h
            cv[s, D : 2 * D] = h
            cv[s, 2 * D : 3 * D] = l
            ch[s, :, 0:D] = h
            ch[s, :, D : 2 * D] = h
            ch[s, :, 2 * D : 3 * D] = l
            h, l = halves(unfold(probs))
            pv[s, 0:D] = h
            pv[s, D : 2 * D] = h
            pv[s, 2 * D : 3 * D] = l
        otab_ref[...] = gtab_ref[...]
        otab_ref[44:45] = heat

    dqkv[...] = jnp.zeros_like(dqkv)
    for s, (lo, hi) in enumerate(spans):

        @pl.when((lo < start + TILE) & (hi > start))
        def _():
            mask = span_mask(start, TILE, lo, hi)
            qm = jnp.where(mask, q_ref[...], 0.0)
            km = jnp.where(mask, k_ref[...], 0.0)
            dm = jnp.where(mask, dmx_ref[...], 0.0)
            dqkv[:, 0:D] += dot_nt(side(km), ch[s]) - qm * side_rows[8 * s : 8 * s + 1]
            dqkv[:, D : 2 * D] += dot_nn(side(qm), cv[s]) - km * side_rows[8 * s + 1 : 8 * s + 2]
            dqkv[:, 2 * D : 3 * D] += dot_nn(side(dm), pv[s])

    h, l = halves(dqkv[...])
    dn = dot_nt(h, wh[...]) + (dot_nt(l, wh[...]) + dot_nt(h, wl[...]))
    xhat, r = normalize(x_ref[...])
    nt = side((xhat * tab(N1G) + tab(N1S)).T)
    dw_ref[...] += dot_nn(nt, jnp.concatenate([h, h, l], axis=0))
    dx_ref[...] = ds1_ref[...] + normalize_back(dn * tab(N1G), xhat, r)
    acc[0:8] += eights(dn * xhat)
    acc[8:16] += eights(dn)
    for i in range(3):
        acc[16 + 8 * i : 24 + 8 * i] += eights(dqkv[:, i * D : i * D + D])

    @pl.when(step == last)
    def _():
        for i, r in enumerate((N1G, N1S, QB, KB, VB)):
            otab_ref[r : r + 1] = jnp.sum(acc[8 * i : 8 * i + 8], axis=0, keepdims=True)


def finish(tall, temp, x, q, k, ds1, dmx, sums, peer, probs, unit, gprob, gpeer, w, tab, gtab):
    tokens = x.shape[0]
    smem = pl.BlockSpec(memory_space=pltpu.SMEM)
    row = pl.BlockSpec((TILE, D), lambda i: (i, 0))

    def whole(v):
        return pl.BlockSpec(v.shape, lambda i: (0,) * v.ndim)

    fixed = (sums, peer, probs, unit, gprob, gpeer, w, tab, gtab)
    return pl.pallas_call(
        finish_kernel,
        grid=(tokens // TILE,),
        out_shape=[
            jax.ShapeDtypeStruct((tokens, D), F32),
            jax.ShapeDtypeStruct((D, 3 * D), F32),
            jax.ShapeDtypeStruct((TABLE, D), F32),
        ],
        in_specs=[smem, smem] + [row] * 5 + [whole(v) for v in fixed],
        out_specs=[
            row,
            pl.BlockSpec((D, 3 * D), lambda i: (0, 0)),
            pl.BlockSpec((TABLE, D), lambda i: (0, 0)),
        ],
        scratch_shapes=[
            pltpu.VMEM((D, 3 * D), BF),
            pltpu.VMEM((D, 3 * D), BF),
            pltpu.VMEM((3, 3 * D, D), BF),
            pltpu.VMEM((3, 3 * D, D), BF),
            pltpu.VMEM((3, D, 3 * D), BF),
            pltpu.VMEM((24, D), F32),
            pltpu.VMEM((40, D), F32),
            pltpu.VMEM((TILE, 3 * D), F32),
        ],
        compiler_params=pltpu.CompilerParams(vmem_limit_bytes=40 << 20),
    )(tall, temp, x, q, k, ds1, dmx, *fixed)


def orth_kernel(x_ref, o_ref, xs):
    def squares(v):
        return jnp.sum(jnp.sum(v * v, axis=0, keepdims=True), axis=1, keepdims=True)

    groups = ((0,), (1,), (2, 3, 4, 5))
    for g in groups:
        norm = squares(x_ref[g[0]])
        for b in g[1:]:
            norm = norm + squares(x_ref[b])
        inv = 1.0 / (jnp.sqrt(norm) + 1e-07)
        for b in g:
            xs[b] = x_ref[b] * inv

    def step(i, carry):
        for g in groups:
            left, right = [], []
            for b in g:
                h, l = halves(xs[b])
                left += [h, l, h]
                right += [h, h, l]
            gram = dot_nt(jnp.concatenate(left, axis=1), jnp.concatenate(right, axis=1))
            h, l = halves(gram)
            square = dot_nn(jnp.concatenate([h, l, h], axis=1), jnp.concatenate([h, h, l], axis=0))
            poly = side(-4.775 * gram + 2.0315 * square)
            for b in g:
                h, l = halves(xs[b])
                xs[b] = 3.4445 * xs[b] + dot_nn(poly, jnp.concatenate([h, h, l], axis=0))
        return carry

    lax.fori_loop(0, 5, step, 0)
    o_ref[...] = xs[...]


def orth_half(x):
    vmem = pl.BlockSpec(memory_space=pltpu.VMEM)
    return pl.pallas_call(
        orth_kernel,
        out_shape=jax.ShapeDtypeStruct(x.shape, F32),
        in_specs=[vmem],
        out_specs=vmem,
        scratch_shapes=[pltpu.VMEM(x.shape, F32)],
        compiler_params=pltpu.CompilerParams(vmem_limit_bytes=48 << 20),
    )(x)


def moment_step(current, one, two, gradient):
    first = BETA1 * one + (1.0 - BETA1) * gradient
    second = BETA2 * two + (1.0 - BETA2) * gradient * gradient
    fix_one = 1.0 - BETA1**STEP
    fix_two = 1.0 - BETA2**STEP
    updated = current - ADAM_RATE * (first / fix_one) / (jnp.sqrt(second / fix_two) + ADAM_FLOOR)
    return first, second, updated


def on_device(
    x4, dy4, tall, wqkv, wp, w1, w2, mqkv, mp, m1, m2, tab, tab_one, tab_two, temp, temp_one, temp_two
):
    shape = x4.shape
    tokens = shape[1] * shape[2]
    x = x4.reshape(tokens, D)
    dy = dy4.reshape(tokens, D)
    core = lax.axis_index("rows")
    q, k, v, sums = project(tall, x, wqkv, tab)
    xe, dye, ve, peer = widen(x, dy, v, sums)
    out, ds1, dmx, gp_, g1, g2t, gtab, probs, unit, gprob = middle(
        tall, temp, xe, dye, ve, sums, peer, wp, w1, w2, tab
    )
    gpeer = swap(gprob[2], 1)
    dx, gq, gtab = finish(
        tall, temp, x, q, k, ds1, dmx, sums, peer, probs, unit, gprob, gpeer, wqkv, tab, gtab
    )
    gq, gp_, g1, g2t, gtab = lax.psum((gq, gp_, g1, g2t, gtab), ("rows", "canvas"))
    g2 = g2t.T
    nq = MUON_KEEP * mqkv + gq
    np_ = MUON_KEEP * mp + gp_
    n1 = MUON_KEEP * m1 + g1
    n2 = MUON_KEEP * m2 + g2

    def cut(v):
        return [v[:, i * D : i * D + D] for i in range(v.shape[1] // D)]

    blocks = cut(nq)
    lower = jnp.stack(blocks[0:2] + cut(n1))
    upper = jnp.stack([blocks[2], np_] + cut(n2.T))
    mine = orth_half(jnp.where(core == 0, lower, upper))
    other = swap(mine, 2)
    lower = jnp.where(core == 0, mine, other)
    upper = jnp.where(core == 0, other, mine)

    def muon(w, orth, large):
        return w * (1.0 - MUON_RATE * DECAY) - MUON_RATE * 0.2 * math.sqrt(large) * orth

    wide = w1.shape[1]
    new_qkv = muon(wqkv, jnp.concatenate([lower[0], lower[1], upper[0]], axis=1), D)
    new_p = muon(wp, upper[1], D)
    new_1 = muon(w1, jnp.concatenate([lower[i] for i in range(2, 6)], axis=1), wide)
    new_2 = muon(w2, jnp.concatenate([upper[i].T for i in range(2, 6)], axis=0), wide)
    small = moment_step(tab, tab_one, tab_two, gtab[0:SMALL])
    heat = jnp.sum(gtab[44].reshape(HEADS, HD), axis=1)
    warm = moment_step(temp, temp_one, temp_two, heat)
    everything = tokens * D * lax.axis_size("rows") * lax.axis_size("canvas")
    rms = jnp.sqrt(jnp.sum(gtab[40:44], axis=1) / everything)
    return (
        out.reshape(shape),
        dx.reshape(shape),
        gq,
        gp_,
        g1,
        g2,
        nq,
        np_,
        n1,
        n2,
        new_qkv,
        new_p,
        new_1,
        new_2,
        new_qkv.astype(BF),
        new_p.astype(BF),
        new_1.astype(BF),
        new_2.astype(BF),
        small[0],
        small[1],
        small[2],
        warm[0],
        warm[1],
        warm[2],
        rms,
    )


def solution(mesh):
    split = P("canvas", "rows", None, None)
    return jax.shard_map(
        on_device,
        mesh=mesh,
        in_specs=(split, split, P("canvas", None)) + (P(),) * 14,
        out_specs=(split, split) + (P(),) * 23,
        check_vma=False,
    )
```

```python
import math

import jax
import jax.numpy as jnp
from jax import lax
from jax.experimental import pallas as pl
from jax.experimental.pallas import tpu as pltpu
from jax.sharding import PartitionSpec as P

BF = jnp.bfloat16
F32 = jnp.float32
MESH_ID = pl.DeviceIdType.MESH

EPS = 1e-06
ROOT_HALF = 1.0 / math.sqrt(2.0)
ROOT_TWOPI = 1.0 / math.sqrt(2.0 * math.pi)
STEP = 10
MUON_RATE = 0.2
MUON_KEEP = 0.95
DECAY = 0.01
ADAM_RATE = 0.2
BETA1 = 0.9
BETA2 = 0.95
ADAM_FLOOR = 1e-08

HEADS = 8
HD = 48
D = HEADS * HD
COLS = 32
HALO = 4 * COLS
TILE = 256

N1G, N1S, N3G, N3S, N2G, N2S, SA, SL, SM, QB, KB, VB, PB, C1B, BG, BS, C2B, F2B = range(18)
F1B, K1R, K2R = 18, 22, 31
SMALL = 40
TABLE = 48


def halves(v):
    hi = v.astype(BF)
    return hi, (v - hi.astype(F32)).astype(BF)


def side(v):
    h, l = halves(v)
    return jnp.concatenate([h, l, h], axis=1)


def dot_nn(a, b):
    return lax.dot_general(a, b, (((1,), (0,)), ((), ())), preferred_element_type=F32)


def dot_nt(a, b):
    return lax.dot_general(a, b, (((1,), (1,)), ((), ())), preferred_element_type=F32)


def normalize(v):
    mean = jnp.mean(v, axis=1, keepdims=True)
    c = v - mean
    r = lax.rsqrt(jnp.mean(c * c, axis=1, keepdims=True) + EPS)
    return c * r, r


def normalize_back(e, xhat, r):
    return r * (
        e - jnp.mean(e, axis=1, keepdims=True) - xhat * jnp.mean(e * xhat, axis=1, keepdims=True)
    )


def gelu_parts(v):
    phi = 0.5 * (1.0 + lax.erf(v * ROOT_HALF))
    return v * phi, phi + v * jnp.exp(-0.5 * v * v) * ROOT_TWOPI


def eights(v):
    total = v[0:8]
    for i in range(8, v.shape[0], 8):
        total = total + v[i : i + 8]
    return total


def sweep(count, size, body):
    def one(i, carry):
        body(pl.multiple_of(i * size, size))
        return carry

    lax.fori_loop(0, count // size, one, 0)


def image_ends(tall_ref):
    e0 = tall_ref[0, 0]
    e1 = e0 + tall_ref[0, 1]
    return e0, e1, e1 + tall_ref[0, 2]


def slots(tall_ref, core, first_row, rows_all):
    e0, e1, e2 = image_ends(tall_ref)
    low = (jnp.where(core == 0, 0, e2), jnp.where(core == 0, e0, 0), e1)
    high = (jnp.where(core == 0, e0, rows_all), jnp.where(core == 0, e1, 0), e2)
    return [((a - first_row) * COLS, (b - first_row) * COLS) for a, b in zip(low, high)]


def span_mask(start, rows, lo, hi):
    token = start + lax.broadcasted_iota(jnp.int32, (rows, D), 0)
    return (token >= lo) & (token < hi)


def lane_head():
    return lax.broadcasted_iota(jnp.int32, (HD, D), 1) // HD


def lane_slot():
    return lax.broadcasted_iota(jnp.int32, (HD, D), 1) % HD


def fold(full):
    head = lane_head()
    total = jnp.where(head == 0, full[0:HD], 0.0)
    for h in range(1, HEADS):
        total = total + jnp.where(head == h, full[h * HD : h * HD + HD], 0.0)
    return total


def unfold(small):
    head = lane_head()
    return jnp.concatenate([jnp.where(head == h, small, 0.0) for h in range(HEADS)], axis=0)


def group_ones():
    a = lax.broadcasted_iota(jnp.int32, (D, D), 0) // HD
    b = lax.broadcasted_iota(jnp.int32, (D, D), 1) // HD
    return jnp.where(a == b, 1.0, 0.0).astype(BF)


def group_sum(v, ones):
    h = v.astype(BF)
    rest = v - h.astype(F32)
    m = rest.astype(BF)
    l = (rest - m.astype(F32)).astype(BF)
    return dot_nn(h, ones) + (dot_nn(m, ones) + dot_nn(l, ones))


def row_to_fold(row, ones):
    slot = lax.broadcasted_iota(jnp.int32, (HD, D), 0)
    return group_sum(jnp.where(lane_slot() == slot, jnp.broadcast_to(row, (HD, D)), 0.0), ones)


def fold_to_row(small):
    slot = lax.broadcasted_iota(jnp.int32, (HD, D), 0)
    return jnp.sum(jnp.where(lane_slot() == slot, small, 0.0), axis=0, keepdims=True)


def head_row(temp_ref):
    head = lax.broadcasted_iota(jnp.int32, (1, D), 1) // HD
    row = jnp.where(head == 0, temp_ref[0], 0.0)
    for h in range(1, HEADS):
        row = row + jnp.where(head == h, temp_ref[h], 0.0)
    return row


def project_kernel(tall_ref, x_ref, w_ref, tab_ref, q_ref, k_ref, v_ref, sums_ref, wcat, cross):
    step = pl.program_id(0)
    core = lax.axis_index("rows")
    rows_all = 2 * pl.num_programs(0) * TILE // COLS
    spans = slots(tall_ref, core, core * (rows_all // 2), rows_all)
    start = step * TILE

    @pl.when(step == 0)
    def _():
        def part(o):
            h, l = halves(w_ref[pl.ds(o, 16)])
            wcat[pl.ds(o, 16)] = h
            wcat[pl.ds(D + o, 16)] = h
            wcat[pl.ds(2 * D + o, 16)] = l

        sweep(D, 16, part)
        cross[...] = jnp.zeros_like(cross)
        sums_ref[...] = jnp.zeros_like(sums_ref)

    xhat, _ = normalize(x_ref[...])
    lhs = side(xhat * tab_ref[N1G : N1G + 1] + tab_ref[N1S : N1S + 1])
    q = dot_nn(lhs, wcat[:, 0:D]) + tab_ref[QB : QB + 1]
    q_ref[...] = q
    k = dot_nn(lhs, wcat[:, D : 2 * D]) + tab_ref[KB : KB + 1]
    k_ref[...] = k
    v_ref[...] = dot_nn(lhs, wcat[:, 2 * D : 3 * D]) + tab_ref[VB : VB + 1]
    qt = side(q.T)
    for s, (lo, hi) in enumerate(spans):

        @pl.when((lo < start + TILE) & (hi > start))
        def _():
            mask = span_mask(start, TILE, lo, hi)
            kh, kl = halves(jnp.where(mask, k_ref[...], 0.0))
            cross[s] += dot_nn(qt, jnp.concatenate([kh, kh, kl], axis=0))
            qm = jnp.where(mask, q_ref[...], 0.0)
            km = jnp.where(mask, k_ref[...], 0.0)
            sums_ref[s, HD : HD + 1] += jnp.sum(qm * qm, axis=0, keepdims=True)
            sums_ref[s, HD + 1 : HD + 2] += jnp.sum(km * km, axis=0, keepdims=True)

    @pl.when(step == pl.num_programs(0) - 1)
    def _():
        for s in range(3):
            sums_ref[s, 0:HD] = fold(cross[s])


def project(tall, x, w, tab):
    tokens = x.shape[0]
    row = pl.BlockSpec((TILE, D), lambda i: (i, 0))
    return pl.pallas_call(
        project_kernel,
        grid=(tokens // TILE,),
        out_shape=[jax.ShapeDtypeStruct((tokens, D), F32)] * 3
        + [jax.ShapeDtypeStruct((3, HD + 8, D), F32)],
        in_specs=[
            pl.BlockSpec(memory_space=pltpu.SMEM),
            row,
            pl.BlockSpec((D, 3 * D), lambda i: (0, 0)),
            pl.BlockSpec((SMALL, D), lambda i: (0, 0)),
        ],
        out_specs=[row, row, row, pl.BlockSpec((3, HD + 8, D), lambda i: (0, 0, 0))],
        scratch_shapes=[pltpu.VMEM((3 * D, 3 * D), BF), pltpu.VMEM((3, D, D), F32)],
        compiler_params=pltpu.CompilerParams(vmem_limit_bytes=40 << 20),
    )(tall, x, w, tab)


def widen_kernel(x_ref, dy_ref, v_ref, sums_ref, halo_ref, peer_ref, send_sem, recv_sem):
    core = lax.axis_index("rows")
    tokens = x_ref.shape[0]
    barrier = pltpu.get_barrier_semaphore()
    pl.semaphore_signal(barrier, inc=1, device_id={"rows": 1 - core}, device_id_type=MESH_ID)
    pl.semaphore_wait(barrier, 1)
    edge = pl.ds(pl.multiple_of((1 - core) * (tokens - HALO), HALO), HALO)
    pairs = [(src.at[edge], halo_ref.at[i]) for i, src in enumerate((x_ref, dy_ref, v_ref))]
    pairs.append((sums_ref.at[2], peer_ref))
    copies = []
    for i, (src, dst) in enumerate(pairs):
        copies.append(
            pltpu.make_async_remote_copy(
                src_ref=src,
                dst_ref=dst,
                send_sem=send_sem.at[i],
                recv_sem=recv_sem.at[i],
                device_id={"rows": 1 - core},
                device_id_type=MESH_ID,
            )
        )
        copies[-1].start()
    for copy in copies:
        copy.wait()


def widen(x, dy, v, sums):
    anywhere = pl.BlockSpec(memory_space=pl.ANY)
    return pl.pallas_call(
        widen_kernel,
        out_shape=[
            jax.ShapeDtypeStruct((3, HALO, D), F32),
            jax.ShapeDtypeStruct(sums.shape[1:], F32),
        ],
        in_specs=[anywhere] * 4,
        out_specs=[anywhere] * 2,
        scratch_shapes=[pltpu.SemaphoreType.DMA((4,)), pltpu.SemaphoreType.DMA((4,))],
        compiler_params=pltpu.CompilerParams(collective_id=0, has_side_effects=True),
    )(x, dy, v, sums)


def swap_kernel(src, dst, send_sem, recv_sem):
    core = lax.axis_index("rows")
    barrier = pltpu.get_barrier_semaphore()
    pl.semaphore_signal(barrier, inc=1, device_id={"rows": 1 - core}, device_id_type=MESH_ID)
    pl.semaphore_wait(barrier, 1)
    copy = pltpu.make_async_remote_copy(
        src_ref=src,
        dst_ref=dst,
        send_sem=send_sem,
        recv_sem=recv_sem,
        device_id={"rows": 1 - core},
        device_id_type=MESH_ID,
    )
    copy.start()
    copy.wait()


def swap(v, number):
    return pl.pallas_call(
        swap_kernel,
        out_shape=jax.ShapeDtypeStruct(v.shape, F32),
        in_specs=[pl.BlockSpec(memory_space=pl.ANY)],
        out_specs=pl.BlockSpec(memory_space=pl.ANY),
        scratch_shapes=[pltpu.SemaphoreType.DMA, pltpu.SemaphoreType.DMA],
        compiler_params=pltpu.CompilerParams(collective_id=number, has_side_effects=True),
    )(v)


def shifted(u, col):
    left = jnp.where(col == 0, 0.0, pltpu.roll(u, 1, 0))
    right = jnp.where(col == COLS - 1, 0.0, pltpu.roll(u, COLS - 1, 0))
    return left, u, right


def row_flags(tall_ref, rows_all):
    ends = image_ends(tall_ref)

    def above(row):
        first = (row == 0) | (row == ends[0]) | (row == ends[1]) | (row == ends[2])
        return jnp.where(first, 0.0, 1.0)

    def below(row):
        return jnp.where(row + 1 == rows_all, 0.0, above(row + 1))

    return above, below


def middle_kernel(
    tall_ref,
    temp_ref,
    x_hbm,
    dy_hbm,
    v_hbm,
    halo_hbm,
    sums_ref,
    peer_ref,
    wp_ref,
    w1_ref,
    w2_ref,
    tab_ref,
    out_ref,
    ds1_ref,
    dmx_ref,
    dwp_ref,
    dw_ref,
    gtab_ref,
    probs_ref,
    unit_ref,
    gprob_ref,
    wpv,
    wph,
    w1c,
    w2c,
    pcat,
    mixed,
    s1,
    li,
    act,
    slope,
    mid,
    lo_,
    s2,
    ds2,
    gp,
    z,
    n2c,
    dzc,
    hid_h,
    hid_l,
    hslope,
    b1_ref,
    b1g_ref,
    acc,
    cross,
    x_ref,
    dy_ref,
    v_ref,
    load_sem,
):
    core = lax.axis_index("rows")
    wide = x_ref.shape[0]
    tokens = wide - HALO
    dw1_ref, dw2_ref = dw_ref.at[0], dw_ref.at[1]
    loads = []
    for i, (src, dst) in enumerate(((x_hbm, x_ref), (dy_hbm, dy_ref), (v_hbm, v_ref))):
        own = pl.ds(pl.multiple_of(core * HALO, HALO), tokens)
        far = pl.ds(pl.multiple_of((1 - core) * tokens, HALO), HALO)
        loads.append(pltpu.make_async_copy(src, dst.at[own], load_sem.at[2 * i]))
        loads.append(pltpu.make_async_copy(halo_hbm.at[i], dst.at[far], load_sem.at[2 * i + 1]))
    for load in loads:
        load.start()
    own_rows = tokens // COLS
    rows_wide = wide // COLS
    rows_all = 2 * own_rows
    first_row = core * (own_rows - HALO // COLS)
    own_off = pl.multiple_of(core * HALO, HALO)
    mlp = w1_ref.shape[1]
    spans = slots(tall_ref, core, first_row, rows_all)
    above, below = row_flags(tall_ref, rows_all)

    def tab(r):
        return tab_ref[r : r + 1]

    def part_p(o):
        h, l = halves(wp_ref[pl.ds(o, 16)])
        wpv[pl.ds(o, 16)] = h
        wpv[pl.ds(D + o, 16)] = h
        wpv[pl.ds(2 * D + o, 16)] = l
        wph[pl.ds(o, 16), 0:D] = h
        wph[pl.ds(o, 16), D : 2 * D] = h
        wph[pl.ds(o, 16), 2 * D : 3 * D] = l

    sweep(D, 16, part_p)

    def part_1(o):
        h, l = halves(w1_ref[pl.ds(o, 16)])
        w1c[pl.ds(o, 16)] = h
        w1c[pl.ds(D + o, 16)] = h
        w1c[pl.ds(2 * D + o, 16)] = l

    sweep(D, 16, part_1)

    def part_2(o):
        h, l = halves(w2_ref[pl.ds(o, 32)])
        w2c[pl.ds(o, 32), 0:D] = h
        w2c[pl.ds(o, 32), D : 2 * D] = h
        w2c[pl.ds(o, 32), 2 * D : 3 * D] = l

    sweep(mlp, 32, part_2)

    ones = group_ones()
    temp = head_row(temp_ref)
    for s in range(3):
        sums = sums_ref[s]
        if s == 2:
            sums = sums + peer_ref[...]
        inv_q = lax.rsqrt(sums[HD : HD + 1] + EPS)
        inv_k = lax.rsqrt(sums[HD + 1 : HD + 2] + EPS)
        unit = sums[0:HD] * row_to_fold(inv_q, ones) * inv_k
        unit_ref[s] = unit
        weight = jnp.exp(temp * unit)
        probs = weight / group_sum(weight, ones)
        probs_ref[s] = probs
        h, l = halves(unfold(probs))
        pcat[s, :, 0:D] = h
        pcat[s, :, D : 2 * D] = h
        pcat[s, :, 2 * D : 3 * D] = l

    acc[...] = jnp.zeros_like(acc)
    gtab_ref[...] = jnp.zeros_like(gtab_ref)

    def add(r, v):
        acc[8 * r : 8 * r + 8] += v

    for load in loads:
        load.wait()

    def attend(o):
        size = wide // 3
        mixed[pl.ds(o, size)] = jnp.zeros((size, D), F32)
        for s, (lo, hi) in enumerate(spans):

            @pl.when((lo < o + size) & (hi > o))
            def _():
                vm = jnp.where(span_mask(o, size, lo, hi), v_ref[pl.ds(o, size)], 0.0)
                mixed[pl.ds(o, size)] += dot_nt(side(vm), pcat[s])

        z[...] = dot_nn(side(mixed[pl.ds(o, size)]), wpv[...]) + tab(PB)

        def finish(i):
            branch = tab(SA) * z[pl.ds(i, COLS)]
            at = pl.multiple_of(o + i, COLS)
            stream = x_ref[pl.ds(at, COLS)] + branch
            s1[pl.ds(at, COLS)] = stream
            xhat, _ = normalize(stream)
            li[pl.ds(at + COLS, COLS)] = xhat * tab(N3G) + tab(N3S)
            mine = jnp.where((at >= own_off) & (at < own_off + tokens), 1.0, 0.0)
            add(41, mine * eights(branch * branch))

        sweep(size, COLS, finish)

    sweep(wide, wide // 3, attend)

    pad = jnp.zeros((COLS, D), F32)
    for buf in (li, mid, gp, ds2):
        buf[0:COLS] = pad
        buf[wide + COLS : wide + 2 * COLS] = pad

    def convolve(src, base, flip, scale_row, lane, visit, source=None):
        lanes = pl.ds(lane, 128)
        taps = [tab_ref[base + t : base + t + 1, lanes] for t in range(9)]
        if flip:
            taps = taps[::-1]
        if scale_row is not None:
            taps = [t * scale_row for t in taps]
        taps = [jnp.broadcast_to(t, (COLS, 128)) for t in taps]
        col = lax.broadcasted_iota(jnp.int32, (COLS, 128), 0)
        zero = jnp.zeros((COLS, 128), F32)

        def one(r, carry):
            partial, from_above = carry
            at = pl.multiple_of(r * COLS + COLS, COLS)
            views = shifted(src[pl.ds(at, COLS), lanes], col)
            rows = [
                views[0] * taps[3 * a] + views[1] * taps[3 * a + 1] + views[2] * taps[3 * a + 2]
                for a in range(3)
            ]
            visit(r - 1, partial + below(first_row + r - 1) * rows[2])
            if source is not None:
                source(r, views)
            return rows[1] + above(first_row + r) * from_above, rows[0]

        lax.fori_loop(0, rows_wide + 1, one, (zero, zero))

    for lane in range(0, D, 128):
        lanes = pl.ds(lane, 128)

        def first(r, value):
            at = pl.multiple_of(r * COLS + COLS, COLS)
            a, s = gelu_parts(value + tab_ref[C1B : C1B + 1, lanes])
            act[pl.ds(at, COLS), lanes] = a
            slope[pl.ds(at, COLS), lanes] = s
            mid[pl.ds(at, COLS), lanes] = a * tab_ref[BG : BG + 1, lanes] + tab_ref[BS : BS + 1, lanes]

        convolve(li, K1R, False, None, lane, first)

    for lane in range(0, D, 128):
        lanes = pl.ds(lane, 128)

        def second(r, value):
            at = pl.multiple_of(r * COLS + COLS, COLS)
            value = value + tab_ref[C2B : C2B + 1, lanes]
            lo_[pl.ds(at, COLS), lanes] = value

        convolve(mid, K2R, False, None, lane, second)

    def join(o):
        branch = tab(SL) * lo_[pl.ds(o + COLS, COLS)]
        s2[pl.ds(o, COLS)] = s1[pl.ds(o, COLS)] + branch
        mine = jnp.where((o >= own_off) & (o < own_off + tokens), 1.0, 0.0)
        add(42, mine * eights(branch * branch))

    sweep(wide, COLS, join)

    dw1_ref[...] = jnp.zeros_like(dw1_ref)
    dw2_ref[...] = jnp.zeros_like(dw2_ref)
    b1g_ref[...] = jnp.zeros_like(b1g_ref)
    for i in range(mlp // D):
        b1_ref[0:1, i * D : i * D + D] = tab(F1B + i)

    def feed(o, size, own):
        rows = pl.ds(0, size)
        chunk = 16

        def enter(i):
            xhat, _ = normalize(s2[pl.ds(pl.multiple_of(o + i, chunk), chunk)])
            n2 = xhat * tab(N2G) + tab(N2S)
            h, l = halves(n2)
            n2c[pl.ds(i, chunk), 0:D] = h
            n2c[pl.ds(i, chunk), D : 2 * D] = l
            n2c[pl.ds(i, chunk), 2 * D : 3 * D] = h

        sweep(size, chunk, enter)

        def up(j):
            lanes = pl.ds(j, 256)
            pre = dot_nn(n2c[rows], w1c[:, lanes]) + b1_ref[0:1, lanes]
            a, s = gelu_parts(pre)
            h, l = halves(a)
            hid_h[rows, lanes] = h
            hid_l[rows, lanes] = l
            hslope[rows, lanes] = s

        sweep(mlp, 256, up)
        w2h, w2l = w2c[:, 0:D], w2c[:, 2 * D : 3 * D]
        z[rows] = (
            dot_nn(hid_h[rows], w2h) + (dot_nn(hid_l[rows], w2h) + dot_nn(hid_h[rows], w2l))
        ) + tab(F2B)

        def turn(i):
            at = pl.multiple_of(o + i, chunk)
            dy = dy_ref[pl.ds(at, chunk)]
            dz = tab(SM) * dy
            h, l = halves(dz)
            dzc[pl.ds(i, chunk), 0:D] = h
            dzc[pl.ds(i, chunk), D : 2 * D] = l
            dzc[pl.ds(i, chunk), 2 * D : 3 * D] = h
            if own:
                raw = z[pl.ds(i, chunk)]
                branch = tab(SM) * raw
                result = s2[pl.ds(at, chunk)] + branch
                out_ref[pl.ds(pl.multiple_of(at - own_off, chunk), chunk)] = result
                add(40, eights(result * result))
                add(43, eights(branch * branch))
                add(SM, eights(dy * raw))
                add(F2B, eights(dz))

        sweep(size, chunk, turn)
        if own:
            nt = n2c[rows, 0:D].T, n2c[rows, D : 2 * D].T
            dt = dzc[rows, 0:D].T, dzc[rows, D : 2 * D].T

        def down(j):
            lanes = pl.ds(j, 256)
            dpre = dot_nt(dzc[rows], w2c[lanes, :]) * hslope[rows, lanes]
            h, l = halves(dpre)
            if own:
                b1g_ref[:, lanes] += eights(dpre)
                dw1_ref[:, lanes] += dot_nn(nt[0], h) + (dot_nn(nt[1], h) + dot_nn(nt[0], l))
                hh, hl = hid_h[rows, lanes], hid_l[rows, lanes]
                dw2_ref[:, lanes] += dot_nn(dt[0], hh) + (dot_nn(dt[1], hh) + dot_nn(dt[0], hl))
            hid_h[rows, lanes] = h
            hid_l[rows, lanes] = l

        sweep(mlp, 256, down)
        w1h, w1l = w1c[0:D], w1c[2 * D : 3 * D]
        z[rows] = dot_nt(hid_h[rows], w1h) + (
            dot_nt(hid_l[rows], w1h) + dot_nt(hid_h[rows], w1l)
        )

        def leave(i):
            at = pl.multiple_of(o + i, chunk)
            xhat, r = normalize(s2[pl.ds(at, chunk)])
            dn = z[pl.ds(i, chunk)]
            ds2[pl.ds(at + COLS, chunk)] = dy_ref[pl.ds(at, chunk)] + normalize_back(dn * tab(N2G), xhat, r)
            if own:
                add(N2G, eights(dn * xhat))
                add(N2S, eights(dn))

        sweep(size, chunk, leave)

    def feed_one(i, carry):
        feed(pl.multiple_of(own_off + i * TILE, 128), TILE, True)
        return carry

    lax.fori_loop(0, tokens // TILE, feed_one, 0)
    edge = HALO // 2
    feed(pl.multiple_of(tokens - core * (tokens - edge), edge), edge, False)
    rest = pl.multiple_of(COLS + (1 - core) * (tokens + edge), COLS)
    ds2[pl.ds(rest, edge)] = jnp.zeros((edge, D), F32)

    def is_own(row):
        return (row >= core * (HALO // COLS)) & (row < core * (HALO // COLS) + own_rows)

    def tap_sums(base, other, lanes):
        def source(r, views):
            mine = jnp.where(is_own(r), 1.0, 0.0)
            flags = (mine * above(first_row + r), mine, mine * below(first_row + r))
            for a in range(3):
                near = jnp.minimum(r + a, rows_wide + 1)
                held = other[pl.ds(pl.multiple_of(near * COLS, COLS), COLS), lanes]
                for b in range(3):
                    t = 8 * (base + 3 * a + b)
                    acc[t : t + 8, lanes] += flags[a] * eights(views[2 - b] * held)

        return source

    for lane in range(0, D, 128):
        lanes = pl.ds(lane, 128)

        def third(r, value):
            at = pl.multiple_of(r * COLS + COLS, COLS)
            mine = jnp.where(is_own(r), 1.0, 0.0)
            grad = value * tab_ref[BG : BG + 1, lanes] * slope[pl.ds(at, COLS), lanes]
            gp[pl.ds(at, COLS), lanes] = grad
            acc[8 * BG : 8 * BG + 8, lanes] += mine * eights(value * act[pl.ds(at, COLS), lanes])
            acc[8 * BS : 8 * BS + 8, lanes] += mine * eights(value)
            acc[8 * C1B : 8 * C1B + 8, lanes] += mine * eights(grad)

        convolve(
            ds2, K2R, True, tab_ref[SL : SL + 1, lanes], lane, third, tap_sums(K2R, mid, lanes)
        )

    for lane in range(0, D, 128):
        lanes = pl.ds(lane, 128)

        def fourth(r, value):
            slope[pl.ds(pl.multiple_of(r * COLS + COLS, COLS), COLS), lanes] = value

        convolve(gp, K1R, True, None, lane, fourth, tap_sums(K1R, li, lanes))

    dwp_ref[...] = jnp.zeros_like(dwp_ref)
    cross[...] = jnp.zeros_like(cross)

    def back(step, carry):
        here = pl.multiple_of(step * TILE, TILE)
        o = pl.multiple_of(own_off + here, 128)

        def chunk(i):
            at = pl.multiple_of(o + i, COLS)
            xhat, r = normalize(s1[pl.ds(at, COLS)])
            grad = slope[pl.ds(at + COLS, COLS)]
            above_grad = ds2[pl.ds(at + COLS, COLS)]
            result = above_grad + normalize_back(grad * tab(N3G), xhat, r)
            ds1_ref[pl.ds(pl.multiple_of(here + i, COLS), COLS)] = result
            z[pl.ds(i, COLS)] = result
            h, l = halves(tab(SA) * result)
            dzc[pl.ds(i, COLS), 0:D] = h
            dzc[pl.ds(i, COLS), D : 2 * D] = l
            dzc[pl.ds(i, COLS), 2 * D : 3 * D] = h
            add(N3G, eights(grad * xhat))
            add(N3S, eights(grad))
            add(SL, eights(above_grad * lo_[pl.ds(at + COLS, COLS)]))
            add(C2B, eights(above_grad))
            add(PB, eights(result))

        sweep(TILE, COLS, chunk)
        rows = pl.ds(0, TILE)
        dmx = dot_nt(dzc[rows], wph[...])
        dmx_ref[pl.ds(here, TILE)] = dmx
        h, l = halves(z[rows])
        dwp_ref[...] += dot_nn(side(mixed[pl.ds(o, TILE)].T), jnp.concatenate([h, h, l], axis=0))
        dmxt = side(dmx.T)
        for s, (lo, hi) in enumerate(spans):

            @pl.when((lo < o + TILE) & (hi > o))
            def _():
                vm = jnp.where(span_mask(o, TILE, lo, hi), v_ref[pl.ds(o, TILE)], 0.0)
                vh, vl = halves(vm)
                cross[s] += dot_nn(dmxt, jnp.concatenate([vh, vh, vl], axis=0))

        return carry

    lax.fori_loop(0, tokens // TILE, back, 0)
    for s in range(3):
        gprob_ref[s] = fold(cross[s])

    def total(r):
        return jnp.sum(acc[8 * r : 8 * r + 8], axis=0, keepdims=True)

    for r in (N3G, N3S, N2G, N2S, SL, SM, C1B, BG, BS, F2B, 40, 41, 42, 43):
        gtab_ref[r : r + 1] = total(r)
    for t in range(9):
        gtab_ref[K1R + t : K1R + t + 1] = total(K1R + t)
        gtab_ref[K2R + t : K2R + t + 1] = total(K2R + t) * tab(SL)
    gtab_ref[C2B : C2B + 1] = total(C2B) * tab(SL)
    gtab_ref[PB : PB + 1] = total(PB) * tab(SA)
    raw = dwp_ref[...]
    gtab_ref[SA : SA + 1] = jnp.sum(raw * wp_ref[...], axis=0, keepdims=True) + total(PB) * tab(PB)
    dwp_ref[...] = raw * tab(SA)
    for i in range(mlp // D):
        gtab_ref[F1B + i : F1B + i + 1] = jnp.sum(b1g_ref[:, i * D : i * D + D], axis=0, keepdims=True)


def middle(tall, temp, x, dy, v, halo, sums, peer, wp, w1, w2, tab):
    tokens = x.shape[0]
    wide = tokens + HALO
    mlp = w1.shape[1]
    smem = pl.BlockSpec(memory_space=pltpu.SMEM)
    vmem = pl.BlockSpec(memory_space=pltpu.VMEM)
    anywhere = pl.BlockSpec(memory_space=pl.ANY)

    def f(*shape):
        return jax.ShapeDtypeStruct(shape, F32)

    def s(*shape):
        return pltpu.VMEM(shape, F32)

    def b(*shape):
        return pltpu.VMEM(shape, BF)

    padded = s(wide + 2 * COLS, D)
    return pl.pallas_call(
        middle_kernel,
        out_shape=[
            f(tokens, D),
            f(tokens, D),
            f(tokens, D),
            f(D, D),
            f(2, D, mlp),
            f(TABLE, D),
            f(3, HD, D),
            f(3, HD, D),
            f(3, HD, D),
        ],
        in_specs=[smem, smem] + [anywhere] * 4 + [vmem] * 6,
        out_specs=[vmem] * 9,
        scratch_shapes=[
            b(3 * D, D),
            b(D, 3 * D),
            b(3 * D, mlp),
            b(mlp, 3 * D),
            b(3, D, 3 * D),
            s(wide, D),
            s(wide, D),
            padded,
            padded,
            padded,
            padded,
            padded,
            s(wide, D),
            padded,
            padded,
            s(wide // 3, D),
            b(TILE, 3 * D),
            b(TILE, 3 * D),
            b(TILE, mlp),
            b(TILE, mlp),
            s(TILE, mlp),
            s(8, mlp),
            s(8, mlp),
            s(8 * TABLE, D),
            s(3, D, D),
            s(wide, D),
            s(wide, D),
            s(wide, D),
            pltpu.SemaphoreType.DMA((6,)),
        ],
        compiler_params=pltpu.CompilerParams(vmem_limit_bytes=60 << 20),
    )(tall, temp, x, dy, v, halo, sums, peer, wp, w1, w2, tab)


def finish_kernel(
    tall_ref,
    temp_ref,
    x_ref,
    q_ref,
    k_ref,
    ds1_ref,
    dmx_ref,
    sums_ref,
    peer_ref,
    probs_ref,
    unit_ref,
    gprob_ref,
    gpeer_ref,
    w_ref,
    tab_ref,
    gtab_ref,
    dwp_ref,
    dx_ref,
    dw_ref,
    otab_ref,
    wh,
    wl,
    pv,
    cv,
    ch,
    side_rows,
    acc,
    dqkv,
):
    step = pl.program_id(0)
    last = pl.num_programs(0) - 1
    core = lax.axis_index("rows")
    rows_all = 2 * pl.num_programs(0) * TILE // COLS
    spans = slots(tall_ref, core, core * (rows_all // 2), rows_all)
    start = step * TILE

    def tab(r):
        return tab_ref[r : r + 1]

    @pl.when(step == 0)
    def _():
        def part(o):
            h, l = halves(w_ref[pl.ds(o, 16)])
            wh[pl.ds(o, 16)] = h
            wl[pl.ds(o, 16)] = l

        sweep(D, 16, part)
        dw_ref[...] = jnp.zeros_like(dw_ref)
        dw_ref[1, :, D : 2 * D] = dwp_ref[...]
        acc[...] = jnp.zeros_like(acc)
        ones = group_ones()
        temp = head_row(temp_ref)
        heat = jnp.zeros((1, D), F32)
        for s in range(3):
            sums = sums_ref[s]
            grad = gprob_ref[s]
            if s == 2:
                sums = sums + peer_ref[...]
                grad = grad + gpeer_ref[...]
            inv_q = lax.rsqrt(sums[HD : HD + 1] + EPS)
            inv_k = lax.rsqrt(sums[HD + 1 : HD + 2] + EPS)
            probs = probs_ref[s]
            unit = unit_ref[s]
            scores = probs * (grad - group_sum(probs * grad, ones))
            part_heat = jnp.sum(scores * unit, axis=0, keepdims=True)
            heat = heat + (part_heat if s < 2 else jnp.where(core == 0, part_heat, 0.0))
            pull = temp * scores
            both = pull * unit
            side_rows[8 * s : 8 * s + 1] = fold_to_row(group_sum(both, ones)) * inv_q * inv_q
            side_rows[8 * s + 1 : 8 * s + 2] = jnp.sum(both, axis=0, keepdims=True) * inv_k * inv_k
            h, l = halves(unfold(pull * row_to_fold(inv_q, ones) * inv_k))
            cv[s, 0:D] = h
            cv[s, D : 2 * D] = h
            cv[s, 2 * D : 3 * D] = l
            ch[s, :, 0:D] = h
            ch[s, :, D : 2 * D] = h
            ch[s, :, 2 * D : 3 * D] = l
            h, l = halves(unfold(probs))
            pv[s, 0:D] = h
            pv[s, D : 2 * D] = h
            pv[s, 2 * D : 3 * D] = l
        otab_ref[...] = gtab_ref[...]
        otab_ref[44:45] = heat

    dqkv[...] = jnp.zeros_like(dqkv)
    for s, (lo, hi) in enumerate(spans):

        @pl.when((lo < start + TILE) & (hi > start))
        def _():
            mask = span_mask(start, TILE, lo, hi)
            qm = jnp.where(mask, q_ref[...], 0.0)
            km = jnp.where(mask, k_ref[...], 0.0)
            dm = jnp.where(mask, dmx_ref[...], 0.0)
            dqkv[:, 0:D] += dot_nt(side(km), ch[s]) - qm * side_rows[8 * s : 8 * s + 1]
            dqkv[:, D : 2 * D] += dot_nn(side(qm), cv[s]) - km * side_rows[8 * s + 1 : 8 * s + 2]
            dqkv[:, 2 * D : 3 * D] += dot_nn(side(dm), pv[s])

    h, l = halves(dqkv[...])
    dn = dot_nt(h, wh[...]) + (dot_nt(l, wh[...]) + dot_nt(h, wl[...]))
    xhat, r = normalize(x_ref[...])
    nt = side((xhat * tab(N1G) + tab(N1S)).T)
    grads = dot_nn(nt, jnp.concatenate([h, h, l], axis=0))
    dw_ref[0] += grads[:, 0 : 2 * D]
    dw_ref[1, :, 0:D] += grads[:, 2 * D : 3 * D]
    dx_ref[...] = ds1_ref[...] + normalize_back(dn * tab(N1G), xhat, r)
    acc[0:8] += eights(dn * xhat)
    acc[8:16] += eights(dn)
    for i in range(3):
        acc[16 + 8 * i : 24 + 8 * i] += eights(dqkv[:, i * D : i * D + D])

    @pl.when(step == last)
    def _():
        for i, r in enumerate((N1G, N1S, QB, KB, VB)):
            otab_ref[r : r + 1] = jnp.sum(acc[8 * i : 8 * i + 8], axis=0, keepdims=True)


def finish(tall, temp, x, q, k, ds1, dmx, sums, peer, probs, unit, gprob, gpeer, w, tab, gtab, dwp):
    tokens = x.shape[0]
    smem = pl.BlockSpec(memory_space=pltpu.SMEM)
    row = pl.BlockSpec((TILE, D), lambda i: (i, 0))

    def whole(v):
        return pl.BlockSpec(v.shape, lambda i: (0,) * v.ndim)

    fixed = (sums, peer, probs, unit, gprob, gpeer, w, tab, gtab, dwp)
    return pl.pallas_call(
        finish_kernel,
        grid=(tokens // TILE,),
        out_shape=[
            jax.ShapeDtypeStruct((tokens, D), F32),
            jax.ShapeDtypeStruct((2, D, 2 * D), F32),
            jax.ShapeDtypeStruct((TABLE, D), F32),
        ],
        in_specs=[smem, smem] + [row] * 5 + [whole(v) for v in fixed],
        out_specs=[
            row,
            pl.BlockSpec((2, D, 2 * D), lambda i: (0, 0, 0)),
            pl.BlockSpec((TABLE, D), lambda i: (0, 0)),
        ],
        scratch_shapes=[
            pltpu.VMEM((D, 3 * D), BF),
            pltpu.VMEM((D, 3 * D), BF),
            pltpu.VMEM((3, 3 * D, D), BF),
            pltpu.VMEM((3, 3 * D, D), BF),
            pltpu.VMEM((3, D, 3 * D), BF),
            pltpu.VMEM((24, D), F32),
            pltpu.VMEM((40, D), F32),
            pltpu.VMEM((TILE, 3 * D), F32),
        ],
        compiler_params=pltpu.CompilerParams(vmem_limit_bytes=40 << 20),
    )(tall, temp, x, q, k, ds1, dmx, *fixed)


PART = 2 * D
ORDERS = ((0, 1, 2, 3), (1, 2, 0, 3), (2, 0, 1, 3))
KEPT = PART // 16
LAND = (0, PART // 2, PART * 3 // 4, PART * 7 // 8)
TROWS = TABLE // 2


def reduce_kernel(
    mid_ref,
    end_ref,
    tab_ref,
    all_ref,
    otab_ref,
    buf,
    first,
    land,
    tbuf,
    tland,
    own_sem,
    pair_send,
    pair_recv,
    send_sem,
    recv_sem,
    back_send,
    back_recv,
    tsend,
    trecv,
    out_sem,
    out_send,
    out_recv,
):
    core = lax.axis_index("rows")
    chip = lax.axis_index("canvas")
    bits = (lax.axis_size("canvas") - 1).bit_length()
    mine = [lax.rem(lax.div(chip, 1 << b), 2) for b in range(bits)]
    there = [{"canvas": chip + (1 - 2 * mine[b]) * (1 << b)} for b in range(bits)]
    twin = {"rows": 1 - core}
    barrier = pltpu.get_barrier_semaphore()
    for other in [twin] + there:
        pl.semaphore_signal(barrier, inc=1, device_id=other, device_id_type=MESH_ID)

    def remote(src, dst, send, recv, other):
        copy = pltpu.make_async_remote_copy(
            src_ref=src,
            dst_ref=dst,
            send_sem=send,
            recv_sem=recv,
            device_id=other,
            device_id_type=MESH_ID,
        )
        copy.start()
        return copy

    def block(which, i):
        if i < 2:
            return end_ref.at[which, :, i * D : i * D + D]
        return mid_ref.at[which, :, (i - 2) * D : (i - 1) * D]

    def place(ref, i):
        p, q = ((2, i) if i < 2 else ((i - 2) // 2, i % 2))
        return ref.at[p, pl.ds(q * D, D)]

    turns = (2, 4, 0, 3, 5, 1)
    own = {}
    for n, i in enumerate(turns):
        own[i] = pltpu.make_async_copy(block(core, i), place(buf, i), own_sem.at[i])
        own[i].start()
    town = pltpu.make_async_copy(
        tab_ref.at[pl.ds(pl.multiple_of(core * TROWS, 8), TROWS)], tbuf, own_sem.at[6]
    )
    town.start()
    pl.semaphore_wait(barrier, bits + 1)
    pair = {}
    for i in turns:
        pair[i] = remote(block(1 - core, i), place(first, i), pair_send.at[i], pair_recv.at[i], twin)
    tpair = remote(
        tab_ref.at[pl.ds(pl.multiple_of((1 - core) * TROWS, 8), TROWS)],
        tland.at[bits],
        tsend.at[bits],
        trecv.at[bits],
        twin,
    )

    def accumulate(p, at, src, src_at, rows):
        def one(i, carry):
            here = pl.ds(pl.multiple_of(at + i * 16, 8), 16)
            buf[p, here] += src[p, pl.ds(pl.multiple_of(src_at + i * 16, 8), 16)]
            return carry

        lax.fori_loop(0, rows // 16, one, 0)

    start = [0, 0, 0]
    moves = {}

    def send(p, s):
        b = ORDERS[p][s]
        half = PART >> (s + 1)
        away = pl.multiple_of(start[p] + (1 - mine[b]) * half, 16)
        moves[p, s] = remote(
            buf.at[p, pl.ds(away, half)],
            land.at[p, pl.ds(LAND[s], half)],
            send_sem.at[p, s],
            recv_sem.at[p, s],
            there[b],
        )
        start[p] = start[p] + mine[b] * half

    for p in range(3):
        for i in ((2, 3), (4, 5), (0, 1))[p]:
            own[i].wait()
            pair[i].wait()
        accumulate(p, 0, first, 0, PART)
        send(p, 0)
    town.wait()
    tpair.wait()
    tbuf[...] += tland[bits]
    for s in range(4):
        tmove = remote(tbuf, tland.at[s], tsend.at[s], trecv.at[s], there[s])
        for p in range(3):
            moves[p, s].wait()
            accumulate(p, start[p], land, LAND[s], PART >> (s + 1))
            if s < 3:
                send(p, s + 1)
        tmove.wait()
        tbuf[...] += tland[s]
    for b in range(4, bits):
        for p in range(3):
            extra = remote(
                buf.at[p, pl.ds(pl.multiple_of(start[p], 16), KEPT)],
                land.at[p, pl.ds(PART + (b - 4) * KEPT, KEPT)],
                send_sem.at[p, b],
                recv_sem.at[p, b],
                there[b],
            )
            extra.wait()
            accumulate(p, start[p], land, PART + (b - 4) * KEPT, KEPT)
        tmove = remote(tbuf, tland.at[b], tsend.at[b], trecv.at[b], there[b])
        tmove.wait()
        tbuf[...] += tland[b]
    half = pl.ds(pl.multiple_of(core * TROWS, 8), TROWS)
    outs = [
        pltpu.make_async_copy(tbuf, otab_ref.at[half], out_sem.at[6]),
        remote(tbuf, otab_ref.at[half], out_send.at[6], out_recv.at[6], twin),
    ]
    outs[0].start()

    def share(p, s):
        b = ORDERS[p][s]
        rows = PART >> (s + 1)
        held = pl.ds(pl.multiple_of(start[p], 16), rows)
        moves[p, s] = remote(
            first.at[p, held], first.at[p, held], back_send.at[p, s], back_recv.at[p, s], there[b]
        )
        start[p] = start[p] - mine[b] * rows

    for p in range(3):
        held = pl.ds(pl.multiple_of(start[p], 16), KEPT)
        first[p, held] = buf[p, held]
        share(p, 3)
    for s in range(3, -1, -1):
        for p in range(3):
            moves[p, s].wait()
            if s > 0:
                share(p, s - 1)
            else:
                for i in ((2, 3), (4, 5), (0, 1))[p]:
                    src, dst = place(first, i), all_ref.at[core, :, i * D : i * D + D]
                    local = pltpu.make_async_copy(src, dst, out_sem.at[i])
                    local.start()
                    outs += [local, remote(src, dst, out_send.at[i], out_recv.at[i], twin)]
    for copy in outs:
        copy.wait()


def reduce_all(mid, end, tab):
    bits = (lax.axis_size("canvas") - 1).bit_length()
    anywhere = pl.BlockSpec(memory_space=pl.ANY)
    dma = pltpu.SemaphoreType.DMA
    steps = max(bits, 4)
    return pl.pallas_call(
        reduce_kernel,
        out_shape=[
            jax.ShapeDtypeStruct((2, D, 6 * D), F32),
            jax.ShapeDtypeStruct((TABLE, D), F32),
        ],
        in_specs=[anywhere] * 3,
        out_specs=[anywhere] * 2,
        scratch_shapes=[
            pltpu.VMEM((3, PART, D), F32),
            pltpu.VMEM((3, PART, D), F32),
            pltpu.VMEM((3, PART + (steps - 4) * KEPT, D), F32),
            pltpu.VMEM((TROWS, D), F32),
            pltpu.VMEM((bits + 1, TROWS, D), F32),
            dma((7,)),
            dma((6,)),
            dma((6,)),
            dma((3, steps)),
            dma((3, steps)),
            dma((3, 4)),
            dma((3, 4)),
            dma((bits + 1,)),
            dma((bits + 1,)),
            dma((7,)),
            dma((7,)),
            dma((7,)),
        ],
        compiler_params=pltpu.CompilerParams(
            collective_id=3, has_side_effects=True, vmem_limit_bytes=32 << 20
        ),
    )(mid, end, tab)


def orth_kernel(
    all_hbm,
    mq_hbm,
    mp_hbm,
    m1_hbm,
    m2_hbm,
    gq_out,
    gp_out,
    g1_out,
    g2_out,
    nq_out,
    np_out,
    n1_out,
    n2_out,
    orth_ref,
    low,
    high,
    nat,
    mq,
    mp,
    m1,
    m2,
    xs,
    in_sem,
    out_sem,
):
    core = lax.axis_index("rows")
    blocks = m1.shape[1] // D
    pairs = (
        (all_hbm.at[0], low),
        (all_hbm.at[1], high),
        (mq_hbm, mq),
        (mp_hbm, mp),
        (m1_hbm, m1),
        (m2_hbm, m2),
    )
    loads = [pltpu.make_async_copy(a, b, in_sem.at[i]) for i, (a, b) in enumerate(pairs)]
    for load in loads:
        load.start()
    for load in loads:
        load.wait()
    outs = []

    def store(src, dst):
        outs.append(pltpu.make_async_copy(src, dst, out_sem.at[len(outs)]))
        outs[-1].start()

    store(low.at[:, 0 : 2 * D], gq_out.at[:, 0 : 2 * D])
    store(high.at[:, 0:D], gq_out.at[:, 2 * D : 3 * D])
    store(high.at[:, D : 2 * D], gp_out)
    store(low.at[:, 2 * D : 6 * D], g1_out)
    for b in range(blocks):
        nat[b * D : b * D + D] = high[:, (2 + b) * D : (3 + b) * D].T
    store(nat, g2_out)

    def small(o):
        rows = pl.ds(o, 16)
        mq[rows, 0 : 2 * D] = MUON_KEEP * mq[rows, 0 : 2 * D] + low[rows, 0 : 2 * D]
        mq[rows, 2 * D : 3 * D] = MUON_KEEP * mq[rows, 2 * D : 3 * D] + high[rows, 0:D]
        mp[rows] = MUON_KEEP * mp[rows] + high[rows, D : 2 * D]
        m1[rows] = MUON_KEEP * m1[rows] + low[rows, 2 * D : 6 * D]

    sweep(D, 16, small)

    def large(o):
        rows = pl.ds(o, 32)
        m2[rows] = MUON_KEEP * m2[rows] + nat[rows]

    sweep(blocks * D, 32, large)
    store(mq, nq_out)
    store(mp, np_out)
    store(m1, n1_out)
    store(m2, n2_out)

    @pl.when(core == 0)
    def _():
        xs[0] = mq[:, 0:D]
        xs[1] = mq[:, D : 2 * D]
        for b in range(blocks):
            xs[2 + b] = m1[:, b * D : b * D + D]

    @pl.when(core == 1)
    def _():
        xs[0] = mq[:, 2 * D : 3 * D]
        xs[1] = mp[...]
        for b in range(blocks):
            xs[2 + b] = m2[b * D : b * D + D].T

    def squares(v):
        return jnp.sum(jnp.sum(v * v, axis=0, keepdims=True), axis=1, keepdims=True)

    groups = ((0,), (1,), tuple(range(2, 2 + blocks)))
    for g in groups:
        norm = squares(xs[g[0]])
        for b in g[1:]:
            norm = norm + squares(xs[b])
        inv = 1.0 / (jnp.sqrt(norm) + 1e-07)
        for b in g:
            xs[b] = xs[b] * inv

    def step(i, carry):
        for g in groups:
            left, right = [], []
            for b in g:
                h, l = halves(xs[b])
                left += [h, l, h]
                right += [h, h, l]
            gram = dot_nt(jnp.concatenate(left, axis=1), jnp.concatenate(right, axis=1))
            h, l = halves(gram)
            square = dot_nn(jnp.concatenate([h, l, h], axis=1), jnp.concatenate([h, h, l], axis=0))
            poly = side(-4.775 * gram + 2.0315 * square)
            for b in g:
                h, l = halves(xs[b])
                xs[b] = 3.4445 * xs[b] + dot_nn(poly, jnp.concatenate([h, h, l], axis=0))
        return carry

    lax.fori_loop(0, 5, step, 0)

    @pl.when(core == 0)
    def _():
        orth_ref[...] = xs[...]

    @pl.when(core == 1)
    def _():
        orth_ref[0:2] = xs[0:2]
        for b in range(blocks):
            orth_ref[2 + b] = xs[2 + b].T

    for copy in outs:
        copy.wait()


def orthogonalize(everything, mq, mp, m1, m2):
    anywhere = pl.BlockSpec(memory_space=pl.ANY)
    args = (mq, mp, m1, m2)
    blocks = 2 + m1.shape[1] // D
    return pl.pallas_call(
        orth_kernel,
        out_shape=[jax.ShapeDtypeStruct(a.shape, F32) for a in args + args]
        + [jax.ShapeDtypeStruct((blocks, D, D), F32)],
        in_specs=[anywhere] * 5,
        out_specs=[anywhere] * 8 + [pl.BlockSpec(memory_space=pltpu.VMEM)],
        scratch_shapes=[
            pltpu.VMEM(everything.shape[1:], F32),
            pltpu.VMEM(everything.shape[1:], F32),
            pltpu.VMEM(m2.shape, F32),
            pltpu.VMEM(mq.shape, F32),
            pltpu.VMEM(mp.shape, F32),
            pltpu.VMEM(m1.shape, F32),
            pltpu.VMEM(m2.shape, F32),
            pltpu.VMEM((blocks, D, D), F32),
            pltpu.SemaphoreType.DMA((6,)),
            pltpu.SemaphoreType.DMA((9,)),
        ],
        compiler_params=pltpu.CompilerParams(vmem_limit_bytes=56 << 20),
    )(everything, *args)


def pair_kernel(own_ref, both_ref, own_sem, send_sem, recv_sem):
    core = lax.axis_index("rows")
    barrier = pltpu.get_barrier_semaphore()
    pl.semaphore_signal(barrier, inc=1, device_id={"rows": 1 - core}, device_id_type=MESH_ID)
    local = pltpu.make_async_copy(own_ref, both_ref.at[core], own_sem)
    local.start()
    pl.semaphore_wait(barrier, 1)
    copy = pltpu.make_async_remote_copy(
        src_ref=own_ref,
        dst_ref=both_ref.at[core],
        send_sem=send_sem,
        recv_sem=recv_sem,
        device_id={"rows": 1 - core},
        device_id_type=MESH_ID,
    )
    copy.start()
    local.wait()
    copy.wait()


def pair_up(own):
    dma = pltpu.SemaphoreType.DMA
    return pl.pallas_call(
        pair_kernel,
        out_shape=jax.ShapeDtypeStruct((2,) + own.shape, F32),
        in_specs=[pl.BlockSpec(memory_space=pltpu.VMEM)],
        out_specs=pl.BlockSpec(memory_space=pl.ANY),
        scratch_shapes=[dma, dma, dma],
        compiler_params=pltpu.CompilerParams(
            collective_id=2, has_side_effects=True, vmem_limit_bytes=16 << 20
        ),
    )(own)


def moment_step(current, one, two, gradient):
    first = BETA1 * one + (1.0 - BETA1) * gradient
    second = BETA2 * two + (1.0 - BETA2) * gradient * gradient
    fix_one = 1.0 - BETA1**STEP
    fix_two = 1.0 - BETA2**STEP
    updated = current - ADAM_RATE * (first / fix_one) / (jnp.sqrt(second / fix_two) + ADAM_FLOOR)
    return first, second, updated


def update_kernel(
    rows_ref,
    last_ref,
    wq_ref,
    wp_ref,
    w1_ref,
    w2_ref,
    tab_ref,
    one_ref,
    two_ref,
    gtab_ref,
    nq_ref,
    np_ref,
    n1_ref,
    n2_ref,
    cq_ref,
    cp_ref,
    c1_ref,
    c2_ref,
    first_ref,
    second_ref,
    small_ref,
):
    mlp = w1_ref.shape[1]

    def put(new_ref, copy_ref, w, orth, large, lanes):
        new = w * (1.0 - MUON_RATE * DECAY) - MUON_RATE * 0.2 * math.sqrt(large) * orth
        new_ref[:, lanes] = new
        copy_ref[:, lanes] = new.astype(BF)

    for i in range(3):
        lanes = slice(i * D, i * D + D)
        orth = rows_ref[0, i] if i < 2 else rows_ref[1, 0]
        put(nq_ref, cq_ref, wq_ref[:, lanes], orth, D, lanes)
    put(np_ref, cp_ref, wp_ref[...], rows_ref[1, 1], D, slice(0, D))
    for i in range(mlp // D):
        lanes = slice(i * D, i * D + D)
        put(n1_ref, c1_ref, w1_ref[:, lanes], rows_ref[0, 2 + i], mlp, lanes)
    put(n2_ref, c2_ref, w2_ref[...], last_ref[0, 0], mlp, slice(0, D))
    first, second, small = moment_step(tab_ref[...], one_ref[...], two_ref[...], gtab_ref[0:SMALL])
    first_ref[...] = first
    second_ref[...] = second
    small_ref[...] = small


def update(both, wq, wp, w1, w2, tab, one, two, gtab):
    steps = w2.shape[0] // D
    piece = D // steps

    def rows(v):
        size = v.shape[0] // steps
        return pl.BlockSpec((size, v.shape[1]), lambda i: (i, 0))

    def whole(v):
        return pl.BlockSpec(v.shape, lambda i: (0, 0))

    weights = (wq, wp, w1, w2)
    return pl.pallas_call(
        update_kernel,
        grid=(steps,),
        out_shape=[jax.ShapeDtypeStruct(w.shape, F32) for w in weights]
        + [jax.ShapeDtypeStruct(w.shape, BF) for w in weights]
        + [jax.ShapeDtypeStruct(tab.shape, F32)] * 3,
        in_specs=[
            pl.BlockSpec((2, 2 + steps, piece, D), lambda i: (0, 0, i, 0)),
            pl.BlockSpec((1, 1, D, D), lambda i: (1, 2 + i, 0, 0)),
        ]
        + [rows(w) for w in weights]
        + [whole(v) for v in (tab, one, two, gtab)],
        out_specs=[rows(w) for w in weights] * 2 + [whole(tab)] * 3,
        compiler_params=pltpu.CompilerParams(vmem_limit_bytes=32 << 20),
    )(both, both, *weights, tab, one, two, gtab)


def on_device(
    x4, dy4, tall, wqkv, wp, w1, w2, mqkv, mp, m1, m2, tab, tab_one, tab_two, temp, temp_one, temp_two
):
    shape = x4.shape
    tokens = shape[1] * shape[2]
    x = x4.reshape(tokens, D)
    dy = dy4.reshape(tokens, D)
    q, k, v, sums = project(tall, x, wqkv, tab)
    halo, peer = widen(x, dy, v, sums)
    out, ds1, dmx, dwp, mid, gtab, probs, unit, gprob = middle(
        tall, temp, x, dy, v, halo, sums, peer, wp, w1, w2, tab
    )
    gpeer = swap(gprob[2], 1)
    dx, end, gtab = finish(
        tall, temp, x, q, k, ds1, dmx, sums, peer, probs, unit, gprob, gpeer, wqkv, tab, gtab, dwp
    )
    everything, gtab = reduce_all(mid, end, gtab)
    *grads, orth = orthogonalize(everything, mqkv, mp, m1, m2)
    results = update(pair_up(orth), wqkv, wp, w1, w2, tab, tab_one, tab_two, gtab)
    heat = jnp.sum(gtab[44].reshape(HEADS, HD), axis=1)
    warm = moment_step(temp, temp_one, temp_two, heat)
    count = tokens * D * lax.axis_size("rows") * lax.axis_size("canvas")
    rms = jnp.sqrt(jnp.sum(gtab[40:44], axis=1) / count)
    return (out.reshape(shape), dx.reshape(shape), *grads, *results, *warm, rms)


def solution(mesh):
    split = P("canvas", "rows", None, None)
    return jax.shard_map(
        on_device,
        mesh=mesh,
        in_specs=(split, split, P("canvas", None)) + (P(),) * 14,
        out_specs=(split, split) + (P(),) * 23,
        check_vma=False,
    )
```

```python
import math

import jax
import jax.numpy as jnp
from jax import lax
from jax.experimental import pallas as pl
from jax.experimental.pallas import tpu as pltpu
from jax.sharding import PartitionSpec as P

BF = jnp.bfloat16
F32 = jnp.float32
MESH_ID = pl.DeviceIdType.MESH

EPS = 1e-06
ROOT_HALF = 1.0 / math.sqrt(2.0)
ROOT_TWOPI = 1.0 / math.sqrt(2.0 * math.pi)
STEP = 10
MUON_RATE = 0.2
MUON_KEEP = 0.95
DECAY = 0.01
ADAM_RATE = 0.2
BETA1 = 0.9
BETA2 = 0.95
ADAM_FLOOR = 1e-08

HEADS = 8
HD = 48
D = HEADS * HD
COLS = 32
HALO = 4 * COLS
TILE = 256

N1G, N1S, N3G, N3S, N2G, N2S, SA, SL, SM, QB, KB, VB, PB, C1B, BG, BS, C2B, F2B = range(18)
F1B, K1R, K2R = 18, 22, 31
SMALL = 40
TABLE = 48


def halves(v):
    hi = v.astype(BF)
    return hi, (v - hi.astype(F32)).astype(BF)


def side(v):
    h, l = halves(v)
    return jnp.concatenate([h, l, h], axis=1)


def dot_nn(a, b):
    return lax.dot_general(a, b, (((1,), (0,)), ((), ())), preferred_element_type=F32)


def dot_nt(a, b):
    return lax.dot_general(a, b, (((1,), (1,)), ((), ())), preferred_element_type=F32)


def normalize(v):
    mean = jnp.mean(v, axis=1, keepdims=True)
    c = v - mean
    r = lax.rsqrt(jnp.mean(c * c, axis=1, keepdims=True) + EPS)
    return c * r, r


def normalize_back(e, xhat, r):
    return r * (
        e - jnp.mean(e, axis=1, keepdims=True) - xhat * jnp.mean(e * xhat, axis=1, keepdims=True)
    )


def gelu_parts(v):
    phi = 0.5 * (1.0 + lax.erf(v * ROOT_HALF))
    return v * phi, phi + v * jnp.exp(-0.5 * v * v) * ROOT_TWOPI


def eights(v):
    total = v[0:8]
    for i in range(8, v.shape[0], 8):
        total = total + v[i : i + 8]
    return total


def sweep(count, size, body):
    def one(i, carry):
        body(pl.multiple_of(i * size, size))
        return carry

    lax.fori_loop(0, count // size, one, 0)


def image_ends(tall_ref):
    e0 = tall_ref[0, 0]
    e1 = e0 + tall_ref[0, 1]
    return e0, e1, e1 + tall_ref[0, 2]


def slots(tall_ref, core, first_row, rows_all):
    e0, e1, e2 = image_ends(tall_ref)
    low = (jnp.where(core == 0, 0, e2), jnp.where(core == 0, e0, 0), e1)
    high = (jnp.where(core == 0, e0, rows_all), jnp.where(core == 0, e1, 0), e2)
    return [((a - first_row) * COLS, (b - first_row) * COLS) for a, b in zip(low, high)]


def span_mask(start, rows, lo, hi):
    token = start + lax.broadcasted_iota(jnp.int32, (rows, D), 0)
    return (token >= lo) & (token < hi)


def lane_head():
    return lax.broadcasted_iota(jnp.int32, (HD, D), 1) // HD


def lane_slot():
    return lax.broadcasted_iota(jnp.int32, (HD, D), 1) % HD


def fold(full):
    head = lane_head()
    total = jnp.where(head == 0, full[0:HD], 0.0)
    for h in range(1, HEADS):
        total = total + jnp.where(head == h, full[h * HD : h * HD + HD], 0.0)
    return total


def unfold(small):
    head = lane_head()
    return jnp.concatenate([jnp.where(head == h, small, 0.0) for h in range(HEADS)], axis=0)


def group_ones():
    a = lax.broadcasted_iota(jnp.int32, (D, D), 0) // HD
    b = lax.broadcasted_iota(jnp.int32, (D, D), 1) // HD
    return jnp.where(a == b, 1.0, 0.0).astype(BF)


def group_sum(v, ones):
    h = v.astype(BF)
    rest = v - h.astype(F32)
    m = rest.astype(BF)
    l = (rest - m.astype(F32)).astype(BF)
    return dot_nn(h, ones) + (dot_nn(m, ones) + dot_nn(l, ones))


def row_to_fold(row, ones):
    slot = lax.broadcasted_iota(jnp.int32, (HD, D), 0)
    return group_sum(jnp.where(lane_slot() == slot, jnp.broadcast_to(row, (HD, D)), 0.0), ones)


def fold_to_row(small):
    slot = lax.broadcasted_iota(jnp.int32, (HD, D), 0)
    return jnp.sum(jnp.where(lane_slot() == slot, small, 0.0), axis=0, keepdims=True)


def head_row(temp_ref):
    head = lax.broadcasted_iota(jnp.int32, (1, D), 1) // HD
    row = jnp.where(head == 0, temp_ref[0], 0.0)
    for h in range(1, HEADS):
        row = row + jnp.where(head == h, temp_ref[h], 0.0)
    return row


def project_kernel(tall_ref, x_ref, w_ref, tab_ref, q_ref, k_ref, v_ref, sums_ref, wcat, cross):
    step = pl.program_id(0)
    core = lax.axis_index("rows")
    rows_all = 2 * pl.num_programs(0) * TILE // COLS
    spans = slots(tall_ref, core, core * (rows_all // 2), rows_all)
    start = step * TILE

    @pl.when(step == 0)
    def _():
        def part(o):
            h, l = halves(w_ref[pl.ds(o, 64)])
            wcat[pl.ds(o, 64)] = h
            wcat[pl.ds(D + o, 64)] = h
            wcat[pl.ds(2 * D + o, 64)] = l

        sweep(D, 64, part)
        cross[...] = jnp.zeros_like(cross)
        sums_ref[...] = jnp.zeros_like(sums_ref)

    xhat, _ = normalize(x_ref[...])
    lhs = side(xhat * tab_ref[N1G : N1G + 1] + tab_ref[N1S : N1S + 1])
    q = dot_nn(lhs, wcat[:, 0:D]) + tab_ref[QB : QB + 1]
    q_ref[...] = q
    k = dot_nn(lhs, wcat[:, D : 2 * D]) + tab_ref[KB : KB + 1]
    k_ref[...] = k
    v_ref[...] = dot_nn(lhs, wcat[:, 2 * D : 3 * D]) + tab_ref[VB : VB + 1]
    qt = side(q.T)
    for s, (lo, hi) in enumerate(spans):

        @pl.when((lo < start + TILE) & (hi > start))
        def _():
            mask = span_mask(start, TILE, lo, hi)
            kh, kl = halves(jnp.where(mask, k_ref[...], 0.0))
            cross[s] += dot_nn(qt, jnp.concatenate([kh, kh, kl], axis=0))
            qm = jnp.where(mask, q_ref[...], 0.0)
            km = jnp.where(mask, k_ref[...], 0.0)
            sums_ref[s, HD : HD + 1] += jnp.sum(qm * qm, axis=0, keepdims=True)
            sums_ref[s, HD + 1 : HD + 2] += jnp.sum(km * km, axis=0, keepdims=True)

    @pl.when(step == pl.num_programs(0) - 1)
    def _():
        for s in range(3):
            sums_ref[s, 0:HD] = fold(cross[s])


def project(tall, x, w, tab):
    tokens = x.shape[0]
    row = pl.BlockSpec((TILE, D), lambda i: (i, 0))
    return pl.pallas_call(
        project_kernel,
        grid=(tokens // TILE,),
        out_shape=[jax.ShapeDtypeStruct((tokens, D), F32)] * 3
        + [jax.ShapeDtypeStruct((3, HD + 8, D), F32)],
        in_specs=[
            pl.BlockSpec(memory_space=pltpu.SMEM),
            row,
            pl.BlockSpec((D, 3 * D), lambda i: (0, 0)),
            pl.BlockSpec((SMALL, D), lambda i: (0, 0)),
        ],
        out_specs=[row, row, row, pl.BlockSpec((3, HD + 8, D), lambda i: (0, 0, 0))],
        scratch_shapes=[pltpu.VMEM((3 * D, 3 * D), BF), pltpu.VMEM((3, D, D), F32)],
        compiler_params=pltpu.CompilerParams(vmem_limit_bytes=60 << 20),
    )(tall, x, w, tab)


def widen_kernel(x_ref, dy_ref, v_ref, sums_ref, halo_ref, peer_ref, send_sem, recv_sem):
    core = lax.axis_index("rows")
    tokens = x_ref.shape[0]
    barrier = pltpu.get_barrier_semaphore()
    pl.semaphore_signal(barrier, inc=1, device_id={"rows": 1 - core}, device_id_type=MESH_ID)
    pl.semaphore_wait(barrier, 1)
    edge = pl.ds(pl.multiple_of((1 - core) * (tokens - HALO), HALO), HALO)
    pairs = [(src.at[edge], halo_ref.at[i]) for i, src in enumerate((x_ref, dy_ref, v_ref))]
    pairs.append((sums_ref.at[2], peer_ref))
    copies = []
    for i, (src, dst) in enumerate(pairs):
        copies.append(
            pltpu.make_async_remote_copy(
                src_ref=src,
                dst_ref=dst,
                send_sem=send_sem.at[i],
                recv_sem=recv_sem.at[i],
                device_id={"rows": 1 - core},
                device_id_type=MESH_ID,
            )
        )
        copies[-1].start()
    for copy in copies:
        copy.wait()


def widen(x, dy, v, sums):
    anywhere = pl.BlockSpec(memory_space=pl.ANY)
    return pl.pallas_call(
        widen_kernel,
        out_shape=[
            jax.ShapeDtypeStruct((3, HALO, D), F32),
            jax.ShapeDtypeStruct(sums.shape[1:], F32),
        ],
        in_specs=[anywhere] * 4,
        out_specs=[anywhere] * 2,
        scratch_shapes=[pltpu.SemaphoreType.DMA((4,)), pltpu.SemaphoreType.DMA((4,))],
        compiler_params=pltpu.CompilerParams(collective_id=0, has_side_effects=True),
    )(x, dy, v, sums)


def swap_kernel(src, dst, send_sem, recv_sem):
    core = lax.axis_index("rows")
    barrier = pltpu.get_barrier_semaphore()
    pl.semaphore_signal(barrier, inc=1, device_id={"rows": 1 - core}, device_id_type=MESH_ID)
    pl.semaphore_wait(barrier, 1)
    copy = pltpu.make_async_remote_copy(
        src_ref=src.at[2],
        dst_ref=dst,
        send_sem=send_sem,
        recv_sem=recv_sem,
        device_id={"rows": 1 - core},
        device_id_type=MESH_ID,
    )
    copy.start()
    copy.wait()


def swap(v, number):
    return pl.pallas_call(
        swap_kernel,
        out_shape=jax.ShapeDtypeStruct(v.shape[1:], F32),
        in_specs=[pl.BlockSpec(memory_space=pl.ANY)],
        out_specs=pl.BlockSpec(memory_space=pl.ANY),
        scratch_shapes=[pltpu.SemaphoreType.DMA, pltpu.SemaphoreType.DMA],
        compiler_params=pltpu.CompilerParams(collective_id=number, has_side_effects=True),
    )(v)


def row_flags(tall_ref, rows_all):
    ends = image_ends(tall_ref)

    def above(row):
        first = (row == 0) | (row == ends[0]) | (row == ends[1]) | (row == ends[2])
        return jnp.where(first, 0.0, 1.0)

    def below(row):
        return jnp.where(row + 1 == rows_all, 0.0, above(row + 1))

    return above, below


def middle_kernel(
    tall_ref,
    temp_ref,
    x_hbm,
    dy_hbm,
    v_hbm,
    halo_hbm,
    sums_ref,
    peer_ref,
    wp_ref,
    w1_ref,
    w2_ref,
    tab_ref,
    out_ref,
    ds1_ref,
    dmx_ref,
    dwp_ref,
    dw_ref,
    gtab_ref,
    probs_ref,
    unit_ref,
    gprob_ref,
    wpv,
    wph,
    w1c,
    w2c,
    pcat,
    mixed,
    s1,
    li,
    act,
    slope,
    mid,
    s2,
    ds2,
    gp,
    z,
    n2c,
    dzc,
    hid_h,
    hid_l,
    hslope,
    b1_ref,
    b1g_ref,
    acc,
    cross,
    x_ref,
    dy_ref,
    v_ref,
    flags,
    nt,
    dt,
    load_sem,
):
    core = lax.axis_index("rows")
    wide = x_ref.shape[0]
    tokens = wide - HALO
    dw1_ref, dw2_ref = dw_ref.at[0], dw_ref.at[1]
    lo_ = x_ref
    loads = []
    for i, (src, dst) in enumerate(((x_hbm, x_ref), (dy_hbm, dy_ref), (v_hbm, v_ref))):
        own = pl.ds(pl.multiple_of(core * HALO, HALO), tokens)
        far = pl.ds(pl.multiple_of((1 - core) * tokens, HALO), HALO)
        loads.append(pltpu.make_async_copy(src, dst.at[own], load_sem.at[2 * i]))
        loads.append(pltpu.make_async_copy(halo_hbm.at[i], dst.at[far], load_sem.at[2 * i + 1]))
    for load in loads:
        load.start()
    own_rows = tokens // COLS
    rows_wide = wide // COLS
    rows_all = 2 * own_rows
    first_row = core * (own_rows - HALO // COLS)
    own_off = pl.multiple_of(core * HALO, HALO)
    mlp = w1_ref.shape[1]
    spans = slots(tall_ref, core, first_row, rows_all)
    above, below = row_flags(tall_ref, rows_all)

    def tab(r):
        return tab_ref[r : r + 1]

    def is_own(row):
        return (row >= core * (HALO // COLS)) & (row < core * (HALO // COLS) + own_rows)

    def part_p(o):
        rows = pl.ds(o, 192)
        h, l = halves(wp_ref[rows])
        wpv[rows] = h
        wpv[pl.ds(D + o, 192)] = h
        wpv[pl.ds(2 * D + o, 192)] = l
        wph[rows, 0:D] = h
        wph[rows, D : 2 * D] = h
        wph[rows, 2 * D : 3 * D] = l

    sweep(D, 192, part_p)

    def part_1(o):
        rows = pl.ds(o, 64)
        h, l = halves(w1_ref[rows])
        w1c[rows] = h
        w1c[pl.ds(D + o, 64)] = h
        w1c[pl.ds(2 * D + o, 64)] = l

    sweep(D, 64, part_1)

    def part_2(o):
        rows = pl.ds(o, 256)
        h, l = halves(w2_ref[rows])
        w2c[rows, 0:D] = h
        w2c[rows, D : 2 * D] = h
        w2c[rows, 2 * D : 3 * D] = l

    sweep(mlp, 256, part_2)

    ones = group_ones()
    temp = head_row(temp_ref)
    for s in range(3):
        sums = sums_ref[s]
        if s == 2:
            sums = sums + peer_ref[...]
        inv_q = lax.rsqrt(sums[HD : HD + 1] + EPS)
        inv_k = lax.rsqrt(sums[HD + 1 : HD + 2] + EPS)
        unit = sums[0:HD] * row_to_fold(inv_q, ones) * inv_k
        unit_ref[s] = unit
        weight = jnp.exp(temp * unit)
        probs = weight / group_sum(weight, ones)
        probs_ref[s] = probs
        h, l = halves(unfold(probs))
        pcat[s, :, 0:D] = h
        pcat[s, :, D : 2 * D] = h
        pcat[s, :, 2 * D : 3 * D] = l

    acc[...] = jnp.zeros_like(acc)
    gtab_ref[...] = jnp.zeros_like(gtab_ref)

    def add(r, v):
        acc[8 * r : 8 * r + 8] += v

    for load in loads:
        load.wait()

    def own_part(o, size):
        token = o + lax.broadcasted_iota(jnp.int32, (size, D), 0)
        return jnp.where((token >= own_off) & (token < own_off + tokens), 1.0, 0.0)

    def attend(o):
        size = wide // 3
        mixed[pl.ds(o, size)] = jnp.zeros((size, D), F32)
        for s, (lo, hi) in enumerate(spans):

            @pl.when((lo < o + size) & (hi > o))
            def _():
                vm = jnp.where(span_mask(o, size, lo, hi), v_ref[pl.ds(o, size)], 0.0)
                mixed[pl.ds(o, size)] += dot_nt(side(vm), pcat[s])

        z[...] = dot_nn(side(mixed[pl.ds(o, size)]), wpv[...]) + tab(PB)
        rows = pl.ds(o, size)
        branch = tab(SA) * z[...]
        stream = x_ref[rows] + branch
        s1[rows] = stream
        xhat, _ = normalize(stream)
        li[pl.ds(pl.multiple_of(o + COLS, COLS), size)] = xhat * tab(N3G) + tab(N3S)
        add(41, eights(own_part(o, size) * branch * branch))

    sweep(wide, wide // 3, attend)

    pad = jnp.zeros((COLS, D), F32)
    for buf in (li, mid, gp, ds2):
        buf[0:COLS] = pad
        buf[wide + COLS : wide + 2 * COLS] = pad

    for r in range(rows_wide):
        row = first_row + r
        mine = jnp.where(is_own(r), 1.0, 0.0)
        for n, flag in enumerate((above(row), below(row), mine)):
            flags[n, r * COLS : r * COLS + COLS] = jnp.full((COLS, 128), flag, F32)

    block = 12 * COLS
    col = lax.rem(lax.broadcasted_iota(jnp.int32, (block + 2 * COLS, 128), 0), COLS)

    def convolve(src, base, flip, scale, visit, other=None):
        def one(n, carry):
            lanes = pl.ds(pl.multiple_of(lax.rem(n, 3) * 128, 128), 128)
            o = pl.multiple_of(lax.div(n, 3) * block, block)
            rows = pl.ds(o, block)
            taps = [tab_ref[base + t : base + t + 1, lanes] for t in range(9)]
            if flip:
                taps = taps[::-1]
            if scale is not None:
                taps = [t * tab_ref[scale : scale + 1, lanes] for t in taps]
            u = src[pl.ds(o, block + 2 * COLS), lanes]
            left = jnp.where(col == 0, 0.0, pltpu.roll(u, 1, 0))
            right = jnp.where(col == COLS - 1, 0.0, pltpu.roll(u, block + 2 * COLS - 1, 0))
            up, down = flags[0, rows], flags[1, rows]

            def line(a):
                cut = slice(a * COLS, a * COLS + block)
                return left[cut] * taps[3 * a] + u[cut] * taps[3 * a + 1] + right[cut] * taps[3 * a + 2]

            visit(o, rows, lanes, line(1) + up * line(0) + down * line(2))
            if other is not None:
                near = other[pl.ds(o, block + 2 * COLS), lanes]
                mine = flags[2, rows]
                held = (
                    mine * up * near[0:block],
                    mine * near[COLS : COLS + block],
                    mine * down * near[2 * COLS : 2 * COLS + block],
                )
                inner = slice(COLS, COLS + block)
                for a in range(3):
                    for b, view in enumerate((right, u, left)):
                        t = 8 * (base + 3 * a + b)
                        acc[t : t + 8, lanes] += eights(view[inner] * held[a])
            return carry

        lax.fori_loop(0, 3 * (wide // block), one, 0)

    def first(o, rows, lanes, value):
        at = pl.ds(o + COLS, block)
        a, s = gelu_parts(value + tab_ref[C1B : C1B + 1, lanes])
        act[rows, lanes] = a
        slope[rows, lanes] = s
        mid[at, lanes] = a * tab_ref[BG : BG + 1, lanes] + tab_ref[BS : BS + 1, lanes]

    convolve(li, K1R, False, None, first)

    def second(o, rows, lanes, value):
        value = value + tab_ref[C2B : C2B + 1, lanes]
        lo_[rows, lanes] = value
        branch = tab_ref[SL : SL + 1, lanes] * value
        s2[rows, lanes] = s1[rows, lanes] + branch
        acc[8 * 42 : 8 * 42 + 8, lanes] += eights(flags[2, rows] * branch * branch)

    convolve(mid, K2R, False, None, second)

    dw1_ref[...] = jnp.zeros_like(dw1_ref)
    dw2_ref[...] = jnp.zeros_like(dw2_ref)
    b1g_ref[...] = jnp.zeros_like(b1g_ref)
    for i in range(mlp // D):
        b1_ref[0:1, i * D : i * D + D] = tab(F1B + i)

    def feed(o, size, own):
        rows = pl.ds(0, size)
        here = pl.ds(o, size)
        xhat, _ = normalize(s2[here])
        n2 = xhat * tab(N2G) + tab(N2S)
        h, l = halves(n2)
        n2c[rows, 0:D] = h
        n2c[rows, D : 2 * D] = l
        n2c[rows, 2 * D : 3 * D] = h
        if own:
            nt[...] = side(n2.T)

        def up(j):
            lanes = pl.ds(j, 256)
            pre = dot_nn(n2c[rows], w1c[:, lanes]) + b1_ref[0:1, lanes]
            a, s = gelu_parts(pre)
            h, l = halves(a)
            hid_h[rows, lanes] = h
            hid_l[rows, lanes] = l
            hslope[rows, lanes] = s

        sweep(mlp, 256, up)
        w2h, w2l = w2c[:, 0:D], w2c[:, 2 * D : 3 * D]
        raw = (
            dot_nn(hid_h[rows], w2h) + (dot_nn(hid_l[rows], w2h) + dot_nn(hid_h[rows], w2l))
        ) + tab(F2B)
        dy = dy_ref[here]
        dz = tab(SM) * dy
        h, l = halves(dz)
        dzc[rows, 0:D] = h
        dzc[rows, D : 2 * D] = l
        dzc[rows, 2 * D : 3 * D] = h
        if own:
            dt[...] = side(dz.T)
            branch = tab(SM) * raw
            result = s2[here] + branch
            out_ref[pl.ds(pl.multiple_of(o - own_off, size), size)] = result
            add(40, eights(result * result))
            add(43, eights(branch * branch))
            add(SM, eights(dy * raw))
            add(F2B, eights(dz))

        def down(j):
            lanes = pl.ds(j, 256)
            dpre = dot_nt(dzc[rows], w2c[lanes, :]) * hslope[rows, lanes]
            h, l = halves(dpre)
            if own:
                b1g_ref[:, lanes] += eights(dpre)
                dw1_ref[:, lanes] += dot_nn(nt[...], jnp.concatenate([h, h, l], axis=0))
                hh, hl = hid_h[rows, lanes], hid_l[rows, lanes]
                dw2_ref[:, lanes] += dot_nn(dt[...], jnp.concatenate([hh, hh, hl], axis=0))
            hid_h[rows, lanes] = h
            hid_l[rows, lanes] = l

        sweep(mlp, 256, down)
        w1h, w1l = w1c[0:D], w1c[2 * D : 3 * D]
        dn = dot_nt(hid_h[rows], w1h) + (dot_nt(hid_l[rows], w1h) + dot_nt(hid_h[rows], w1l))
        xhat, r = normalize(s2[here])
        ds2[pl.ds(pl.multiple_of(o + COLS, COLS), size)] = dy_ref[here] + normalize_back(
            dn * tab(N2G), xhat, r
        )
        if own:
            add(N2G, eights(dn * xhat))
            add(N2S, eights(dn))

    def feed_one(i, carry):
        feed(pl.multiple_of(own_off + i * TILE, 128), TILE, True)
        return carry

    lax.fori_loop(0, tokens // TILE, feed_one, 0)
    edge = HALO // 2
    feed(pl.multiple_of(tokens - core * (tokens - edge), edge), edge, False)
    rest = pl.multiple_of(COLS + (1 - core) * (tokens + edge), COLS)
    ds2[pl.ds(rest, edge)] = jnp.zeros((edge, D), F32)

    def third(o, rows, lanes, value):
        grad = value * tab_ref[BG : BG + 1, lanes] * slope[rows, lanes]
        gp[pl.ds(o + COLS, block), lanes] = grad
        held = flags[2, rows] * value
        acc[8 * BG : 8 * BG + 8, lanes] += eights(held * act[rows, lanes])
        acc[8 * BS : 8 * BS + 8, lanes] += eights(held)
        acc[8 * C1B : 8 * C1B + 8, lanes] += eights(flags[2, rows] * grad)

    convolve(ds2, K2R, True, SL, third, mid)

    def fourth(o, rows, lanes, value):
        slope[rows, lanes] = value

    convolve(gp, K1R, True, None, fourth, li)

    dwp_ref[...] = jnp.zeros_like(dwp_ref)
    cross[...] = jnp.zeros_like(cross)

    def back(step, carry):
        here = pl.multiple_of(step * TILE, TILE)
        o = pl.multiple_of(own_off + here, 128)

        here_wide = pl.ds(o, TILE)
        xhat, r = normalize(s1[here_wide])
        grad = slope[here_wide]
        grad_two = ds2[pl.ds(pl.multiple_of(o + COLS, COLS), TILE)]
        result = grad_two + normalize_back(grad * tab(N3G), xhat, r)
        ds1_ref[pl.ds(here, TILE)] = result
        add(N3G, eights(grad * xhat))
        add(N3S, eights(grad))
        add(SL, eights(grad_two * lo_[here_wide]))
        add(C2B, eights(grad_two))
        add(PB, eights(result))
        dmx = dot_nt(side(tab(SA) * result), wph[...])
        dmx_ref[pl.ds(here, TILE)] = dmx
        h, l = halves(result)
        dwp_ref[...] += dot_nn(side(mixed[pl.ds(o, TILE)].T), jnp.concatenate([h, h, l], axis=0))
        dmxt = side(dmx.T)
        for s, (lo, hi) in enumerate(spans):

            @pl.when((lo < o + TILE) & (hi > o))
            def _():
                vm = jnp.where(span_mask(o, TILE, lo, hi), v_ref[pl.ds(o, TILE)], 0.0)
                vh, vl = halves(vm)
                cross[s] += dot_nn(dmxt, jnp.concatenate([vh, vh, vl], axis=0))

        return carry

    lax.fori_loop(0, tokens // TILE, back, 0)
    for s in range(3):
        gprob_ref[s] = fold(cross[s])

    def total(r):
        return jnp.sum(acc[8 * r : 8 * r + 8], axis=0, keepdims=True)

    for r in (N3G, N3S, N2G, N2S, SL, SM, C1B, BG, BS, F2B, 40, 41, 42, 43):
        gtab_ref[r : r + 1] = total(r)
    for t in range(9):
        gtab_ref[K1R + t : K1R + t + 1] = total(K1R + t)
        gtab_ref[K2R + t : K2R + t + 1] = total(K2R + t) * tab(SL)
    gtab_ref[C2B : C2B + 1] = total(C2B) * tab(SL)
    gtab_ref[PB : PB + 1] = total(PB) * tab(SA)
    raw = dwp_ref[...]
    gtab_ref[SA : SA + 1] = jnp.sum(raw * wp_ref[...], axis=0, keepdims=True) + total(PB) * tab(PB)
    dwp_ref[...] = raw * tab(SA)
    for i in range(mlp // D):
        gtab_ref[F1B + i : F1B + i + 1] = jnp.sum(b1g_ref[:, i * D : i * D + D], axis=0, keepdims=True)


def middle(tall, temp, x, dy, v, halo, sums, peer, wp, w1, w2, tab):
    tokens = x.shape[0]
    wide = tokens + HALO
    mlp = w1.shape[1]
    smem = pl.BlockSpec(memory_space=pltpu.SMEM)
    vmem = pl.BlockSpec(memory_space=pltpu.VMEM)
    anywhere = pl.BlockSpec(memory_space=pl.ANY)

    def f(*shape):
        return jax.ShapeDtypeStruct(shape, F32)

    def s(*shape):
        return pltpu.VMEM(shape, F32)

    def b(*shape):
        return pltpu.VMEM(shape, BF)

    padded = s(wide + 2 * COLS, D)
    return pl.pallas_call(
        middle_kernel,
        out_shape=[
            f(tokens, D),
            f(tokens, D),
            f(tokens, D),
            f(D, D),
            f(2, D, mlp),
            f(TABLE, D),
            f(3, HD, D),
            f(3, HD, D),
            f(3, HD, D),
        ],
        in_specs=[smem, smem] + [anywhere] * 4 + [vmem] * 6,
        out_specs=[vmem] * 9,
        scratch_shapes=[
            b(3 * D, D),
            b(D, 3 * D),
            b(3 * D, mlp),
            b(mlp, 3 * D),
            b(3, D, 3 * D),
            s(wide, D),
            s(wide, D),
            padded,
            s(wide, D),
            s(wide, D),
            padded,
            s(wide, D),
            padded,
            padded,
            s(wide // 3, D),
            b(TILE, 3 * D),
            b(TILE, 3 * D),
            b(TILE, mlp),
            b(TILE, mlp),
            s(TILE, mlp),
            s(8, mlp),
            s(8, mlp),
            s(8 * TABLE, D),
            s(3, D, D),
            s(wide, D),
            s(wide, D),
            s(wide, D),
            s(3, wide, 128),
            b(D, 3 * TILE),
            b(D, 3 * TILE),
            pltpu.SemaphoreType.DMA((6,)),
        ],
        compiler_params=pltpu.CompilerParams(vmem_limit_bytes=60 << 20),
    )(tall, temp, x, dy, v, halo, sums, peer, wp, w1, w2, tab)


def finish_kernel(
    tall_ref,
    temp_ref,
    x_ref,
    q_ref,
    k_ref,
    ds1_ref,
    dmx_ref,
    sums_ref,
    peer_ref,
    probs_ref,
    unit_ref,
    gprob_ref,
    gpeer_ref,
    w_ref,
    tab_ref,
    gtab_ref,
    dwp_ref,
    dx_ref,
    dw_ref,
    otab_ref,
    wh,
    wl,
    pv,
    cv,
    ch,
    side_rows,
    acc,
    dqkv,
):
    step = pl.program_id(0)
    last = pl.num_programs(0) - 1
    core = lax.axis_index("rows")
    rows_all = 2 * pl.num_programs(0) * TILE // COLS
    spans = slots(tall_ref, core, core * (rows_all // 2), rows_all)
    start = step * TILE

    def tab(r):
        return tab_ref[r : r + 1]

    @pl.when(step == 0)
    def _():
        def part(o):
            h, l = halves(w_ref[pl.ds(o, 64)])
            wh[pl.ds(o, 64)] = h
            wl[pl.ds(o, 64)] = l

        sweep(D, 64, part)
        dw_ref[...] = jnp.zeros_like(dw_ref)
        dw_ref[1, :, D : 2 * D] = dwp_ref[...]
        acc[...] = jnp.zeros_like(acc)
        ones = group_ones()
        temp = head_row(temp_ref)
        heat = jnp.zeros((1, D), F32)
        for s in range(3):
            sums = sums_ref[s]
            grad = gprob_ref[s]
            if s == 2:
                sums = sums + peer_ref[...]
                grad = grad + gpeer_ref[...]
            inv_q = lax.rsqrt(sums[HD : HD + 1] + EPS)
            inv_k = lax.rsqrt(sums[HD + 1 : HD + 2] + EPS)
            probs = probs_ref[s]
            unit = unit_ref[s]
            scores = probs * (grad - group_sum(probs * grad, ones))
            part_heat = jnp.sum(scores * unit, axis=0, keepdims=True)
            heat = heat + (part_heat if s < 2 else jnp.where(core == 0, part_heat, 0.0))
            pull = temp * scores
            both = pull * unit
            side_rows[8 * s : 8 * s + 1] = fold_to_row(group_sum(both, ones)) * inv_q * inv_q
            side_rows[8 * s + 1 : 8 * s + 2] = jnp.sum(both, axis=0, keepdims=True) * inv_k * inv_k
            h, l = halves(unfold(pull * row_to_fold(inv_q, ones) * inv_k))
            cv[s, 0:D] = h
            cv[s, D : 2 * D] = h
            cv[s, 2 * D : 3 * D] = l
            ch[s, :, 0:D] = h
            ch[s, :, D : 2 * D] = h
            ch[s, :, 2 * D : 3 * D] = l
            h, l = halves(unfold(probs))
            pv[s, 0:D] = h
            pv[s, D : 2 * D] = h
            pv[s, 2 * D : 3 * D] = l
        otab_ref[...] = gtab_ref[...]
        otab_ref[44:45] = heat

    dqkv[...] = jnp.zeros_like(dqkv)
    for s, (lo, hi) in enumerate(spans):

        @pl.when((lo < start + TILE) & (hi > start))
        def _():
            mask = span_mask(start, TILE, lo, hi)
            qm = jnp.where(mask, q_ref[...], 0.0)
            km = jnp.where(mask, k_ref[...], 0.0)
            dm = jnp.where(mask, dmx_ref[...], 0.0)
            dqkv[:, 0:D] += dot_nt(side(km), ch[s]) - qm * side_rows[8 * s : 8 * s + 1]
            dqkv[:, D : 2 * D] += dot_nn(side(qm), cv[s]) - km * side_rows[8 * s + 1 : 8 * s + 2]
            dqkv[:, 2 * D : 3 * D] += dot_nn(side(dm), pv[s])

    h, l = halves(dqkv[...])
    dn = dot_nt(h, wh[...]) + (dot_nt(l, wh[...]) + dot_nt(h, wl[...]))
    xhat, r = normalize(x_ref[...])
    nt = side((xhat * tab(N1G) + tab(N1S)).T)
    grads = dot_nn(nt, jnp.concatenate([h, h, l], axis=0))
    dw_ref[0] += grads[:, 0 : 2 * D]
    dw_ref[1, :, 0:D] += grads[:, 2 * D : 3 * D]
    dx_ref[...] = ds1_ref[...] + normalize_back(dn * tab(N1G), xhat, r)
    acc[0:8] += eights(dn * xhat)
    acc[8:16] += eights(dn)
    for i in range(3):
        acc[16 + 8 * i : 24 + 8 * i] += eights(dqkv[:, i * D : i * D + D])

    @pl.when(step == last)
    def _():
        for i, r in enumerate((N1G, N1S, QB, KB, VB)):
            otab_ref[r : r + 1] = jnp.sum(acc[8 * i : 8 * i + 8], axis=0, keepdims=True)


def finish(tall, temp, x, q, k, ds1, dmx, sums, peer, probs, unit, gprob, gpeer, w, tab, gtab, dwp):
    tokens = x.shape[0]
    smem = pl.BlockSpec(memory_space=pltpu.SMEM)
    row = pl.BlockSpec((TILE, D), lambda i: (i, 0))

    def whole(v):
        return pl.BlockSpec(v.shape, lambda i: (0,) * v.ndim)

    fixed = (sums, peer, probs, unit, gprob, gpeer, w, tab, gtab, dwp)
    return pl.pallas_call(
        finish_kernel,
        grid=(tokens // TILE,),
        out_shape=[
            jax.ShapeDtypeStruct((tokens, D), F32),
            jax.ShapeDtypeStruct((2, D, 2 * D), F32),
            jax.ShapeDtypeStruct((TABLE, D), F32),
        ],
        in_specs=[smem, smem] + [row] * 5 + [whole(v) for v in fixed],
        out_specs=[
            row,
            pl.BlockSpec((2, D, 2 * D), lambda i: (0, 0, 0)),
            pl.BlockSpec((TABLE, D), lambda i: (0, 0)),
        ],
        scratch_shapes=[
            pltpu.VMEM((D, 3 * D), BF),
            pltpu.VMEM((D, 3 * D), BF),
            pltpu.VMEM((3, 3 * D, D), BF),
            pltpu.VMEM((3, 3 * D, D), BF),
            pltpu.VMEM((3, D, 3 * D), BF),
            pltpu.VMEM((24, D), F32),
            pltpu.VMEM((40, D), F32),
            pltpu.VMEM((TILE, 3 * D), F32),
        ],
        compiler_params=pltpu.CompilerParams(vmem_limit_bytes=60 << 20),
    )(tall, temp, x, q, k, ds1, dmx, *fixed)


PART = 2 * D
ORDERS = ((0, 1, 2, 3), (1, 2, 0, 3), (2, 0, 1, 3))
KEPT = PART // 16
LAND = (0, PART // 2, PART * 3 // 4, PART * 7 // 8)
TROWS = TABLE // 2


def reduce_kernel(
    mid_ref,
    end_ref,
    tab_ref,
    all_ref,
    otab_ref,
    buf,
    first,
    land,
    tbuf,
    tland,
    own_sem,
    pair_send,
    pair_recv,
    send_sem,
    recv_sem,
    back_send,
    back_recv,
    tsend,
    trecv,
    out_sem,
    out_send,
    out_recv,
):
    core = lax.axis_index("rows")
    chip = lax.axis_index("canvas")
    bits = (lax.axis_size("canvas") - 1).bit_length()
    mine = [lax.rem(lax.div(chip, 1 << b), 2) for b in range(bits)]
    there = [{"canvas": chip + (1 - 2 * mine[b]) * (1 << b)} for b in range(bits)]
    twin = {"rows": 1 - core}
    barrier = pltpu.get_barrier_semaphore()
    for other in [twin] + there:
        pl.semaphore_signal(barrier, inc=1, device_id=other, device_id_type=MESH_ID)

    def remote(src, dst, send, recv, other):
        copy = pltpu.make_async_remote_copy(
            src_ref=src,
            dst_ref=dst,
            send_sem=send,
            recv_sem=recv,
            device_id=other,
            device_id_type=MESH_ID,
        )
        copy.start()
        return copy

    def block(which, i):
        if i < 2:
            return end_ref.at[which, :, i * D : i * D + D]
        return mid_ref.at[which, :, (i - 2) * D : (i - 1) * D]

    def place(ref, i):
        p, q = ((2, i) if i < 2 else ((i - 2) // 2, i % 2))
        return ref.at[p, pl.ds(q * D, D)]

    turns = (2, 4, 0, 3, 5, 1)
    own = {}
    for n, i in enumerate(turns):
        own[i] = pltpu.make_async_copy(block(core, i), place(buf, i), own_sem.at[i])
        own[i].start()
    town = pltpu.make_async_copy(
        tab_ref.at[pl.ds(pl.multiple_of(core * TROWS, 8), TROWS)], tbuf, own_sem.at[6]
    )
    town.start()
    pl.semaphore_wait(barrier, bits + 1)
    pair = {}
    for i in turns:
        pair[i] = remote(block(1 - core, i), place(first, i), pair_send.at[i], pair_recv.at[i], twin)
    tpair = remote(
        tab_ref.at[pl.ds(pl.multiple_of((1 - core) * TROWS, 8), TROWS)],
        tland.at[bits],
        tsend.at[bits],
        trecv.at[bits],
        twin,
    )

    def accumulate(p, at, src, src_at, rows):
        size = min(rows, 96)

        def one(i, carry):
            here = pl.ds(pl.multiple_of(at + i * size, 16), size)
            buf[p, here] += src[p, pl.ds(pl.multiple_of(src_at + i * size, 16), size)]
            return carry

        lax.fori_loop(0, rows // size, one, 0)

    start = [0, 0, 0]
    moves = {}

    def send(p, s):
        b = ORDERS[p][s]
        half = PART >> (s + 1)
        away = pl.multiple_of(start[p] + (1 - mine[b]) * half, 16)
        moves[p, s] = remote(
            buf.at[p, pl.ds(away, half)],
            land.at[p, pl.ds(LAND[s], half)],
            send_sem.at[p, s],
            recv_sem.at[p, s],
            there[b],
        )
        start[p] = start[p] + mine[b] * half

    for p in range(3):
        for i in ((2, 3), (4, 5), (0, 1))[p]:
            own[i].wait()
            pair[i].wait()
        accumulate(p, 0, first, 0, PART)
        send(p, 0)
    town.wait()
    tpair.wait()
    tbuf[...] += tland[bits]
    for s in range(4):
        tmove = remote(tbuf, tland.at[s], tsend.at[s], trecv.at[s], there[s])
        for p in range(3):
            moves[p, s].wait()
            accumulate(p, start[p], land, LAND[s], PART >> (s + 1))
            if s < 3:
                send(p, s + 1)
        tmove.wait()
        tbuf[...] += tland[s]
    for b in range(4, bits):
        for p in range(3):
            extra = remote(
                buf.at[p, pl.ds(pl.multiple_of(start[p], 16), KEPT)],
                land.at[p, pl.ds(PART + (b - 4) * KEPT, KEPT)],
                send_sem.at[p, b],
                recv_sem.at[p, b],
                there[b],
            )
            extra.wait()
            accumulate(p, start[p], land, PART + (b - 4) * KEPT, KEPT)
        tmove = remote(tbuf, tland.at[b], tsend.at[b], trecv.at[b], there[b])
        tmove.wait()
        tbuf[...] += tland[b]
    half = pl.ds(pl.multiple_of(core * TROWS, 8), TROWS)
    outs = [
        pltpu.make_async_copy(tbuf, otab_ref.at[half], out_sem.at[6]),
        remote(tbuf, otab_ref.at[half], out_send.at[6], out_recv.at[6], twin),
    ]
    outs[0].start()

    def share(p, s):
        b = ORDERS[p][s]
        rows = PART >> (s + 1)
        held = pl.ds(pl.multiple_of(start[p], 16), rows)
        moves[p, s] = remote(
            first.at[p, held], first.at[p, held], back_send.at[p, s], back_recv.at[p, s], there[b]
        )
        start[p] = start[p] - mine[b] * rows

    for p in range(3):
        held = pl.ds(pl.multiple_of(start[p], 16), KEPT)
        first[p, held] = buf[p, held]
        share(p, 3)
    for s in range(3, -1, -1):
        for p in range(3):
            moves[p, s].wait()
            if s > 0:
                share(p, s - 1)
            else:
                for i in ((2, 3), (4, 5), (0, 1))[p]:
                    src, dst = place(first, i), all_ref.at[core, :, i * D : i * D + D]
                    local = pltpu.make_async_copy(src, dst, out_sem.at[i])
                    local.start()
                    outs += [local, remote(src, dst, out_send.at[i], out_recv.at[i], twin)]
    for copy in outs:
        copy.wait()


def reduce_all(mid, end, tab):
    bits = (lax.axis_size("canvas") - 1).bit_length()
    anywhere = pl.BlockSpec(memory_space=pl.ANY)
    dma = pltpu.SemaphoreType.DMA
    steps = max(bits, 4)
    return pl.pallas_call(
        reduce_kernel,
        out_shape=[
            jax.ShapeDtypeStruct((2, D, 6 * D), F32),
            jax.ShapeDtypeStruct((TABLE, D), F32),
        ],
        in_specs=[anywhere] * 3,
        out_specs=[anywhere] * 2,
        scratch_shapes=[
            pltpu.VMEM((3, PART, D), F32),
            pltpu.VMEM((3, PART, D), F32),
            pltpu.VMEM((3, PART + (steps - 4) * KEPT, D), F32),
            pltpu.VMEM((TROWS, D), F32),
            pltpu.VMEM((bits + 1, TROWS, D), F32),
            dma((7,)),
            dma((6,)),
            dma((6,)),
            dma((3, steps)),
            dma((3, steps)),
            dma((3, 4)),
            dma((3, 4)),
            dma((bits + 1,)),
            dma((bits + 1,)),
            dma((7,)),
            dma((7,)),
            dma((7,)),
        ],
        compiler_params=pltpu.CompilerParams(
            collective_id=3, has_side_effects=True, vmem_limit_bytes=60 << 20
        ),
    )(mid, end, tab)


def orth_kernel(
    all_hbm,
    mq_hbm,
    mp_hbm,
    m1_hbm,
    m2_hbm,
    gq_out,
    gp_out,
    g1_out,
    g2_out,
    nq_out,
    np_out,
    n1_out,
    n2_out,
    orth_ref,
    low,
    high,
    nat,
    mq,
    mp,
    m1,
    m2,
    xs,
    in_sem,
    out_sem,
):
    core = lax.axis_index("rows")
    blocks = m1.shape[1] // D
    pairs = (
        (all_hbm.at[0], low),
        (all_hbm.at[1], high),
        (mq_hbm, mq),
        (mp_hbm, mp),
        (m1_hbm, m1),
        (m2_hbm, m2),
    )
    loads = [pltpu.make_async_copy(a, b, in_sem.at[i]) for i, (a, b) in enumerate(pairs)]
    for load in loads:
        load.start()
    for load in loads:
        load.wait()
    outs = []

    def store(src, dst):
        outs.append(pltpu.make_async_copy(src, dst, out_sem.at[len(outs)]))
        outs[-1].start()

    store(low.at[:, 0 : 2 * D], gq_out.at[:, 0 : 2 * D])
    store(high.at[:, 0:D], gq_out.at[:, 2 * D : 3 * D])
    store(high.at[:, D : 2 * D], gp_out)
    store(low.at[:, 2 * D : 6 * D], g1_out)
    for b in range(blocks):
        nat[b * D : b * D + D] = high[:, (2 + b) * D : (3 + b) * D].T
    store(nat, g2_out)

    def small(o):
        rows = pl.ds(o, 64)
        mq[rows, 0 : 2 * D] = MUON_KEEP * mq[rows, 0 : 2 * D] + low[rows, 0 : 2 * D]
        mq[rows, 2 * D : 3 * D] = MUON_KEEP * mq[rows, 2 * D : 3 * D] + high[rows, 0:D]
        mp[rows] = MUON_KEEP * mp[rows] + high[rows, D : 2 * D]
        m1[rows] = MUON_KEEP * m1[rows] + low[rows, 2 * D : 6 * D]

    sweep(D, 64, small)

    def large(o):
        rows = pl.ds(o, 128)
        m2[rows] = MUON_KEEP * m2[rows] + nat[rows]

    sweep(blocks * D, 128, large)
    store(mq, nq_out)
    store(mp, np_out)
    store(m1, n1_out)
    store(m2, n2_out)

    @pl.when(core == 0)
    def _():
        xs[0] = mq[:, 0:D]
        xs[1] = mq[:, D : 2 * D]
        for b in range(blocks):
            xs[2 + b] = m1[:, b * D : b * D + D]

    @pl.when(core == 1)
    def _():
        xs[0] = mq[:, 2 * D : 3 * D]
        xs[1] = mp[...]
        for b in range(blocks):
            xs[2 + b] = m2[b * D : b * D + D].T

    def squares(v):
        return jnp.sum(jnp.sum(v * v, axis=0, keepdims=True), axis=1, keepdims=True)

    groups = ((0,), (1,), tuple(range(2, 2 + blocks)))
    for g in groups:
        norm = squares(xs[g[0]])
        for b in g[1:]:
            norm = norm + squares(xs[b])
        inv = 1.0 / (jnp.sqrt(norm) + 1e-07)
        for b in g:
            xs[b] = xs[b] * inv

    def step(i, carry):
        for g in groups:
            left, right = [], []
            for b in g:
                h, l = halves(xs[b])
                left += [h, l, h]
                right += [h, h, l]
            gram = dot_nt(jnp.concatenate(left, axis=1), jnp.concatenate(right, axis=1))
            h, l = halves(gram)
            square = dot_nn(jnp.concatenate([h, l, h], axis=1), jnp.concatenate([h, h, l], axis=0))
            poly = side(-4.775 * gram + 2.0315 * square)
            for b in g:
                h, l = halves(xs[b])
                xs[b] = 3.4445 * xs[b] + dot_nn(poly, jnp.concatenate([h, h, l], axis=0))
        return carry

    lax.fori_loop(0, 5, step, 0)

    @pl.when(core == 0)
    def _():
        orth_ref[...] = xs[...]

    @pl.when(core == 1)
    def _():
        orth_ref[0:2] = xs[0:2]
        for b in range(blocks):
            orth_ref[2 + b] = xs[2 + b].T

    for copy in outs:
        copy.wait()


def orthogonalize(everything, mq, mp, m1, m2):
    anywhere = pl.BlockSpec(memory_space=pl.ANY)
    args = (mq, mp, m1, m2)
    blocks = 2 + m1.shape[1] // D
    return pl.pallas_call(
        orth_kernel,
        out_shape=[jax.ShapeDtypeStruct(a.shape, F32) for a in args + args]
        + [jax.ShapeDtypeStruct((blocks, D, D), F32)],
        in_specs=[anywhere] * 5,
        out_specs=[anywhere] * 8 + [pl.BlockSpec(memory_space=pltpu.VMEM)],
        scratch_shapes=[
            pltpu.VMEM(everything.shape[1:], F32),
            pltpu.VMEM(everything.shape[1:], F32),
            pltpu.VMEM(m2.shape, F32),
            pltpu.VMEM(mq.shape, F32),
            pltpu.VMEM(mp.shape, F32),
            pltpu.VMEM(m1.shape, F32),
            pltpu.VMEM(m2.shape, F32),
            pltpu.VMEM((blocks, D, D), F32),
            pltpu.SemaphoreType.DMA((6,)),
            pltpu.SemaphoreType.DMA((9,)),
        ],
        compiler_params=pltpu.CompilerParams(vmem_limit_bytes=60 << 20),
    )(everything, *args)


def pair_kernel(own_ref, both_ref, own_sem, send_sem, recv_sem):
    core = lax.axis_index("rows")
    barrier = pltpu.get_barrier_semaphore()
    pl.semaphore_signal(barrier, inc=1, device_id={"rows": 1 - core}, device_id_type=MESH_ID)
    local = pltpu.make_async_copy(own_ref, both_ref.at[core], own_sem)
    local.start()
    pl.semaphore_wait(barrier, 1)
    copy = pltpu.make_async_remote_copy(
        src_ref=own_ref,
        dst_ref=both_ref.at[core],
        send_sem=send_sem,
        recv_sem=recv_sem,
        device_id={"rows": 1 - core},
        device_id_type=MESH_ID,
    )
    copy.start()
    local.wait()
    copy.wait()


def pair_up(own):
    dma = pltpu.SemaphoreType.DMA
    return pl.pallas_call(
        pair_kernel,
        out_shape=jax.ShapeDtypeStruct((2,) + own.shape, F32),
        in_specs=[pl.BlockSpec(memory_space=pltpu.VMEM)],
        out_specs=pl.BlockSpec(memory_space=pl.ANY),
        scratch_shapes=[dma, dma, dma],
        compiler_params=pltpu.CompilerParams(
            collective_id=2, has_side_effects=True, vmem_limit_bytes=60 << 20
        ),
    )(own)


def moment_step(current, one, two, gradient):
    first = BETA1 * one + (1.0 - BETA1) * gradient
    second = BETA2 * two + (1.0 - BETA2) * gradient * gradient
    fix_one = 1.0 - BETA1**STEP
    fix_two = 1.0 - BETA2**STEP
    updated = current - ADAM_RATE * (first / fix_one) / (jnp.sqrt(second / fix_two) + ADAM_FLOOR)
    return first, second, updated


def update_kernel(
    rows_ref,
    last_ref,
    wq_ref,
    wp_ref,
    w1_ref,
    w2_ref,
    tab_ref,
    one_ref,
    two_ref,
    gtab_ref,
    nq_ref,
    np_ref,
    n1_ref,
    n2_ref,
    cq_ref,
    cp_ref,
    c1_ref,
    c2_ref,
    first_ref,
    second_ref,
    small_ref,
):
    mlp = w1_ref.shape[1]

    def put(new_ref, copy_ref, w, orth, large, lanes):
        new = w * (1.0 - MUON_RATE * DECAY) - MUON_RATE * 0.2 * math.sqrt(large) * orth
        new_ref[:, lanes] = new
        copy_ref[:, lanes] = new.astype(BF)

    for i in range(3):
        lanes = slice(i * D, i * D + D)
        orth = rows_ref[0, i] if i < 2 else rows_ref[1, 0]
        put(nq_ref, cq_ref, wq_ref[:, lanes], orth, D, lanes)
    put(np_ref, cp_ref, wp_ref[...], rows_ref[1, 1], D, slice(0, D))
    for i in range(mlp // D):
        lanes = slice(i * D, i * D + D)
        put(n1_ref, c1_ref, w1_ref[:, lanes], rows_ref[0, 2 + i], mlp, lanes)
    put(n2_ref, c2_ref, w2_ref[...], last_ref[0, 0], mlp, slice(0, D))
    first, second, small = moment_step(tab_ref[...], one_ref[...], two_ref[...], gtab_ref[0:SMALL])
    first_ref[...] = first
    second_ref[...] = second
    small_ref[...] = small


def update(both, wq, wp, w1, w2, tab, one, two, gtab):
    steps = w2.shape[0] // D
    piece = D // steps

    def rows(v):
        size = v.shape[0] // steps
        return pl.BlockSpec((size, v.shape[1]), lambda i: (i, 0))

    def whole(v):
        return pl.BlockSpec(v.shape, lambda i: (0, 0))

    weights = (wq, wp, w1, w2)
    return pl.pallas_call(
        update_kernel,
        grid=(steps,),
        out_shape=[jax.ShapeDtypeStruct(w.shape, F32) for w in weights]
        + [jax.ShapeDtypeStruct(w.shape, BF) for w in weights]
        + [jax.ShapeDtypeStruct(tab.shape, F32)] * 3,
        in_specs=[
            pl.BlockSpec((2, 2 + steps, piece, D), lambda i: (0, 0, i, 0)),
            pl.BlockSpec((1, 1, D, D), lambda i: (1, 2 + i, 0, 0)),
        ]
        + [rows(w) for w in weights]
        + [whole(v) for v in (tab, one, two, gtab)],
        out_specs=[rows(w) for w in weights] * 2 + [whole(tab)] * 3,
        compiler_params=pltpu.CompilerParams(vmem_limit_bytes=60 << 20),
    )(both, both, *weights, tab, one, two, gtab)


def on_device(
    x4, dy4, tall, wqkv, wp, w1, w2, mqkv, mp, m1, m2, tab, tab_one, tab_two, temp, temp_one, temp_two
):
    shape = x4.shape
    tokens = shape[1] * shape[2]
    x = x4.reshape(tokens, D)
    dy = dy4.reshape(tokens, D)
    q, k, v, sums = project(tall, x, wqkv, tab)
    halo, peer = widen(x, dy, v, sums)
    out, ds1, dmx, dwp, mid, gtab, probs, unit, gprob = middle(
        tall, temp, x, dy, v, halo, sums, peer, wp, w1, w2, tab
    )
    gpeer = swap(gprob, 1)
    dx, end, gtab = finish(
        tall, temp, x, q, k, ds1, dmx, sums, peer, probs, unit, gprob, gpeer, wqkv, tab, gtab, dwp
    )
    everything, gtab = reduce_all(mid, end, gtab)
    *grads, orth = orthogonalize(everything, mqkv, mp, m1, m2)
    results = update(pair_up(orth), wqkv, wp, w1, w2, tab, tab_one, tab_two, gtab)
    heat = jnp.sum(gtab[44].reshape(HEADS, HD), axis=1)
    warm = moment_step(temp, temp_one, temp_two, heat)
    count = tokens * D * lax.axis_size("rows") * lax.axis_size("canvas")
    rms = jnp.sqrt(jnp.sum(gtab[40:44], axis=1) / count)
    return (out.reshape(shape), dx.reshape(shape), *grads, *results, *warm, rms)


def solution(mesh):
    split = P("canvas", "rows", None, None)
    return jax.shard_map(
        on_device,
        mesh=mesh,
        in_specs=(split, split, P("canvas", None)) + (P(),) * 14,
        out_specs=(split, split) + (P(),) * 23,
        check_vma=False,
    )
```

```python
import math

import jax
import jax.numpy as jnp
from jax import lax
from jax.experimental import pallas as pl
from jax.experimental.pallas import tpu as pltpu
from jax.sharding import PartitionSpec as P

BF = jnp.bfloat16
F32 = jnp.float32
MESH_ID = pl.DeviceIdType.MESH

EPS = 1e-06
ROOT_HALF = 1.0 / math.sqrt(2.0)
ROOT_TWOPI = 1.0 / math.sqrt(2.0 * math.pi)
STEP = 10
MUON_RATE = 0.2
MUON_KEEP = 0.95
DECAY = 0.01
ADAM_RATE = 0.2
BETA1 = 0.9
BETA2 = 0.95
ADAM_FLOOR = 1e-08

HEADS = 8
HD = 48
D = HEADS * HD
COLS = 32
HALO = 4 * COLS
TILE = 256

N1G, N1S, N3G, N3S, N2G, N2S, SA, SL, SM, QB, KB, VB, PB, C1B, BG, BS, C2B, F2B = range(18)
F1B, K1R, K2R = 18, 22, 31
SMALL = 40
TABLE = 48


def halves(v):
    hi = v.astype(BF)
    return hi, (v - hi.astype(F32)).astype(BF)


def side(v):
    h, l = halves(v)
    return jnp.concatenate([h, l, h], axis=1)


def dot_nn(a, b):
    return lax.dot_general(a, b, (((1,), (0,)), ((), ())), preferred_element_type=F32)


def dot_nt(a, b):
    return lax.dot_general(a, b, (((1,), (1,)), ((), ())), preferred_element_type=F32)


def normalize(v):
    mean = jnp.mean(v, axis=1, keepdims=True)
    c = v - mean
    r = lax.rsqrt(jnp.mean(c * c, axis=1, keepdims=True) + EPS)
    return c * r, r


def normalize_back(e, xhat, r):
    return r * (
        e - jnp.mean(e, axis=1, keepdims=True) - xhat * jnp.mean(e * xhat, axis=1, keepdims=True)
    )


def gelu_parts(v):
    phi = 0.5 * (1.0 + lax.erf(v * ROOT_HALF))
    return v * phi, phi + v * jnp.exp(-0.5 * v * v) * ROOT_TWOPI


def eights(v):
    total = v[0:8]
    for i in range(8, v.shape[0], 8):
        total = total + v[i : i + 8]
    return total


def sweep(count, size, body):
    def one(i, carry):
        body(pl.multiple_of(i * size, size))
        return carry

    lax.fori_loop(0, count // size, one, 0)


def image_ends(tall_ref):
    e0 = tall_ref[0, 0]
    e1 = e0 + tall_ref[0, 1]
    return e0, e1, e1 + tall_ref[0, 2]


def slots(tall_ref, core, first_row, rows_all):
    e0, e1, e2 = image_ends(tall_ref)
    low = (jnp.where(core == 0, 0, e2), jnp.where(core == 0, e0, 0), e1)
    high = (jnp.where(core == 0, e0, rows_all), jnp.where(core == 0, e1, 0), e2)
    return [((a - first_row) * COLS, (b - first_row) * COLS) for a, b in zip(low, high)]


def span_mask(start, rows, lo, hi):
    token = start + lax.broadcasted_iota(jnp.int32, (rows, D), 0)
    return (token >= lo) & (token < hi)


def lane_head():
    return lax.broadcasted_iota(jnp.int32, (HD, D), 1) // HD


def lane_slot():
    return lax.broadcasted_iota(jnp.int32, (HD, D), 1) % HD


def fold(full):
    head = lane_head()
    total = jnp.where(head == 0, full[0:HD], 0.0)
    for h in range(1, HEADS):
        total = total + jnp.where(head == h, full[h * HD : h * HD + HD], 0.0)
    return total


def unfold(small):
    head = lane_head()
    return jnp.concatenate([jnp.where(head == h, small, 0.0) for h in range(HEADS)], axis=0)


def group_ones():
    a = lax.broadcasted_iota(jnp.int32, (D, D), 0) // HD
    b = lax.broadcasted_iota(jnp.int32, (D, D), 1) // HD
    return jnp.where(a == b, 1.0, 0.0).astype(BF)


def group_sum(v, ones):
    h = v.astype(BF)
    rest = v - h.astype(F32)
    m = rest.astype(BF)
    l = (rest - m.astype(F32)).astype(BF)
    return dot_nn(h, ones) + (dot_nn(m, ones) + dot_nn(l, ones))


def row_to_fold(row, ones):
    slot = lax.broadcasted_iota(jnp.int32, (HD, D), 0)
    return group_sum(jnp.where(lane_slot() == slot, jnp.broadcast_to(row, (HD, D)), 0.0), ones)


def fold_to_row(small):
    slot = lax.broadcasted_iota(jnp.int32, (HD, D), 0)
    return jnp.sum(jnp.where(lane_slot() == slot, small, 0.0), axis=0, keepdims=True)


def head_row(temp_ref):
    head = lax.broadcasted_iota(jnp.int32, (1, D), 1) // HD
    row = jnp.where(head == 0, temp_ref[0], 0.0)
    for h in range(1, HEADS):
        row = row + jnp.where(head == h, temp_ref[h], 0.0)
    return row


def project_kernel(tall_ref, x_ref, w_ref, tab_ref, q_ref, k_ref, v_ref, sums_ref, wcat, cross):
    step = pl.program_id(0)
    core = lax.axis_index("rows")
    rows_all = 2 * pl.num_programs(0) * TILE // COLS
    spans = slots(tall_ref, core, core * (rows_all // 2), rows_all)
    start = step * TILE

    @pl.when(step == 0)
    def _():
        def part(o):
            h, l = halves(w_ref[pl.ds(o, 64)])
            wcat[pl.ds(o, 64)] = h
            wcat[pl.ds(D + o, 64)] = h
            wcat[pl.ds(2 * D + o, 64)] = l

        sweep(D, 64, part)
        cross[...] = jnp.zeros_like(cross)
        sums_ref[...] = jnp.zeros_like(sums_ref)

    xhat, _ = normalize(x_ref[...])
    lhs = side(xhat * tab_ref[N1G : N1G + 1] + tab_ref[N1S : N1S + 1])
    q = dot_nn(lhs, wcat[:, 0:D]) + tab_ref[QB : QB + 1]
    q_ref[...] = q
    k = dot_nn(lhs, wcat[:, D : 2 * D]) + tab_ref[KB : KB + 1]
    k_ref[...] = k
    v_ref[...] = dot_nn(lhs, wcat[:, 2 * D : 3 * D]) + tab_ref[VB : VB + 1]
    qt = side(q.T)
    for s, (lo, hi) in enumerate(spans):

        @pl.when((lo < start + TILE) & (hi > start))
        def _():
            mask = span_mask(start, TILE, lo, hi)
            kh, kl = halves(jnp.where(mask, k_ref[...], 0.0))
            cross[s] += dot_nn(qt, jnp.concatenate([kh, kh, kl], axis=0))
            qm = jnp.where(mask, q_ref[...], 0.0)
            km = jnp.where(mask, k_ref[...], 0.0)
            sums_ref[s, HD : HD + 1] += jnp.sum(qm * qm, axis=0, keepdims=True)
            sums_ref[s, HD + 1 : HD + 2] += jnp.sum(km * km, axis=0, keepdims=True)

    @pl.when(step == pl.num_programs(0) - 1)
    def _():
        for s in range(3):
            sums_ref[s, 0:HD] = fold(cross[s])


def project(tall, x, w, tab):
    tokens = x.shape[0]
    row = pl.BlockSpec((TILE, D), lambda i: (i, 0))
    return pl.pallas_call(
        project_kernel,
        grid=(tokens // TILE,),
        out_shape=[jax.ShapeDtypeStruct((tokens, D), F32)] * 3
        + [jax.ShapeDtypeStruct((3, HD + 8, D), F32)],
        in_specs=[
            pl.BlockSpec(memory_space=pltpu.SMEM),
            row,
            pl.BlockSpec((D, 3 * D), lambda i: (0, 0)),
            pl.BlockSpec((SMALL, D), lambda i: (0, 0)),
        ],
        out_specs=[row, row, row, pl.BlockSpec((3, HD + 8, D), lambda i: (0, 0, 0))],
        scratch_shapes=[pltpu.VMEM((3 * D, 3 * D), BF), pltpu.VMEM((3, D, D), F32)],
        compiler_params=pltpu.CompilerParams(vmem_limit_bytes=60 << 20),
    )(tall, x, w, tab)


def widen_kernel(x_ref, dy_ref, v_ref, sums_ref, halo_ref, peer_ref, send_sem, recv_sem):
    core = lax.axis_index("rows")
    tokens = x_ref.shape[0]
    barrier = pltpu.get_barrier_semaphore()
    pl.semaphore_signal(barrier, inc=1, device_id={"rows": 1 - core}, device_id_type=MESH_ID)
    pl.semaphore_wait(barrier, 1)
    edge = pl.ds(pl.multiple_of((1 - core) * (tokens - HALO), HALO), HALO)
    pairs = [(src.at[edge], halo_ref.at[i]) for i, src in enumerate((x_ref, dy_ref, v_ref))]
    pairs.append((sums_ref.at[2], peer_ref))
    copies = []
    for i, (src, dst) in enumerate(pairs):
        copies.append(
            pltpu.make_async_remote_copy(
                src_ref=src,
                dst_ref=dst,
                send_sem=send_sem.at[i],
                recv_sem=recv_sem.at[i],
                device_id={"rows": 1 - core},
                device_id_type=MESH_ID,
            )
        )
        copies[-1].start()
    for copy in copies:
        copy.wait()


def widen(x, dy, v, sums):
    anywhere = pl.BlockSpec(memory_space=pl.ANY)
    return pl.pallas_call(
        widen_kernel,
        out_shape=[
            jax.ShapeDtypeStruct((3, HALO, D), F32),
            jax.ShapeDtypeStruct(sums.shape[1:], F32),
        ],
        in_specs=[anywhere] * 4,
        out_specs=[anywhere] * 2,
        scratch_shapes=[pltpu.SemaphoreType.DMA((4,)), pltpu.SemaphoreType.DMA((4,))],
        compiler_params=pltpu.CompilerParams(collective_id=0, has_side_effects=True),
    )(x, dy, v, sums)


def row_flags(tall_ref, rows_all):
    ends = image_ends(tall_ref)

    def above(row):
        first = (row == 0) | (row == ends[0]) | (row == ends[1]) | (row == ends[2])
        return jnp.where(first, 0.0, 1.0)

    def below(row):
        return jnp.where(row + 1 == rows_all, 0.0, above(row + 1))

    return above, below


def middle_kernel(
    tall_ref,
    temp_ref,
    x_hbm,
    dy_hbm,
    v_hbm,
    halo_hbm,
    sums_ref,
    peer_ref,
    wp_ref,
    w1_ref,
    w2_ref,
    tab_ref,
    out_ref,
    ds1_ref,
    dmx_ref,
    dwp_ref,
    dw_ref,
    gtab_ref,
    probs_ref,
    unit_ref,
    gprob_ref,
    wpv,
    wph,
    w1c,
    w2c,
    pcat,
    mixed,
    s1,
    li,
    act,
    slope,
    mid,
    s2,
    ds2,
    gp,
    z,
    n2c,
    dzc,
    hid_h,
    hid_l,
    hslope,
    b1_ref,
    b1g_ref,
    acc,
    cross,
    x_ref,
    dy_ref,
    v_ref,
    flags,
    nt,
    dt,
    load_sem,
):
    core = lax.axis_index("rows")
    wide = x_ref.shape[0]
    tokens = wide - HALO
    dw1_ref, dw2_ref = dw_ref.at[0], dw_ref.at[1]
    lo_ = x_ref
    loads = []
    for i, (src, dst) in enumerate(((x_hbm, x_ref), (dy_hbm, dy_ref), (v_hbm, v_ref))):
        own = pl.ds(pl.multiple_of(core * HALO, HALO), tokens)
        far = pl.ds(pl.multiple_of((1 - core) * tokens, HALO), HALO)
        loads.append(pltpu.make_async_copy(src, dst.at[own], load_sem.at[2 * i]))
        loads.append(pltpu.make_async_copy(halo_hbm.at[i], dst.at[far], load_sem.at[2 * i + 1]))
    for load in loads:
        load.start()
    own_rows = tokens // COLS
    rows_wide = wide // COLS
    rows_all = 2 * own_rows
    first_row = core * (own_rows - HALO // COLS)
    own_off = pl.multiple_of(core * HALO, HALO)
    mlp = w1_ref.shape[1]
    spans = slots(tall_ref, core, first_row, rows_all)
    above, below = row_flags(tall_ref, rows_all)

    def tab(r):
        return tab_ref[r : r + 1]

    def is_own(row):
        return (row >= core * (HALO // COLS)) & (row < core * (HALO // COLS) + own_rows)

    def part_p(o):
        rows = pl.ds(o, 192)
        h, l = halves(wp_ref[rows])
        wpv[rows] = h
        wpv[pl.ds(D + o, 192)] = h
        wpv[pl.ds(2 * D + o, 192)] = l
        wph[rows, 0:D] = h
        wph[rows, D : 2 * D] = h
        wph[rows, 2 * D : 3 * D] = l

    sweep(D, 192, part_p)

    def part_1(o):
        rows = pl.ds(o, 64)
        h, l = halves(w1_ref[rows])
        w1c[rows] = h
        w1c[pl.ds(D + o, 64)] = h
        w1c[pl.ds(2 * D + o, 64)] = l

    sweep(D, 64, part_1)

    def part_2(o):
        rows = pl.ds(o, 256)
        h, l = halves(w2_ref[rows])
        w2c[rows, 0:D] = h
        w2c[rows, D : 2 * D] = h
        w2c[rows, 2 * D : 3 * D] = l

    sweep(mlp, 256, part_2)

    ones = group_ones()
    temp = head_row(temp_ref)
    for s in range(3):
        sums = sums_ref[s]
        if s == 2:
            sums = sums + peer_ref[...]
        inv_q = lax.rsqrt(sums[HD : HD + 1] + EPS)
        inv_k = lax.rsqrt(sums[HD + 1 : HD + 2] + EPS)
        unit = sums[0:HD] * row_to_fold(inv_q, ones) * inv_k
        unit_ref[s] = unit
        weight = jnp.exp(temp * unit)
        probs = weight / group_sum(weight, ones)
        probs_ref[s] = probs
        h, l = halves(unfold(probs))
        pcat[s, :, 0:D] = h
        pcat[s, :, D : 2 * D] = h
        pcat[s, :, 2 * D : 3 * D] = l

    acc[...] = jnp.zeros_like(acc)
    gtab_ref[...] = jnp.zeros_like(gtab_ref)

    def add(r, v):
        acc[8 * r : 8 * r + 8] += v

    for load in loads:
        load.wait()

    def own_part(o, size):
        token = o + lax.broadcasted_iota(jnp.int32, (size, D), 0)
        return jnp.where((token >= own_off) & (token < own_off + tokens), 1.0, 0.0)

    def attend(o):
        size = wide // 3
        mixed[pl.ds(o, size)] = jnp.zeros((size, D), F32)
        for s, (lo, hi) in enumerate(spans):

            @pl.when((lo < o + size) & (hi > o))
            def _():
                vm = jnp.where(span_mask(o, size, lo, hi), v_ref[pl.ds(o, size)], 0.0)
                mixed[pl.ds(o, size)] += dot_nt(side(vm), pcat[s])

        z[...] = dot_nn(side(mixed[pl.ds(o, size)]), wpv[...]) + tab(PB)
        rows = pl.ds(o, size)
        branch = tab(SA) * z[...]
        stream = x_ref[rows] + branch
        s1[rows] = stream
        xhat, _ = normalize(stream)
        li[pl.ds(pl.multiple_of(o + COLS, COLS), size)] = xhat * tab(N3G) + tab(N3S)
        add(41, eights(own_part(o, size) * branch * branch))

    sweep(wide, wide // 3, attend)

    pad = jnp.zeros((COLS, D), F32)
    for buf in (li, mid, gp, ds2):
        buf[0:COLS] = pad
        buf[wide + COLS : wide + 2 * COLS] = pad

    for r in range(rows_wide):
        row = first_row + r
        mine = jnp.where(is_own(r), 1.0, 0.0)
        for n, flag in enumerate((above(row), below(row), mine)):
            flags[n, r * COLS : r * COLS + COLS] = jnp.full((COLS, 128), flag, F32)

    block = 12 * COLS
    col = lax.rem(lax.broadcasted_iota(jnp.int32, (block + 2 * COLS, 128), 0), COLS)

    def convolve(src, base, flip, scale, visit, other=None):
        def one(n, carry):
            lanes = pl.ds(pl.multiple_of(lax.rem(n, 3) * 128, 128), 128)
            o = pl.multiple_of(lax.div(n, 3) * block, block)
            rows = pl.ds(o, block)
            taps = [tab_ref[base + t : base + t + 1, lanes] for t in range(9)]
            if flip:
                taps = taps[::-1]
            if scale is not None:
                taps = [t * tab_ref[scale : scale + 1, lanes] for t in taps]
            u = src[pl.ds(o, block + 2 * COLS), lanes]
            left = jnp.where(col == 0, 0.0, pltpu.roll(u, 1, 0))
            right = jnp.where(col == COLS - 1, 0.0, pltpu.roll(u, block + 2 * COLS - 1, 0))
            up, down = flags[0, rows], flags[1, rows]

            def line(a):
                cut = slice(a * COLS, a * COLS + block)
                return left[cut] * taps[3 * a] + u[cut] * taps[3 * a + 1] + right[cut] * taps[3 * a + 2]

            visit(o, rows, lanes, line(1) + up * line(0) + down * line(2))
            if other is not None:
                near = other[pl.ds(o, block + 2 * COLS), lanes]
                mine = flags[2, rows]
                held = (
                    mine * up * near[0:block],
                    mine * near[COLS : COLS + block],
                    mine * down * near[2 * COLS : 2 * COLS + block],
                )
                inner = slice(COLS, COLS + block)
                for a in range(3):
                    for b, view in enumerate((right, u, left)):
                        t = 8 * (base + 3 * a + b)
                        acc[t : t + 8, lanes] += eights(view[inner] * held[a])
            return carry

        lax.fori_loop(0, 3 * (wide // block), one, 0)

    def first(o, rows, lanes, value):
        at = pl.ds(o + COLS, block)
        a, s = gelu_parts(value + tab_ref[C1B : C1B + 1, lanes])
        act[rows, lanes] = a
        slope[rows, lanes] = s
        mid[at, lanes] = a * tab_ref[BG : BG + 1, lanes] + tab_ref[BS : BS + 1, lanes]

    convolve(li, K1R, False, None, first)

    def second(o, rows, lanes, value):
        value = value + tab_ref[C2B : C2B + 1, lanes]
        lo_[rows, lanes] = value
        branch = tab_ref[SL : SL + 1, lanes] * value
        s2[rows, lanes] = s1[rows, lanes] + branch
        acc[8 * 42 : 8 * 42 + 8, lanes] += eights(flags[2, rows] * branch * branch)

    convolve(mid, K2R, False, None, second)

    dw1_ref[...] = jnp.zeros_like(dw1_ref)
    dw2_ref[...] = jnp.zeros_like(dw2_ref)
    b1g_ref[...] = jnp.zeros_like(b1g_ref)
    for i in range(mlp // D):
        b1_ref[0:1, i * D : i * D + D] = tab(F1B + i)

    def feed(o, size, own):
        rows = pl.ds(0, size)
        here = pl.ds(o, size)
        xhat, _ = normalize(s2[here])
        n2 = xhat * tab(N2G) + tab(N2S)
        h, l = halves(n2)
        n2c[rows, 0:D] = h
        n2c[rows, D : 2 * D] = l
        n2c[rows, 2 * D : 3 * D] = h
        if own:
            nt[...] = side(n2.T)

        def up(j):
            lanes = pl.ds(j, 256)
            pre = dot_nn(n2c[rows], w1c[:, lanes]) + b1_ref[0:1, lanes]
            a, s = gelu_parts(pre)
            h, l = halves(a)
            hid_h[rows, lanes] = h
            hid_l[rows, lanes] = l
            hslope[rows, lanes] = s

        sweep(mlp, 256, up)
        w2h, w2l = w2c[:, 0:D], w2c[:, 2 * D : 3 * D]
        raw = (
            dot_nn(hid_h[rows], w2h) + (dot_nn(hid_l[rows], w2h) + dot_nn(hid_h[rows], w2l))
        ) + tab(F2B)
        dy = dy_ref[here]
        dz = tab(SM) * dy
        h, l = halves(dz)
        dzc[rows, 0:D] = h
        dzc[rows, D : 2 * D] = l
        dzc[rows, 2 * D : 3 * D] = h
        if own:
            dt[...] = side(dz.T)
            branch = tab(SM) * raw
            result = s2[here] + branch
            out_ref[pl.ds(pl.multiple_of(o - own_off, size), size)] = result
            add(40, eights(result * result))
            add(43, eights(branch * branch))
            add(SM, eights(dy * raw))
            add(F2B, eights(dz))

        def down(j):
            lanes = pl.ds(j, 256)
            dpre = dot_nt(dzc[rows], w2c[lanes, :]) * hslope[rows, lanes]
            h, l = halves(dpre)
            if own:
                b1g_ref[:, lanes] += eights(dpre)
                dw1_ref[:, lanes] += dot_nn(nt[...], jnp.concatenate([h, h, l], axis=0))
                hh, hl = hid_h[rows, lanes], hid_l[rows, lanes]
                dw2_ref[:, lanes] += dot_nn(dt[...], jnp.concatenate([hh, hh, hl], axis=0))
            hid_h[rows, lanes] = h
            hid_l[rows, lanes] = l

        sweep(mlp, 256, down)
        w1h, w1l = w1c[0:D], w1c[2 * D : 3 * D]
        dn = dot_nt(hid_h[rows], w1h) + (dot_nt(hid_l[rows], w1h) + dot_nt(hid_h[rows], w1l))
        xhat, r = normalize(s2[here])
        ds2[pl.ds(pl.multiple_of(o + COLS, COLS), size)] = dy_ref[here] + normalize_back(
            dn * tab(N2G), xhat, r
        )
        if own:
            add(N2G, eights(dn * xhat))
            add(N2S, eights(dn))

    def feed_one(i, carry):
        feed(pl.multiple_of(own_off + i * TILE, 128), TILE, True)
        return carry

    lax.fori_loop(0, tokens // TILE, feed_one, 0)
    edge = HALO // 2
    feed(pl.multiple_of(tokens - core * (tokens - edge), edge), edge, False)
    rest = pl.multiple_of(COLS + (1 - core) * (tokens + edge), COLS)
    ds2[pl.ds(rest, edge)] = jnp.zeros((edge, D), F32)

    def third(o, rows, lanes, value):
        grad = value * tab_ref[BG : BG + 1, lanes] * slope[rows, lanes]
        gp[pl.ds(o + COLS, block), lanes] = grad
        held = flags[2, rows] * value
        acc[8 * BG : 8 * BG + 8, lanes] += eights(held * act[rows, lanes])
        acc[8 * BS : 8 * BS + 8, lanes] += eights(held)
        acc[8 * C1B : 8 * C1B + 8, lanes] += eights(flags[2, rows] * grad)

    convolve(ds2, K2R, True, SL, third, mid)

    def fourth(o, rows, lanes, value):
        slope[rows, lanes] = value

    convolve(gp, K1R, True, None, fourth, li)

    dwp_ref[...] = jnp.zeros_like(dwp_ref)
    cross[...] = jnp.zeros_like(cross)

    def back(step, carry):
        here = pl.multiple_of(step * TILE, TILE)
        o = pl.multiple_of(own_off + here, 128)

        here_wide = pl.ds(o, TILE)
        xhat, r = normalize(s1[here_wide])
        grad = slope[here_wide]
        grad_two = ds2[pl.ds(pl.multiple_of(o + COLS, COLS), TILE)]
        result = grad_two + normalize_back(grad * tab(N3G), xhat, r)
        ds1_ref[pl.ds(here, TILE)] = result
        add(N3G, eights(grad * xhat))
        add(N3S, eights(grad))
        add(SL, eights(grad_two * lo_[here_wide]))
        add(C2B, eights(grad_two))
        add(PB, eights(result))
        dmx = dot_nt(side(tab(SA) * result), wph[...])
        dmx_ref[pl.ds(here, TILE)] = dmx
        h, l = halves(result)
        dwp_ref[...] += dot_nn(side(mixed[pl.ds(o, TILE)].T), jnp.concatenate([h, h, l], axis=0))
        dmxt = side(dmx.T)
        for s, (lo, hi) in enumerate(spans):

            @pl.when((lo < o + TILE) & (hi > o))
            def _():
                vm = jnp.where(span_mask(o, TILE, lo, hi), v_ref[pl.ds(o, TILE)], 0.0)
                vh, vl = halves(vm)
                cross[s] += dot_nn(dmxt, jnp.concatenate([vh, vh, vl], axis=0))

        return carry

    lax.fori_loop(0, tokens // TILE, back, 0)
    for s in range(3):
        gprob_ref[s] = fold(cross[s])

    def total(r):
        return jnp.sum(acc[8 * r : 8 * r + 8], axis=0, keepdims=True)

    for r in (N3G, N3S, N2G, N2S, SL, SM, C1B, BG, BS, F2B, 40, 41, 42, 43):
        gtab_ref[r : r + 1] = total(r)
    for t in range(9):
        gtab_ref[K1R + t : K1R + t + 1] = total(K1R + t)
        gtab_ref[K2R + t : K2R + t + 1] = total(K2R + t) * tab(SL)
    gtab_ref[C2B : C2B + 1] = total(C2B) * tab(SL)
    gtab_ref[PB : PB + 1] = total(PB) * tab(SA)
    raw = dwp_ref[...]
    gtab_ref[SA : SA + 1] = jnp.sum(raw * wp_ref[...], axis=0, keepdims=True) + total(PB) * tab(PB)
    dwp_ref[...] = raw * tab(SA)
    for i in range(mlp // D):
        gtab_ref[F1B + i : F1B + i + 1] = jnp.sum(b1g_ref[:, i * D : i * D + D], axis=0, keepdims=True)


def middle(tall, temp, x, dy, v, halo, sums, peer, wp, w1, w2, tab):
    tokens = x.shape[0]
    wide = tokens + HALO
    mlp = w1.shape[1]
    smem = pl.BlockSpec(memory_space=pltpu.SMEM)
    vmem = pl.BlockSpec(memory_space=pltpu.VMEM)
    anywhere = pl.BlockSpec(memory_space=pl.ANY)

    def f(*shape):
        return jax.ShapeDtypeStruct(shape, F32)

    def s(*shape):
        return pltpu.VMEM(shape, F32)

    def b(*shape):
        return pltpu.VMEM(shape, BF)

    padded = s(wide + 2 * COLS, D)
    return pl.pallas_call(
        middle_kernel,
        out_shape=[
            f(tokens, D),
            f(tokens, D),
            f(tokens, D),
            f(D, D),
            f(2, D, mlp),
            f(TABLE, D),
            f(3, HD, D),
            f(3, HD, D),
            f(3, HD, D),
        ],
        in_specs=[smem, smem] + [anywhere] * 4 + [vmem] * 6,
        out_specs=[vmem] * 9,
        scratch_shapes=[
            b(3 * D, D),
            b(D, 3 * D),
            b(3 * D, mlp),
            b(mlp, 3 * D),
            b(3, D, 3 * D),
            s(wide, D),
            s(wide, D),
            padded,
            s(wide, D),
            s(wide, D),
            padded,
            s(wide, D),
            padded,
            padded,
            s(wide // 3, D),
            b(TILE, 3 * D),
            b(TILE, 3 * D),
            b(TILE, mlp),
            b(TILE, mlp),
            s(TILE, mlp),
            s(8, mlp),
            s(8, mlp),
            s(8 * TABLE, D),
            s(3, D, D),
            s(wide, D),
            s(wide, D),
            s(wide, D),
            s(3, wide, 128),
            b(D, 3 * TILE),
            b(D, 3 * TILE),
            pltpu.SemaphoreType.DMA((6,)),
        ],
        compiler_params=pltpu.CompilerParams(vmem_limit_bytes=60 << 20),
    )(tall, temp, x, dy, v, halo, sums, peer, wp, w1, w2, tab)


ORDERS = ((0, 1, 2, 3), (1, 2, 0, 3), (2, 0, 1, 3))
DMA = pltpu.SemaphoreType.DMA


class Links:
    def __init__(self):
        self.core = lax.axis_index("rows")
        chip = lax.axis_index("canvas")
        self.bits = (lax.axis_size("canvas") - 1).bit_length()
        self.mine = [lax.rem(lax.div(chip, 1 << b), 2) for b in range(self.bits)]
        self.there = [{"canvas": chip + (1 - 2 * m) * (1 << b)} for b, m in enumerate(self.mine)]
        self.twin = {"rows": 1 - self.core}

    def greet(self):
        barrier = pltpu.get_barrier_semaphore()
        for other in [self.twin] + self.there:
            pl.semaphore_signal(barrier, inc=1, device_id=other, device_id_type=MESH_ID)
        pl.semaphore_wait(barrier, self.bits + 1)


def remote(src, dst, send, recv, other):
    return pltpu.make_async_remote_copy(
        src_ref=src,
        dst_ref=dst,
        send_sem=send,
        recv_sem=recv,
        device_id=other,
        device_id_type=MESH_ID,
    )


class Total:
    def __init__(self, links, src, dst, work):
        self.links = links
        self.src = src
        self.dst = dst
        (
            self.buf,
            self.first,
            self.land,
            self.own_sem,
            self.pair_send,
            self.pair_recv,
            self.send_sem,
            self.recv_sem,
            self.back_send,
            self.back_recv,
            self.out_sem,
            self.out_send,
            self.out_recv,
        ) = work
        self.part = self.buf.shape[0] // 3
        self.blocks = self.buf.shape[0] // D
        self.kept = self.part // 16

    @staticmethod
    def scratch(blocks, bits):
        rows = blocks * D
        steps = max(bits, 4)
        part = rows // 3
        return [
            pltpu.VMEM((rows, D), F32),
            pltpu.VMEM((rows, D), F32),
            pltpu.VMEM((3, part + (steps - 4) * (part // 16), D), F32),
            DMA((blocks,)),
            DMA((blocks,)),
            DMA((blocks,)),
            DMA((3, steps)),
            DMA((3, steps)),
            DMA((3, 4)),
            DMA((3, 4)),
            DMA((blocks,)),
            DMA((blocks,)),
            DMA((blocks,)),
        ]

    def start(self, p, s):
        at = p * self.part
        for t in range(s):
            at = at + self.links.mine[ORDERS[p][t]] * (self.part >> (t + 1))
        return at

    def add(self, at, src, src_at, rows):
        size = 96 if rows % 96 == 0 else 16

        def one(i, carry):
            here = pl.ds(pl.multiple_of(at + i * size, 16), size)
            self.buf[here] += src[pl.ds(pl.multiple_of(src_at + i * size, 16), size)]
            return carry

        lax.fori_loop(0, rows // size, one, 0)

    def pairs(self):
        core = self.links.core
        copies = []
        for i in range(self.blocks):
            lanes = slice(i * D, i * D + D)
            rows = pl.ds(i * D, D)
            copies.append(
                pltpu.make_async_copy(
                    self.src.at[core, :, lanes], self.buf.at[rows], self.own_sem.at[i]
                )
            )
            copies.append(
                remote(
                    self.src.at[1 - core, :, lanes],
                    self.first.at[rows],
                    self.pair_send.at[i],
                    self.pair_recv.at[i],
                    self.links.twin,
                )
            )
        return copies

    def begin(self):
        for copy in self.pairs():
            copy.start()

    def move(self, p, s):
        b = ORDERS[p][s]
        half = self.part >> (s + 1)
        away = pl.multiple_of(self.start(p, s) + (1 - self.links.mine[b]) * half, 16)
        at = self.part - (self.part >> s)
        return remote(
            self.buf.at[pl.ds(away, half)],
            self.land.at[p, pl.ds(at, half)],
            self.send_sem.at[p, s],
            self.recv_sem.at[p, s],
            self.links.there[b],
        )

    def join(self):
        for copy in self.pairs():
            copy.wait()
        self.add(0, self.first, 0, self.buf.shape[0])
        for p in range(3):
            self.move(p, 0).start()

    def down(self, s):
        for p in range(3):
            self.move(p, s).wait()
            self.add(self.start(p, s + 1), self.land.at[p], self.part - (self.part >> s), self.part >> (s + 1))
            if s < 3:
                self.move(p, s + 1).start()
        if s < 3:
            return
        for b in range(4, self.links.bits):
            extra = []
            for p in range(3):
                extra.append(
                    remote(
                        self.buf.at[pl.ds(pl.multiple_of(self.start(p, 4), 16), self.kept)],
                        self.land.at[p, pl.ds(self.part + (b - 4) * self.kept, self.kept)],
                        self.send_sem.at[p, b],
                        self.recv_sem.at[p, b],
                        self.links.there[b],
                    )
                )
                extra[-1].start()
            for p in range(3):
                extra[p].wait()
                self.add(self.start(p, 4), self.land.at[p], self.part + (b - 4) * self.kept, self.kept)
        for p in range(3):
            held = pl.ds(pl.multiple_of(self.start(p, 4), 16), self.kept)
            self.first[held] = self.buf[held]
            self.back(p, 3).start()

    def back(self, p, s):
        rows = self.part >> (s + 1)
        held = pl.ds(pl.multiple_of(self.start(p, s + 1), 16), rows)
        return remote(
            self.first.at[held],
            self.first.at[held],
            self.back_send.at[p, s],
            self.back_recv.at[p, s],
            self.links.there[ORDERS[p][s]],
        )

    def up(self, s):
        for p in range(3):
            self.back(p, s).wait()
            if s > 0:
                self.back(p, s - 1).start()
        if s == 0:
            for copy in self.outs():
                copy.start()

    def outs(self):
        copies = []
        for i in range(self.blocks):
            src = self.first.at[pl.ds(i * D, D)]
            dst = self.dst.at[self.links.core, :, i * D : i * D + D]
            copies.append(pltpu.make_async_copy(src, dst, self.out_sem.at[i]))
            copies.append(
                remote(src, dst, self.out_send.at[i], self.out_recv.at[i], self.links.twin)
            )
        return copies

    def end(self):
        for copy in self.outs():
            copy.wait()


def finish_kernel(
    tall_ref,
    temp_ref,
    x_ref,
    q_ref,
    k_ref,
    ds1_ref,
    dmx_ref,
    sums_ref,
    peer_ref,
    probs_ref,
    unit_ref,
    gprob_ref,
    w_ref,
    tab_ref,
    gtab_ref,
    dwp_ref,
    mid_hbm,
    dx_ref,
    dw_ref,
    otab_ref,
    sum_hbm,
    wh,
    wl,
    pv,
    cv,
    ch,
    side_rows,
    acc,
    gpeer_ref,
    gsend,
    grecv,
    *work,
):
    step = pl.program_id(0)
    last = pl.num_programs(0) - 1
    links = Links()
    core = links.core
    total = Total(links, mid_hbm, sum_hbm, work)
    rows_all = 2 * pl.num_programs(0) * TILE // COLS
    spans = slots(tall_ref, core, core * (rows_all // 2), rows_all)
    start = step * TILE

    def tab(r):
        return tab_ref[r : r + 1]

    @pl.when(step == 0)
    def _():
        links.greet()
        swap = remote(gprob_ref.at[2], gpeer_ref, gsend, grecv, links.twin)
        swap.start()
        total.begin()

        def part(o):
            h, l = halves(w_ref[pl.ds(o, 64)])
            wh[pl.ds(o, 64)] = h
            wl[pl.ds(o, 64)] = l

        sweep(D, 64, part)
        dw_ref[...] = jnp.zeros_like(dw_ref)
        dw_ref[1, :, D : 2 * D] = dwp_ref[...]
        acc[...] = jnp.zeros_like(acc)
        ones = group_ones()
        temp = head_row(temp_ref)
        heat = jnp.zeros((1, D), F32)
        for s in range(3):
            sums = sums_ref[s]
            grad = gprob_ref[s]
            if s == 2:
                swap.wait()
                sums = sums + peer_ref[...]
                grad = grad + gpeer_ref[...]
            inv_q = lax.rsqrt(sums[HD : HD + 1] + EPS)
            inv_k = lax.rsqrt(sums[HD + 1 : HD + 2] + EPS)
            probs = probs_ref[s]
            unit = unit_ref[s]
            scores = probs * (grad - group_sum(probs * grad, ones))
            part_heat = jnp.sum(scores * unit, axis=0, keepdims=True)
            heat = heat + (part_heat if s < 2 else jnp.where(core == 0, part_heat, 0.0))
            pull = temp * scores
            both = pull * unit
            side_rows[8 * s : 8 * s + 1] = fold_to_row(group_sum(both, ones)) * inv_q * inv_q
            side_rows[8 * s + 1 : 8 * s + 2] = jnp.sum(both, axis=0, keepdims=True) * inv_k * inv_k
            across = slice(3 * s * D, 3 * s * D + 3 * D)
            h, l = halves(unfold(pull * row_to_fold(inv_q, ones) * inv_k))
            cv[across] = jnp.concatenate([h, h, l], axis=0)
            ch[:, across] = jnp.concatenate([h, h, l], axis=1)
            h, l = halves(unfold(probs))
            pv[across] = jnp.concatenate([h, h, l], axis=0)
        otab_ref[...] = gtab_ref[...]
        otab_ref[44:45] = heat
        total.join()

    masks = [span_mask(start, TILE, lo, hi) for lo, hi in spans]

    def by_slot(v):
        return jnp.concatenate([side(jnp.where(mask, v, 0.0)) for mask in masks], axis=1)

    def rows_of(r):
        return sum(jnp.where(mask, side_rows[8 * s + r : 8 * s + r + 1], 0.0) for s, mask in enumerate(masks))

    q, k = q_ref[...], k_ref[...]
    dq = dot_nt(by_slot(k), ch[...]) - q * rows_of(0)
    dk = dot_nn(by_slot(q), cv[...]) - k * rows_of(1)
    dv = dot_nn(by_slot(dmx_ref[...]), pv[...])
    dqkv = jnp.concatenate([dq, dk, dv], axis=1)

    @pl.when(step == 1)
    def _():
        total.down(1)

    h, l = halves(dqkv)
    dn = dot_nt(h, wh[...]) + (dot_nt(l, wh[...]) + dot_nt(h, wl[...]))
    xhat, r = normalize(x_ref[...])
    nt = side((xhat * tab(N1G) + tab(N1S)).T)
    grads = dot_nn(nt, jnp.concatenate([h, h, l], axis=0))
    dw_ref[0] += grads[:, 0 : 2 * D]
    dw_ref[1, :, 0:D] += grads[:, 2 * D : 3 * D]
    dx_ref[...] = ds1_ref[...] + normalize_back(dn * tab(N1G), xhat, r)
    acc[0:8] += eights(dn * xhat)
    acc[8:16] += eights(dn)
    for i, v in enumerate((dq, dk, dv)):
        acc[16 + 8 * i : 24 + 8 * i] += eights(v)

    @pl.when(step == 0)
    def _():
        total.down(0)

    @pl.when(step == 1)
    def _():
        total.down(2)

    @pl.when(step == 2)
    def _():
        total.down(3)

    @pl.when(step == last)
    def _():
        for i, r in enumerate((N1G, N1S, QB, KB, VB)):
            otab_ref[r : r + 1] = jnp.sum(acc[8 * i : 8 * i + 8], axis=0, keepdims=True)
        for s in range(3, -1, -1):
            total.up(s)
        total.end()


def finish(tall, temp, x, q, k, ds1, dmx, sums, peer, probs, unit, gprob, w, tab, gtab, dwp, mid):
    tokens = x.shape[0]
    smem = pl.BlockSpec(memory_space=pltpu.SMEM)
    anywhere = pl.BlockSpec(memory_space=pl.ANY)
    row = pl.BlockSpec((TILE, D), lambda i: (i, 0))
    bits = (lax.axis_size("canvas") - 1).bit_length()

    def whole(v):
        return pl.BlockSpec(v.shape, lambda i: (0,) * v.ndim)

    fixed = (sums, peer, probs, unit, gprob, w, tab, gtab, dwp)
    return pl.pallas_call(
        finish_kernel,
        grid=(tokens // TILE,),
        out_shape=[
            jax.ShapeDtypeStruct((tokens, D), F32),
            jax.ShapeDtypeStruct((2, D, 2 * D), F32),
            jax.ShapeDtypeStruct((TABLE, D), F32),
            jax.ShapeDtypeStruct(mid.shape, F32),
        ],
        in_specs=[smem, smem] + [row] * 5 + [whole(v) for v in fixed] + [anywhere],
        out_specs=[
            row,
            pl.BlockSpec((2, D, 2 * D), lambda i: (0, 0, 0)),
            pl.BlockSpec((TABLE, D), lambda i: (0, 0)),
            anywhere,
        ],
        scratch_shapes=[
            pltpu.VMEM((D, 3 * D), BF),
            pltpu.VMEM((D, 3 * D), BF),
            pltpu.VMEM((9 * D, D), BF),
            pltpu.VMEM((9 * D, D), BF),
            pltpu.VMEM((D, 9 * D), BF),
            pltpu.VMEM((24, D), F32),
            pltpu.VMEM((40, D), F32),
            pltpu.VMEM(gprob.shape[1:], F32),
            DMA,
            DMA,
        ]
        + Total.scratch(mid.shape[2] // D, bits),
        compiler_params=pltpu.CompilerParams(
            collective_id=1, has_side_effects=True, vmem_limit_bytes=60 << 20
        ),
    )(tall, temp, x, q, k, ds1, dmx, *fixed, mid)


def unit_norm(xs, group):
    norm = 0.0
    for b in group:
        norm = norm + jnp.sum(jnp.sum(xs[b] * xs[b], axis=0, keepdims=True), axis=1, keepdims=True)
    inv = 1.0 / (jnp.sqrt(norm) + 1e-07)
    for b in group:
        xs[b] = xs[b] * inv


def polynomial(xs, group):
    left, right = [], []
    for b in group:
        h, l = halves(xs[b])
        left += [h, l, h]
        right += [h, h, l]
    gram = dot_nt(jnp.concatenate(left, axis=1), jnp.concatenate(right, axis=1))
    h, l = halves(gram)
    square = dot_nn(jnp.concatenate([h, l, h], axis=1), jnp.concatenate([h, h, l], axis=0))
    return side(-4.775 * gram + 2.0315 * square)


def apply_to(xs, group, poly):
    for b in group:
        h, l = halves(xs[b])
        xs[b] = 3.4445 * xs[b] + dot_nn(poly, jnp.concatenate([h, h, l], axis=0))


def wide_kernel(
    end_hbm,
    tab_hbm,
    mid_hbm,
    m1_hbm,
    m2_hbm,
    sum_hbm,
    otab_hbm,
    orth_hbm,
    xs,
    grad,
    m1,
    m2,
    poly,
    tbuf,
    tland,
    load_sem,
    tsend,
    trecv,
    tout,
    *work,
):
    links = Links()
    core = links.core
    total = Total(links, end_hbm, sum_hbm, work)
    blocks = m1.shape[1] // D
    group = tuple(range(blocks))
    trows = tbuf.shape[0]
    near = pl.ds(pl.multiple_of(core * trows, 8), trows)
    far = pl.ds(pl.multiple_of((1 - core) * trows, 8), trows)
    pairs = ((mid_hbm.at[core], grad), (m1_hbm, m1), (m2_hbm, m2), (tab_hbm.at[near], tbuf))
    loads = [pltpu.make_async_copy(a, b, load_sem.at[i]) for i, (a, b) in enumerate(pairs)]
    for load in loads:
        load.start()
    links.greet()
    total.begin()
    top = links.bits

    def table(n):
        if n == top:
            return remote(tab_hbm.at[far], tland.at[n], tsend.at[n], trecv.at[n], links.twin)
        return remote(tbuf, tland.at[n], tsend.at[n], trecv.at[n], links.there[n])

    def table_step(n):
        table(n).start()
        table(n).wait()
        tbuf[...] += tland[n]

    table(top).start()
    for load in loads:
        load.wait()

    @pl.when(core == 0)
    def _():
        for b in group:
            lanes = slice(b * D, b * D + D)
            xs[b] = MUON_KEEP * m1[:, lanes] + grad[:, lanes]

    @pl.when(core == 1)
    def _():
        for b in group:
            xs[b] = MUON_KEEP * m2[b * D : b * D + D].T + grad[:, b * D : b * D + D]

    unit_norm(xs, group)
    table(top).wait()
    tbuf[...] += tland[top]
    total.join()

    def step(i, carry):
        poly[...] = polynomial(xs, group)

        @pl.when(i == 1)
        def _():
            total.down(1)
            table_step(1)

        @pl.when(i == 2)
        def _():
            total.down(3)
            table_step(3)

        @pl.when(i == 3)
        def _():
            total.up(2)

        apply_to(xs, group, poly[...])

        @pl.when(i == 0)
        def _():
            total.down(0)
            table_step(0)

        @pl.when(i == 1)
        def _():
            total.down(2)
            table_step(2)

        @pl.when(i == 2)
        def _():
            total.up(3)

        @pl.when(i == 3)
        def _():
            total.up(1)

        @pl.when(i == 4)
        def _():
            total.up(0)

        return carry

    lax.fori_loop(0, 5, step, 0)
    for b in range(4, links.bits):
        table_step(b)
    touts = [
        pltpu.make_async_copy(tbuf, otab_hbm.at[near], tout.at[0]),
        remote(tbuf, otab_hbm.at[near], tout.at[1], tout.at[2], links.twin),
    ]
    for copy in touts:
        copy.start()

    @pl.when(core == 1)
    def _():
        for b in group:
            xs[b] = xs[b].T

    orth = pltpu.make_async_copy(xs, orth_hbm.at[core], load_sem.at[0])
    orth.start()
    total.end()
    for copy in touts + [orth]:
        copy.wait()


def wide_blocks(end, tab, mid, m1, m2):
    bits = (lax.axis_size("canvas") - 1).bit_length()
    anywhere = pl.BlockSpec(memory_space=pl.ANY)
    blocks = m1.shape[1] // D
    return pl.pallas_call(
        wide_kernel,
        out_shape=[
            jax.ShapeDtypeStruct(end.shape, F32),
            jax.ShapeDtypeStruct((TABLE, D), F32),
            jax.ShapeDtypeStruct((2, blocks, D, D), F32),
        ],
        in_specs=[anywhere] * 5,
        out_specs=[anywhere] * 3,
        scratch_shapes=[
            pltpu.VMEM((blocks, D, D), F32),
            pltpu.VMEM(m1.shape, F32),
            pltpu.VMEM(m1.shape, F32),
            pltpu.VMEM(m2.shape, F32),
            pltpu.VMEM((D, 3 * D), BF),
            pltpu.VMEM((TABLE // 2, D), F32),
            pltpu.VMEM((bits + 1, TABLE // 2, D), F32),
            DMA((4,)),
            DMA((bits + 1,)),
            DMA((bits + 1,)),
            DMA((3,)),
        ]
        + Total.scratch(end.shape[2] // D, bits),
        compiler_params=pltpu.CompilerParams(
            collective_id=2, has_side_effects=True, vmem_limit_bytes=60 << 20
        ),
    )(end, tab, mid, m1, m2)


def square_kernel(
    end_hbm,
    mid_hbm,
    mq_hbm,
    mp_hbm,
    m1_hbm,
    m2_hbm,
    gq_out,
    gp_out,
    g1_out,
    g2_out,
    nq_out,
    np_out,
    n1_out,
    n2_out,
    orth_hbm,
    end,
    mid,
    nat,
    mq,
    mp,
    m1,
    m2,
    xs,
    in_sem,
    out_sem,
):
    core = lax.axis_index("rows")
    blocks = m1.shape[1] // D
    pairs = ((end_hbm, end), (mq_hbm, mq), (mp_hbm, mp), (mid_hbm, mid), (m1_hbm, m1), (m2_hbm, m2))
    loads = [pltpu.make_async_copy(a, b, in_sem.at[i]) for i, (a, b) in enumerate(pairs)]
    for load in loads:
        load.start()
    for load in loads[0:3]:
        load.wait()
    outs = []

    def store(src, dst):
        outs.append(pltpu.make_async_copy(src, dst, out_sem.at[len(outs)]))
        outs[-1].start()

    store(end.at[0], gq_out.at[:, 0 : 2 * D])
    store(end.at[1, :, 0:D], gq_out.at[:, 2 * D : 3 * D])
    store(end.at[1, :, D : 2 * D], gp_out)

    def small(o):
        rows = pl.ds(o, 64)
        mq[rows, 0 : 2 * D] = MUON_KEEP * mq[rows, 0 : 2 * D] + end[0, rows]
        mq[rows, 2 * D : 3 * D] = MUON_KEEP * mq[rows, 2 * D : 3 * D] + end[1, rows, 0:D]
        mp[rows] = MUON_KEEP * mp[rows] + end[1, rows, D : 2 * D]

    sweep(D, 64, small)
    store(mq, nq_out)
    store(mp, np_out)

    @pl.when(core == 0)
    def _():
        xs[0] = mq[:, 0:D]
        xs[1] = mq[:, D : 2 * D]

    @pl.when(core == 1)
    def _():
        xs[0] = mq[:, 2 * D : 3 * D]
        xs[1] = mp[...]

    for b in range(2):
        unit_norm(xs, (b,))

    def step(i, carry):
        for b in range(2):
            apply_to(xs, (b,), polynomial(xs, (b,)))
        return carry

    lax.fori_loop(0, 2, step, 0)
    for load in loads[3:]:
        load.wait()
    store(mid.at[0], g1_out)
    for b in range(blocks):
        nat[b * D : b * D + D] = mid[1, :, b * D : b * D + D].T
    store(nat, g2_out)

    def large(o):
        rows = pl.ds(o, 64)
        m1[rows] = MUON_KEEP * m1[rows] + mid[0, rows]

    sweep(D, 64, large)
    store(m1, n1_out)

    def larger(o):
        rows = pl.ds(o, 256)
        m2[rows] = MUON_KEEP * m2[rows] + nat[rows]

    sweep(blocks * D, 256, larger)
    store(m2, n2_out)
    lax.fori_loop(2, 5, step, 0)
    store(xs, orth_hbm.at[core])
    for copy in outs:
        copy.wait()


def square_blocks(end, mid, mq, mp, m1, m2):
    anywhere = pl.BlockSpec(memory_space=pl.ANY)
    args = (mq, mp, m1, m2)
    return pl.pallas_call(
        square_kernel,
        out_shape=[jax.ShapeDtypeStruct(a.shape, F32) for a in args + args]
        + [jax.ShapeDtypeStruct((2, 2, D, D), F32)],
        in_specs=[anywhere] * 6,
        out_specs=[anywhere] * 9,
        scratch_shapes=[
            pltpu.VMEM(end.shape, F32),
            pltpu.VMEM(mid.shape, F32),
            pltpu.VMEM(m2.shape, F32),
            pltpu.VMEM(mq.shape, F32),
            pltpu.VMEM(mp.shape, F32),
            pltpu.VMEM(m1.shape, F32),
            pltpu.VMEM(m2.shape, F32),
            pltpu.VMEM((2, D, D), F32),
            DMA((6,)),
            DMA((11,)),
        ],
        compiler_params=pltpu.CompilerParams(vmem_limit_bytes=60 << 20),
    )(end, mid, *args)


def trade_kernel(wide_in, square_in, wide_ref, square_ref, send_sem, recv_sem):
    core = lax.axis_index("rows")
    twin = {"rows": 1 - core}
    barrier = pltpu.get_barrier_semaphore()
    pl.semaphore_signal(barrier, inc=1, device_id=twin, device_id_type=MESH_ID)
    pl.semaphore_wait(barrier, 1)
    copies = [
        remote(ref.at[core], ref.at[core], send_sem.at[i], recv_sem.at[i], twin)
        for i, ref in enumerate((wide_ref, square_ref))
    ]
    for copy in copies:
        copy.start()
    for copy in copies:
        copy.wait()


def trade(wide, square):
    anywhere = pl.BlockSpec(memory_space=pl.ANY)
    return pl.pallas_call(
        trade_kernel,
        out_shape=[jax.ShapeDtypeStruct(v.shape, F32) for v in (wide, square)],
        in_specs=[anywhere] * 2,
        out_specs=[anywhere] * 2,
        input_output_aliases={0: 0, 1: 1},
        scratch_shapes=[DMA((2,)), DMA((2,))],
        compiler_params=pltpu.CompilerParams(collective_id=3, has_side_effects=True),
    )(wide, square)


def moment_step(current, one, two, gradient):
    first = BETA1 * one + (1.0 - BETA1) * gradient
    second = BETA2 * two + (1.0 - BETA2) * gradient * gradient
    fix_one = 1.0 - BETA1**STEP
    fix_two = 1.0 - BETA2**STEP
    updated = current - ADAM_RATE * (first / fix_one) / (jnp.sqrt(second / fix_two) + ADAM_FLOOR)
    return first, second, updated


def update_kernel(
    wide_ref,
    last_ref,
    square_ref,
    wq_ref,
    wp_ref,
    w1_ref,
    w2_ref,
    tab_ref,
    one_ref,
    two_ref,
    gtab_ref,
    nq_ref,
    np_ref,
    n1_ref,
    n2_ref,
    cq_ref,
    cp_ref,
    c1_ref,
    c2_ref,
    first_ref,
    second_ref,
    small_ref,
):
    mlp = w1_ref.shape[1]

    def put(new_ref, copy_ref, w, orth, large, lanes):
        new = w * (1.0 - MUON_RATE * DECAY) - MUON_RATE * 0.2 * math.sqrt(large) * orth
        new_ref[:, lanes] = new
        copy_ref[:, lanes] = new.astype(BF)

    for i in range(3):
        lanes = slice(i * D, i * D + D)
        orth = square_ref[0, i] if i < 2 else square_ref[1, 0]
        put(nq_ref, cq_ref, wq_ref[:, lanes], orth, D, lanes)
    put(np_ref, cp_ref, wp_ref[...], square_ref[1, 1], D, slice(0, D))
    for i in range(mlp // D):
        lanes = slice(i * D, i * D + D)
        put(n1_ref, c1_ref, w1_ref[:, lanes], wide_ref[0, i], mlp, lanes)
    put(n2_ref, c2_ref, w2_ref[...], last_ref[0, 0], mlp, slice(0, D))
    first, second, small = moment_step(tab_ref[...], one_ref[...], two_ref[...], gtab_ref[0:SMALL])
    first_ref[...] = first
    second_ref[...] = second
    small_ref[...] = small


def update(wide, square, wq, wp, w1, w2, tab, one, two, gtab):
    blocks = w2.shape[0] // D
    steps = 2 * blocks
    piece = D // steps

    def rows(v):
        size = v.shape[0] // steps
        return pl.BlockSpec((size, v.shape[1]), lambda i: (i, 0))

    def whole(v):
        return pl.BlockSpec(v.shape, lambda i: (0, 0))

    weights = (wq, wp, w1, w2)
    return pl.pallas_call(
        update_kernel,
        grid=(steps,),
        out_shape=[jax.ShapeDtypeStruct(w.shape, F32) for w in weights]
        + [jax.ShapeDtypeStruct(w.shape, BF) for w in weights]
        + [jax.ShapeDtypeStruct(tab.shape, F32)] * 3,
        in_specs=[
            pl.BlockSpec((1, blocks, piece, D), lambda i: (0, 0, i, 0)),
            pl.BlockSpec((1, 1, D // 2, D), lambda i: (1, i // 2, i % 2, 0)),
            pl.BlockSpec((2, 2, piece, D), lambda i: (0, 0, i, 0)),
        ]
        + [rows(w) for w in weights]
        + [whole(v) for v in (tab, one, two, gtab)],
        out_specs=[rows(w) for w in weights] * 2 + [whole(tab)] * 3,
        compiler_params=pltpu.CompilerParams(vmem_limit_bytes=60 << 20),
    )(wide, wide, square, *weights, tab, one, two, gtab)


def on_device(
    x4, dy4, tall, wqkv, wp, w1, w2, mqkv, mp, m1, m2, tab, tab_one, tab_two, temp, temp_one, temp_two
):
    shape = x4.shape
    tokens = shape[1] * shape[2]
    x = x4.reshape(tokens, D)
    dy = dy4.reshape(tokens, D)
    q, k, v, sums = project(tall, x, wqkv, tab)
    halo, peer = widen(x, dy, v, sums)
    out, ds1, dmx, dwp, mid, gtab, probs, unit, gprob = middle(
        tall, temp, x, dy, v, halo, sums, peer, wp, w1, w2, tab
    )
    dx, end, gtab, mid = finish(
        tall, temp, x, q, k, ds1, dmx, sums, peer, probs, unit, gprob, wqkv, tab, gtab, dwp, mid
    )
    end, gtab, wide = wide_blocks(end, gtab, mid, m1, m2)
    *grads, square = square_blocks(end, mid, mqkv, mp, m1, m2)
    wide, square = trade(wide, square)
    results = update(wide, square, wqkv, wp, w1, w2, tab, tab_one, tab_two, gtab)
    heat = jnp.sum(gtab[44].reshape(HEADS, HD), axis=1)
    warm = moment_step(temp, temp_one, temp_two, heat)
    count = tokens * D * lax.axis_size("rows") * lax.axis_size("canvas")
    rms = jnp.sqrt(jnp.sum(gtab[40:44], axis=1) / count)
    return (out.reshape(shape), dx.reshape(shape), *grads, *results, *warm, rms)


def solution(mesh):
    split = P("canvas", "rows", None, None)
    return jax.shard_map(
        on_device,
        mesh=mesh,
        in_specs=(split, split, P("canvas", None)) + (P(),) * 14,
        out_specs=(split, split) + (P(),) * 23,
        check_vma=False,
    )
```

```python
import math

import jax
import jax.numpy as jnp
from jax import lax
from jax.experimental import pallas as pl
from jax.experimental.pallas import tpu as pltpu
from jax.sharding import PartitionSpec as P

BF = jnp.bfloat16
F32 = jnp.float32
MESH_ID = pl.DeviceIdType.MESH

EPS = 1e-06
ROOT_HALF = 1.0 / math.sqrt(2.0)
ROOT_TWOPI = 1.0 / math.sqrt(2.0 * math.pi)
STEP = 10
MUON_RATE = 0.2
MUON_KEEP = 0.95
DECAY = 0.01
ADAM_RATE = 0.2
BETA1 = 0.9
BETA2 = 0.95
ADAM_FLOOR = 1e-08

HEADS = 8
HD = 48
D = HEADS * HD
COLS = 32
HALO = 4 * COLS
TILE = 256

N1G, N1S, N3G, N3S, N2G, N2S, SA, SL, SM, QB, KB, VB, PB, C1B, BG, BS, C2B, F2B = range(18)
F1B, K1R, K2R = 18, 22, 31
SMALL = 40
TABLE = 48


def halves(v):
    hi = v.astype(BF)
    return hi, (v - hi.astype(F32)).astype(BF)


def side(v):
    h, l = halves(v)
    return jnp.concatenate([h, l, h], axis=1)


def dot_nn(a, b):
    return lax.dot_general(a, b, (((1,), (0,)), ((), ())), preferred_element_type=F32)


def dot_nt(a, b):
    return lax.dot_general(a, b, (((1,), (1,)), ((), ())), preferred_element_type=F32)


def normalize(v):
    mean = jnp.mean(v, axis=1, keepdims=True)
    c = v - mean
    r = lax.rsqrt(jnp.mean(c * c, axis=1, keepdims=True) + EPS)
    return c * r, r


def normalize_back(e, xhat, r):
    return r * (
        e - jnp.mean(e, axis=1, keepdims=True) - xhat * jnp.mean(e * xhat, axis=1, keepdims=True)
    )


def gelu_parts(v):
    phi = 0.5 * (1.0 + lax.erf(v * ROOT_HALF))
    return v * phi, phi + v * jnp.exp(-0.5 * v * v) * ROOT_TWOPI


def eights(v):
    total = v[0:8]
    for i in range(8, v.shape[0], 8):
        total = total + v[i : i + 8]
    return total


def sweep(count, size, body):
    def one(i, carry):
        body(pl.multiple_of(i * size, size))
        return carry

    lax.fori_loop(0, count // size, one, 0)


def image_ends(tall_ref):
    e0 = tall_ref[0, 0]
    e1 = e0 + tall_ref[0, 1]
    return e0, e1, e1 + tall_ref[0, 2]


def slots(tall_ref, core, first_row, rows_all):
    e0, e1, e2 = image_ends(tall_ref)
    low = (jnp.where(core == 0, 0, e2), jnp.where(core == 0, e0, 0), e1)
    high = (jnp.where(core == 0, e0, rows_all), jnp.where(core == 0, e1, 0), e2)
    return [((a - first_row) * COLS, (b - first_row) * COLS) for a, b in zip(low, high)]


def span_mask(start, rows, lo, hi):
    token = start + lax.broadcasted_iota(jnp.int32, (rows, D), 0)
    return (token >= lo) & (token < hi)


def lane_head():
    return lax.broadcasted_iota(jnp.int32, (HD, D), 1) // HD


def lane_slot():
    return lax.broadcasted_iota(jnp.int32, (HD, D), 1) % HD


def fold(full):
    head = lane_head()
    total = jnp.where(head == 0, full[0:HD], 0.0)
    for h in range(1, HEADS):
        total = total + jnp.where(head == h, full[h * HD : h * HD + HD], 0.0)
    return total


def unfold(small):
    head = lane_head()
    return jnp.concatenate([jnp.where(head == h, small, 0.0) for h in range(HEADS)], axis=0)


def group_ones():
    a = lax.broadcasted_iota(jnp.int32, (D, D), 0) // HD
    b = lax.broadcasted_iota(jnp.int32, (D, D), 1) // HD
    return jnp.where(a == b, 1.0, 0.0).astype(BF)


def group_sum(v, ones):
    h = v.astype(BF)
    rest = v - h.astype(F32)
    m = rest.astype(BF)
    l = (rest - m.astype(F32)).astype(BF)
    return dot_nn(h, ones) + (dot_nn(m, ones) + dot_nn(l, ones))


def row_to_fold(row, ones):
    slot = lax.broadcasted_iota(jnp.int32, (HD, D), 0)
    return group_sum(jnp.where(lane_slot() == slot, jnp.broadcast_to(row, (HD, D)), 0.0), ones)


def fold_to_row(small):
    slot = lax.broadcasted_iota(jnp.int32, (HD, D), 0)
    return jnp.sum(jnp.where(lane_slot() == slot, small, 0.0), axis=0, keepdims=True)


def head_row(temp_ref):
    head = lax.broadcasted_iota(jnp.int32, (1, D), 1) // HD
    row = jnp.where(head == 0, temp_ref[0], 0.0)
    for h in range(1, HEADS):
        row = row + jnp.where(head == h, temp_ref[h], 0.0)
    return row


def project_kernel(tall_ref, x_ref, w_ref, tab_ref, q_ref, k_ref, v_ref, sums_ref, wcat, cross):
    step = pl.program_id(0)
    core = lax.axis_index("rows")
    rows_all = 2 * pl.num_programs(0) * TILE // COLS
    spans = slots(tall_ref, core, core * (rows_all // 2), rows_all)
    start = step * TILE

    @pl.when(step == 0)
    def _():
        def part(o):
            h, l = halves(w_ref[pl.ds(o, 64)])
            wcat[pl.ds(o, 64)] = h
            wcat[pl.ds(D + o, 64)] = h
            wcat[pl.ds(2 * D + o, 64)] = l

        sweep(D, 64, part)
        cross[...] = jnp.zeros_like(cross)
        sums_ref[...] = jnp.zeros_like(sums_ref)

    xhat, _ = normalize(x_ref[...])
    lhs = side(xhat * tab_ref[N1G : N1G + 1] + tab_ref[N1S : N1S + 1])
    q = dot_nn(lhs, wcat[:, 0:D]) + tab_ref[QB : QB + 1]
    q_ref[...] = q
    k = dot_nn(lhs, wcat[:, D : 2 * D]) + tab_ref[KB : KB + 1]
    k_ref[...] = k
    v_ref[...] = dot_nn(lhs, wcat[:, 2 * D : 3 * D]) + tab_ref[VB : VB + 1]
    qt = side(q.T)
    for s, (lo, hi) in enumerate(spans):

        @pl.when((lo < start + TILE) & (hi > start))
        def _():
            mask = span_mask(start, TILE, lo, hi)
            kh, kl = halves(jnp.where(mask, k_ref[...], 0.0))
            cross[s] += dot_nn(qt, jnp.concatenate([kh, kh, kl], axis=0))
            qm = jnp.where(mask, q_ref[...], 0.0)
            km = jnp.where(mask, k_ref[...], 0.0)
            sums_ref[s, HD : HD + 1] += jnp.sum(qm * qm, axis=0, keepdims=True)
            sums_ref[s, HD + 1 : HD + 2] += jnp.sum(km * km, axis=0, keepdims=True)

    @pl.when(step == pl.num_programs(0) - 1)
    def _():
        for s in range(3):
            sums_ref[s, 0:HD] = fold(cross[s])


def project(tall, x, w, tab):
    tokens = x.shape[0]
    row = pl.BlockSpec((TILE, D), lambda i: (i, 0))
    return pl.pallas_call(
        project_kernel,
        grid=(tokens // TILE,),
        out_shape=[jax.ShapeDtypeStruct((tokens, D), F32)] * 3
        + [jax.ShapeDtypeStruct((3, HD + 8, D), F32)],
        in_specs=[
            pl.BlockSpec(memory_space=pltpu.SMEM),
            row,
            pl.BlockSpec((D, 3 * D), lambda i: (0, 0)),
            pl.BlockSpec((SMALL, D), lambda i: (0, 0)),
        ],
        out_specs=[row, row, row, pl.BlockSpec((3, HD + 8, D), lambda i: (0, 0, 0))],
        scratch_shapes=[pltpu.VMEM((3 * D, 3 * D), BF), pltpu.VMEM((3, D, D), F32)],
        compiler_params=pltpu.CompilerParams(vmem_limit_bytes=60 << 20),
    )(tall, x, w, tab)


ORDERS = ((0, 1, 2, 3), (1, 2, 0, 3), (2, 0, 1, 3))
PIECE = 256
SHARD = D // 16
DMA = pltpu.SemaphoreType.DMA


class Links:
    def __init__(self):
        self.core = lax.axis_index("rows")
        chip = lax.axis_index("canvas")
        self.bits = (lax.axis_size("canvas") - 1).bit_length()
        self.mine = [lax.rem(lax.div(chip, 1 << b), 2) for b in range(self.bits)]
        self.there = [{"canvas": chip + (1 - 2 * m) * (1 << b)} for b, m in enumerate(self.mine)]
        self.twin = {"rows": 1 - self.core}

    def greet(self):
        barrier = pltpu.get_barrier_semaphore()
        for other in [self.twin] + self.there:
            pl.semaphore_signal(barrier, inc=1, device_id=other, device_id_type=MESH_ID)
        pl.semaphore_wait(barrier, self.bits + 1)


def remote(src, dst, send, recv, other):
    return pltpu.make_async_remote_copy(
        src_ref=src,
        dst_ref=dst,
        send_sem=send,
        recv_sem=recv,
        device_id=other,
        device_id_type=MESH_ID,
    )


class Pieces:
    def __init__(self, links, lanes):
        self.links = links
        self.count = lanes // PIECE

    def lanes(self, p):
        return slice(p * PIECE, p * PIECE + PIECE)

    def bit(self, p, s):
        return ORDERS[p % 3][s]

    def start(self, p, s):
        at = 0
        for t in range(s):
            at = at + self.links.mine[self.bit(p, t)] * (D >> (t + 1))
        return at

    def held(self, p, s):
        return pl.ds(pl.multiple_of(self.start(p, s), 8), D >> s)


class Reduce(Pieces):
    def __init__(self, links, src, buf, work):
        super().__init__(links, src.shape[2])
        self.src, self.buf = src, buf
        self.first, self.land, self.pair_sem, self.send_sem, self.recv_sem = work

    @staticmethod
    def scratch(lanes, bits):
        steps = max(bits, 4)
        count = lanes // PIECE
        return [
            pltpu.VMEM((D, lanes), F32),
            pltpu.VMEM((D - SHARD + (steps - 4) * SHARD, lanes), F32),
            DMA((2, count)),
            DMA((count, steps)),
            DMA((count, steps)),
        ]

    def add(self, p, rows, src, src_rows):
        lanes = self.lanes(p)
        self.buf[rows, lanes] += src[src_rows, lanes]

    def pair(self, p):
        lanes = self.lanes(p)
        return remote(
            self.src.at[1 - self.links.core, :, lanes],
            self.first.at[:, lanes],
            self.pair_sem.at[0, p],
            self.pair_sem.at[1, p],
            self.links.twin,
        )

    def move(self, p, s):
        b = self.bit(p, s)
        half = D >> (s + 1)
        away = pl.multiple_of(self.start(p, s) + (1 - self.links.mine[b]) * half, 8)
        lanes = self.lanes(p)
        return remote(
            self.buf.at[pl.ds(away, half), lanes],
            self.land.at[pl.ds(D - (D >> s), half), lanes],
            self.send_sem.at[p, s],
            self.recv_sem.at[p, s],
            self.links.there[b],
        )

    def begin(self):
        for p in range(self.count):
            self.pair(p).start()

    def join(self):
        for p in range(self.count):
            self.pair(p).wait()
            self.add(p, pl.ds(0, D), self.first, pl.ds(0, D))
            self.move(p, 0).start()

    def down(self, s):
        for p in range(self.count):
            self.move(p, s).wait()
            self.add(p, self.held(p, s + 1), self.land, pl.ds(D - (D >> s), D >> (s + 1)))
            if s < 3:
                self.move(p, s + 1).start()
        if s == 3:
            for b in range(4, self.links.bits):
                self.swap(b)

    def swap(self, b):
        at = pl.ds(D - SHARD + (b - 4) * SHARD, SHARD)
        copies = []
        for p in range(self.count):
            lanes = self.lanes(p)
            copies.append(
                remote(
                    self.buf.at[self.held(p, 4), lanes],
                    self.land.at[at, lanes],
                    self.send_sem.at[p, b],
                    self.recv_sem.at[p, b],
                    self.links.there[b],
                )
            )
            copies[-1].start()
        for p in range(self.count):
            copies[p].wait()
            self.add(p, self.held(p, 4), self.land, at)


class Gather(Pieces):
    def __init__(self, links, whole, dst, work):
        super().__init__(links, whole.shape[1])
        self.whole, self.dst = whole, dst
        self.send_sem, self.recv_sem, self.out_sem = work

    @staticmethod
    def scratch(lanes):
        count = lanes // PIECE
        return [DMA((count, 4)), DMA((count, 4)), DMA((3, count))]

    def back(self, p, s):
        view = self.whole.at[self.held(p, s + 1), self.lanes(p)]
        return remote(
            view,
            view,
            self.send_sem.at[p, s],
            self.recv_sem.at[p, s],
            self.links.there[self.bit(p, s)],
        )

    def outs(self, p):
        src = self.whole.at[:, self.lanes(p)]
        dst = self.dst.at[self.links.core, :, self.lanes(p)]
        return (
            pltpu.make_async_copy(src, dst, self.out_sem.at[0, p]),
            remote(src, dst, self.out_sem.at[1, p], self.out_sem.at[2, p], self.links.twin),
        )

    def begin(self):
        for p in range(self.count):
            self.back(p, 3).start()

    def up(self, s):
        for p in range(self.count):
            self.back(p, s).wait()
            if s > 0:
                self.back(p, s - 1).start()
            else:
                for copy in self.outs(p):
                    copy.start()

    def end(self):
        for p in range(self.count):
            for copy in self.outs(p):
                copy.wait()


def row_flags(tall_ref, rows_all):
    ends = image_ends(tall_ref)

    def above(row):
        first = (row == 0) | (row == ends[0]) | (row == ends[1]) | (row == ends[2])
        return jnp.where(first, 0.0, 1.0)

    def below(row):
        return jnp.where(row + 1 == rows_all, 0.0, above(row + 1))

    return above, below


def middle_kernel(
    tall_ref,
    temp_ref,
    x_hbm,
    dy_hbm,
    v_hbm,
    sums_ref,
    wp_ref,
    w1_hbm,
    w2_ref,
    tab_ref,
    out_hbm,
    ds1_hbm,
    dmx_hbm,
    dwp_ref,
    shard_ref,
    gtab_ref,
    probs_ref,
    unit_ref,
    gprob_ref,
    joint_ref,
    wpv,
    wph,
    w1c,
    w2c,
    pcat,
    mixed,
    s1,
    li,
    act,
    slope,
    mid,
    s2,
    ds2,
    gp,
    z,
    n2c,
    dzc,
    hid_h,
    hid_l,
    hslope,
    b1_ref,
    b1g_ref,
    acc,
    cross,
    x_ref,
    dy_ref,
    v_ref,
    flags,
    nt,
    dt,
    peer_ref,
    dw_ref,
    load_sem,
    store_sem,
    edge_sem,
    *work,
):
    links = Links()
    core = links.core
    wide = x_ref.shape[0]
    tokens = wide - HALO
    dw1_ref, dw2_ref = dw_ref.at[0], dw_ref.at[1]
    reduce = Reduce(links, dw_ref, dw_ref.at[core], work)
    w1_ref = work[0]
    lo_ = x_ref
    own = pl.ds(pl.multiple_of(core * HALO, HALO), tokens)
    pairs = ((w1_hbm, w1_ref), (v_hbm, v_ref.at[own]), (x_hbm, x_ref.at[own]), (dy_hbm, dy_ref.at[own]))
    loads = [pltpu.make_async_copy(a, b, load_sem.at[i]) for i, (a, b) in enumerate(pairs)]
    for load in loads:
        load.start()
    links.greet()
    edge = pl.ds(pl.multiple_of((1 - core) * (tokens - HALO), HALO), HALO)
    far = pl.ds(pl.multiple_of(core * tokens, HALO), HALO)
    pairs = (
        (sums_ref.at[2], peer_ref),
        (v_hbm.at[edge], v_ref.at[far]),
        (x_hbm.at[edge], x_ref.at[far]),
        (dy_hbm.at[edge], dy_ref.at[far]),
    )
    edges = [
        remote(a, b, edge_sem.at[0, i], edge_sem.at[1, i], links.twin)
        for i, (a, b) in enumerate(pairs)
    ]
    own_rows = tokens // COLS
    rows_wide = wide // COLS
    rows_all = 2 * own_rows
    first_row = core * (own_rows - HALO // COLS)
    own_off = pl.multiple_of(core * HALO, HALO)
    mlp = w1_hbm.shape[1]
    spans = slots(tall_ref, core, first_row, rows_all)
    above, below = row_flags(tall_ref, rows_all)

    def tab(r):
        return tab_ref[r : r + 1]

    def is_own(row):
        return (row >= core * (HALO // COLS)) & (row < core * (HALO // COLS) + own_rows)

    loads[0].wait()

    def part_1(o):
        rows = pl.ds(o, 64)
        h, l = halves(w1_ref[rows])
        w1c[rows] = h
        w1c[pl.ds(D + o, 64)] = h
        w1c[pl.ds(2 * D + o, 64)] = l

    sweep(D, 64, part_1)
    for copy in edges:
        copy.start()
    def part_p(o):
        rows = pl.ds(o, 192)
        h, l = halves(wp_ref[rows])
        wpv[rows] = h
        wpv[pl.ds(D + o, 192)] = h
        wpv[pl.ds(2 * D + o, 192)] = l
        wph[rows, 0:D] = h
        wph[rows, D : 2 * D] = h
        wph[rows, 2 * D : 3 * D] = l

    sweep(D, 192, part_p)


    def part_2(o):
        rows = pl.ds(o, 256)
        h, l = halves(w2_ref[rows])
        w2c[rows, 0:D] = h
        w2c[rows, D : 2 * D] = h
        w2c[rows, 2 * D : 3 * D] = l

    sweep(mlp, 256, part_2)

    edges[0].wait()
    ones = group_ones()
    temp = head_row(temp_ref)
    for s in range(3):
        sums = sums_ref[s]
        if s == 2:
            sums = sums + peer_ref[...]
            joint_ref[...] = sums
        inv_q = lax.rsqrt(sums[HD : HD + 1] + EPS)
        inv_k = lax.rsqrt(sums[HD + 1 : HD + 2] + EPS)
        unit = sums[0:HD] * row_to_fold(inv_q, ones) * inv_k
        unit_ref[s] = unit
        weight = jnp.exp(temp * unit)
        probs = weight / group_sum(weight, ones)
        probs_ref[s] = probs
        h, l = halves(unfold(probs))
        pcat[:, 3 * s * D : 3 * s * D + 3 * D] = jnp.concatenate([h, h, l], axis=1)

    acc[...] = jnp.zeros_like(acc)
    gtab_ref[...] = jnp.zeros_like(gtab_ref)

    def add(r, v):
        acc[8 * r : 8 * r + 8] += v

    for copy in loads[1:] + edges[1:]:
        copy.wait()

    def own_part(o, size):
        token = o + lax.broadcasted_iota(jnp.int32, (size, D), 0)
        return jnp.where((token >= own_off) & (token < own_off + tokens), 1.0, 0.0)

    def attend(o):
        size = wide // 3
        v = v_ref[pl.ds(o, size)]
        by_slot = [side(jnp.where(span_mask(o, size, lo, hi), v, 0.0)) for lo, hi in spans]
        mix = dot_nt(jnp.concatenate(by_slot, axis=1), pcat[...])
        mixed[pl.ds(o, size)] = mix
        z[...] = dot_nn(side(mix), wpv[...]) + tab(PB)
        rows = pl.ds(o, size)
        branch = tab(SA) * z[...]
        stream = x_ref[rows] + branch
        s1[rows] = stream
        xhat, _ = normalize(stream)
        li[pl.ds(pl.multiple_of(o + COLS, COLS), size)] = xhat * tab(N3G) + tab(N3S)
        add(41, eights(own_part(o, size) * branch * branch))

    sweep(wide, wide // 3, attend)

    pad = jnp.zeros((COLS, D), F32)
    for buf in (li, mid, gp, ds2):
        buf[0:COLS] = pad
        buf[wide + COLS : wide + 2 * COLS] = pad

    for r in range(rows_wide):
        row = first_row + r
        mine = jnp.where(is_own(r), 1.0, 0.0)
        for n, flag in enumerate((above(row), below(row), mine)):
            flags[n, r * COLS : r * COLS + COLS] = jnp.full((COLS, 128), flag, F32)

    block = 12 * COLS
    col = lax.rem(lax.broadcasted_iota(jnp.int32, (block + 2 * COLS, 128), 0), COLS)

    def convolve(src, base, flip, scale, visit, other=None):
        def one(n, carry):
            lanes = pl.ds(pl.multiple_of(lax.rem(n, 3) * 128, 128), 128)
            o = pl.multiple_of(lax.div(n, 3) * block, block)
            rows = pl.ds(o, block)
            taps = [tab_ref[base + t : base + t + 1, lanes] for t in range(9)]
            if flip:
                taps = taps[::-1]
            if scale is not None:
                taps = [t * tab_ref[scale : scale + 1, lanes] for t in taps]
            u = src[pl.ds(o, block + 2 * COLS), lanes]
            left = jnp.where(col == 0, 0.0, pltpu.roll(u, 1, 0))
            right = jnp.where(col == COLS - 1, 0.0, pltpu.roll(u, block + 2 * COLS - 1, 0))
            up, down = flags[0, rows], flags[1, rows]

            def line(a):
                cut = slice(a * COLS, a * COLS + block)
                return left[cut] * taps[3 * a] + u[cut] * taps[3 * a + 1] + right[cut] * taps[3 * a + 2]

            visit(o, rows, lanes, line(1) + up * line(0) + down * line(2))
            if other is not None:
                near = other[pl.ds(o, block + 2 * COLS), lanes]
                mine = flags[2, rows]
                held = (
                    mine * up * near[0:block],
                    mine * near[COLS : COLS + block],
                    mine * down * near[2 * COLS : 2 * COLS + block],
                )
                inner = slice(COLS, COLS + block)
                for a in range(3):
                    for b, view in enumerate((right, u, left)):
                        t = 8 * (base + 3 * a + b)
                        acc[t : t + 8, lanes] += eights(view[inner] * held[a])
            return carry

        lax.fori_loop(0, 3 * (wide // block), one, 0)

    def first(o, rows, lanes, value):
        at = pl.ds(o + COLS, block)
        a, s = gelu_parts(value + tab_ref[C1B : C1B + 1, lanes])
        act[rows, lanes] = a
        slope[rows, lanes] = s
        mid[at, lanes] = a * tab_ref[BG : BG + 1, lanes] + tab_ref[BS : BS + 1, lanes]

    convolve(li, K1R, False, None, first)

    def second(o, rows, lanes, value):
        value = value + tab_ref[C2B : C2B + 1, lanes]
        lo_[rows, lanes] = value
        branch = tab_ref[SL : SL + 1, lanes] * value
        s2[rows, lanes] = s1[rows, lanes] + branch
        acc[8 * 42 : 8 * 42 + 8, lanes] += eights(flags[2, rows] * branch * branch)

    convolve(mid, K2R, False, None, second)

    dw1_ref[...] = jnp.zeros_like(dw1_ref)
    dw2_ref[...] = jnp.zeros_like(dw2_ref)
    b1g_ref[...] = jnp.zeros_like(b1g_ref)
    for i in range(mlp // D):
        b1_ref[0:1, i * D : i * D + D] = tab(F1B + i)

    def feed(o, size, own):
        rows = pl.ds(0, size)
        here = pl.ds(o, size)
        xhat, _ = normalize(s2[here])
        n2 = xhat * tab(N2G) + tab(N2S)
        h, l = halves(n2)
        n2c[rows, 0:D] = h
        n2c[rows, D : 2 * D] = l
        n2c[rows, 2 * D : 3 * D] = h
        if own:
            nt[...] = side(n2.T)

        raw = tab(F2B)
        pre = dot_nn(n2c[rows], w1c[:, 0:256])
        for j in range(0, mlp, 256):
            lanes = pl.ds(j, 256)
            a, s = gelu_parts(pre + b1_ref[0:1, lanes])
            if j + 256 < mlp:
                pre = dot_nn(n2c[rows], w1c[:, j + 256 : j + 512])
            h, l = halves(a)
            hid_h[rows, lanes] = h
            hid_l[rows, lanes] = l
            hslope[rows, lanes] = s
            w2h, w2l = w2c[lanes, 0:D], w2c[lanes, 2 * D : 3 * D]
            raw = raw + (dot_nn(h, w2h) + (dot_nn(l, w2h) + dot_nn(h, w2l)))
        dy = dy_ref[here]
        dz = tab(SM) * dy
        h, l = halves(dz)
        dzc[rows, 0:D] = h
        dzc[rows, D : 2 * D] = l
        dzc[rows, 2 * D : 3 * D] = h
        if own:
            dt[...] = side(dz.T)
            branch = tab(SM) * raw
            result = s2[here] + branch
            add(40, eights(result * result))
            add(43, eights(branch * branch))
            add(SM, eights(dy * raw))
            add(F2B, eights(dz))

        def down(j):
            lanes = pl.ds(j, 256)
            dpre = dot_nt(dzc[rows], w2c[lanes, :]) * hslope[rows, lanes]
            h, l = halves(dpre)
            if own:
                b1g_ref[:, lanes] += eights(dpre)
                dw1_ref[:, lanes] += dot_nn(nt[...], jnp.concatenate([h, h, l], axis=0))
                hh, hl = hid_h[rows, lanes], hid_l[rows, lanes]
                dw2_ref[:, lanes] += dot_nn(dt[...], jnp.concatenate([hh, hh, hl], axis=0))
            hid_h[rows, lanes] = h
            hid_l[rows, lanes] = l

        sweep(mlp, 256, down)
        w1h, w1l = w1c[0:D], w1c[2 * D : 3 * D]
        dn = dot_nt(hid_h[rows], w1h) + (dot_nt(hid_l[rows], w1h) + dot_nt(hid_h[rows], w1l))
        xhat, r = normalize(s2[here])
        if own:
            s2[here] = result
        ds2[pl.ds(pl.multiple_of(o + COLS, COLS), size)] = dy_ref[here] + normalize_back(
            dn * tab(N2G), xhat, r
        )
        if own:
            add(N2G, eights(dn * xhat))
            add(N2S, eights(dn))

    def feed_one(i, carry):
        feed(pl.multiple_of(own_off + i * TILE, 128), TILE, True)
        return carry

    lax.fori_loop(0, tokens // TILE, feed_one, 0)
    reduce.begin()
    stores = [pltpu.make_async_copy(s2.at[own], out_hbm, store_sem.at[0])]
    stores[0].start()
    edge = HALO // 2
    feed(pl.multiple_of(tokens - core * (tokens - edge), edge), edge, False)
    rest = pl.multiple_of(COLS + (1 - core) * (tokens + edge), COLS)
    ds2[pl.ds(rest, edge)] = jnp.zeros((edge, D), F32)
    reduce.join()

    def third(o, rows, lanes, value):
        grad = value * tab_ref[BG : BG + 1, lanes] * slope[rows, lanes]
        gp[pl.ds(o + COLS, block), lanes] = grad
        held = flags[2, rows] * value
        acc[8 * BG : 8 * BG + 8, lanes] += eights(held * act[rows, lanes])
        acc[8 * BS : 8 * BS + 8, lanes] += eights(held)
        acc[8 * C1B : 8 * C1B + 8, lanes] += eights(flags[2, rows] * grad)

    convolve(ds2, K2R, True, SL, third, mid)
    reduce.down(0)

    def fourth(o, rows, lanes, value):
        slope[rows, lanes] = value

    convolve(gp, K1R, True, None, fourth, li)
    reduce.down(1)

    dwp_ref[...] = jnp.zeros_like(dwp_ref)
    cross[...] = jnp.zeros_like(cross)

    def back(step, carry):
        here = pl.multiple_of(step * TILE, TILE)
        o = pl.multiple_of(own_off + here, 128)

        here_wide = pl.ds(o, TILE)
        xhat, r = normalize(s1[here_wide])
        grad = slope[here_wide]
        grad_two = ds2[pl.ds(pl.multiple_of(o + COLS, COLS), TILE)]
        result = grad_two + normalize_back(grad * tab(N3G), xhat, r)
        slope[here_wide] = result
        add(N3G, eights(grad * xhat))
        add(N3S, eights(grad))
        add(SL, eights(grad_two * lo_[here_wide]))
        add(C2B, eights(grad_two))
        add(PB, eights(result))
        dmx = dot_nt(side(tab(SA) * result), wph[...])
        act[here_wide] = dmx
        h, l = halves(result)
        dwp_ref[...] += dot_nn(side(mixed[pl.ds(o, TILE)].T), jnp.concatenate([h, h, l], axis=0))
        v = v_ref[pl.ds(o, TILE)]
        by_slot = [halves(jnp.where(span_mask(o, TILE, lo, hi), v, 0.0)) for lo, hi in spans]
        high = jnp.concatenate([h for h, l in by_slot], axis=1)
        low = jnp.concatenate([l for h, l in by_slot], axis=1)
        cross[...] += dot_nn(side(dmx.T), jnp.concatenate([high, high, low], axis=0))

        @pl.when(step == 1)
        def _():
            reduce.down(2)

        return carry

    lax.fori_loop(0, tokens // TILE, back, 0)
    for src, dst in ((slope, ds1_hbm), (act, dmx_hbm)):
        stores.append(pltpu.make_async_copy(src.at[own], dst, store_sem.at[len(stores)]))
        stores[-1].start()
    for s in range(3):
        gprob_ref[s] = fold(cross[:, s * D : s * D + D])

    def total(r):
        return jnp.sum(acc[8 * r : 8 * r + 8], axis=0, keepdims=True)

    for r in (N3G, N3S, N2G, N2S, SL, SM, C1B, BG, BS, F2B, 40, 41, 42, 43):
        gtab_ref[r : r + 1] = total(r)
    for t in range(9):
        gtab_ref[K1R + t : K1R + t + 1] = total(K1R + t)
        gtab_ref[K2R + t : K2R + t + 1] = total(K2R + t) * tab(SL)
    gtab_ref[C2B : C2B + 1] = total(C2B) * tab(SL)
    gtab_ref[PB : PB + 1] = total(PB) * tab(SA)
    raw = dwp_ref[...]
    gtab_ref[SA : SA + 1] = jnp.sum(raw * wp_ref[...], axis=0, keepdims=True) + total(PB) * tab(PB)
    dwp_ref[...] = raw * tab(SA)
    for i in range(mlp // D):
        gtab_ref[F1B + i : F1B + i + 1] = jnp.sum(b1g_ref[:, i * D : i * D + D], axis=0, keepdims=True)
    reduce.down(3)
    for p in range(reduce.count):
        lanes = reduce.lanes(p)
        shard_ref[:, lanes] = reduce.buf[reduce.held(p, 4), lanes]
    for copy in stores:
        copy.wait()


def middle(tall, temp, x, dy, v, sums, wp, w1, w2, tab):
    tokens = x.shape[0]
    wide = tokens + HALO
    mlp = w1.shape[1]
    smem = pl.BlockSpec(memory_space=pltpu.SMEM)
    vmem = pl.BlockSpec(memory_space=pltpu.VMEM)
    anywhere = pl.BlockSpec(memory_space=pl.ANY)

    def f(*shape):
        return jax.ShapeDtypeStruct(shape, F32)

    def s(*shape):
        return pltpu.VMEM(shape, F32)

    def b(*shape):
        return pltpu.VMEM(shape, BF)

    padded = s(wide + 2 * COLS, D)
    return pl.pallas_call(
        middle_kernel,
        out_shape=[
            f(tokens, D),
            f(tokens, D),
            f(tokens, D),
            f(D, D),
            f(SHARD, mlp),
            f(TABLE, D),
            f(3, HD, D),
            f(3, HD, D),
            f(3, HD, D),
            f(*sums.shape[1:]),
        ],
        in_specs=[smem, smem] + [anywhere] * 3 + [vmem, vmem, anywhere, vmem, vmem],
        out_specs=[anywhere] * 3 + [vmem] * 7,
        scratch_shapes=[
            b(3 * D, D),
            b(D, 3 * D),
            b(3 * D, mlp),
            b(mlp, 3 * D),
            b(D, 9 * D),
            s(wide, D),
            s(wide, D),
            padded,
            s(wide, D),
            s(wide, D),
            padded,
            s(wide, D),
            padded,
            padded,
            s(wide // 3, D),
            b(TILE, 3 * D),
            b(TILE, 3 * D),
            b(TILE, mlp),
            b(TILE, mlp),
            s(TILE, mlp),
            s(8, mlp),
            s(8, mlp),
            s(8 * TABLE, D),
            s(D, 3 * D),
            s(wide, D),
            s(wide, D),
            s(wide, D),
            s(3, wide, 128),
            b(D, 3 * TILE),
            b(D, 3 * TILE),
            s(*sums.shape[1:]),
            s(2, D, mlp),
            DMA((4,)),
            DMA((3,)),
            DMA((2, 4)),
        ]
        + Reduce.scratch(mlp, (lax.axis_size("canvas") - 1).bit_length()),
        compiler_params=pltpu.CompilerParams(
            collective_id=0, has_side_effects=True, vmem_limit_bytes=60 << 20
        ),
    )(tall, temp, x, dy, v, sums, wp, w1, w2, tab)


def finish_kernel(
    tall_ref,
    temp_ref,
    x_ref,
    q_ref,
    k_ref,
    ds1_ref,
    dmx_ref,
    sums_ref,
    peer_ref,
    probs_ref,
    unit_ref,
    gprob_ref,
    w_ref,
    tab_ref,
    gtab_ref,
    dwp_ref,
    shard_ref,
    dx_ref,
    dw_ref,
    otab_ref,
    sum_hbm,
    wh,
    wl,
    pv,
    cv,
    ch,
    side_rows,
    acc,
    gpeer_ref,
    whole,
    gsend,
    grecv,
    *work,
):
    step = pl.program_id(0)
    last = pl.num_programs(0) - 1
    links = Links()
    core = links.core
    gather = Gather(links, whole, sum_hbm, work)
    rows_all = 2 * pl.num_programs(0) * TILE // COLS
    spans = slots(tall_ref, core, core * (rows_all // 2), rows_all)
    start = step * TILE

    def tab(r):
        return tab_ref[r : r + 1]

    @pl.when(step == 0)
    def _():
        links.greet()
        swap = remote(gprob_ref.at[2], gpeer_ref, gsend, grecv, links.twin)
        swap.start()
        for p in range(gather.count):
            lanes = gather.lanes(p)
            whole[gather.held(p, 4), lanes] = shard_ref[:, lanes]
        gather.begin()

        def part(o):
            h, l = halves(w_ref[pl.ds(o, 64)])
            wh[pl.ds(o, 64)] = h
            wl[pl.ds(o, 64)] = l

        sweep(D, 64, part)
        dw_ref[...] = jnp.zeros_like(dw_ref)
        dw_ref[1, :, D : 2 * D] = dwp_ref[...]
        acc[...] = jnp.zeros_like(acc)
        ones = group_ones()
        temp = head_row(temp_ref)
        heat = jnp.zeros((1, D), F32)
        for s in range(3):
            sums = sums_ref[s]
            grad = gprob_ref[s]
            if s == 2:
                swap.wait()
                sums = peer_ref[...]
                grad = grad + gpeer_ref[...]
            inv_q = lax.rsqrt(sums[HD : HD + 1] + EPS)
            inv_k = lax.rsqrt(sums[HD + 1 : HD + 2] + EPS)
            probs = probs_ref[s]
            unit = unit_ref[s]
            scores = probs * (grad - group_sum(probs * grad, ones))
            part_heat = jnp.sum(scores * unit, axis=0, keepdims=True)
            heat = heat + (part_heat if s < 2 else jnp.where(core == 0, part_heat, 0.0))
            pull = temp * scores
            both = pull * unit
            side_rows[8 * s : 8 * s + 1] = fold_to_row(group_sum(both, ones)) * inv_q * inv_q
            side_rows[8 * s + 1 : 8 * s + 2] = jnp.sum(both, axis=0, keepdims=True) * inv_k * inv_k
            across = slice(3 * s * D, 3 * s * D + 3 * D)
            h, l = halves(unfold(pull * row_to_fold(inv_q, ones) * inv_k))
            cv[across] = jnp.concatenate([h, h, l], axis=0)
            ch[:, across] = jnp.concatenate([h, h, l], axis=1)
            h, l = halves(unfold(probs))
            pv[across] = jnp.concatenate([h, h, l], axis=0)
        otab_ref[...] = gtab_ref[...]
        otab_ref[44:45] = heat

    masks = [span_mask(start, TILE, lo, hi) for lo, hi in spans]

    def by_slot(v):
        return jnp.concatenate([side(jnp.where(mask, v, 0.0)) for mask in masks], axis=1)

    def rows_of(r):
        return sum(jnp.where(mask, side_rows[8 * s + r : 8 * s + r + 1], 0.0) for s, mask in enumerate(masks))

    q, k = q_ref[...], k_ref[...]
    dq = dot_nt(by_slot(k), ch[...]) - q * rows_of(0)
    dk = dot_nn(by_slot(q), cv[...]) - k * rows_of(1)
    dv = dot_nn(by_slot(dmx_ref[...]), pv[...])
    dqkv = jnp.concatenate([dq, dk, dv], axis=1)

    @pl.when(step == 1)
    def _():
        gather.up(2)

    @pl.when(step == 2)
    def _():
        gather.up(1)

    h, l = halves(dqkv)
    dn = dot_nt(h, wh[...]) + (dot_nt(l, wh[...]) + dot_nt(h, wl[...]))
    xhat, r = normalize(x_ref[...])
    nt = side((xhat * tab(N1G) + tab(N1S)).T)
    grads = dot_nn(nt, jnp.concatenate([h, h, l], axis=0))
    dw_ref[0] += grads[:, 0 : 2 * D]
    dw_ref[1, :, 0:D] += grads[:, 2 * D : 3 * D]
    dx_ref[...] = ds1_ref[...] + normalize_back(dn * tab(N1G), xhat, r)
    acc[0:8] += eights(dn * xhat)
    acc[8:16] += eights(dn)
    for i, v in enumerate((dq, dk, dv)):
        acc[16 + 8 * i : 24 + 8 * i] += eights(v)

    @pl.when(step == 0)
    def _():
        gather.up(3)

    @pl.when(step == last)
    def _():
        for i, r in enumerate((N1G, N1S, QB, KB, VB)):
            otab_ref[r : r + 1] = jnp.sum(acc[8 * i : 8 * i + 8], axis=0, keepdims=True)
        gather.up(0)
        gather.end()


def finish(tall, temp, x, q, k, ds1, dmx, sums, peer, probs, unit, gprob, w, tab, gtab, dwp, shard):
    tokens = x.shape[0]
    smem = pl.BlockSpec(memory_space=pltpu.SMEM)
    anywhere = pl.BlockSpec(memory_space=pl.ANY)
    row = pl.BlockSpec((TILE, D), lambda i: (i, 0))

    def whole(v):
        return pl.BlockSpec(v.shape, lambda i: (0,) * v.ndim)

    fixed = (sums, peer, probs, unit, gprob, w, tab, gtab, dwp, shard)
    return pl.pallas_call(
        finish_kernel,
        grid=(tokens // TILE,),
        out_shape=[
            jax.ShapeDtypeStruct((tokens, D), F32),
            jax.ShapeDtypeStruct((2, D, 2 * D), F32),
            jax.ShapeDtypeStruct((TABLE, D), F32),
            jax.ShapeDtypeStruct((2, D, shard.shape[1]), F32),
        ],
        in_specs=[smem, smem] + [row] * 5 + [whole(v) for v in fixed],
        out_specs=[
            row,
            pl.BlockSpec((2, D, 2 * D), lambda i: (0, 0, 0)),
            pl.BlockSpec((TABLE, D), lambda i: (0, 0)),
            anywhere,
        ],
        scratch_shapes=[
            pltpu.VMEM((D, 3 * D), BF),
            pltpu.VMEM((D, 3 * D), BF),
            pltpu.VMEM((9 * D, D), BF),
            pltpu.VMEM((9 * D, D), BF),
            pltpu.VMEM((D, 9 * D), BF),
            pltpu.VMEM((24, D), F32),
            pltpu.VMEM((40, D), F32),
            pltpu.VMEM(gprob.shape[1:], F32),
            pltpu.VMEM((D, shard.shape[1]), F32),
            DMA,
            DMA,
        ]
        + Gather.scratch(shard.shape[1]),
        compiler_params=pltpu.CompilerParams(
            collective_id=1, has_side_effects=True, vmem_limit_bytes=60 << 20
        ),
    )(tall, temp, x, q, k, ds1, dmx, *fixed)


def unit_norm(xs, group):
    norm = 0.0
    for b in group:
        norm = norm + jnp.sum(jnp.sum(xs[b] * xs[b], axis=0, keepdims=True), axis=1, keepdims=True)
    inv = 1.0 / (jnp.sqrt(norm) + 1e-07)
    for b in group:
        xs[b] = xs[b] * inv


def polynomial(xs, group):
    left, right = [], []
    for b in group:
        h, l = halves(xs[b])
        left += [h, l, h]
        right += [h, h, l]
    gram = dot_nt(jnp.concatenate(left, axis=1), jnp.concatenate(right, axis=1))
    h, l = halves(gram)
    square = dot_nn(jnp.concatenate([h, l, h], axis=1), jnp.concatenate([h, h, l], axis=0))
    return side(-4.775 * gram + 2.0315 * square)


def apply_to(xs, group, poly):
    for b in group:
        h, l = halves(xs[b])
        xs[b] = 3.4445 * xs[b] + dot_nn(poly, jnp.concatenate([h, h, l], axis=0))


def wide_kernel(
    end_hbm,
    tab_hbm,
    mid_hbm,
    m1_hbm,
    m2_hbm,
    sum_hbm,
    otab_hbm,
    orth_hbm,
    xs,
    grad,
    m1,
    m2,
    poly,
    tbuf,
    tland,
    load_sem,
    tsend,
    trecv,
    tout,
    buf,
    own_sem,
    *work,
):
    links = Links()
    core = links.core
    reduce = Reduce(links, end_hbm, buf, work[:5])
    gather = Gather(links, work[0], sum_hbm, work[5:])
    own = pltpu.make_async_copy(end_hbm.at[core], buf, own_sem)
    own.start()
    blocks = m1.shape[1] // D
    group = tuple(range(blocks))
    trows = tbuf.shape[0]
    near = pl.ds(pl.multiple_of(core * trows, 8), trows)
    far = pl.ds(pl.multiple_of((1 - core) * trows, 8), trows)
    pairs = ((mid_hbm.at[core], grad), (m1_hbm, m1), (m2_hbm, m2), (tab_hbm.at[near], tbuf))
    loads = [pltpu.make_async_copy(a, b, load_sem.at[i]) for i, (a, b) in enumerate(pairs)]
    for load in loads:
        load.start()
    links.greet()
    reduce.begin()
    top = links.bits

    def table(n):
        if n == top:
            return remote(tab_hbm.at[far], tland.at[n], tsend.at[n], trecv.at[n], links.twin)
        return remote(tbuf, tland.at[n], tsend.at[n], trecv.at[n], links.there[n])

    def table_step(n):
        table(n).start()
        table(n).wait()
        tbuf[...] += tland[n]

    table(top).start()
    for load in loads:
        load.wait()

    @pl.when(core == 0)
    def _():
        for b in group:
            lanes = slice(b * D, b * D + D)
            xs[b] = MUON_KEEP * m1[:, lanes] + grad[:, lanes]

    @pl.when(core == 1)
    def _():
        for b in group:
            xs[b] = MUON_KEEP * m2[b * D : b * D + D].T + grad[:, b * D : b * D + D]

    unit_norm(xs, group)
    table(top).wait()
    tbuf[...] += tland[top]
    own.wait()
    reduce.join()

    def step(i, carry):
        poly[...] = polynomial(xs, group)

        @pl.when(i == 1)
        def _():
            reduce.down(1)
            table_step(1)

        @pl.when(i == 2)
        def _():
            reduce.down(3)
            for p in range(gather.count):
                lanes = gather.lanes(p)
                gather.whole[gather.held(p, 4), lanes] = buf[gather.held(p, 4), lanes]
            gather.begin()
            table_step(3)

        @pl.when(i == 3)
        def _():
            gather.up(2)

        apply_to(xs, group, poly[...])

        @pl.when(i == 0)
        def _():
            reduce.down(0)
            table_step(0)

        @pl.when(i == 1)
        def _():
            reduce.down(2)
            table_step(2)

        @pl.when(i == 2)
        def _():
            gather.up(3)

        @pl.when(i == 3)
        def _():
            gather.up(1)

        @pl.when(i == 4)
        def _():
            gather.up(0)

        return carry

    lax.fori_loop(0, 5, step, 0)
    for b in range(4, links.bits):
        table_step(b)
    touts = [
        pltpu.make_async_copy(tbuf, otab_hbm.at[near], tout.at[0]),
        remote(tbuf, otab_hbm.at[near], tout.at[1], tout.at[2], links.twin),
    ]
    for copy in touts:
        copy.start()

    @pl.when(core == 1)
    def _():
        for b in group:
            xs[b] = xs[b].T

    orth = pltpu.make_async_copy(xs, orth_hbm.at[core], load_sem.at[0])
    orth.start()
    gather.end()
    for copy in touts + [orth]:
        copy.wait()


def wide_blocks(end, tab, mid, m1, m2):
    bits = (lax.axis_size("canvas") - 1).bit_length()
    anywhere = pl.BlockSpec(memory_space=pl.ANY)
    blocks = m1.shape[1] // D
    return pl.pallas_call(
        wide_kernel,
        out_shape=[
            jax.ShapeDtypeStruct(end.shape, F32),
            jax.ShapeDtypeStruct((TABLE, D), F32),
            jax.ShapeDtypeStruct((2, blocks, D, D), F32),
        ],
        in_specs=[anywhere] * 5,
        out_specs=[anywhere] * 3,
        scratch_shapes=[
            pltpu.VMEM((blocks, D, D), F32),
            pltpu.VMEM(m1.shape, F32),
            pltpu.VMEM(m1.shape, F32),
            pltpu.VMEM(m2.shape, F32),
            pltpu.VMEM((D, 3 * D), BF),
            pltpu.VMEM((TABLE // 2, D), F32),
            pltpu.VMEM((bits + 1, TABLE // 2, D), F32),
            DMA((4,)),
            DMA((bits + 1,)),
            DMA((bits + 1,)),
            DMA((3,)),
            pltpu.VMEM(end.shape[1:], F32),
            DMA,
        ]
        + Reduce.scratch(end.shape[2], bits)
        + Gather.scratch(end.shape[2]),
        compiler_params=pltpu.CompilerParams(
            collective_id=2, has_side_effects=True, vmem_limit_bytes=60 << 20
        ),
    )(end, tab, mid, m1, m2)


def square_kernel(
    end_hbm,
    mid_hbm,
    mq_hbm,
    mp_hbm,
    m1_hbm,
    m2_hbm,
    gq_out,
    gp_out,
    g1_out,
    g2_out,
    nq_out,
    np_out,
    n1_out,
    n2_out,
    orth_hbm,
    end,
    mid,
    nat,
    mq,
    mp,
    m1,
    m2,
    xs,
    in_sem,
    out_sem,
):
    core = lax.axis_index("rows")
    blocks = m1.shape[1] // D
    pairs = ((end_hbm, end), (mq_hbm, mq), (mp_hbm, mp), (mid_hbm, mid), (m1_hbm, m1), (m2_hbm, m2))
    loads = [pltpu.make_async_copy(a, b, in_sem.at[i]) for i, (a, b) in enumerate(pairs)]
    for load in loads:
        load.start()
    for load in loads[0:3]:
        load.wait()
    outs = []

    def store(src, dst):
        outs.append(pltpu.make_async_copy(src, dst, out_sem.at[len(outs)]))
        outs[-1].start()

    store(end.at[0], gq_out.at[:, 0 : 2 * D])
    store(end.at[1, :, 0:D], gq_out.at[:, 2 * D : 3 * D])
    store(end.at[1, :, D : 2 * D], gp_out)

    def small(o):
        rows = pl.ds(o, 64)
        mq[rows, 0 : 2 * D] = MUON_KEEP * mq[rows, 0 : 2 * D] + end[0, rows]
        mq[rows, 2 * D : 3 * D] = MUON_KEEP * mq[rows, 2 * D : 3 * D] + end[1, rows, 0:D]
        mp[rows] = MUON_KEEP * mp[rows] + end[1, rows, D : 2 * D]

    sweep(D, 64, small)
    store(mq, nq_out)
    store(mp, np_out)

    @pl.when(core == 0)
    def _():
        xs[0] = mq[:, 0:D]
        xs[1] = mq[:, D : 2 * D]

    @pl.when(core == 1)
    def _():
        xs[0] = mq[:, 2 * D : 3 * D]
        xs[1] = mp[...]

    for b in range(2):
        unit_norm(xs, (b,))

    def step(i, carry):
        for b in range(2):
            apply_to(xs, (b,), polynomial(xs, (b,)))
        return carry

    lax.fori_loop(0, 2, step, 0)
    for load in loads[3:]:
        load.wait()
    store(mid.at[0], g1_out)
    for b in range(blocks):
        nat[b * D : b * D + D] = mid[1, :, b * D : b * D + D].T
    store(nat, g2_out)

    def large(o):
        rows = pl.ds(o, 64)
        m1[rows] = MUON_KEEP * m1[rows] + mid[0, rows]

    sweep(D, 64, large)
    store(m1, n1_out)

    def larger(o):
        rows = pl.ds(o, 256)
        m2[rows] = MUON_KEEP * m2[rows] + nat[rows]

    sweep(blocks * D, 256, larger)
    store(m2, n2_out)
    lax.fori_loop(2, 5, step, 0)
    store(xs, orth_hbm.at[core])
    for copy in outs:
        copy.wait()


def square_blocks(end, mid, mq, mp, m1, m2):
    anywhere = pl.BlockSpec(memory_space=pl.ANY)
    args = (mq, mp, m1, m2)
    return pl.pallas_call(
        square_kernel,
        out_shape=[jax.ShapeDtypeStruct(a.shape, F32) for a in args + args]
        + [jax.ShapeDtypeStruct((2, 2, D, D), F32)],
        in_specs=[anywhere] * 6,
        out_specs=[anywhere] * 9,
        scratch_shapes=[
            pltpu.VMEM(end.shape, F32),
            pltpu.VMEM(mid.shape, F32),
            pltpu.VMEM(m2.shape, F32),
            pltpu.VMEM(mq.shape, F32),
            pltpu.VMEM(mp.shape, F32),
            pltpu.VMEM(m1.shape, F32),
            pltpu.VMEM(m2.shape, F32),
            pltpu.VMEM((2, D, D), F32),
            DMA((6,)),
            DMA((11,)),
        ],
        compiler_params=pltpu.CompilerParams(vmem_limit_bytes=60 << 20),
    )(end, mid, *args)


def trade_kernel(wide_in, square_in, wide_ref, square_ref, send_sem, recv_sem):
    core = lax.axis_index("rows")
    twin = {"rows": 1 - core}
    barrier = pltpu.get_barrier_semaphore()
    pl.semaphore_signal(barrier, inc=1, device_id=twin, device_id_type=MESH_ID)
    pl.semaphore_wait(barrier, 1)
    copies = [
        remote(ref.at[core], ref.at[core], send_sem.at[i], recv_sem.at[i], twin)
        for i, ref in enumerate((wide_ref, square_ref))
    ]
    for copy in copies:
        copy.start()
    for copy in copies:
        copy.wait()


def trade(wide, square):
    anywhere = pl.BlockSpec(memory_space=pl.ANY)
    return pl.pallas_call(
        trade_kernel,
        out_shape=[jax.ShapeDtypeStruct(v.shape, F32) for v in (wide, square)],
        in_specs=[anywhere] * 2,
        out_specs=[anywhere] * 2,
        input_output_aliases={0: 0, 1: 1},
        scratch_shapes=[DMA((2,)), DMA((2,))],
        compiler_params=pltpu.CompilerParams(collective_id=3, has_side_effects=True),
    )(wide, square)


def moment_step(current, one, two, gradient):
    first = BETA1 * one + (1.0 - BETA1) * gradient
    second = BETA2 * two + (1.0 - BETA2) * gradient * gradient
    fix_one = 1.0 - BETA1**STEP
    fix_two = 1.0 - BETA2**STEP
    updated = current - ADAM_RATE * (first / fix_one) / (jnp.sqrt(second / fix_two) + ADAM_FLOOR)
    return first, second, updated


def update_kernel(
    wide_ref,
    last_ref,
    square_ref,
    wq_ref,
    wp_ref,
    w1_ref,
    w2_ref,
    tab_ref,
    one_ref,
    two_ref,
    gtab_ref,
    nq_ref,
    np_ref,
    n1_ref,
    n2_ref,
    cq_ref,
    cp_ref,
    c1_ref,
    c2_ref,
    first_ref,
    second_ref,
    small_ref,
):
    mlp = w1_ref.shape[1]

    def put(new_ref, copy_ref, w, orth, large, lanes):
        new = w * (1.0 - MUON_RATE * DECAY) - MUON_RATE * 0.2 * math.sqrt(large) * orth
        new_ref[:, lanes] = new
        copy_ref[:, lanes] = new.astype(BF)

    for i in range(3):
        lanes = slice(i * D, i * D + D)
        orth = square_ref[0, i] if i < 2 else square_ref[1, 0]
        put(nq_ref, cq_ref, wq_ref[:, lanes], orth, D, lanes)
    put(np_ref, cp_ref, wp_ref[...], square_ref[1, 1], D, slice(0, D))
    for i in range(mlp // D):
        lanes = slice(i * D, i * D + D)
        put(n1_ref, c1_ref, w1_ref[:, lanes], wide_ref[0, i], mlp, lanes)
    put(n2_ref, c2_ref, w2_ref[...], last_ref[0, 0], mlp, slice(0, D))
    first, second, small = moment_step(tab_ref[...], one_ref[...], two_ref[...], gtab_ref[0:SMALL])
    first_ref[...] = first
    second_ref[...] = second
    small_ref[...] = small


def update(wide, square, wq, wp, w1, w2, tab, one, two, gtab):
    blocks = w2.shape[0] // D
    steps = 2 * blocks
    piece = D // steps

    def rows(v):
        size = v.shape[0] // steps
        return pl.BlockSpec((size, v.shape[1]), lambda i: (i, 0))

    def whole(v):
        return pl.BlockSpec(v.shape, lambda i: (0, 0))

    weights = (wq, wp, w1, w2)
    return pl.pallas_call(
        update_kernel,
        grid=(steps,),
        out_shape=[jax.ShapeDtypeStruct(w.shape, F32) for w in weights]
        + [jax.ShapeDtypeStruct(w.shape, BF) for w in weights]
        + [jax.ShapeDtypeStruct(tab.shape, F32)] * 3,
        in_specs=[
            pl.BlockSpec((1, blocks, piece, D), lambda i: (0, 0, i, 0)),
            pl.BlockSpec((1, 1, D // 2, D), lambda i: (1, i // 2, i % 2, 0)),
            pl.BlockSpec((2, 2, piece, D), lambda i: (0, 0, i, 0)),
        ]
        + [rows(w) for w in weights]
        + [whole(v) for v in (tab, one, two, gtab)],
        out_specs=[rows(w) for w in weights] * 2 + [whole(tab)] * 3,
        compiler_params=pltpu.CompilerParams(vmem_limit_bytes=60 << 20),
    )(wide, wide, square, *weights, tab, one, two, gtab)


def on_device(
    x4, dy4, tall, wqkv, wp, w1, w2, mqkv, mp, m1, m2, tab, tab_one, tab_two, temp, temp_one, temp_two
):
    shape = x4.shape
    tokens = shape[1] * shape[2]
    x = x4.reshape(tokens, D)
    dy = dy4.reshape(tokens, D)
    q, k, v, sums = project(tall, x, wqkv, tab)
    out, ds1, dmx, dwp, shard, gtab, probs, unit, gprob, joint = middle(
        tall, temp, x, dy, v, sums, wp, w1, w2, tab
    )
    dx, end, gtab, mid = finish(
        tall, temp, x, q, k, ds1, dmx, sums, joint, probs, unit, gprob, wqkv, tab, gtab, dwp, shard
    )
    end, gtab, wide = wide_blocks(end, gtab, mid, m1, m2)
    *grads, square = square_blocks(end, mid, mqkv, mp, m1, m2)
    wide, square = trade(wide, square)
    results = update(wide, square, wqkv, wp, w1, w2, tab, tab_one, tab_two, gtab)
    heat = jnp.sum(gtab[44].reshape(HEADS, HD), axis=1)
    warm = moment_step(temp, temp_one, temp_two, heat)
    count = tokens * D * lax.axis_size("rows") * lax.axis_size("canvas")
    rms = jnp.sqrt(jnp.sum(gtab[40:44], axis=1) / count)
    return (out.reshape(shape), dx.reshape(shape), *grads, *results, *warm, rms)


def solution(mesh):
    split = P("canvas", "rows", None, None)
    return jax.shard_map(
        on_device,
        mesh=mesh,
        in_specs=(split, split, P("canvas", None)) + (P(),) * 14,
        out_specs=(split, split) + (P(),) * 23,
        check_vma=False,
    )
```

```python
import math

import jax
import jax.numpy as jnp
from jax import lax
from jax.experimental import pallas as pl
from jax.experimental.pallas import tpu as pltpu
from jax.sharding import PartitionSpec as P

BF = jnp.bfloat16
F32 = jnp.float32
MESH_ID = pl.DeviceIdType.MESH

EPS = 1e-06
ROOT_HALF = 1.0 / math.sqrt(2.0)
ROOT_TWOPI = 1.0 / math.sqrt(2.0 * math.pi)
STEP = 10
MUON_RATE = 0.2
MUON_KEEP = 0.95
DECAY = 0.01
ADAM_RATE = 0.2
BETA1 = 0.9
BETA2 = 0.95
ADAM_FLOOR = 1e-08

HEADS = 8
HD = 48
D = HEADS * HD
COLS = 32
HALO = 4 * COLS
TILE = 256

N1G, N1S, N3G, N3S, N2G, N2S, SA, SL, SM, QB, KB, VB, PB, C1B, BG, BS, C2B, F2B = range(18)
F1B, K1R, K2R = 18, 22, 31
SMALL = 40
TABLE = 48


def halves(v):
    hi = v.astype(BF)
    return hi, (v - hi.astype(F32)).astype(BF)


def side(v):
    h, l = halves(v)
    return jnp.concatenate([h, l, h], axis=1)


def dot_nn(a, b):
    return lax.dot_general(a, b, (((1,), (0,)), ((), ())), preferred_element_type=F32)


def dot_nt(a, b):
    return lax.dot_general(a, b, (((1,), (1,)), ((), ())), preferred_element_type=F32)


def normalize(v):
    mean = jnp.mean(v, axis=1, keepdims=True)
    c = v - mean
    r = lax.rsqrt(jnp.mean(c * c, axis=1, keepdims=True) + EPS)
    return c * r, r


def normalize_back(e, xhat, r):
    return r * (
        e - jnp.mean(e, axis=1, keepdims=True) - xhat * jnp.mean(e * xhat, axis=1, keepdims=True)
    )


def gelu_parts(v):
    phi = 0.5 * (1.0 + lax.erf(v * ROOT_HALF))
    return v * phi, phi + v * jnp.exp(-0.5 * v * v) * ROOT_TWOPI


def eights(v):
    total = v[0:8]
    for i in range(8, v.shape[0], 8):
        total = total + v[i : i + 8]
    return total


def sweep(count, size, body):
    def one(i, carry):
        body(pl.multiple_of(i * size, size))
        return carry

    lax.fori_loop(0, count // size, one, 0)


def image_ends(tall_ref):
    e0 = tall_ref[0, 0]
    e1 = e0 + tall_ref[0, 1]
    return e0, e1, e1 + tall_ref[0, 2]


def slots(tall_ref, core, first_row, rows_all):
    e0, e1, e2 = image_ends(tall_ref)
    low = (jnp.where(core == 0, 0, e2), jnp.where(core == 0, e0, 0), e1)
    high = (jnp.where(core == 0, e0, rows_all), jnp.where(core == 0, e1, 0), e2)
    return [((a - first_row) * COLS, (b - first_row) * COLS) for a, b in zip(low, high)]


def span_mask(start, rows, lo, hi):
    token = start + lax.broadcasted_iota(jnp.int32, (rows, D), 0)
    return (token >= lo) & (token < hi)


def lane_head():
    return lax.broadcasted_iota(jnp.int32, (HD, D), 1) // HD


def lane_slot():
    return lax.broadcasted_iota(jnp.int32, (HD, D), 1) % HD


def fold(full):
    head = lane_head()
    total = jnp.where(head == 0, full[0:HD], 0.0)
    for h in range(1, HEADS):
        total = total + jnp.where(head == h, full[h * HD : h * HD + HD], 0.0)
    return total


def unfold(small):
    head = lane_head()
    return jnp.concatenate([jnp.where(head == h, small, 0.0) for h in range(HEADS)], axis=0)


def group_ones():
    a = lax.broadcasted_iota(jnp.int32, (D, D), 0) // HD
    b = lax.broadcasted_iota(jnp.int32, (D, D), 1) // HD
    return jnp.where(a == b, 1.0, 0.0).astype(BF)


def group_sum(v, ones):
    h = v.astype(BF)
    rest = v - h.astype(F32)
    m = rest.astype(BF)
    l = (rest - m.astype(F32)).astype(BF)
    return dot_nn(h, ones) + (dot_nn(m, ones) + dot_nn(l, ones))


def row_to_fold(row, ones):
    slot = lax.broadcasted_iota(jnp.int32, (HD, D), 0)
    return group_sum(jnp.where(lane_slot() == slot, jnp.broadcast_to(row, (HD, D)), 0.0), ones)


def fold_to_row(small):
    slot = lax.broadcasted_iota(jnp.int32, (HD, D), 0)
    return jnp.sum(jnp.where(lane_slot() == slot, small, 0.0), axis=0, keepdims=True)


def head_row(temp_ref):
    head = lax.broadcasted_iota(jnp.int32, (1, D), 1) // HD
    row = jnp.where(head == 0, temp_ref[0], 0.0)
    for h in range(1, HEADS):
        row = row + jnp.where(head == h, temp_ref[h], 0.0)
    return row


def project_kernel(tall_ref, x_ref, w_ref, tab_ref, q_ref, k_ref, v_ref, sums_ref, wcat, cross):
    step = pl.program_id(0)
    core = lax.axis_index("rows")
    rows_all = 2 * pl.num_programs(0) * TILE // COLS
    spans = slots(tall_ref, core, core * (rows_all // 2), rows_all)
    start = step * TILE

    @pl.when(step == 0)
    def _():
        def part(o):
            h, l = halves(w_ref[pl.ds(o, 64)])
            wcat[pl.ds(o, 64)] = h
            wcat[pl.ds(D + o, 64)] = h
            wcat[pl.ds(2 * D + o, 64)] = l

        sweep(D, 64, part)
        cross[...] = jnp.zeros_like(cross)
        sums_ref[...] = jnp.zeros_like(sums_ref)

    xhat, _ = normalize(x_ref[...])
    lhs = side(xhat * tab_ref[N1G : N1G + 1] + tab_ref[N1S : N1S + 1])
    q = dot_nn(lhs, wcat[:, 0:D]) + tab_ref[QB : QB + 1]
    q_ref[...] = q
    k = dot_nn(lhs, wcat[:, D : 2 * D]) + tab_ref[KB : KB + 1]
    k_ref[...] = k
    v_ref[...] = dot_nn(lhs, wcat[:, 2 * D : 3 * D]) + tab_ref[VB : VB + 1]
    qt = side(q.T)
    for s, (lo, hi) in enumerate(spans):

        @pl.when((lo < start + TILE) & (hi > start))
        def _():
            mask = span_mask(start, TILE, lo, hi)
            kh, kl = halves(jnp.where(mask, k_ref[...], 0.0))
            cross[s] += dot_nn(qt, jnp.concatenate([kh, kh, kl], axis=0))
            qm = jnp.where(mask, q_ref[...], 0.0)
            km = jnp.where(mask, k_ref[...], 0.0)
            sums_ref[s, HD : HD + 1] += jnp.sum(qm * qm, axis=0, keepdims=True)
            sums_ref[s, HD + 1 : HD + 2] += jnp.sum(km * km, axis=0, keepdims=True)

    @pl.when(step == pl.num_programs(0) - 1)
    def _():
        for s in range(3):
            sums_ref[s, 0:HD] = fold(cross[s])


def project(tall, x, w, tab):
    tokens = x.shape[0]
    row = pl.BlockSpec((TILE, D), lambda i: (i, 0))
    return pl.pallas_call(
        project_kernel,
        grid=(tokens // TILE,),
        out_shape=[jax.ShapeDtypeStruct((tokens, D), F32)] * 3
        + [jax.ShapeDtypeStruct((3, HD + 8, D), F32)],
        in_specs=[
            pl.BlockSpec(memory_space=pltpu.SMEM),
            row,
            pl.BlockSpec((D, 3 * D), lambda i: (0, 0)),
            pl.BlockSpec((SMALL, D), lambda i: (0, 0)),
        ],
        out_specs=[row, row, row, pl.BlockSpec((3, HD + 8, D), lambda i: (0, 0, 0))],
        scratch_shapes=[pltpu.VMEM((3 * D, 3 * D), BF), pltpu.VMEM((3, D, D), F32)],
        compiler_params=pltpu.CompilerParams(vmem_limit_bytes=60 << 20),
    )(tall, x, w, tab)


ORDERS = ((0, 1, 2, 3), (1, 2, 0, 3), (2, 0, 1, 3))
PIECE = 256
SHARD = D // 16
DMA = pltpu.SemaphoreType.DMA


class Links:
    def __init__(self):
        self.core = lax.axis_index("rows")
        chip = lax.axis_index("canvas")
        self.bits = (lax.axis_size("canvas") - 1).bit_length()
        self.mine = [lax.rem(lax.div(chip, 1 << b), 2) for b in range(self.bits)]
        self.there = [{"canvas": chip + (1 - 2 * m) * (1 << b)} for b, m in enumerate(self.mine)]
        self.twin = {"rows": 1 - self.core}

    def call(self):
        barrier = pltpu.get_barrier_semaphore()
        for other in [self.twin] + self.there:
            pl.semaphore_signal(barrier, inc=1, device_id=other, device_id_type=MESH_ID)

    def answer(self):
        pl.semaphore_wait(pltpu.get_barrier_semaphore(), self.bits + 1)

    def greet(self):
        self.call()
        self.answer()


def remote(src, dst, send, recv, other):
    return pltpu.make_async_remote_copy(
        src_ref=src,
        dst_ref=dst,
        send_sem=send,
        recv_sem=recv,
        device_id=other,
        device_id_type=MESH_ID,
    )


class Pieces:
    def __init__(self, links, lanes):
        self.links = links
        self.count = lanes // PIECE

    def lanes(self, p):
        return slice(p * PIECE, p * PIECE + PIECE)

    def bit(self, p, s):
        return ORDERS[p % 3][s]

    def start(self, p, s):
        at = 0
        for t in range(s):
            at = at + self.links.mine[self.bit(p, t)] * (D >> (t + 1))
        return at

    def held(self, p, s):
        return pl.ds(pl.multiple_of(self.start(p, s), 8), D >> s)


class Reduce(Pieces):
    def __init__(self, links, src, buf, work):
        super().__init__(links, src.shape[2])
        self.src, self.buf = src, buf
        self.first, self.land, self.pair_sem, self.send_sem, self.recv_sem = work

    @staticmethod
    def scratch(lanes, bits):
        steps = max(bits, 4)
        count = lanes // PIECE
        return [
            pltpu.VMEM((D, lanes), F32),
            pltpu.VMEM((D - SHARD + (steps - 4) * SHARD, lanes), F32),
            DMA((2, count)),
            DMA((count, steps)),
            DMA((count, steps)),
        ]

    def add(self, p, rows, src, src_rows):
        lanes = self.lanes(p)
        self.buf[rows, lanes] += src[src_rows, lanes]

    def pair(self, p):
        lanes = self.lanes(p)
        return remote(
            self.src.at[1 - self.links.core, :, lanes],
            self.first.at[:, lanes],
            self.pair_sem.at[0, p],
            self.pair_sem.at[1, p],
            self.links.twin,
        )

    def move(self, p, s):
        b = self.bit(p, s)
        half = D >> (s + 1)
        away = pl.multiple_of(self.start(p, s) + (1 - self.links.mine[b]) * half, 8)
        lanes = self.lanes(p)
        return remote(
            self.buf.at[pl.ds(away, half), lanes],
            self.land.at[pl.ds(D - (D >> s), half), lanes],
            self.send_sem.at[p, s],
            self.recv_sem.at[p, s],
            self.links.there[b],
        )

    def begin(self):
        for p in range(self.count):
            self.pair(p).start()

    def join(self):
        for p in range(self.count):
            self.pair(p).wait()
            self.add(p, pl.ds(0, D), self.first, pl.ds(0, D))
            self.move(p, 0).start()

    def down(self, s):
        for p in range(self.count):
            self.move(p, s).wait()
            self.add(p, self.held(p, s + 1), self.land, pl.ds(D - (D >> s), D >> (s + 1)))
            if s < 3:
                self.move(p, s + 1).start()
        if s == 3:
            for b in range(4, self.links.bits):
                self.swap(b)

    def swap(self, b):
        at = pl.ds(D - SHARD + (b - 4) * SHARD, SHARD)
        copies = []
        for p in range(self.count):
            lanes = self.lanes(p)
            copies.append(
                remote(
                    self.buf.at[self.held(p, 4), lanes],
                    self.land.at[at, lanes],
                    self.send_sem.at[p, b],
                    self.recv_sem.at[p, b],
                    self.links.there[b],
                )
            )
            copies[-1].start()
        for p in range(self.count):
            copies[p].wait()
            self.add(p, self.held(p, 4), self.land, at)


class Gather(Pieces):
    def __init__(self, links, whole, dst, work):
        super().__init__(links, whole.shape[1])
        self.whole, self.dst = whole, dst
        self.send_sem, self.recv_sem, self.out_sem = work

    @staticmethod
    def scratch(lanes):
        count = lanes // PIECE
        return [DMA((count, 4)), DMA((count, 4)), DMA((3, count))]

    def back(self, p, s):
        view = self.whole.at[self.held(p, s + 1), self.lanes(p)]
        return remote(
            view,
            view,
            self.send_sem.at[p, s],
            self.recv_sem.at[p, s],
            self.links.there[self.bit(p, s)],
        )

    def outs(self, p):
        src = self.whole.at[:, self.lanes(p)]
        dst = self.dst.at[self.links.core, :, self.lanes(p)]
        return (
            pltpu.make_async_copy(src, dst, self.out_sem.at[0, p]),
            remote(src, dst, self.out_sem.at[1, p], self.out_sem.at[2, p], self.links.twin),
        )

    def begin(self):
        for p in range(self.count):
            self.back(p, 3).start()

    def up(self, s):
        for p in range(self.count):
            self.back(p, s).wait()
            if s > 0:
                self.back(p, s - 1).start()
            else:
                for copy in self.outs(p):
                    copy.start()

    def end(self):
        for p in range(self.count):
            for copy in self.outs(p):
                copy.wait()


def row_flags(tall_ref, rows_all):
    ends = image_ends(tall_ref)

    def above(row):
        first = (row == 0) | (row == ends[0]) | (row == ends[1]) | (row == ends[2])
        return jnp.where(first, 0.0, 1.0)

    def below(row):
        return jnp.where(row + 1 == rows_all, 0.0, above(row + 1))

    return above, below


def middle_kernel(
    tall_ref,
    temp_ref,
    x_hbm,
    dy_hbm,
    v_hbm,
    sums_ref,
    wp_ref,
    w1_hbm,
    w2_ref,
    tab_ref,
    out_hbm,
    ds1_hbm,
    dmx_hbm,
    dwp_ref,
    shard_ref,
    gtab_ref,
    probs_ref,
    unit_ref,
    gprob_ref,
    joint_ref,
    wpv,
    wph,
    w1c,
    w2c,
    pcat,
    mixed,
    s1,
    li,
    act,
    slope,
    mid,
    s2,
    ds2,
    gp,
    z,
    n2c,
    dzc,
    b1_ref,
    b1g_ref,
    acc,
    cross,
    x_ref,
    dy_ref,
    v_ref,
    flags,
    nt,
    dt,
    peer_ref,
    dw_ref,
    load_sem,
    store_sem,
    edge_sem,
    *work,
):
    links = Links()
    core = links.core
    wide = x_ref.shape[0]
    tokens = wide - HALO
    dw1_ref, dw2_ref = dw_ref.at[0], dw_ref.at[1]
    reduce = Reduce(links, dw_ref, dw_ref.at[core], work)
    w1_ref = work[0]
    lo_ = x_ref
    own = pl.ds(pl.multiple_of(core * HALO, HALO), tokens)
    pairs = ((w1_hbm, w1_ref), (v_hbm, v_ref.at[own]), (x_hbm, x_ref.at[own]), (dy_hbm, dy_ref.at[own]))
    loads = [pltpu.make_async_copy(a, b, load_sem.at[i]) for i, (a, b) in enumerate(pairs)]
    for load in loads:
        load.start()
    links.call()
    edge = pl.ds(pl.multiple_of((1 - core) * (tokens - HALO), HALO), HALO)
    far = pl.ds(pl.multiple_of(core * tokens, HALO), HALO)
    pairs = (
        (sums_ref.at[2], peer_ref),
        (v_hbm.at[edge], v_ref.at[far]),
        (x_hbm.at[edge], x_ref.at[far]),
        (dy_hbm.at[edge], dy_ref.at[far]),
    )
    edges = [
        remote(a, b, edge_sem.at[0, i], edge_sem.at[1, i], links.twin)
        for i, (a, b) in enumerate(pairs)
    ]
    own_rows = tokens // COLS
    rows_wide = wide // COLS
    rows_all = 2 * own_rows
    first_row = core * (own_rows - HALO // COLS)
    own_off = pl.multiple_of(core * HALO, HALO)
    mlp = w1_hbm.shape[1]
    spans = slots(tall_ref, core, first_row, rows_all)
    above, below = row_flags(tall_ref, rows_all)

    def tab(r):
        return tab_ref[r : r + 1]

    def is_own(row):
        return (row >= core * (HALO // COLS)) & (row < core * (HALO // COLS) + own_rows)

    loads[0].wait()

    def part_1(o):
        rows = pl.ds(o, 64)
        h, l = halves(w1_ref[rows])
        w1c[rows] = h
        w1c[pl.ds(D + o, 64)] = h
        w1c[pl.ds(2 * D + o, 64)] = l

    sweep(D, 64, part_1)
    links.answer()
    for copy in edges:
        copy.start()

    def part_p(o):
        rows = pl.ds(o, 192)
        h, l = halves(wp_ref[rows])
        wpv[rows] = h
        wpv[pl.ds(D + o, 192)] = h
        wpv[pl.ds(2 * D + o, 192)] = l
        wph[rows, 0:D] = h
        wph[rows, D : 2 * D] = h
        wph[rows, 2 * D : 3 * D] = l

    sweep(D, 192, part_p)

    def part_2(o):
        rows = pl.ds(o, 256)
        h, l = halves(w2_ref[rows])
        w2c[rows, 0:D] = h
        w2c[rows, D : 2 * D] = h
        w2c[rows, 2 * D : 3 * D] = l

    sweep(mlp, 256, part_2)

    edges[0].wait()
    ones = group_ones()
    temp = head_row(temp_ref)
    for s in range(3):
        sums = sums_ref[s]
        if s == 2:
            sums = sums + peer_ref[...]
            joint_ref[...] = sums
        inv_q = lax.rsqrt(sums[HD : HD + 1] + EPS)
        inv_k = lax.rsqrt(sums[HD + 1 : HD + 2] + EPS)
        unit = sums[0:HD] * row_to_fold(inv_q, ones) * inv_k
        unit_ref[s] = unit
        weight = jnp.exp(temp * unit)
        probs = weight / group_sum(weight, ones)
        probs_ref[s] = probs
        h, l = halves(unfold(probs))
        pcat[:, 3 * s * D : 3 * s * D + 3 * D] = jnp.concatenate([h, h, l], axis=1)

    acc[...] = jnp.zeros_like(acc)
    gtab_ref[...] = jnp.zeros_like(gtab_ref)

    def add(r, v):
        acc[8 * r : 8 * r + 8] += v

    for copy in loads[1:] + edges[1:]:
        copy.wait()

    def own_part(o, size):
        token = o + lax.broadcasted_iota(jnp.int32, (size, D), 0)
        return jnp.where((token >= own_off) & (token < own_off + tokens), 1.0, 0.0)

    def attend(o):
        size = wide // 3
        v = v_ref[pl.ds(o, size)]
        by_slot = [side(jnp.where(span_mask(o, size, lo, hi), v, 0.0)) for lo, hi in spans]
        mix = dot_nt(jnp.concatenate(by_slot, axis=1), pcat[...])
        mixed[pl.ds(o, size)] = mix
        z[...] = dot_nn(side(mix), wpv[...]) + tab(PB)
        rows = pl.ds(o, size)
        branch = tab(SA) * z[...]
        stream = x_ref[rows] + branch
        s1[rows] = stream
        xhat, _ = normalize(stream)
        li[pl.ds(pl.multiple_of(o + COLS, COLS), size)] = xhat * tab(N3G) + tab(N3S)
        add(41, eights(own_part(o, size) * branch * branch))

    sweep(wide, wide // 3, attend)

    pad = jnp.zeros((COLS, D), F32)
    for buf in (li, mid, gp, ds2):
        buf[0:COLS] = pad
        buf[wide + COLS : wide + 2 * COLS] = pad

    for r in range(rows_wide):
        row = first_row + r
        mine = jnp.where(is_own(r), 1.0, 0.0)
        for n, flag in enumerate((above(row), below(row), mine)):
            flags[n, r * COLS : r * COLS + COLS] = jnp.full((COLS, 128), flag, F32)

    block = 12 * COLS
    col = lax.rem(lax.broadcasted_iota(jnp.int32, (block + 2 * COLS, 128), 0), COLS)

    def convolve(src, base, flip, scale, visit, other=None):
        def one(n, carry):
            lanes = pl.ds(pl.multiple_of(lax.rem(n, 3) * 128, 128), 128)
            o = pl.multiple_of(lax.div(n, 3) * block, block)
            rows = pl.ds(o, block)
            taps = [tab_ref[base + t : base + t + 1, lanes] for t in range(9)]
            if flip:
                taps = taps[::-1]
            if scale is not None:
                taps = [t * tab_ref[scale : scale + 1, lanes] for t in taps]
            u = src[pl.ds(o, block + 2 * COLS), lanes]
            left = jnp.where(col == 0, 0.0, pltpu.roll(u, 1, 0))
            right = jnp.where(col == COLS - 1, 0.0, pltpu.roll(u, block + 2 * COLS - 1, 0))
            up, down = flags[0, rows], flags[1, rows]

            def line(a):
                cut = slice(a * COLS, a * COLS + block)
                return left[cut] * taps[3 * a] + u[cut] * taps[3 * a + 1] + right[cut] * taps[3 * a + 2]

            visit(o, rows, lanes, line(1) + up * line(0) + down * line(2))
            if other is not None:
                near = other[pl.ds(o, block + 2 * COLS), lanes]
                mine = flags[2, rows]
                held = (
                    mine * up * near[0:block],
                    mine * near[COLS : COLS + block],
                    mine * down * near[2 * COLS : 2 * COLS + block],
                )
                inner = slice(COLS, COLS + block)
                for a in range(3):
                    for b, view in enumerate((right, u, left)):
                        t = 8 * (base + 3 * a + b)
                        acc[t : t + 8, lanes] += eights(view[inner] * held[a])
            return carry

        lax.fori_loop(0, 3 * (wide // block), one, 0)

    def first(o, rows, lanes, value):
        at = pl.ds(o + COLS, block)
        a, s = gelu_parts(value + tab_ref[C1B : C1B + 1, lanes])
        act[rows, lanes] = a
        slope[rows, lanes] = s
        mid[at, lanes] = a * tab_ref[BG : BG + 1, lanes] + tab_ref[BS : BS + 1, lanes]

    convolve(li, K1R, False, None, first)

    def second(o, rows, lanes, value):
        value = value + tab_ref[C2B : C2B + 1, lanes]
        lo_[rows, lanes] = value
        branch = tab_ref[SL : SL + 1, lanes] * value
        s2[rows, lanes] = s1[rows, lanes] + branch
        acc[8 * 42 : 8 * 42 + 8, lanes] += eights(flags[2, rows] * branch * branch)

    convolve(mid, K2R, False, None, second)

    dw1_ref[...] = jnp.zeros_like(dw1_ref)
    dw2_ref[...] = jnp.zeros_like(dw2_ref)
    b1g_ref[...] = jnp.zeros_like(b1g_ref)
    for i in range(mlp // D):
        b1_ref[0:1, i * D : i * D + D] = tab(F1B + i)

    def feed(o, size, own):
        rows = pl.ds(0, size)
        here = pl.ds(o, size)
        xhat, _ = normalize(s2[here])
        n2 = xhat * tab(N2G) + tab(N2S)
        n2c[rows] = side(n2)
        dz = tab(SM) * dy_ref[here]
        dzc[rows] = side(dz)
        if own:
            nt[...] = side(n2.T)
            dt[...] = side(dz.T)
            add(F2B, eights(dz))

        def enter(j):
            return dot_nn(n2c[rows], w1c[:, j : j + PIECE]), dot_nt(dzc[rows], w2c[j : j + PIECE])

        raw, dn = tab(F2B), 0.0
        ready = enter(0)
        for j in range(0, mlp, PIECE):
            lanes = slice(j, j + PIECE)
            pre, dh = ready
            if j + PIECE < mlp:
                ready = enter(j + PIECE)
            a, slope_j = gelu_parts(pre + b1_ref[0:1, lanes])
            dp = dh * slope_j
            ah, al = halves(a)
            ph, pl_ = halves(dp)
            w2h, w2l = w2c[lanes, 0:D], w2c[lanes, 2 * D : 3 * D]
            raw = raw + (dot_nn(ah, w2h) + (dot_nn(al, w2h) + dot_nn(ah, w2l)))
            w1h, w1l = w1c[0:D, lanes], w1c[2 * D : 3 * D, lanes]
            dn = dn + (dot_nt(ph, w1h) + (dot_nt(pl_, w1h) + dot_nt(ph, w1l)))
            if own:
                b1g_ref[:, lanes] += eights(dp)
                dw1_ref[:, lanes] += dot_nn(nt[...], jnp.concatenate([ph, ph, pl_], axis=0))
                dw2_ref[:, lanes] += dot_nn(dt[...], jnp.concatenate([ah, ah, al], axis=0))
        dy = dy_ref[here]
        xhat, r = normalize(s2[here])
        ds2[pl.ds(pl.multiple_of(o + COLS, COLS), size)] = dy + normalize_back(dn * tab(N2G), xhat, r)
        if own:
            branch = tab(SM) * raw
            result = s2[here] + branch
            s2[here] = result
            add(40, eights(result * result))
            add(43, eights(branch * branch))
            add(SM, eights(dy * raw))
            add(N2G, eights(dn * xhat))
            add(N2S, eights(dn))

    def feed_one(i, carry):
        feed(pl.multiple_of(own_off + i * TILE, 128), TILE, True)
        return carry

    lax.fori_loop(0, tokens // TILE, feed_one, 0)
    reduce.begin()
    stores = [pltpu.make_async_copy(s2.at[own], out_hbm, store_sem.at[0])]
    stores[0].start()
    edge = HALO // 2
    feed(pl.multiple_of(tokens - core * (tokens - edge), edge), edge, False)
    rest = pl.multiple_of(COLS + (1 - core) * (tokens + edge), COLS)
    ds2[pl.ds(rest, edge)] = jnp.zeros((edge, D), F32)
    reduce.join()

    def third(o, rows, lanes, value):
        grad = value * tab_ref[BG : BG + 1, lanes] * slope[rows, lanes]
        gp[pl.ds(o + COLS, block), lanes] = grad
        held = flags[2, rows] * value
        acc[8 * BG : 8 * BG + 8, lanes] += eights(held * act[rows, lanes])
        acc[8 * BS : 8 * BS + 8, lanes] += eights(held)
        acc[8 * C1B : 8 * C1B + 8, lanes] += eights(flags[2, rows] * grad)

    convolve(ds2, K2R, True, SL, third, mid)
    reduce.down(0)

    def fourth(o, rows, lanes, value):
        slope[rows, lanes] = value

    convolve(gp, K1R, True, None, fourth, li)
    reduce.down(1)

    dwp_ref[...] = jnp.zeros_like(dwp_ref)
    cross[...] = jnp.zeros_like(cross)

    def back(step, carry):
        here = pl.multiple_of(step * TILE, TILE)
        o = pl.multiple_of(own_off + here, 128)

        here_wide = pl.ds(o, TILE)
        xhat, r = normalize(s1[here_wide])
        grad = slope[here_wide]
        grad_two = ds2[pl.ds(pl.multiple_of(o + COLS, COLS), TILE)]
        result = grad_two + normalize_back(grad * tab(N3G), xhat, r)
        slope[here_wide] = result
        add(N3G, eights(grad * xhat))
        add(N3S, eights(grad))
        add(SL, eights(grad_two * lo_[here_wide]))
        add(C2B, eights(grad_two))
        add(PB, eights(result))
        dmx = dot_nt(side(tab(SA) * result), wph[...])
        act[here_wide] = dmx
        h, l = halves(result)
        dwp_ref[...] += dot_nn(side(mixed[pl.ds(o, TILE)].T), jnp.concatenate([h, h, l], axis=0))
        v = v_ref[pl.ds(o, TILE)]
        by_slot = [halves(jnp.where(span_mask(o, TILE, lo, hi), v, 0.0)) for lo, hi in spans]
        high = jnp.concatenate([h for h, l in by_slot], axis=1)
        low = jnp.concatenate([l for h, l in by_slot], axis=1)
        cross[...] += dot_nn(side(dmx.T), jnp.concatenate([high, high, low], axis=0))

        @pl.when(step == 1)
        def _():
            reduce.down(2)

        return carry

    lax.fori_loop(0, tokens // TILE, back, 0)
    for src, dst in ((slope, ds1_hbm), (act, dmx_hbm)):
        stores.append(pltpu.make_async_copy(src.at[own], dst, store_sem.at[len(stores)]))
        stores[-1].start()
    for s in range(3):
        gprob_ref[s] = fold(cross[:, s * D : s * D + D])

    def total(r):
        return jnp.sum(acc[8 * r : 8 * r + 8], axis=0, keepdims=True)

    for r in (N3G, N3S, N2G, N2S, SL, SM, C1B, BG, BS, F2B, 40, 41, 42, 43):
        gtab_ref[r : r + 1] = total(r)
    for t in range(9):
        gtab_ref[K1R + t : K1R + t + 1] = total(K1R + t)
        gtab_ref[K2R + t : K2R + t + 1] = total(K2R + t) * tab(SL)
    gtab_ref[C2B : C2B + 1] = total(C2B) * tab(SL)
    gtab_ref[PB : PB + 1] = total(PB) * tab(SA)
    raw = dwp_ref[...]
    gtab_ref[SA : SA + 1] = jnp.sum(raw * wp_ref[...], axis=0, keepdims=True) + total(PB) * tab(PB)
    dwp_ref[...] = raw * tab(SA)
    for i in range(mlp // D):
        gtab_ref[F1B + i : F1B + i + 1] = jnp.sum(b1g_ref[:, i * D : i * D + D], axis=0, keepdims=True)
    reduce.down(3)
    for p in range(reduce.count):
        lanes = reduce.lanes(p)
        shard_ref[:, lanes] = reduce.buf[reduce.held(p, 4), lanes]
    for copy in stores:
        copy.wait()


def middle(tall, temp, x, dy, v, sums, wp, w1, w2, tab):
    tokens = x.shape[0]
    wide = tokens + HALO
    mlp = w1.shape[1]
    smem = pl.BlockSpec(memory_space=pltpu.SMEM)
    vmem = pl.BlockSpec(memory_space=pltpu.VMEM)
    anywhere = pl.BlockSpec(memory_space=pl.ANY)

    def f(*shape):
        return jax.ShapeDtypeStruct(shape, F32)

    def s(*shape):
        return pltpu.VMEM(shape, F32)

    def b(*shape):
        return pltpu.VMEM(shape, BF)

    padded = s(wide + 2 * COLS, D)
    return pl.pallas_call(
        middle_kernel,
        out_shape=[
            f(tokens, D),
            f(tokens, D),
            f(tokens, D),
            f(D, D),
            f(SHARD, mlp),
            f(TABLE, D),
            f(3, HD, D),
            f(3, HD, D),
            f(3, HD, D),
            f(*sums.shape[1:]),
        ],
        in_specs=[smem, smem] + [anywhere] * 3 + [vmem, vmem, anywhere, vmem, vmem],
        out_specs=[anywhere] * 3 + [vmem] * 7,
        scratch_shapes=[
            b(3 * D, D),
            b(D, 3 * D),
            b(3 * D, mlp),
            b(mlp, 3 * D),
            b(D, 9 * D),
            s(wide, D),
            s(wide, D),
            padded,
            s(wide, D),
            s(wide, D),
            padded,
            s(wide, D),
            padded,
            padded,
            s(wide // 3, D),
            b(TILE, 3 * D),
            b(TILE, 3 * D),
            s(8, mlp),
            s(8, mlp),
            s(8 * TABLE, D),
            s(D, 3 * D),
            s(wide, D),
            s(wide, D),
            s(wide, D),
            s(3, wide, 128),
            b(D, 3 * TILE),
            b(D, 3 * TILE),
            s(*sums.shape[1:]),
            s(2, D, mlp),
            DMA((4,)),
            DMA((3,)),
            DMA((2, 4)),
        ]
        + Reduce.scratch(mlp, (lax.axis_size("canvas") - 1).bit_length()),
        compiler_params=pltpu.CompilerParams(
            collective_id=0, has_side_effects=True, vmem_limit_bytes=60 << 20
        ),
    )(tall, temp, x, dy, v, sums, wp, w1, w2, tab)


def finish_kernel(
    tall_ref,
    temp_ref,
    x_ref,
    q_ref,
    k_ref,
    ds1_ref,
    dmx_ref,
    sums_ref,
    peer_ref,
    probs_ref,
    unit_ref,
    gprob_ref,
    w_ref,
    tab_ref,
    gtab_ref,
    dwp_ref,
    shard_ref,
    dx_ref,
    dw_ref,
    otab_ref,
    sum_hbm,
    wh,
    wl,
    pv,
    cv,
    ch,
    side_rows,
    acc,
    gpeer_ref,
    whole,
    gsend,
    grecv,
    *work,
):
    step = pl.program_id(0)
    last = pl.num_programs(0) - 1
    links = Links()
    core = links.core
    gather = Gather(links, whole, sum_hbm, work)
    rows_all = 2 * pl.num_programs(0) * TILE // COLS
    spans = slots(tall_ref, core, core * (rows_all // 2), rows_all)
    start = step * TILE

    def tab(r):
        return tab_ref[r : r + 1]

    @pl.when(step == 0)
    def _():
        links.greet()
        swap = remote(gprob_ref.at[2], gpeer_ref, gsend, grecv, links.twin)
        swap.start()
        for p in range(gather.count):
            lanes = gather.lanes(p)
            whole[gather.held(p, 4), lanes] = shard_ref[:, lanes]
        gather.begin()

        def part(o):
            h, l = halves(w_ref[pl.ds(o, 64)])
            wh[pl.ds(o, 64)] = h
            wl[pl.ds(o, 64)] = l

        sweep(D, 64, part)
        dw_ref[...] = jnp.zeros_like(dw_ref)
        dw_ref[1, :, D : 2 * D] = dwp_ref[...]
        acc[...] = jnp.zeros_like(acc)
        ones = group_ones()
        temp = head_row(temp_ref)
        heat = jnp.zeros((1, D), F32)
        for s in range(3):
            sums = sums_ref[s]
            grad = gprob_ref[s]
            if s == 2:
                swap.wait()
                sums = peer_ref[...]
                grad = grad + gpeer_ref[...]
            inv_q = lax.rsqrt(sums[HD : HD + 1] + EPS)
            inv_k = lax.rsqrt(sums[HD + 1 : HD + 2] + EPS)
            probs = probs_ref[s]
            unit = unit_ref[s]
            scores = probs * (grad - group_sum(probs * grad, ones))
            part_heat = jnp.sum(scores * unit, axis=0, keepdims=True)
            heat = heat + (part_heat if s < 2 else jnp.where(core == 0, part_heat, 0.0))
            pull = temp * scores
            both = pull * unit
            side_rows[8 * s : 8 * s + 1] = fold_to_row(group_sum(both, ones)) * inv_q * inv_q
            side_rows[8 * s + 1 : 8 * s + 2] = jnp.sum(both, axis=0, keepdims=True) * inv_k * inv_k
            across = slice(3 * s * D, 3 * s * D + 3 * D)
            h, l = halves(unfold(pull * row_to_fold(inv_q, ones) * inv_k))
            cv[across] = jnp.concatenate([h, h, l], axis=0)
            ch[:, across] = jnp.concatenate([h, h, l], axis=1)
            h, l = halves(unfold(probs))
            pv[across] = jnp.concatenate([h, h, l], axis=0)
        otab_ref[...] = gtab_ref[...]
        otab_ref[44:45] = heat

    masks = [span_mask(start, TILE, lo, hi) for lo, hi in spans]

    def by_slot(v):
        return jnp.concatenate([side(jnp.where(mask, v, 0.0)) for mask in masks], axis=1)

    def rows_of(r):
        return sum(jnp.where(mask, side_rows[8 * s + r : 8 * s + r + 1], 0.0) for s, mask in enumerate(masks))

    q, k = q_ref[...], k_ref[...]
    dq = dot_nt(by_slot(k), ch[...]) - q * rows_of(0)
    dk = dot_nn(by_slot(q), cv[...]) - k * rows_of(1)
    dv = dot_nn(by_slot(dmx_ref[...]), pv[...])
    dqkv = jnp.concatenate([dq, dk, dv], axis=1)

    @pl.when(step == 1)
    def _():
        gather.up(2)

    @pl.when(step == 2)
    def _():
        gather.up(1)

    h, l = halves(dqkv)
    dn = dot_nt(h, wh[...]) + (dot_nt(l, wh[...]) + dot_nt(h, wl[...]))
    xhat, r = normalize(x_ref[...])
    nt = side((xhat * tab(N1G) + tab(N1S)).T)
    grads = dot_nn(nt, jnp.concatenate([h, h, l], axis=0))
    dw_ref[0] += grads[:, 0 : 2 * D]
    dw_ref[1, :, 0:D] += grads[:, 2 * D : 3 * D]
    dx_ref[...] = ds1_ref[...] + normalize_back(dn * tab(N1G), xhat, r)
    acc[0:8] += eights(dn * xhat)
    acc[8:16] += eights(dn)
    for i, v in enumerate((dq, dk, dv)):
        acc[16 + 8 * i : 24 + 8 * i] += eights(v)

    @pl.when(step == 0)
    def _():
        gather.up(3)

    @pl.when(step == last)
    def _():
        for i, r in enumerate((N1G, N1S, QB, KB, VB)):
            otab_ref[r : r + 1] = jnp.sum(acc[8 * i : 8 * i + 8], axis=0, keepdims=True)
        gather.up(0)
        gather.end()


def finish(tall, temp, x, q, k, ds1, dmx, sums, peer, probs, unit, gprob, w, tab, gtab, dwp, shard):
    tokens = x.shape[0]
    smem = pl.BlockSpec(memory_space=pltpu.SMEM)
    anywhere = pl.BlockSpec(memory_space=pl.ANY)
    row = pl.BlockSpec((TILE, D), lambda i: (i, 0))

    def whole(v):
        return pl.BlockSpec(v.shape, lambda i: (0,) * v.ndim)

    fixed = (sums, peer, probs, unit, gprob, w, tab, gtab, dwp, shard)
    return pl.pallas_call(
        finish_kernel,
        grid=(tokens // TILE,),
        out_shape=[
            jax.ShapeDtypeStruct((tokens, D), F32),
            jax.ShapeDtypeStruct((2, D, 2 * D), F32),
            jax.ShapeDtypeStruct((TABLE, D), F32),
            jax.ShapeDtypeStruct((2, D, shard.shape[1]), F32),
        ],
        in_specs=[smem, smem] + [row] * 5 + [whole(v) for v in fixed],
        out_specs=[
            row,
            pl.BlockSpec((2, D, 2 * D), lambda i: (0, 0, 0)),
            pl.BlockSpec((TABLE, D), lambda i: (0, 0)),
            anywhere,
        ],
        scratch_shapes=[
            pltpu.VMEM((D, 3 * D), BF),
            pltpu.VMEM((D, 3 * D), BF),
            pltpu.VMEM((9 * D, D), BF),
            pltpu.VMEM((9 * D, D), BF),
            pltpu.VMEM((D, 9 * D), BF),
            pltpu.VMEM((24, D), F32),
            pltpu.VMEM((40, D), F32),
            pltpu.VMEM(gprob.shape[1:], F32),
            pltpu.VMEM((D, shard.shape[1]), F32),
            DMA,
            DMA,
        ]
        + Gather.scratch(shard.shape[1]),
        compiler_params=pltpu.CompilerParams(
            collective_id=1, has_side_effects=True, vmem_limit_bytes=60 << 20
        ),
    )(tall, temp, x, q, k, ds1, dmx, *fixed)


NS_A, NS_B, NS_C = 3.4445, -4.7750, 2.0315


def times(a, b):
    return dot_nn(
        jnp.concatenate([a[0], a[1], a[0]], axis=1), jnp.concatenate([b[0], b[0], b[1]], axis=0)
    )


def inverse_norm(v):
    total = jnp.sum(jnp.sum(v * v, axis=0, keepdims=True), axis=1, keepdims=True)
    return 1.0 / (jnp.sqrt(total) + 1e-07)


def wide_kernel(
    end_hbm,
    tab_hbm,
    mid_hbm,
    m1_hbm,
    m2_hbm,
    sum_hbm,
    otab_hbm,
    orth_hbm,
    xs,
    x,
    m1,
    m2,
    xc,
    tbuf,
    tland,
    load_sem,
    tsend,
    trecv,
    tout,
    buf,
    own_sem,
    *work,
):
    links = Links()
    core = links.core
    reduce = Reduce(links, end_hbm, buf, work[:5])
    gather = Gather(links, work[0], sum_hbm, work[5:])
    own = pltpu.make_async_copy(end_hbm.at[core], buf, own_sem)
    own.start()
    wide = m1.shape[1]
    blocks = wide // D
    trows = tbuf.shape[0]
    near = pl.ds(pl.multiple_of(core * trows, 8), trows)
    far = pl.ds(pl.multiple_of((1 - core) * trows, 8), trows)
    pairs = ((mid_hbm.at[core], x), (m1_hbm, m1), (m2_hbm, m2), (tab_hbm.at[near], tbuf))
    loads = [pltpu.make_async_copy(a, b, load_sem.at[i]) for i, (a, b) in enumerate(pairs)]
    for load in loads:
        load.start()
    links.greet()
    reduce.begin()
    top = links.bits

    def table(n):
        if n == top:
            return remote(tab_hbm.at[far], tland.at[n], tsend.at[n], trecv.at[n], links.twin)
        return remote(tbuf, tland.at[n], tsend.at[n], trecv.at[n], links.there[n])

    def table_land(n):
        table(n).wait()
        tbuf[...] += tland[n]

    table(top).start()
    for load in loads:
        load.wait()

    @pl.when(core == 0)
    def _():
        x[...] = MUON_KEEP * m1[...] + x[...]

    @pl.when(core == 1)
    def _():
        for b in range(blocks):
            lanes = slice(b * D, b * D + D)
            x[:, lanes] = MUON_KEEP * m2[lanes].T + x[:, lanes]

    own.wait()
    table_land(top)
    reduce.join()
    table(0).start()
    inv = inverse_norm(x[...])
    chunks = [slice(o, o + 2 * PIECE) for o in range(0, wide, 2 * PIECE)]

    def keep(lanes, v):
        h, l = halves(v)
        xc[0:D, lanes] = h
        xc[D : 2 * D, lanes] = h
        xc[2 * D : 3 * D, lanes] = l

    def kept(lanes):
        return xc[0:D, lanes].astype(F32) + xc[2 * D : 3 * D, lanes].astype(F32)

    for lanes in chunks:
        keep(lanes, x[:, lanes] * inv)

    def gram():
        h, l = xc[0:D], xc[2 * D : 3 * D]
        return dot_nt(h, h) + (dot_nt(l, h) + dot_nt(h, l))

    def two_steps(events):
        g0 = gram()
        g = halves(g0)
        events[0]()
        p0 = NS_B * g0 + NS_C * times(g, g)
        p = halves(p0)
        t = NS_A * g0 + times(p, g)
        events[1]()
        g1 = NS_A * t + times(halves(t), p)
        g = halves(g1)
        p1 = NS_B * g1 + NS_C * times(g, g)
        events[2]()
        both = side(NS_A * (p0 + p1) + times(halves(p1), p))
        for lanes in chunks:
            keep(lanes, NS_A * NS_A * kept(lanes) + dot_nn(both, xc[:, lanes]))
        events[3]()

    def down(s):
        def event():
            reduce.down(s)
            table_land(s)
            if s < 3:
                table(s + 1).start()
                return
            for b in range(4, links.bits):
                table(b).start()
                table_land(b)
            for p in range(gather.count):
                lanes = gather.lanes(p)
                gather.whole[gather.held(p, 4), lanes] = buf[gather.held(p, 4), lanes]
            gather.begin()
            for copy in touts:
                copy.start()

        return event

    touts = [
        pltpu.make_async_copy(tbuf, otab_hbm.at[near], tout.at[0]),
        remote(tbuf, otab_hbm.at[near], tout.at[1], tout.at[2], links.twin),
    ]

    def nothing():
        return None

    two_steps([nothing, down(0), nothing, down(1)])
    two_steps([nothing, down(2), nothing, down(3)])
    g0 = gram()
    g = halves(g0)
    gather.up(3)
    last = side(NS_B * g0 + NS_C * times(g, g))
    for lanes in chunks:
        x[:, lanes] = NS_A * kept(lanes) + dot_nn(last, xc[:, lanes])
    gather.up(2)

    @pl.when(core == 0)
    def _():
        for b in range(blocks):
            xs[b] = x[:, b * D : b * D + D]

    @pl.when(core == 1)
    def _():
        for b in range(blocks):
            xs[b] = x[:, b * D : b * D + D].T

    orth = [
        pltpu.make_async_copy(xs, orth_hbm.at[core], tout.at[3]),
        remote(xs, orth_hbm.at[core], tout.at[4], tout.at[5], links.twin),
    ]
    for copy in orth:
        copy.start()
    gather.up(1)
    gather.up(0)
    gather.end()
    for copy in touts + orth:
        copy.wait()


def wide_blocks(end, tab, mid, m1, m2):
    bits = (lax.axis_size("canvas") - 1).bit_length()
    anywhere = pl.BlockSpec(memory_space=pl.ANY)
    blocks = m1.shape[1] // D
    return pl.pallas_call(
        wide_kernel,
        out_shape=[
            jax.ShapeDtypeStruct(end.shape, F32),
            jax.ShapeDtypeStruct((TABLE, D), F32),
            jax.ShapeDtypeStruct((2, blocks, D, D), F32),
        ],
        in_specs=[anywhere] * 5,
        out_specs=[anywhere] * 3,
        scratch_shapes=[
            pltpu.VMEM((blocks, D, D), F32),
            pltpu.VMEM(m1.shape, F32),
            pltpu.VMEM(m1.shape, F32),
            pltpu.VMEM(m2.shape, F32),
            pltpu.VMEM((3 * D, m1.shape[1]), BF),
            pltpu.VMEM((TABLE // 2, D), F32),
            pltpu.VMEM((bits + 1, TABLE // 2, D), F32),
            DMA((4,)),
            DMA((bits + 1,)),
            DMA((bits + 1,)),
            DMA((6,)),
            pltpu.VMEM(end.shape[1:], F32),
            DMA,
        ]
        + Reduce.scratch(end.shape[2], bits)
        + Gather.scratch(end.shape[2]),
        compiler_params=pltpu.CompilerParams(
            collective_id=2, has_side_effects=True, vmem_limit_bytes=60 << 20
        ),
    )(end, tab, mid, m1, m2)


def muon(w, orth, large):
    return w * (1.0 - MUON_RATE * DECAY) - MUON_RATE * 0.2 * math.sqrt(large) * orth


def square_kernel(
    end_hbm,
    mid_hbm,
    wide_hbm,
    mq_hbm,
    mp_hbm,
    m1_hbm,
    m2_hbm,
    w1_hbm,
    w2_hbm,
    gq_out,
    gp_out,
    g1_out,
    g2_out,
    nq_out,
    np_out,
    n1_out,
    n2_out,
    w1_out,
    w2_out,
    c1_out,
    c2_out,
    orth_hbm,
    end,
    mid,
    nat,
    mq,
    mp,
    m1,
    m2,
    w1,
    w2,
    c1,
    c2,
    wide,
    xh,
    xl,
    xs,
    in_sem,
    out_sem,
):
    core = lax.axis_index("rows")
    mlp = m1.shape[1]
    blocks = mlp // D
    pairs = (
        (end_hbm, end),
        (mq_hbm, mq),
        (mp_hbm, mp),
        (mid_hbm, mid),
        (m1_hbm, m1),
        (m2_hbm, m2),
        (w1_hbm, w1),
        (w2_hbm, w2),
        (wide_hbm, wide),
    )
    loads = [pltpu.make_async_copy(a, b, in_sem.at[i]) for i, (a, b) in enumerate(pairs)]
    for load in loads:
        load.start()
    for load in loads[0:3]:
        load.wait()
    outs = []

    def store(src, dst):
        outs.append(pltpu.make_async_copy(src, dst, out_sem.at[len(outs)]))
        outs[-1].start()

    store(end.at[0], gq_out.at[:, 0 : 2 * D])
    store(end.at[1, :, 0:D], gq_out.at[:, 2 * D : 3 * D])
    store(end.at[1, :, D : 2 * D], gp_out)

    def small(o):
        rows = pl.ds(o, 128)
        mq[rows, 0 : 2 * D] = MUON_KEEP * mq[rows, 0 : 2 * D] + end[0, rows]
        mq[rows, 2 * D : 3 * D] = MUON_KEEP * mq[rows, 2 * D : 3 * D] + end[1, rows, 0:D]
        mp[rows] = MUON_KEEP * mp[rows] + end[1, rows, D : 2 * D]

    sweep(D, 128, small)
    store(mq, nq_out)
    store(mp, np_out)

    def keep(b, v):
        xh[b], xl[b] = halves(v)

    @pl.when(core == 0)
    def _():
        xs[0] = mq[:, 0:D]
        xs[1] = mq[:, D : 2 * D]

    @pl.when(core == 1)
    def _():
        xs[0] = mq[:, 2 * D : 3 * D]
        xs[1] = mp[...]

    for b in range(2):
        keep(b, xs[b] * inverse_norm(xs[b]))

    def step(i, carry):
        x = [(xh[b], xl[b]) for b in range(2)]
        g = [
            dot_nt(jnp.concatenate([h, l, h], axis=1), jnp.concatenate([h, h, l], axis=1))
            for h, l in x
        ]
        pairs = [halves(v) for v in g]
        p = [NS_B * v + NS_C * times(w, w) for v, w in zip(g, pairs)]
        pairs = [halves(v) for v in p]
        for b in range(2):
            h, l = x[b]
            keep(b, NS_A * (h.astype(F32) + l.astype(F32)) + times(pairs[b], x[b]))
        return carry

    lax.fori_loop(0, 2, step, 0)
    for load in loads[3:6]:
        load.wait()
    store(mid.at[0], g1_out)
    for b in range(blocks):
        nat[b * D : b * D + D] = mid[1, :, b * D : b * D + D].T
    store(nat, g2_out)

    def large(o):
        rows = pl.ds(o, 64)
        m1[rows] = MUON_KEEP * m1[rows] + mid[0, rows]

    sweep(D, 64, large)
    store(m1, n1_out)

    def larger(o):
        rows = pl.ds(o, 256)
        m2[rows] = MUON_KEEP * m2[rows] + nat[rows]

    sweep(mlp, 256, larger)
    store(m2, n2_out)
    lax.fori_loop(2, 4, step, 0)
    for load in loads[6:]:
        load.wait()
    for b in range(blocks):
        at = slice(b * D, b * D + D)
        new = muon(w1[:, at], wide[0, b], mlp)
        w1[:, at] = new
        c1[:, at] = new.astype(BF)
        new = muon(w2[at], wide[1, b], mlp)
        w2[at] = new
        c2[at] = new.astype(BF)
    store(w1, w1_out)
    store(w2, w2_out)
    store(c1, c1_out)
    store(c2, c2_out)
    lax.fori_loop(4, 5, step, 0)
    for b in range(2):
        xs[b] = xh[b].astype(F32) + xl[b].astype(F32)
    store(xs, orth_hbm)
    for copy in outs:
        copy.wait()


def square_blocks(end, mid, wide, mq, mp, m1, m2, w1, w2):
    anywhere = pl.BlockSpec(memory_space=pl.ANY)

    def like(v, kind=F32):
        return jax.ShapeDtypeStruct(v.shape, kind)

    def room(v, kind=F32):
        return pltpu.VMEM(v.shape, kind)

    return pl.pallas_call(
        square_kernel,
        out_shape=[like(v) for v in (mq, mp, m1, m2, mq, mp, m1, m2, w1, w2)]
        + [like(w1, BF), like(w2, BF), jax.ShapeDtypeStruct((2, D, D), F32)],
        in_specs=[anywhere] * 9,
        out_specs=[anywhere] * 13,
        scratch_shapes=[room(v) for v in (end, mid, m2, mq, mp, m1, m2, w1, w2)]
        + [room(w1, BF), room(w2, BF), room(wide)]
        + [
            pltpu.VMEM((2, D, D), BF),
            pltpu.VMEM((2, D, D), BF),
            pltpu.VMEM((2, D, D), F32),
            DMA((9,)),
            DMA((14,)),
        ],
        compiler_params=pltpu.CompilerParams(vmem_limit_bytes=60 << 20),
    )(end, mid, wide, mq, mp, m1, m2, w1, w2)


def trade_kernel(own_ref, peer_ref, send_sem, recv_sem):
    core = lax.axis_index("rows")
    twin = {"rows": 1 - core}
    barrier = pltpu.get_barrier_semaphore()
    pl.semaphore_signal(barrier, inc=1, device_id=twin, device_id_type=MESH_ID)
    pl.semaphore_wait(barrier, 1)
    copy = remote(own_ref, peer_ref, send_sem, recv_sem, twin)
    copy.start()
    copy.wait()


def trade(own):
    anywhere = pl.BlockSpec(memory_space=pl.ANY)
    return pl.pallas_call(
        trade_kernel,
        out_shape=jax.ShapeDtypeStruct(own.shape, F32),
        in_specs=[anywhere],
        out_specs=anywhere,
        scratch_shapes=[DMA, DMA],
        compiler_params=pltpu.CompilerParams(collective_id=3, has_side_effects=True),
    )(own)


def moment_step(current, one, two, gradient):
    first = BETA1 * one + (1.0 - BETA1) * gradient
    second = BETA2 * two + (1.0 - BETA2) * gradient * gradient
    fix_one = 1.0 - BETA1**STEP
    fix_two = 1.0 - BETA2**STEP
    updated = current - ADAM_RATE * (first / fix_one) / (jnp.sqrt(second / fix_two) + ADAM_FLOOR)
    return first, second, updated


def update_kernel(
    own_ref,
    peer_ref,
    wq_ref,
    wp_ref,
    tab_ref,
    one_ref,
    two_ref,
    gtab_ref,
    nq_ref,
    np_ref,
    cq_ref,
    cp_ref,
    first_ref,
    second_ref,
    small_ref,
):
    lower = lax.axis_index("rows") == 0
    own, peer = own_ref[...], peer_ref[...]
    low, high = jnp.where(lower, own, peer), jnp.where(lower, peer, own)
    for i, orth in enumerate((low[0], low[1], high[0])):
        lanes = slice(i * D, i * D + D)
        new = muon(wq_ref[:, lanes], orth, D)
        nq_ref[:, lanes] = new
        cq_ref[:, lanes] = new.astype(BF)
    new = muon(wp_ref[...], high[1], D)
    np_ref[...] = new
    cp_ref[...] = new.astype(BF)
    first, second, small = moment_step(tab_ref[...], one_ref[...], two_ref[...], gtab_ref[0:SMALL])
    first_ref[...] = first
    second_ref[...] = second
    small_ref[...] = small


def update(own, peer, wq, wp, tab, one, two, gtab):
    steps = 3
    piece = D // steps

    def rows(v):
        return pl.BlockSpec((piece, v.shape[1]), lambda i: (i, 0))

    def whole(v):
        return pl.BlockSpec(v.shape, lambda i: (0, 0))

    square = pl.BlockSpec((2, piece, D), lambda i: (0, i, 0))
    weights = (wq, wp)
    return pl.pallas_call(
        update_kernel,
        grid=(steps,),
        out_shape=[jax.ShapeDtypeStruct(w.shape, F32) for w in weights]
        + [jax.ShapeDtypeStruct(w.shape, BF) for w in weights]
        + [jax.ShapeDtypeStruct(tab.shape, F32)] * 3,
        in_specs=[square, square]
        + [rows(w) for w in weights]
        + [whole(v) for v in (tab, one, two, gtab)],
        out_specs=[rows(w) for w in weights] * 2 + [whole(tab)] * 3,
        compiler_params=pltpu.CompilerParams(vmem_limit_bytes=60 << 20),
    )(own, peer, *weights, tab, one, two, gtab)


def on_device(
    x4, dy4, tall, wqkv, wp, w1, w2, mqkv, mp, m1, m2, tab, tab_one, tab_two, temp, temp_one, temp_two
):
    shape = x4.shape
    tokens = shape[1] * shape[2]
    x = x4.reshape(tokens, D)
    dy = dy4.reshape(tokens, D)
    q, k, v, sums = project(tall, x, wqkv, tab)
    out, ds1, dmx, dwp, shard, gtab, probs, unit, gprob, joint = middle(
        tall, temp, x, dy, v, sums, wp, w1, w2, tab
    )
    dx, end, gtab, mid = finish(
        tall, temp, x, q, k, ds1, dmx, sums, joint, probs, unit, gprob, wqkv, tab, gtab, dwp, shard
    )
    end, gtab, wide = wide_blocks(end, gtab, mid, m1, m2)
    *grads, new_1, new_2, copy_1, copy_2, square = square_blocks(
        end, mid, wide, mqkv, mp, m1, m2, w1, w2
    )
    new_q, new_p, copy_q, copy_p, *small = update(
        square, trade(square), wqkv, wp, tab, tab_one, tab_two, gtab
    )
    results = (new_q, new_p, new_1, new_2, copy_q, copy_p, copy_1, copy_2, *small)
    heat = jnp.sum(gtab[44].reshape(HEADS, HD), axis=1)
    warm = moment_step(temp, temp_one, temp_two, heat)
    count = tokens * D * lax.axis_size("rows") * lax.axis_size("canvas")
    rms = jnp.sqrt(jnp.sum(gtab[40:44], axis=1) / count)
    return (out.reshape(shape), dx.reshape(shape), *grads, *results, *warm, rms)


def solution(mesh):
    split = P("canvas", "rows", None, None)
    return jax.shard_map(
        on_device,
        mesh=mesh,
        in_specs=(split, split, P("canvas", None)) + (P(),) * 14,
        out_specs=(split, split) + (P(),) * 23,
        check_vma=False,
    )
```

```python
import math

import jax
import jax.numpy as jnp
from jax import lax
from jax.experimental import pallas as pl
from jax.experimental.pallas import tpu as pltpu
from jax.sharding import PartitionSpec as P

BF = jnp.bfloat16
F32 = jnp.float32
MESH_ID = pl.DeviceIdType.MESH

EPS = 1e-06
ROOT_HALF = 1.0 / math.sqrt(2.0)
ROOT_TWOPI = 1.0 / math.sqrt(2.0 * math.pi)
STEP = 10
MUON_RATE = 0.2
MUON_KEEP = 0.95
DECAY = 0.01
ADAM_RATE = 0.2
BETA1 = 0.9
BETA2 = 0.95
ADAM_FLOOR = 1e-08

HEADS = 8
HD = 48
D = HEADS * HD
COLS = 32
HALO = 4 * COLS
TILE = 256

N1G, N1S, N3G, N3S, N2G, N2S, SA, SL, SM, QB, KB, VB, PB, C1B, BG, BS, C2B, F2B = range(18)
F1B, K1R, K2R = 18, 22, 31
SMALL = 40
TABLE = 48


def halves(v):
    hi = v.astype(BF)
    return hi, (v - hi.astype(F32)).astype(BF)


def side(v):
    h, l = halves(v)
    return jnp.concatenate([h, l, h], axis=1)


def dot_nn(a, b):
    return lax.dot_general(a, b, (((1,), (0,)), ((), ())), preferred_element_type=F32)


def dot_nt(a, b):
    return lax.dot_general(a, b, (((1,), (1,)), ((), ())), preferred_element_type=F32)


def normalize(v):
    mean = jnp.mean(v, axis=1, keepdims=True)
    c = v - mean
    r = lax.rsqrt(jnp.mean(c * c, axis=1, keepdims=True) + EPS)
    return c * r, r


def normalize_back(e, xhat, r):
    return r * (
        e - jnp.mean(e, axis=1, keepdims=True) - xhat * jnp.mean(e * xhat, axis=1, keepdims=True)
    )


def gelu_parts(v):
    phi = 0.5 * (1.0 + lax.erf(v * ROOT_HALF))
    return v * phi, phi + v * jnp.exp(-0.5 * v * v) * ROOT_TWOPI


def eights(v):
    total = v[0:8]
    for i in range(8, v.shape[0], 8):
        total = total + v[i : i + 8]
    return total


def sweep(count, size, body):
    def one(i, carry):
        body(pl.multiple_of(i * size, size))
        return carry

    lax.fori_loop(0, count // size, one, 0)


def image_ends(tall_ref):
    e0 = tall_ref[0, 0]
    e1 = e0 + tall_ref[0, 1]
    return e0, e1, e1 + tall_ref[0, 2]


def slots(tall_ref, core, first_row, rows_all):
    e0, e1, e2 = image_ends(tall_ref)
    low = (jnp.where(core == 0, 0, e2), jnp.where(core == 0, e0, 0), e1)
    high = (jnp.where(core == 0, e0, rows_all), jnp.where(core == 0, e1, 0), e2)
    return [((a - first_row) * COLS, (b - first_row) * COLS) for a, b in zip(low, high)]


def span_mask(start, rows, lo, hi):
    token = start + lax.broadcasted_iota(jnp.int32, (rows, D), 0)
    return (token >= lo) & (token < hi)


def lane_head():
    return lax.broadcasted_iota(jnp.int32, (HD, D), 1) // HD


def lane_slot():
    return lax.broadcasted_iota(jnp.int32, (HD, D), 1) % HD


def fold(full):
    head = lane_head()
    total = jnp.where(head == 0, full[0:HD], 0.0)
    for h in range(1, HEADS):
        total = total + jnp.where(head == h, full[h * HD : h * HD + HD], 0.0)
    return total


def unfold(small):
    head = lane_head()
    return jnp.concatenate([jnp.where(head == h, small, 0.0) for h in range(HEADS)], axis=0)


def group_ones():
    a = lax.broadcasted_iota(jnp.int32, (D, D), 0) // HD
    b = lax.broadcasted_iota(jnp.int32, (D, D), 1) // HD
    return jnp.where(a == b, 1.0, 0.0).astype(BF)


def group_sum(v, ones):
    h = v.astype(BF)
    rest = v - h.astype(F32)
    m = rest.astype(BF)
    l = (rest - m.astype(F32)).astype(BF)
    return dot_nn(h, ones) + (dot_nn(m, ones) + dot_nn(l, ones))


def row_to_fold(row, ones):
    slot = lax.broadcasted_iota(jnp.int32, (HD, D), 0)
    return group_sum(jnp.where(lane_slot() == slot, jnp.broadcast_to(row, (HD, D)), 0.0), ones)


def fold_to_row(small):
    slot = lax.broadcasted_iota(jnp.int32, (HD, D), 0)
    return jnp.sum(jnp.where(lane_slot() == slot, small, 0.0), axis=0, keepdims=True)


def head_row(temp_ref):
    head = lax.broadcasted_iota(jnp.int32, (1, D), 1) // HD
    row = jnp.where(head == 0, temp_ref[0], 0.0)
    for h in range(1, HEADS):
        row = row + jnp.where(head == h, temp_ref[h], 0.0)
    return row


def project_kernel(tall_ref, x_ref, w_ref, tab_ref, q_ref, k_ref, v_ref, sums_ref, wcat, cross):
    step = pl.program_id(0)
    core = lax.axis_index("rows")
    rows_all = 2 * pl.num_programs(0) * TILE // COLS
    spans = slots(tall_ref, core, core * (rows_all // 2), rows_all)
    start = step * TILE

    @pl.when(step == 0)
    def _():
        def part(o):
            h, l = halves(w_ref[pl.ds(o, 64)])
            wcat[pl.ds(o, 64)] = h
            wcat[pl.ds(D + o, 64)] = h
            wcat[pl.ds(2 * D + o, 64)] = l

        sweep(D, 64, part)
        cross[...] = jnp.zeros_like(cross)
        sums_ref[...] = jnp.zeros_like(sums_ref)

    xhat, _ = normalize(x_ref[...])
    lhs = side(xhat * tab_ref[N1G : N1G + 1] + tab_ref[N1S : N1S + 1])
    q = dot_nn(lhs, wcat[:, 0:D]) + tab_ref[QB : QB + 1]
    q_ref[...] = q
    k = dot_nn(lhs, wcat[:, D : 2 * D]) + tab_ref[KB : KB + 1]
    k_ref[...] = k
    v_ref[...] = dot_nn(lhs, wcat[:, 2 * D : 3 * D]) + tab_ref[VB : VB + 1]
    qt = side(q.T)
    for s, (lo, hi) in enumerate(spans):

        @pl.when((lo < start + TILE) & (hi > start))
        def _():
            mask = span_mask(start, TILE, lo, hi)
            kh, kl = halves(jnp.where(mask, k_ref[...], 0.0))
            cross[s] += dot_nn(qt, jnp.concatenate([kh, kh, kl], axis=0))
            qm = jnp.where(mask, q_ref[...], 0.0)
            km = jnp.where(mask, k_ref[...], 0.0)
            sums_ref[s, HD : HD + 1] += jnp.sum(qm * qm, axis=0, keepdims=True)
            sums_ref[s, HD + 1 : HD + 2] += jnp.sum(km * km, axis=0, keepdims=True)

    @pl.when(step == pl.num_programs(0) - 1)
    def _():
        for s in range(3):
            sums_ref[s, 0:HD] = fold(cross[s])


def project(tall, x, w, tab):
    tokens = x.shape[0]
    row = pl.BlockSpec((TILE, D), lambda i: (i, 0))
    return pl.pallas_call(
        project_kernel,
        grid=(tokens // TILE,),
        out_shape=[jax.ShapeDtypeStruct((tokens, D), F32)] * 3
        + [jax.ShapeDtypeStruct((3, HD + 8, D), F32)],
        in_specs=[
            pl.BlockSpec(memory_space=pltpu.SMEM),
            row,
            pl.BlockSpec((D, 3 * D), lambda i: (0, 0)),
            pl.BlockSpec((SMALL, D), lambda i: (0, 0)),
        ],
        out_specs=[row, row, row, pl.BlockSpec((3, HD + 8, D), lambda i: (0, 0, 0))],
        scratch_shapes=[pltpu.VMEM((3 * D, 3 * D), BF), pltpu.VMEM((3, D, D), F32)],
        compiler_params=pltpu.CompilerParams(vmem_limit_bytes=60 << 20),
    )(tall, x, w, tab)


ORDERS = ((0, 1, 2, 3), (1, 2, 0, 3), (2, 0, 1, 3))
PIECE = 256
SHARD = D // 16
DMA = pltpu.SemaphoreType.DMA


class Links:
    def __init__(self):
        self.core = lax.axis_index("rows")
        chip = lax.axis_index("canvas")
        self.bits = (lax.axis_size("canvas") - 1).bit_length()
        self.mine = [lax.rem(lax.div(chip, 1 << b), 2) for b in range(self.bits)]
        self.there = [{"canvas": chip + (1 - 2 * m) * (1 << b)} for b, m in enumerate(self.mine)]
        self.twin = {"rows": 1 - self.core}

    def call(self):
        barrier = pltpu.get_barrier_semaphore()
        for other in [self.twin] + self.there:
            pl.semaphore_signal(barrier, inc=1, device_id=other, device_id_type=MESH_ID)

    def answer(self):
        pl.semaphore_wait(pltpu.get_barrier_semaphore(), self.bits + 1)

    def greet(self):
        self.call()
        self.answer()


def remote(src, dst, send, recv, other):
    return pltpu.make_async_remote_copy(
        src_ref=src,
        dst_ref=dst,
        send_sem=send,
        recv_sem=recv,
        device_id=other,
        device_id_type=MESH_ID,
    )


class Pieces:
    def __init__(self, links, lanes):
        self.links = links
        self.count = lanes // PIECE

    def lanes(self, p):
        return slice(p * PIECE, p * PIECE + PIECE)

    def bit(self, p, s):
        return ORDERS[p % 3][s]

    def start(self, p, s):
        at = 0
        for t in range(s):
            at = at + self.links.mine[self.bit(p, t)] * (D >> (t + 1))
        return at

    def held(self, p, s):
        return pl.ds(pl.multiple_of(self.start(p, s), 8), D >> s)


class Reduce(Pieces):
    def __init__(self, links, src, buf, work):
        super().__init__(links, src.shape[2])
        self.src, self.buf = src, buf
        self.first, self.land, self.pair_sem, self.send_sem, self.recv_sem = work

    @staticmethod
    def scratch(lanes, bits):
        steps = max(bits, 4)
        count = lanes // PIECE
        return [
            pltpu.VMEM((D, lanes), F32),
            pltpu.VMEM((D - SHARD + (steps - 4) * SHARD, lanes), F32),
            DMA((2, count)),
            DMA((count, steps)),
            DMA((count, steps)),
        ]

    def add(self, p, rows, src, src_rows):
        lanes = self.lanes(p)
        self.buf[rows, lanes] += src[src_rows, lanes]

    def pair(self, p):
        lanes = self.lanes(p)
        return remote(
            self.src.at[1 - self.links.core, :, lanes],
            self.first.at[:, lanes],
            self.pair_sem.at[0, p],
            self.pair_sem.at[1, p],
            self.links.twin,
        )

    def move(self, p, s):
        b = self.bit(p, s)
        half = D >> (s + 1)
        away = pl.multiple_of(self.start(p, s) + (1 - self.links.mine[b]) * half, 8)
        lanes = self.lanes(p)
        return remote(
            self.buf.at[pl.ds(away, half), lanes],
            self.land.at[pl.ds(D - (D >> s), half), lanes],
            self.send_sem.at[p, s],
            self.recv_sem.at[p, s],
            self.links.there[b],
        )

    def begin(self):
        for p in range(self.count):
            self.pair(p).start()

    def join(self):
        for p in range(self.count):
            self.pair(p).wait()
            self.add(p, pl.ds(0, D), self.first, pl.ds(0, D))
            self.move(p, 0).start()

    def down(self, s, last=3):
        for p in range(self.count):
            self.move(p, s).wait()
            self.add(p, self.held(p, s + 1), self.land, pl.ds(D - (D >> s), D >> (s + 1)))
            if s < last:
                self.move(p, s + 1).start()
        if s == 3:
            for b in range(4, self.links.bits):
                self.swap(b)

    def swap(self, b):
        at = pl.ds(D - SHARD + (b - 4) * SHARD, SHARD)
        copies = []
        for p in range(self.count):
            lanes = self.lanes(p)
            copies.append(
                remote(
                    self.buf.at[self.held(p, 4), lanes],
                    self.land.at[at, lanes],
                    self.send_sem.at[p, b],
                    self.recv_sem.at[p, b],
                    self.links.there[b],
                )
            )
            copies[-1].start()
        for p in range(self.count):
            copies[p].wait()
            self.add(p, self.held(p, 4), self.land, at)


class Gather(Pieces):
    def __init__(self, links, whole, dst, work):
        super().__init__(links, whole.shape[1])
        self.whole, self.dst = whole, dst
        self.send_sem, self.recv_sem, self.out_sem = work

    @staticmethod
    def scratch(lanes):
        count = lanes // PIECE
        return [DMA((count, 4)), DMA((count, 4)), DMA((3, count))]

    def back(self, p, s):
        view = self.whole.at[self.held(p, s + 1), self.lanes(p)]
        return remote(
            view,
            view,
            self.send_sem.at[p, s],
            self.recv_sem.at[p, s],
            self.links.there[self.bit(p, s)],
        )

    def outs(self, p):
        src = self.whole.at[:, self.lanes(p)]
        dst = self.dst.at[self.links.core, :, self.lanes(p)]
        return (
            pltpu.make_async_copy(src, dst, self.out_sem.at[0, p]),
            remote(src, dst, self.out_sem.at[1, p], self.out_sem.at[2, p], self.links.twin),
        )

    def begin(self, s=3):
        for p in range(self.count):
            self.back(p, s).start()

    def up(self, s, last=0):
        for p in range(self.count):
            self.back(p, s).wait()
            if s > last:
                self.back(p, s - 1).start()
            elif s == 0:
                for copy in self.outs(p):
                    copy.start()

    def end(self):
        for p in range(self.count):
            for copy in self.outs(p):
                copy.wait()


class Turn(Pieces):
    def __init__(self, links, held, whole, work):
        super().__init__(links, whole.shape[1])
        self.rest, self.whole = held, whole
        self.land, self.send_sem, self.recv_sem = work

    @staticmethod
    def scratch(lanes, bits):
        count = lanes // PIECE
        steps = max(bits, 4) - 3
        return [pltpu.VMEM((steps * SHARD, lanes), F32), DMA((count, steps)), DMA((count, steps))]

    def move(self, p, n):
        lanes = self.lanes(p)
        if n == 0:
            b = self.bit(p, 3)
            at = pl.multiple_of((1 - self.links.mine[b]) * SHARD, 8)
            src = self.rest.at[pl.ds(at, SHARD), lanes]
        else:
            b = 3 + n
            src = self.whole.at[self.held(p, 4), lanes]
        return remote(
            src,
            self.land.at[n * SHARD : n * SHARD + SHARD, lanes],
            self.send_sem.at[p, n],
            self.recv_sem.at[p, n],
            self.links.there[b],
        )

    def begin(self):
        for p in range(self.count):
            self.move(p, 0).start()

    def end(self):
        for p in range(self.count):
            lanes = self.lanes(p)
            at = pl.multiple_of(self.links.mine[self.bit(p, 3)] * SHARD, 8)
            self.move(p, 0).wait()
            self.whole[self.held(p, 4), lanes] = (
                self.rest[pl.ds(at, SHARD), lanes] + self.land[0:SHARD, lanes]
            )
        for n in range(1, self.links.bits - 3):
            for p in range(self.count):
                self.move(p, n).start()
            for p in range(self.count):
                lanes = self.lanes(p)
                self.move(p, n).wait()
                self.whole[self.held(p, 4), lanes] += self.land[n * SHARD : n * SHARD + SHARD, lanes]


def row_flags(tall_ref, rows_all):
    ends = image_ends(tall_ref)

    def above(row):
        first = (row == 0) | (row == ends[0]) | (row == ends[1]) | (row == ends[2])
        return jnp.where(first, 0.0, 1.0)

    def below(row):
        return jnp.where(row + 1 == rows_all, 0.0, above(row + 1))

    return above, below


def middle_kernel(
    tall_ref,
    temp_ref,
    x_hbm,
    dy_hbm,
    v_hbm,
    sums_ref,
    wp_ref,
    w1_hbm,
    w2_ref,
    tab_ref,
    out_hbm,
    ds1_hbm,
    dmx_hbm,
    dwp_ref,
    shard_ref,
    gtab_ref,
    probs_ref,
    unit_ref,
    gprob_ref,
    joint_ref,
    wpv,
    wph,
    w1c,
    w2c,
    pcat,
    mixed,
    s1,
    li,
    act,
    slope,
    mid,
    s2,
    ds2,
    gp,
    n2c,
    dzc,
    b1_ref,
    b1g_ref,
    acc,
    cross,
    x_ref,
    dy_ref,
    v_ref,
    flags,
    nt,
    dt,
    peer_ref,
    dw_ref,
    load_sem,
    store_sem,
    edge_sem,
    *work,
):
    links = Links()
    core = links.core
    wide = x_ref.shape[0]
    tokens = wide - HALO
    dw1_ref, dw2_ref = dw_ref.at[0], dw_ref.at[1]
    reduce = Reduce(links, dw_ref, dw_ref.at[core], work)
    w1_ref = work[0]
    lo_ = x_ref
    own = pl.ds(pl.multiple_of(core * HALO, HALO), tokens)
    pairs = ((w1_hbm, w1_ref), (v_hbm, v_ref.at[own]), (x_hbm, x_ref.at[own]), (dy_hbm, dy_ref.at[own]))
    loads = [pltpu.make_async_copy(a, b, load_sem.at[i]) for i, (a, b) in enumerate(pairs)]
    for load in loads:
        load.start()
    links.call()
    edge = pl.ds(pl.multiple_of((1 - core) * (tokens - HALO), HALO), HALO)
    far = pl.ds(pl.multiple_of(core * tokens, HALO), HALO)
    pairs = (
        (sums_ref.at[2], peer_ref),
        (v_hbm.at[edge], v_ref.at[far]),
        (x_hbm.at[edge], x_ref.at[far]),
        (dy_hbm.at[edge], dy_ref.at[far]),
    )
    edges = [
        remote(a, b, edge_sem.at[0, i], edge_sem.at[1, i], links.twin)
        for i, (a, b) in enumerate(pairs)
    ]
    own_rows = tokens // COLS
    rows_wide = wide // COLS
    rows_all = 2 * own_rows
    first_row = core * (own_rows - HALO // COLS)
    own_off = pl.multiple_of(core * HALO, HALO)
    mlp = w1_hbm.shape[1]
    spans = slots(tall_ref, core, first_row, rows_all)
    above, below = row_flags(tall_ref, rows_all)

    def tab(r):
        return tab_ref[r : r + 1]

    def is_own(row):
        return (row >= core * (HALO // COLS)) & (row < core * (HALO // COLS) + own_rows)

    loads[0].wait()

    def part_1(o):
        rows = pl.ds(o, 64)
        h, l = halves(w1_ref[rows])
        w1c[rows] = h
        w1c[pl.ds(D + o, 64)] = h
        w1c[pl.ds(2 * D + o, 64)] = l

    sweep(D, 64, part_1)
    links.answer()
    for copy in edges:
        copy.start()

    def part_p(o):
        rows = pl.ds(o, 192)
        h, l = halves(wp_ref[rows])
        wpv[rows] = h
        wpv[pl.ds(D + o, 192)] = h
        wpv[pl.ds(2 * D + o, 192)] = l
        wph[rows, 0:D] = h
        wph[rows, D : 2 * D] = h
        wph[rows, 2 * D : 3 * D] = l

    sweep(D, 192, part_p)

    def part_2(o):
        rows = pl.ds(o, 256)
        h, l = halves(w2_ref[rows])
        w2c[rows, 0:D] = h
        w2c[rows, D : 2 * D] = h
        w2c[rows, 2 * D : 3 * D] = l

    sweep(mlp, 256, part_2)

    edges[0].wait()
    ones = group_ones()
    temp = head_row(temp_ref)
    for s in range(3):
        sums = sums_ref[s]
        if s == 2:
            sums = sums + peer_ref[...]
            joint_ref[...] = sums
        inv_q = lax.rsqrt(sums[HD : HD + 1] + EPS)
        inv_k = lax.rsqrt(sums[HD + 1 : HD + 2] + EPS)
        unit = sums[0:HD] * row_to_fold(inv_q, ones) * inv_k
        unit_ref[s] = unit
        weight = jnp.exp(temp * unit)
        probs = weight / group_sum(weight, ones)
        probs_ref[s] = probs
        h, l = halves(unfold(probs))
        pcat[:, 3 * s * D : 3 * s * D + 3 * D] = jnp.concatenate([h, h, l], axis=1)

    acc[...] = jnp.zeros_like(acc)
    gtab_ref[...] = jnp.zeros_like(gtab_ref)

    def add(r, v):
        acc[8 * r : 8 * r + 8] += v

    for copy in loads[1:] + edges[1:]:
        copy.wait()

    def own_part(o, size):
        token = o + lax.broadcasted_iota(jnp.int32, (size, D), 0)
        return jnp.where((token >= own_off) & (token < own_off + tokens), 1.0, 0.0)

    def attend(o):
        size = wide // 3
        v = v_ref[pl.ds(o, size)]
        by_slot = [side(jnp.where(span_mask(o, size, lo, hi), v, 0.0)) for lo, hi in spans]
        mix = dot_nt(jnp.concatenate(by_slot, axis=1), pcat[...])
        mixed[pl.ds(o, size)] = mix
        z = dot_nn(side(mix), wpv[...]) + tab(PB)
        rows = pl.ds(o, size)
        branch = tab(SA) * z
        stream = x_ref[rows] + branch
        s1[rows] = stream
        xhat, _ = normalize(stream)
        li[pl.ds(o + COLS, size)] = xhat * tab(N3G) + tab(N3S)
        add(41, eights(own_part(o, size) * branch * branch))

    for o in range(0, wide, wide // 3):
        attend(o)

    pad = jnp.zeros((COLS, D), F32)
    for buf in (li, mid, gp, ds2):
        buf[0:COLS] = pad
        buf[wide + COLS : wide + 2 * COLS] = pad

    for r in range(rows_wide):
        row = first_row + r
        mine = jnp.where(is_own(r), 1.0, 0.0)
        for n, flag in enumerate((above(row), below(row), mine)):
            flags[n, r * COLS : r * COLS + COLS] = jnp.full((COLS, 128), flag, F32)

    block = 12 * COLS
    col = lax.rem(lax.broadcasted_iota(jnp.int32, (block + 2 * COLS, 128), 0), COLS)

    def convolve(src, base, flip, scale, visit, other=None, begin=0, end=3):
        def one(n, carry):
            lanes = pl.ds(pl.multiple_of(lax.rem(n, 3) * 128, 128), 128)
            m = lax.div(n, 3)
            place = lax.div((m - 1) * (m - 2), 2) + 2 * core * m * (2 - m) + (1 - core) * m * (m - 1)
            o = pl.multiple_of(place * block, block)
            rows = pl.ds(o, block)
            taps = [tab_ref[base + t : base + t + 1, lanes] for t in range(9)]
            if flip:
                taps = taps[::-1]
            if scale is not None:
                taps = [t * tab_ref[scale : scale + 1, lanes] for t in taps]
            u = src[pl.ds(o, block + 2 * COLS), lanes]
            left = jnp.where(col == 0, 0.0, pltpu.roll(u, 1, 0))
            right = jnp.where(col == COLS - 1, 0.0, pltpu.roll(u, block + 2 * COLS - 1, 0))
            up, down = flags[0, rows], flags[1, rows]

            def line(a):
                cut = slice(a * COLS, a * COLS + block)
                return left[cut] * taps[3 * a] + u[cut] * taps[3 * a + 1] + right[cut] * taps[3 * a + 2]

            visit(o, rows, lanes, line(1) + up * line(0) + down * line(2))
            if other is not None:
                near = other[pl.ds(o, block + 2 * COLS), lanes]
                mine = flags[2, rows]
                held = (
                    mine * up * near[0:block],
                    mine * near[COLS : COLS + block],
                    mine * down * near[2 * COLS : 2 * COLS + block],
                )
                inner = slice(COLS, COLS + block)
                for a in range(3):
                    for b, view in enumerate((right, u, left)):
                        t = 8 * (base + 3 * a + b)
                        acc[t : t + 8, lanes] += eights(view[inner] * held[a])
            return carry

        lax.fori_loop(3 * begin, 3 * end, one, 0)

    def first(o, rows, lanes, value):
        at = pl.ds(o + COLS, block)
        a, s = gelu_parts(value + tab_ref[C1B : C1B + 1, lanes])
        act[rows, lanes] = a
        slope[rows, lanes] = s
        mid[at, lanes] = a * tab_ref[BG : BG + 1, lanes] + tab_ref[BS : BS + 1, lanes]

    convolve(li, K1R, False, None, first)

    def second(o, rows, lanes, value):
        value = value + tab_ref[C2B : C2B + 1, lanes]
        lo_[rows, lanes] = value
        branch = tab_ref[SL : SL + 1, lanes] * value
        s2[rows, lanes] = s1[rows, lanes] + branch
        acc[8 * 42 : 8 * 42 + 8, lanes] += eights(flags[2, rows] * branch * branch)

    convolve(mid, K2R, False, None, second)

    dw1_ref[...] = jnp.zeros_like(dw1_ref)
    dw2_ref[...] = jnp.zeros_like(dw2_ref)
    b1g_ref[...] = jnp.zeros_like(b1g_ref)
    for i in range(mlp // D):
        b1_ref[0:1, i * D : i * D + D] = tab(F1B + i)

    def feed(o):
        here = pl.ds(o, TILE)
        xhat, _ = normalize(s2[here])
        n2 = xhat * tab(N2G) + tab(N2S)
        n2c[...] = side(n2)
        dz = tab(SM) * dy_ref[here]
        dzc[...] = side(dz)
        nt[...] = side(n2.T)
        dt[...] = side(dz.T)
        add(F2B, eights(dz))

        def enter(j):
            return dot_nn(n2c[...], w1c[:, j : j + PIECE]), dot_nt(dzc[...], w2c[j : j + PIECE])

        raw, dn = tab(F2B), 0.0
        ready = enter(0)
        for j in range(0, mlp, PIECE):
            lanes = slice(j, j + PIECE)
            pre, dh = ready
            if j + PIECE < mlp:
                ready = enter(j + PIECE)
            a, slope_j = gelu_parts(pre + b1_ref[0:1, lanes])
            dp = dh * slope_j
            ah, al = halves(a)
            ph, pl_ = halves(dp)
            w2h, w2l = w2c[lanes, 0:D], w2c[lanes, 2 * D : 3 * D]
            raw = raw + (dot_nn(ah, w2h) + (dot_nn(al, w2h) + dot_nn(ah, w2l)))
            w1h, w1l = w1c[0:D, lanes], w1c[2 * D : 3 * D, lanes]
            dn = dn + (dot_nt(ph, w1h) + (dot_nt(pl_, w1h) + dot_nt(ph, w1l)))
            b1g_ref[:, lanes] += eights(dp)
            dw1_ref[:, lanes] += dot_nn(nt[...], jnp.concatenate([ph, ph, pl_], axis=0))
            dw2_ref[:, lanes] += dot_nn(dt[...], jnp.concatenate([ah, ah, al], axis=0))
        dy = dy_ref[here]
        xhat, r = normalize(s2[here])
        ds2[pl.ds(pl.multiple_of(o + COLS, COLS), TILE)] = dy + normalize_back(dn * tab(N2G), xhat, r)
        branch = tab(SM) * raw
        result = s2[here] + branch
        s2[here] = result
        add(40, eights(result * result))
        add(43, eights(branch * branch))
        add(SM, eights(dy * raw))
        add(N2G, eights(dn * xhat))
        add(N2S, eights(dn))

    def feed_one(i, carry):
        feed(pl.multiple_of(own_off + i * TILE, 128))
        return carry

    lax.fori_loop(0, tokens // TILE, feed_one, 0)
    reduce.begin()
    stores = [pltpu.make_async_copy(s2.at[own], out_hbm, store_sem.at[0])]
    stores[0].start()
    edge = HALO // 2
    rest = pl.multiple_of(COLS + (1 - core) * (tokens + edge), COLS)
    ds2[pl.ds(rest, edge)] = jnp.zeros((edge, D), F32)
    rows_out = pl.multiple_of(COLS + own_off + (1 - core) * (tokens - edge), COLS)
    rows_in = pl.multiple_of(COLS + edge + core * (tokens - edge), COLS)
    turned = remote(
        ds2.at[pl.ds(rows_out, edge)],
        ds2.at[pl.ds(rows_in, edge)],
        edge_sem.at[0, 4],
        edge_sem.at[1, 4],
        links.twin,
    )
    turned.start()

    def third(o, rows, lanes, value):
        grad = value * tab_ref[BG : BG + 1, lanes] * slope[rows, lanes]
        gp[pl.ds(o + COLS, block), lanes] = grad
        held = flags[2, rows] * value
        acc[8 * BG : 8 * BG + 8, lanes] += eights(held * act[rows, lanes])
        acc[8 * BS : 8 * BS + 8, lanes] += eights(held)
        acc[8 * C1B : 8 * C1B + 8, lanes] += eights(flags[2, rows] * grad)

    convolve(ds2, K2R, True, SL, third, mid, 0, 2)
    reduce.join()
    turned.wait()
    convolve(ds2, K2R, True, SL, third, mid, 2, 3)

    def fourth(o, rows, lanes, value):
        slope[rows, lanes] = value

    convolve(gp, K1R, True, None, fourth, li)

    dwp_ref[...] = jnp.zeros_like(dwp_ref)
    cross[...] = jnp.zeros_like(cross)

    def back(step):
        o = pl.multiple_of(own_off + step * TILE, 128)

        here_wide = pl.ds(o, TILE)
        xhat, r = normalize(s1[here_wide])
        grad = slope[here_wide]
        grad_two = ds2[pl.ds(pl.multiple_of(o + COLS, COLS), TILE)]
        result = grad_two + normalize_back(grad * tab(N3G), xhat, r)
        slope[here_wide] = result
        add(N3G, eights(grad * xhat))
        add(N3S, eights(grad))
        add(SL, eights(grad_two * lo_[here_wide]))
        add(C2B, eights(grad_two))
        add(PB, eights(result))
        dmx = dot_nt(side(tab(SA) * result), wph[...])
        act[here_wide] = dmx
        h, l = halves(result)
        dwp_ref[...] += dot_nn(side(mixed[pl.ds(o, TILE)].T), jnp.concatenate([h, h, l], axis=0))
        v = v_ref[pl.ds(o, TILE)]
        by_slot = [halves(jnp.where(span_mask(o, TILE, lo, hi), v, 0.0)) for lo, hi in spans]
        high = jnp.concatenate([h for h, l in by_slot], axis=1)
        low = jnp.concatenate([l for h, l in by_slot], axis=1)
        cross[...] += dot_nn(side(dmx.T), jnp.concatenate([high, high, low], axis=0))

    count = tokens // TILE
    for step in range(count):
        back(step)
        if step == 0:
            reduce.down(0, 2)
        if step == count - 2:
            reduce.down(1, 2)
    for src, dst in ((slope, ds1_hbm), (act, dmx_hbm)):
        stores.append(pltpu.make_async_copy(src.at[own], dst, store_sem.at[len(stores)]))
        stores[-1].start()
    for s in range(3):
        gprob_ref[s] = fold(cross[:, s * D : s * D + D])

    def total(r):
        return jnp.sum(acc[8 * r : 8 * r + 8], axis=0, keepdims=True)

    for r in (N3G, N3S, N2G, N2S, SL, SM, C1B, BG, BS, F2B, 40, 41, 42, 43):
        gtab_ref[r : r + 1] = total(r)
    for t in range(9):
        gtab_ref[K1R + t : K1R + t + 1] = total(K1R + t)
        gtab_ref[K2R + t : K2R + t + 1] = total(K2R + t) * tab(SL)
    gtab_ref[C2B : C2B + 1] = total(C2B) * tab(SL)
    gtab_ref[PB : PB + 1] = total(PB) * tab(SA)
    raw = dwp_ref[...]
    gtab_ref[SA : SA + 1] = jnp.sum(raw * wp_ref[...], axis=0, keepdims=True) + total(PB) * tab(PB)
    dwp_ref[...] = raw * tab(SA)
    for i in range(mlp // D):
        gtab_ref[F1B + i : F1B + i + 1] = jnp.sum(b1g_ref[:, i * D : i * D + D], axis=0, keepdims=True)
    reduce.down(2, 2)
    for p in range(reduce.count):
        lanes = reduce.lanes(p)
        shard_ref[:, lanes] = reduce.buf[reduce.held(p, 3), lanes]
    for copy in stores:
        copy.wait()


def middle(tall, temp, x, dy, v, sums, wp, w1, w2, tab):
    tokens = x.shape[0]
    wide = tokens + HALO
    mlp = w1.shape[1]
    smem = pl.BlockSpec(memory_space=pltpu.SMEM)
    vmem = pl.BlockSpec(memory_space=pltpu.VMEM)
    anywhere = pl.BlockSpec(memory_space=pl.ANY)

    def f(*shape):
        return jax.ShapeDtypeStruct(shape, F32)

    def s(*shape):
        return pltpu.VMEM(shape, F32)

    def b(*shape):
        return pltpu.VMEM(shape, BF)

    padded = s(wide + 2 * COLS, D)
    return pl.pallas_call(
        middle_kernel,
        out_shape=[
            f(tokens, D),
            f(tokens, D),
            f(tokens, D),
            f(D, D),
            f(2 * SHARD, mlp),
            f(TABLE, D),
            f(3, HD, D),
            f(3, HD, D),
            f(3, HD, D),
            f(*sums.shape[1:]),
        ],
        in_specs=[smem, smem] + [anywhere] * 3 + [vmem, vmem, anywhere, vmem, vmem],
        out_specs=[anywhere] * 3 + [vmem] * 7,
        scratch_shapes=[
            b(3 * D, D),
            b(D, 3 * D),
            b(3 * D, mlp),
            b(mlp, 3 * D),
            b(D, 9 * D),
            s(wide, D),
            s(wide, D),
            padded,
            s(wide, D),
            s(wide, D),
            padded,
            s(wide, D),
            padded,
            padded,
            b(TILE, 3 * D),
            b(TILE, 3 * D),
            s(8, mlp),
            s(8, mlp),
            s(8 * TABLE, D),
            s(D, 3 * D),
            s(wide, D),
            s(wide, D),
            s(wide, D),
            s(3, wide, 128),
            b(D, 3 * TILE),
            b(D, 3 * TILE),
            s(*sums.shape[1:]),
            s(2, D, mlp),
            DMA((4,)),
            DMA((3,)),
            DMA((2, 5)),
        ]
        + Reduce.scratch(mlp, (lax.axis_size("canvas") - 1).bit_length()),
        compiler_params=pltpu.CompilerParams(
            collective_id=0, has_side_effects=True, vmem_limit_bytes=60 << 20
        ),
    )(tall, temp, x, dy, v, sums, wp, w1, w2, tab)


def finish_kernel(
    tall_ref,
    temp_ref,
    x_ref,
    q_ref,
    k_ref,
    ds1_ref,
    dmx_ref,
    sums_ref,
    peer_ref,
    probs_ref,
    unit_ref,
    gprob_ref,
    w_ref,
    tab_ref,
    gtab_ref,
    dwp_ref,
    shard_ref,
    dx_ref,
    dw_ref,
    otab_ref,
    half_hbm,
    wh,
    wl,
    pv,
    cv,
    ch,
    side_rows,
    acc,
    gpeer_ref,
    whole,
    gsend,
    grecv,
    half_sem,
    *work,
):
    step = pl.program_id(0)
    last = pl.num_programs(0) - 1
    links = Links()
    core = links.core
    turn = Turn(links, shard_ref, whole, work[:3])
    gather = Gather(links, whole, None, work[3:])
    rows_all = 2 * pl.num_programs(0) * TILE // COLS
    spans = slots(tall_ref, core, core * (rows_all // 2), rows_all)
    start = step * TILE

    def tab(r):
        return tab_ref[r : r + 1]

    @pl.when(step == 0)
    def _():
        links.greet()
        swap = remote(gprob_ref.at[2], gpeer_ref, gsend, grecv, links.twin)
        swap.start()
        turn.begin()

        def part(o):
            h, l = halves(w_ref[pl.ds(o, 64)])
            wh[pl.ds(o, 64)] = h
            wl[pl.ds(o, 64)] = l

        sweep(D, 64, part)
        dw_ref[...] = jnp.zeros_like(dw_ref)
        dw_ref[1, :, D : 2 * D] = dwp_ref[...]
        acc[...] = jnp.zeros_like(acc)
        ones = group_ones()
        temp = head_row(temp_ref)
        heat = jnp.zeros((1, D), F32)
        for s in range(3):
            sums = sums_ref[s]
            grad = gprob_ref[s]
            if s == 2:
                swap.wait()
                sums = peer_ref[...]
                grad = grad + gpeer_ref[...]
            inv_q = lax.rsqrt(sums[HD : HD + 1] + EPS)
            inv_k = lax.rsqrt(sums[HD + 1 : HD + 2] + EPS)
            probs = probs_ref[s]
            unit = unit_ref[s]
            scores = probs * (grad - group_sum(probs * grad, ones))
            part_heat = jnp.sum(scores * unit, axis=0, keepdims=True)
            heat = heat + (part_heat if s < 2 else jnp.where(core == 0, part_heat, 0.0))
            pull = temp * scores
            both = pull * unit
            side_rows[8 * s : 8 * s + 1] = fold_to_row(group_sum(both, ones)) * inv_q * inv_q
            side_rows[8 * s + 1 : 8 * s + 2] = jnp.sum(both, axis=0, keepdims=True) * inv_k * inv_k
            across = slice(3 * s * D, 3 * s * D + 3 * D)
            h, l = halves(unfold(pull * row_to_fold(inv_q, ones) * inv_k))
            cv[across] = jnp.concatenate([h, h, l], axis=0)
            ch[:, across] = jnp.concatenate([h, h, l], axis=1)
            h, l = halves(unfold(probs))
            pv[across] = jnp.concatenate([h, h, l], axis=0)
        otab_ref[...] = gtab_ref[...]
        otab_ref[44:45] = heat

    masks = [span_mask(start, TILE, lo, hi) for lo, hi in spans]

    def by_slot(v):
        return jnp.concatenate([side(jnp.where(mask, v, 0.0)) for mask in masks], axis=1)

    def rows_of(r):
        return sum(jnp.where(mask, side_rows[8 * s + r : 8 * s + r + 1], 0.0) for s, mask in enumerate(masks))

    q, k = q_ref[...], k_ref[...]
    dq = dot_nt(by_slot(k), ch[...]) - q * rows_of(0)
    dk = dot_nn(by_slot(q), cv[...]) - k * rows_of(1)
    dv = dot_nn(by_slot(dmx_ref[...]), pv[...])
    dqkv = jnp.concatenate([dq, dk, dv], axis=1)

    h, l = halves(dqkv)
    dn = dot_nt(h, wh[...]) + (dot_nt(l, wh[...]) + dot_nt(h, wl[...]))
    xhat, r = normalize(x_ref[...])
    nt = side((xhat * tab(N1G) + tab(N1S)).T)
    grads = dot_nn(nt, jnp.concatenate([h, h, l], axis=0))
    dw_ref[0] += grads[:, 0 : 2 * D]
    dw_ref[1, :, 0:D] += grads[:, 2 * D : 3 * D]
    dx_ref[...] = ds1_ref[...] + normalize_back(dn * tab(N1G), xhat, r)
    acc[0:8] += eights(dn * xhat)
    acc[8:16] += eights(dn)
    for i, v in enumerate((dq, dk, dv)):
        acc[16 + 8 * i : 24 + 8 * i] += eights(v)

    @pl.when(step == 0)
    def _():
        turn.end()
        gather.begin()

    @pl.when(step == 1)
    def _():
        gather.up(3, 1)

    @pl.when(step == 2)
    def _():
        gather.up(2, 1)

    @pl.when(step == last)
    def _():
        for i, r in enumerate((N1G, N1S, QB, KB, VB)):
            otab_ref[r : r + 1] = jnp.sum(acc[8 * i : 8 * i + 8], axis=0, keepdims=True)
        gather.up(1, 1)
        copies = [
            pltpu.make_async_copy(
                whole.at[gather.held(p, 1), gather.lanes(p)],
                half_hbm.at[:, gather.lanes(p)],
                half_sem.at[p],
            )
            for p in range(gather.count)
        ]
        for copy in copies:
            copy.start()
        for copy in copies:
            copy.wait()


def finish(tall, temp, x, q, k, ds1, dmx, sums, peer, probs, unit, gprob, w, tab, gtab, dwp, shard):
    tokens = x.shape[0]
    smem = pl.BlockSpec(memory_space=pltpu.SMEM)
    anywhere = pl.BlockSpec(memory_space=pl.ANY)
    row = pl.BlockSpec((TILE, D), lambda i: (i, 0))
    bits = (lax.axis_size("canvas") - 1).bit_length()

    def whole(v):
        return pl.BlockSpec(v.shape, lambda i: (0,) * v.ndim)

    fixed = (sums, peer, probs, unit, gprob, w, tab, gtab, dwp, shard)
    return pl.pallas_call(
        finish_kernel,
        grid=(tokens // TILE,),
        out_shape=[
            jax.ShapeDtypeStruct((tokens, D), F32),
            jax.ShapeDtypeStruct((2, D, 2 * D), F32),
            jax.ShapeDtypeStruct((TABLE, D), F32),
            jax.ShapeDtypeStruct((D // 2, shard.shape[1]), F32),
        ],
        in_specs=[smem, smem] + [row] * 5 + [whole(v) for v in fixed],
        out_specs=[
            row,
            pl.BlockSpec((2, D, 2 * D), lambda i: (0, 0, 0)),
            pl.BlockSpec((TABLE, D), lambda i: (0, 0)),
            anywhere,
        ],
        scratch_shapes=[
            pltpu.VMEM((D, 3 * D), BF),
            pltpu.VMEM((D, 3 * D), BF),
            pltpu.VMEM((9 * D, D), BF),
            pltpu.VMEM((9 * D, D), BF),
            pltpu.VMEM((D, 9 * D), BF),
            pltpu.VMEM((24, D), F32),
            pltpu.VMEM((40, D), F32),
            pltpu.VMEM(gprob.shape[1:], F32),
            pltpu.VMEM((D, shard.shape[1]), F32),
            DMA,
            DMA,
            DMA((shard.shape[1] // PIECE,)),
        ]
        + Turn.scratch(shard.shape[1], bits)
        + Gather.scratch(shard.shape[1]),
        compiler_params=pltpu.CompilerParams(
            collective_id=1, has_side_effects=True, vmem_limit_bytes=60 << 20
        ),
    )(tall, temp, x, q, k, ds1, dmx, *fixed)


NS_A, NS_B, NS_C = 3.4445, -4.7750, 2.0315


def times(a, b):
    return dot_nn(
        jnp.concatenate([a[0], a[1], a[0]], axis=1), jnp.concatenate([b[0], b[0], b[1]], axis=0)
    )


def inverse_norm(v):
    total = jnp.sum(jnp.sum(v * v, axis=0, keepdims=True), axis=1, keepdims=True)
    return 1.0 / (jnp.sqrt(total) + 1e-07)


def wide_kernel(
    end_hbm,
    tab_hbm,
    half_hbm,
    m1_hbm,
    m2_hbm,
    sum_hbm,
    otab_hbm,
    orth_hbm,
    mid_hbm,
    xs,
    x,
    m1,
    m2,
    xc,
    tbuf,
    tland,
    load_sem,
    tsend,
    trecv,
    tout,
    buf,
    own_sem,
    whole,
    half_sem,
    *work,
):
    links = Links()
    core = links.core
    reduce = Reduce(links, end_hbm, buf, work[:5])
    gather = Gather(links, work[0], sum_hbm, work[5:8])
    late = Gather(links, whole, mid_hbm, work[8:])
    pieces = [
        pltpu.make_async_copy(
            half_hbm.at[:, late.lanes(p)], whole.at[late.held(p, 1), late.lanes(p)], half_sem.at[p]
        )
        for p in range(late.count)
    ]
    for copy in pieces:
        copy.start()
    own = pltpu.make_async_copy(end_hbm.at[core], buf, own_sem)
    own.start()
    wide = m1.shape[1]
    blocks = wide // D
    trows = tbuf.shape[0]
    near = pl.ds(pl.multiple_of(core * trows, 8), trows)
    far = pl.ds(pl.multiple_of((1 - core) * trows, 8), trows)
    pairs = ((m1_hbm, m1), (m2_hbm, m2), (tab_hbm.at[near], tbuf))
    loads = [pltpu.make_async_copy(a, b, load_sem.at[i]) for i, (a, b) in enumerate(pairs)]
    for load in loads:
        load.start()
    links.greet()
    reduce.begin()
    top = links.bits

    def table(n):
        if n == top:
            return remote(tab_hbm.at[far], tland.at[n], tsend.at[n], trecv.at[n], links.twin)
        return remote(tbuf, tland.at[n], tsend.at[n], trecv.at[n], links.there[n])

    def table_land(n):
        table(n).wait()
        tbuf[...] += tland[n]

    def down(s):
        def event():
            reduce.down(s)
            table_land(s)
            if s < 3:
                table(s + 1).start()
                return
            for b in range(4, links.bits):
                table(b).start()
                table_land(b)
            for p in range(gather.count):
                lanes = gather.lanes(p)
                gather.whole[gather.held(p, 4), lanes] = buf[gather.held(p, 4), lanes]
            gather.begin()
            for copy in touts:
                copy.start()

        return event

    touts = [
        pltpu.make_async_copy(tbuf, otab_hbm.at[near], tout.at[0]),
        remote(tbuf, otab_hbm.at[near], tout.at[1], tout.at[2], links.twin),
    ]

    table(top).start()
    for copy in pieces:
        copy.wait()
    late.begin(0)
    for load in loads:
        load.wait()
    own.wait()
    table_land(top)
    reduce.join()
    table(0).start()

    @pl.when(core == 1)
    def _():
        for b in range(blocks):
            xs[b] = m2[b * D : b * D + D].T

    late.up(0)

    @pl.when(core == 0)
    def _():
        x[...] = MUON_KEEP * m1[...] + whole[...]

    @pl.when(core == 1)
    def _():
        for b in range(blocks):
            lanes = slice(b * D, b * D + D)
            x[:, lanes] = MUON_KEEP * xs[b] + whole[:, lanes]

    down(0)()
    inv = inverse_norm(x[...])
    chunks = [slice(o, o + 2 * PIECE) for o in range(0, wide, 2 * PIECE)]

    def keep(lanes, v):
        h, l = halves(v)
        xc[0:D, lanes] = h
        xc[D : 2 * D, lanes] = h
        xc[2 * D : 3 * D, lanes] = l

    def kept(lanes):
        return xc[0:D, lanes].astype(F32) + xc[2 * D : 3 * D, lanes].astype(F32)

    for lanes in chunks:
        keep(lanes, x[:, lanes] * inv)

    def gram():
        h, l = xc[0:D], xc[2 * D : 3 * D]
        return dot_nt(h, h) + (dot_nt(l, h) + dot_nt(h, l))

    def two_steps(events):
        g0 = gram()
        g = halves(g0)
        events[0]()
        p0 = NS_B * g0 + NS_C * times(g, g)
        p = halves(p0)
        t = NS_A * g0 + times(p, g)
        events[1]()
        g1 = NS_A * t + times(halves(t), p)
        g = halves(g1)
        p1 = NS_B * g1 + NS_C * times(g, g)
        events[2]()
        both = side(NS_A * (p0 + p1) + times(halves(p1), p))
        for lanes in chunks:
            keep(lanes, NS_A * NS_A * kept(lanes) + dot_nn(both, xc[:, lanes]))
        events[3]()

    def up(s):
        return lambda: gather.up(s)

    def nothing():
        return None

    two_steps([nothing, down(1), nothing, down(2)])
    two_steps([nothing, down(3), nothing, up(3)])
    g0 = gram()
    g = halves(g0)
    gather.up(2)
    last = side(NS_B * g0 + NS_C * times(g, g))
    for lanes in chunks:
        x[:, lanes] = NS_A * kept(lanes) + dot_nn(last, xc[:, lanes])
    gather.up(1)

    @pl.when(core == 0)
    def _():
        for b in range(blocks):
            xs[b] = x[:, b * D : b * D + D]

    @pl.when(core == 1)
    def _():
        for b in range(blocks):
            xs[b] = x[:, b * D : b * D + D].T

    orth = [
        pltpu.make_async_copy(xs, orth_hbm.at[core], tout.at[3]),
        remote(xs, orth_hbm.at[core], tout.at[4], tout.at[5], links.twin),
    ]
    for copy in orth:
        copy.start()
    gather.up(0)
    gather.end()
    late.end()
    for copy in touts + orth:
        copy.wait()


def wide_blocks(end, tab, half, m1, m2):
    bits = (lax.axis_size("canvas") - 1).bit_length()
    anywhere = pl.BlockSpec(memory_space=pl.ANY)
    blocks = m1.shape[1] // D
    return pl.pallas_call(
        wide_kernel,
        out_shape=[
            jax.ShapeDtypeStruct(end.shape, F32),
            jax.ShapeDtypeStruct((TABLE, D), F32),
            jax.ShapeDtypeStruct((2, blocks, D, D), F32),
            jax.ShapeDtypeStruct((2,) + m1.shape, F32),
        ],
        in_specs=[anywhere] * 5,
        out_specs=[anywhere] * 4,
        scratch_shapes=[
            pltpu.VMEM((blocks, D, D), F32),
            pltpu.VMEM(m1.shape, F32),
            pltpu.VMEM(m1.shape, F32),
            pltpu.VMEM(m2.shape, F32),
            pltpu.VMEM((3 * D, m1.shape[1]), BF),
            pltpu.VMEM((TABLE // 2, D), F32),
            pltpu.VMEM((bits + 1, TABLE // 2, D), F32),
            DMA((3,)),
            DMA((bits + 1,)),
            DMA((bits + 1,)),
            DMA((6,)),
            pltpu.VMEM(end.shape[1:], F32),
            DMA,
            pltpu.VMEM(m1.shape, F32),
            DMA((m1.shape[1] // PIECE,)),
        ]
        + Reduce.scratch(end.shape[2], bits)
        + Gather.scratch(end.shape[2])
        + Gather.scratch(m1.shape[1]),
        compiler_params=pltpu.CompilerParams(
            collective_id=2, has_side_effects=True, vmem_limit_bytes=60 << 20
        ),
    )(end, tab, half, m1, m2)


def muon(w, orth, large):
    return w * (1.0 - MUON_RATE * DECAY) - MUON_RATE * 0.2 * math.sqrt(large) * orth


def square_kernel(
    end_hbm,
    mid_hbm,
    wide_hbm,
    mq_hbm,
    mp_hbm,
    m1_hbm,
    m2_hbm,
    w1_hbm,
    w2_hbm,
    out_hbm,
    dx_hbm,
    gq_out,
    gp_out,
    g1_out,
    g2_out,
    nq_out,
    np_out,
    n1_out,
    n2_out,
    w1_out,
    w2_out,
    c1_out,
    c2_out,
    out_out,
    dx_out,
    orth_hbm,
    end,
    mid,
    nat,
    mq,
    mp,
    m1,
    m2,
    w1,
    w2,
    c1,
    c2,
    wide,
    out,
    dx,
    xh,
    xl,
    xs,
    in_sem,
    out_sem,
):
    core = lax.axis_index("rows")
    mlp = m1.shape[1]
    blocks = mlp // D
    pairs = (
        (end_hbm, end),
        (mq_hbm, mq),
        (mp_hbm, mp),
        (mid_hbm, mid),
        (m1_hbm, m1),
        (m2_hbm, m2),
        (w1_hbm, w1),
        (w2_hbm, w2),
        (wide_hbm, wide),
        (out_hbm, out),
        (dx_hbm, dx),
    )
    loads = [pltpu.make_async_copy(a, b, in_sem.at[i]) for i, (a, b) in enumerate(pairs)]
    for load in loads:
        load.start()
    for load in loads[0:3]:
        load.wait()
    outs = []

    def store(src, dst):
        outs.append(pltpu.make_async_copy(src, dst, out_sem.at[len(outs)]))
        outs[-1].start()

    store(end.at[0], gq_out.at[:, 0 : 2 * D])
    store(end.at[1, :, 0:D], gq_out.at[:, 2 * D : 3 * D])
    store(end.at[1, :, D : 2 * D], gp_out)

    def small(o):
        rows = pl.ds(o, 128)
        mq[rows, 0 : 2 * D] = MUON_KEEP * mq[rows, 0 : 2 * D] + end[0, rows]
        mq[rows, 2 * D : 3 * D] = MUON_KEEP * mq[rows, 2 * D : 3 * D] + end[1, rows, 0:D]
        mp[rows] = MUON_KEEP * mp[rows] + end[1, rows, D : 2 * D]

    sweep(D, 128, small)
    store(mq, nq_out)
    store(mp, np_out)

    def keep(b, v):
        xh[b], xl[b] = halves(v)

    @pl.when(core == 0)
    def _():
        xs[0] = mq[:, 0:D]
        xs[1] = mq[:, D : 2 * D]

    @pl.when(core == 1)
    def _():
        xs[0] = mq[:, 2 * D : 3 * D]
        xs[1] = mp[...]

    for b in range(2):
        keep(b, xs[b] * inverse_norm(xs[b]))

    def step(i, carry):
        x = [(xh[b], xl[b]) for b in range(2)]
        g = [
            dot_nt(jnp.concatenate([h, l, h], axis=1), jnp.concatenate([h, h, l], axis=1))
            for h, l in x
        ]
        pairs = [halves(v) for v in g]
        p = [NS_B * v + NS_C * times(w, w) for v, w in zip(g, pairs)]
        pairs = [halves(v) for v in p]
        for b in range(2):
            h, l = x[b]
            keep(b, NS_A * (h.astype(F32) + l.astype(F32)) + times(pairs[b], x[b]))
        return carry

    lax.fori_loop(0, 2, step, 0)
    for load in loads[3:6]:
        load.wait()
    store(mid.at[0], g1_out)
    for b in range(blocks):
        nat[b * D : b * D + D] = mid[1, :, b * D : b * D + D].T
    store(nat, g2_out)

    def large(o):
        rows = pl.ds(o, 64)
        m1[rows] = MUON_KEEP * m1[rows] + mid[0, rows]

    sweep(D, 64, large)
    store(m1, n1_out)

    def larger(o):
        rows = pl.ds(o, 256)
        m2[rows] = MUON_KEEP * m2[rows] + nat[rows]

    sweep(mlp, 256, larger)
    store(m2, n2_out)
    lax.fori_loop(2, 4, step, 0)
    for load in loads[6:]:
        load.wait()
    for b in range(blocks):
        at = slice(b * D, b * D + D)
        new = muon(w1[:, at], wide[0, b], mlp)
        w1[:, at] = new
        c1[:, at] = new.astype(BF)
        new = muon(w2[at], wide[1, b], mlp)
        w2[at] = new
        c2[at] = new.astype(BF)
    store(out, out_out)
    store(dx, dx_out)
    store(w1, w1_out)
    store(w2, w2_out)
    store(c1, c1_out)
    store(c2, c2_out)
    lax.fori_loop(4, 5, step, 0)
    for b in range(2):
        xs[b] = xh[b].astype(F32) + xl[b].astype(F32)
    store(xs, orth_hbm)
    for copy in outs:
        copy.wait()


def square_blocks(end, mid, wide, mq, mp, m1, m2, w1, w2, out, dx):
    anywhere = pl.BlockSpec(memory_space=pl.ANY)

    def like(v, kind=F32):
        return jax.ShapeDtypeStruct(v.shape, kind)

    def room(v, kind=F32):
        return pltpu.VMEM(v.shape, kind)

    return pl.pallas_call(
        square_kernel,
        out_shape=[like(v) for v in (mq, mp, m1, m2, mq, mp, m1, m2, w1, w2)]
        + [like(w1, BF), like(w2, BF), like(out), like(dx), jax.ShapeDtypeStruct((2, D, D), F32)],
        in_specs=[anywhere] * 11,
        out_specs=[anywhere] * 15,
        scratch_shapes=[room(v) for v in (end, mid, m2, mq, mp, m1, m2, w1, w2)]
        + [room(w1, BF), room(w2, BF), room(wide), room(out), room(dx)]
        + [
            pltpu.VMEM((2, D, D), BF),
            pltpu.VMEM((2, D, D), BF),
            pltpu.VMEM((2, D, D), F32),
            DMA((11,)),
            DMA((16,)),
        ],
        compiler_params=pltpu.CompilerParams(vmem_limit_bytes=60 << 20),
    )(end, mid, wide, mq, mp, m1, m2, w1, w2, out, dx)


def trade_kernel(own_ref, peer_ref, send_sem, recv_sem):
    core = lax.axis_index("rows")
    twin = {"rows": 1 - core}
    barrier = pltpu.get_barrier_semaphore()
    pl.semaphore_signal(barrier, inc=1, device_id=twin, device_id_type=MESH_ID)
    pl.semaphore_wait(barrier, 1)
    copy = remote(own_ref, peer_ref, send_sem, recv_sem, twin)
    copy.start()
    copy.wait()


def trade(own):
    anywhere = pl.BlockSpec(memory_space=pl.ANY)
    return pl.pallas_call(
        trade_kernel,
        out_shape=jax.ShapeDtypeStruct(own.shape, F32),
        in_specs=[anywhere],
        out_specs=anywhere,
        scratch_shapes=[DMA, DMA],
        compiler_params=pltpu.CompilerParams(collective_id=3, has_side_effects=True),
    )(own)


def moment_step(current, one, two, gradient):
    first = BETA1 * one + (1.0 - BETA1) * gradient
    second = BETA2 * two + (1.0 - BETA2) * gradient * gradient
    fix_one = 1.0 - BETA1**STEP
    fix_two = 1.0 - BETA2**STEP
    updated = current - ADAM_RATE * (first / fix_one) / (jnp.sqrt(second / fix_two) + ADAM_FLOOR)
    return first, second, updated


def update_kernel(
    own_ref,
    peer_ref,
    wq_ref,
    wp_ref,
    tab_ref,
    one_ref,
    two_ref,
    gtab_ref,
    nq_ref,
    np_ref,
    cq_ref,
    cp_ref,
    first_ref,
    second_ref,
    small_ref,
):
    lower = lax.axis_index("rows") == 0
    own, peer = own_ref[...], peer_ref[...]
    low, high = jnp.where(lower, own, peer), jnp.where(lower, peer, own)
    for i, orth in enumerate((low[0], low[1], high[0])):
        lanes = slice(i * D, i * D + D)
        new = muon(wq_ref[:, lanes], orth, D)
        nq_ref[:, lanes] = new
        cq_ref[:, lanes] = new.astype(BF)
    new = muon(wp_ref[...], high[1], D)
    np_ref[...] = new
    cp_ref[...] = new.astype(BF)
    first, second, small = moment_step(tab_ref[...], one_ref[...], two_ref[...], gtab_ref[0:SMALL])
    first_ref[...] = first
    second_ref[...] = second
    small_ref[...] = small


def update(own, peer, wq, wp, tab, one, two, gtab):
    steps = 3
    piece = D // steps

    def rows(v):
        return pl.BlockSpec((piece, v.shape[1]), lambda i: (i, 0))

    def whole(v):
        return pl.BlockSpec(v.shape, lambda i: (0, 0))

    square = pl.BlockSpec((2, piece, D), lambda i: (0, i, 0))
    weights = (wq, wp)
    return pl.pallas_call(
        update_kernel,
        grid=(steps,),
        out_shape=[jax.ShapeDtypeStruct(w.shape, F32) for w in weights]
        + [jax.ShapeDtypeStruct(w.shape, BF) for w in weights]
        + [jax.ShapeDtypeStruct(tab.shape, F32)] * 3,
        in_specs=[square, square]
        + [rows(w) for w in weights]
        + [whole(v) for v in (tab, one, two, gtab)],
        out_specs=[rows(w) for w in weights] * 2 + [whole(tab)] * 3,
        compiler_params=pltpu.CompilerParams(vmem_limit_bytes=60 << 20),
    )(own, peer, *weights, tab, one, two, gtab)


def on_device(
    x4, dy4, tall, wqkv, wp, w1, w2, mqkv, mp, m1, m2, tab, tab_one, tab_two, temp, temp_one, temp_two
):
    shape = x4.shape
    tokens = shape[1] * shape[2]
    x = x4.reshape(tokens, D)
    dy = dy4.reshape(tokens, D)
    q, k, v, sums = project(tall, x, wqkv, tab)
    out, ds1, dmx, dwp, shard, gtab, probs, unit, gprob, joint = middle(
        tall, temp, x, dy, v, sums, wp, w1, w2, tab
    )
    dx, end, gtab, half = finish(
        tall, temp, x, q, k, ds1, dmx, sums, joint, probs, unit, gprob, wqkv, tab, gtab, dwp, shard
    )
    end, gtab, wide, mid = wide_blocks(end, gtab, half, m1, m2)
    *grads, new_1, new_2, copy_1, copy_2, out, dx, square = square_blocks(
        end, mid, wide, mqkv, mp, m1, m2, w1, w2, out, dx
    )
    new_q, new_p, copy_q, copy_p, *small = update(
        square, trade(square), wqkv, wp, tab, tab_one, tab_two, gtab
    )
    results = (new_q, new_p, new_1, new_2, copy_q, copy_p, copy_1, copy_2, *small)
    heat = jnp.sum(gtab[44].reshape(HEADS, HD), axis=1)
    warm = moment_step(temp, temp_one, temp_two, heat)
    count = tokens * D * lax.axis_size("rows") * lax.axis_size("canvas")
    rms = jnp.sqrt(jnp.sum(gtab[40:44], axis=1) / count)
    return (out.reshape(shape), dx.reshape(shape), *grads, *results, *warm, rms)


def solution(mesh):
    split = P("canvas", "rows", None, None)
    return jax.shard_map(
        on_device,
        mesh=mesh,
        in_specs=(split, split, P("canvas", None)) + (P(),) * 14,
        out_specs=(split, split) + (P(),) * 23,
        check_vma=False,
    )
```

```python
import math

import jax
import jax.numpy as jnp
from jax import lax
from jax.experimental import pallas as pl
from jax.experimental.pallas import tpu as pltpu
from jax.sharding import PartitionSpec as P

BF = jnp.bfloat16
F32 = jnp.float32
MESH_ID = pl.DeviceIdType.MESH

EPS = 1e-06
ROOT_HALF = 1.0 / math.sqrt(2.0)
ROOT_TWOPI = 1.0 / math.sqrt(2.0 * math.pi)
STEP = 10
MUON_RATE = 0.2
MUON_KEEP = 0.95
DECAY = 0.01
ADAM_RATE = 0.2
BETA1 = 0.9
BETA2 = 0.95
ADAM_FLOOR = 1e-08

HEADS = 8
HD = 48
D = HEADS * HD
COLS = 32
HALO = 4 * COLS
TILE = 256

N1G, N1S, N3G, N3S, N2G, N2S, SA, SL, SM, QB, KB, VB, PB, C1B, BG, BS, C2B, F2B = range(18)
F1B, K1R, K2R = 18, 22, 31
SMALL = 40
TABLE = 48


def halves(v):
    hi = v.astype(BF)
    return hi, (v - hi.astype(F32)).astype(BF)


def side(v):
    h, l = halves(v)
    return jnp.concatenate([h, l, h], axis=1)


def dot_nn(a, b):
    return lax.dot_general(a, b, (((1,), (0,)), ((), ())), preferred_element_type=F32)


def dot_nt(a, b):
    return lax.dot_general(a, b, (((1,), (1,)), ((), ())), preferred_element_type=F32)


def normalize(v):
    mean = jnp.mean(v, axis=1, keepdims=True)
    c = v - mean
    r = lax.rsqrt(jnp.mean(c * c, axis=1, keepdims=True) + EPS)
    return c * r, r


def normalize_back(e, xhat, r):
    return r * (
        e - jnp.mean(e, axis=1, keepdims=True) - xhat * jnp.mean(e * xhat, axis=1, keepdims=True)
    )


def gelu_parts(v):
    phi = 0.5 * (1.0 + lax.erf(v * ROOT_HALF))
    return v * phi, phi + v * jnp.exp(-0.5 * v * v) * ROOT_TWOPI


def eights(v):
    total = v[0:8]
    for i in range(8, v.shape[0], 8):
        total = total + v[i : i + 8]
    return total


def sweep(count, size, body):
    def one(i, carry):
        body(pl.multiple_of(i * size, size))
        return carry

    lax.fori_loop(0, count // size, one, 0)


def image_ends(tall_ref):
    e0 = tall_ref[0, 0]
    e1 = e0 + tall_ref[0, 1]
    return e0, e1, e1 + tall_ref[0, 2]


def slots(tall_ref, core, first_row, rows_all):
    e0, e1, e2 = image_ends(tall_ref)
    low = (jnp.where(core == 0, 0, e2), jnp.where(core == 0, e0, 0), e1)
    high = (jnp.where(core == 0, e0, rows_all), jnp.where(core == 0, e1, 0), e2)
    return [((a - first_row) * COLS, (b - first_row) * COLS) for a, b in zip(low, high)]


def span_mask(start, rows, lo, hi):
    token = start + lax.broadcasted_iota(jnp.int32, (rows, D), 0)
    return (token >= lo) & (token < hi)


def lane_head():
    return lax.broadcasted_iota(jnp.int32, (HD, D), 1) // HD


def lane_slot():
    return lax.broadcasted_iota(jnp.int32, (HD, D), 1) % HD


def fold(full):
    head = lane_head()
    total = jnp.where(head == 0, full[0:HD], 0.0)
    for h in range(1, HEADS):
        total = total + jnp.where(head == h, full[h * HD : h * HD + HD], 0.0)
    return total


def unfold(small):
    head = lane_head()
    return jnp.concatenate([jnp.where(head == h, small, 0.0) for h in range(HEADS)], axis=0)


def group_ones():
    a = lax.broadcasted_iota(jnp.int32, (D, D), 0) // HD
    b = lax.broadcasted_iota(jnp.int32, (D, D), 1) // HD
    return jnp.where(a == b, 1.0, 0.0).astype(BF)


def group_sum(v, ones):
    h = v.astype(BF)
    rest = v - h.astype(F32)
    m = rest.astype(BF)
    l = (rest - m.astype(F32)).astype(BF)
    return dot_nn(h, ones) + (dot_nn(m, ones) + dot_nn(l, ones))


def row_to_fold(row, ones):
    slot = lax.broadcasted_iota(jnp.int32, (HD, D), 0)
    return group_sum(jnp.where(lane_slot() == slot, jnp.broadcast_to(row, (HD, D)), 0.0), ones)


def fold_to_row(small):
    slot = lax.broadcasted_iota(jnp.int32, (HD, D), 0)
    return jnp.sum(jnp.where(lane_slot() == slot, small, 0.0), axis=0, keepdims=True)


def head_row(temp_ref):
    head = lax.broadcasted_iota(jnp.int32, (1, D), 1) // HD
    row = jnp.where(head == 0, temp_ref[0], 0.0)
    for h in range(1, HEADS):
        row = row + jnp.where(head == h, temp_ref[h], 0.0)
    return row


def project_kernel(tall_ref, x_ref, w_ref, tab_ref, q_ref, k_ref, v_ref, sums_ref, wcat, cross):
    step = pl.program_id(0)
    core = lax.axis_index("rows")
    rows_all = 2 * pl.num_programs(0) * TILE // COLS
    spans = slots(tall_ref, core, core * (rows_all // 2), rows_all)
    start = step * TILE

    @pl.when(step == 0)
    def _():
        def part(o):
            h, l = halves(w_ref[pl.ds(o, 64)])
            wcat[pl.ds(o, 64)] = h
            wcat[pl.ds(D + o, 64)] = h
            wcat[pl.ds(2 * D + o, 64)] = l

        sweep(D, 64, part)
        cross[...] = jnp.zeros_like(cross)
        sums_ref[...] = jnp.zeros_like(sums_ref)

    xhat, _ = normalize(x_ref[...])
    lhs = side(xhat * tab_ref[N1G : N1G + 1] + tab_ref[N1S : N1S + 1])
    q = dot_nn(lhs, wcat[:, 0:D]) + tab_ref[QB : QB + 1]
    q_ref[...] = q
    k = dot_nn(lhs, wcat[:, D : 2 * D]) + tab_ref[KB : KB + 1]
    k_ref[...] = k
    v_ref[...] = dot_nn(lhs, wcat[:, 2 * D : 3 * D]) + tab_ref[VB : VB + 1]
    qt = side(q.T)
    for s, (lo, hi) in enumerate(spans):

        @pl.when((lo < start + TILE) & (hi > start))
        def _():
            mask = span_mask(start, TILE, lo, hi)
            kh, kl = halves(jnp.where(mask, k_ref[...], 0.0))
            cross[s] += dot_nn(qt, jnp.concatenate([kh, kh, kl], axis=0))
            qm = jnp.where(mask, q_ref[...], 0.0)
            km = jnp.where(mask, k_ref[...], 0.0)
            sums_ref[s, HD : HD + 1] += jnp.sum(qm * qm, axis=0, keepdims=True)
            sums_ref[s, HD + 1 : HD + 2] += jnp.sum(km * km, axis=0, keepdims=True)

    @pl.when(step == pl.num_programs(0) - 1)
    def _():
        for s in range(3):
            sums_ref[s, 0:HD] = fold(cross[s])


def project(tall, x, w, tab):
    tokens = x.shape[0]
    row = pl.BlockSpec((TILE, D), lambda i: (i, 0))
    return pl.pallas_call(
        project_kernel,
        grid=(tokens // TILE,),
        out_shape=[jax.ShapeDtypeStruct((tokens, D), F32)] * 3
        + [jax.ShapeDtypeStruct((3, HD + 8, D), F32)],
        in_specs=[
            pl.BlockSpec(memory_space=pltpu.SMEM),
            row,
            pl.BlockSpec((D, 3 * D), lambda i: (0, 0)),
            pl.BlockSpec((SMALL, D), lambda i: (0, 0)),
        ],
        out_specs=[row, row, row, pl.BlockSpec((3, HD + 8, D), lambda i: (0, 0, 0))],
        scratch_shapes=[pltpu.VMEM((3 * D, 3 * D), BF), pltpu.VMEM((3, D, D), F32)],
        compiler_params=pltpu.CompilerParams(vmem_limit_bytes=60 << 20),
    )(tall, x, w, tab)


ORDERS = ((0, 1, 2, 3), (1, 2, 0, 3), (2, 0, 1, 3))
EARLY, LATE = range(0, 3), range(3, 6)
PIECE = 256
SHARD = D // 16
DMA = pltpu.SemaphoreType.DMA


class Links:
    def __init__(self):
        self.core = lax.axis_index("rows")
        chip = lax.axis_index("canvas")
        self.bits = (lax.axis_size("canvas") - 1).bit_length()
        self.mine = [lax.rem(lax.div(chip, 1 << b), 2) for b in range(self.bits)]
        self.there = [{"canvas": chip + (1 - 2 * m) * (1 << b)} for b, m in enumerate(self.mine)]
        self.twin = {"rows": 1 - self.core}

    def call(self):
        barrier = pltpu.get_barrier_semaphore()
        for other in [self.twin] + self.there:
            pl.semaphore_signal(barrier, inc=1, device_id=other, device_id_type=MESH_ID)

    def answer(self):
        pl.semaphore_wait(pltpu.get_barrier_semaphore(), self.bits + 1)

    def greet(self):
        self.call()
        self.answer()


def remote(src, dst, send, recv, other):
    return pltpu.make_async_remote_copy(
        src_ref=src,
        dst_ref=dst,
        send_sem=send,
        recv_sem=recv,
        device_id=other,
        device_id_type=MESH_ID,
    )


class Pieces:
    count = 6

    def __init__(self, links, lanes):
        self.links = links
        self.width = lanes // self.count

    def lanes(self, p):
        return slice(p * self.width, p * self.width + self.width)

    def bit(self, p, s):
        return ORDERS[p % 3][s]

    def start(self, p, s):
        at = 0
        for t in range(s):
            at = at + self.links.mine[self.bit(p, t)] * (D >> (t + 1))
        return at

    def held(self, p, s):
        return pl.ds(pl.multiple_of(self.start(p, s), 8), D >> s)


class Reduce(Pieces):
    def __init__(self, links, src, buf, work):
        super().__init__(links, src.shape[2])
        self.src, self.buf = src, buf
        self.first, self.land, self.pair_sem, self.send_sem, self.recv_sem = work

    @classmethod
    def scratch(cls, lanes, bits):
        steps = max(bits, 4)
        return [
            pltpu.VMEM((D, lanes), F32),
            pltpu.VMEM((D - SHARD + (steps - 4) * SHARD, lanes), F32),
            DMA((2, cls.count)),
            DMA((cls.count, steps)),
            DMA((cls.count, steps)),
        ]

    def add(self, p, rows, src, src_rows):
        lanes = self.lanes(p)
        self.buf[rows, lanes] += src[src_rows, lanes]

    def pair(self, p):
        lanes = self.lanes(p)
        return remote(
            self.src.at[1 - self.links.core, :, lanes],
            self.first.at[:, lanes],
            self.pair_sem.at[0, p],
            self.pair_sem.at[1, p],
            self.links.twin,
        )

    def move(self, p, s):
        b = self.bit(p, s)
        half = D >> (s + 1)
        away = pl.multiple_of(self.start(p, s) + (1 - self.links.mine[b]) * half, 8)
        lanes = self.lanes(p)
        return remote(
            self.buf.at[pl.ds(away, half), lanes],
            self.land.at[pl.ds(D - (D >> s), half), lanes],
            self.send_sem.at[p, s],
            self.recv_sem.at[p, s],
            self.links.there[b],
        )

    def begin(self):
        for p in range(self.count):
            self.pair(p).start()

    def join(self, some):
        for p in some:
            self.pair(p).wait()
            self.add(p, pl.ds(0, D), self.first, pl.ds(0, D))
            self.move(p, 0).start()

    def down(self, s, some, last=3):
        for p in some:
            self.move(p, s).wait()
            self.add(p, self.held(p, s + 1), self.land, pl.ds(D - (D >> s), D >> (s + 1)))
            if s < last:
                self.move(p, s + 1).start()
        if s == 3:
            for b in range(4, self.links.bits):
                self.swap(b, some)

    def swap(self, b, some):
        at = pl.ds(D - SHARD + (b - 4) * SHARD, SHARD)
        copies = {}
        for p in some:
            lanes = self.lanes(p)
            copies[p] = remote(
                self.buf.at[self.held(p, 4), lanes],
                self.land.at[at, lanes],
                self.send_sem.at[p, b],
                self.recv_sem.at[p, b],
                self.links.there[b],
            )
            copies[p].start()
        for p in some:
            copies[p].wait()
            self.add(p, self.held(p, 4), self.land, at)


class Gather(Pieces):
    def __init__(self, links, whole, dst, work):
        super().__init__(links, whole.shape[1])
        self.whole, self.dst = whole, dst
        self.send_sem, self.recv_sem, self.out_sem = work

    @classmethod
    def scratch(cls, lanes):
        return [DMA((cls.count, 4)), DMA((cls.count, 4)), DMA((2, 3, cls.count))]

    def back(self, p, s):
        view = self.whole.at[self.held(p, s + 1), self.lanes(p)]
        return remote(
            view,
            view,
            self.send_sem.at[p, s],
            self.recv_sem.at[p, s],
            self.links.there[self.bit(p, s)],
        )

    def outs(self, p, n):
        mine = self.links.mine[self.bit(p, 0)]
        half = D // 2
        at = pl.multiple_of(half * (mine if n == 0 else 1 - mine), 8)
        rows = pl.ds(at, half)
        src = self.whole.at[rows, self.lanes(p)]
        dst = self.dst.at[self.links.core, rows, self.lanes(p)]
        sem = self.out_sem.at[n]
        return (
            pltpu.make_async_copy(src, dst, sem.at[0, p]),
            remote(src, dst, sem.at[1, p], sem.at[2, p], self.links.twin),
        )

    def begin(self, some):
        for p in some:
            self.back(p, 3).start()

    def up(self, s, some):
        for p in some:
            self.back(p, s).wait()
            if s > 0:
                self.back(p, s - 1).start()
            if s < 2:
                for copy in self.outs(p, 1 - s):
                    copy.start()

    def end(self):
        for n in range(2):
            for p in range(self.count):
                for copy in self.outs(p, n):
                    copy.wait()


class Turn(Pieces):
    def __init__(self, links, rest, whole, work):
        super().__init__(links, whole.shape[1])
        self.rest, self.whole = rest, whole
        self.land, self.send_sem, self.recv_sem = work

    @classmethod
    def scratch(cls, lanes, bits):
        steps = max(bits, 4) - 3
        return [
            pltpu.VMEM((steps * SHARD, lanes), F32),
            DMA((cls.count, steps)),
            DMA((cls.count, steps)),
        ]

    def move(self, p, n):
        lanes = self.lanes(p)
        if n == 0:
            b = self.bit(p, 3)
            at = pl.multiple_of((1 - self.links.mine[b]) * SHARD, 8)
            src = self.rest.at[pl.ds(at, SHARD), lanes]
        else:
            b = 3 + n
            src = self.whole.at[self.held(p, 4), lanes]
        return remote(
            src,
            self.land.at[n * SHARD : n * SHARD + SHARD, lanes],
            self.send_sem.at[p, n],
            self.recv_sem.at[p, n],
            self.links.there[b],
        )

    def begin(self):
        for p in range(self.count):
            self.move(p, 0).start()

    def end(self, some):
        for p in some:
            lanes = self.lanes(p)
            at = pl.multiple_of(self.links.mine[self.bit(p, 3)] * SHARD, 8)
            self.move(p, 0).wait()
            self.whole[self.held(p, 4), lanes] = (
                self.rest[pl.ds(at, SHARD), lanes] + self.land[0:SHARD, lanes]
            )
        for n in range(1, self.links.bits - 3):
            for p in some:
                self.move(p, n).start()
            for p in some:
                lanes = self.lanes(p)
                self.move(p, n).wait()
                self.whole[self.held(p, 4), lanes] += self.land[n * SHARD : n * SHARD + SHARD, lanes]


def row_flags(tall_ref, rows_all):
    ends = image_ends(tall_ref)

    def above(row):
        first = (row == 0) | (row == ends[0]) | (row == ends[1]) | (row == ends[2])
        return jnp.where(first, 0.0, 1.0)

    def below(row):
        return jnp.where(row + 1 == rows_all, 0.0, above(row + 1))

    return above, below


def middle_kernel(
    tall_ref,
    temp_ref,
    x_hbm,
    dy_hbm,
    v_hbm,
    sums_ref,
    wp_ref,
    w1_hbm,
    w2_ref,
    tab_ref,
    out_hbm,
    ds1_hbm,
    dmx_hbm,
    dwp_ref,
    shard_ref,
    gtab_ref,
    probs_ref,
    unit_ref,
    gprob_ref,
    joint_ref,
    wpv,
    wph,
    w1c,
    w2c,
    pcat,
    mixed,
    s1,
    li,
    act,
    slope,
    mid,
    s2,
    ds2,
    gp,
    n2c,
    dzc,
    b1_ref,
    b1g_ref,
    acc,
    cross,
    x_ref,
    dy_ref,
    v_ref,
    flags,
    nt,
    dt,
    peer_ref,
    dw_ref,
    load_sem,
    store_sem,
    edge_sem,
    *work,
):
    links = Links()
    core = links.core
    wide = x_ref.shape[0]
    tokens = wide - HALO
    dw1_ref, dw2_ref = dw_ref.at[0], dw_ref.at[1]
    reduce = Reduce(links, dw_ref, dw_ref.at[core], work)
    w1_ref = work[0]
    lo_ = x_ref
    own = pl.ds(pl.multiple_of(core * HALO, HALO), tokens)
    pairs = ((w1_hbm, w1_ref), (v_hbm, v_ref.at[own]), (x_hbm, x_ref.at[own]), (dy_hbm, dy_ref.at[own]))
    loads = [pltpu.make_async_copy(a, b, load_sem.at[i]) for i, (a, b) in enumerate(pairs)]
    for load in loads:
        load.start()
    links.call()
    edge = pl.ds(pl.multiple_of((1 - core) * (tokens - HALO), HALO), HALO)
    far = pl.ds(pl.multiple_of(core * tokens, HALO), HALO)
    pairs = (
        (sums_ref.at[2], peer_ref),
        (v_hbm.at[edge], v_ref.at[far]),
        (x_hbm.at[edge], x_ref.at[far]),
        (dy_hbm.at[edge], dy_ref.at[far]),
    )
    edges = [
        remote(a, b, edge_sem.at[0, i], edge_sem.at[1, i], links.twin)
        for i, (a, b) in enumerate(pairs)
    ]
    own_rows = tokens // COLS
    rows_wide = wide // COLS
    rows_all = 2 * own_rows
    first_row = core * (own_rows - HALO // COLS)
    own_off = pl.multiple_of(core * HALO, HALO)
    mlp = w1_hbm.shape[1]
    spans = slots(tall_ref, core, first_row, rows_all)
    above, below = row_flags(tall_ref, rows_all)

    def tab(r):
        return tab_ref[r : r + 1]

    def is_own(row):
        return (row >= core * (HALO // COLS)) & (row < core * (HALO // COLS) + own_rows)

    loads[0].wait()

    def part_1(o):
        rows = pl.ds(o, 64)
        h, l = halves(w1_ref[rows])
        w1c[rows] = h
        w1c[pl.ds(D + o, 64)] = h
        w1c[pl.ds(2 * D + o, 64)] = l

    sweep(D, 64, part_1)
    links.answer()
    for copy in edges:
        copy.start()

    def part_p(o):
        rows = pl.ds(o, 192)
        h, l = halves(wp_ref[rows])
        wpv[rows] = h
        wpv[pl.ds(D + o, 192)] = h
        wpv[pl.ds(2 * D + o, 192)] = l
        wph[rows, 0:D] = h
        wph[rows, D : 2 * D] = h
        wph[rows, 2 * D : 3 * D] = l

    sweep(D, 192, part_p)

    def part_2(o):
        rows = pl.ds(o, 256)
        h, l = halves(w2_ref[rows])
        w2c[rows, 0:D] = h
        w2c[rows, D : 2 * D] = h
        w2c[rows, 2 * D : 3 * D] = l

    sweep(mlp, 256, part_2)

    edges[0].wait()
    ones = group_ones()
    temp = head_row(temp_ref)
    for s in range(3):
        sums = sums_ref[s]
        if s == 2:
            sums = sums + peer_ref[...]
            joint_ref[...] = sums
        inv_q = lax.rsqrt(sums[HD : HD + 1] + EPS)
        inv_k = lax.rsqrt(sums[HD + 1 : HD + 2] + EPS)
        unit = sums[0:HD] * row_to_fold(inv_q, ones) * inv_k
        unit_ref[s] = unit
        weight = jnp.exp(temp * unit)
        probs = weight / group_sum(weight, ones)
        probs_ref[s] = probs
        h, l = halves(unfold(probs))
        pcat[:, 3 * s * D : 3 * s * D + 3 * D] = jnp.concatenate([h, h, l], axis=1)

    acc[...] = jnp.zeros_like(acc)
    gtab_ref[...] = jnp.zeros_like(gtab_ref)

    def add(r, v):
        acc[8 * r : 8 * r + 8] += v

    for copy in loads[1:] + edges[1:]:
        copy.wait()

    def own_part(o, size):
        token = o + lax.broadcasted_iota(jnp.int32, (size, D), 0)
        return jnp.where((token >= own_off) & (token < own_off + tokens), 1.0, 0.0)

    def attend(o):
        size = wide // 3
        v = v_ref[pl.ds(o, size)]
        by_slot = [side(jnp.where(span_mask(o, size, lo, hi), v, 0.0)) for lo, hi in spans]
        mix = dot_nt(jnp.concatenate(by_slot, axis=1), pcat[...])
        mixed[pl.ds(o, size)] = mix
        z = dot_nn(side(mix), wpv[...]) + tab(PB)
        rows = pl.ds(o, size)
        branch = tab(SA) * z
        stream = x_ref[rows] + branch
        s1[rows] = stream
        xhat, _ = normalize(stream)
        li[pl.ds(o + COLS, size)] = xhat * tab(N3G) + tab(N3S)
        add(41, eights(own_part(o, size) * branch * branch))

    for o in range(0, wide, wide // 3):
        attend(o)

    pad = jnp.zeros((COLS, D), F32)
    for buf in (li, mid, gp, ds2):
        buf[0:COLS] = pad
        buf[wide + COLS : wide + 2 * COLS] = pad

    for r in range(rows_wide):
        row = first_row + r
        mine = jnp.where(is_own(r), 1.0, 0.0)
        for n, flag in enumerate((above(row), below(row), mine)):
            flags[n, r * COLS : r * COLS + COLS] = jnp.full((COLS, 128), flag, F32)

    block = 12 * COLS
    col = lax.rem(lax.broadcasted_iota(jnp.int32, (block + 2 * COLS, 128), 0), COLS)

    def convolve(src, base, flip, scale, visit, other=None, events=()):
        def one(n, carry):
            for when, event in events:
                pl.when(n == when)(event)
            lanes = pl.ds(pl.multiple_of(lax.rem(n, 3) * 128, 128), 128)
            m = lax.div(n, 3)
            place = lax.div((m - 1) * (m - 2), 2) + 2 * core * m * (2 - m) + (1 - core) * m * (m - 1)
            o = pl.multiple_of(place * block, block)
            rows = pl.ds(o, block)
            taps = [tab_ref[base + t : base + t + 1, lanes] for t in range(9)]
            if flip:
                taps = taps[::-1]
            if scale is not None:
                taps = [t * tab_ref[scale : scale + 1, lanes] for t in taps]
            u = src[pl.ds(o, block + 2 * COLS), lanes]
            left = jnp.where(col == 0, 0.0, pltpu.roll(u, 1, 0))
            right = jnp.where(col == COLS - 1, 0.0, pltpu.roll(u, block + 2 * COLS - 1, 0))
            up, down = flags[0, rows], flags[1, rows]

            def line(a):
                cut = slice(a * COLS, a * COLS + block)
                return left[cut] * taps[3 * a] + u[cut] * taps[3 * a + 1] + right[cut] * taps[3 * a + 2]

            visit(o, rows, lanes, line(1) + up * line(0) + down * line(2))
            if other is not None:
                near = other[pl.ds(o, block + 2 * COLS), lanes]
                mine = flags[2, rows]
                held = (
                    mine * up * near[0:block],
                    mine * near[COLS : COLS + block],
                    mine * down * near[2 * COLS : 2 * COLS + block],
                )
                inner = slice(COLS, COLS + block)
                for a in range(3):
                    for b, view in enumerate((right, u, left)):
                        t = 8 * (base + 3 * a + b)
                        acc[t : t + 8, lanes] += eights(view[inner] * held[a])
            return carry

        lax.fori_loop(0, 3 * (wide // block), one, 0)

    def first(o, rows, lanes, value):
        at = pl.ds(o + COLS, block)
        a, s = gelu_parts(value + tab_ref[C1B : C1B + 1, lanes])
        act[rows, lanes] = a
        slope[rows, lanes] = s
        mid[at, lanes] = a * tab_ref[BG : BG + 1, lanes] + tab_ref[BS : BS + 1, lanes]

    convolve(li, K1R, False, None, first)

    def second(o, rows, lanes, value):
        value = value + tab_ref[C2B : C2B + 1, lanes]
        lo_[rows, lanes] = value
        branch = tab_ref[SL : SL + 1, lanes] * value
        s2[rows, lanes] = s1[rows, lanes] + branch
        acc[8 * 42 : 8 * 42 + 8, lanes] += eights(flags[2, rows] * branch * branch)

    convolve(mid, K2R, False, None, second)

    dw1_ref[...] = jnp.zeros_like(dw1_ref)
    dw2_ref[...] = jnp.zeros_like(dw2_ref)
    b1g_ref[...] = jnp.zeros_like(b1g_ref)
    for i in range(mlp // D):
        b1_ref[0:1, i * D : i * D + D] = tab(F1B + i)

    def feed(o):
        here = pl.ds(o, TILE)
        xhat, _ = normalize(s2[here])
        n2 = xhat * tab(N2G) + tab(N2S)
        n2c[...] = side(n2)
        dz = tab(SM) * dy_ref[here]
        dzc[...] = side(dz)
        nt[...] = side(n2.T)
        dt[...] = side(dz.T)
        add(F2B, eights(dz))

        def enter(j):
            return dot_nn(n2c[...], w1c[:, j : j + PIECE]), dot_nt(dzc[...], w2c[j : j + PIECE])

        raw, dn = tab(F2B), 0.0
        ready = enter(0)
        for j in range(0, mlp, PIECE):
            lanes = slice(j, j + PIECE)
            pre, dh = ready
            if j + PIECE < mlp:
                ready = enter(j + PIECE)
            a, slope_j = gelu_parts(pre + b1_ref[0:1, lanes])
            dp = dh * slope_j
            ah, al = halves(a)
            ph, pl_ = halves(dp)
            w2h, w2l = w2c[lanes, 0:D], w2c[lanes, 2 * D : 3 * D]
            raw = raw + (dot_nn(ah, w2h) + (dot_nn(al, w2h) + dot_nn(ah, w2l)))
            w1h, w1l = w1c[0:D, lanes], w1c[2 * D : 3 * D, lanes]
            dn = dn + (dot_nt(ph, w1h) + (dot_nt(pl_, w1h) + dot_nt(ph, w1l)))
            b1g_ref[:, lanes] += eights(dp)
            dw1_ref[:, lanes] += dot_nn(nt[...], jnp.concatenate([ph, ph, pl_], axis=0))
            dw2_ref[:, lanes] += dot_nn(dt[...], jnp.concatenate([ah, ah, al], axis=0))
        dy = dy_ref[here]
        xhat, r = normalize(s2[here])
        ds2[pl.ds(pl.multiple_of(o + COLS, COLS), TILE)] = dy + normalize_back(dn * tab(N2G), xhat, r)
        branch = tab(SM) * raw
        result = s2[here] + branch
        s2[here] = result
        add(40, eights(result * result))
        add(43, eights(branch * branch))
        add(SM, eights(dy * raw))
        add(N2G, eights(dn * xhat))
        add(N2S, eights(dn))

    def feed_one(i, carry):
        feed(pl.multiple_of(own_off + i * TILE, 128))
        return carry

    lax.fori_loop(0, tokens // TILE, feed_one, 0)
    reduce.begin()
    stores = [pltpu.make_async_copy(s2.at[own], out_hbm, store_sem.at[0])]
    stores[0].start()
    edge = HALO // 2
    rest = pl.multiple_of(COLS + (1 - core) * (tokens + edge), COLS)
    ds2[pl.ds(rest, edge)] = jnp.zeros((edge, D), F32)
    rows_out = pl.multiple_of(COLS + own_off + (1 - core) * (tokens - edge), COLS)
    rows_in = pl.multiple_of(COLS + edge + core * (tokens - edge), COLS)
    turned = remote(
        ds2.at[pl.ds(rows_out, edge)],
        ds2.at[pl.ds(rows_in, edge)],
        edge_sem.at[0, 4],
        edge_sem.at[1, 4],
        links.twin,
    )
    turned.start()

    def third(o, rows, lanes, value):
        grad = value * tab_ref[BG : BG + 1, lanes] * slope[rows, lanes]
        gp[pl.ds(o + COLS, block), lanes] = grad
        held = flags[2, rows] * value
        acc[8 * BG : 8 * BG + 8, lanes] += eights(held * act[rows, lanes])
        acc[8 * BS : 8 * BS + 8, lanes] += eights(held)
        acc[8 * C1B : 8 * C1B + 8, lanes] += eights(flags[2, rows] * grad)

    convolve(
        ds2,
        K2R,
        True,
        SL,
        third,
        mid,
        ((5, lambda: reduce.join(EARLY)), (6, turned.wait), (8, lambda: reduce.join(LATE))),
    )

    def fourth(o, rows, lanes, value):
        slope[rows, lanes] = value

    convolve(gp, K1R, True, None, fourth, li, ((6, lambda: reduce.down(0, EARLY, 2)),))

    dwp_ref[...] = jnp.zeros_like(dwp_ref)
    cross[...] = jnp.zeros_like(cross)

    def back(step):
        o = pl.multiple_of(own_off + step * TILE, 128)

        here_wide = pl.ds(o, TILE)
        xhat, r = normalize(s1[here_wide])
        grad = slope[here_wide]
        grad_two = ds2[pl.ds(pl.multiple_of(o + COLS, COLS), TILE)]
        result = grad_two + normalize_back(grad * tab(N3G), xhat, r)
        slope[here_wide] = result
        add(N3G, eights(grad * xhat))
        add(N3S, eights(grad))
        add(SL, eights(grad_two * lo_[here_wide]))
        add(C2B, eights(grad_two))
        add(PB, eights(result))
        dmx = dot_nt(side(tab(SA) * result), wph[...])
        act[here_wide] = dmx
        h, l = halves(result)
        dwp_ref[...] += dot_nn(side(mixed[pl.ds(o, TILE)].T), jnp.concatenate([h, h, l], axis=0))
        v = v_ref[pl.ds(o, TILE)]
        by_slot = [halves(jnp.where(span_mask(o, TILE, lo, hi), v, 0.0)) for lo, hi in spans]
        high = jnp.concatenate([h for h, l in by_slot], axis=1)
        low = jnp.concatenate([l for h, l in by_slot], axis=1)
        cross[...] += dot_nn(side(dmx.T), jnp.concatenate([high, high, low], axis=0))

    count = tokens // TILE
    for step in range(count):
        back(step)
        if step == 0:
            reduce.down(0, LATE, 2)
        if step == 1:
            reduce.down(1, EARLY, 2)
        if step == 2:
            reduce.down(1, LATE, 2)
    for src, dst in ((slope, ds1_hbm), (act, dmx_hbm)):
        stores.append(pltpu.make_async_copy(src.at[own], dst, store_sem.at[len(stores)]))
        stores[-1].start()
    for s in range(3):
        gprob_ref[s] = fold(cross[:, s * D : s * D + D])

    def total(r):
        return jnp.sum(acc[8 * r : 8 * r + 8], axis=0, keepdims=True)

    for r in (N3G, N3S, N2G, N2S, SL, SM, C1B, BG, BS, F2B, 40, 41, 42, 43):
        gtab_ref[r : r + 1] = total(r)
    for t in range(9):
        gtab_ref[K1R + t : K1R + t + 1] = total(K1R + t)
        gtab_ref[K2R + t : K2R + t + 1] = total(K2R + t) * tab(SL)
    gtab_ref[C2B : C2B + 1] = total(C2B) * tab(SL)
    gtab_ref[PB : PB + 1] = total(PB) * tab(SA)
    raw = dwp_ref[...]
    gtab_ref[SA : SA + 1] = jnp.sum(raw * wp_ref[...], axis=0, keepdims=True) + total(PB) * tab(PB)
    dwp_ref[...] = raw * tab(SA)
    for i in range(mlp // D):
        gtab_ref[F1B + i : F1B + i + 1] = jnp.sum(b1g_ref[:, i * D : i * D + D], axis=0, keepdims=True)
    reduce.down(2, EARLY, 2)
    reduce.down(2, LATE, 2)
    for p in range(reduce.count):
        lanes = reduce.lanes(p)
        shard_ref[:, lanes] = reduce.buf[reduce.held(p, 3), lanes]
    for copy in stores:
        copy.wait()


def middle(tall, temp, x, dy, v, sums, wp, w1, w2, tab):
    tokens = x.shape[0]
    wide = tokens + HALO
    mlp = w1.shape[1]
    smem = pl.BlockSpec(memory_space=pltpu.SMEM)
    vmem = pl.BlockSpec(memory_space=pltpu.VMEM)
    anywhere = pl.BlockSpec(memory_space=pl.ANY)

    def f(*shape):
        return jax.ShapeDtypeStruct(shape, F32)

    def s(*shape):
        return pltpu.VMEM(shape, F32)

    def b(*shape):
        return pltpu.VMEM(shape, BF)

    padded = s(wide + 2 * COLS, D)
    return pl.pallas_call(
        middle_kernel,
        out_shape=[
            f(tokens, D),
            f(tokens, D),
            f(tokens, D),
            f(D, D),
            f(2 * SHARD, mlp),
            f(TABLE, D),
            f(3, HD, D),
            f(3, HD, D),
            f(3, HD, D),
            f(*sums.shape[1:]),
        ],
        in_specs=[smem, smem] + [anywhere] * 3 + [vmem, vmem, anywhere, vmem, vmem],
        out_specs=[anywhere] * 3 + [vmem] * 7,
        scratch_shapes=[
            b(3 * D, D),
            b(D, 3 * D),
            b(3 * D, mlp),
            b(mlp, 3 * D),
            b(D, 9 * D),
            s(wide, D),
            s(wide, D),
            padded,
            s(wide, D),
            s(wide, D),
            padded,
            s(wide, D),
            padded,
            padded,
            b(TILE, 3 * D),
            b(TILE, 3 * D),
            s(8, mlp),
            s(8, mlp),
            s(8 * TABLE, D),
            s(D, 3 * D),
            s(wide, D),
            s(wide, D),
            s(wide, D),
            s(3, wide, 128),
            b(D, 3 * TILE),
            b(D, 3 * TILE),
            s(*sums.shape[1:]),
            s(2, D, mlp),
            DMA((4,)),
            DMA((3,)),
            DMA((2, 5)),
        ]
        + Reduce.scratch(mlp, (lax.axis_size("canvas") - 1).bit_length()),
        compiler_params=pltpu.CompilerParams(
            collective_id=0, has_side_effects=True, vmem_limit_bytes=60 << 20
        ),
    )(tall, temp, x, dy, v, sums, wp, w1, w2, tab)


def finish_kernel(
    tall_ref,
    temp_ref,
    x_ref,
    q_ref,
    k_ref,
    ds1_ref,
    dmx_ref,
    sums_ref,
    peer_ref,
    probs_ref,
    unit_ref,
    gprob_ref,
    w_ref,
    tab_ref,
    gtab_ref,
    dwp_ref,
    shard_ref,
    dx_ref,
    dw_ref,
    otab_ref,
    sum_hbm,
    wh,
    wl,
    pv,
    cv,
    ch,
    side_rows,
    acc,
    gpeer_ref,
    whole,
    gsend,
    grecv,
    *work,
):
    step = pl.program_id(0)
    last = pl.num_programs(0) - 1
    links = Links()
    core = links.core
    turn = Turn(links, shard_ref, whole, work[:3])
    gather = Gather(links, whole, sum_hbm, work[3:])
    rows_all = 2 * pl.num_programs(0) * TILE // COLS
    spans = slots(tall_ref, core, core * (rows_all // 2), rows_all)
    start = step * TILE

    def tab(r):
        return tab_ref[r : r + 1]

    @pl.when(step == 0)
    def _():
        links.greet()
        swap = remote(gprob_ref.at[2], gpeer_ref, gsend, grecv, links.twin)
        swap.start()
        turn.begin()

        def part(o):
            h, l = halves(w_ref[pl.ds(o, 64)])
            wh[pl.ds(o, 64)] = h
            wl[pl.ds(o, 64)] = l

        sweep(D, 64, part)
        dw_ref[...] = jnp.zeros_like(dw_ref)
        dw_ref[1, :, D : 2 * D] = dwp_ref[...]
        acc[...] = jnp.zeros_like(acc)
        ones = group_ones()
        temp = head_row(temp_ref)
        heat = jnp.zeros((1, D), F32)
        for s in range(3):
            sums = sums_ref[s]
            grad = gprob_ref[s]
            if s == 2:
                swap.wait()
                sums = peer_ref[...]
                grad = grad + gpeer_ref[...]
            inv_q = lax.rsqrt(sums[HD : HD + 1] + EPS)
            inv_k = lax.rsqrt(sums[HD + 1 : HD + 2] + EPS)
            probs = probs_ref[s]
            unit = unit_ref[s]
            scores = probs * (grad - group_sum(probs * grad, ones))
            part_heat = jnp.sum(scores * unit, axis=0, keepdims=True)
            heat = heat + (part_heat if s < 2 else jnp.where(core == 0, part_heat, 0.0))
            pull = temp * scores
            both = pull * unit
            side_rows[8 * s : 8 * s + 1] = fold_to_row(group_sum(both, ones)) * inv_q * inv_q
            side_rows[8 * s + 1 : 8 * s + 2] = jnp.sum(both, axis=0, keepdims=True) * inv_k * inv_k
            across = slice(3 * s * D, 3 * s * D + 3 * D)
            h, l = halves(unfold(pull * row_to_fold(inv_q, ones) * inv_k))
            cv[across] = jnp.concatenate([h, h, l], axis=0)
            ch[:, across] = jnp.concatenate([h, h, l], axis=1)
            h, l = halves(unfold(probs))
            pv[across] = jnp.concatenate([h, h, l], axis=0)
        otab_ref[...] = gtab_ref[...]
        otab_ref[44:45] = heat

    masks = [span_mask(start, TILE, lo, hi) for lo, hi in spans]

    def by_slot(v):
        return jnp.concatenate([side(jnp.where(mask, v, 0.0)) for mask in masks], axis=1)

    def rows_of(r):
        return sum(jnp.where(mask, side_rows[8 * s + r : 8 * s + r + 1], 0.0) for s, mask in enumerate(masks))

    def at(n, *events):
        @pl.when(step == n)
        def _():
            for event, *args in events:
                event(*args)

    q, k = q_ref[...], k_ref[...]
    dq = dot_nt(by_slot(k), ch[...]) - q * rows_of(0)
    dk = dot_nn(by_slot(q), cv[...]) - k * rows_of(1)
    dv = dot_nn(by_slot(dmx_ref[...]), pv[...])
    dqkv = jnp.concatenate([dq, dk, dv], axis=1)
    at(0, (turn.end, EARLY), (gather.begin, EARLY))
    at(1, (gather.up, 3, EARLY))
    at(2, (gather.up, 2, LATE))
    at(3, (gather.up, 1, LATE))

    h, l = halves(dqkv)
    dn = dot_nt(h, wh[...]) + (dot_nt(l, wh[...]) + dot_nt(h, wl[...]))
    xhat, r = normalize(x_ref[...])
    nt = side((xhat * tab(N1G) + tab(N1S)).T)
    grads = dot_nn(nt, jnp.concatenate([h, h, l], axis=0))
    dw_ref[0] += grads[:, 0 : 2 * D]
    dw_ref[1, :, 0:D] += grads[:, 2 * D : 3 * D]
    dx_ref[...] = ds1_ref[...] + normalize_back(dn * tab(N1G), xhat, r)
    acc[0:8] += eights(dn * xhat)
    acc[8:16] += eights(dn)
    for i, v in enumerate((dq, dk, dv)):
        acc[16 + 8 * i : 24 + 8 * i] += eights(v)

    at(0, (turn.end, LATE), (gather.begin, LATE))
    at(1, (gather.up, 3, LATE), (gather.up, 2, EARLY))
    at(2, (gather.up, 1, EARLY))

    @pl.when(step == last)
    def _():
        for i, r in enumerate((N1G, N1S, QB, KB, VB)):
            otab_ref[r : r + 1] = jnp.sum(acc[8 * i : 8 * i + 8], axis=0, keepdims=True)
        gather.up(0, EARLY)
        gather.up(0, LATE)
        gather.end()


def finish(tall, temp, x, q, k, ds1, dmx, sums, peer, probs, unit, gprob, w, tab, gtab, dwp, shard):
    tokens = x.shape[0]
    smem = pl.BlockSpec(memory_space=pltpu.SMEM)
    anywhere = pl.BlockSpec(memory_space=pl.ANY)
    row = pl.BlockSpec((TILE, D), lambda i: (i, 0))
    bits = (lax.axis_size("canvas") - 1).bit_length()

    def whole(v):
        return pl.BlockSpec(v.shape, lambda i: (0,) * v.ndim)

    fixed = (sums, peer, probs, unit, gprob, w, tab, gtab, dwp, shard)
    return pl.pallas_call(
        finish_kernel,
        grid=(tokens // TILE,),
        out_shape=[
            jax.ShapeDtypeStruct((tokens, D), F32),
            jax.ShapeDtypeStruct((2, D, 2 * D), F32),
            jax.ShapeDtypeStruct((TABLE, D), F32),
            jax.ShapeDtypeStruct((2, D, shard.shape[1]), F32),
        ],
        in_specs=[smem, smem] + [row] * 5 + [whole(v) for v in fixed],
        out_specs=[
            row,
            pl.BlockSpec((2, D, 2 * D), lambda i: (0, 0, 0)),
            pl.BlockSpec((TABLE, D), lambda i: (0, 0)),
            anywhere,
        ],
        scratch_shapes=[
            pltpu.VMEM((D, 3 * D), BF),
            pltpu.VMEM((D, 3 * D), BF),
            pltpu.VMEM((9 * D, D), BF),
            pltpu.VMEM((9 * D, D), BF),
            pltpu.VMEM((D, 9 * D), BF),
            pltpu.VMEM((24, D), F32),
            pltpu.VMEM((40, D), F32),
            pltpu.VMEM(gprob.shape[1:], F32),
            pltpu.VMEM((D, shard.shape[1]), F32),
            DMA,
            DMA,
        ]
        + Turn.scratch(shard.shape[1], bits)
        + Gather.scratch(shard.shape[1]),
        compiler_params=pltpu.CompilerParams(
            collective_id=1, has_side_effects=True, vmem_limit_bytes=60 << 20
        ),
    )(tall, temp, x, q, k, ds1, dmx, *fixed)


NS_A, NS_B, NS_C = 3.4445, -4.7750, 2.0315


def times(a, b):
    return dot_nn(
        jnp.concatenate([a[0], a[1], a[0]], axis=1), jnp.concatenate([b[0], b[0], b[1]], axis=0)
    )


def inverse_norm(v):
    total = jnp.sum(jnp.sum(v * v, axis=0, keepdims=True), axis=1, keepdims=True)
    return 1.0 / (jnp.sqrt(total) + 1e-07)


def wide_kernel(
    end_hbm,
    tab_hbm,
    mid_hbm,
    m1_hbm,
    m2_hbm,
    sum_hbm,
    otab_hbm,
    orth_hbm,
    xs,
    x,
    m1,
    m2,
    xc,
    tbuf,
    tland,
    load_sem,
    tsend,
    trecv,
    tout,
    buf,
    own_sem,
    *work,
):
    links = Links()
    core = links.core
    reduce = Reduce(links, end_hbm, buf, work[:5])
    gather = Gather(links, work[0], sum_hbm, work[5:])
    own = pltpu.make_async_copy(end_hbm.at[core], buf, own_sem)
    own.start()
    wide = m1.shape[1]
    blocks = wide // D
    trows = tbuf.shape[0]
    near = pl.ds(pl.multiple_of(core * trows, 8), trows)
    far = pl.ds(pl.multiple_of((1 - core) * trows, 8), trows)
    pairs = ((mid_hbm.at[core], x), (m1_hbm, m1), (m2_hbm, m2), (tab_hbm.at[near], tbuf))
    loads = [pltpu.make_async_copy(a, b, load_sem.at[i]) for i, (a, b) in enumerate(pairs)]
    for load in loads:
        load.start()
    links.greet()
    reduce.begin()
    top = links.bits

    def table(n):
        if n == top:
            return remote(tab_hbm.at[far], tland.at[n], tsend.at[n], trecv.at[n], links.twin)
        return remote(tbuf, tland.at[n], tsend.at[n], trecv.at[n], links.there[n])

    def table_land(n):
        table(n).wait()
        tbuf[...] += tland[n]

    def down(s, some):
        reduce.down(s, some)
        if some is EARLY:
            table_land(s)
            if s < 3:
                table(s + 1).start()
        elif s == 3:
            for b in range(4, links.bits):
                table(b).start()
                table_land(b)
            for copy in touts:
                copy.start()
        if s == 3:
            for p in some:
                lanes = gather.lanes(p)
                gather.whole[gather.held(p, 4), lanes] = buf[gather.held(p, 4), lanes]
            gather.begin(some)

    touts = [
        pltpu.make_async_copy(tbuf, otab_hbm.at[near], tout.at[0]),
        remote(tbuf, otab_hbm.at[near], tout.at[1], tout.at[2], links.twin),
    ]

    table(top).start()
    for load in loads:
        load.wait()
    own.wait()
    table_land(top)
    reduce.join(EARLY)
    table(0).start()

    @pl.when(core == 0)
    def _():
        x[...] = MUON_KEEP * m1[...] + x[...]

    @pl.when(core == 1)
    def _():
        for b in range(blocks):
            lanes = slice(b * D, b * D + D)
            x[:, lanes] = MUON_KEEP * m2[lanes].T + x[:, lanes]

    reduce.join(LATE)
    inv = inverse_norm(x[...])
    chunks = [slice(o, o + 2 * PIECE) for o in range(0, wide, 2 * PIECE)]

    def keep(lanes, v):
        h, l = halves(v)
        xc[0:D, lanes] = h
        xc[D : 2 * D, lanes] = h
        xc[2 * D : 3 * D, lanes] = l

    def kept(lanes):
        return xc[0:D, lanes].astype(F32) + xc[2 * D : 3 * D, lanes].astype(F32)

    for lanes in chunks:
        keep(lanes, x[:, lanes] * inv)

    def gram():
        h, l = xc[0:D], xc[2 * D : 3 * D]
        return dot_nt(h, h) + (dot_nt(l, h) + dot_nt(h, l))

    def two_steps(events):
        g0 = gram()
        g = halves(g0)
        events(0)
        p0 = NS_B * g0 + NS_C * times(g, g)
        p = halves(p0)
        t = NS_A * g0 + times(p, g)
        events(1)
        g1 = NS_A * t + times(halves(t), p)
        g = halves(g1)
        p1 = NS_B * g1 + NS_C * times(g, g)
        events(2)
        both = side(NS_A * (p0 + p1) + times(halves(p1), p))
        for lanes in chunks:
            keep(lanes, NS_A * NS_A * kept(lanes) + dot_nn(both, xc[:, lanes]))
        events(3)

    def first(n):
        if n == 0:
            down(0, LATE)
        if n == 1:
            down(1, EARLY)
        if n == 2:
            down(1, LATE)
            down(2, EARLY)
        if n == 3:
            down(2, LATE)

    def second(n):
        if n == 0:
            down(3, EARLY)
        if n == 1:
            down(3, LATE)
        if n == 2:
            gather.up(3, EARLY)
        if n == 3:
            gather.up(3, LATE)
            gather.up(2, EARLY)

    down(0, EARLY)
    two_steps(first)
    two_steps(second)
    g0 = gram()
    g = halves(g0)
    gather.up(2, LATE)
    last = side(NS_B * g0 + NS_C * times(g, g))
    for lanes in chunks:
        x[:, lanes] = NS_A * kept(lanes) + dot_nn(last, xc[:, lanes])
    gather.up(1, EARLY)

    @pl.when(core == 0)
    def _():
        for b in range(blocks):
            xs[b] = x[:, b * D : b * D + D]

    @pl.when(core == 1)
    def _():
        for b in range(blocks):
            xs[b] = x[:, b * D : b * D + D].T

    orth = [
        pltpu.make_async_copy(xs, orth_hbm.at[core], tout.at[3]),
        remote(xs, orth_hbm.at[core], tout.at[4], tout.at[5], links.twin),
    ]
    for copy in orth:
        copy.start()
    gather.up(1, LATE)
    gather.up(0, EARLY)
    gather.up(0, LATE)
    gather.end()
    for copy in touts + orth:
        copy.wait()


def wide_blocks(end, tab, mid, m1, m2):
    bits = (lax.axis_size("canvas") - 1).bit_length()
    anywhere = pl.BlockSpec(memory_space=pl.ANY)
    blocks = m1.shape[1] // D
    return pl.pallas_call(
        wide_kernel,
        out_shape=[
            jax.ShapeDtypeStruct(end.shape, F32),
            jax.ShapeDtypeStruct((TABLE, D), F32),
            jax.ShapeDtypeStruct((2, blocks, D, D), F32),
        ],
        in_specs=[anywhere] * 5,
        out_specs=[anywhere] * 3,
        scratch_shapes=[
            pltpu.VMEM((blocks, D, D), F32),
            pltpu.VMEM(m1.shape, F32),
            pltpu.VMEM(m1.shape, F32),
            pltpu.VMEM(m2.shape, F32),
            pltpu.VMEM((3 * D, m1.shape[1]), BF),
            pltpu.VMEM((TABLE // 2, D), F32),
            pltpu.VMEM((bits + 1, TABLE // 2, D), F32),
            DMA((4,)),
            DMA((bits + 1,)),
            DMA((bits + 1,)),
            DMA((6,)),
            pltpu.VMEM(end.shape[1:], F32),
            DMA,
        ]
        + Reduce.scratch(end.shape[2], bits)
        + Gather.scratch(end.shape[2]),
        compiler_params=pltpu.CompilerParams(
            collective_id=2, has_side_effects=True, vmem_limit_bytes=60 << 20
        ),
    )(end, tab, mid, m1, m2)


def muon(w, orth, large):
    return w * (1.0 - MUON_RATE * DECAY) - MUON_RATE * 0.2 * math.sqrt(large) * orth


def square_kernel(
    end_hbm,
    mid_hbm,
    wide_hbm,
    mq_hbm,
    mp_hbm,
    m1_hbm,
    m2_hbm,
    w1_hbm,
    w2_hbm,
    out_hbm,
    dx_hbm,
    gq_out,
    gp_out,
    g1_out,
    g2_out,
    nq_out,
    np_out,
    n1_out,
    n2_out,
    w1_out,
    w2_out,
    c1_out,
    c2_out,
    out_out,
    dx_out,
    orth_hbm,
    end,
    mid,
    nat,
    mq,
    mp,
    m1,
    m2,
    w1,
    w2,
    c1,
    c2,
    wide,
    out,
    dx,
    xh,
    xl,
    xs,
    in_sem,
    out_sem,
):
    core = lax.axis_index("rows")
    mlp = m1.shape[1]
    blocks = mlp // D
    pairs = (
        (end_hbm, end),
        (mq_hbm, mq),
        (mp_hbm, mp),
        (mid_hbm, mid),
        (m1_hbm, m1),
        (m2_hbm, m2),
        (w1_hbm, w1),
        (w2_hbm, w2),
        (wide_hbm, wide),
        (out_hbm, out),
        (dx_hbm, dx),
    )
    loads = [pltpu.make_async_copy(a, b, in_sem.at[i]) for i, (a, b) in enumerate(pairs)]
    for load in loads:
        load.start()
    for load in loads[0:3]:
        load.wait()
    outs = (
        (end.at[0], gq_out.at[:, 0 : 2 * D]),
        (end.at[1, :, 0:D], gq_out.at[:, 2 * D : 3 * D]),
        (end.at[1, :, D : 2 * D], gp_out),
        (mq, nq_out),
        (mp, np_out),
        (mid.at[0], g1_out),
        (nat, g2_out),
        (m1, n1_out),
        (m2, n2_out),
        (out, out_out),
        (dx, dx_out),
        (w1, w1_out),
        (w2, w2_out),
        (c1, c1_out),
        (c2, c2_out),
        (xs, orth_hbm),
    )

    def store(*which):
        return [pltpu.make_async_copy(*outs[n], out_sem.at[n]) for n in which]

    def send(*which):
        for copy in store(*which):
            copy.start()

    send(0, 1, 2)

    def small(o):
        rows = pl.ds(o, 128)
        mq[rows, 0 : 2 * D] = MUON_KEEP * mq[rows, 0 : 2 * D] + end[0, rows]
        mq[rows, 2 * D : 3 * D] = MUON_KEEP * mq[rows, 2 * D : 3 * D] + end[1, rows, 0:D]
        mp[rows] = MUON_KEEP * mp[rows] + end[1, rows, D : 2 * D]

    sweep(D, 128, small)
    send(3, 4)

    def keep(b, v):
        xh[b], xl[b] = halves(v)

    @pl.when(core == 0)
    def _():
        xs[0] = mq[:, 0:D]
        xs[1] = mq[:, D : 2 * D]

    @pl.when(core == 1)
    def _():
        xs[0] = mq[:, 2 * D : 3 * D]
        xs[1] = mp[...]

    for b in range(2):
        keep(b, xs[b] * inverse_norm(xs[b]))

    def step(i, carry):
        x = [(xh[b], xl[b]) for b in range(2)]
        g = [
            dot_nt(jnp.concatenate([h, l, h], axis=1), jnp.concatenate([h, h, l], axis=1))
            for h, l in x
        ]
        pairs = [halves(v) for v in g]
        p = [NS_B * v + NS_C * times(w, w) for v, w in zip(g, pairs)]
        pairs = [halves(v) for v in p]
        for b in range(2):
            h, l = x[b]
            keep(b, NS_A * (h.astype(F32) + l.astype(F32)) + times(pairs[b], x[b]))
        pl.when(i == 1)(moments)
        pl.when(i == 2)(weights)
        return carry

    def moments():
        for load in loads[3:6]:
            load.wait()
        send(5)
        for b in range(blocks):
            nat[b * D : b * D + D] = mid[1, :, b * D : b * D + D].T
        send(6)

        def large(o):
            rows = pl.ds(o, 64)
            m1[rows] = MUON_KEEP * m1[rows] + mid[0, rows]

        sweep(D, 64, large)
        send(7)

        def larger(o):
            rows = pl.ds(o, 256)
            m2[rows] = MUON_KEEP * m2[rows] + nat[rows]

        sweep(mlp, 256, larger)
        send(8)

    def weights():
        for load in loads[6:]:
            load.wait()
        send(9, 10)
        for b in range(blocks):
            at = slice(b * D, b * D + D)
            new = muon(w1[:, at], wide[0, b], mlp)
            w1[:, at] = new
            c1[:, at] = new.astype(BF)
            new = muon(w2[at], wide[1, b], mlp)
            w2[at] = new
            c2[at] = new.astype(BF)
        send(11, 12, 13, 14)

    lax.fori_loop(0, 5, step, 0)
    for b in range(2):
        xs[b] = xh[b].astype(F32) + xl[b].astype(F32)
    send(15)
    for copy in store(*range(len(outs))):
        copy.wait()


def square_blocks(end, mid, wide, mq, mp, m1, m2, w1, w2, out, dx):
    anywhere = pl.BlockSpec(memory_space=pl.ANY)

    def like(v, kind=F32):
        return jax.ShapeDtypeStruct(v.shape, kind)

    def room(v, kind=F32):
        return pltpu.VMEM(v.shape, kind)

    return pl.pallas_call(
        square_kernel,
        out_shape=[like(v) for v in (mq, mp, m1, m2, mq, mp, m1, m2, w1, w2)]
        + [like(w1, BF), like(w2, BF), like(out), like(dx), jax.ShapeDtypeStruct((2, D, D), F32)],
        in_specs=[anywhere] * 11,
        out_specs=[anywhere] * 15,
        scratch_shapes=[room(v) for v in (end, mid, m2, mq, mp, m1, m2, w1, w2)]
        + [room(w1, BF), room(w2, BF), room(wide), room(out), room(dx)]
        + [
            pltpu.VMEM((2, D, D), BF),
            pltpu.VMEM((2, D, D), BF),
            pltpu.VMEM((2, D, D), F32),
            DMA((11,)),
            DMA((16,)),
        ],
        compiler_params=pltpu.CompilerParams(vmem_limit_bytes=60 << 20),
    )(end, mid, wide, mq, mp, m1, m2, w1, w2, out, dx)


def trade_kernel(own_ref, peer_ref, send_sem, recv_sem):
    core = lax.axis_index("rows")
    twin = {"rows": 1 - core}
    barrier = pltpu.get_barrier_semaphore()
    pl.semaphore_signal(barrier, inc=1, device_id=twin, device_id_type=MESH_ID)
    pl.semaphore_wait(barrier, 1)
    copy = remote(own_ref, peer_ref, send_sem, recv_sem, twin)
    copy.start()
    copy.wait()


def trade(own):
    anywhere = pl.BlockSpec(memory_space=pl.ANY)
    return pl.pallas_call(
        trade_kernel,
        out_shape=jax.ShapeDtypeStruct(own.shape, F32),
        in_specs=[anywhere],
        out_specs=anywhere,
        scratch_shapes=[DMA, DMA],
        compiler_params=pltpu.CompilerParams(collective_id=3, has_side_effects=True),
    )(own)


def moment_step(current, one, two, gradient):
    first = BETA1 * one + (1.0 - BETA1) * gradient
    second = BETA2 * two + (1.0 - BETA2) * gradient * gradient
    fix_one = 1.0 - BETA1**STEP
    fix_two = 1.0 - BETA2**STEP
    updated = current - ADAM_RATE * (first / fix_one) / (jnp.sqrt(second / fix_two) + ADAM_FLOOR)
    return first, second, updated


def update_kernel(
    own_ref,
    peer_ref,
    wq_ref,
    wp_ref,
    tab_ref,
    one_ref,
    two_ref,
    gtab_ref,
    nq_ref,
    np_ref,
    cq_ref,
    cp_ref,
    first_ref,
    second_ref,
    small_ref,
):
    lower = lax.axis_index("rows") == 0
    own, peer = own_ref[...], peer_ref[...]
    low, high = jnp.where(lower, own, peer), jnp.where(lower, peer, own)
    for i, orth in enumerate((low[0], low[1], high[0])):
        lanes = slice(i * D, i * D + D)
        new = muon(wq_ref[:, lanes], orth, D)
        nq_ref[:, lanes] = new
        cq_ref[:, lanes] = new.astype(BF)
    new = muon(wp_ref[...], high[1], D)
    np_ref[...] = new
    cp_ref[...] = new.astype(BF)
    first, second, small = moment_step(tab_ref[...], one_ref[...], two_ref[...], gtab_ref[0:SMALL])
    first_ref[...] = first
    second_ref[...] = second
    small_ref[...] = small


def update(own, peer, wq, wp, tab, one, two, gtab):
    steps = 3
    piece = D // steps

    def rows(v):
        return pl.BlockSpec((piece, v.shape[1]), lambda i: (i, 0))

    def whole(v):
        return pl.BlockSpec(v.shape, lambda i: (0, 0))

    square = pl.BlockSpec((2, piece, D), lambda i: (0, i, 0))
    weights = (wq, wp)
    return pl.pallas_call(
        update_kernel,
        grid=(steps,),
        out_shape=[jax.ShapeDtypeStruct(w.shape, F32) for w in weights]
        + [jax.ShapeDtypeStruct(w.shape, BF) for w in weights]
        + [jax.ShapeDtypeStruct(tab.shape, F32)] * 3,
        in_specs=[square, square]
        + [rows(w) for w in weights]
        + [whole(v) for v in (tab, one, two, gtab)],
        out_specs=[rows(w) for w in weights] * 2 + [whole(tab)] * 3,
        compiler_params=pltpu.CompilerParams(vmem_limit_bytes=60 << 20),
    )(own, peer, *weights, tab, one, two, gtab)


def on_device(
    x4, dy4, tall, wqkv, wp, w1, w2, mqkv, mp, m1, m2, tab, tab_one, tab_two, temp, temp_one, temp_two
):
    shape = x4.shape
    tokens = shape[1] * shape[2]
    x = x4.reshape(tokens, D)
    dy = dy4.reshape(tokens, D)
    q, k, v, sums = project(tall, x, wqkv, tab)
    out, ds1, dmx, dwp, shard, gtab, probs, unit, gprob, joint = middle(
        tall, temp, x, dy, v, sums, wp, w1, w2, tab
    )
    dx, end, gtab, mid = finish(
        tall, temp, x, q, k, ds1, dmx, sums, joint, probs, unit, gprob, wqkv, tab, gtab, dwp, shard
    )
    end, gtab, wide = wide_blocks(end, gtab, mid, m1, m2)
    *grads, new_1, new_2, copy_1, copy_2, out, dx, square = square_blocks(
        end, mid, wide, mqkv, mp, m1, m2, w1, w2, out, dx
    )
    new_q, new_p, copy_q, copy_p, *small = update(
        square, trade(square), wqkv, wp, tab, tab_one, tab_two, gtab
    )
    results = (new_q, new_p, new_1, new_2, copy_q, copy_p, copy_1, copy_2, *small)
    heat = jnp.sum(gtab[44].reshape(HEADS, HD), axis=1)
    warm = moment_step(temp, temp_one, temp_two, heat)
    count = tokens * D * lax.axis_size("rows") * lax.axis_size("canvas")
    rms = jnp.sqrt(jnp.sum(gtab[40:44], axis=1) / count)
    return (out.reshape(shape), dx.reshape(shape), *grads, *results, *warm, rms)


def solution(mesh):
    split = P("canvas", "rows", None, None)
    return jax.shard_map(
        on_device,
        mesh=mesh,
        in_specs=(split, split, P("canvas", None)) + (P(),) * 14,
        out_specs=(split, split) + (P(),) * 23,
        check_vma=False,
    )
```

```python
import functools
import math

import jax
import jax.numpy as jnp
from jax import lax
from jax.experimental import pallas as pl
from jax.experimental.pallas import tpu as pltpu
from jax.sharding import PartitionSpec as P

BF = jnp.bfloat16
F32 = jnp.float32
MESH_ID = pl.DeviceIdType.MESH

EPS = 1e-06
ROOT_HALF = 1.0 / math.sqrt(2.0)
ROOT_TWOPI = 1.0 / math.sqrt(2.0 * math.pi)
STEP = 10
MUON_RATE = 0.2
MUON_KEEP = 0.95
DECAY = 0.01
ADAM_RATE = 0.2
BETA1 = 0.9
BETA2 = 0.95
ADAM_FLOOR = 1e-08

HEADS = 8
HD = 48
D = HEADS * HD
COLS = 32
HALO = 4 * COLS
TILE = 256

N1G, N1S, N3G, N3S, N2G, N2S, SA, SL, SM, QB, KB, VB, PB, C1B, BG, BS, C2B, F2B = range(18)
F1B, K1R, K2R = 18, 22, 31
SMALL = 40
TABLE = 48


def halves(v):
    hi = v.astype(BF)
    return hi, (v - hi.astype(F32)).astype(BF)


def side(v):
    h, l = halves(v)
    return jnp.concatenate([h, l, h], axis=1)


def dot_nn(a, b):
    return lax.dot_general(a, b, (((1,), (0,)), ((), ())), preferred_element_type=F32)


def dot_nt(a, b):
    return lax.dot_general(a, b, (((1,), (1,)), ((), ())), preferred_element_type=F32)


def normalize(v):
    mean = jnp.mean(v, axis=1, keepdims=True)
    c = v - mean
    r = lax.rsqrt(jnp.mean(c * c, axis=1, keepdims=True) + EPS)
    return c * r, r


def normalize_back(e, xhat, r):
    return r * (
        e - jnp.mean(e, axis=1, keepdims=True) - xhat * jnp.mean(e * xhat, axis=1, keepdims=True)
    )


def gelu_parts(v):
    phi = 0.5 * (1.0 + lax.erf(v * ROOT_HALF))
    return v * phi, phi + v * jnp.exp(-0.5 * v * v) * ROOT_TWOPI


def eights(v):
    total = v[0:8]
    for i in range(8, v.shape[0], 8):
        total = total + v[i : i + 8]
    return total


def sweep(count, size, body):
    def one(i, carry):
        body(pl.multiple_of(i * size, size))
        return carry

    lax.fori_loop(0, count // size, one, 0)


def image_ends(tall_ref):
    e0 = tall_ref[0, 0]
    e1 = e0 + tall_ref[0, 1]
    return e0, e1, e1 + tall_ref[0, 2]


def slots(tall_ref, core, first_row, rows_all):
    e0, e1, e2 = image_ends(tall_ref)
    low = (jnp.where(core == 0, 0, e2), jnp.where(core == 0, e0, 0), e1)
    high = (jnp.where(core == 0, e0, rows_all), jnp.where(core == 0, e1, 0), e2)
    return [((a - first_row) * COLS, (b - first_row) * COLS) for a, b in zip(low, high)]


def span_mask(start, rows, lo, hi):
    token = start + lax.broadcasted_iota(jnp.int32, (rows, D), 0)
    return (token >= lo) & (token < hi)


def slot_masks(start, rows, spans):
    return [jnp.where(span_mask(start, rows, lo, hi), 1.0, 0.0).astype(BF) for lo, hi in spans]


def by_slot(v, masks):
    h, l = halves(v)
    parts = []
    for mask in masks:
        hm = h * mask
        parts += [hm, l * mask, hm]
    return jnp.concatenate(parts, axis=1)


def slots_below(v, masks):
    h, l = halves(v)
    high = jnp.concatenate([h * mask for mask in masks], axis=1)
    return jnp.concatenate([high, high, jnp.concatenate([l * mask for mask in masks], axis=1)], axis=0)


def lane_head():
    return lax.broadcasted_iota(jnp.int32, (HD, D), 1) // HD


def lane_slot():
    return lax.broadcasted_iota(jnp.int32, (HD, D), 1) % HD


def fold(full):
    head = lane_head()
    total = jnp.where(head == 0, full[0:HD], 0.0)
    for h in range(1, HEADS):
        total = total + jnp.where(head == h, full[h * HD : h * HD + HD], 0.0)
    return total


def unfold(small):
    head = lane_head()
    return jnp.concatenate([jnp.where(head == h, small, 0.0) for h in range(HEADS)], axis=0)


def group_ones():
    a = lax.broadcasted_iota(jnp.int32, (D, D), 0) // HD
    b = lax.broadcasted_iota(jnp.int32, (D, D), 1) // HD
    return jnp.where(a == b, 1.0, 0.0).astype(BF)


def group_sum(v, ones):
    h = v.astype(BF)
    rest = v - h.astype(F32)
    m = rest.astype(BF)
    l = (rest - m.astype(F32)).astype(BF)
    return dot_nn(h, ones) + (dot_nn(m, ones) + dot_nn(l, ones))


def row_to_fold(row, ones):
    slot = lax.broadcasted_iota(jnp.int32, (HD, D), 0)
    return group_sum(jnp.where(lane_slot() == slot, jnp.broadcast_to(row, (HD, D)), 0.0), ones)


def fold_to_row(small):
    slot = lax.broadcasted_iota(jnp.int32, (HD, D), 0)
    return jnp.sum(jnp.where(lane_slot() == slot, small, 0.0), axis=0, keepdims=True)


def head_row(temp_ref):
    head = lax.broadcasted_iota(jnp.int32, (1, D), 1) // HD
    row = jnp.where(head == 0, temp_ref[0], 0.0)
    for h in range(1, HEADS):
        row = row + jnp.where(head == h, temp_ref[h], 0.0)
    return row


def project_kernel(tall_ref, x_ref, w_ref, tab_ref, q_ref, k_ref, v_ref, sums_ref, wcat, cross):
    step = pl.program_id(0)
    core = lax.axis_index("rows")
    rows_all = 2 * pl.num_programs(0) * TILE // COLS
    spans = slots(tall_ref, core, core * (rows_all // 2), rows_all)
    start = step * TILE

    @pl.when(step == 0)
    def _():
        def part(o):
            h, l = halves(w_ref[pl.ds(o, 64)])
            wcat[pl.ds(o, 64)] = h
            wcat[pl.ds(D + o, 64)] = h
            wcat[pl.ds(2 * D + o, 64)] = l

        sweep(D, 64, part)
        cross[...] = jnp.zeros_like(cross)
        sums_ref[...] = jnp.zeros_like(sums_ref)

    xhat, _ = normalize(x_ref[...])
    lhs = side(xhat * tab_ref[N1G : N1G + 1] + tab_ref[N1S : N1S + 1])
    q = dot_nn(lhs, wcat[:, 0:D]) + tab_ref[QB : QB + 1]
    q_ref[...] = q
    k = dot_nn(lhs, wcat[:, D : 2 * D]) + tab_ref[KB : KB + 1]
    k_ref[...] = k
    v_ref[...] = dot_nn(lhs, wcat[:, 2 * D : 3 * D]) + tab_ref[VB : VB + 1]
    cross[...] += dot_nn(side(q.T), slots_below(k, slot_masks(start, TILE, spans)))
    for s, (lo, hi) in enumerate(spans):
        mask = span_mask(start, TILE, lo, hi)
        for n, v in enumerate((q, k)):
            row = HD + n
            sums_ref[s, row : row + 1] += jnp.sum(jnp.where(mask, v * v, 0.0), axis=0, keepdims=True)

    @pl.when(step == pl.num_programs(0) - 1)
    def _():
        for s in range(3):
            sums_ref[s, 0:HD] = fold(cross[:, s * D : s * D + D])


def project(tall, x, w, tab):
    tokens = x.shape[0]
    row = pl.BlockSpec((TILE, D), lambda i: (i, 0))
    return pl.pallas_call(
        project_kernel,
        grid=(tokens // TILE,),
        out_shape=[jax.ShapeDtypeStruct((tokens, D), F32)] * 3
        + [jax.ShapeDtypeStruct((3, HD + 8, D), F32)],
        in_specs=[
            pl.BlockSpec(memory_space=pltpu.SMEM),
            row,
            pl.BlockSpec((D, 3 * D), lambda i: (0, 0)),
            pl.BlockSpec((SMALL, D), lambda i: (0, 0)),
        ],
        out_specs=[row, row, row, pl.BlockSpec((3, HD + 8, D), lambda i: (0, 0, 0))],
        scratch_shapes=[pltpu.VMEM((3 * D, 3 * D), BF), pltpu.VMEM((D, 3 * D), F32)],
        compiler_params=pltpu.CompilerParams(vmem_limit_bytes=60 << 20),
    )(tall, x, w, tab)


ORDERS = ((0, 1, 2, 3), (1, 2, 0, 3), (2, 0, 1, 3))
EARLY, LATE = range(0, 3), range(3, 6)
PIECE = 256
SHARD = D // 16
DMA = pltpu.SemaphoreType.DMA


class Links:
    def __init__(self):
        self.core = lax.axis_index("rows")
        chip = lax.axis_index("canvas")
        self.bits = (lax.axis_size("canvas") - 1).bit_length()
        self.mine = [lax.rem(lax.div(chip, 1 << b), 2) for b in range(self.bits)]
        self.there = [{"canvas": chip + (1 - 2 * m) * (1 << b)} for b, m in enumerate(self.mine)]
        self.twin = {"rows": 1 - self.core}

    def call(self):
        barrier = pltpu.get_barrier_semaphore()
        for other in [self.twin] + self.there:
            pl.semaphore_signal(barrier, inc=1, device_id=other, device_id_type=MESH_ID)

    def answer(self):
        pl.semaphore_wait(pltpu.get_barrier_semaphore(), self.bits + 1)

    def greet(self):
        self.call()
        self.answer()


def remote(src, dst, send, recv, other):
    return pltpu.make_async_remote_copy(
        src_ref=src,
        dst_ref=dst,
        send_sem=send,
        recv_sem=recv,
        device_id=other,
        device_id_type=MESH_ID,
    )


class Pieces:
    count = 6

    def __init__(self, links, lanes):
        self.links = links
        self.width = lanes // self.count

    def lanes(self, p):
        return slice(p * self.width, p * self.width + self.width)

    def bit(self, p, s):
        return ORDERS[p % 3][s]

    def start(self, p, s):
        at = 0
        for t in range(s):
            at = at + self.links.mine[self.bit(p, t)] * (D >> (t + 1))
        return at

    def held(self, p, s):
        return pl.ds(pl.multiple_of(self.start(p, s), 8), D >> s)


class Reduce(Pieces):
    def __init__(self, links, src, buf, work):
        super().__init__(links, src.shape[-1])
        self.src, self.buf = src, buf
        self.first, self.land, self.pair_sem, self.send_sem, self.recv_sem = work

    @classmethod
    def scratch(cls, lanes, bits):
        steps = max(bits, 4)
        return [
            pltpu.VMEM((D, lanes), F32),
            pltpu.VMEM((D - SHARD + (steps - 4) * SHARD, lanes), F32),
            DMA((2, cls.count)),
            DMA((cls.count, steps)),
            DMA((cls.count, steps)),
        ]

    def add(self, p, rows, src, src_rows):
        lanes = self.lanes(p)
        self.buf[rows, lanes] += src[src_rows, lanes]

    def pair(self, p):
        lanes = self.lanes(p)
        return remote(
            self.src.at[1 - self.links.core, :, lanes],
            self.first.at[:, lanes],
            self.pair_sem.at[0, p],
            self.pair_sem.at[1, p],
            self.links.twin,
        )

    def move(self, p, s):
        b = self.bit(p, s)
        half = D >> (s + 1)
        away = pl.multiple_of(self.start(p, s) + (1 - self.links.mine[b]) * half, 8)
        lanes = self.lanes(p)
        return remote(
            self.buf.at[pl.ds(away, half), lanes],
            self.land.at[pl.ds(D - (D >> s), half), lanes],
            self.send_sem.at[p, s],
            self.recv_sem.at[p, s],
            self.links.there[b],
        )

    def begin(self):
        for p in range(self.count):
            self.pair(p).start()

    def join(self, some):
        for p in some:
            self.pair(p).wait()
            self.add(p, pl.ds(0, D), self.first, pl.ds(0, D))
            self.move(p, 0).start()

    def launch(self):
        for p in range(self.count):
            self.move(p, 0).start()

    def down(self, s, some, last=3):
        for p in some:
            self.move(p, s).wait()
            self.add(p, self.held(p, s + 1), self.land, pl.ds(D - (D >> s), D >> (s + 1)))
            if s < last:
                self.move(p, s + 1).start()
        if s == 3:
            for b in range(4, self.links.bits):
                self.swap(b, some)

    def swap(self, b, some):
        at = pl.ds(D - SHARD + (b - 4) * SHARD, SHARD)
        copies = {}
        for p in some:
            lanes = self.lanes(p)
            copies[p] = remote(
                self.buf.at[self.held(p, 4), lanes],
                self.land.at[at, lanes],
                self.send_sem.at[p, b],
                self.recv_sem.at[p, b],
                self.links.there[b],
            )
            copies[p].start()
        for p in some:
            copies[p].wait()
            self.add(p, self.held(p, 4), self.land, at)


class Gather(Pieces):
    def __init__(self, links, whole, dst, work):
        super().__init__(links, whole.shape[1])
        self.whole, self.dst = whole, dst
        self.send_sem, self.recv_sem, self.out_sem = work

    @classmethod
    def scratch(cls, lanes):
        return [DMA((cls.count, 4)), DMA((cls.count, 4)), DMA((2, 3, cls.count))]

    def back(self, p, s):
        view = self.whole.at[self.held(p, s + 1), self.lanes(p)]
        return remote(
            view,
            view,
            self.send_sem.at[p, s],
            self.recv_sem.at[p, s],
            self.links.there[self.bit(p, s)],
        )

    def outs(self, p, n):
        mine = self.links.mine[self.bit(p, 0)]
        half = D // 2
        at = pl.multiple_of(half * (mine if n == 0 else 1 - mine), 8)
        rows = pl.ds(at, half)
        src = self.whole.at[rows, self.lanes(p)]
        dst = self.dst.at[self.links.core, rows, self.lanes(p)]
        sem = self.out_sem.at[n]
        return (
            pltpu.make_async_copy(src, dst, sem.at[0, p]),
            remote(src, dst, sem.at[1, p], sem.at[2, p], self.links.twin),
        )

    def begin(self, some):
        for p in some:
            self.back(p, 3).start()

    def up(self, s, some):
        for p in some:
            self.back(p, s).wait()
            if s > 0:
                self.back(p, s - 1).start()
            if s < 2:
                for copy in self.outs(p, 1 - s):
                    copy.start()

    def end(self):
        for n in range(2):
            for p in range(self.count):
                for copy in self.outs(p, n):
                    copy.wait()


class Turn(Pieces):
    def __init__(self, links, rest, whole, work):
        super().__init__(links, whole.shape[1])
        self.rest, self.whole = rest, whole
        self.land, self.send_sem, self.recv_sem = work

    @classmethod
    def scratch(cls, lanes, bits):
        steps = max(bits, 4) - 3
        return [
            pltpu.VMEM((steps * SHARD, lanes), F32),
            DMA((cls.count, steps)),
            DMA((cls.count, steps)),
        ]

    def move(self, p, n):
        lanes = self.lanes(p)
        if n == 0:
            b = self.bit(p, 3)
            at = pl.multiple_of((1 - self.links.mine[b]) * SHARD, 8)
            src = self.rest.at[pl.ds(at, SHARD), lanes]
        else:
            b = 3 + n
            src = self.whole.at[self.held(p, 4), lanes]
        return remote(
            src,
            self.land.at[n * SHARD : n * SHARD + SHARD, lanes],
            self.send_sem.at[p, n],
            self.recv_sem.at[p, n],
            self.links.there[b],
        )

    def begin(self):
        for p in range(self.count):
            self.move(p, 0).start()

    def end(self, some):
        for p in some:
            lanes = self.lanes(p)
            at = pl.multiple_of(self.links.mine[self.bit(p, 3)] * SHARD, 8)
            self.move(p, 0).wait()
            self.whole[self.held(p, 4), lanes] = (
                self.rest[pl.ds(at, SHARD), lanes] + self.land[0:SHARD, lanes]
            )
        for n in range(1, self.links.bits - 3):
            for p in some:
                self.move(p, n).start()
            for p in some:
                lanes = self.lanes(p)
                self.move(p, n).wait()
                self.whole[self.held(p, 4), lanes] += self.land[n * SHARD : n * SHARD + SHARD, lanes]


def row_flags(tall_ref, rows_all):
    ends = image_ends(tall_ref)

    def above(row):
        first = (row == 0) | (row == ends[0]) | (row == ends[1]) | (row == ends[2])
        return jnp.where(first, 0.0, 1.0)

    def below(row):
        return jnp.where(row + 1 == rows_all, 0.0, above(row + 1))

    return above, below


def middle_kernel(
    tall_ref,
    temp_ref,
    x_hbm,
    dy_hbm,
    v_hbm,
    sums_ref,
    wp_ref,
    w1_hbm,
    w2_ref,
    tab_ref,
    out_hbm,
    ds1_hbm,
    dmx_hbm,
    dwp_ref,
    shard_ref,
    gtab_ref,
    probs_ref,
    unit_ref,
    gprob_ref,
    joint_ref,
    wpv,
    wph,
    w1c,
    w2c,
    pcat,
    mixed,
    s1,
    li,
    act,
    slope,
    mid,
    s2,
    ds2,
    gp,
    n2c,
    dzc,
    b1_ref,
    b1g_ref,
    acc,
    cross,
    x_ref,
    dy_ref,
    v_ref,
    flags,
    nt,
    dt,
    peer_ref,
    dw_ref,
    load_sem,
    store_sem,
    edge_sem,
    *work,
):
    links = Links()
    core = links.core
    wide = x_ref.shape[0]
    tokens = wide - HALO
    dw1_ref, dw2_ref = dw_ref.at[0], dw_ref.at[1]
    reduce = Reduce(links, dw_ref, dw_ref.at[core], work)
    w1_ref = work[0]
    lo_ = x_ref
    own = pl.ds(pl.multiple_of(core * HALO, HALO), tokens)
    pairs = ((w1_hbm, w1_ref), (v_hbm, v_ref.at[own]), (x_hbm, x_ref.at[own]), (dy_hbm, dy_ref.at[own]))
    loads = [pltpu.make_async_copy(a, b, load_sem.at[i]) for i, (a, b) in enumerate(pairs)]
    for load in loads:
        load.start()
    links.call()
    edge = pl.ds(pl.multiple_of((1 - core) * (tokens - HALO), HALO), HALO)
    far = pl.ds(pl.multiple_of(core * tokens, HALO), HALO)
    pairs = (
        (sums_ref.at[2], peer_ref),
        (v_hbm.at[edge], v_ref.at[far]),
        (x_hbm.at[edge], x_ref.at[far]),
        (dy_hbm.at[edge], dy_ref.at[far]),
    )
    edges = [
        remote(a, b, edge_sem.at[0, i], edge_sem.at[1, i], links.twin)
        for i, (a, b) in enumerate(pairs)
    ]
    own_rows = tokens // COLS
    rows_wide = wide // COLS
    rows_all = 2 * own_rows
    first_row = core * (own_rows - HALO // COLS)
    own_off = pl.multiple_of(core * HALO, HALO)
    mlp = w1_hbm.shape[1]
    spans = slots(tall_ref, core, first_row, rows_all)
    above, below = row_flags(tall_ref, rows_all)

    def tab(r):
        return tab_ref[r : r + 1]

    def is_own(row):
        return (row >= core * (HALO // COLS)) & (row < core * (HALO // COLS) + own_rows)

    loads[0].wait()

    def part_1(o):
        rows = pl.ds(o, 64)
        h, l = halves(w1_ref[rows])
        w1c[rows] = h
        w1c[pl.ds(D + o, 64)] = h
        w1c[pl.ds(2 * D + o, 64)] = l

    sweep(D, 64, part_1)
    links.answer()
    for copy in edges:
        copy.start()

    def part_p(o):
        rows = pl.ds(o, 192)
        h, l = halves(wp_ref[rows])
        wpv[rows] = h
        wpv[pl.ds(D + o, 192)] = h
        wpv[pl.ds(2 * D + o, 192)] = l
        wph[rows, 0:D] = h
        wph[rows, D : 2 * D] = h
        wph[rows, 2 * D : 3 * D] = l

    sweep(D, 192, part_p)

    def part_2(o):
        rows = pl.ds(o, 256)
        h, l = halves(w2_ref[rows])
        w2c[rows, 0:D] = h
        w2c[rows, D : 2 * D] = h
        w2c[rows, 2 * D : 3 * D] = l

    sweep(mlp, 256, part_2)

    edges[0].wait()
    ones = group_ones()
    temp = head_row(temp_ref)
    for s in range(3):
        sums = sums_ref[s]
        if s == 2:
            sums = sums + peer_ref[...]
            joint_ref[...] = sums
        inv_q = lax.rsqrt(sums[HD : HD + 1] + EPS)
        inv_k = lax.rsqrt(sums[HD + 1 : HD + 2] + EPS)
        unit = sums[0:HD] * row_to_fold(inv_q, ones) * inv_k
        unit_ref[s] = unit
        weight = jnp.exp(temp * unit)
        probs = weight / group_sum(weight, ones)
        probs_ref[s] = probs
        h, l = halves(unfold(probs))
        pcat[:, 3 * s * D : 3 * s * D + 3 * D] = jnp.concatenate([h, h, l], axis=1)

    acc[...] = jnp.zeros_like(acc)
    gtab_ref[...] = jnp.zeros_like(gtab_ref)

    def add(r, v):
        acc[8 * r : 8 * r + 8] += v

    for copy in loads[1:] + edges[1:]:
        copy.wait()

    def own_part(o, size):
        token = o + lax.broadcasted_iota(jnp.int32, (size, D), 0)
        return jnp.where((token >= own_off) & (token < own_off + tokens), 1.0, 0.0)

    def attend(o):
        size = wide // 3
        mix = dot_nt(by_slot(v_ref[pl.ds(o, size)], slot_masks(o, size, spans)), pcat[...])
        mixed[pl.ds(o, size)] = mix
        z = dot_nn(side(mix), wpv[...]) + tab(PB)
        rows = pl.ds(o, size)
        branch = tab(SA) * z
        stream = x_ref[rows] + branch
        s1[rows] = stream
        xhat, _ = normalize(stream)
        li[pl.ds(o + COLS, size)] = xhat * tab(N3G) + tab(N3S)
        add(41, eights(own_part(o, size) * branch * branch))

    for o in range(0, wide, wide // 3):
        attend(o)

    pad = jnp.zeros((COLS, D), F32)
    for buf in (li, mid, gp, ds2):
        buf[0:COLS] = pad
        buf[wide + COLS : wide + 2 * COLS] = pad

    for r in range(rows_wide):
        row = first_row + r
        mine = jnp.where(is_own(r), 1.0, 0.0)
        for n, flag in enumerate((above(row), below(row), mine)):
            flags[n, r * COLS : r * COLS + COLS] = jnp.full((COLS, 128), flag, F32)

    block = 12 * COLS
    col = lax.rem(lax.broadcasted_iota(jnp.int32, (block + 2 * COLS, 128), 0), COLS)

    def convolve(src, base, flip, scale, visit, other=None, events=()):
        def one(n, carry):
            for when, event in events:
                pl.when(n == when)(event)
            lanes = pl.ds(pl.multiple_of(lax.rem(n, 3) * 128, 128), 128)
            m = lax.div(n, 3)
            place = lax.div((m - 1) * (m - 2), 2) + 2 * core * m * (2 - m) + (1 - core) * m * (m - 1)
            o = pl.multiple_of(place * block, block)
            rows = pl.ds(o, block)
            taps = [tab_ref[base + t : base + t + 1, lanes] for t in range(9)]
            if flip:
                taps = taps[::-1]
            if scale is not None:
                taps = [t * tab_ref[scale : scale + 1, lanes] for t in taps]
            u = src[pl.ds(o, block + 2 * COLS), lanes]
            left = jnp.where(col == 0, 0.0, pltpu.roll(u, 1, 0))
            right = jnp.where(col == COLS - 1, 0.0, pltpu.roll(u, block + 2 * COLS - 1, 0))
            up, down = flags[0, rows], flags[1, rows]

            def line(a):
                cut = slice(a * COLS, a * COLS + block)
                return left[cut] * taps[3 * a] + u[cut] * taps[3 * a + 1] + right[cut] * taps[3 * a + 2]

            visit(o, rows, lanes, line(1) + up * line(0) + down * line(2))
            if other is not None:
                near = other[pl.ds(o, block + 2 * COLS), lanes]
                mine = flags[2, rows]
                held = (
                    mine * up * near[0:block],
                    mine * near[COLS : COLS + block],
                    mine * down * near[2 * COLS : 2 * COLS + block],
                )
                inner = slice(COLS, COLS + block)
                for a in range(3):
                    for b, view in enumerate((right, u, left)):
                        t = 8 * (base + 3 * a + b)
                        acc[t : t + 8, lanes] += eights(view[inner] * held[a])
            return carry

        lax.fori_loop(0, 3 * (wide // block), one, 0)

    def first(o, rows, lanes, value):
        at = pl.ds(o + COLS, block)
        a, s = gelu_parts(value + tab_ref[C1B : C1B + 1, lanes])
        act[rows, lanes] = a
        slope[rows, lanes] = s
        mid[at, lanes] = a * tab_ref[BG : BG + 1, lanes] + tab_ref[BS : BS + 1, lanes]

    convolve(li, K1R, False, None, first)

    def second(o, rows, lanes, value):
        value = value + tab_ref[C2B : C2B + 1, lanes]
        lo_[rows, lanes] = value
        branch = tab_ref[SL : SL + 1, lanes] * value
        s2[rows, lanes] = s1[rows, lanes] + branch
        acc[8 * 42 : 8 * 42 + 8, lanes] += eights(flags[2, rows] * branch * branch)

    convolve(mid, K2R, False, None, second)

    dw1_ref[...] = jnp.zeros_like(dw1_ref)
    dw2_ref[...] = jnp.zeros_like(dw2_ref)
    b1g_ref[...] = jnp.zeros_like(b1g_ref)
    for i in range(mlp // D):
        b1_ref[0:1, i * D : i * D + D] = tab(F1B + i)

    def feed(o):
        here = pl.ds(o, TILE)
        xhat, _ = normalize(s2[here])
        n2 = xhat * tab(N2G) + tab(N2S)
        n2c[...] = side(n2)
        dz = tab(SM) * dy_ref[here]
        dzc[...] = side(dz)
        nt[...] = side(n2.T)
        dt[...] = side(dz.T)
        add(F2B, eights(dz))

        def enter(j):
            return dot_nn(n2c[...], w1c[:, j : j + PIECE]), dot_nt(dzc[...], w2c[j : j + PIECE])

        raw, dn = tab(F2B), 0.0
        ready = enter(0)
        for j in range(0, mlp, PIECE):
            lanes = slice(j, j + PIECE)
            pre, dh = ready
            if j + PIECE < mlp:
                ready = enter(j + PIECE)
            a, slope_j = gelu_parts(pre + b1_ref[0:1, lanes])
            dp = dh * slope_j
            ah, al = halves(a)
            ph, pl_ = halves(dp)
            w2h, w2l = w2c[lanes, 0:D], w2c[lanes, 2 * D : 3 * D]
            raw = raw + (dot_nn(ah, w2h) + (dot_nn(al, w2h) + dot_nn(ah, w2l)))
            w1h, w1l = w1c[0:D, lanes], w1c[2 * D : 3 * D, lanes]
            dn = dn + (dot_nt(ph, w1h) + (dot_nt(pl_, w1h) + dot_nt(ph, w1l)))
            b1g_ref[:, lanes] += eights(dp)
            dw1_ref[:, lanes] += dot_nn(nt[...], jnp.concatenate([ph, ph, pl_], axis=0))
            dw2_ref[:, lanes] += dot_nn(dt[...], jnp.concatenate([ah, ah, al], axis=0))
        dy = dy_ref[here]
        xhat, r = normalize(s2[here])
        ds2[pl.ds(pl.multiple_of(o + COLS, COLS), TILE)] = dy + normalize_back(dn * tab(N2G), xhat, r)
        branch = tab(SM) * raw
        result = s2[here] + branch
        s2[here] = result
        add(40, eights(result * result))
        add(43, eights(branch * branch))
        add(SM, eights(dy * raw))
        add(N2G, eights(dn * xhat))
        add(N2S, eights(dn))

    def feed_one(i, carry):
        feed(pl.multiple_of(own_off + i * TILE, 128))
        return carry

    lax.fori_loop(0, tokens // TILE, feed_one, 0)
    reduce.begin()
    stores = [pltpu.make_async_copy(s2.at[own], out_hbm, store_sem.at[0])]
    stores[0].start()
    edge = HALO // 2
    rest = pl.multiple_of(COLS + (1 - core) * (tokens + edge), COLS)
    ds2[pl.ds(rest, edge)] = jnp.zeros((edge, D), F32)
    rows_out = pl.multiple_of(COLS + own_off + (1 - core) * (tokens - edge), COLS)
    rows_in = pl.multiple_of(COLS + edge + core * (tokens - edge), COLS)
    turned = remote(
        ds2.at[pl.ds(rows_out, edge)],
        ds2.at[pl.ds(rows_in, edge)],
        edge_sem.at[0, 4],
        edge_sem.at[1, 4],
        links.twin,
    )
    turned.start()

    def third(o, rows, lanes, value):
        grad = value * tab_ref[BG : BG + 1, lanes] * slope[rows, lanes]
        gp[pl.ds(o + COLS, block), lanes] = grad
        held = flags[2, rows] * value
        acc[8 * BG : 8 * BG + 8, lanes] += eights(held * act[rows, lanes])
        acc[8 * BS : 8 * BS + 8, lanes] += eights(held)
        acc[8 * C1B : 8 * C1B + 8, lanes] += eights(flags[2, rows] * grad)

    convolve(
        ds2,
        K2R,
        True,
        SL,
        third,
        mid,
        ((5, lambda: reduce.join(EARLY)), (6, turned.wait), (8, lambda: reduce.join(LATE))),
    )

    def fourth(o, rows, lanes, value):
        slope[rows, lanes] = value

    convolve(gp, K1R, True, None, fourth, li, ((6, lambda: reduce.down(0, EARLY, 2)),))

    dwp_ref[...] = jnp.zeros_like(dwp_ref)
    cross[...] = jnp.zeros_like(cross)

    def back(step):
        o = pl.multiple_of(own_off + step * TILE, 128)

        here_wide = pl.ds(o, TILE)
        xhat, r = normalize(s1[here_wide])
        grad = slope[here_wide]
        grad_two = ds2[pl.ds(pl.multiple_of(o + COLS, COLS), TILE)]
        result = grad_two + normalize_back(grad * tab(N3G), xhat, r)
        slope[here_wide] = result
        add(N3G, eights(grad * xhat))
        add(N3S, eights(grad))
        add(SL, eights(grad_two * lo_[here_wide]))
        add(C2B, eights(grad_two))
        add(PB, eights(result))
        dmx = dot_nt(side(tab(SA) * result), wph[...])
        act[here_wide] = dmx
        h, l = halves(result)
        dwp_ref[...] += dot_nn(side(mixed[pl.ds(o, TILE)].T), jnp.concatenate([h, h, l], axis=0))
        cross[...] += dot_nn(side(dmx.T), slots_below(v_ref[pl.ds(o, TILE)], slot_masks(o, TILE, spans)))

    count = tokens // TILE
    for step in range(count):
        back(step)
        if step == 0:
            reduce.down(0, LATE, 2)
        if step == 1:
            reduce.down(1, EARLY, 2)
        if step == 2:
            reduce.down(1, LATE, 2)
    for src, dst in ((slope, ds1_hbm), (act, dmx_hbm)):
        stores.append(pltpu.make_async_copy(src.at[own], dst, store_sem.at[len(stores)]))
        stores[-1].start()
    for s in range(3):
        gprob_ref[s] = fold(cross[:, s * D : s * D + D])

    def total(r):
        return jnp.sum(acc[8 * r : 8 * r + 8], axis=0, keepdims=True)

    for r in (N3G, N3S, N2G, N2S, SL, SM, C1B, BG, BS, F2B, 40, 41, 42, 43):
        gtab_ref[r : r + 1] = total(r)
    for t in range(9):
        gtab_ref[K1R + t : K1R + t + 1] = total(K1R + t)
        gtab_ref[K2R + t : K2R + t + 1] = total(K2R + t) * tab(SL)
    gtab_ref[C2B : C2B + 1] = total(C2B) * tab(SL)
    gtab_ref[PB : PB + 1] = total(PB) * tab(SA)
    raw = dwp_ref[...]
    gtab_ref[SA : SA + 1] = jnp.sum(raw * wp_ref[...], axis=0, keepdims=True) + total(PB) * tab(PB)
    dwp_ref[...] = raw * tab(SA)
    for i in range(mlp // D):
        gtab_ref[F1B + i : F1B + i + 1] = jnp.sum(b1g_ref[:, i * D : i * D + D], axis=0, keepdims=True)
    reduce.down(2, EARLY, 2)
    reduce.down(2, LATE, 2)
    for p in range(reduce.count):
        lanes = reduce.lanes(p)
        shard_ref[:, lanes] = reduce.buf[reduce.held(p, 3), lanes]
    for copy in stores:
        copy.wait()


def middle(tall, temp, x, dy, v, sums, wp, w1, w2, tab):
    tokens = x.shape[0]
    wide = tokens + HALO
    mlp = w1.shape[1]
    smem = pl.BlockSpec(memory_space=pltpu.SMEM)
    vmem = pl.BlockSpec(memory_space=pltpu.VMEM)
    anywhere = pl.BlockSpec(memory_space=pl.ANY)

    def f(*shape):
        return jax.ShapeDtypeStruct(shape, F32)

    def s(*shape):
        return pltpu.VMEM(shape, F32)

    def b(*shape):
        return pltpu.VMEM(shape, BF)

    padded = s(wide + 2 * COLS, D)
    return pl.pallas_call(
        middle_kernel,
        out_shape=[
            f(tokens, D),
            f(tokens, D),
            f(tokens, D),
            f(D, D),
            f(2 * SHARD, mlp),
            f(TABLE, D),
            f(3, HD, D),
            f(3, HD, D),
            f(3, HD, D),
            f(*sums.shape[1:]),
        ],
        in_specs=[smem, smem] + [anywhere] * 3 + [vmem, vmem, anywhere, vmem, vmem],
        out_specs=[anywhere] * 3 + [vmem] * 7,
        scratch_shapes=[
            b(3 * D, D),
            b(D, 3 * D),
            b(3 * D, mlp),
            b(mlp, 3 * D),
            b(D, 9 * D),
            s(wide, D),
            s(wide, D),
            padded,
            s(wide, D),
            s(wide, D),
            padded,
            s(wide, D),
            padded,
            padded,
            b(TILE, 3 * D),
            b(TILE, 3 * D),
            s(8, mlp),
            s(8, mlp),
            s(8 * TABLE, D),
            s(D, 3 * D),
            s(wide, D),
            s(wide, D),
            s(wide, D),
            s(3, wide, 128),
            b(D, 3 * TILE),
            b(D, 3 * TILE),
            s(*sums.shape[1:]),
            s(2, D, mlp),
            DMA((4,)),
            DMA((3,)),
            DMA((2, 5)),
        ]
        + Reduce.scratch(mlp, (lax.axis_size("canvas") - 1).bit_length()),
        compiler_params=pltpu.CompilerParams(
            collective_id=0, has_side_effects=True, vmem_limit_bytes=60 << 20
        ),
    )(tall, temp, x, dy, v, sums, wp, w1, w2, tab)


def finish_kernel(
    tall_ref,
    temp_ref,
    x_ref,
    q_ref,
    k_ref,
    ds1_ref,
    dmx_ref,
    sums_ref,
    peer_ref,
    probs_ref,
    unit_ref,
    gprob_ref,
    w_ref,
    tab_ref,
    gtab_ref,
    dwp_ref,
    shard_ref,
    dx_ref,
    end_ref,
    town_ref,
    sum_hbm,
    wh,
    wl,
    pv,
    cv,
    ch,
    side_rows,
    acc,
    gpeer_ref,
    whole,
    dw_ref,
    otab_ref,
    end_first,
    tab_first,
    gsend,
    grecv,
    pair_sem,
    *work,
):
    step = pl.program_id(0)
    last = pl.num_programs(0) - 1
    links = Links()
    core = links.core
    turn = Turn(links, shard_ref, whole, work[:3])
    gather = Gather(links, whole, sum_hbm, work[3:])
    rows_all = 2 * pl.num_programs(0) * TILE // COLS
    spans = slots(tall_ref, core, core * (rows_all // 2), rows_all)
    start = step * TILE

    def tab(r):
        return tab_ref[r : r + 1]

    @pl.when(step == 0)
    def _():
        links.greet()
        swap = remote(gprob_ref.at[2], gpeer_ref, gsend, grecv, links.twin)
        swap.start()
        turn.begin()

        def part(o):
            h, l = halves(w_ref[pl.ds(o, 64)])
            wh[pl.ds(o, 64)] = h
            wl[pl.ds(o, 64)] = l

        sweep(D, 64, part)
        dw_ref[...] = jnp.zeros_like(dw_ref)
        dw_ref[1, :, D : 2 * D] = dwp_ref[...]
        acc[...] = jnp.zeros_like(acc)
        ones = group_ones()
        temp = head_row(temp_ref)
        heat = jnp.zeros((1, D), F32)
        for s in range(3):
            sums = sums_ref[s]
            grad = gprob_ref[s]
            if s == 2:
                swap.wait()
                sums = peer_ref[...]
                grad = grad + gpeer_ref[...]
            inv_q = lax.rsqrt(sums[HD : HD + 1] + EPS)
            inv_k = lax.rsqrt(sums[HD + 1 : HD + 2] + EPS)
            probs = probs_ref[s]
            unit = unit_ref[s]
            scores = probs * (grad - group_sum(probs * grad, ones))
            part_heat = jnp.sum(scores * unit, axis=0, keepdims=True)
            heat = heat + (part_heat if s < 2 else jnp.where(core == 0, part_heat, 0.0))
            pull = temp * scores
            both = pull * unit
            side_rows[8 * s : 8 * s + 1] = fold_to_row(group_sum(both, ones)) * inv_q * inv_q
            side_rows[8 * s + 1 : 8 * s + 2] = jnp.sum(both, axis=0, keepdims=True) * inv_k * inv_k
            across = slice(3 * s * D, 3 * s * D + 3 * D)
            h, l = halves(unfold(pull * row_to_fold(inv_q, ones) * inv_k))
            cv[across] = jnp.concatenate([h, h, l], axis=0)
            ch[:, across] = jnp.concatenate([h, h, l], axis=1)
            h, l = halves(unfold(probs))
            pv[across] = jnp.concatenate([h, h, l], axis=0)
        otab_ref[...] = gtab_ref[...]
        otab_ref[44:45] = heat

    masks = [span_mask(start, TILE, lo, hi) for lo, hi in spans]
    factors = slot_masks(start, TILE, spans)

    def rows_of(r):
        return sum(jnp.where(mask, side_rows[8 * s + r : 8 * s + r + 1], 0.0) for s, mask in enumerate(masks))

    def at(n, *events):
        @pl.when(step == n)
        def _():
            for event, *args in events:
                event(*args)

    q, k = q_ref[...], k_ref[...]
    dq = dot_nt(by_slot(k, factors), ch[...]) - q * rows_of(0)
    dk = dot_nn(by_slot(q, factors), cv[...]) - k * rows_of(1)
    dv = dot_nn(by_slot(dmx_ref[...], factors), pv[...])
    dqkv = jnp.concatenate([dq, dk, dv], axis=1)
    at(0, (turn.end, EARLY), (gather.begin, EARLY))
    at(1, (gather.up, 3, EARLY))
    at(2, (gather.up, 2, LATE))
    at(3, (gather.up, 1, LATE))

    h, l = halves(dqkv)
    dn = dot_nt(h, wh[...]) + (dot_nt(l, wh[...]) + dot_nt(h, wl[...]))
    xhat, r = normalize(x_ref[...])
    nt = side((xhat * tab(N1G) + tab(N1S)).T)
    grads = dot_nn(nt, jnp.concatenate([h, h, l], axis=0))
    dw_ref[0] += grads[:, 0 : 2 * D]
    dw_ref[1, :, 0:D] += grads[:, 2 * D : 3 * D]
    dx_ref[...] = ds1_ref[...] + normalize_back(dn * tab(N1G), xhat, r)
    acc[0:8] += eights(dn * xhat)
    acc[8:16] += eights(dn)
    for i, v in enumerate((dq, dk, dv)):
        acc[16 + 8 * i : 24 + 8 * i] += eights(v)

    at(0, (turn.end, LATE), (gather.begin, LATE))
    at(1, (gather.up, 3, LATE), (gather.up, 2, EARLY))
    at(2, (gather.up, 1, EARLY))

    @pl.when(step == last)
    def _():
        for i, r in enumerate((N1G, N1S, QB, KB, VB)):
            otab_ref[r : r + 1] = jnp.sum(acc[8 * i : 8 * i + 8], axis=0, keepdims=True)
        trows = tab_first.shape[0]
        near = pl.ds(pl.multiple_of(core * trows, 8), trows)
        far = pl.ds(pl.multiple_of((1 - core) * trows, 8), trows)
        pairs = [(otab_ref.at[far], tab_first)]
        for p in range(end_first.shape[1] // 128):
            lanes = slice(p * 128, p * 128 + 128)
            pairs.append((dw_ref.at[1 - core, :, lanes], end_first.at[:, lanes]))
        copies = [
            remote(a, b, pair_sem.at[0, i], pair_sem.at[1, i], links.twin)
            for i, (a, b) in enumerate(pairs)
        ]
        for copy in copies:
            copy.start()
        gather.up(0, EARLY)
        gather.up(0, LATE)
        for copy in copies:
            copy.wait()
        town_ref[...] = otab_ref[near] + tab_first[...]
        end_ref[...] = dw_ref[core] + end_first[...]
        gather.end()


def finish(tall, temp, x, q, k, ds1, dmx, sums, peer, probs, unit, gprob, w, tab, gtab, dwp, shard):
    tokens = x.shape[0]
    smem = pl.BlockSpec(memory_space=pltpu.SMEM)
    anywhere = pl.BlockSpec(memory_space=pl.ANY)
    row = pl.BlockSpec((TILE, D), lambda i: (i, 0))
    bits = (lax.axis_size("canvas") - 1).bit_length()

    def whole(v):
        return pl.BlockSpec(v.shape, lambda i: (0,) * v.ndim)

    fixed = (sums, peer, probs, unit, gprob, w, tab, gtab, dwp, shard)
    return pl.pallas_call(
        finish_kernel,
        grid=(tokens // TILE,),
        out_shape=[
            jax.ShapeDtypeStruct((tokens, D), F32),
            jax.ShapeDtypeStruct((D, 2 * D), F32),
            jax.ShapeDtypeStruct((TABLE // 2, D), F32),
            jax.ShapeDtypeStruct((2, D, shard.shape[1]), F32),
        ],
        in_specs=[smem, smem] + [row] * 5 + [whole(v) for v in fixed],
        out_specs=[
            row,
            pl.BlockSpec((D, 2 * D), lambda i: (0, 0)),
            pl.BlockSpec((TABLE // 2, D), lambda i: (0, 0)),
            anywhere,
        ],
        scratch_shapes=[
            pltpu.VMEM((D, 3 * D), BF),
            pltpu.VMEM((D, 3 * D), BF),
            pltpu.VMEM((9 * D, D), BF),
            pltpu.VMEM((9 * D, D), BF),
            pltpu.VMEM((D, 9 * D), BF),
            pltpu.VMEM((24, D), F32),
            pltpu.VMEM((40, D), F32),
            pltpu.VMEM(gprob.shape[1:], F32),
            pltpu.VMEM((D, shard.shape[1]), F32),
            pltpu.VMEM((2, D, 2 * D), F32),
            pltpu.VMEM((TABLE, D), F32),
            pltpu.VMEM((D, 2 * D), F32),
            pltpu.VMEM((TABLE // 2, D), F32),
            DMA,
            DMA,
            DMA((2, 1 + 2 * D // 128)),
        ]
        + Turn.scratch(shard.shape[1], bits)
        + Gather.scratch(shard.shape[1]),
        compiler_params=pltpu.CompilerParams(
            collective_id=1, has_side_effects=True, vmem_limit_bytes=60 << 20
        ),
    )(tall, temp, x, q, k, ds1, dmx, *fixed)


NS_A, NS_B, NS_C = 3.4445, -4.7750, 2.0315


def times(a, b):
    return dot_nn(
        jnp.concatenate([a[0], a[1], a[0]], axis=1), jnp.concatenate([b[0], b[0], b[1]], axis=0)
    )


def inverse_norm(v):
    total = jnp.sum(jnp.sum(v * v, axis=0, keepdims=True), axis=1, keepdims=True)
    return 1.0 / (jnp.sqrt(total) + 1e-07)


def wide_kernel(
    end_hbm,
    tab_hbm,
    mid_hbm,
    m1_hbm,
    m2_hbm,
    sum_hbm,
    otab_hbm,
    orth_hbm,
    xs,
    x,
    m1,
    m2,
    xc,
    tbuf,
    tland,
    load_sem,
    tsend,
    trecv,
    tout,
    buf,
    own_sem,
    *work,
):
    links = Links()
    core = links.core
    reduce = Reduce(links, buf, buf, work[:5])
    gather = Gather(links, work[0], sum_hbm, work[5:])
    own = pltpu.make_async_copy(end_hbm, buf, own_sem)
    own.start()
    wide = m1.shape[1]
    blocks = wide // D
    trows = tbuf.shape[0]
    near = pl.ds(pl.multiple_of(core * trows, 8), trows)
    pairs = ((mid_hbm.at[core], x), (m1_hbm, m1), (m2_hbm, m2), (tab_hbm, tbuf))
    loads = [pltpu.make_async_copy(a, b, load_sem.at[i]) for i, (a, b) in enumerate(pairs)]
    for load in loads:
        load.start()
    links.greet()
    own.wait()
    reduce.launch()

    def table(n):
        return remote(tbuf, tland.at[n], tsend.at[n], trecv.at[n], links.there[n])

    def table_land(n):
        table(n).wait()
        tbuf[...] += tland[n]

    def down(s, some):
        reduce.down(s, some)
        if some is EARLY:
            table_land(s)
            if s < 3:
                table(s + 1).start()
        elif s == 3:
            for b in range(4, links.bits):
                table(b).start()
                table_land(b)
            for copy in touts:
                copy.start()
        if s == 3:
            for p in some:
                lanes = gather.lanes(p)
                gather.whole[gather.held(p, 4), lanes] = buf[gather.held(p, 4), lanes]
            gather.begin(some)

    touts = [
        pltpu.make_async_copy(tbuf, otab_hbm.at[near], tout.at[0]),
        remote(tbuf, otab_hbm.at[near], tout.at[1], tout.at[2], links.twin),
    ]

    for load in loads:
        load.wait()
    table(0).start()

    @pl.when(core == 0)
    def _():
        x[...] = MUON_KEEP * m1[...] + x[...]

    @pl.when(core == 1)
    def _():
        for b in range(blocks):
            lanes = slice(b * D, b * D + D)
            x[:, lanes] = MUON_KEEP * m2[lanes].T + x[:, lanes]

    inv = inverse_norm(x[...])
    chunks = [slice(o, o + 2 * PIECE) for o in range(0, wide, 2 * PIECE)]

    def keep(lanes, v):
        h, l = halves(v)
        xc[0:D, lanes] = h
        xc[D : 2 * D, lanes] = h
        xc[2 * D : 3 * D, lanes] = l

    def kept(lanes):
        return xc[0:D, lanes].astype(F32) + xc[2 * D : 3 * D, lanes].astype(F32)

    for lanes in chunks:
        keep(lanes, x[:, lanes] * inv)

    def gram():
        h, l = xc[0:D], xc[2 * D : 3 * D]
        return dot_nt(h, h) + (dot_nt(l, h) + dot_nt(h, l))

    def two_steps(events):
        g0 = gram()
        g = halves(g0)
        events(0)
        p0 = NS_B * g0 + NS_C * times(g, g)
        p = halves(p0)
        t = NS_A * g0 + times(p, g)
        events(1)
        g1 = NS_A * t + times(halves(t), p)
        g = halves(g1)
        p1 = NS_B * g1 + NS_C * times(g, g)
        events(2)
        both = side(NS_A * (p0 + p1) + times(halves(p1), p))
        for lanes in chunks:
            keep(lanes, NS_A * NS_A * kept(lanes) + dot_nn(both, xc[:, lanes]))
        events(3)

    def first(n):
        if n == 0:
            down(0, LATE)
        if n == 1:
            down(1, EARLY)
        if n == 2:
            down(1, LATE)
            down(2, EARLY)
        if n == 3:
            down(2, LATE)

    def second(n):
        if n == 0:
            down(3, EARLY)
        if n == 1:
            down(3, LATE)
        if n == 2:
            gather.up(3, EARLY)
        if n == 3:
            gather.up(3, LATE)
            gather.up(2, EARLY)

    down(0, EARLY)
    two_steps(first)
    two_steps(second)
    g0 = gram()
    g = halves(g0)
    gather.up(2, LATE)
    last = side(NS_B * g0 + NS_C * times(g, g))
    for lanes in chunks:
        x[:, lanes] = NS_A * kept(lanes) + dot_nn(last, xc[:, lanes])
    gather.up(1, EARLY)

    @pl.when(core == 0)
    def _():
        for b in range(blocks):
            xs[b] = x[:, b * D : b * D + D]

    @pl.when(core == 1)
    def _():
        for b in range(blocks):
            xs[b] = x[:, b * D : b * D + D].T

    orth = [
        pltpu.make_async_copy(xs, orth_hbm.at[core], tout.at[3]),
        remote(xs, orth_hbm.at[core], tout.at[4], tout.at[5], links.twin),
    ]
    for copy in orth:
        copy.start()
    gather.up(1, LATE)
    gather.up(0, EARLY)
    gather.up(0, LATE)
    gather.end()
    for copy in touts + orth:
        copy.wait()


def wide_blocks(end, tab, mid, m1, m2):
    bits = (lax.axis_size("canvas") - 1).bit_length()
    anywhere = pl.BlockSpec(memory_space=pl.ANY)
    blocks = m1.shape[1] // D
    return pl.pallas_call(
        wide_kernel,
        out_shape=[
            jax.ShapeDtypeStruct((2,) + end.shape, F32),
            jax.ShapeDtypeStruct((TABLE, D), F32),
            jax.ShapeDtypeStruct((2, blocks, D, D), F32),
        ],
        in_specs=[anywhere] * 5,
        out_specs=[anywhere] * 3,
        scratch_shapes=[
            pltpu.VMEM((blocks, D, D), F32),
            pltpu.VMEM(m1.shape, F32),
            pltpu.VMEM(m1.shape, F32),
            pltpu.VMEM(m2.shape, F32),
            pltpu.VMEM((3 * D, m1.shape[1]), BF),
            pltpu.VMEM((TABLE // 2, D), F32),
            pltpu.VMEM((bits, TABLE // 2, D), F32),
            DMA((4,)),
            DMA((bits,)),
            DMA((bits,)),
            DMA((6,)),
            pltpu.VMEM(end.shape, F32),
            DMA,
        ]
        + Reduce.scratch(end.shape[1], bits)
        + Gather.scratch(end.shape[1]),
        compiler_params=pltpu.CompilerParams(
            collective_id=2, has_side_effects=True, vmem_limit_bytes=60 << 20
        ),
    )(end, tab, mid, m1, m2)


def muon(w, orth, large):
    return w * (1.0 - MUON_RATE * DECAY) - MUON_RATE * 0.2 * math.sqrt(large) * orth


def square_kernel(
    end_hbm,
    mid_hbm,
    wide_hbm,
    mq_hbm,
    mp_hbm,
    m1_hbm,
    m2_hbm,
    w1_hbm,
    w2_hbm,
    out_hbm,
    dx_hbm,
    gq_out,
    gp_out,
    g1_out,
    g2_out,
    nq_out,
    np_out,
    n1_out,
    n2_out,
    w1_out,
    w2_out,
    c1_out,
    c2_out,
    out_out,
    dx_out,
    orth_hbm,
    end,
    mid,
    nat,
    mq,
    mp,
    m1,
    m2,
    w1,
    w2,
    c1,
    c2,
    wide,
    out,
    dx,
    xh,
    xl,
    xs,
    in_sem,
    out_sem,
):
    core = lax.axis_index("rows")
    mlp = m1.shape[1]
    blocks = mlp // D
    pairs = (
        (end_hbm, end),
        (mq_hbm, mq),
        (mp_hbm, mp),
        (mid_hbm, mid),
        (m1_hbm, m1),
        (m2_hbm, m2),
        (w1_hbm, w1),
        (w2_hbm, w2),
        (wide_hbm, wide),
        (out_hbm, out),
        (dx_hbm, dx),
    )
    loads = [pltpu.make_async_copy(a, b, in_sem.at[i]) for i, (a, b) in enumerate(pairs)]
    for load in loads:
        load.start()
    for load in loads[0:3]:
        load.wait()
    outs = (
        (end.at[0], gq_out.at[:, 0 : 2 * D]),
        (end.at[1, :, 0:D], gq_out.at[:, 2 * D : 3 * D]),
        (end.at[1, :, D : 2 * D], gp_out),
        (mq, nq_out),
        (mp, np_out),
        (mid.at[0], g1_out),
        (nat, g2_out),
        (m1, n1_out),
        (m2, n2_out),
        (out, out_out),
        (dx, dx_out),
        (w1, w1_out),
        (w2, w2_out),
        (c1, c1_out),
        (c2, c2_out),
        (xs, orth_hbm),
    )

    def store(*which):
        return [pltpu.make_async_copy(*outs[n], out_sem.at[n]) for n in which]

    def send(*which):
        for copy in store(*which):
            copy.start()

    send(0, 1, 2)

    def small(o):
        rows = pl.ds(o, 128)
        mq[rows, 0 : 2 * D] = MUON_KEEP * mq[rows, 0 : 2 * D] + end[0, rows]
        mq[rows, 2 * D : 3 * D] = MUON_KEEP * mq[rows, 2 * D : 3 * D] + end[1, rows, 0:D]
        mp[rows] = MUON_KEEP * mp[rows] + end[1, rows, D : 2 * D]

    sweep(D, 128, small)
    send(3, 4)

    def keep(b, v):
        xh[b], xl[b] = halves(v)

    @pl.when(core == 0)
    def _():
        xs[0] = mq[:, 0:D]
        xs[1] = mq[:, D : 2 * D]

    @pl.when(core == 1)
    def _():
        xs[0] = mq[:, 2 * D : 3 * D]
        xs[1] = mp[...]

    for b in range(2):
        keep(b, xs[b] * inverse_norm(xs[b]))

    def step(i, carry):
        x = [(xh[b], xl[b]) for b in range(2)]
        g = [
            dot_nt(jnp.concatenate([h, l, h], axis=1), jnp.concatenate([h, h, l], axis=1))
            for h, l in x
        ]
        pairs = [halves(v) for v in g]
        p = [NS_B * v + NS_C * times(w, w) for v, w in zip(g, pairs)]
        pairs = [halves(v) for v in p]
        for b in range(2):
            h, l = x[b]
            keep(b, NS_A * (h.astype(F32) + l.astype(F32)) + times(pairs[b], x[b]))
        pl.when(i == 1)(moments)
        pl.when(i == 2)(weights)
        return carry

    def moments():
        for load in loads[3:6]:
            load.wait()
        send(5)
        for b in range(blocks):
            nat[b * D : b * D + D] = mid[1, :, b * D : b * D + D].T
        send(6)

        def large(o):
            rows = pl.ds(o, 64)
            m1[rows] = MUON_KEEP * m1[rows] + mid[0, rows]

        sweep(D, 64, large)
        send(7)

        def larger(o):
            rows = pl.ds(o, 256)
            m2[rows] = MUON_KEEP * m2[rows] + nat[rows]

        sweep(mlp, 256, larger)
        send(8)

    def weights():
        for load in loads[6:]:
            load.wait()
        send(9, 10)
        for b in range(blocks):
            at = slice(b * D, b * D + D)
            new = muon(w1[:, at], wide[0, b], mlp)
            w1[:, at] = new
            c1[:, at] = new.astype(BF)
            new = muon(w2[at], wide[1, b], mlp)
            w2[at] = new
            c2[at] = new.astype(BF)
        send(11, 12, 13, 14)

    lax.fori_loop(0, 5, step, 0)
    for b in range(2):
        xs[b] = xh[b].astype(F32) + xl[b].astype(F32)
    send(15)
    for copy in store(*range(len(outs))):
        copy.wait()


def square_blocks(end, mid, wide, mq, mp, m1, m2, w1, w2, out, dx):
    anywhere = pl.BlockSpec(memory_space=pl.ANY)

    def like(v, kind=F32):
        return jax.ShapeDtypeStruct(v.shape, kind)

    def room(v, kind=F32):
        return pltpu.VMEM(v.shape, kind)

    return pl.pallas_call(
        square_kernel,
        out_shape=[like(v) for v in (mq, mp, m1, m2, mq, mp, m1, m2, w1, w2)]
        + [like(w1, BF), like(w2, BF), like(out), like(dx), jax.ShapeDtypeStruct((2, D, D), F32)],
        in_specs=[anywhere] * 11,
        out_specs=[anywhere] * 15,
        scratch_shapes=[room(v) for v in (end, mid, m2, mq, mp, m1, m2, w1, w2)]
        + [room(w1, BF), room(w2, BF), room(wide), room(out), room(dx)]
        + [
            pltpu.VMEM((2, D, D), BF),
            pltpu.VMEM((2, D, D), BF),
            pltpu.VMEM((2, D, D), F32),
            DMA((11,)),
            DMA((16,)),
        ],
        compiler_params=pltpu.CompilerParams(vmem_limit_bytes=60 << 20),
    )(end, mid, wide, mq, mp, m1, m2, w1, w2, out, dx)


def trade_kernel(own_ref, peer_ref, send_sem, recv_sem):
    core = lax.axis_index("rows")
    twin = {"rows": 1 - core}
    barrier = pltpu.get_barrier_semaphore()
    pl.semaphore_signal(barrier, inc=1, device_id=twin, device_id_type=MESH_ID)
    pl.semaphore_wait(barrier, 1)
    copy = remote(own_ref, peer_ref, send_sem, recv_sem, twin)
    copy.start()
    copy.wait()


def trade(own):
    anywhere = pl.BlockSpec(memory_space=pl.ANY)
    return pl.pallas_call(
        trade_kernel,
        out_shape=jax.ShapeDtypeStruct(own.shape, F32),
        in_specs=[anywhere],
        out_specs=anywhere,
        scratch_shapes=[DMA, DMA],
        compiler_params=pltpu.CompilerParams(collective_id=3, has_side_effects=True),
    )(own)


def moment_step(current, one, two, gradient):
    first = BETA1 * one + (1.0 - BETA1) * gradient
    second = BETA2 * two + (1.0 - BETA2) * gradient * gradient
    fix_one = 1.0 - BETA1**STEP
    fix_two = 1.0 - BETA2**STEP
    updated = current - ADAM_RATE * (first / fix_one) / (jnp.sqrt(second / fix_two) + ADAM_FLOOR)
    return first, second, updated


def update_kernel(
    count,
    temp_ref,
    heat_one_ref,
    heat_two_ref,
    own_ref,
    peer_ref,
    wq_ref,
    wp_ref,
    tab_ref,
    one_ref,
    two_ref,
    gtab_ref,
    nq_ref,
    np_ref,
    cq_ref,
    cp_ref,
    first_ref,
    second_ref,
    small_ref,
    heat_first_ref,
    heat_second_ref,
    heat_ref,
    rms_ref,
):
    lower = lax.axis_index("rows") == 0
    own, peer = own_ref[...], peer_ref[...]
    low, high = jnp.where(lower, own, peer), jnp.where(lower, peer, own)
    for i, orth in enumerate((low[0], low[1], high[0])):
        lanes = slice(i * D, i * D + D)
        new = muon(wq_ref[:, lanes], orth, D)
        nq_ref[:, lanes] = new
        cq_ref[:, lanes] = new.astype(BF)
    new = muon(wp_ref[...], high[1], D)
    np_ref[...] = new
    cp_ref[...] = new.astype(BF)
    first, second, small = moment_step(tab_ref[...], one_ref[...], two_ref[...], gtab_ref[0:SMALL])
    first_ref[...] = first
    second_ref[...] = second
    small_ref[...] = small

    @pl.when(pl.program_id(0) == 0)
    def _():
        head = lax.broadcasted_iota(jnp.int32, (HEADS, D), 0)
        lane = lax.broadcasted_iota(jnp.int32, (HEADS, D), 1) // HD
        heat = jnp.sum(jnp.where(head == lane, gtab_ref[44:45], 0.0), axis=1, keepdims=True)
        head = lax.broadcasted_iota(jnp.int32, (HEADS, 1), 0)

        def column(ref):
            v = jnp.where(head == 0, ref[0], 0.0)
            for h in range(1, HEADS):
                v = jnp.where(head == h, ref[h], v)
            return v

        results = moment_step(column(temp_ref), column(heat_one_ref), column(heat_two_ref), heat)
        for ref, v in zip((heat_first_ref, heat_second_ref, heat_ref), results):
            for h in range(HEADS):
                ref[h] = v[h, 0]
        rms = jnp.sqrt(jnp.sum(gtab_ref[40:44], axis=1, keepdims=True) / count)
        for n in range(4):
            rms_ref[n] = rms[n, 0]


def update(count, temp, heat_one, heat_two, own, peer, wq, wp, tab, one, two, gtab):
    steps = 3
    piece = D // steps

    def rows(v):
        return pl.BlockSpec((piece, v.shape[1]), lambda i: (i, 0))

    def whole(v):
        return pl.BlockSpec(v.shape, lambda i: (0, 0))

    square = pl.BlockSpec((2, piece, D), lambda i: (0, i, 0))
    weights = (wq, wp)
    smem = pl.BlockSpec(memory_space=pltpu.SMEM)
    return pl.pallas_call(
        functools.partial(update_kernel, count),
        grid=(steps,),
        out_shape=[jax.ShapeDtypeStruct(w.shape, F32) for w in weights]
        + [jax.ShapeDtypeStruct(w.shape, BF) for w in weights]
        + [jax.ShapeDtypeStruct(tab.shape, F32)] * 3
        + [jax.ShapeDtypeStruct(temp.shape, F32)] * 3
        + [jax.ShapeDtypeStruct((4,), F32)],
        in_specs=[smem] * 3
        + [square, square]
        + [rows(w) for w in weights]
        + [whole(v) for v in (tab, one, two, gtab)],
        out_specs=[rows(w) for w in weights] * 2 + [whole(tab)] * 3 + [smem] * 4,
        compiler_params=pltpu.CompilerParams(vmem_limit_bytes=60 << 20),
    )(temp, heat_one, heat_two, own, peer, *weights, tab, one, two, gtab)


def on_device(
    x4, dy4, tall, wqkv, wp, w1, w2, mqkv, mp, m1, m2, tab, tab_one, tab_two, temp, temp_one, temp_two
):
    shape = x4.shape
    tokens = shape[1] * shape[2]
    x = x4.reshape(tokens, D)
    dy = dy4.reshape(tokens, D)
    q, k, v, sums = project(tall, x, wqkv, tab)
    out, ds1, dmx, dwp, shard, gtab, probs, unit, gprob, joint = middle(
        tall, temp, x, dy, v, sums, wp, w1, w2, tab
    )
    dx, end, gtab, mid = finish(
        tall, temp, x, q, k, ds1, dmx, sums, joint, probs, unit, gprob, wqkv, tab, gtab, dwp, shard
    )
    end, gtab, wide = wide_blocks(end, gtab, mid, m1, m2)
    *grads, new_1, new_2, copy_1, copy_2, out, dx, square = square_blocks(
        end, mid, wide, mqkv, mp, m1, m2, w1, w2, out, dx
    )
    count = tokens * D * lax.axis_size("rows") * lax.axis_size("canvas")
    new_q, new_p, copy_q, copy_p, *small = update(
        count, temp, temp_one, temp_two, square, trade(square), wqkv, wp, tab, tab_one, tab_two, gtab
    )
    new = (new_q, new_p, new_1, new_2, copy_q, copy_p, copy_1, copy_2)
    return (out.reshape(shape), dx.reshape(shape), *grads, *new, *small)


def solution(mesh):
    split = P("canvas", "rows", None, None)
    return jax.shard_map(
        on_device,
        mesh=mesh,
        in_specs=(split, split, P("canvas", None)) + (P(),) * 14,
        out_specs=(split, split) + (P(),) * 23,
        check_vma=False,
    )
```

```python
import functools
import math

import jax
import jax.numpy as jnp
from jax import lax
from jax.experimental import pallas as pl
from jax.experimental.pallas import tpu as pltpu
from jax.sharding import PartitionSpec as P

BF = jnp.bfloat16
F32 = jnp.float32
MESH_ID = pl.DeviceIdType.MESH

EPS = 1e-06
ROOT_HALF = 1.0 / math.sqrt(2.0)
ROOT_TWOPI = 1.0 / math.sqrt(2.0 * math.pi)
STEP = 10
MUON_RATE = 0.2
MUON_KEEP = 0.95
DECAY = 0.01
ADAM_RATE = 0.2
BETA1 = 0.9
BETA2 = 0.95
ADAM_FLOOR = 1e-08

HEADS = 8
HD = 48
D = HEADS * HD
COLS = 32
HALO = 4 * COLS
TILE = 256

N1G, N1S, N3G, N3S, N2G, N2S, SA, SL, SM, QB, KB, VB, PB, C1B, BG, BS, C2B, F2B = range(18)
F1B, K1R, K2R = 18, 22, 31
SMALL = 40
TABLE = 48


def halves(v):
    hi = v.astype(BF)
    return hi, (v - hi.astype(F32)).astype(BF)


def side(v):
    h, l = halves(v)
    return jnp.concatenate([h, l, h], axis=1)


def dot_nn(a, b):
    return lax.dot_general(a, b, (((1,), (0,)), ((), ())), preferred_element_type=F32)


def dot_nt(a, b):
    return lax.dot_general(a, b, (((1,), (1,)), ((), ())), preferred_element_type=F32)


def normalize(v):
    mean = jnp.mean(v, axis=1, keepdims=True)
    c = v - mean
    r = lax.rsqrt(jnp.mean(c * c, axis=1, keepdims=True) + EPS)
    return c * r, r


def normalize_back(e, xhat, r):
    return r * (
        e - jnp.mean(e, axis=1, keepdims=True) - xhat * jnp.mean(e * xhat, axis=1, keepdims=True)
    )


def gelu_parts(v):
    phi = 0.5 * (1.0 + lax.erf(v * ROOT_HALF))
    return v * phi, phi + v * jnp.exp(-0.5 * v * v) * ROOT_TWOPI


def eights(v):
    total = v[0:8]
    for i in range(8, v.shape[0], 8):
        total = total + v[i : i + 8]
    return total


def sweep(count, size, body):
    def one(i, carry):
        body(pl.multiple_of(i * size, size))
        return carry

    lax.fori_loop(0, count // size, one, 0)


def image_ends(tall_ref):
    e0 = tall_ref[0, 0]
    e1 = e0 + tall_ref[0, 1]
    return e0, e1, e1 + tall_ref[0, 2]


def slots(tall_ref, core, first_row, rows_all):
    e0, e1, e2 = image_ends(tall_ref)
    low = (jnp.where(core == 0, 0, e2), jnp.where(core == 0, e0, 0), e1)
    high = (jnp.where(core == 0, e0, rows_all), jnp.where(core == 0, e1, 0), e2)
    return [((a - first_row) * COLS, (b - first_row) * COLS) for a, b in zip(low, high)]


def span_mask(start, rows, lo, hi):
    token = start + lax.broadcasted_iota(jnp.int32, (rows, D), 0)
    return (token >= lo) & (token < hi)


def slot_masks(start, rows, spans):
    return [jnp.where(span_mask(start, rows, lo, hi), 1.0, 0.0).astype(BF) for lo, hi in spans]


def by_slot(v, masks):
    h, l = halves(v)
    parts = []
    for mask in masks:
        hm = h * mask
        parts += [hm, l * mask, hm]
    return jnp.concatenate(parts, axis=1)


def slots_below(v, masks):
    h, l = halves(v)
    high = jnp.concatenate([h * mask for mask in masks], axis=1)
    return jnp.concatenate([high, high, jnp.concatenate([l * mask for mask in masks], axis=1)], axis=0)


def lane_head():
    return lax.broadcasted_iota(jnp.int32, (HD, D), 1) // HD


def lane_slot():
    return lax.broadcasted_iota(jnp.int32, (HD, D), 1) % HD


def fold(full):
    head = lane_head()
    total = jnp.where(head == 0, full[0:HD], 0.0)
    for h in range(1, HEADS):
        total = total + jnp.where(head == h, full[h * HD : h * HD + HD], 0.0)
    return total


def unfold(small):
    head = lane_head()
    return jnp.concatenate([jnp.where(head == h, small, 0.0) for h in range(HEADS)], axis=0)


def group_ones():
    a = lax.broadcasted_iota(jnp.int32, (D, D), 0) // HD
    b = lax.broadcasted_iota(jnp.int32, (D, D), 1) // HD
    return jnp.where(a == b, 1.0, 0.0).astype(BF)


def group_sum(v, ones):
    h = v.astype(BF)
    rest = v - h.astype(F32)
    m = rest.astype(BF)
    l = (rest - m.astype(F32)).astype(BF)
    return dot_nn(h, ones) + (dot_nn(m, ones) + dot_nn(l, ones))


def row_to_fold(row, ones):
    slot = lax.broadcasted_iota(jnp.int32, (HD, D), 0)
    return group_sum(jnp.where(lane_slot() == slot, jnp.broadcast_to(row, (HD, D)), 0.0), ones)


def fold_to_row(small):
    slot = lax.broadcasted_iota(jnp.int32, (HD, D), 0)
    return jnp.sum(jnp.where(lane_slot() == slot, small, 0.0), axis=0, keepdims=True)


def head_row(temp_ref):
    head = lax.broadcasted_iota(jnp.int32, (1, D), 1) // HD
    row = jnp.where(head == 0, temp_ref[0], 0.0)
    for h in range(1, HEADS):
        row = row + jnp.where(head == h, temp_ref[h], 0.0)
    return row


def project_kernel(tall_ref, x_ref, w_ref, tab_ref, q_ref, k_ref, v_ref, sums_ref, wcat, cross):
    step = pl.program_id(0)
    core = lax.axis_index("rows")
    rows_all = 2 * pl.num_programs(0) * TILE // COLS
    spans = slots(tall_ref, core, core * (rows_all // 2), rows_all)
    start = step * TILE

    @pl.when(step == 0)
    def _():
        def part(o):
            h, l = halves(w_ref[pl.ds(o, 64)])
            wcat[pl.ds(o, 64)] = h
            wcat[pl.ds(D + o, 64)] = h
            wcat[pl.ds(2 * D + o, 64)] = l

        sweep(D, 64, part)
        cross[...] = jnp.zeros_like(cross)
        sums_ref[...] = jnp.zeros_like(sums_ref)

    xhat, _ = normalize(x_ref[...])
    lhs = side(xhat * tab_ref[N1G : N1G + 1] + tab_ref[N1S : N1S + 1])
    q = dot_nn(lhs, wcat[:, 0:D]) + tab_ref[QB : QB + 1]
    q_ref[...] = q
    k = dot_nn(lhs, wcat[:, D : 2 * D]) + tab_ref[KB : KB + 1]
    k_ref[...] = k
    v_ref[...] = dot_nn(lhs, wcat[:, 2 * D : 3 * D]) + tab_ref[VB : VB + 1]
    cross[...] += dot_nn(side(q.T), slots_below(k, slot_masks(start, TILE, spans)))
    for s, (lo, hi) in enumerate(spans):
        mask = span_mask(start, TILE, lo, hi)
        for n, v in enumerate((q, k)):
            row = HD + n
            sums_ref[s, row : row + 1] += jnp.sum(jnp.where(mask, v * v, 0.0), axis=0, keepdims=True)

    @pl.when(step == pl.num_programs(0) - 1)
    def _():
        for s in range(3):
            sums_ref[s, 0:HD] = fold(cross[:, s * D : s * D + D])


def project(tall, x, w, tab):
    tokens = x.shape[0]
    row = pl.BlockSpec((TILE, D), lambda i: (i, 0))
    return pl.pallas_call(
        project_kernel,
        grid=(tokens // TILE,),
        out_shape=[jax.ShapeDtypeStruct((tokens, D), F32)] * 3
        + [jax.ShapeDtypeStruct((3, HD + 8, D), F32)],
        in_specs=[
            pl.BlockSpec(memory_space=pltpu.SMEM),
            row,
            pl.BlockSpec((D, 3 * D), lambda i: (0, 0)),
            pl.BlockSpec((SMALL, D), lambda i: (0, 0)),
        ],
        out_specs=[row, row, row, pl.BlockSpec((3, HD + 8, D), lambda i: (0, 0, 0))],
        scratch_shapes=[pltpu.VMEM((3 * D, 3 * D), BF), pltpu.VMEM((D, 3 * D), F32)],
        compiler_params=pltpu.CompilerParams(vmem_limit_bytes=60 << 20),
    )(tall, x, w, tab)


ORDERS = ((0, 1, 2, 3), (1, 2, 0, 3), (2, 0, 1, 3))
EARLY, LATE = range(0, 3), range(3, 6)
PIECE = 256
SHARD = D // 16
DMA = pltpu.SemaphoreType.DMA


class Links:
    def __init__(self):
        self.core = lax.axis_index("rows")
        chip = lax.axis_index("canvas")
        self.bits = (lax.axis_size("canvas") - 1).bit_length()
        self.mine = [lax.rem(lax.div(chip, 1 << b), 2) for b in range(self.bits)]
        self.there = [{"canvas": chip + (1 - 2 * m) * (1 << b)} for b, m in enumerate(self.mine)]
        self.twin = {"rows": 1 - self.core}

    def call(self):
        barrier = pltpu.get_barrier_semaphore()
        for other in [self.twin] + self.there:
            pl.semaphore_signal(barrier, inc=1, device_id=other, device_id_type=MESH_ID)

    def answer(self):
        pl.semaphore_wait(pltpu.get_barrier_semaphore(), self.bits + 1)

    def greet(self):
        self.call()
        self.answer()


def remote(src, dst, send, recv, other):
    return pltpu.make_async_remote_copy(
        src_ref=src,
        dst_ref=dst,
        send_sem=send,
        recv_sem=recv,
        device_id=other,
        device_id_type=MESH_ID,
    )


class Pieces:
    count = 6

    def __init__(self, links, lanes):
        self.links = links
        self.width = lanes // self.count

    def lanes(self, p):
        return slice(p * self.width, p * self.width + self.width)

    def bit(self, p, s):
        return ORDERS[p % 3][s]

    def start(self, p, s):
        at = 0
        for t in range(s):
            at = at + self.links.mine[self.bit(p, t)] * (D >> (t + 1))
        return at

    def held(self, p, s):
        return pl.ds(pl.multiple_of(self.start(p, s), 8), D >> s)


class Reduce(Pieces):
    def __init__(self, links, src, buf, work):
        super().__init__(links, src.shape[-1])
        self.src, self.buf = src, buf
        self.first, self.land, self.pair_sem, self.send_sem, self.recv_sem = work

    @classmethod
    def scratch(cls, lanes, bits):
        steps = max(bits, 4)
        return [
            pltpu.VMEM((D, lanes), F32),
            pltpu.VMEM((D - SHARD + (steps - 4) * SHARD, lanes), F32),
            DMA((2, cls.count)),
            DMA((cls.count, steps)),
            DMA((cls.count, steps)),
        ]

    def add(self, p, rows, src, src_rows):
        lanes = self.lanes(p)
        self.buf[rows, lanes] += src[src_rows, lanes]

    def pair(self, p):
        lanes = self.lanes(p)
        return remote(
            self.src.at[1 - self.links.core, :, lanes],
            self.first.at[:, lanes],
            self.pair_sem.at[0, p],
            self.pair_sem.at[1, p],
            self.links.twin,
        )

    def move(self, p, s):
        b = self.bit(p, s)
        half = D >> (s + 1)
        away = pl.multiple_of(self.start(p, s) + (1 - self.links.mine[b]) * half, 8)
        lanes = self.lanes(p)
        return remote(
            self.buf.at[pl.ds(away, half), lanes],
            self.land.at[pl.ds(D - (D >> s), half), lanes],
            self.send_sem.at[p, s],
            self.recv_sem.at[p, s],
            self.links.there[b],
        )

    def begin(self):
        for p in range(self.count):
            self.pair(p).start()

    def join(self, some):
        for p in some:
            self.pair(p).wait()
            self.add(p, pl.ds(0, D), self.first, pl.ds(0, D))
            self.move(p, 0).start()

    def launch(self):
        for p in range(self.count):
            self.move(p, 0).start()

    def down(self, s, some, last=3):
        for p in some:
            self.move(p, s).wait()
            self.add(p, self.held(p, s + 1), self.land, pl.ds(D - (D >> s), D >> (s + 1)))
            if s < last:
                self.move(p, s + 1).start()
        if s == 3:
            for b in range(4, self.links.bits):
                self.swap(b, some)

    def swap(self, b, some):
        at = pl.ds(D - SHARD + (b - 4) * SHARD, SHARD)
        copies = {}
        for p in some:
            lanes = self.lanes(p)
            copies[p] = remote(
                self.buf.at[self.held(p, 4), lanes],
                self.land.at[at, lanes],
                self.send_sem.at[p, b],
                self.recv_sem.at[p, b],
                self.links.there[b],
            )
            copies[p].start()
        for p in some:
            copies[p].wait()
            self.add(p, self.held(p, 4), self.land, at)


class Gather(Pieces):
    def __init__(self, links, whole, dst, work):
        super().__init__(links, whole.shape[1])
        self.whole, self.dst = whole, dst
        self.send_sem, self.recv_sem, self.out_sem = work

    @classmethod
    def scratch(cls, lanes):
        return [DMA((cls.count, 4)), DMA((cls.count, 4)), DMA((2, 3, cls.count))]

    def back(self, p, s):
        view = self.whole.at[self.held(p, s + 1), self.lanes(p)]
        return remote(
            view,
            view,
            self.send_sem.at[p, s],
            self.recv_sem.at[p, s],
            self.links.there[self.bit(p, s)],
        )

    def outs(self, p, n):
        mine = self.links.mine[self.bit(p, 0)]
        half = D // 2
        at = pl.multiple_of(half * (mine if n == 0 else 1 - mine), 8)
        rows = pl.ds(at, half)
        src = self.whole.at[rows, self.lanes(p)]
        dst = self.dst.at[self.links.core, rows, self.lanes(p)]
        sem = self.out_sem.at[n]
        return (
            pltpu.make_async_copy(src, dst, sem.at[0, p]),
            remote(src, dst, sem.at[1, p], sem.at[2, p], self.links.twin),
        )

    def begin(self, some):
        for p in some:
            self.back(p, 3).start()

    def up(self, s, some):
        for p in some:
            self.back(p, s).wait()
            if s > 0:
                self.back(p, s - 1).start()
            if s < 2:
                for copy in self.outs(p, 1 - s):
                    copy.start()

    def end(self):
        for n in range(2):
            for p in range(self.count):
                for copy in self.outs(p, n):
                    copy.wait()


def row_flags(tall_ref, rows_all):
    ends = image_ends(tall_ref)

    def above(row):
        first = (row == 0) | (row == ends[0]) | (row == ends[1]) | (row == ends[2])
        return jnp.where(first, 0.0, 1.0)

    def below(row):
        return jnp.where(row + 1 == rows_all, 0.0, above(row + 1))

    return above, below


def middle_kernel(
    tall_ref,
    temp_ref,
    x_hbm,
    dy_hbm,
    v_hbm,
    sums_ref,
    wp_ref,
    w1_hbm,
    w2_ref,
    tab_ref,
    out_hbm,
    ds1_hbm,
    dmx_hbm,
    dwp_ref,
    shard_ref,
    gtab_ref,
    probs_ref,
    unit_ref,
    gprob_ref,
    joint_ref,
    wpv,
    wph,
    w1c,
    w2c,
    pcat,
    mixed,
    s1,
    li,
    act,
    slope,
    mid,
    s2,
    ds2,
    gp,
    n2h,
    n2l,
    dzh,
    dzl,
    dtl,
    b1_ref,
    b1g_ref,
    acc,
    x_ref,
    dy_ref,
    v_ref,
    flags,
    peer_ref,
    dw_ref,
    load_sem,
    store_sem,
    edge_sem,
    *work,
):
    links = Links()
    core = links.core
    wide = x_ref.shape[0]
    tokens = wide - HALO
    dw1_ref, dw2_ref = dw_ref.at[0], dw_ref.at[1]
    reduce = Reduce(links, dw_ref, dw_ref.at[core], work)
    w1_ref = work[0]
    cross = work[0].at[:, 0 : 3 * D]
    nth, ntl, dth = (pcat.at[:, i * tokens : i * tokens + tokens] for i in range(3))
    lo_ = x_ref
    own = pl.ds(pl.multiple_of(core * HALO, HALO), tokens)
    pairs = ((w1_hbm, w1_ref), (v_hbm, v_ref.at[own]), (x_hbm, x_ref.at[own]), (dy_hbm, dy_ref.at[own]))
    loads = [pltpu.make_async_copy(a, b, load_sem.at[i]) for i, (a, b) in enumerate(pairs)]
    for load in loads:
        load.start()
    links.call()
    edge = pl.ds(pl.multiple_of((1 - core) * (tokens - HALO), HALO), HALO)
    far = pl.ds(pl.multiple_of(core * tokens, HALO), HALO)
    pairs = (
        (sums_ref.at[2], peer_ref),
        (v_hbm.at[edge], v_ref.at[far]),
        (x_hbm.at[edge], x_ref.at[far]),
        (dy_hbm.at[edge], dy_ref.at[far]),
    )
    edges = [
        remote(a, b, edge_sem.at[0, i], edge_sem.at[1, i], links.twin)
        for i, (a, b) in enumerate(pairs)
    ]
    own_rows = tokens // COLS
    rows_wide = wide // COLS
    rows_all = 2 * own_rows
    first_row = core * (own_rows - HALO // COLS)
    own_off = pl.multiple_of(core * HALO, HALO)
    mlp = w1_hbm.shape[1]
    spans = slots(tall_ref, core, first_row, rows_all)
    above, below = row_flags(tall_ref, rows_all)

    def tab(r):
        return tab_ref[r : r + 1]

    def is_own(row):
        return (row >= core * (HALO // COLS)) & (row < core * (HALO // COLS) + own_rows)

    loads[0].wait()

    def part_1(o):
        rows = pl.ds(o, 64)
        h, l = halves(w1_ref[rows])
        w1c[rows] = h
        w1c[pl.ds(D + o, 64)] = h
        w1c[pl.ds(2 * D + o, 64)] = l

    sweep(D, 64, part_1)
    links.answer()
    for copy in edges:
        copy.start()

    def part_p(o):
        rows = pl.ds(o, 192)
        h, l = halves(wp_ref[rows])
        wpv[rows] = h
        wpv[pl.ds(D + o, 192)] = h
        wpv[pl.ds(2 * D + o, 192)] = l
        wph[rows, 0:D] = h
        wph[rows, D : 2 * D] = h
        wph[rows, 2 * D : 3 * D] = l

    sweep(D, 192, part_p)

    def part_2(o):
        rows = pl.ds(o, 256)
        h, l = halves(w2_ref[rows])
        w2c[rows, 0:D] = h
        w2c[rows, D : 2 * D] = h
        w2c[rows, 2 * D : 3 * D] = l

    sweep(mlp, 256, part_2)

    edges[0].wait()
    ones = group_ones()
    temp = head_row(temp_ref)
    for s in range(3):
        sums = sums_ref[s]
        if s == 2:
            sums = sums + peer_ref[...]
            joint_ref[...] = sums
        inv_q = lax.rsqrt(sums[HD : HD + 1] + EPS)
        inv_k = lax.rsqrt(sums[HD + 1 : HD + 2] + EPS)
        unit = sums[0:HD] * row_to_fold(inv_q, ones) * inv_k
        unit_ref[s] = unit
        weight = jnp.exp(temp * unit)
        probs = weight / group_sum(weight, ones)
        probs_ref[s] = probs
        h, l = halves(unfold(probs))
        pcat[:, 3 * s * D : 3 * s * D + 3 * D] = jnp.concatenate([h, h, l], axis=1)

    acc[...] = jnp.zeros_like(acc)
    gtab_ref[...] = jnp.zeros_like(gtab_ref)

    def add(r, v):
        acc[8 * r : 8 * r + 8] += v

    for copy in loads[1:] + edges[1:]:
        copy.wait()

    def own_part(o, size):
        token = o + lax.broadcasted_iota(jnp.int32, (size, D), 0)
        return jnp.where((token >= own_off) & (token < own_off + tokens), 1.0, 0.0)

    def attend(o):
        size = wide // 3
        mix = dot_nt(by_slot(v_ref[pl.ds(o, size)], slot_masks(o, size, spans)), pcat[...])
        mixed[pl.ds(o, size)] = mix
        z = dot_nn(side(mix), wpv[...]) + tab(PB)
        rows = pl.ds(o, size)
        branch = tab(SA) * z
        stream = x_ref[rows] + branch
        s1[rows] = stream
        xhat, _ = normalize(stream)
        li[pl.ds(o + COLS, size)] = xhat * tab(N3G) + tab(N3S)
        add(41, eights(own_part(o, size) * branch * branch))

    for o in range(0, wide, wide // 3):
        attend(o)

    pad = jnp.zeros((COLS, D), F32)
    for buf in (li, mid, gp, ds2):
        buf[0:COLS] = pad
        buf[wide + COLS : wide + 2 * COLS] = pad

    for r in range(rows_wide):
        row = first_row + r
        mine = jnp.where(is_own(r), 1.0, 0.0)
        for n, flag in enumerate((above(row), below(row), mine)):
            flags[n, r * COLS : r * COLS + COLS] = jnp.full((COLS, 128), flag, F32)

    block = 12 * COLS
    col = lax.rem(lax.broadcasted_iota(jnp.int32, (block + 2 * COLS, 128), 0), COLS)

    def convolve(src, base, flip, scale, visit, other=None, events=()):
        def one(n, carry):
            for when, event in events:
                pl.when(n == when)(event)
            lanes = pl.ds(pl.multiple_of(lax.rem(n, 3) * 128, 128), 128)
            m = lax.div(n, 3)
            place = lax.div((m - 1) * (m - 2), 2) + 2 * core * m * (2 - m) + (1 - core) * m * (m - 1)
            o = pl.multiple_of(place * block, block)
            rows = pl.ds(o, block)
            taps = [tab_ref[base + t : base + t + 1, lanes] for t in range(9)]
            if flip:
                taps = taps[::-1]
            if scale is not None:
                taps = [t * tab_ref[scale : scale + 1, lanes] for t in taps]
            u = src[pl.ds(o, block + 2 * COLS), lanes]
            left = jnp.where(col == 0, 0.0, pltpu.roll(u, 1, 0))
            right = jnp.where(col == COLS - 1, 0.0, pltpu.roll(u, block + 2 * COLS - 1, 0))
            up, down = flags[0, rows], flags[1, rows]

            def line(a):
                cut = slice(a * COLS, a * COLS + block)
                return left[cut] * taps[3 * a] + u[cut] * taps[3 * a + 1] + right[cut] * taps[3 * a + 2]

            visit(o, rows, lanes, line(1) + up * line(0) + down * line(2))
            if other is not None:
                near = other[pl.ds(o, block + 2 * COLS), lanes]
                mine = flags[2, rows]
                held = (
                    mine * up * near[0:block],
                    mine * near[COLS : COLS + block],
                    mine * down * near[2 * COLS : 2 * COLS + block],
                )
                inner = slice(COLS, COLS + block)
                for a in range(3):
                    for b, view in enumerate((right, u, left)):
                        t = 8 * (base + 3 * a + b)
                        acc[t : t + 8, lanes] += eights(view[inner] * held[a])
            return carry

        lax.fori_loop(0, 3 * (wide // block), one, 0)

    def first(o, rows, lanes, value):
        at = pl.ds(o + COLS, block)
        a, s = gelu_parts(value + tab_ref[C1B : C1B + 1, lanes])
        act[rows, lanes] = a
        slope[rows, lanes] = s
        mid[at, lanes] = a * tab_ref[BG : BG + 1, lanes] + tab_ref[BS : BS + 1, lanes]

    convolve(li, K1R, False, None, first)

    def second(o, rows, lanes, value):
        value = value + tab_ref[C2B : C2B + 1, lanes]
        lo_[rows, lanes] = value
        branch = tab_ref[SL : SL + 1, lanes] * value
        s2[rows, lanes] = s1[rows, lanes] + branch
        acc[8 * 42 : 8 * 42 + 8, lanes] += eights(flags[2, rows] * branch * branch)

    convolve(mid, K2R, False, None, second)

    for i in range(mlp // D):
        b1_ref[0:1, i * D : i * D + D] = tab(F1B + i)
    count = tokens // TILE

    def tile(t):
        return pl.ds(pl.multiple_of(own_off + t * TILE, 128), TILE)

    def padded_tile(t):
        return pl.ds(pl.multiple_of(own_off + t * TILE + COLS, COLS), TILE)

    def prepare(t):
        here, rows = tile(t), slice(t * TILE, t * TILE + TILE)
        xhat, _ = normalize(s2[here])
        n2 = xhat * tab(N2G) + tab(N2S)
        dz = tab(SM) * dy_ref[here]
        add(F2B, eights(dz))
        n2h[rows], n2l[rows] = halves(n2)
        dzh[rows], dzl[rows] = halves(dz)
        nth[:, rows], ntl[:, rows] = halves(n2.T)
        dth[:, rows], dtl[:, rows] = halves(dz.T)
        gp[padded_tile(t)] = jnp.broadcast_to(tab(F2B), (TILE, D))
        ds2[padded_tile(t)] = jnp.zeros((TILE, D), F32)

    for t in range(count):
        prepare(t)

    def across(h, l, rows):
        return jnp.concatenate([h[rows], l[rows], h[rows]], axis=1)

    def along(h, l, lanes):
        return jnp.concatenate([h[:, lanes], l[:, lanes], h[:, lanes]], axis=1)

    def feed(n, carry):
        lanes = pl.ds(pl.multiple_of(n * PIECE, PIECE), PIECE)
        w1n, w2n = w1c[:, lanes], w2c[lanes]
        w1h, w1l = w1c[0:D, lanes], w1c[2 * D : 3 * D, lanes]
        w2h, w2l = w2c[lanes, 0:D], w2c[lanes, 2 * D : 3 * D]

        def enter(t):
            rows = slice(t * TILE, t * TILE + TILE)
            return dot_nn(across(n2h, n2l, rows), w1n), dot_nt(across(dzh, dzl, rows), w2n)

        bias_sum = grad_one = grad_two = 0.0
        ready = enter(0)
        for t in range(count):
            rows = slice(t * TILE, t * TILE + TILE)
            pre, dh = ready
            if t + 1 < count:
                ready = enter(t + 1)
            a, slope_n = gelu_parts(pre + b1_ref[0:1, lanes])
            dp = dh * slope_n
            ah, al = halves(a)
            ph, pl_ = halves(dp)
            gp[padded_tile(t)] += dot_nn(ah, w2h) + (dot_nn(al, w2h) + dot_nn(ah, w2l))
            ds2[padded_tile(t)] += dot_nt(ph, w1h) + (dot_nt(pl_, w1h) + dot_nt(ph, w1l))
            bias_sum = bias_sum + eights(dp)
            grad_one = grad_one + dot_nn(along(nth, ntl, rows), jnp.concatenate([ph, ph, pl_], axis=0))
            grad_two = grad_two + dot_nn(along(dth, dtl, rows), jnp.concatenate([ah, ah, al], axis=0))
        b1g_ref[:, lanes] = bias_sum
        dw1_ref[:, lanes] = grad_one
        dw2_ref[:, lanes] = grad_two
        for done in range(reduce.count):
            pl.when(n == done)(functools.partial(advance, done))
        return carry

    def advance(n):
        reduce.pair(n).start()
        if n >= 1:
            reduce.join([n - 1])
        for s in range(3):
            if n - 3 - s >= 0:
                reduce.down(s, [n - 3 - s])

    lax.fori_loop(0, reduce.count, feed, 0)

    def leave(t, carry):
        here = tile(t)
        xhat, r = normalize(s2[here])
        dy = dy_ref[here]
        dn = ds2[padded_tile(t)]
        ds2[padded_tile(t)] = dy + normalize_back(dn * tab(N2G), xhat, r)
        raw = gp[padded_tile(t)]
        branch = tab(SM) * raw
        result = s2[here] + branch
        s2[here] = result
        add(40, eights(result * result))
        add(43, eights(branch * branch))
        add(SM, eights(dy * raw))
        add(N2G, eights(dn * xhat))
        add(N2S, eights(dn))
        return carry

    lax.fori_loop(0, count, leave, 0)
    stores = [pltpu.make_async_copy(s2.at[own], out_hbm, store_sem.at[0])]
    stores[0].start()
    edge = HALO // 2
    rest = pl.multiple_of(COLS + (1 - core) * (tokens + edge), COLS)
    ds2[pl.ds(rest, edge)] = jnp.zeros((edge, D), F32)
    rows_out = pl.multiple_of(COLS + own_off + (1 - core) * (tokens - edge), COLS)
    rows_in = pl.multiple_of(COLS + edge + core * (tokens - edge), COLS)
    turned = remote(
        ds2.at[pl.ds(rows_out, edge)],
        ds2.at[pl.ds(rows_in, edge)],
        edge_sem.at[0, 4],
        edge_sem.at[1, 4],
        links.twin,
    )
    turned.start()

    def serve(join, *steps):
        reduce.join(join)
        for s, some in enumerate(steps):
            reduce.down(s, some)

    serve([5], [3], [2], [1], [0])

    def third(o, rows, lanes, value):
        grad = value * tab_ref[BG : BG + 1, lanes] * slope[rows, lanes]
        gp[pl.ds(o + COLS, block), lanes] = grad
        held = flags[2, rows] * value
        acc[8 * BG : 8 * BG + 8, lanes] += eights(held * act[rows, lanes])
        acc[8 * BS : 8 * BS + 8, lanes] += eights(held)
        acc[8 * C1B : 8 * C1B + 8, lanes] += eights(flags[2, rows] * grad)

    convolve(
        ds2,
        K2R,
        True,
        SL,
        third,
        mid,
        ((3, lambda: serve([], [4], [3], [2], [1])), (6, turned.wait)),
    )
    serve([], [5], [4], [3], [2])

    def fourth(o, rows, lanes, value):
        slope[rows, lanes] = value

    convolve(gp, K1R, True, None, fourth, li, ((5, lambda: serve([], [], [5], [4], [3])),))

    dwp_ref[...] = jnp.zeros_like(dwp_ref)
    cross[...] = jnp.zeros_like(cross)

    def back(step):
        o = pl.multiple_of(own_off + step * TILE, 128)

        here_wide = pl.ds(o, TILE)
        xhat, r = normalize(s1[here_wide])
        grad = slope[here_wide]
        grad_two = ds2[pl.ds(pl.multiple_of(o + COLS, COLS), TILE)]
        result = grad_two + normalize_back(grad * tab(N3G), xhat, r)
        slope[here_wide] = result
        add(N3G, eights(grad * xhat))
        add(N3S, eights(grad))
        add(SL, eights(grad_two * lo_[here_wide]))
        add(C2B, eights(grad_two))
        add(PB, eights(result))
        dmx = dot_nt(side(tab(SA) * result), wph[...])
        act[here_wide] = dmx
        h, l = halves(result)
        dwp_ref[...] += dot_nn(side(mixed[pl.ds(o, TILE)].T), jnp.concatenate([h, h, l], axis=0))
        cross[...] += dot_nn(side(dmx.T), slots_below(v_ref[pl.ds(o, TILE)], slot_masks(o, TILE, spans)))

    for step in range(count):
        back(step)
        if step == 0:
            serve([], [], [], [5], [4])
        if step == 2:
            serve([], [], [], [], [5])
    for src, dst in ((slope, ds1_hbm), (act, dmx_hbm)):
        stores.append(pltpu.make_async_copy(src.at[own], dst, store_sem.at[len(stores)]))
        stores[-1].start()
    for s in range(3):
        gprob_ref[s] = fold(cross[:, s * D : s * D + D])

    def total(r):
        return jnp.sum(acc[8 * r : 8 * r + 8], axis=0, keepdims=True)

    for r in (N3G, N3S, N2G, N2S, SL, SM, C1B, BG, BS, F2B, 40, 41, 42, 43):
        gtab_ref[r : r + 1] = total(r)
    for t in range(9):
        gtab_ref[K1R + t : K1R + t + 1] = total(K1R + t)
        gtab_ref[K2R + t : K2R + t + 1] = total(K2R + t) * tab(SL)
    gtab_ref[C2B : C2B + 1] = total(C2B) * tab(SL)
    gtab_ref[PB : PB + 1] = total(PB) * tab(SA)
    raw = dwp_ref[...]
    gtab_ref[SA : SA + 1] = jnp.sum(raw * wp_ref[...], axis=0, keepdims=True) + total(PB) * tab(PB)
    dwp_ref[...] = raw * tab(SA)
    for i in range(mlp // D):
        gtab_ref[F1B + i : F1B + i + 1] = jnp.sum(b1g_ref[:, i * D : i * D + D], axis=0, keepdims=True)
    for p in range(reduce.count):
        lanes = reduce.lanes(p)
        shard_ref[:, lanes] = reduce.buf[reduce.held(p, 4), lanes]
    for copy in stores:
        copy.wait()


def middle(tall, temp, x, dy, v, sums, wp, w1, w2, tab):
    tokens = x.shape[0]
    wide = tokens + HALO
    mlp = w1.shape[1]
    smem = pl.BlockSpec(memory_space=pltpu.SMEM)
    vmem = pl.BlockSpec(memory_space=pltpu.VMEM)
    anywhere = pl.BlockSpec(memory_space=pl.ANY)

    def f(*shape):
        return jax.ShapeDtypeStruct(shape, F32)

    def s(*shape):
        return pltpu.VMEM(shape, F32)

    def b(*shape):
        return pltpu.VMEM(shape, BF)

    padded = s(wide + 2 * COLS, D)
    return pl.pallas_call(
        middle_kernel,
        out_shape=[
            f(tokens, D),
            f(tokens, D),
            f(tokens, D),
            f(D, D),
            f(SHARD, mlp),
            f(TABLE, D),
            f(3, HD, D),
            f(3, HD, D),
            f(3, HD, D),
            f(*sums.shape[1:]),
        ],
        in_specs=[smem, smem] + [anywhere] * 3 + [vmem, vmem, anywhere, vmem, vmem],
        out_specs=[anywhere] * 3 + [vmem] * 7,
        scratch_shapes=[
            b(3 * D, D),
            b(D, 3 * D),
            b(3 * D, mlp),
            b(mlp, 3 * D),
            b(D, 9 * D),
            s(wide, D),
            s(wide, D),
            padded,
            s(wide, D),
            s(wide, D),
            padded,
            s(wide, D),
            padded,
            padded,
            b(tokens, D),
            b(tokens, D),
            b(tokens, D),
            b(tokens, D),
            b(D, tokens),
            s(8, mlp),
            s(8, mlp),
            s(8 * TABLE, D),
            s(wide, D),
            s(wide, D),
            s(wide, D),
            s(3, wide, 128),
            s(*sums.shape[1:]),
            s(2, D, mlp),
            DMA((4,)),
            DMA((3,)),
            DMA((2, 5)),
        ]
        + Reduce.scratch(mlp, (lax.axis_size("canvas") - 1).bit_length()),
        compiler_params=pltpu.CompilerParams(
            collective_id=0, has_side_effects=True, vmem_limit_bytes=60 << 20
        ),
    )(tall, temp, x, dy, v, sums, wp, w1, w2, tab)


def finish_kernel(
    tall_ref,
    temp_ref,
    x_ref,
    q_ref,
    k_ref,
    ds1_ref,
    dmx_ref,
    sums_ref,
    peer_ref,
    probs_ref,
    unit_ref,
    gprob_ref,
    w_ref,
    tab_ref,
    gtab_ref,
    dwp_ref,
    shard_ref,
    dx_ref,
    end_ref,
    town_ref,
    sum_hbm,
    wh,
    wl,
    pv,
    cv,
    ch,
    side_rows,
    acc,
    gpeer_ref,
    whole,
    dw_ref,
    otab_ref,
    end_first,
    tab_first,
    gsend,
    grecv,
    pair_sem,
    *work,
):
    step = pl.program_id(0)
    last = pl.num_programs(0) - 1
    links = Links()
    core = links.core
    gather = Gather(links, whole, sum_hbm, work)
    rows_all = 2 * pl.num_programs(0) * TILE // COLS
    spans = slots(tall_ref, core, core * (rows_all // 2), rows_all)
    start = step * TILE

    def tab(r):
        return tab_ref[r : r + 1]

    @pl.when(step == 0)
    def _():
        links.greet()
        swap = remote(gprob_ref.at[2], gpeer_ref, gsend, grecv, links.twin)
        swap.start()
        for p in range(gather.count):
            lanes = gather.lanes(p)
            whole[gather.held(p, 4), lanes] = shard_ref[:, lanes]
        gather.begin(range(gather.count))

        def part(o):
            h, l = halves(w_ref[pl.ds(o, 64)])
            wh[pl.ds(o, 64)] = h
            wl[pl.ds(o, 64)] = l

        sweep(D, 64, part)
        dw_ref[...] = jnp.zeros_like(dw_ref)
        dw_ref[1, :, D : 2 * D] = dwp_ref[...]
        acc[...] = jnp.zeros_like(acc)
        ones = group_ones()
        temp = head_row(temp_ref)
        heat = jnp.zeros((1, D), F32)
        for s in range(3):
            sums = sums_ref[s]
            grad = gprob_ref[s]
            if s == 2:
                swap.wait()
                sums = peer_ref[...]
                grad = grad + gpeer_ref[...]
            inv_q = lax.rsqrt(sums[HD : HD + 1] + EPS)
            inv_k = lax.rsqrt(sums[HD + 1 : HD + 2] + EPS)
            probs = probs_ref[s]
            unit = unit_ref[s]
            scores = probs * (grad - group_sum(probs * grad, ones))
            part_heat = jnp.sum(scores * unit, axis=0, keepdims=True)
            heat = heat + (part_heat if s < 2 else jnp.where(core == 0, part_heat, 0.0))
            pull = temp * scores
            both = pull * unit
            side_rows[8 * s : 8 * s + 1] = fold_to_row(group_sum(both, ones)) * inv_q * inv_q
            side_rows[8 * s + 1 : 8 * s + 2] = jnp.sum(both, axis=0, keepdims=True) * inv_k * inv_k
            across = slice(3 * s * D, 3 * s * D + 3 * D)
            h, l = halves(unfold(pull * row_to_fold(inv_q, ones) * inv_k))
            cv[across] = jnp.concatenate([h, h, l], axis=0)
            ch[:, across] = jnp.concatenate([h, h, l], axis=1)
            h, l = halves(unfold(probs))
            pv[across] = jnp.concatenate([h, h, l], axis=0)
        otab_ref[...] = gtab_ref[...]
        otab_ref[44:45] = heat

    masks = [span_mask(start, TILE, lo, hi) for lo, hi in spans]
    factors = slot_masks(start, TILE, spans)

    def rows_of(r):
        return sum(jnp.where(mask, side_rows[8 * s + r : 8 * s + r + 1], 0.0) for s, mask in enumerate(masks))

    def at(n, *events):
        @pl.when(step == n)
        def _():
            for event, *args in events:
                event(*args)

    q, k = q_ref[...], k_ref[...]
    dq = dot_nt(by_slot(k, factors), ch[...]) - q * rows_of(0)
    dk = dot_nn(by_slot(q, factors), cv[...]) - k * rows_of(1)
    dv = dot_nn(by_slot(dmx_ref[...], factors), pv[...])
    dqkv = jnp.concatenate([dq, dk, dv], axis=1)
    at(0, (gather.up, 3, EARLY))
    at(1, (gather.up, 2, EARLY))
    at(2, (gather.up, 1, EARLY))

    h, l = halves(dqkv)
    dn = dot_nt(h, wh[...]) + (dot_nt(l, wh[...]) + dot_nt(h, wl[...]))
    xhat, r = normalize(x_ref[...])
    nt = side((xhat * tab(N1G) + tab(N1S)).T)
    grads = dot_nn(nt, jnp.concatenate([h, h, l], axis=0))
    dw_ref[0] += grads[:, 0 : 2 * D]
    dw_ref[1, :, 0:D] += grads[:, 2 * D : 3 * D]
    dx_ref[...] = ds1_ref[...] + normalize_back(dn * tab(N1G), xhat, r)
    acc[0:8] += eights(dn * xhat)
    acc[8:16] += eights(dn)
    for i, v in enumerate((dq, dk, dv)):
        acc[16 + 8 * i : 24 + 8 * i] += eights(v)

    at(0, (gather.up, 3, LATE))
    at(1, (gather.up, 2, LATE))
    at(2, (gather.up, 1, LATE))

    @pl.when(step == last)
    def _():
        for i, r in enumerate((N1G, N1S, QB, KB, VB)):
            otab_ref[r : r + 1] = jnp.sum(acc[8 * i : 8 * i + 8], axis=0, keepdims=True)
        trows = tab_first.shape[0]
        near = pl.ds(pl.multiple_of(core * trows, 8), trows)
        far = pl.ds(pl.multiple_of((1 - core) * trows, 8), trows)
        pairs = [(otab_ref.at[far], tab_first)]
        for p in range(end_first.shape[1] // 128):
            lanes = slice(p * 128, p * 128 + 128)
            pairs.append((dw_ref.at[1 - core, :, lanes], end_first.at[:, lanes]))
        copies = [
            remote(a, b, pair_sem.at[0, i], pair_sem.at[1, i], links.twin)
            for i, (a, b) in enumerate(pairs)
        ]
        for copy in copies:
            copy.start()
        gather.up(0, EARLY)
        gather.up(0, LATE)
        for copy in copies:
            copy.wait()
        town_ref[...] = otab_ref[near] + tab_first[...]
        end_ref[...] = dw_ref[core] + end_first[...]
        gather.end()


def finish(tall, temp, x, q, k, ds1, dmx, sums, peer, probs, unit, gprob, w, tab, gtab, dwp, shard):
    tokens = x.shape[0]
    smem = pl.BlockSpec(memory_space=pltpu.SMEM)
    anywhere = pl.BlockSpec(memory_space=pl.ANY)
    row = pl.BlockSpec((TILE, D), lambda i: (i, 0))

    def whole(v):
        return pl.BlockSpec(v.shape, lambda i: (0,) * v.ndim)

    fixed = (sums, peer, probs, unit, gprob, w, tab, gtab, dwp, shard)
    return pl.pallas_call(
        finish_kernel,
        grid=(tokens // TILE,),
        out_shape=[
            jax.ShapeDtypeStruct((tokens, D), F32),
            jax.ShapeDtypeStruct((D, 2 * D), F32),
            jax.ShapeDtypeStruct((TABLE // 2, D), F32),
            jax.ShapeDtypeStruct((2, D, shard.shape[1]), F32),
        ],
        in_specs=[smem, smem] + [row] * 5 + [whole(v) for v in fixed],
        out_specs=[
            row,
            pl.BlockSpec((D, 2 * D), lambda i: (0, 0)),
            pl.BlockSpec((TABLE // 2, D), lambda i: (0, 0)),
            anywhere,
        ],
        scratch_shapes=[
            pltpu.VMEM((D, 3 * D), BF),
            pltpu.VMEM((D, 3 * D), BF),
            pltpu.VMEM((9 * D, D), BF),
            pltpu.VMEM((9 * D, D), BF),
            pltpu.VMEM((D, 9 * D), BF),
            pltpu.VMEM((24, D), F32),
            pltpu.VMEM((40, D), F32),
            pltpu.VMEM(gprob.shape[1:], F32),
            pltpu.VMEM((D, shard.shape[1]), F32),
            pltpu.VMEM((2, D, 2 * D), F32),
            pltpu.VMEM((TABLE, D), F32),
            pltpu.VMEM((D, 2 * D), F32),
            pltpu.VMEM((TABLE // 2, D), F32),
            DMA,
            DMA,
            DMA((2, 1 + 2 * D // 128)),
        ]
        + Gather.scratch(shard.shape[1]),
        compiler_params=pltpu.CompilerParams(
            collective_id=1, has_side_effects=True, vmem_limit_bytes=60 << 20
        ),
    )(tall, temp, x, q, k, ds1, dmx, *fixed)


NS_A, NS_B, NS_C = 3.4445, -4.7750, 2.0315


def times(a, b):
    return dot_nn(
        jnp.concatenate([a[0], a[1], a[0]], axis=1), jnp.concatenate([b[0], b[0], b[1]], axis=0)
    )


def inverse_norm(v):
    total = jnp.sum(jnp.sum(v * v, axis=0, keepdims=True), axis=1, keepdims=True)
    return 1.0 / (jnp.sqrt(total) + 1e-07)


def wide_kernel(
    end_hbm,
    tab_hbm,
    mid_hbm,
    m1_hbm,
    m2_hbm,
    sum_hbm,
    otab_hbm,
    orth_hbm,
    xs,
    x,
    m1,
    m2,
    xc,
    tbuf,
    tland,
    load_sem,
    tsend,
    trecv,
    tout,
    buf,
    own_sem,
    *work,
):
    links = Links()
    core = links.core
    reduce = Reduce(links, buf, buf, work[:5])
    gather = Gather(links, work[0], sum_hbm, work[5:])
    own = pltpu.make_async_copy(end_hbm, buf, own_sem)
    own.start()
    wide = m1.shape[1]
    blocks = wide // D
    trows = tbuf.shape[0]
    near = pl.ds(pl.multiple_of(core * trows, 8), trows)
    pairs = ((mid_hbm.at[core], x), (m1_hbm, m1), (m2_hbm, m2), (tab_hbm, tbuf))
    loads = [pltpu.make_async_copy(a, b, load_sem.at[i]) for i, (a, b) in enumerate(pairs)]
    for load in loads:
        load.start()
    links.greet()
    own.wait()
    reduce.launch()

    def table(n):
        return remote(tbuf, tland.at[n], tsend.at[n], trecv.at[n], links.there[n])

    def table_land(n):
        table(n).wait()
        tbuf[...] += tland[n]

    def down(s, some):
        reduce.down(s, some)
        if some is EARLY:
            table_land(s)
            if s < 3:
                table(s + 1).start()
        elif s == 3:
            for b in range(4, links.bits):
                table(b).start()
                table_land(b)
            for copy in touts:
                copy.start()
        if s == 3:
            for p in some:
                lanes = gather.lanes(p)
                gather.whole[gather.held(p, 4), lanes] = buf[gather.held(p, 4), lanes]
            gather.begin(some)

    touts = [
        pltpu.make_async_copy(tbuf, otab_hbm.at[near], tout.at[0]),
        remote(tbuf, otab_hbm.at[near], tout.at[1], tout.at[2], links.twin),
    ]

    for load in loads:
        load.wait()
    table(0).start()

    @pl.when(core == 0)
    def _():
        x[...] = MUON_KEEP * m1[...] + x[...]

    @pl.when(core == 1)
    def _():
        for b in range(blocks):
            lanes = slice(b * D, b * D + D)
            x[:, lanes] = MUON_KEEP * m2[lanes].T + x[:, lanes]

    inv = inverse_norm(x[...])
    chunks = [slice(o, o + 2 * PIECE) for o in range(0, wide, 2 * PIECE)]

    def keep(lanes, v):
        h, l = halves(v)
        xc[0:D, lanes] = h
        xc[D : 2 * D, lanes] = h
        xc[2 * D : 3 * D, lanes] = l

    def kept(lanes):
        return xc[0:D, lanes].astype(F32) + xc[2 * D : 3 * D, lanes].astype(F32)

    for lanes in chunks:
        keep(lanes, x[:, lanes] * inv)

    def gram():
        h, l = xc[0:D], xc[2 * D : 3 * D]
        return dot_nt(h, h) + (dot_nt(l, h) + dot_nt(h, l))

    def two_steps(events):
        g0 = gram()
        g = halves(g0)
        events(0)
        p0 = NS_B * g0 + NS_C * times(g, g)
        p = halves(p0)
        t = NS_A * g0 + times(p, g)
        events(1)
        g1 = NS_A * t + times(halves(t), p)
        g = halves(g1)
        p1 = NS_B * g1 + NS_C * times(g, g)
        events(2)
        both = side(NS_A * (p0 + p1) + times(halves(p1), p))
        for lanes in chunks:
            keep(lanes, NS_A * NS_A * kept(lanes) + dot_nn(both, xc[:, lanes]))
        events(3)

    def first(n):
        if n == 0:
            down(0, LATE)
        if n == 1:
            down(1, EARLY)
        if n == 2:
            down(1, LATE)
            down(2, EARLY)
        if n == 3:
            down(2, LATE)

    def second(n):
        if n == 0:
            down(3, EARLY)
        if n == 1:
            down(3, LATE)
        if n == 2:
            gather.up(3, EARLY)
        if n == 3:
            gather.up(3, LATE)
            gather.up(2, EARLY)

    down(0, EARLY)
    two_steps(first)
    two_steps(second)
    g0 = gram()
    g = halves(g0)
    gather.up(2, LATE)
    last = side(NS_B * g0 + NS_C * times(g, g))
    for lanes in chunks:
        x[:, lanes] = NS_A * kept(lanes) + dot_nn(last, xc[:, lanes])
    gather.up(1, EARLY)

    @pl.when(core == 0)
    def _():
        for b in range(blocks):
            xs[b] = x[:, b * D : b * D + D]

    @pl.when(core == 1)
    def _():
        for b in range(blocks):
            xs[b] = x[:, b * D : b * D + D].T

    orth = [
        pltpu.make_async_copy(xs, orth_hbm.at[core], tout.at[3]),
        remote(xs, orth_hbm.at[core], tout.at[4], tout.at[5], links.twin),
    ]
    for copy in orth:
        copy.start()
    gather.up(1, LATE)
    gather.up(0, EARLY)
    gather.up(0, LATE)
    gather.end()
    for copy in touts + orth:
        copy.wait()


def wide_blocks(end, tab, mid, m1, m2):
    bits = (lax.axis_size("canvas") - 1).bit_length()
    anywhere = pl.BlockSpec(memory_space=pl.ANY)
    blocks = m1.shape[1] // D
    return pl.pallas_call(
        wide_kernel,
        out_shape=[
            jax.ShapeDtypeStruct((2,) + end.shape, F32),
            jax.ShapeDtypeStruct((TABLE, D), F32),
            jax.ShapeDtypeStruct((2, blocks, D, D), F32),
        ],
        in_specs=[anywhere] * 5,
        out_specs=[anywhere] * 3,
        scratch_shapes=[
            pltpu.VMEM((blocks, D, D), F32),
            pltpu.VMEM(m1.shape, F32),
            pltpu.VMEM(m1.shape, F32),
            pltpu.VMEM(m2.shape, F32),
            pltpu.VMEM((3 * D, m1.shape[1]), BF),
            pltpu.VMEM((TABLE // 2, D), F32),
            pltpu.VMEM((bits, TABLE // 2, D), F32),
            DMA((4,)),
            DMA((bits,)),
            DMA((bits,)),
            DMA((6,)),
            pltpu.VMEM(end.shape, F32),
            DMA,
        ]
        + Reduce.scratch(end.shape[1], bits)
        + Gather.scratch(end.shape[1]),
        compiler_params=pltpu.CompilerParams(
            collective_id=2, has_side_effects=True, vmem_limit_bytes=60 << 20
        ),
    )(end, tab, mid, m1, m2)


def muon(w, orth, large):
    return w * (1.0 - MUON_RATE * DECAY) - MUON_RATE * 0.2 * math.sqrt(large) * orth


def square_kernel(
    end_hbm,
    mid_hbm,
    wide_hbm,
    mq_hbm,
    mp_hbm,
    m1_hbm,
    m2_hbm,
    w1_hbm,
    w2_hbm,
    out_hbm,
    dx_hbm,
    gq_out,
    gp_out,
    g1_out,
    g2_out,
    nq_out,
    np_out,
    n1_out,
    n2_out,
    w1_out,
    w2_out,
    c1_out,
    c2_out,
    out_out,
    dx_out,
    orth_hbm,
    end,
    mid,
    nat,
    mq,
    mp,
    m1,
    m2,
    w1,
    w2,
    c1,
    c2,
    wide,
    out,
    dx,
    xh,
    xl,
    xs,
    in_sem,
    out_sem,
):
    core = lax.axis_index("rows")
    mlp = m1.shape[1]
    blocks = mlp // D
    pairs = (
        (end_hbm, end),
        (mq_hbm, mq),
        (mp_hbm, mp),
        (mid_hbm, mid),
        (m1_hbm, m1),
        (m2_hbm, m2),
        (w1_hbm, w1),
        (w2_hbm, w2),
        (wide_hbm, wide),
        (out_hbm, out),
        (dx_hbm, dx),
    )
    loads = [pltpu.make_async_copy(a, b, in_sem.at[i]) for i, (a, b) in enumerate(pairs)]
    for load in loads:
        load.start()
    for load in loads[0:3]:
        load.wait()
    outs = (
        (end.at[0], gq_out.at[:, 0 : 2 * D]),
        (end.at[1, :, 0:D], gq_out.at[:, 2 * D : 3 * D]),
        (end.at[1, :, D : 2 * D], gp_out),
        (mq, nq_out),
        (mp, np_out),
        (mid.at[0], g1_out),
        (nat, g2_out),
        (m1, n1_out),
        (m2, n2_out),
        (out, out_out),
        (dx, dx_out),
        (w1, w1_out),
        (w2, w2_out),
        (c1, c1_out),
        (c2, c2_out),
        (xs, orth_hbm),
    )

    def store(*which):
        return [pltpu.make_async_copy(*outs[n], out_sem.at[n]) for n in which]

    def send(*which):
        for copy in store(*which):
            copy.start()

    send(0, 1, 2)

    def small(o):
        rows = pl.ds(o, 128)
        mq[rows, 0 : 2 * D] = MUON_KEEP * mq[rows, 0 : 2 * D] + end[0, rows]
        mq[rows, 2 * D : 3 * D] = MUON_KEEP * mq[rows, 2 * D : 3 * D] + end[1, rows, 0:D]
        mp[rows] = MUON_KEEP * mp[rows] + end[1, rows, D : 2 * D]

    sweep(D, 128, small)
    send(3, 4)

    def keep(b, v):
        xh[b], xl[b] = halves(v)

    @pl.when(core == 0)
    def _():
        xs[0] = mq[:, 0:D]
        xs[1] = mq[:, D : 2 * D]

    @pl.when(core == 1)
    def _():
        xs[0] = mq[:, 2 * D : 3 * D]
        xs[1] = mp[...]

    for b in range(2):
        keep(b, xs[b] * inverse_norm(xs[b]))

    def step(i, carry):
        x = [(xh[b], xl[b]) for b in range(2)]
        g = [
            dot_nt(jnp.concatenate([h, l, h], axis=1), jnp.concatenate([h, h, l], axis=1))
            for h, l in x
        ]
        pairs = [halves(v) for v in g]
        p = [NS_B * v + NS_C * times(w, w) for v, w in zip(g, pairs)]
        pairs = [halves(v) for v in p]
        for b in range(2):
            h, l = x[b]
            keep(b, NS_A * (h.astype(F32) + l.astype(F32)) + times(pairs[b], x[b]))
        pl.when(i == 1)(moments)
        pl.when(i == 2)(weights)
        return carry

    def moments():
        for load in loads[3:6]:
            load.wait()
        send(5)
        for b in range(blocks):
            nat[b * D : b * D + D] = mid[1, :, b * D : b * D + D].T
        send(6)

        def large(o):
            rows = pl.ds(o, 64)
            m1[rows] = MUON_KEEP * m1[rows] + mid[0, rows]

        sweep(D, 64, large)
        send(7)

        def larger(o):
            rows = pl.ds(o, 256)
            m2[rows] = MUON_KEEP * m2[rows] + nat[rows]

        sweep(mlp, 256, larger)
        send(8)

    def weights():
        for load in loads[6:]:
            load.wait()
        send(9, 10)
        for b in range(blocks):
            at = slice(b * D, b * D + D)
            new = muon(w1[:, at], wide[0, b], mlp)
            w1[:, at] = new
            c1[:, at] = new.astype(BF)
            new = muon(w2[at], wide[1, b], mlp)
            w2[at] = new
            c2[at] = new.astype(BF)
        send(11, 12, 13, 14)

    lax.fori_loop(0, 5, step, 0)
    for b in range(2):
        xs[b] = xh[b].astype(F32) + xl[b].astype(F32)
    send(15)
    for copy in store(*range(len(outs))):
        copy.wait()


def square_blocks(end, mid, wide, mq, mp, m1, m2, w1, w2, out, dx):
    anywhere = pl.BlockSpec(memory_space=pl.ANY)

    def like(v, kind=F32):
        return jax.ShapeDtypeStruct(v.shape, kind)

    def room(v, kind=F32):
        return pltpu.VMEM(v.shape, kind)

    return pl.pallas_call(
        square_kernel,
        out_shape=[like(v) for v in (mq, mp, m1, m2, mq, mp, m1, m2, w1, w2)]
        + [like(w1, BF), like(w2, BF), like(out), like(dx), jax.ShapeDtypeStruct((2, D, D), F32)],
        in_specs=[anywhere] * 11,
        out_specs=[anywhere] * 15,
        scratch_shapes=[room(v) for v in (end, mid, m2, mq, mp, m1, m2, w1, w2)]
        + [room(w1, BF), room(w2, BF), room(wide), room(out), room(dx)]
        + [
            pltpu.VMEM((2, D, D), BF),
            pltpu.VMEM((2, D, D), BF),
            pltpu.VMEM((2, D, D), F32),
            DMA((11,)),
            DMA((16,)),
        ],
        compiler_params=pltpu.CompilerParams(vmem_limit_bytes=60 << 20),
    )(end, mid, wide, mq, mp, m1, m2, w1, w2, out, dx)


def trade_kernel(own_ref, peer_ref, send_sem, recv_sem):
    core = lax.axis_index("rows")
    twin = {"rows": 1 - core}
    barrier = pltpu.get_barrier_semaphore()
    pl.semaphore_signal(barrier, inc=1, device_id=twin, device_id_type=MESH_ID)
    pl.semaphore_wait(barrier, 1)
    copy = remote(own_ref, peer_ref, send_sem, recv_sem, twin)
    copy.start()
    copy.wait()


def trade(own):
    anywhere = pl.BlockSpec(memory_space=pl.ANY)
    return pl.pallas_call(
        trade_kernel,
        out_shape=jax.ShapeDtypeStruct(own.shape, F32),
        in_specs=[anywhere],
        out_specs=anywhere,
        scratch_shapes=[DMA, DMA],
        compiler_params=pltpu.CompilerParams(collective_id=3, has_side_effects=True),
    )(own)


def moment_step(current, one, two, gradient):
    first = BETA1 * one + (1.0 - BETA1) * gradient
    second = BETA2 * two + (1.0 - BETA2) * gradient * gradient
    fix_one = 1.0 - BETA1**STEP
    fix_two = 1.0 - BETA2**STEP
    updated = current - ADAM_RATE * (first / fix_one) / (jnp.sqrt(second / fix_two) + ADAM_FLOOR)
    return first, second, updated


def update_kernel(
    count,
    temp_ref,
    heat_one_ref,
    heat_two_ref,
    own_ref,
    peer_ref,
    wq_ref,
    wp_ref,
    tab_ref,
    one_ref,
    two_ref,
    gtab_ref,
    nq_ref,
    np_ref,
    cq_ref,
    cp_ref,
    first_ref,
    second_ref,
    small_ref,
    heat_first_ref,
    heat_second_ref,
    heat_ref,
    rms_ref,
):
    lower = lax.axis_index("rows") == 0
    own, peer = own_ref[...], peer_ref[...]
    low, high = jnp.where(lower, own, peer), jnp.where(lower, peer, own)
    for i, orth in enumerate((low[0], low[1], high[0])):
        lanes = slice(i * D, i * D + D)
        new = muon(wq_ref[:, lanes], orth, D)
        nq_ref[:, lanes] = new
        cq_ref[:, lanes] = new.astype(BF)
    new = muon(wp_ref[...], high[1], D)
    np_ref[...] = new
    cp_ref[...] = new.astype(BF)
    first, second, small = moment_step(tab_ref[...], one_ref[...], two_ref[...], gtab_ref[0:SMALL])
    first_ref[...] = first
    second_ref[...] = second
    small_ref[...] = small

    @pl.when(pl.program_id(0) == 0)
    def _():
        head = lax.broadcasted_iota(jnp.int32, (HEADS, D), 0)
        lane = lax.broadcasted_iota(jnp.int32, (HEADS, D), 1) // HD
        heat = jnp.sum(jnp.where(head == lane, gtab_ref[44:45], 0.0), axis=1, keepdims=True)
        head = lax.broadcasted_iota(jnp.int32, (HEADS, 1), 0)

        def column(ref):
            v = jnp.where(head == 0, ref[0], 0.0)
            for h in range(1, HEADS):
                v = jnp.where(head == h, ref[h], v)
            return v

        results = moment_step(column(temp_ref), column(heat_one_ref), column(heat_two_ref), heat)
        for ref, v in zip((heat_first_ref, heat_second_ref, heat_ref), results):
            for h in range(HEADS):
                ref[h] = v[h, 0]
        rms = jnp.sqrt(jnp.sum(gtab_ref[40:44], axis=1, keepdims=True) / count)
        for n in range(4):
            rms_ref[n] = rms[n, 0]


def update(count, temp, heat_one, heat_two, own, peer, wq, wp, tab, one, two, gtab):
    steps = 3
    piece = D // steps

    def rows(v):
        return pl.BlockSpec((piece, v.shape[1]), lambda i: (i, 0))

    def whole(v):
        return pl.BlockSpec(v.shape, lambda i: (0, 0))

    square = pl.BlockSpec((2, piece, D), lambda i: (0, i, 0))
    weights = (wq, wp)
    smem = pl.BlockSpec(memory_space=pltpu.SMEM)
    return pl.pallas_call(
        functools.partial(update_kernel, count),
        grid=(steps,),
        out_shape=[jax.ShapeDtypeStruct(w.shape, F32) for w in weights]
        + [jax.ShapeDtypeStruct(w.shape, BF) for w in weights]
        + [jax.ShapeDtypeStruct(tab.shape, F32)] * 3
        + [jax.ShapeDtypeStruct(temp.shape, F32)] * 3
        + [jax.ShapeDtypeStruct((4,), F32)],
        in_specs=[smem] * 3
        + [square, square]
        + [rows(w) for w in weights]
        + [whole(v) for v in (tab, one, two, gtab)],
        out_specs=[rows(w) for w in weights] * 2 + [whole(tab)] * 3 + [smem] * 4,
        compiler_params=pltpu.CompilerParams(vmem_limit_bytes=60 << 20),
    )(temp, heat_one, heat_two, own, peer, *weights, tab, one, two, gtab)


def on_device(
    x4, dy4, tall, wqkv, wp, w1, w2, mqkv, mp, m1, m2, tab, tab_one, tab_two, temp, temp_one, temp_two
):
    shape = x4.shape
    tokens = shape[1] * shape[2]
    x = x4.reshape(tokens, D)
    dy = dy4.reshape(tokens, D)
    q, k, v, sums = project(tall, x, wqkv, tab)
    out, ds1, dmx, dwp, shard, gtab, probs, unit, gprob, joint = middle(
        tall, temp, x, dy, v, sums, wp, w1, w2, tab
    )
    dx, end, gtab, mid = finish(
        tall, temp, x, q, k, ds1, dmx, sums, joint, probs, unit, gprob, wqkv, tab, gtab, dwp, shard
    )
    end, gtab, wide = wide_blocks(end, gtab, mid, m1, m2)
    *grads, new_1, new_2, copy_1, copy_2, out, dx, square = square_blocks(
        end, mid, wide, mqkv, mp, m1, m2, w1, w2, out, dx
    )
    count = tokens * D * lax.axis_size("rows") * lax.axis_size("canvas")
    new_q, new_p, copy_q, copy_p, *small = update(
        count, temp, temp_one, temp_two, square, trade(square), wqkv, wp, tab, tab_one, tab_two, gtab
    )
    new = (new_q, new_p, new_1, new_2, copy_q, copy_p, copy_1, copy_2)
    return (out.reshape(shape), dx.reshape(shape), *grads, *new, *small)


def solution(mesh):
    split = P("canvas", "rows", None, None)
    return jax.shard_map(
        on_device,
        mesh=mesh,
        in_specs=(split, split, P("canvas", None)) + (P(),) * 14,
        out_specs=(split, split) + (P(),) * 23,
        check_vma=False,
    )
```

```python
import functools
import math

import jax
import jax.numpy as jnp
from jax import lax
from jax.experimental import pallas as pl
from jax.experimental.pallas import tpu as pltpu
from jax.sharding import PartitionSpec as P

BF = jnp.bfloat16
F32 = jnp.float32
MESH_ID = pl.DeviceIdType.MESH

EPS = 1e-06
ROOT_HALF = 1.0 / math.sqrt(2.0)
ROOT_TWOPI = 1.0 / math.sqrt(2.0 * math.pi)
STEP = 10
MUON_RATE = 0.2
MUON_KEEP = 0.95
DECAY = 0.01
ADAM_RATE = 0.2
BETA1 = 0.9
BETA2 = 0.95
ADAM_FLOOR = 1e-08

HEADS = 8
HD = 48
D = HEADS * HD
COLS = 32
HALO = 4 * COLS
TILE = 256

N1G, N1S, N3G, N3S, N2G, N2S, SA, SL, SM, QB, KB, VB, PB, C1B, BG, BS, C2B, F2B = range(18)
F1B, K1R, K2R = 18, 22, 31
SMALL = 40
TABLE = 48


def halves(v):
    hi = v.astype(BF)
    return hi, (v - hi.astype(F32)).astype(BF)


def side(v):
    h, l = halves(v)
    return jnp.concatenate([h, l, h], axis=1)


def dot_nn(a, b):
    return lax.dot_general(a, b, (((1,), (0,)), ((), ())), preferred_element_type=F32)


def dot_nt(a, b):
    return lax.dot_general(a, b, (((1,), (1,)), ((), ())), preferred_element_type=F32)


def normalize(v):
    mean = jnp.mean(v, axis=1, keepdims=True)
    c = v - mean
    r = lax.rsqrt(jnp.mean(c * c, axis=1, keepdims=True) + EPS)
    return c * r, r


def normalize_back(e, xhat, r):
    return r * (
        e - jnp.mean(e, axis=1, keepdims=True) - xhat * jnp.mean(e * xhat, axis=1, keepdims=True)
    )


def gelu_parts(v):
    phi = 0.5 * (1.0 + lax.erf(v * ROOT_HALF))
    return v * phi, phi + v * jnp.exp(-0.5 * v * v) * ROOT_TWOPI


def eights(v):
    total = v[0:8]
    for i in range(8, v.shape[0], 8):
        total = total + v[i : i + 8]
    return total


def sweep(count, size, body):
    def one(i, carry):
        body(pl.multiple_of(i * size, size))
        return carry

    lax.fori_loop(0, count // size, one, 0)


def image_ends(tall_ref):
    e0 = tall_ref[0, 0]
    e1 = e0 + tall_ref[0, 1]
    return e0, e1, e1 + tall_ref[0, 2]


def slots(tall_ref, core, first_row, rows_all):
    e0, e1, e2 = image_ends(tall_ref)
    low = (jnp.where(core == 0, 0, e2), jnp.where(core == 0, e0, 0), e1)
    high = (jnp.where(core == 0, e0, rows_all), jnp.where(core == 0, e1, 0), e2)
    return [((a - first_row) * COLS, (b - first_row) * COLS) for a, b in zip(low, high)]


def span_mask(start, rows, lo, hi):
    token = start + lax.broadcasted_iota(jnp.int32, (rows, D), 0)
    return (token >= lo) & (token < hi)


def slot_masks(start, rows, spans):
    return [jnp.where(span_mask(start, rows, lo, hi), 1.0, 0.0).astype(BF) for lo, hi in spans]


def by_slot(v, masks):
    h, l = halves(v)
    parts = []
    for mask in masks:
        hm = h * mask
        parts += [hm, l * mask, hm]
    return parts


def whole_and_far(parts):
    return jnp.concatenate(parts, axis=1), jnp.concatenate([p[:, 128:] for p in parts], axis=1)


def mix_nt(parts, ref):
    every, far = whole_and_far(parts)
    corner = [ref[256:D, n * D + 128 : n * D + D] for n in range(len(parts))]
    return jnp.concatenate(
        [dot_nt(every, ref[0:256]), dot_nt(far, jnp.concatenate(corner, axis=1))], axis=1
    )


def mix_nn(parts, ref):
    every, far = whole_and_far(parts)
    corner = [ref[n * D + 128 : n * D + D, 256:D] for n in range(len(parts))]
    return jnp.concatenate(
        [dot_nn(every, ref[:, 0:256]), dot_nn(far, jnp.concatenate(corner, axis=0))], axis=1
    )


def slots_below(v, masks):
    h, l = halves(v)
    high = jnp.concatenate([h * mask for mask in masks], axis=1)
    return jnp.concatenate([high, high, jnp.concatenate([l * mask for mask in masks], axis=1)], axis=0)


def lane_head():
    return lax.broadcasted_iota(jnp.int32, (HD, D), 1) // HD


def lane_slot():
    return lax.broadcasted_iota(jnp.int32, (HD, D), 1) % HD


def fold(full):
    head = lane_head()
    total = jnp.where(head == 0, full[0:HD], 0.0)
    for h in range(1, HEADS):
        total = total + jnp.where(head == h, full[h * HD : h * HD + HD], 0.0)
    return total


def unfold(small):
    head = lane_head()
    return jnp.concatenate([jnp.where(head == h, small, 0.0) for h in range(HEADS)], axis=0)


def group_ones():
    a = lax.broadcasted_iota(jnp.int32, (D, D), 0) // HD
    b = lax.broadcasted_iota(jnp.int32, (D, D), 1) // HD
    return jnp.where(a == b, 1.0, 0.0).astype(BF)


def group_sum(v, ones):
    h = v.astype(BF)
    rest = v - h.astype(F32)
    m = rest.astype(BF)
    l = (rest - m.astype(F32)).astype(BF)
    return dot_nn(h, ones) + (dot_nn(m, ones) + dot_nn(l, ones))


def row_to_fold(row, ones):
    slot = lax.broadcasted_iota(jnp.int32, (HD, D), 0)
    return group_sum(jnp.where(lane_slot() == slot, jnp.broadcast_to(row, (HD, D)), 0.0), ones)


def fold_to_row(small):
    slot = lax.broadcasted_iota(jnp.int32, (HD, D), 0)
    return jnp.sum(jnp.where(lane_slot() == slot, small, 0.0), axis=0, keepdims=True)


def head_row(temp_ref):
    head = lax.broadcasted_iota(jnp.int32, (1, D), 1) // HD
    row = jnp.where(head == 0, temp_ref[0], 0.0)
    for h in range(1, HEADS):
        row = row + jnp.where(head == h, temp_ref[h], 0.0)
    return row


def project_kernel(tall_ref, x_ref, w_ref, tab_ref, q_ref, k_ref, v_ref, sums_ref, wcat, cross):
    step = pl.program_id(0)
    core = lax.axis_index("rows")
    rows_all = 2 * pl.num_programs(0) * TILE // COLS
    spans = slots(tall_ref, core, core * (rows_all // 2), rows_all)
    start = step * TILE

    @pl.when(step == 0)
    def _():
        def part(o):
            h, l = halves(w_ref[pl.ds(o, 64)])
            wcat[pl.ds(o, 64)] = h
            wcat[pl.ds(D + o, 64)] = h
            wcat[pl.ds(2 * D + o, 64)] = l

        sweep(D, 64, part)
        cross[...] = jnp.zeros_like(cross)
        sums_ref[...] = jnp.zeros_like(sums_ref)

    xhat, _ = normalize(x_ref[...])
    lhs = side(xhat * tab_ref[N1G : N1G + 1] + tab_ref[N1S : N1S + 1])
    q = dot_nn(lhs, wcat[:, 0:D]) + tab_ref[QB : QB + 1]
    q_ref[...] = q
    k = dot_nn(lhs, wcat[:, D : 2 * D]) + tab_ref[KB : KB + 1]
    k_ref[...] = k
    v_ref[...] = dot_nn(lhs, wcat[:, 2 * D : 3 * D]) + tab_ref[VB : VB + 1]
    cross[...] += dot_nn(side(q.T), slots_below(k, slot_masks(start, TILE, spans)))
    for s, (lo, hi) in enumerate(spans):
        mask = span_mask(start, TILE, lo, hi)
        for n, v in enumerate((q, k)):
            row = HD + n
            sums_ref[s, row : row + 1] += jnp.sum(jnp.where(mask, v * v, 0.0), axis=0, keepdims=True)

    @pl.when(step == pl.num_programs(0) - 1)
    def _():
        for s in range(3):
            sums_ref[s, 0:HD] = fold(cross[:, s * D : s * D + D])


def project(tall, x, w, tab):
    tokens = x.shape[0]
    row = pl.BlockSpec((TILE, D), lambda i: (i, 0))
    return pl.pallas_call(
        project_kernel,
        grid=(tokens // TILE,),
        out_shape=[jax.ShapeDtypeStruct((tokens, D), F32)] * 3
        + [jax.ShapeDtypeStruct((3, HD + 8, D), F32)],
        in_specs=[
            pl.BlockSpec(memory_space=pltpu.SMEM),
            row,
            pl.BlockSpec((D, 3 * D), lambda i: (0, 0)),
            pl.BlockSpec((SMALL, D), lambda i: (0, 0)),
        ],
        out_specs=[row, row, row, pl.BlockSpec((3, HD + 8, D), lambda i: (0, 0, 0))],
        scratch_shapes=[pltpu.VMEM((3 * D, 3 * D), BF), pltpu.VMEM((D, 3 * D), F32)],
        compiler_params=pltpu.CompilerParams(vmem_limit_bytes=60 << 20),
    )(tall, x, w, tab)


ORDERS = ((0, 1, 2, 3), (1, 2, 0, 3), (2, 0, 1, 3))
EARLY, LATE = range(0, 3), range(3, 6)
PIECE = 256
SHARD = D // 16
DMA = pltpu.SemaphoreType.DMA


class Links:
    def __init__(self):
        self.core = lax.axis_index("rows")
        chip = lax.axis_index("canvas")
        self.bits = (lax.axis_size("canvas") - 1).bit_length()
        self.mine = [lax.rem(lax.div(chip, 1 << b), 2) for b in range(self.bits)]
        self.there = [{"canvas": chip + (1 - 2 * m) * (1 << b)} for b, m in enumerate(self.mine)]
        self.twin = {"rows": 1 - self.core}

    def call(self):
        barrier = pltpu.get_barrier_semaphore()
        for other in [self.twin] + self.there:
            pl.semaphore_signal(barrier, inc=1, device_id=other, device_id_type=MESH_ID)

    def answer(self):
        pl.semaphore_wait(pltpu.get_barrier_semaphore(), self.bits + 1)

    def greet(self):
        self.call()
        self.answer()


def remote(src, dst, send, recv, other):
    return pltpu.make_async_remote_copy(
        src_ref=src,
        dst_ref=dst,
        send_sem=send,
        recv_sem=recv,
        device_id=other,
        device_id_type=MESH_ID,
    )


class Pieces:
    count = 6

    def __init__(self, links, lanes):
        self.links = links
        self.width = lanes // self.count

    def lanes(self, p):
        return slice(p * self.width, p * self.width + self.width)

    def bit(self, p, s):
        return ORDERS[p % 3][s]

    def start(self, p, s):
        at = 0
        for t in range(s):
            at = at + self.links.mine[self.bit(p, t)] * (D >> (t + 1))
        return at

    def held(self, p, s):
        return pl.ds(pl.multiple_of(self.start(p, s), 8), D >> s)


class Reduce(Pieces):
    def __init__(self, links, src, buf, work):
        super().__init__(links, src.shape[-1])
        self.src, self.buf = src, buf
        self.first, self.land, self.pair_sem, self.send_sem, self.recv_sem = work

    @classmethod
    def scratch(cls, lanes, bits):
        steps = max(bits, 4)
        return [
            pltpu.VMEM((D, lanes), F32),
            pltpu.VMEM((D - SHARD + (steps - 4) * SHARD, lanes), F32),
            DMA((2, cls.count)),
            DMA((cls.count, steps)),
            DMA((cls.count, steps)),
        ]

    def add(self, p, rows, src, src_rows):
        lanes = self.lanes(p)
        self.buf[rows, lanes] += src[src_rows, lanes]

    def pair(self, p):
        lanes = self.lanes(p)
        return remote(
            self.src.at[1 - self.links.core, :, lanes],
            self.first.at[:, lanes],
            self.pair_sem.at[0, p],
            self.pair_sem.at[1, p],
            self.links.twin,
        )

    def move(self, p, s):
        b = self.bit(p, s)
        half = D >> (s + 1)
        away = pl.multiple_of(self.start(p, s) + (1 - self.links.mine[b]) * half, 8)
        lanes = self.lanes(p)
        return remote(
            self.buf.at[pl.ds(away, half), lanes],
            self.land.at[pl.ds(D - (D >> s), half), lanes],
            self.send_sem.at[p, s],
            self.recv_sem.at[p, s],
            self.links.there[b],
        )

    def begin(self):
        for p in range(self.count):
            self.pair(p).start()

    def join(self, some):
        for p in some:
            self.pair(p).wait()
            self.add(p, pl.ds(0, D), self.first, pl.ds(0, D))
            self.move(p, 0).start()

    def launch(self):
        for p in range(self.count):
            self.move(p, 0).start()

    def down(self, s, some, last=3):
        for p in some:
            self.move(p, s).wait()
            self.add(p, self.held(p, s + 1), self.land, pl.ds(D - (D >> s), D >> (s + 1)))
            if s < last:
                self.move(p, s + 1).start()
        if s == 3:
            for b in range(4, self.links.bits):
                self.swap(b, some)

    def swap(self, b, some):
        at = pl.ds(D - SHARD + (b - 4) * SHARD, SHARD)
        copies = {}
        for p in some:
            lanes = self.lanes(p)
            copies[p] = remote(
                self.buf.at[self.held(p, 4), lanes],
                self.land.at[at, lanes],
                self.send_sem.at[p, b],
                self.recv_sem.at[p, b],
                self.links.there[b],
            )
            copies[p].start()
        for p in some:
            copies[p].wait()
            self.add(p, self.held(p, 4), self.land, at)


class Gather(Pieces):
    def __init__(self, links, whole, dst, work):
        super().__init__(links, whole.shape[1])
        self.whole, self.dst = whole, dst
        self.send_sem, self.recv_sem, self.out_sem = work

    @classmethod
    def scratch(cls, lanes):
        return [DMA((cls.count, 4)), DMA((cls.count, 4)), DMA((2, 3, cls.count))]

    def back(self, p, s):
        view = self.whole.at[self.held(p, s + 1), self.lanes(p)]
        return remote(
            view,
            view,
            self.send_sem.at[p, s],
            self.recv_sem.at[p, s],
            self.links.there[self.bit(p, s)],
        )

    def outs(self, p, n):
        mine = self.links.mine[self.bit(p, 0)]
        half = D // 2
        at = pl.multiple_of(half * (mine if n == 0 else 1 - mine), 8)
        rows = pl.ds(at, half)
        src = self.whole.at[rows, self.lanes(p)]
        dst = self.dst.at[self.links.core, rows, self.lanes(p)]
        sem = self.out_sem.at[n]
        return (
            pltpu.make_async_copy(src, dst, sem.at[0, p]),
            remote(src, dst, sem.at[1, p], sem.at[2, p], self.links.twin),
        )

    def begin(self, some):
        for p in some:
            self.back(p, 3).start()

    def up(self, s, some):
        for p in some:
            self.back(p, s).wait()
            if s > 0:
                self.back(p, s - 1).start()
            if s < 2:
                for copy in self.outs(p, 1 - s):
                    copy.start()

    def end(self):
        for n in range(2):
            for p in range(self.count):
                for copy in self.outs(p, n):
                    copy.wait()


class Turn(Pieces):
    def __init__(self, links, rest, whole, work):
        super().__init__(links, whole.shape[1])
        self.rest, self.whole = rest, whole
        self.land, self.send_sem, self.recv_sem = work

    @classmethod
    def scratch(cls, lanes, bits):
        steps = max(bits, 4) - 3
        return [
            pltpu.VMEM((steps * SHARD, lanes), F32),
            DMA((cls.count, steps)),
            DMA((cls.count, steps)),
        ]

    def move(self, p, n):
        lanes = self.lanes(p)
        if n == 0:
            b = self.bit(p, 3)
            at = pl.multiple_of((1 - self.links.mine[b]) * SHARD, 8)
            src = self.rest.at[pl.ds(at, SHARD), lanes]
        else:
            b = 3 + n
            src = self.whole.at[self.held(p, 4), lanes]
        return remote(
            src,
            self.land.at[n * SHARD : n * SHARD + SHARD, lanes],
            self.send_sem.at[p, n],
            self.recv_sem.at[p, n],
            self.links.there[b],
        )

    def begin(self):
        for p in range(self.count):
            self.move(p, 0).start()

    def end(self, some):
        for p in some:
            lanes = self.lanes(p)
            at = pl.multiple_of(self.links.mine[self.bit(p, 3)] * SHARD, 8)
            self.move(p, 0).wait()
            self.whole[self.held(p, 4), lanes] = (
                self.rest[pl.ds(at, SHARD), lanes] + self.land[0:SHARD, lanes]
            )
        for n in range(1, self.links.bits - 3):
            for p in some:
                self.move(p, n).start()
            for p in some:
                lanes = self.lanes(p)
                self.move(p, n).wait()
                self.whole[self.held(p, 4), lanes] += self.land[n * SHARD : n * SHARD + SHARD, lanes]


def row_flags(tall_ref, rows_all):
    ends = image_ends(tall_ref)

    def above(row):
        first = (row == 0) | (row == ends[0]) | (row == ends[1]) | (row == ends[2])
        return jnp.where(first, 0.0, 1.0)

    def below(row):
        return jnp.where(row + 1 == rows_all, 0.0, above(row + 1))

    return above, below


def middle_kernel(
    tall_ref,
    temp_ref,
    x_hbm,
    dy_hbm,
    v_hbm,
    sums_ref,
    wp_ref,
    w1_hbm,
    w2_ref,
    tab_ref,
    out_hbm,
    ds1_hbm,
    dmx_hbm,
    dwp_ref,
    shard_ref,
    gtab_ref,
    probs_ref,
    unit_ref,
    gprob_ref,
    joint_ref,
    wpv,
    wph,
    w1c,
    w2c,
    pcat,
    mixed,
    s1,
    li,
    act,
    slope,
    mid,
    s2,
    ds2,
    gp,
    n2c,
    dzc,
    b1_ref,
    b1g_ref,
    acc,
    cross,
    x_ref,
    dy_ref,
    v_ref,
    flags,
    nt,
    dt,
    peer_ref,
    dw_ref,
    load_sem,
    store_sem,
    edge_sem,
    *work,
):
    links = Links()
    core = links.core
    wide = x_ref.shape[0]
    tokens = wide - HALO
    dw1_ref, dw2_ref = dw_ref.at[0], dw_ref.at[1]
    reduce = Reduce(links, dw_ref, dw_ref.at[core], work)
    w1_ref = work[0]
    lo_ = x_ref
    own = pl.ds(pl.multiple_of(core * HALO, HALO), tokens)
    pairs = ((w1_hbm, w1_ref), (v_hbm, v_ref.at[own]), (x_hbm, x_ref.at[own]), (dy_hbm, dy_ref.at[own]))
    loads = [pltpu.make_async_copy(a, b, load_sem.at[i]) for i, (a, b) in enumerate(pairs)]
    for load in loads:
        load.start()
    links.call()
    edge = pl.ds(pl.multiple_of((1 - core) * (tokens - HALO), HALO), HALO)
    far = pl.ds(pl.multiple_of(core * tokens, HALO), HALO)
    pairs = (
        (sums_ref.at[2], peer_ref),
        (v_hbm.at[edge], v_ref.at[far]),
        (x_hbm.at[edge], x_ref.at[far]),
        (dy_hbm.at[edge], dy_ref.at[far]),
    )
    edges = [
        remote(a, b, edge_sem.at[0, i], edge_sem.at[1, i], links.twin)
        for i, (a, b) in enumerate(pairs)
    ]
    own_rows = tokens // COLS
    rows_wide = wide // COLS
    rows_all = 2 * own_rows
    first_row = core * (own_rows - HALO // COLS)
    own_off = pl.multiple_of(core * HALO, HALO)
    mlp = w1_hbm.shape[1]
    spans = slots(tall_ref, core, first_row, rows_all)
    above, below = row_flags(tall_ref, rows_all)

    def tab(r):
        return tab_ref[r : r + 1]

    def is_own(row):
        return (row >= core * (HALO // COLS)) & (row < core * (HALO // COLS) + own_rows)

    loads[0].wait()

    def part_1(o):
        rows = pl.ds(o, 64)
        h, l = halves(w1_ref[rows])
        w1c[rows] = h
        w1c[pl.ds(D + o, 64)] = h
        w1c[pl.ds(2 * D + o, 64)] = l

    sweep(D, 64, part_1)
    links.answer()
    for copy in edges:
        copy.start()

    def part_p(o):
        rows = pl.ds(o, 192)
        h, l = halves(wp_ref[rows])
        wpv[rows] = h
        wpv[pl.ds(D + o, 192)] = h
        wpv[pl.ds(2 * D + o, 192)] = l
        wph[rows, 0:D] = h
        wph[rows, D : 2 * D] = h
        wph[rows, 2 * D : 3 * D] = l

    sweep(D, 192, part_p)

    def part_2(o):
        rows = pl.ds(o, 256)
        h, l = halves(w2_ref[rows])
        w2c[rows, 0:D] = h
        w2c[rows, D : 2 * D] = h
        w2c[rows, 2 * D : 3 * D] = l

    sweep(mlp, 256, part_2)

    edges[0].wait()
    ones = group_ones()
    temp = head_row(temp_ref)
    for s in range(3):
        sums = sums_ref[s]
        if s == 2:
            sums = sums + peer_ref[...]
            joint_ref[...] = sums
        inv_q = lax.rsqrt(sums[HD : HD + 1] + EPS)
        inv_k = lax.rsqrt(sums[HD + 1 : HD + 2] + EPS)
        unit = sums[0:HD] * row_to_fold(inv_q, ones) * inv_k
        unit_ref[s] = unit
        weight = jnp.exp(temp * unit)
        probs = weight / group_sum(weight, ones)
        probs_ref[s] = probs
        h, l = halves(unfold(probs))
        pcat[:, 3 * s * D : 3 * s * D + 3 * D] = jnp.concatenate([h, h, l], axis=1)

    acc[...] = jnp.zeros_like(acc)
    gtab_ref[...] = jnp.zeros_like(gtab_ref)

    def add(r, v):
        acc[8 * r : 8 * r + 8] += v

    for copy in loads[1:] + edges[1:]:
        copy.wait()

    def own_part(o, size):
        token = o + lax.broadcasted_iota(jnp.int32, (size, D), 0)
        return jnp.where((token >= own_off) & (token < own_off + tokens), 1.0, 0.0)

    def attend(o):
        size = wide // 3
        mix = mix_nt(by_slot(v_ref[pl.ds(o, size)], slot_masks(o, size, spans)), pcat)
        mixed[pl.ds(o, size)] = mix
        z = dot_nn(side(mix), wpv[...]) + tab(PB)
        rows = pl.ds(o, size)
        branch = tab(SA) * z
        stream = x_ref[rows] + branch
        s1[rows] = stream
        xhat, _ = normalize(stream)
        li[pl.ds(o + COLS, size)] = xhat * tab(N3G) + tab(N3S)
        add(41, eights(own_part(o, size) * branch * branch))

    for o in range(0, wide, wide // 3):
        attend(o)

    pad = jnp.zeros((COLS, D), F32)
    for buf in (li, mid, gp, ds2):
        buf[0:COLS] = pad
        buf[wide + COLS : wide + 2 * COLS] = pad

    for r in range(rows_wide):
        row = first_row + r
        mine = jnp.where(is_own(r), 1.0, 0.0)
        for n, flag in enumerate((above(row), below(row), mine)):
            flags[n, r * COLS : r * COLS + COLS] = jnp.full((COLS, 128), flag, F32)

    block = 12 * COLS
    col = lax.rem(lax.broadcasted_iota(jnp.int32, (block + 2 * COLS, 128), 0), COLS)

    def convolve(src, base, flip, scale, visit, other=None, events=()):
        def one(n, carry):
            for when, event in events:
                pl.when(n == when)(event)
            lanes = pl.ds(pl.multiple_of(lax.rem(n, 3) * 128, 128), 128)
            m = lax.div(n, 3)
            place = lax.div((m - 1) * (m - 2), 2) + 2 * core * m * (2 - m) + (1 - core) * m * (m - 1)
            o = pl.multiple_of(place * block, block)
            rows = pl.ds(o, block)
            taps = [tab_ref[base + t : base + t + 1, lanes] for t in range(9)]
            if flip:
                taps = taps[::-1]
            if scale is not None:
                taps = [t * tab_ref[scale : scale + 1, lanes] for t in taps]
            u = src[pl.ds(o, block + 2 * COLS), lanes]
            left = jnp.where(col == 0, 0.0, pltpu.roll(u, 1, 0))
            right = jnp.where(col == COLS - 1, 0.0, pltpu.roll(u, block + 2 * COLS - 1, 0))
            up, down = flags[0, rows], flags[1, rows]

            def line(a):
                cut = slice(a * COLS, a * COLS + block)
                return left[cut] * taps[3 * a] + u[cut] * taps[3 * a + 1] + right[cut] * taps[3 * a + 2]

            visit(o, rows, lanes, line(1) + up * line(0) + down * line(2))
            if other is not None:
                near = other[pl.ds(o, block + 2 * COLS), lanes]
                mine = flags[2, rows]
                held = (
                    mine * up * near[0:block],
                    mine * near[COLS : COLS + block],
                    mine * down * near[2 * COLS : 2 * COLS + block],
                )
                inner = slice(COLS, COLS + block)
                for a in range(3):
                    for b, view in enumerate((right, u, left)):
                        t = 8 * (base + 3 * a + b)
                        acc[t : t + 8, lanes] += eights(view[inner] * held[a])
            return carry

        lax.fori_loop(0, 3 * (wide // block), one, 0)

    def first(o, rows, lanes, value):
        at = pl.ds(o + COLS, block)
        a, s = gelu_parts(value + tab_ref[C1B : C1B + 1, lanes])
        act[rows, lanes] = a
        slope[rows, lanes] = s
        mid[at, lanes] = a * tab_ref[BG : BG + 1, lanes] + tab_ref[BS : BS + 1, lanes]

    convolve(li, K1R, False, None, first)

    def second(o, rows, lanes, value):
        value = value + tab_ref[C2B : C2B + 1, lanes]
        lo_[rows, lanes] = value
        branch = tab_ref[SL : SL + 1, lanes] * value
        s2[rows, lanes] = s1[rows, lanes] + branch
        acc[8 * 42 : 8 * 42 + 8, lanes] += eights(flags[2, rows] * branch * branch)

    convolve(mid, K2R, False, None, second)

    dw1_ref[...] = jnp.zeros_like(dw1_ref)
    dw2_ref[...] = jnp.zeros_like(dw2_ref)
    b1g_ref[...] = jnp.zeros_like(b1g_ref)
    for i in range(mlp // D):
        b1_ref[0:1, i * D : i * D + D] = tab(F1B + i)

    def feed(o):
        here = pl.ds(o, TILE)
        xhat, _ = normalize(s2[here])
        n2 = xhat * tab(N2G) + tab(N2S)
        n2c[...] = side(n2)
        dz = tab(SM) * dy_ref[here]
        dzc[...] = side(dz)
        nt[...] = side(n2.T)
        dt[...] = side(dz.T)
        add(F2B, eights(dz))

        def enter(j):
            return dot_nn(n2c[...], w1c[:, j : j + PIECE]), dot_nt(dzc[...], w2c[j : j + PIECE])

        raw, dn = tab(F2B), 0.0
        ready = enter(0)
        for j in range(0, mlp, PIECE):
            lanes = slice(j, j + PIECE)
            pre, dh = ready
            if j + PIECE < mlp:
                ready = enter(j + PIECE)
            a, slope_j = gelu_parts(pre + b1_ref[0:1, lanes])
            dp = dh * slope_j
            ah, al = halves(a)
            ph, pl_ = halves(dp)
            w2h, w2l = w2c[lanes, 0:D], w2c[lanes, 2 * D : 3 * D]
            raw = raw + (dot_nn(ah, w2h) + (dot_nn(al, w2h) + dot_nn(ah, w2l)))
            w1h, w1l = w1c[0:D, lanes], w1c[2 * D : 3 * D, lanes]
            dn = dn + (dot_nt(ph, w1h) + (dot_nt(pl_, w1h) + dot_nt(ph, w1l)))
            b1g_ref[:, lanes] += eights(dp)
            dw1_ref[:, lanes] += dot_nn(nt[...], jnp.concatenate([ph, ph, pl_], axis=0))
            dw2_ref[:, lanes] += dot_nn(dt[...], jnp.concatenate([ah, ah, al], axis=0))
        dy = dy_ref[here]
        xhat, r = normalize(s2[here])
        ds2[pl.ds(pl.multiple_of(o + COLS, COLS), TILE)] = dy + normalize_back(dn * tab(N2G), xhat, r)
        branch = tab(SM) * raw
        result = s2[here] + branch
        s2[here] = result
        add(40, eights(result * result))
        add(43, eights(branch * branch))
        add(SM, eights(dy * raw))
        add(N2G, eights(dn * xhat))
        add(N2S, eights(dn))

    def feed_one(i, carry):
        feed(pl.multiple_of(own_off + i * TILE, 128))
        return carry

    lax.fori_loop(0, tokens // TILE, feed_one, 0)
    reduce.begin()
    stores = [pltpu.make_async_copy(s2.at[own], out_hbm, store_sem.at[0])]
    stores[0].start()
    edge = HALO // 2
    rest = pl.multiple_of(COLS + (1 - core) * (tokens + edge), COLS)
    ds2[pl.ds(rest, edge)] = jnp.zeros((edge, D), F32)
    rows_out = pl.multiple_of(COLS + own_off + (1 - core) * (tokens - edge), COLS)
    rows_in = pl.multiple_of(COLS + edge + core * (tokens - edge), COLS)
    turned = remote(
        ds2.at[pl.ds(rows_out, edge)],
        ds2.at[pl.ds(rows_in, edge)],
        edge_sem.at[0, 4],
        edge_sem.at[1, 4],
        links.twin,
    )
    turned.start()

    def third(o, rows, lanes, value):
        grad = value * tab_ref[BG : BG + 1, lanes] * slope[rows, lanes]
        gp[pl.ds(o + COLS, block), lanes] = grad
        held = flags[2, rows] * value
        acc[8 * BG : 8 * BG + 8, lanes] += eights(held * act[rows, lanes])
        acc[8 * BS : 8 * BS + 8, lanes] += eights(held)
        acc[8 * C1B : 8 * C1B + 8, lanes] += eights(flags[2, rows] * grad)

    convolve(
        ds2,
        K2R,
        True,
        SL,
        third,
        mid,
        ((5, lambda: reduce.join(EARLY)), (6, turned.wait), (8, lambda: reduce.join(LATE))),
    )

    def fourth(o, rows, lanes, value):
        slope[rows, lanes] = value

    convolve(gp, K1R, True, None, fourth, li, ((6, lambda: reduce.down(0, EARLY, 2)),))

    dwp_ref[...] = jnp.zeros_like(dwp_ref)
    cross[...] = jnp.zeros_like(cross)

    def back(step):
        o = pl.multiple_of(own_off + step * TILE, 128)

        here_wide = pl.ds(o, TILE)
        xhat, r = normalize(s1[here_wide])
        grad = slope[here_wide]
        grad_two = ds2[pl.ds(pl.multiple_of(o + COLS, COLS), TILE)]
        result = grad_two + normalize_back(grad * tab(N3G), xhat, r)
        slope[here_wide] = result
        add(N3G, eights(grad * xhat))
        add(N3S, eights(grad))
        add(SL, eights(grad_two * lo_[here_wide]))
        add(C2B, eights(grad_two))
        add(PB, eights(result))
        dmx = dot_nt(side(tab(SA) * result), wph[...])
        act[here_wide] = dmx
        h, l = halves(result)
        dwp_ref[...] += dot_nn(side(mixed[pl.ds(o, TILE)].T), jnp.concatenate([h, h, l], axis=0))
        cross[...] += dot_nn(side(dmx.T), slots_below(v_ref[pl.ds(o, TILE)], slot_masks(o, TILE, spans)))

    count = tokens // TILE
    for step in range(count):
        back(step)
        if step == 0:
            reduce.down(0, LATE, 2)
        if step == 1:
            reduce.down(1, EARLY, 2)
        if step == 2:
            reduce.down(1, LATE, 2)
    for src, dst in ((slope, ds1_hbm), (act, dmx_hbm)):
        stores.append(pltpu.make_async_copy(src.at[own], dst, store_sem.at[len(stores)]))
        stores[-1].start()
    for s in range(3):
        gprob_ref[s] = fold(cross[:, s * D : s * D + D])

    def total(r):
        return jnp.sum(acc[8 * r : 8 * r + 8], axis=0, keepdims=True)

    for r in (N3G, N3S, N2G, N2S, SL, SM, C1B, BG, BS, F2B, 40, 41, 42, 43):
        gtab_ref[r : r + 1] = total(r)
    for t in range(9):
        gtab_ref[K1R + t : K1R + t + 1] = total(K1R + t)
        gtab_ref[K2R + t : K2R + t + 1] = total(K2R + t) * tab(SL)
    gtab_ref[C2B : C2B + 1] = total(C2B) * tab(SL)
    gtab_ref[PB : PB + 1] = total(PB) * tab(SA)
    raw = dwp_ref[...]
    gtab_ref[SA : SA + 1] = jnp.sum(raw * wp_ref[...], axis=0, keepdims=True) + total(PB) * tab(PB)
    dwp_ref[...] = raw * tab(SA)
    for i in range(mlp // D):
        gtab_ref[F1B + i : F1B + i + 1] = jnp.sum(b1g_ref[:, i * D : i * D + D], axis=0, keepdims=True)
    reduce.down(2, EARLY, 2)
    reduce.down(2, LATE, 2)
    for p in range(reduce.count):
        lanes = reduce.lanes(p)
        shard_ref[:, lanes] = reduce.buf[reduce.held(p, 3), lanes]
    for copy in stores:
        copy.wait()


def middle(tall, temp, x, dy, v, sums, wp, w1, w2, tab):
    tokens = x.shape[0]
    wide = tokens + HALO
    mlp = w1.shape[1]
    smem = pl.BlockSpec(memory_space=pltpu.SMEM)
    vmem = pl.BlockSpec(memory_space=pltpu.VMEM)
    anywhere = pl.BlockSpec(memory_space=pl.ANY)

    def f(*shape):
        return jax.ShapeDtypeStruct(shape, F32)

    def s(*shape):
        return pltpu.VMEM(shape, F32)

    def b(*shape):
        return pltpu.VMEM(shape, BF)

    padded = s(wide + 2 * COLS, D)
    return pl.pallas_call(
        middle_kernel,
        out_shape=[
            f(tokens, D),
            f(tokens, D),
            f(tokens, D),
            f(D, D),
            f(2 * SHARD, mlp),
            f(TABLE, D),
            f(3, HD, D),
            f(3, HD, D),
            f(3, HD, D),
            f(*sums.shape[1:]),
        ],
        in_specs=[smem, smem] + [anywhere] * 3 + [vmem, vmem, anywhere, vmem, vmem],
        out_specs=[anywhere] * 3 + [vmem] * 7,
        scratch_shapes=[
            b(3 * D, D),
            b(D, 3 * D),
            b(3 * D, mlp),
            b(mlp, 3 * D),
            b(D, 9 * D),
            s(wide, D),
            s(wide, D),
            padded,
            s(wide, D),
            s(wide, D),
            padded,
            s(wide, D),
            padded,
            padded,
            b(TILE, 3 * D),
            b(TILE, 3 * D),
            s(8, mlp),
            s(8, mlp),
            s(8 * TABLE, D),
            s(D, 3 * D),
            s(wide, D),
            s(wide, D),
            s(wide, D),
            s(3, wide, 128),
            b(D, 3 * TILE),
            b(D, 3 * TILE),
            s(*sums.shape[1:]),
            s(2, D, mlp),
            DMA((4,)),
            DMA((3,)),
            DMA((2, 5)),
        ]
        + Reduce.scratch(mlp, (lax.axis_size("canvas") - 1).bit_length()),
        compiler_params=pltpu.CompilerParams(
            collective_id=0, has_side_effects=True, vmem_limit_bytes=60 << 20
        ),
    )(tall, temp, x, dy, v, sums, wp, w1, w2, tab)


def finish_kernel(
    tall_ref,
    temp_ref,
    x_ref,
    q_ref,
    k_ref,
    ds1_ref,
    dmx_ref,
    sums_ref,
    peer_ref,
    probs_ref,
    unit_ref,
    gprob_ref,
    w_ref,
    tab_ref,
    gtab_ref,
    dwp_ref,
    shard_ref,
    dx_ref,
    end_ref,
    town_ref,
    sum_hbm,
    wh,
    wl,
    pv,
    cv,
    ch,
    side_rows,
    acc,
    gpeer_ref,
    whole,
    dw_ref,
    otab_ref,
    end_first,
    tab_first,
    gsend,
    grecv,
    pair_sem,
    *work,
):
    step = pl.program_id(0)
    last = pl.num_programs(0) - 1
    links = Links()
    core = links.core
    turn = Turn(links, shard_ref, whole, work[:3])
    gather = Gather(links, whole, sum_hbm, work[3:])
    rows_all = 2 * pl.num_programs(0) * TILE // COLS
    spans = slots(tall_ref, core, core * (rows_all // 2), rows_all)
    start = step * TILE

    def tab(r):
        return tab_ref[r : r + 1]

    @pl.when(step == 0)
    def _():
        links.greet()
        swap = remote(gprob_ref.at[2], gpeer_ref, gsend, grecv, links.twin)
        swap.start()
        turn.begin()

        def part(o):
            h, l = halves(w_ref[pl.ds(o, 64)])
            wh[pl.ds(o, 64)] = h
            wl[pl.ds(o, 64)] = l

        sweep(D, 64, part)
        dw_ref[...] = jnp.zeros_like(dw_ref)
        dw_ref[1, :, D : 2 * D] = dwp_ref[...]
        acc[...] = jnp.zeros_like(acc)
        ones = group_ones()
        temp = head_row(temp_ref)
        heat = jnp.zeros((1, D), F32)
        for s in range(3):
            sums = sums_ref[s]
            grad = gprob_ref[s]
            if s == 2:
                swap.wait()
                sums = peer_ref[...]
                grad = grad + gpeer_ref[...]
            inv_q = lax.rsqrt(sums[HD : HD + 1] + EPS)
            inv_k = lax.rsqrt(sums[HD + 1 : HD + 2] + EPS)
            probs = probs_ref[s]
            unit = unit_ref[s]
            scores = probs * (grad - group_sum(probs * grad, ones))
            part_heat = jnp.sum(scores * unit, axis=0, keepdims=True)
            heat = heat + (part_heat if s < 2 else jnp.where(core == 0, part_heat, 0.0))
            pull = temp * scores
            both = pull * unit
            side_rows[8 * s : 8 * s + 1] = fold_to_row(group_sum(both, ones)) * inv_q * inv_q
            side_rows[8 * s + 1 : 8 * s + 2] = jnp.sum(both, axis=0, keepdims=True) * inv_k * inv_k
            across = slice(3 * s * D, 3 * s * D + 3 * D)
            h, l = halves(unfold(pull * row_to_fold(inv_q, ones) * inv_k))
            cv[across] = jnp.concatenate([h, h, l], axis=0)
            ch[:, across] = jnp.concatenate([h, h, l], axis=1)
            h, l = halves(unfold(probs))
            pv[across] = jnp.concatenate([h, h, l], axis=0)
        otab_ref[...] = gtab_ref[...]
        otab_ref[44:45] = heat

    masks = [span_mask(start, TILE, lo, hi) for lo, hi in spans]
    factors = slot_masks(start, TILE, spans)

    def rows_of(r):
        return sum(jnp.where(mask, side_rows[8 * s + r : 8 * s + r + 1], 0.0) for s, mask in enumerate(masks))

    def at(n, *events):
        @pl.when(step == n)
        def _():
            for event, *args in events:
                event(*args)

    q, k = q_ref[...], k_ref[...]
    dq = mix_nt(by_slot(k, factors), ch) - q * rows_of(0)
    dk = mix_nn(by_slot(q, factors), cv) - k * rows_of(1)
    dv = mix_nn(by_slot(dmx_ref[...], factors), pv)
    dqkv = jnp.concatenate([dq, dk, dv], axis=1)
    at(0, (turn.end, EARLY), (gather.begin, EARLY))
    at(1, (gather.up, 3, EARLY))
    at(2, (gather.up, 2, LATE))
    at(3, (gather.up, 1, LATE))

    h, l = halves(dqkv)
    dn = dot_nt(h, wh[...]) + (dot_nt(l, wh[...]) + dot_nt(h, wl[...]))
    xhat, r = normalize(x_ref[...])
    nt = side((xhat * tab(N1G) + tab(N1S)).T)
    grads = dot_nn(nt, jnp.concatenate([h, h, l], axis=0))
    dw_ref[0] += grads[:, 0 : 2 * D]
    dw_ref[1, :, 0:D] += grads[:, 2 * D : 3 * D]
    dx_ref[...] = ds1_ref[...] + normalize_back(dn * tab(N1G), xhat, r)
    acc[0:8] += eights(dn * xhat)
    acc[8:16] += eights(dn)
    for i, v in enumerate((dq, dk, dv)):
        acc[16 + 8 * i : 24 + 8 * i] += eights(v)

    at(0, (turn.end, LATE), (gather.begin, LATE))
    at(1, (gather.up, 3, LATE), (gather.up, 2, EARLY))
    at(2, (gather.up, 1, EARLY))

    @pl.when(step == last)
    def _():
        for i, r in enumerate((N1G, N1S, QB, KB, VB)):
            otab_ref[r : r + 1] = jnp.sum(acc[8 * i : 8 * i + 8], axis=0, keepdims=True)
        trows = tab_first.shape[0]
        near = pl.ds(pl.multiple_of(core * trows, 8), trows)
        far = pl.ds(pl.multiple_of((1 - core) * trows, 8), trows)
        pairs = [(otab_ref.at[far], tab_first)]
        for p in range(end_first.shape[1] // 128):
            lanes = slice(p * 128, p * 128 + 128)
            pairs.append((dw_ref.at[1 - core, :, lanes], end_first.at[:, lanes]))
        copies = [
            remote(a, b, pair_sem.at[0, i], pair_sem.at[1, i], links.twin)
            for i, (a, b) in enumerate(pairs)
        ]
        for copy in copies:
            copy.start()
        gather.up(0, EARLY)
        gather.up(0, LATE)
        for copy in copies:
            copy.wait()
        town_ref[...] = otab_ref[near] + tab_first[...]
        end_ref[...] = dw_ref[core] + end_first[...]
        gather.end()


def finish(tall, temp, x, q, k, ds1, dmx, sums, peer, probs, unit, gprob, w, tab, gtab, dwp, shard):
    tokens = x.shape[0]
    smem = pl.BlockSpec(memory_space=pltpu.SMEM)
    anywhere = pl.BlockSpec(memory_space=pl.ANY)
    row = pl.BlockSpec((TILE, D), lambda i: (i, 0))
    bits = (lax.axis_size("canvas") - 1).bit_length()

    def whole(v):
        return pl.BlockSpec(v.shape, lambda i: (0,) * v.ndim)

    fixed = (sums, peer, probs, unit, gprob, w, tab, gtab, dwp, shard)
    return pl.pallas_call(
        finish_kernel,
        grid=(tokens // TILE,),
        out_shape=[
            jax.ShapeDtypeStruct((tokens, D), F32),
            jax.ShapeDtypeStruct((D, 2 * D), F32),
            jax.ShapeDtypeStruct((TABLE // 2, D), F32),
            jax.ShapeDtypeStruct((2, D, shard.shape[1]), F32),
        ],
        in_specs=[smem, smem] + [row] * 5 + [whole(v) for v in fixed],
        out_specs=[
            row,
            pl.BlockSpec((D, 2 * D), lambda i: (0, 0)),
            pl.BlockSpec((TABLE // 2, D), lambda i: (0, 0)),
            anywhere,
        ],
        scratch_shapes=[
            pltpu.VMEM((D, 3 * D), BF),
            pltpu.VMEM((D, 3 * D), BF),
            pltpu.VMEM((9 * D, D), BF),
            pltpu.VMEM((9 * D, D), BF),
            pltpu.VMEM((D, 9 * D), BF),
            pltpu.VMEM((24, D), F32),
            pltpu.VMEM((40, D), F32),
            pltpu.VMEM(gprob.shape[1:], F32),
            pltpu.VMEM((D, shard.shape[1]), F32),
            pltpu.VMEM((2, D, 2 * D), F32),
            pltpu.VMEM((TABLE, D), F32),
            pltpu.VMEM((D, 2 * D), F32),
            pltpu.VMEM((TABLE // 2, D), F32),
            DMA,
            DMA,
            DMA((2, 1 + 2 * D // 128)),
        ]
        + Turn.scratch(shard.shape[1], bits)
        + Gather.scratch(shard.shape[1]),
        compiler_params=pltpu.CompilerParams(
            collective_id=1, has_side_effects=True, vmem_limit_bytes=60 << 20
        ),
    )(tall, temp, x, q, k, ds1, dmx, *fixed)


NS_A, NS_B, NS_C = 3.4445, -4.7750, 2.0315


def times(a, b):
    return dot_nn(
        jnp.concatenate([a[0], a[1], a[0]], axis=1), jnp.concatenate([b[0], b[0], b[1]], axis=0)
    )


def mirrored(left, corner):
    edge = left.shape[1]
    return jnp.concatenate([left, jnp.concatenate([left[edge:].T, corner], axis=0)], axis=1)


EDGE = 2 * 128


def times_symmetric(a, b):
    lhs = jnp.concatenate([a[0], a[1], a[0]], axis=1)
    rhs = jnp.concatenate([b[0], b[0], b[1]], axis=0)
    return mirrored(dot_nn(lhs, rhs[:, :EDGE]), dot_nn(lhs[EDGE:], rhs[:, EDGE:]))


def gram_of(h, l):
    left = dot_nt(h, h[:EDGE]) + (dot_nt(l, h[:EDGE]) + dot_nt(h, l[:EDGE]))
    he, le = h[EDGE:], l[EDGE:]
    return mirrored(left, dot_nt(he, he) + (dot_nt(le, he) + dot_nt(he, le)))


def inverse_norm(v):
    total = jnp.sum(jnp.sum(v * v, axis=0, keepdims=True), axis=1, keepdims=True)
    return 1.0 / (jnp.sqrt(total) + 1e-07)


def wide_kernel(
    end_hbm,
    tab_hbm,
    mid_hbm,
    m1_hbm,
    m2_hbm,
    sum_hbm,
    otab_hbm,
    orth_hbm,
    xs,
    x,
    m1,
    m2,
    xc,
    tbuf,
    tland,
    load_sem,
    tsend,
    trecv,
    tout,
    buf,
    own_sem,
    *work,
):
    links = Links()
    core = links.core
    reduce = Reduce(links, buf, buf, work[:5])
    gather = Gather(links, work[0], sum_hbm, work[5:])
    own = pltpu.make_async_copy(end_hbm, buf, own_sem)
    own.start()
    wide = m1.shape[1]
    blocks = wide // D
    trows = tbuf.shape[0]
    near = pl.ds(pl.multiple_of(core * trows, 8), trows)
    pairs = ((mid_hbm.at[core], x), (m1_hbm, m1), (m2_hbm, m2), (tab_hbm, tbuf))
    loads = [pltpu.make_async_copy(a, b, load_sem.at[i]) for i, (a, b) in enumerate(pairs)]
    for load in loads:
        load.start()
    links.greet()
    own.wait()
    reduce.launch()

    def table(n):
        return remote(tbuf, tland.at[n], tsend.at[n], trecv.at[n], links.there[n])

    def table_land(n):
        table(n).wait()
        tbuf[...] += tland[n]

    def down(s, some):
        reduce.down(s, some)
        if some is EARLY:
            table_land(s)
            if s < 3:
                table(s + 1).start()
        elif s == 3:
            for b in range(4, links.bits):
                table(b).start()
                table_land(b)
            for copy in touts:
                copy.start()
        if s == 3:
            for p in some:
                lanes = gather.lanes(p)
                gather.whole[gather.held(p, 4), lanes] = buf[gather.held(p, 4), lanes]
            gather.begin(some)

    touts = [
        pltpu.make_async_copy(tbuf, otab_hbm.at[near], tout.at[0]),
        remote(tbuf, otab_hbm.at[near], tout.at[1], tout.at[2], links.twin),
    ]

    for load in loads:
        load.wait()
    table(0).start()

    @pl.when(core == 0)
    def _():
        x[...] = MUON_KEEP * m1[...] + x[...]

    @pl.when(core == 1)
    def _():
        for b in range(blocks):
            lanes = slice(b * D, b * D + D)
            x[:, lanes] = MUON_KEEP * m2[lanes].T + x[:, lanes]

    inv = inverse_norm(x[...])
    chunks = [slice(o, o + 2 * PIECE) for o in range(0, wide, 2 * PIECE)]

    def keep(lanes, v):
        h, l = halves(v)
        xc[0:D, lanes] = h
        xc[D : 2 * D, lanes] = h
        xc[2 * D : 3 * D, lanes] = l

    def kept(lanes):
        return xc[0:D, lanes].astype(F32) + xc[2 * D : 3 * D, lanes].astype(F32)

    for lanes in chunks:
        keep(lanes, x[:, lanes] * inv)

    def gram():
        return gram_of(xc[0:D], xc[2 * D : 3 * D])

    def two_steps(events):
        g0 = gram()
        g = halves(g0)
        events(0)
        p0 = NS_B * g0 + NS_C * times_symmetric(g, g)
        p = halves(p0)
        events(1)
        t = NS_A * g0 + times_symmetric(p, g)
        events(2)
        g1 = NS_A * t + times_symmetric(halves(t), p)
        g = halves(g1)
        events(3)
        p1 = NS_B * g1 + NS_C * times_symmetric(g, g)
        events(4)
        both = side(NS_A * (p0 + p1) + times_symmetric(halves(p1), p))
        events(5)
        for c, lanes in enumerate(chunks):
            keep(lanes, NS_A * NS_A * kept(lanes) + dot_nn(both, xc[:, lanes]))
            events(6 + c)

    def run(schedule):
        def events(n):
            for event, *args in schedule.get(n, ()):
                event(*args)

        return events

    down(0, EARLY)
    two_steps(
        run(
            {
                0: ((down, 0, LATE),),
                2: ((down, 1, EARLY),),
                4: ((down, 1, LATE),),
                5: ((down, 2, EARLY),),
                7: ((down, 2, LATE),),
            }
        )
    )
    two_steps(
        run(
            {
                0: ((down, 3, EARLY),),
                2: ((down, 3, LATE),),
                4: ((gather.up, 3, EARLY),),
                6: ((gather.up, 3, LATE),),
                7: ((gather.up, 2, EARLY),),
            }
        )
    )
    g0 = gram()
    g = halves(g0)
    gather.up(2, LATE)
    last = side(NS_B * g0 + NS_C * times_symmetric(g, g))
    gather.up(1, EARLY)
    for c, lanes in enumerate(chunks):
        x[:, lanes] = NS_A * kept(lanes) + dot_nn(last, xc[:, lanes])
        if c == 1:
            gather.up(1, LATE)

    @pl.when(core == 0)
    def _():
        for b in range(blocks):
            xs[b] = x[:, b * D : b * D + D]

    @pl.when(core == 1)
    def _():
        for b in range(blocks):
            xs[b] = x[:, b * D : b * D + D].T

    orth = [
        pltpu.make_async_copy(xs, orth_hbm.at[core], tout.at[3]),
        remote(xs, orth_hbm.at[core], tout.at[4], tout.at[5], links.twin),
    ]
    for copy in orth:
        copy.start()
    gather.up(0, EARLY)
    gather.up(0, LATE)
    gather.end()
    for copy in touts + orth:
        copy.wait()


def wide_blocks(end, tab, mid, m1, m2):
    bits = (lax.axis_size("canvas") - 1).bit_length()
    anywhere = pl.BlockSpec(memory_space=pl.ANY)
    blocks = m1.shape[1] // D
    return pl.pallas_call(
        wide_kernel,
        out_shape=[
            jax.ShapeDtypeStruct((2,) + end.shape, F32),
            jax.ShapeDtypeStruct((TABLE, D), F32),
            jax.ShapeDtypeStruct((2, blocks, D, D), F32),
        ],
        in_specs=[anywhere] * 5,
        out_specs=[anywhere] * 3,
        scratch_shapes=[
            pltpu.VMEM((blocks, D, D), F32),
            pltpu.VMEM(m1.shape, F32),
            pltpu.VMEM(m1.shape, F32),
            pltpu.VMEM(m2.shape, F32),
            pltpu.VMEM((3 * D, m1.shape[1]), BF),
            pltpu.VMEM((TABLE // 2, D), F32),
            pltpu.VMEM((bits, TABLE // 2, D), F32),
            DMA((4,)),
            DMA((bits,)),
            DMA((bits,)),
            DMA((6,)),
            pltpu.VMEM(end.shape, F32),
            DMA,
        ]
        + Reduce.scratch(end.shape[1], bits)
        + Gather.scratch(end.shape[1]),
        compiler_params=pltpu.CompilerParams(
            collective_id=2, has_side_effects=True, vmem_limit_bytes=60 << 20
        ),
    )(end, tab, mid, m1, m2)


def muon(w, orth, large):
    return w * (1.0 - MUON_RATE * DECAY) - MUON_RATE * 0.2 * math.sqrt(large) * orth


def square_kernel(
    end_hbm,
    mid_hbm,
    wide_hbm,
    mq_hbm,
    mp_hbm,
    m1_hbm,
    m2_hbm,
    w1_hbm,
    w2_hbm,
    out_hbm,
    dx_hbm,
    gq_out,
    gp_out,
    g1_out,
    g2_out,
    nq_out,
    np_out,
    n1_out,
    n2_out,
    w1_out,
    w2_out,
    c1_out,
    c2_out,
    out_out,
    dx_out,
    orth_hbm,
    end,
    mid,
    nat,
    mq,
    mp,
    m1,
    m2,
    w1,
    w2,
    c1,
    c2,
    wide,
    out,
    dx,
    xh,
    xl,
    xs,
    in_sem,
    out_sem,
):
    core = lax.axis_index("rows")
    mlp = m1.shape[1]
    blocks = mlp // D
    pairs = (
        (end_hbm, end),
        (mq_hbm, mq),
        (mp_hbm, mp),
        (mid_hbm, mid),
        (m1_hbm, m1),
        (m2_hbm, m2),
        (w1_hbm, w1),
        (w2_hbm, w2),
        (wide_hbm, wide),
        (out_hbm, out),
        (dx_hbm, dx),
    )
    loads = [pltpu.make_async_copy(a, b, in_sem.at[i]) for i, (a, b) in enumerate(pairs)]
    for load in loads:
        load.start()
    for load in loads[0:3]:
        load.wait()
    outs = (
        (end.at[0], gq_out.at[:, 0 : 2 * D]),
        (end.at[1, :, 0:D], gq_out.at[:, 2 * D : 3 * D]),
        (end.at[1, :, D : 2 * D], gp_out),
        (mq, nq_out),
        (mp, np_out),
        (mid.at[0], g1_out),
        (nat, g2_out),
        (m1, n1_out),
        (m2, n2_out),
        (out, out_out),
        (dx, dx_out),
        (w1, w1_out),
        (w2, w2_out),
        (c1, c1_out),
        (c2, c2_out),
        (xs, orth_hbm),
    )

    def store(*which):
        return [pltpu.make_async_copy(*outs[n], out_sem.at[n]) for n in which]

    def send(*which):
        for copy in store(*which):
            copy.start()

    send(0, 1, 2)

    def small(o):
        rows = pl.ds(o, 128)
        mq[rows, 0 : 2 * D] = MUON_KEEP * mq[rows, 0 : 2 * D] + end[0, rows]
        mq[rows, 2 * D : 3 * D] = MUON_KEEP * mq[rows, 2 * D : 3 * D] + end[1, rows, 0:D]
        mp[rows] = MUON_KEEP * mp[rows] + end[1, rows, D : 2 * D]

    sweep(D, 128, small)
    send(3, 4)

    def keep(b, v):
        xh[b], xl[b] = halves(v)

    @pl.when(core == 0)
    def _():
        xs[0] = mq[:, 0:D]
        xs[1] = mq[:, D : 2 * D]

    @pl.when(core == 1)
    def _():
        xs[0] = mq[:, 2 * D : 3 * D]
        xs[1] = mp[...]

    for b in range(2):
        keep(b, xs[b] * inverse_norm(xs[b]))

    def step(i, carry):
        x = [(xh[b], xl[b]) for b in range(2)]
        g = [gram_of(h, l) for h, l in x]
        pairs = [halves(v) for v in g]
        p = [NS_B * v + NS_C * times_symmetric(w, w) for v, w in zip(g, pairs)]
        pairs = [halves(v) for v in p]
        for b in range(2):
            h, l = x[b]
            keep(b, NS_A * (h.astype(F32) + l.astype(F32)) + times(pairs[b], x[b]))
        pl.when(i == 1)(moments)
        pl.when(i == 2)(weights)
        return carry

    def moments():
        for load in loads[3:6]:
            load.wait()
        send(5)
        for b in range(blocks):
            nat[b * D : b * D + D] = mid[1, :, b * D : b * D + D].T
        send(6)

        def large(o):
            rows = pl.ds(o, 64)
            m1[rows] = MUON_KEEP * m1[rows] + mid[0, rows]

        sweep(D, 64, large)
        send(7)

        def larger(o):
            rows = pl.ds(o, 256)
            m2[rows] = MUON_KEEP * m2[rows] + nat[rows]

        sweep(mlp, 256, larger)
        send(8)

    def weights():
        for load in loads[6:]:
            load.wait()
        send(9, 10)
        for b in range(blocks):
            at = slice(b * D, b * D + D)
            new = muon(w1[:, at], wide[0, b], mlp)
            w1[:, at] = new
            c1[:, at] = new.astype(BF)
            new = muon(w2[at], wide[1, b], mlp)
            w2[at] = new
            c2[at] = new.astype(BF)
        send(11, 12, 13, 14)

    lax.fori_loop(0, 5, step, 0)
    for b in range(2):
        xs[b] = xh[b].astype(F32) + xl[b].astype(F32)
    send(15)
    for copy in store(*range(len(outs))):
        copy.wait()


def square_blocks(end, mid, wide, mq, mp, m1, m2, w1, w2, out, dx):
    anywhere = pl.BlockSpec(memory_space=pl.ANY)

    def like(v, kind=F32):
        return jax.ShapeDtypeStruct(v.shape, kind)

    def room(v, kind=F32):
        return pltpu.VMEM(v.shape, kind)

    return pl.pallas_call(
        square_kernel,
        out_shape=[like(v) for v in (mq, mp, m1, m2, mq, mp, m1, m2, w1, w2)]
        + [like(w1, BF), like(w2, BF), like(out), like(dx), jax.ShapeDtypeStruct((2, D, D), F32)],
        in_specs=[anywhere] * 11,
        out_specs=[anywhere] * 15,
        scratch_shapes=[room(v) for v in (end, mid, m2, mq, mp, m1, m2, w1, w2)]
        + [room(w1, BF), room(w2, BF), room(wide), room(out), room(dx)]
        + [
            pltpu.VMEM((2, D, D), BF),
            pltpu.VMEM((2, D, D), BF),
            pltpu.VMEM((2, D, D), F32),
            DMA((11,)),
            DMA((16,)),
        ],
        compiler_params=pltpu.CompilerParams(vmem_limit_bytes=60 << 20),
    )(end, mid, wide, mq, mp, m1, m2, w1, w2, out, dx)


def trade_kernel(own_ref, peer_ref, send_sem, recv_sem):
    core = lax.axis_index("rows")
    twin = {"rows": 1 - core}
    barrier = pltpu.get_barrier_semaphore()
    pl.semaphore_signal(barrier, inc=1, device_id=twin, device_id_type=MESH_ID)
    pl.semaphore_wait(barrier, 1)
    copy = remote(own_ref, peer_ref, send_sem, recv_sem, twin)
    copy.start()
    copy.wait()


def trade(own):
    anywhere = pl.BlockSpec(memory_space=pl.ANY)
    return pl.pallas_call(
        trade_kernel,
        out_shape=jax.ShapeDtypeStruct(own.shape, F32),
        in_specs=[anywhere],
        out_specs=anywhere,
        scratch_shapes=[DMA, DMA],
        compiler_params=pltpu.CompilerParams(collective_id=3, has_side_effects=True),
    )(own)


def moment_step(current, one, two, gradient):
    first = BETA1 * one + (1.0 - BETA1) * gradient
    second = BETA2 * two + (1.0 - BETA2) * gradient * gradient
    fix_one = 1.0 - BETA1**STEP
    fix_two = 1.0 - BETA2**STEP
    updated = current - ADAM_RATE * (first / fix_one) / (jnp.sqrt(second / fix_two) + ADAM_FLOOR)
    return first, second, updated


def update_kernel(
    count,
    temp_ref,
    heat_one_ref,
    heat_two_ref,
    own_ref,
    peer_ref,
    wq_ref,
    wp_ref,
    tab_ref,
    one_ref,
    two_ref,
    gtab_ref,
    nq_ref,
    np_ref,
    cq_ref,
    cp_ref,
    first_ref,
    second_ref,
    small_ref,
    heat_first_ref,
    heat_second_ref,
    heat_ref,
    rms_ref,
):
    lower = lax.axis_index("rows") == 0
    own, peer = own_ref[...], peer_ref[...]
    low, high = jnp.where(lower, own, peer), jnp.where(lower, peer, own)
    for i, orth in enumerate((low[0], low[1], high[0])):
        lanes = slice(i * D, i * D + D)
        new = muon(wq_ref[:, lanes], orth, D)
        nq_ref[:, lanes] = new
        cq_ref[:, lanes] = new.astype(BF)
    new = muon(wp_ref[...], high[1], D)
    np_ref[...] = new
    cp_ref[...] = new.astype(BF)
    first, second, small = moment_step(tab_ref[...], one_ref[...], two_ref[...], gtab_ref[0:SMALL])
    first_ref[...] = first
    second_ref[...] = second
    small_ref[...] = small

    @pl.when(pl.program_id(0) == 0)
    def _():
        head = lax.broadcasted_iota(jnp.int32, (HEADS, D), 0)
        lane = lax.broadcasted_iota(jnp.int32, (HEADS, D), 1) // HD
        heat = jnp.sum(jnp.where(head == lane, gtab_ref[44:45], 0.0), axis=1, keepdims=True)
        head = lax.broadcasted_iota(jnp.int32, (HEADS, 1), 0)

        def column(ref):
            v = jnp.where(head == 0, ref[0], 0.0)
            for h in range(1, HEADS):
                v = jnp.where(head == h, ref[h], v)
            return v

        results = moment_step(column(temp_ref), column(heat_one_ref), column(heat_two_ref), heat)
        for ref, v in zip((heat_first_ref, heat_second_ref, heat_ref), results):
            for h in range(HEADS):
                ref[h] = v[h, 0]
        rms = jnp.sqrt(jnp.sum(gtab_ref[40:44], axis=1, keepdims=True) / count)
        for n in range(4):
            rms_ref[n] = rms[n, 0]


def update(count, temp, heat_one, heat_two, own, peer, wq, wp, tab, one, two, gtab):
    steps = 3
    piece = D // steps

    def rows(v):
        return pl.BlockSpec((piece, v.shape[1]), lambda i: (i, 0))

    def whole(v):
        return pl.BlockSpec(v.shape, lambda i: (0, 0))

    square = pl.BlockSpec((2, piece, D), lambda i: (0, i, 0))
    weights = (wq, wp)
    smem = pl.BlockSpec(memory_space=pltpu.SMEM)
    return pl.pallas_call(
        functools.partial(update_kernel, count),
        grid=(steps,),
        out_shape=[jax.ShapeDtypeStruct(w.shape, F32) for w in weights]
        + [jax.ShapeDtypeStruct(w.shape, BF) for w in weights]
        + [jax.ShapeDtypeStruct(tab.shape, F32)] * 3
        + [jax.ShapeDtypeStruct(temp.shape, F32)] * 3
        + [jax.ShapeDtypeStruct((4,), F32)],
        in_specs=[smem] * 3
        + [square, square]
        + [rows(w) for w in weights]
        + [whole(v) for v in (tab, one, two, gtab)],
        out_specs=[rows(w) for w in weights] * 2 + [whole(tab)] * 3 + [smem] * 4,
        compiler_params=pltpu.CompilerParams(vmem_limit_bytes=60 << 20),
    )(temp, heat_one, heat_two, own, peer, *weights, tab, one, two, gtab)


def on_device(
    x4, dy4, tall, wqkv, wp, w1, w2, mqkv, mp, m1, m2, tab, tab_one, tab_two, temp, temp_one, temp_two
):
    shape = x4.shape
    tokens = shape[1] * shape[2]
    x = x4.reshape(tokens, D)
    dy = dy4.reshape(tokens, D)
    q, k, v, sums = project(tall, x, wqkv, tab)
    out, ds1, dmx, dwp, shard, gtab, probs, unit, gprob, joint = middle(
        tall, temp, x, dy, v, sums, wp, w1, w2, tab
    )
    dx, end, gtab, mid = finish(
        tall, temp, x, q, k, ds1, dmx, sums, joint, probs, unit, gprob, wqkv, tab, gtab, dwp, shard
    )
    end, gtab, wide = wide_blocks(end, gtab, mid, m1, m2)
    *grads, new_1, new_2, copy_1, copy_2, out, dx, square = square_blocks(
        end, mid, wide, mqkv, mp, m1, m2, w1, w2, out, dx
    )
    count = tokens * D * lax.axis_size("rows") * lax.axis_size("canvas")
    new_q, new_p, copy_q, copy_p, *small = update(
        count, temp, temp_one, temp_two, square, trade(square), wqkv, wp, tab, tab_one, tab_two, gtab
    )
    new = (new_q, new_p, new_1, new_2, copy_q, copy_p, copy_1, copy_2)
    return (out.reshape(shape), dx.reshape(shape), *grads, *new, *small)


def solution(mesh):
    split = P("canvas", "rows", None, None)
    return jax.shard_map(
        on_device,
        mesh=mesh,
        in_specs=(split, split, P("canvas", None)) + (P(),) * 14,
        out_specs=(split, split) + (P(),) * 23,
        check_vma=False,
    )
```

```python
import functools
import math

import jax
import jax.numpy as jnp
from jax import lax
from jax.experimental import pallas as pl
from jax.experimental.pallas import tpu as pltpu
from jax.sharding import PartitionSpec as P

BF = jnp.bfloat16
F32 = jnp.float32
MESH_ID = pl.DeviceIdType.MESH

EPS = 1e-06
ROOT_HALF = 1.0 / math.sqrt(2.0)
ROOT_TWOPI = 1.0 / math.sqrt(2.0 * math.pi)
STEP = 10
MUON_RATE = 0.2
MUON_KEEP = 0.95
DECAY = 0.01
ADAM_RATE = 0.2
BETA1 = 0.9
BETA2 = 0.95
ADAM_FLOOR = 1e-08

HEADS = 8
HD = 48
D = HEADS * HD
COLS = 32
HALO = 4 * COLS
TILE = 256

N1G, N1S, N3G, N3S, N2G, N2S, SA, SL, SM, QB, KB, VB, PB, C1B, BG, BS, C2B, F2B = range(18)
F1B, K1R, K2R = 18, 22, 31
SMALL = 40
TABLE = 48


def halves(v):
    hi = v.astype(BF)
    return hi, (v - hi.astype(F32)).astype(BF)


def side(v):
    h, l = halves(v)
    return jnp.concatenate([h, l, h], axis=1)


def dot_nn(a, b):
    return lax.dot_general(a, b, (((1,), (0,)), ((), ())), preferred_element_type=F32)


def dot_nt(a, b):
    return lax.dot_general(a, b, (((1,), (1,)), ((), ())), preferred_element_type=F32)


def normalize(v):
    mean = jnp.mean(v, axis=1, keepdims=True)
    c = v - mean
    r = lax.rsqrt(jnp.mean(c * c, axis=1, keepdims=True) + EPS)
    return c * r, r


def normalize_back(e, xhat, r):
    return r * (
        e - jnp.mean(e, axis=1, keepdims=True) - xhat * jnp.mean(e * xhat, axis=1, keepdims=True)
    )


def gelu_parts(v):
    phi = 0.5 * (1.0 + lax.erf(v * ROOT_HALF))
    return v * phi, phi + v * jnp.exp(-0.5 * v * v) * ROOT_TWOPI


def eights(v):
    total = v[0:8]
    for i in range(8, v.shape[0], 8):
        total = total + v[i : i + 8]
    return total


def sweep(count, size, body):
    def one(i, carry):
        body(pl.multiple_of(i * size, size))
        return carry

    lax.fori_loop(0, count // size, one, 0)


def image_ends(tall_ref):
    e0 = tall_ref[0, 0]
    e1 = e0 + tall_ref[0, 1]
    return e0, e1, e1 + tall_ref[0, 2]


def slots(tall_ref, core, first_row, rows_all):
    e0, e1, e2 = image_ends(tall_ref)
    low = (jnp.where(core == 0, 0, e2), jnp.where(core == 0, e0, 0), e1)
    high = (jnp.where(core == 0, e0, rows_all), jnp.where(core == 0, e1, 0), e2)
    return [((a - first_row) * COLS, (b - first_row) * COLS) for a, b in zip(low, high)]


def span_mask(start, rows, lo, hi):
    token = start + lax.broadcasted_iota(jnp.int32, (rows, D), 0)
    return (token >= lo) & (token < hi)


def slot_masks(start, rows, spans):
    return [jnp.where(span_mask(start, rows, lo, hi), 1.0, 0.0).astype(BF) for lo, hi in spans]


def by_slot(v, masks):
    h, l = halves(v)
    parts = []
    for mask in masks:
        hm = h * mask
        parts += [hm, l * mask, hm]
    return parts


def whole_and_far(parts):
    return jnp.concatenate(parts, axis=1), jnp.concatenate([p[:, 128:] for p in parts], axis=1)


def mix_nt(parts, ref):
    every, far = whole_and_far(parts)
    corner = [ref[256:D, n * D + 128 : n * D + D] for n in range(len(parts))]
    return jnp.concatenate(
        [dot_nt(every, ref[0:256]), dot_nt(far, jnp.concatenate(corner, axis=1))], axis=1
    )


def mix_nn(parts, ref):
    every, far = whole_and_far(parts)
    corner = [ref[n * D + 128 : n * D + D, 256:D] for n in range(len(parts))]
    return jnp.concatenate(
        [dot_nn(every, ref[:, 0:256]), dot_nn(far, jnp.concatenate(corner, axis=0))], axis=1
    )


def slots_below(v, masks):
    h, l = halves(v)
    high = jnp.concatenate([h * mask for mask in masks], axis=1)
    return jnp.concatenate([high, high, jnp.concatenate([l * mask for mask in masks], axis=1)], axis=0)


def lane_head():
    return lax.broadcasted_iota(jnp.int32, (HD, D), 1) // HD


def lane_slot():
    return lax.broadcasted_iota(jnp.int32, (HD, D), 1) % HD


def fold(full):
    head = lane_head()
    total = jnp.where(head == 0, full[0:HD], 0.0)
    for h in range(1, HEADS):
        total = total + jnp.where(head == h, full[h * HD : h * HD + HD], 0.0)
    return total


def unfold(small):
    head = lane_head()
    return jnp.concatenate([jnp.where(head == h, small, 0.0) for h in range(HEADS)], axis=0)


def group_ones():
    a = lax.broadcasted_iota(jnp.int32, (D, D), 0) // HD
    b = lax.broadcasted_iota(jnp.int32, (D, D), 1) // HD
    return jnp.where(a == b, 1.0, 0.0).astype(BF)


def group_sum(v, ones):
    h = v.astype(BF)
    rest = v - h.astype(F32)
    m = rest.astype(BF)
    l = (rest - m.astype(F32)).astype(BF)
    return dot_nn(h, ones) + (dot_nn(m, ones) + dot_nn(l, ones))


def row_to_fold(row, ones):
    slot = lax.broadcasted_iota(jnp.int32, (HD, D), 0)
    return group_sum(jnp.where(lane_slot() == slot, jnp.broadcast_to(row, (HD, D)), 0.0), ones)


def fold_to_row(small):
    slot = lax.broadcasted_iota(jnp.int32, (HD, D), 0)
    return jnp.sum(jnp.where(lane_slot() == slot, small, 0.0), axis=0, keepdims=True)


def head_row(temp_ref):
    head = lax.broadcasted_iota(jnp.int32, (1, D), 1) // HD
    row = jnp.where(head == 0, temp_ref[0], 0.0)
    for h in range(1, HEADS):
        row = row + jnp.where(head == h, temp_ref[h], 0.0)
    return row


def project_kernel(tall_ref, x_ref, w_ref, tab_ref, q_ref, k_ref, v_ref, sums_ref, wcat, cross):
    step = pl.program_id(0)
    core = lax.axis_index("rows")
    rows_all = 2 * pl.num_programs(0) * TILE // COLS
    spans = slots(tall_ref, core, core * (rows_all // 2), rows_all)
    start = step * TILE

    @pl.when(step == 0)
    def _():
        def part(o):
            h, l = halves(w_ref[pl.ds(o, 64)])
            wcat[pl.ds(o, 64)] = h
            wcat[pl.ds(D + o, 64)] = h
            wcat[pl.ds(2 * D + o, 64)] = l

        sweep(D, 64, part)
        cross[...] = jnp.zeros_like(cross)
        sums_ref[...] = jnp.zeros_like(sums_ref)

    xhat, _ = normalize(x_ref[...])
    lhs = side(xhat * tab_ref[N1G : N1G + 1] + tab_ref[N1S : N1S + 1])
    qkv = dot_nn(lhs, wcat[...])
    q = qkv[:, 0:D] + tab_ref[QB : QB + 1]
    q_ref[...] = q
    k = qkv[:, D : 2 * D] + tab_ref[KB : KB + 1]
    k_ref[...] = k
    v_ref[...] = qkv[:, 2 * D : 3 * D] + tab_ref[VB : VB + 1]
    cross[...] += dot_nn(side(q.T), slots_below(k, slot_masks(start, TILE, spans)))
    for s, (lo, hi) in enumerate(spans):
        mask = span_mask(start, TILE, lo, hi)
        for n, v in enumerate((q, k)):
            row = HD + n
            sums_ref[s, row : row + 1] += jnp.sum(jnp.where(mask, v * v, 0.0), axis=0, keepdims=True)

    @pl.when(step == pl.num_programs(0) - 1)
    def _():
        for s in range(3):
            sums_ref[s, 0:HD] = fold(cross[:, s * D : s * D + D])


def project(tall, x, w, tab):
    tokens = x.shape[0]
    row = pl.BlockSpec((TILE, D), lambda i: (i, 0))
    return pl.pallas_call(
        project_kernel,
        grid=(tokens // TILE,),
        out_shape=[jax.ShapeDtypeStruct((tokens, D), F32)] * 3
        + [jax.ShapeDtypeStruct((3, HD + 8, D), F32)],
        in_specs=[
            pl.BlockSpec(memory_space=pltpu.SMEM),
            row,
            pl.BlockSpec((D, 3 * D), lambda i: (0, 0)),
            pl.BlockSpec((SMALL, D), lambda i: (0, 0)),
        ],
        out_specs=[row, row, row, pl.BlockSpec((3, HD + 8, D), lambda i: (0, 0, 0))],
        scratch_shapes=[pltpu.VMEM((3 * D, 3 * D), BF), pltpu.VMEM((D, 3 * D), F32)],
        compiler_params=pltpu.CompilerParams(vmem_limit_bytes=60 << 20),
    )(tall, x, w, tab)


ORDERS = ((0, 1, 2, 3), (1, 2, 0, 3), (2, 0, 1, 3))
EARLY, LATE = range(0, 3), range(3, 6)
PIECE = 256
GROUP = 768
SHARD = D // 16
DMA = pltpu.SemaphoreType.DMA


class Links:
    def __init__(self):
        self.core = lax.axis_index("rows")
        chip = lax.axis_index("canvas")
        self.bits = (lax.axis_size("canvas") - 1).bit_length()
        self.mine = [lax.rem(lax.div(chip, 1 << b), 2) for b in range(self.bits)]
        self.there = [{"canvas": chip + (1 - 2 * m) * (1 << b)} for b, m in enumerate(self.mine)]
        self.twin = {"rows": 1 - self.core}

    def call(self):
        barrier = pltpu.get_barrier_semaphore()
        for other in [self.twin] + self.there:
            pl.semaphore_signal(barrier, inc=1, device_id=other, device_id_type=MESH_ID)

    def answer(self):
        pl.semaphore_wait(pltpu.get_barrier_semaphore(), self.bits + 1)

    def greet(self):
        self.call()
        self.answer()


def remote(src, dst, send, recv, other):
    return pltpu.make_async_remote_copy(
        src_ref=src,
        dst_ref=dst,
        send_sem=send,
        recv_sem=recv,
        device_id=other,
        device_id_type=MESH_ID,
    )


class Pieces:
    count = 6

    def __init__(self, links, lanes):
        self.links = links
        self.width = lanes // self.count

    def lanes(self, p):
        return slice(p * self.width, p * self.width + self.width)

    def bit(self, p, s):
        return ORDERS[p % 3][s]

    def start(self, p, s):
        at = 0
        for t in range(s):
            at = at + self.links.mine[self.bit(p, t)] * (D >> (t + 1))
        return at

    def held(self, p, s):
        return pl.ds(pl.multiple_of(self.start(p, s), 8), D >> s)


class Reduce(Pieces):
    def __init__(self, links, src, buf, work):
        super().__init__(links, src.shape[-1])
        self.src, self.buf = src, buf
        self.first, self.land, self.pair_sem, self.send_sem, self.recv_sem = work

    @classmethod
    def scratch(cls, lanes, bits):
        steps = max(bits, 4)
        return [
            pltpu.VMEM((D, lanes), F32),
            pltpu.VMEM((D - SHARD + (steps - 4) * SHARD, lanes), F32),
            DMA((2, cls.count)),
            DMA((cls.count, steps)),
            DMA((cls.count, steps)),
        ]

    def add(self, p, rows, src, src_rows):
        lanes = self.lanes(p)
        self.buf[rows, lanes] += src[src_rows, lanes]

    def pair(self, p):
        lanes = self.lanes(p)
        return remote(
            self.src.at[1 - self.links.core, :, lanes],
            self.first.at[:, lanes],
            self.pair_sem.at[0, p],
            self.pair_sem.at[1, p],
            self.links.twin,
        )

    def move(self, p, s):
        b = self.bit(p, s)
        half = D >> (s + 1)
        away = pl.multiple_of(self.start(p, s) + (1 - self.links.mine[b]) * half, 8)
        lanes = self.lanes(p)
        return remote(
            self.buf.at[pl.ds(away, half), lanes],
            self.land.at[pl.ds(D - (D >> s), half), lanes],
            self.send_sem.at[p, s],
            self.recv_sem.at[p, s],
            self.links.there[b],
        )

    def begin(self):
        for p in range(self.count):
            self.pair(p).start()

    def join(self, some):
        for p in some:
            self.pair(p).wait()
            self.add(p, pl.ds(0, D), self.first, pl.ds(0, D))
            self.move(p, 0).start()

    def launch(self):
        for p in range(self.count):
            self.move(p, 0).start()

    def down(self, s, some, last=3):
        for p in some:
            self.move(p, s).wait()
            self.add(p, self.held(p, s + 1), self.land, pl.ds(D - (D >> s), D >> (s + 1)))
            if s < last:
                self.move(p, s + 1).start()
        if s == 3:
            for b in range(4, self.links.bits):
                self.swap(b, some)

    def swap(self, b, some):
        at = pl.ds(D - SHARD + (b - 4) * SHARD, SHARD)
        copies = {}
        for p in some:
            lanes = self.lanes(p)
            copies[p] = remote(
                self.buf.at[self.held(p, 4), lanes],
                self.land.at[at, lanes],
                self.send_sem.at[p, b],
                self.recv_sem.at[p, b],
                self.links.there[b],
            )
            copies[p].start()
        for p in some:
            copies[p].wait()
            self.add(p, self.held(p, 4), self.land, at)


class Gather(Pieces):
    def __init__(self, links, whole, dst, work):
        super().__init__(links, whole.shape[1])
        self.whole, self.dst = whole, dst
        self.send_sem, self.recv_sem, self.out_sem = work

    @classmethod
    def scratch(cls, lanes):
        return [DMA((cls.count, 4)), DMA((cls.count, 4)), DMA((2, 3, cls.count))]

    def back(self, p, s):
        view = self.whole.at[self.held(p, s + 1), self.lanes(p)]
        return remote(
            view,
            view,
            self.send_sem.at[p, s],
            self.recv_sem.at[p, s],
            self.links.there[self.bit(p, s)],
        )

    def outs(self, p, n):
        mine = self.links.mine[self.bit(p, 0)]
        half = D // 2
        at = pl.multiple_of(half * (mine if n == 0 else 1 - mine), 8)
        rows = pl.ds(at, half)
        src = self.whole.at[rows, self.lanes(p)]
        dst = self.dst.at[self.links.core, rows, self.lanes(p)]
        sem = self.out_sem.at[n]
        return (
            pltpu.make_async_copy(src, dst, sem.at[0, p]),
            remote(src, dst, sem.at[1, p], sem.at[2, p], self.links.twin),
        )

    def begin(self, some):
        for p in some:
            self.back(p, 3).start()

    def up(self, s, some):
        for p in some:
            self.back(p, s).wait()
            if s > 0:
                self.back(p, s - 1).start()
            if s < 2:
                for copy in self.outs(p, 1 - s):
                    copy.start()

    def end(self):
        for n in range(2):
            for p in range(self.count):
                for copy in self.outs(p, n):
                    copy.wait()


class Turn(Pieces):
    def __init__(self, links, rest, whole, work):
        super().__init__(links, whole.shape[1])
        self.rest, self.whole = rest, whole
        self.land, self.send_sem, self.recv_sem = work

    @classmethod
    def scratch(cls, lanes, bits):
        steps = max(bits, 4) - 3
        return [
            pltpu.VMEM((steps * SHARD, lanes), F32),
            DMA((cls.count, steps)),
            DMA((cls.count, steps)),
        ]

    def move(self, p, n):
        lanes = self.lanes(p)
        if n == 0:
            b = self.bit(p, 3)
            at = pl.multiple_of((1 - self.links.mine[b]) * SHARD, 8)
            src = self.rest.at[pl.ds(at, SHARD), lanes]
        else:
            b = 3 + n
            src = self.whole.at[self.held(p, 4), lanes]
        return remote(
            src,
            self.land.at[n * SHARD : n * SHARD + SHARD, lanes],
            self.send_sem.at[p, n],
            self.recv_sem.at[p, n],
            self.links.there[b],
        )

    def begin(self):
        for p in range(self.count):
            self.move(p, 0).start()

    def end(self, some):
        for p in some:
            lanes = self.lanes(p)
            at = pl.multiple_of(self.links.mine[self.bit(p, 3)] * SHARD, 8)
            self.move(p, 0).wait()
            self.whole[self.held(p, 4), lanes] = (
                self.rest[pl.ds(at, SHARD), lanes] + self.land[0:SHARD, lanes]
            )
        for n in range(1, self.links.bits - 3):
            for p in some:
                self.move(p, n).start()
            for p in some:
                lanes = self.lanes(p)
                self.move(p, n).wait()
                self.whole[self.held(p, 4), lanes] += self.land[n * SHARD : n * SHARD + SHARD, lanes]


def row_flags(tall_ref, rows_all):
    ends = image_ends(tall_ref)

    def above(row):
        first = (row == 0) | (row == ends[0]) | (row == ends[1]) | (row == ends[2])
        return jnp.where(first, 0.0, 1.0)

    def below(row):
        return jnp.where(row + 1 == rows_all, 0.0, above(row + 1))

    return above, below


def middle_kernel(
    tall_ref,
    temp_ref,
    x_hbm,
    dy_hbm,
    v_hbm,
    sums_ref,
    wp_ref,
    w1_hbm,
    w2_ref,
    tab_ref,
    out_hbm,
    ds1_hbm,
    dmx_hbm,
    dwp_ref,
    shard_ref,
    gtab_ref,
    probs_ref,
    unit_ref,
    gprob_ref,
    joint_ref,
    wpv,
    wph,
    w1c,
    w2c,
    pcat,
    mixed,
    s1,
    li,
    act,
    slope,
    mid,
    s2,
    ds2,
    gp,
    n2c,
    dzc,
    b1_ref,
    b1g_ref,
    acc,
    cross,
    x_ref,
    dy_ref,
    v_ref,
    flags,
    nt,
    dt,
    peer_ref,
    dw_ref,
    load_sem,
    store_sem,
    edge_sem,
    *work,
):
    links = Links()
    core = links.core
    wide = x_ref.shape[0]
    tokens = wide - HALO
    dw1_ref, dw2_ref = dw_ref.at[0], dw_ref.at[1]
    reduce = Reduce(links, dw_ref, dw_ref.at[core], work)
    w1_ref = work[0]
    lo_ = x_ref
    own = pl.ds(pl.multiple_of(core * HALO, HALO), tokens)
    pairs = ((w1_hbm, w1_ref), (v_hbm, v_ref.at[own]), (x_hbm, x_ref.at[own]), (dy_hbm, dy_ref.at[own]))
    loads = [pltpu.make_async_copy(a, b, load_sem.at[i]) for i, (a, b) in enumerate(pairs)]
    for load in loads:
        load.start()
    links.call()
    edge = pl.ds(pl.multiple_of((1 - core) * (tokens - HALO), HALO), HALO)
    far = pl.ds(pl.multiple_of(core * tokens, HALO), HALO)
    pairs = (
        (sums_ref.at[2], peer_ref),
        (v_hbm.at[edge], v_ref.at[far]),
        (x_hbm.at[edge], x_ref.at[far]),
        (dy_hbm.at[edge], dy_ref.at[far]),
    )
    edges = [
        remote(a, b, edge_sem.at[0, i], edge_sem.at[1, i], links.twin)
        for i, (a, b) in enumerate(pairs)
    ]
    own_rows = tokens // COLS
    rows_wide = wide // COLS
    rows_all = 2 * own_rows
    first_row = core * (own_rows - HALO // COLS)
    own_off = pl.multiple_of(core * HALO, HALO)
    mlp = w1_hbm.shape[1]
    spans = slots(tall_ref, core, first_row, rows_all)
    above, below = row_flags(tall_ref, rows_all)

    def tab(r):
        return tab_ref[r : r + 1]

    def is_own(row):
        return (row >= core * (HALO // COLS)) & (row < core * (HALO // COLS) + own_rows)

    loads[0].wait()

    def part_1(o):
        rows = pl.ds(o, 64)
        h, l = halves(w1_ref[rows])
        w1c[rows] = h
        w1c[pl.ds(D + o, 64)] = h
        w1c[pl.ds(2 * D + o, 64)] = l

    sweep(D, 64, part_1)
    links.answer()
    for copy in edges:
        copy.start()

    def part_p(o):
        rows = pl.ds(o, 192)
        h, l = halves(wp_ref[rows])
        wpv[rows] = h
        wpv[pl.ds(D + o, 192)] = h
        wpv[pl.ds(2 * D + o, 192)] = l
        wph[rows, 0:D] = h
        wph[rows, D : 2 * D] = h
        wph[rows, 2 * D : 3 * D] = l

    sweep(D, 192, part_p)

    def part_2(o):
        rows = pl.ds(o, 256)
        h, l = halves(w2_ref[rows])
        w2c[rows, 0:D] = h
        w2c[rows, D : 2 * D] = h
        w2c[rows, 2 * D : 3 * D] = l

    sweep(mlp, 256, part_2)

    edges[0].wait()
    ones = group_ones()
    temp = head_row(temp_ref)
    joint_ref[...] = sums_ref[2] + peer_ref[...]

    def probabilities(s, carry):
        sums = jnp.where(s == 2, joint_ref[...], sums_ref[s])
        inv_q = lax.rsqrt(sums[HD : HD + 1] + EPS)
        inv_k = lax.rsqrt(sums[HD + 1 : HD + 2] + EPS)
        unit = sums[0:HD] * row_to_fold(inv_q, ones) * inv_k
        unit_ref[s] = unit
        weight = jnp.exp(temp * unit)
        probs = weight / group_sum(weight, ones)
        probs_ref[s] = probs
        h, l = halves(unfold(probs))
        lanes = pl.ds(pl.multiple_of(3 * D * s, 128), 3 * D)
        pcat[:, lanes] = jnp.concatenate([h, h, l], axis=1)
        return carry

    lax.fori_loop(0, 3, probabilities, 0)

    acc[...] = jnp.zeros_like(acc)
    gtab_ref[...] = jnp.zeros_like(gtab_ref)

    def add(r, v):
        acc[8 * r : 8 * r + 8] += v

    for copy in loads[1:] + edges[1:]:
        copy.wait()

    def own_part(o, size):
        token = o + lax.broadcasted_iota(jnp.int32, (size, D), 0)
        return jnp.where((token >= own_off) & (token < own_off + tokens), 1.0, 0.0)

    def attend(o):
        size = wide // 3
        mix = mix_nt(by_slot(v_ref[pl.ds(o, size)], slot_masks(o, size, spans)), pcat)
        mixed[pl.ds(o, size)] = mix
        z = dot_nn(side(mix), wpv[...]) + tab(PB)
        rows = pl.ds(o, size)
        branch = tab(SA) * z
        stream = x_ref[rows] + branch
        s1[rows] = stream
        xhat, _ = normalize(stream)
        li[pl.ds(pl.multiple_of(o + COLS, COLS), size)] = xhat * tab(N3G) + tab(N3S)
        add(41, eights(own_part(o, size) * branch * branch))

    sweep(wide, wide // 3, attend)

    pad = jnp.zeros((COLS, D), F32)
    for buf in (li, mid, gp, ds2):
        buf[0:COLS] = pad
        buf[wide + COLS : wide + 2 * COLS] = pad

    for r in range(rows_wide):
        row = first_row + r
        mine = jnp.where(is_own(r), 1.0, 0.0)
        for n, flag in enumerate((above(row), below(row), mine)):
            flags[n, r * COLS : r * COLS + COLS] = jnp.full((COLS, 128), flag, F32)

    block = 12 * COLS
    col = lax.rem(lax.broadcasted_iota(jnp.int32, (block + 2 * COLS, 128), 0), COLS)

    def convolve(src, base, flip, scale, visit, other=None, events=()):
        def one(n, carry):
            for when, event in events:
                pl.when(n == when)(event)
            lanes = pl.ds(pl.multiple_of(lax.rem(n, 3) * 128, 128), 128)
            m = lax.div(n, 3)
            place = lax.div((m - 1) * (m - 2), 2) + 2 * core * m * (2 - m) + (1 - core) * m * (m - 1)
            o = pl.multiple_of(place * block, block)
            rows = pl.ds(o, block)
            taps = [tab_ref[base + t : base + t + 1, lanes] for t in range(9)]
            if flip:
                taps = taps[::-1]
            if scale is not None:
                taps = [t * tab_ref[scale : scale + 1, lanes] for t in taps]
            u = src[pl.ds(o, block + 2 * COLS), lanes]
            left = jnp.where(col == 0, 0.0, pltpu.roll(u, 1, 0))
            right = jnp.where(col == COLS - 1, 0.0, pltpu.roll(u, block + 2 * COLS - 1, 0))
            up, down = flags[0, rows], flags[1, rows]

            def line(a):
                cut = slice(a * COLS, a * COLS + block)
                return left[cut] * taps[3 * a] + u[cut] * taps[3 * a + 1] + right[cut] * taps[3 * a + 2]

            visit(o, rows, lanes, line(1) + up * line(0) + down * line(2))
            if other is not None:
                near = other[pl.ds(o, block + 2 * COLS), lanes]
                mine = flags[2, rows]
                held = (
                    mine * up * near[0:block],
                    mine * near[COLS : COLS + block],
                    mine * down * near[2 * COLS : 2 * COLS + block],
                )
                inner = slice(COLS, COLS + block)
                for a in range(3):
                    for b, view in enumerate((right, u, left)):
                        t = 8 * (base + 3 * a + b)
                        acc[t : t + 8, lanes] += eights(view[inner] * held[a])
            return carry

        lax.fori_loop(0, 3 * (wide // block), one, 0)

    def first(o, rows, lanes, value):
        at = pl.ds(o + COLS, block)
        a, s = gelu_parts(value + tab_ref[C1B : C1B + 1, lanes])
        act[rows, lanes] = a
        slope[rows, lanes] = s
        mid[at, lanes] = a * tab_ref[BG : BG + 1, lanes] + tab_ref[BS : BS + 1, lanes]

    convolve(li, K1R, False, None, first)

    def second(o, rows, lanes, value):
        value = value + tab_ref[C2B : C2B + 1, lanes]
        lo_[rows, lanes] = value
        branch = tab_ref[SL : SL + 1, lanes] * value
        s2[rows, lanes] = s1[rows, lanes] + branch
        acc[8 * 42 : 8 * 42 + 8, lanes] += eights(flags[2, rows] * branch * branch)

    convolve(mid, K2R, False, None, second)

    dw1_ref[...] = jnp.zeros_like(dw1_ref)
    dw2_ref[...] = jnp.zeros_like(dw2_ref)
    b1g_ref[...] = jnp.zeros_like(b1g_ref)
    for i in range(mlp // D):
        b1_ref[0:1, i * D : i * D + D] = tab(F1B + i)

    def feed(o):
        here = pl.ds(o, TILE)
        xhat, _ = normalize(s2[here])
        n2 = xhat * tab(N2G) + tab(N2S)
        n2c[...] = side(n2)
        dz = tab(SM) * dy_ref[here]
        dzc[...] = side(dz)
        nt[...] = side(n2.T)
        dt[...] = side(dz.T)
        add(F2B, eights(dz))

        padded = pl.ds(pl.multiple_of(o + COLS, COLS), TILE)
        gp[COLS : COLS + TILE] = jnp.broadcast_to(tab(F2B), (TILE, D))
        ds2[padded] = jnp.zeros((TILE, D), F32)

        def chunk(j):
            return pl.ds(pl.multiple_of(j, PIECE), PIECE)

        def enter(j):
            return dot_nn(n2c[...], w1c[:, chunk(j)]), dot_nt(dzc[...], w2c[chunk(j)])

        def chunks(first):
            raw = dn = 0.0
            ready = enter(first)
            for j in range(0, GROUP, PIECE):
                lanes = chunk(first + j)
                pre, dh = ready
                if j + PIECE < GROUP:
                    ready = enter(first + j + PIECE)
                a, slope_j = gelu_parts(pre + b1_ref[0:1, lanes])
                dp = dh * slope_j
                ah, al = halves(a)
                ph, pl_ = halves(dp)
                w2h, w2l = w2c[lanes, 0:D], w2c[lanes, 2 * D : 3 * D]
                raw = raw + (dot_nn(ah, w2h) + (dot_nn(al, w2h) + dot_nn(ah, w2l)))
                w1h, w1l = w1c[0:D, lanes], w1c[2 * D : 3 * D, lanes]
                dn = dn + (dot_nt(ph, w1h) + (dot_nt(pl_, w1h) + dot_nt(ph, w1l)))
                b1g_ref[:, lanes] += eights(dp)
                dw1_ref[:, lanes] += dot_nn(nt[...], jnp.concatenate([ph, ph, pl_], axis=0))
                dw2_ref[:, lanes] += dot_nn(dt[...], jnp.concatenate([ah, ah, al], axis=0))
            gp[COLS : COLS + TILE] += raw
            ds2[padded] += dn

        sweep(mlp, GROUP, chunks)
        raw, dn = gp[COLS : COLS + TILE], ds2[padded]
        dy = dy_ref[here]
        xhat, r = normalize(s2[here])
        ds2[pl.ds(pl.multiple_of(o + COLS, COLS), TILE)] = dy + normalize_back(dn * tab(N2G), xhat, r)
        branch = tab(SM) * raw
        result = s2[here] + branch
        s2[here] = result
        add(40, eights(result * result))
        add(43, eights(branch * branch))
        add(SM, eights(dy * raw))
        add(N2G, eights(dn * xhat))
        add(N2S, eights(dn))

    def feed_one(i, carry):
        feed(pl.multiple_of(own_off + i * TILE, 128))
        return carry

    lax.fori_loop(0, tokens // TILE, feed_one, 0)
    reduce.begin()
    stores = [pltpu.make_async_copy(s2.at[own], out_hbm, store_sem.at[0])]
    stores[0].start()
    edge = HALO // 2
    rest = pl.multiple_of(COLS + (1 - core) * (tokens + edge), COLS)
    ds2[pl.ds(rest, edge)] = jnp.zeros((edge, D), F32)
    rows_out = pl.multiple_of(COLS + own_off + (1 - core) * (tokens - edge), COLS)
    rows_in = pl.multiple_of(COLS + edge + core * (tokens - edge), COLS)
    turned = remote(
        ds2.at[pl.ds(rows_out, edge)],
        ds2.at[pl.ds(rows_in, edge)],
        edge_sem.at[0, 4],
        edge_sem.at[1, 4],
        links.twin,
    )
    turned.start()

    def third(o, rows, lanes, value):
        grad = value * tab_ref[BG : BG + 1, lanes] * slope[rows, lanes]
        gp[pl.ds(o + COLS, block), lanes] = grad
        held = flags[2, rows] * value
        acc[8 * BG : 8 * BG + 8, lanes] += eights(held * act[rows, lanes])
        acc[8 * BS : 8 * BS + 8, lanes] += eights(held)
        acc[8 * C1B : 8 * C1B + 8, lanes] += eights(flags[2, rows] * grad)

    convolve(
        ds2,
        K2R,
        True,
        SL,
        third,
        mid,
        ((5, lambda: reduce.join(EARLY)), (6, turned.wait), (8, lambda: reduce.join(LATE))),
    )

    def fourth(o, rows, lanes, value):
        slope[rows, lanes] = value

    convolve(gp, K1R, True, None, fourth, li, ((6, lambda: reduce.down(0, EARLY, 2)),))

    dwp_ref[...] = jnp.zeros_like(dwp_ref)
    cross[...] = jnp.zeros_like(cross)

    def back(step):
        o = pl.multiple_of(own_off + step * TILE, 128)

        here_wide = pl.ds(o, TILE)
        xhat, r = normalize(s1[here_wide])
        grad = slope[here_wide]
        grad_two = ds2[pl.ds(pl.multiple_of(o + COLS, COLS), TILE)]
        result = grad_two + normalize_back(grad * tab(N3G), xhat, r)
        slope[here_wide] = result
        add(N3G, eights(grad * xhat))
        add(N3S, eights(grad))
        add(SL, eights(grad_two * lo_[here_wide]))
        add(C2B, eights(grad_two))
        add(PB, eights(result))
        dmx = dot_nt(side(tab(SA) * result), wph[...])
        act[here_wide] = dmx
        h, l = halves(result)
        dwp_ref[...] += dot_nn(side(mixed[pl.ds(o, TILE)].T), jnp.concatenate([h, h, l], axis=0))
        cross[...] += dot_nn(side(dmx.T), slots_below(v_ref[pl.ds(o, TILE)], slot_masks(o, TILE, spans)))

    def back_one(step, carry):
        back(step)
        pl.when(step == 0)(lambda: reduce.down(0, LATE, 2))
        pl.when(step == 1)(lambda: reduce.down(1, EARLY, 2))
        pl.when(step == 2)(lambda: reduce.down(1, LATE, 2))
        return carry

    lax.fori_loop(0, tokens // TILE, back_one, 0)
    for src, dst in ((slope, ds1_hbm), (act, dmx_hbm)):
        stores.append(pltpu.make_async_copy(src.at[own], dst, store_sem.at[len(stores)]))
        stores[-1].start()
    for s in range(3):
        gprob_ref[s] = fold(cross[:, s * D : s * D + D])

    def total(r):
        return jnp.sum(acc[8 * r : 8 * r + 8], axis=0, keepdims=True)

    for r in (N3G, N3S, N2G, N2S, SL, SM, C1B, BG, BS, F2B, 40, 41, 42, 43):
        gtab_ref[r : r + 1] = total(r)
    for t in range(9):
        gtab_ref[K1R + t : K1R + t + 1] = total(K1R + t)
        gtab_ref[K2R + t : K2R + t + 1] = total(K2R + t) * tab(SL)
    gtab_ref[C2B : C2B + 1] = total(C2B) * tab(SL)
    gtab_ref[PB : PB + 1] = total(PB) * tab(SA)
    raw = dwp_ref[...]
    gtab_ref[SA : SA + 1] = jnp.sum(raw * wp_ref[...], axis=0, keepdims=True) + total(PB) * tab(PB)
    dwp_ref[...] = raw * tab(SA)
    for i in range(mlp // D):
        gtab_ref[F1B + i : F1B + i + 1] = jnp.sum(b1g_ref[:, i * D : i * D + D], axis=0, keepdims=True)
    reduce.down(2, EARLY, 2)
    reduce.down(2, LATE, 2)
    for p in range(reduce.count):
        lanes = reduce.lanes(p)
        shard_ref[:, lanes] = reduce.buf[reduce.held(p, 3), lanes]
    for copy in stores:
        copy.wait()


def middle(tall, temp, x, dy, v, sums, wp, w1, w2, tab):
    tokens = x.shape[0]
    wide = tokens + HALO
    mlp = w1.shape[1]
    smem = pl.BlockSpec(memory_space=pltpu.SMEM)
    vmem = pl.BlockSpec(memory_space=pltpu.VMEM)
    anywhere = pl.BlockSpec(memory_space=pl.ANY)

    def f(*shape):
        return jax.ShapeDtypeStruct(shape, F32)

    def s(*shape):
        return pltpu.VMEM(shape, F32)

    def b(*shape):
        return pltpu.VMEM(shape, BF)

    padded = s(wide + 2 * COLS, D)
    return pl.pallas_call(
        middle_kernel,
        out_shape=[
            f(tokens, D),
            f(tokens, D),
            f(tokens, D),
            f(D, D),
            f(2 * SHARD, mlp),
            f(TABLE, D),
            f(3, HD, D),
            f(3, HD, D),
            f(3, HD, D),
            f(*sums.shape[1:]),
        ],
        in_specs=[smem, smem] + [anywhere] * 3 + [vmem, vmem, anywhere, vmem, vmem],
        out_specs=[anywhere] * 3 + [vmem] * 7,
        scratch_shapes=[
            b(3 * D, D),
            b(D, 3 * D),
            b(3 * D, mlp),
            b(mlp, 3 * D),
            b(D, 9 * D),
            s(wide, D),
            s(wide, D),
            padded,
            s(wide, D),
            s(wide, D),
            padded,
            s(wide, D),
            padded,
            padded,
            b(TILE, 3 * D),
            b(TILE, 3 * D),
            s(8, mlp),
            s(8, mlp),
            s(8 * TABLE, D),
            s(D, 3 * D),
            s(wide, D),
            s(wide, D),
            s(wide, D),
            s(3, wide, 128),
            b(D, 3 * TILE),
            b(D, 3 * TILE),
            s(*sums.shape[1:]),
            s(2, D, mlp),
            DMA((4,)),
            DMA((3,)),
            DMA((2, 5)),
        ]
        + Reduce.scratch(mlp, (lax.axis_size("canvas") - 1).bit_length()),
        compiler_params=pltpu.CompilerParams(
            collective_id=0, has_side_effects=True, vmem_limit_bytes=60 << 20
        ),
    )(tall, temp, x, dy, v, sums, wp, w1, w2, tab)


def finish_kernel(
    tall_ref,
    temp_ref,
    x_ref,
    q_ref,
    k_ref,
    ds1_ref,
    dmx_ref,
    sums_ref,
    peer_ref,
    probs_ref,
    unit_ref,
    gprob_ref,
    w_ref,
    tab_ref,
    gtab_ref,
    dwp_ref,
    shard_ref,
    dx_ref,
    end_ref,
    town_ref,
    sum_hbm,
    wh,
    wl,
    pv,
    cv,
    ch,
    side_rows,
    acc,
    gpeer_ref,
    whole,
    dw_ref,
    otab_ref,
    end_first,
    tab_first,
    gsend,
    grecv,
    pair_sem,
    *work,
):
    step = pl.program_id(0)
    last = pl.num_programs(0) - 1
    links = Links()
    core = links.core
    turn = Turn(links, shard_ref, whole, work[:3])
    gather = Gather(links, whole, sum_hbm, work[3:])
    rows_all = 2 * pl.num_programs(0) * TILE // COLS
    spans = slots(tall_ref, core, core * (rows_all // 2), rows_all)
    start = step * TILE

    def tab(r):
        return tab_ref[r : r + 1]

    @pl.when(step == 0)
    def _():
        links.greet()
        swap = remote(gprob_ref.at[2], gpeer_ref, gsend, grecv, links.twin)
        swap.start()
        turn.begin()

        def part(o):
            h, l = halves(w_ref[pl.ds(o, 64)])
            wh[pl.ds(o, 64)] = h
            wl[pl.ds(o, 64)] = l

        sweep(D, 64, part)
        dw_ref[...] = jnp.zeros_like(dw_ref)
        dw_ref[1, :, D : 2 * D] = dwp_ref[...]
        acc[...] = jnp.zeros_like(acc)
        ones = group_ones()
        temp = head_row(temp_ref)
        swap.wait()

        def slot(s, heat):
            sums = jnp.where(s == 2, peer_ref[...], sums_ref[s])
            grad = gprob_ref[s] + jnp.where(s == 2, gpeer_ref[...], 0.0)
            inv_q = lax.rsqrt(sums[HD : HD + 1] + EPS)
            inv_k = lax.rsqrt(sums[HD + 1 : HD + 2] + EPS)
            probs = probs_ref[s]
            unit = unit_ref[s]
            scores = probs * (grad - group_sum(probs * grad, ones))
            part_heat = jnp.sum(scores * unit, axis=0, keepdims=True)
            heat = heat + jnp.where((s < 2) | (core == 0), part_heat, 0.0)
            pull = temp * scores
            both = pull * unit
            query = fold_to_row(group_sum(both, ones)) * inv_q * inv_q
            key = jnp.sum(both, axis=0, keepdims=True) * inv_k * inv_k
            side_rows[pl.ds(pl.multiple_of(8 * s, 8), 8)] = jnp.concatenate(
                [query, key, jnp.zeros((6, D), F32)], axis=0
            )
            across = pl.ds(pl.multiple_of(3 * D * s, 128), 3 * D)
            h, l = halves(unfold(pull * row_to_fold(inv_q, ones) * inv_k))
            cv[across] = jnp.concatenate([h, h, l], axis=0)
            ch[:, across] = jnp.concatenate([h, h, l], axis=1)
            h, l = halves(unfold(probs))
            pv[across] = jnp.concatenate([h, h, l], axis=0)
            return heat

        heat = lax.fori_loop(0, 3, slot, jnp.zeros((1, D), F32))
        otab_ref[...] = gtab_ref[...]
        otab_ref[44:45] = heat

    masks = [span_mask(start, TILE, lo, hi) for lo, hi in spans]
    factors = slot_masks(start, TILE, spans)

    def rows_of(r):
        return sum(jnp.where(mask, side_rows[8 * s + r : 8 * s + r + 1], 0.0) for s, mask in enumerate(masks))

    def at(n, *events):
        @pl.when(step == n)
        def _():
            for event, *args in events:
                event(*args)

    q, k = q_ref[...], k_ref[...]
    dq = mix_nt(by_slot(k, factors), ch) - q * rows_of(0)
    dk = mix_nn(by_slot(q, factors), cv) - k * rows_of(1)
    dv = mix_nn(by_slot(dmx_ref[...], factors), pv)
    dqkv = jnp.concatenate([dq, dk, dv], axis=1)
    at(0, (turn.end, EARLY), (gather.begin, EARLY))
    at(1, (gather.up, 3, EARLY))
    at(2, (gather.up, 2, LATE))
    at(3, (gather.up, 1, LATE))

    h, l = halves(dqkv)
    dn = dot_nt(h, wh[...]) + (dot_nt(l, wh[...]) + dot_nt(h, wl[...]))
    xhat, r = normalize(x_ref[...])
    nt = side((xhat * tab(N1G) + tab(N1S)).T)
    grads = dot_nn(nt, jnp.concatenate([h, h, l], axis=0))
    dw_ref[0] += grads[:, 0 : 2 * D]
    dw_ref[1, :, 0:D] += grads[:, 2 * D : 3 * D]
    dx_ref[...] = ds1_ref[...] + normalize_back(dn * tab(N1G), xhat, r)
    acc[0:8] += eights(dn * xhat)
    acc[8:16] += eights(dn)
    for i, v in enumerate((dq, dk, dv)):
        acc[16 + 8 * i : 24 + 8 * i] += eights(v)

    at(0, (turn.end, LATE), (gather.begin, LATE))
    at(1, (gather.up, 3, LATE), (gather.up, 2, EARLY))
    at(2, (gather.up, 1, EARLY))

    @pl.when(step == last)
    def _():
        for i, r in enumerate((N1G, N1S, QB, KB, VB)):
            otab_ref[r : r + 1] = jnp.sum(acc[8 * i : 8 * i + 8], axis=0, keepdims=True)
        trows = tab_first.shape[0]
        near = pl.ds(pl.multiple_of(core * trows, 8), trows)
        far = pl.ds(pl.multiple_of((1 - core) * trows, 8), trows)
        pairs = [(otab_ref.at[far], tab_first)]
        for p in range(end_first.shape[1] // 128):
            lanes = slice(p * 128, p * 128 + 128)
            pairs.append((dw_ref.at[1 - core, :, lanes], end_first.at[:, lanes]))
        copies = [
            remote(a, b, pair_sem.at[0, i], pair_sem.at[1, i], links.twin)
            for i, (a, b) in enumerate(pairs)
        ]
        for copy in copies:
            copy.start()
        gather.up(0, EARLY)
        gather.up(0, LATE)
        for copy in copies:
            copy.wait()
        town_ref[...] = otab_ref[near] + tab_first[...]
        end_ref[...] = dw_ref[core] + end_first[...]
        gather.end()


def finish(tall, temp, x, q, k, ds1, dmx, sums, peer, probs, unit, gprob, w, tab, gtab, dwp, shard):
    tokens = x.shape[0]
    smem = pl.BlockSpec(memory_space=pltpu.SMEM)
    anywhere = pl.BlockSpec(memory_space=pl.ANY)
    row = pl.BlockSpec((TILE, D), lambda i: (i, 0))
    bits = (lax.axis_size("canvas") - 1).bit_length()

    def whole(v):
        return pl.BlockSpec(v.shape, lambda i: (0,) * v.ndim)

    fixed = (sums, peer, probs, unit, gprob, w, tab, gtab, dwp, shard)
    return pl.pallas_call(
        finish_kernel,
        grid=(tokens // TILE,),
        out_shape=[
            jax.ShapeDtypeStruct((tokens, D), F32),
            jax.ShapeDtypeStruct((D, 2 * D), F32),
            jax.ShapeDtypeStruct((TABLE // 2, D), F32),
            jax.ShapeDtypeStruct((2, D, shard.shape[1]), F32),
        ],
        in_specs=[smem, smem] + [row] * 5 + [whole(v) for v in fixed],
        out_specs=[
            row,
            pl.BlockSpec((D, 2 * D), lambda i: (0, 0)),
            pl.BlockSpec((TABLE // 2, D), lambda i: (0, 0)),
            anywhere,
        ],
        scratch_shapes=[
            pltpu.VMEM((D, 3 * D), BF),
            pltpu.VMEM((D, 3 * D), BF),
            pltpu.VMEM((9 * D, D), BF),
            pltpu.VMEM((9 * D, D), BF),
            pltpu.VMEM((D, 9 * D), BF),
            pltpu.VMEM((24, D), F32),
            pltpu.VMEM((40, D), F32),
            pltpu.VMEM(gprob.shape[1:], F32),
            pltpu.VMEM((D, shard.shape[1]), F32),
            pltpu.VMEM((2, D, 2 * D), F32),
            pltpu.VMEM((TABLE, D), F32),
            pltpu.VMEM((D, 2 * D), F32),
            pltpu.VMEM((TABLE // 2, D), F32),
            DMA,
            DMA,
            DMA((2, 1 + 2 * D // 128)),
        ]
        + Turn.scratch(shard.shape[1], bits)
        + Gather.scratch(shard.shape[1]),
        compiler_params=pltpu.CompilerParams(
            collective_id=1, has_side_effects=True, vmem_limit_bytes=60 << 20
        ),
    )(tall, temp, x, q, k, ds1, dmx, *fixed)


NS_A, NS_B, NS_C = 3.4445, -4.7750, 2.0315


def times(a, b):
    return dot_nn(
        jnp.concatenate([a[0], a[1], a[0]], axis=1), jnp.concatenate([b[0], b[0], b[1]], axis=0)
    )


def mirrored(left, corner):
    edge = left.shape[1]
    return jnp.concatenate([left, jnp.concatenate([left[edge:].T, corner], axis=0)], axis=1)


EDGE = 2 * 128


def times_symmetric(a, b):
    lhs = jnp.concatenate([a[0], a[1], a[0]], axis=1)
    rhs = jnp.concatenate([b[0], b[0], b[1]], axis=0)
    return mirrored(dot_nn(lhs, rhs[:, :EDGE]), dot_nn(lhs[EDGE:], rhs[:, EDGE:]))


def gram_of(h, l):
    left = dot_nt(h, h[:EDGE]) + (dot_nt(l, h[:EDGE]) + dot_nt(h, l[:EDGE]))
    he, le = h[EDGE:], l[EDGE:]
    return mirrored(left, dot_nt(he, he) + (dot_nt(le, he) + dot_nt(he, le)))


def inverse_norm(v):
    total = jnp.sum(jnp.sum(v * v, axis=0, keepdims=True), axis=1, keepdims=True)
    return 1.0 / (jnp.sqrt(total) + 1e-07)


def wide_kernel(
    end_hbm,
    tab_hbm,
    mid_hbm,
    m1_hbm,
    m2_hbm,
    sum_hbm,
    otab_hbm,
    orth_hbm,
    xs,
    x,
    m1,
    m2,
    xc,
    poly,
    tbuf,
    tland,
    load_sem,
    tsend,
    trecv,
    tout,
    buf,
    own_sem,
    *work,
):
    links = Links()
    core = links.core
    reduce = Reduce(links, buf, buf, work[:5])
    gather = Gather(links, work[0], sum_hbm, work[5:])
    own = pltpu.make_async_copy(end_hbm, buf, own_sem)
    own.start()
    wide = m1.shape[1]
    blocks = wide // D
    trows = tbuf.shape[0]
    near = pl.ds(pl.multiple_of(core * trows, 8), trows)
    pairs = ((mid_hbm.at[core], x), (m1_hbm, m1), (m2_hbm, m2), (tab_hbm, tbuf))
    loads = [pltpu.make_async_copy(a, b, load_sem.at[i]) for i, (a, b) in enumerate(pairs)]
    for load in loads:
        load.start()
    links.greet()
    own.wait()
    reduce.launch()

    def table(n):
        return remote(tbuf, tland.at[n], tsend.at[n], trecv.at[n], links.there[n])

    def table_land(n):
        table(n).wait()
        tbuf[...] += tland[n]

    def down(s, some):
        reduce.down(s, some)
        if some is EARLY:
            table_land(s)
            if s < 3:
                table(s + 1).start()
        elif s == 3:
            for b in range(4, links.bits):
                table(b).start()
                table_land(b)
            for copy in touts:
                copy.start()
        if s == 3:
            for p in some:
                lanes = gather.lanes(p)
                gather.whole[gather.held(p, 4), lanes] = buf[gather.held(p, 4), lanes]
            gather.begin(some)

    touts = [
        pltpu.make_async_copy(tbuf, otab_hbm.at[near], tout.at[0]),
        remote(tbuf, otab_hbm.at[near], tout.at[1], tout.at[2], links.twin),
    ]

    for load in loads:
        load.wait()
    table(0).start()

    @pl.when(core == 0)
    def _():
        x[...] = MUON_KEEP * m1[...] + x[...]

    @pl.when(core == 1)
    def _():
        for b in range(blocks):
            lanes = slice(b * D, b * D + D)
            x[:, lanes] = MUON_KEEP * m2[lanes].T + x[:, lanes]

    inv = inverse_norm(x[...])
    chunks = [slice(o, o + 2 * PIECE) for o in range(0, wide, 2 * PIECE)]

    def keep(lanes, v):
        h, l = halves(v)
        xc[0:D, lanes] = h
        xc[D : 2 * D, lanes] = h
        xc[2 * D : 3 * D, lanes] = l

    def kept(lanes):
        return xc[0:D, lanes].astype(F32) + xc[2 * D : 3 * D, lanes].astype(F32)

    for lanes in chunks:
        keep(lanes, x[:, lanes] * inv)

    def gram():
        return gram_of(xc[0:D], xc[2 * D : 3 * D])

    schedule = {
        (0, 0): ((down, 0, LATE),),
        (0, 2): ((down, 1, EARLY),),
        (1, 0): ((down, 1, LATE),),
        (1, 1): ((down, 2, EARLY),),
        (1, 2): ((down, 2, LATE), (down, 3, EARLY)),
        (2, 0): ((down, 3, LATE),),
        (2, 1): ((gather.up, 3, EARLY),),
        (2, 2): ((gather.up, 3, LATE),),
        (3, 0): ((gather.up, 2, EARLY),),
        (3, 1): ((gather.up, 2, LATE),),
        (3, 2): ((gather.up, 1, EARLY),),
        (4, 0): ((gather.up, 1, LATE),),
    }

    def step(i, carry):
        def events(n):
            for turn in range(5):
                if (turn, n) in schedule:

                    @pl.when(i == turn)
                    def _():
                        for event, *args in schedule[turn, n]:
                            event(*args)

        g0 = gram()
        g = halves(g0)
        events(0)
        poly[...] = side(NS_B * g0 + NS_C * times_symmetric(g, g))
        events(1)

        def apply_to(o):
            lanes = pl.ds(pl.multiple_of(o, 2 * PIECE), 2 * PIECE)
            keep(lanes, NS_A * kept(lanes) + dot_nn(poly[...], xc[:, lanes]))

        sweep(wide, 2 * PIECE, apply_to)
        events(2)
        return carry

    down(0, EARLY)
    lax.fori_loop(0, 5, step, 0)
    for lanes in chunks:
        x[:, lanes] = kept(lanes)

    @pl.when(core == 0)
    def _():
        for b in range(blocks):
            xs[b] = x[:, b * D : b * D + D]

    @pl.when(core == 1)
    def _():
        for b in range(blocks):
            xs[b] = x[:, b * D : b * D + D].T

    orth = [
        pltpu.make_async_copy(xs, orth_hbm.at[core], tout.at[3]),
        remote(xs, orth_hbm.at[core], tout.at[4], tout.at[5], links.twin),
    ]
    for copy in orth:
        copy.start()
    gather.up(0, EARLY)
    gather.up(0, LATE)
    gather.end()
    for copy in touts + orth:
        copy.wait()


def wide_blocks(end, tab, mid, m1, m2):
    bits = (lax.axis_size("canvas") - 1).bit_length()
    anywhere = pl.BlockSpec(memory_space=pl.ANY)
    blocks = m1.shape[1] // D
    return pl.pallas_call(
        wide_kernel,
        out_shape=[
            jax.ShapeDtypeStruct((2,) + end.shape, F32),
            jax.ShapeDtypeStruct((TABLE, D), F32),
            jax.ShapeDtypeStruct((2, blocks, D, D), F32),
        ],
        in_specs=[anywhere] * 5,
        out_specs=[anywhere] * 3,
        scratch_shapes=[
            pltpu.VMEM((blocks, D, D), F32),
            pltpu.VMEM(m1.shape, F32),
            pltpu.VMEM(m1.shape, F32),
            pltpu.VMEM(m2.shape, F32),
            pltpu.VMEM((3 * D, m1.shape[1]), BF),
            pltpu.VMEM((D, 3 * D), BF),
            pltpu.VMEM((TABLE // 2, D), F32),
            pltpu.VMEM((bits, TABLE // 2, D), F32),
            DMA((4,)),
            DMA((bits,)),
            DMA((bits,)),
            DMA((6,)),
            pltpu.VMEM(end.shape, F32),
            DMA,
        ]
        + Reduce.scratch(end.shape[1], bits)
        + Gather.scratch(end.shape[1]),
        compiler_params=pltpu.CompilerParams(
            collective_id=2, has_side_effects=True, vmem_limit_bytes=60 << 20
        ),
    )(end, tab, mid, m1, m2)


def muon(w, orth, large):
    return w * (1.0 - MUON_RATE * DECAY) - MUON_RATE * 0.2 * math.sqrt(large) * orth


def square_kernel(
    end_hbm,
    mid_hbm,
    wide_hbm,
    mq_hbm,
    mp_hbm,
    m1_hbm,
    m2_hbm,
    w1_hbm,
    w2_hbm,
    out_hbm,
    dx_hbm,
    gq_out,
    gp_out,
    g1_out,
    g2_out,
    nq_out,
    np_out,
    n1_out,
    n2_out,
    w1_out,
    w2_out,
    c1_out,
    c2_out,
    out_out,
    dx_out,
    orth_hbm,
    end,
    mid,
    nat,
    mq,
    mp,
    m1,
    m2,
    w1,
    w2,
    c1,
    c2,
    wide,
    out,
    dx,
    xh,
    xl,
    xs,
    in_sem,
    out_sem,
):
    core = lax.axis_index("rows")
    mlp = m1.shape[1]
    blocks = mlp // D
    pairs = (
        (end_hbm, end),
        (mq_hbm, mq),
        (mp_hbm, mp),
        (mid_hbm, mid),
        (m1_hbm, m1),
        (m2_hbm, m2),
        (w1_hbm, w1),
        (w2_hbm, w2),
        (wide_hbm, wide),
        (out_hbm, out),
        (dx_hbm, dx),
    )
    loads = [pltpu.make_async_copy(a, b, in_sem.at[i]) for i, (a, b) in enumerate(pairs)]
    for load in loads:
        load.start()
    for load in loads[0:3]:
        load.wait()
    outs = (
        (end.at[0], gq_out.at[:, 0 : 2 * D]),
        (end.at[1, :, 0:D], gq_out.at[:, 2 * D : 3 * D]),
        (end.at[1, :, D : 2 * D], gp_out),
        (mq, nq_out),
        (mp, np_out),
        (mid.at[0], g1_out),
        (nat, g2_out),
        (m1, n1_out),
        (m2, n2_out),
        (out, out_out),
        (dx, dx_out),
        (w1, w1_out),
        (w2, w2_out),
        (c1, c1_out),
        (c2, c2_out),
        (xs, orth_hbm),
    )

    def store(*which):
        return [pltpu.make_async_copy(*outs[n], out_sem.at[n]) for n in which]

    def send(*which):
        for copy in store(*which):
            copy.start()

    send(0, 1, 2)

    def small(o):
        rows = pl.ds(o, 128)
        mq[rows, 0 : 2 * D] = MUON_KEEP * mq[rows, 0 : 2 * D] + end[0, rows]
        mq[rows, 2 * D : 3 * D] = MUON_KEEP * mq[rows, 2 * D : 3 * D] + end[1, rows, 0:D]
        mp[rows] = MUON_KEEP * mp[rows] + end[1, rows, D : 2 * D]

    sweep(D, 128, small)
    send(3, 4)

    def keep(b, v):
        xh[b], xl[b] = halves(v)

    @pl.when(core == 0)
    def _():
        xs[0] = mq[:, 0:D]
        xs[1] = mq[:, D : 2 * D]

    @pl.when(core == 1)
    def _():
        xs[0] = mq[:, 2 * D : 3 * D]
        xs[1] = mp[...]

    for b in range(2):
        keep(b, xs[b] * inverse_norm(xs[b]))

    def step(i, carry):
        x = [(xh[b], xl[b]) for b in range(2)]
        g = [gram_of(h, l) for h, l in x]
        pairs = [halves(v) for v in g]
        p = [NS_B * v + NS_C * times_symmetric(w, w) for v, w in zip(g, pairs)]
        pairs = [halves(v) for v in p]
        for b in range(2):
            h, l = x[b]
            keep(b, NS_A * (h.astype(F32) + l.astype(F32)) + times(pairs[b], x[b]))
        pl.when(i == 1)(moments)
        pl.when(i == 2)(weights)
        return carry

    def moments():
        for load in loads[3:6]:
            load.wait()
        send(5)
        for b in range(blocks):
            nat[b * D : b * D + D] = mid[1, :, b * D : b * D + D].T
        send(6)

        def large(o):
            rows = pl.ds(o, 64)
            m1[rows] = MUON_KEEP * m1[rows] + mid[0, rows]

        sweep(D, 64, large)
        send(7)

        def larger(o):
            rows = pl.ds(o, 256)
            m2[rows] = MUON_KEEP * m2[rows] + nat[rows]

        sweep(mlp, 256, larger)
        send(8)

    def weights():
        for load in loads[6:]:
            load.wait()
        send(9, 10)

        def block(o):
            at = pl.ds(o, D)
            b = lax.div(o, D)
            new = muon(w1[:, at], wide[0, b], mlp)
            w1[:, at] = new
            c1[:, at] = new.astype(BF)
            new = muon(w2[at], wide[1, b], mlp)
            w2[at] = new
            c2[at] = new.astype(BF)

        sweep(mlp, D, block)
        send(11, 12, 13, 14)

    lax.fori_loop(0, 5, step, 0)
    for b in range(2):
        xs[b] = xh[b].astype(F32) + xl[b].astype(F32)
    send(15)
    for copy in store(*range(len(outs))):
        copy.wait()


def square_blocks(end, mid, wide, mq, mp, m1, m2, w1, w2, out, dx):
    anywhere = pl.BlockSpec(memory_space=pl.ANY)

    def like(v, kind=F32):
        return jax.ShapeDtypeStruct(v.shape, kind)

    def room(v, kind=F32):
        return pltpu.VMEM(v.shape, kind)

    return pl.pallas_call(
        square_kernel,
        out_shape=[like(v) for v in (mq, mp, m1, m2, mq, mp, m1, m2, w1, w2)]
        + [like(w1, BF), like(w2, BF), like(out), like(dx), jax.ShapeDtypeStruct((2, D, D), F32)],
        in_specs=[anywhere] * 11,
        out_specs=[anywhere] * 15,
        scratch_shapes=[room(v) for v in (end, mid, m2, mq, mp, m1, m2, w1, w2)]
        + [room(w1, BF), room(w2, BF), room(wide), room(out), room(dx)]
        + [
            pltpu.VMEM((2, D, D), BF),
            pltpu.VMEM((2, D, D), BF),
            pltpu.VMEM((2, D, D), F32),
            DMA((11,)),
            DMA((16,)),
        ],
        compiler_params=pltpu.CompilerParams(vmem_limit_bytes=60 << 20),
    )(end, mid, wide, mq, mp, m1, m2, w1, w2, out, dx)


def trade_kernel(own_ref, peer_ref, send_sem, recv_sem):
    core = lax.axis_index("rows")
    twin = {"rows": 1 - core}
    barrier = pltpu.get_barrier_semaphore()
    pl.semaphore_signal(barrier, inc=1, device_id=twin, device_id_type=MESH_ID)
    pl.semaphore_wait(barrier, 1)
    copy = remote(own_ref, peer_ref, send_sem, recv_sem, twin)
    copy.start()
    copy.wait()


def trade(own):
    anywhere = pl.BlockSpec(memory_space=pl.ANY)
    return pl.pallas_call(
        trade_kernel,
        out_shape=jax.ShapeDtypeStruct(own.shape, F32),
        in_specs=[anywhere],
        out_specs=anywhere,
        scratch_shapes=[DMA, DMA],
        compiler_params=pltpu.CompilerParams(collective_id=3, has_side_effects=True),
    )(own)


def moment_step(current, one, two, gradient):
    first = BETA1 * one + (1.0 - BETA1) * gradient
    second = BETA2 * two + (1.0 - BETA2) * gradient * gradient
    fix_one = 1.0 - BETA1**STEP
    fix_two = 1.0 - BETA2**STEP
    updated = current - ADAM_RATE * (first / fix_one) / (jnp.sqrt(second / fix_two) + ADAM_FLOOR)
    return first, second, updated


def update_kernel(
    count,
    temp_ref,
    heat_one_ref,
    heat_two_ref,
    own_ref,
    peer_ref,
    wq_ref,
    wp_ref,
    tab_ref,
    one_ref,
    two_ref,
    gtab_ref,
    nq_ref,
    np_ref,
    cq_ref,
    cp_ref,
    first_ref,
    second_ref,
    small_ref,
    heat_first_ref,
    heat_second_ref,
    heat_ref,
    rms_ref,
):
    lower = lax.axis_index("rows") == 0
    own, peer = own_ref[...], peer_ref[...]
    low, high = jnp.where(lower, own, peer), jnp.where(lower, peer, own)
    for i, orth in enumerate((low[0], low[1], high[0])):
        lanes = slice(i * D, i * D + D)
        new = muon(wq_ref[:, lanes], orth, D)
        nq_ref[:, lanes] = new
        cq_ref[:, lanes] = new.astype(BF)
    new = muon(wp_ref[...], high[1], D)
    np_ref[...] = new
    cp_ref[...] = new.astype(BF)
    first, second, small = moment_step(tab_ref[...], one_ref[...], two_ref[...], gtab_ref[0:SMALL])
    first_ref[...] = first
    second_ref[...] = second
    small_ref[...] = small

    @pl.when(pl.program_id(0) == 0)
    def _():
        head = lax.broadcasted_iota(jnp.int32, (HEADS, D), 0)
        lane = lax.broadcasted_iota(jnp.int32, (HEADS, D), 1) // HD
        heat = jnp.sum(jnp.where(head == lane, gtab_ref[44:45], 0.0), axis=1, keepdims=True)
        head = lax.broadcasted_iota(jnp.int32, (HEADS, 1), 0)

        def column(ref):
            v = jnp.where(head == 0, ref[0], 0.0)
            for h in range(1, HEADS):
                v = jnp.where(head == h, ref[h], v)
            return v

        results = moment_step(column(temp_ref), column(heat_one_ref), column(heat_two_ref), heat)
        for ref, v in zip((heat_first_ref, heat_second_ref, heat_ref), results):
            for h in range(HEADS):
                ref[h] = v[h, 0]
        rms = jnp.sqrt(jnp.sum(gtab_ref[40:44], axis=1, keepdims=True) / count)
        for n in range(4):
            rms_ref[n] = rms[n, 0]


def update(count, temp, heat_one, heat_two, own, peer, wq, wp, tab, one, two, gtab):
    steps = 3
    piece = D // steps

    def rows(v):
        return pl.BlockSpec((piece, v.shape[1]), lambda i: (i, 0))

    def whole(v):
        return pl.BlockSpec(v.shape, lambda i: (0, 0))

    square = pl.BlockSpec((2, piece, D), lambda i: (0, i, 0))
    weights = (wq, wp)
    smem = pl.BlockSpec(memory_space=pltpu.SMEM)
    return pl.pallas_call(
        functools.partial(update_kernel, count),
        grid=(steps,),
        out_shape=[jax.ShapeDtypeStruct(w.shape, F32) for w in weights]
        + [jax.ShapeDtypeStruct(w.shape, BF) for w in weights]
        + [jax.ShapeDtypeStruct(tab.shape, F32)] * 3
        + [jax.ShapeDtypeStruct(temp.shape, F32)] * 3
        + [jax.ShapeDtypeStruct((4,), F32)],
        in_specs=[smem] * 3
        + [square, square]
        + [rows(w) for w in weights]
        + [whole(v) for v in (tab, one, two, gtab)],
        out_specs=[rows(w) for w in weights] * 2 + [whole(tab)] * 3 + [smem] * 4,
        compiler_params=pltpu.CompilerParams(vmem_limit_bytes=60 << 20),
    )(temp, heat_one, heat_two, own, peer, *weights, tab, one, two, gtab)


def on_device(
    x4, dy4, tall, wqkv, wp, w1, w2, mqkv, mp, m1, m2, tab, tab_one, tab_two, temp, temp_one, temp_two
):
    shape = x4.shape
    tokens = shape[1] * shape[2]
    x = x4.reshape(tokens, D)
    dy = dy4.reshape(tokens, D)
    q, k, v, sums = project(tall, x, wqkv, tab)
    out, ds1, dmx, dwp, shard, gtab, probs, unit, gprob, joint = middle(
        tall, temp, x, dy, v, sums, wp, w1, w2, tab
    )
    dx, end, gtab, mid = finish(
        tall, temp, x, q, k, ds1, dmx, sums, joint, probs, unit, gprob, wqkv, tab, gtab, dwp, shard
    )
    end, gtab, wide = wide_blocks(end, gtab, mid, m1, m2)
    *grads, new_1, new_2, copy_1, copy_2, out, dx, square = square_blocks(
        end, mid, wide, mqkv, mp, m1, m2, w1, w2, out, dx
    )
    count = tokens * D * lax.axis_size("rows") * lax.axis_size("canvas")
    new_q, new_p, copy_q, copy_p, *small = update(
        count, temp, temp_one, temp_two, square, trade(square), wqkv, wp, tab, tab_one, tab_two, gtab
    )
    new = (new_q, new_p, new_1, new_2, copy_q, copy_p, copy_1, copy_2)
    return (out.reshape(shape), dx.reshape(shape), *grads, *new, *small)


def solution(mesh):
    split = P("canvas", "rows", None, None)
    return jax.shard_map(
        on_device,
        mesh=mesh,
        in_specs=(split, split, P("canvas", None)) + (P(),) * 14,
        out_specs=(split, split) + (P(),) * 23,
        check_vma=False,
    )
```

```python
import functools
import math

import jax
import jax.numpy as jnp
from jax import lax
from jax.experimental import pallas as pl
from jax.experimental.pallas import tpu as pltpu
from jax.sharding import PartitionSpec as P

BF = jnp.bfloat16
F32 = jnp.float32
MESH_ID = pl.DeviceIdType.MESH

EPS = 1e-06
ROOT_HALF = 1.0 / math.sqrt(2.0)
ROOT_TWOPI = 1.0 / math.sqrt(2.0 * math.pi)
STEP = 10
MUON_RATE = 0.2
MUON_KEEP = 0.95
DECAY = 0.01
ADAM_RATE = 0.2
BETA1 = 0.9
BETA2 = 0.95
ADAM_FLOOR = 1e-08

HEADS = 8
HD = 48
D = HEADS * HD
COLS = 32
HALO = 4 * COLS
TILE = 256

N1G, N1S, N3G, N3S, N2G, N2S, SA, SL, SM, QB, KB, VB, PB, C1B, BG, BS, C2B, F2B = range(18)
F1B, K1R, K2R = 18, 22, 31
SMALL = 40
TABLE = 48


def halves(v):
    hi = v.astype(BF)
    return hi, (v - hi.astype(F32)).astype(BF)


def side(v):
    h, l = halves(v)
    return jnp.concatenate([h, l, h], axis=1)


def dot_nn(a, b):
    return lax.dot_general(a, b, (((1,), (0,)), ((), ())), preferred_element_type=F32)


def dot_nt(a, b):
    return lax.dot_general(a, b, (((1,), (1,)), ((), ())), preferred_element_type=F32)


def normalize(v):
    mean = jnp.mean(v, axis=1, keepdims=True)
    c = v - mean
    r = lax.rsqrt(jnp.mean(c * c, axis=1, keepdims=True) + EPS)
    return c * r, r


def normalize_back(e, xhat, r):
    return r * (
        e - jnp.mean(e, axis=1, keepdims=True) - xhat * jnp.mean(e * xhat, axis=1, keepdims=True)
    )


def gelu_parts(v):
    phi = 0.5 * (1.0 + lax.erf(v * ROOT_HALF))
    return v * phi, phi + v * jnp.exp(-0.5 * v * v) * ROOT_TWOPI


def eights(v):
    total = v[0:8]
    for i in range(8, v.shape[0], 8):
        total = total + v[i : i + 8]
    return total


def sweep(count, size, body):
    def one(i, carry):
        body(pl.multiple_of(i * size, size))
        return carry

    lax.fori_loop(0, count // size, one, 0)


def image_ends(tall_ref):
    e0 = tall_ref[0, 0]
    e1 = e0 + tall_ref[0, 1]
    return e0, e1, e1 + tall_ref[0, 2]


def slots(tall_ref, core, first_row, rows_all):
    e0, e1, e2 = image_ends(tall_ref)
    low = (jnp.where(core == 0, 0, e2), jnp.where(core == 0, e0, 0), e1)
    high = (jnp.where(core == 0, e0, rows_all), jnp.where(core == 0, e1, 0), e2)
    return [((a - first_row) * COLS, (b - first_row) * COLS) for a, b in zip(low, high)]


def span_mask(start, rows, lo, hi):
    token = start + lax.broadcasted_iota(jnp.int32, (rows, D), 0)
    return (token >= lo) & (token < hi)


def slot_masks(start, rows, spans):
    return [jnp.where(span_mask(start, rows, lo, hi), 1.0, 0.0).astype(BF) for lo, hi in spans]


def by_slot(v, masks):
    h, l = halves(v)
    parts = []
    for mask in masks:
        hm = h * mask
        parts += [hm, l * mask, hm]
    return parts


def whole_and_far(parts):
    return jnp.concatenate(parts, axis=1), jnp.concatenate([p[:, 128:] for p in parts], axis=1)


def mix_nt(parts, ref):
    every, far = whole_and_far(parts)
    corner = [ref[256:D, n * D + 128 : n * D + D] for n in range(len(parts))]
    return jnp.concatenate(
        [dot_nt(every, ref[0:256]), dot_nt(far, jnp.concatenate(corner, axis=1))], axis=1
    )


def mix_nn(parts, ref):
    every, far = whole_and_far(parts)
    corner = [ref[n * D + 128 : n * D + D, 256:D] for n in range(len(parts))]
    return jnp.concatenate(
        [dot_nn(every, ref[:, 0:256]), dot_nn(far, jnp.concatenate(corner, axis=0))], axis=1
    )


def slots_below(v, masks):
    h, l = halves(v)
    high = jnp.concatenate([h * mask for mask in masks], axis=1)
    return jnp.concatenate([high, high, jnp.concatenate([l * mask for mask in masks], axis=1)], axis=0)


def lane_head():
    return lax.broadcasted_iota(jnp.int32, (HD, D), 1) // HD


def lane_slot():
    return lax.broadcasted_iota(jnp.int32, (HD, D), 1) % HD


def fold(full):
    head = lane_head()
    total = jnp.where(head == 0, full[0:HD], 0.0)
    for h in range(1, HEADS):
        total = total + jnp.where(head == h, full[h * HD : h * HD + HD], 0.0)
    return total


def unfold(small):
    head = lane_head()
    return jnp.concatenate([jnp.where(head == h, small, 0.0) for h in range(HEADS)], axis=0)


def group_ones():
    a = lax.broadcasted_iota(jnp.int32, (D, D), 0) // HD
    b = lax.broadcasted_iota(jnp.int32, (D, D), 1) // HD
    return jnp.where(a == b, 1.0, 0.0).astype(BF)


def group_sum(v, ones):
    h = v.astype(BF)
    rest = v - h.astype(F32)
    m = rest.astype(BF)
    l = (rest - m.astype(F32)).astype(BF)
    return dot_nn(h, ones) + (dot_nn(m, ones) + dot_nn(l, ones))


def row_to_fold(row, ones):
    slot = lax.broadcasted_iota(jnp.int32, (HD, D), 0)
    return group_sum(jnp.where(lane_slot() == slot, jnp.broadcast_to(row, (HD, D)), 0.0), ones)


def fold_to_row(small):
    slot = lax.broadcasted_iota(jnp.int32, (HD, D), 0)
    return jnp.sum(jnp.where(lane_slot() == slot, small, 0.0), axis=0, keepdims=True)


def head_row(temp_ref):
    head = lax.broadcasted_iota(jnp.int32, (1, D), 1) // HD
    row = jnp.where(head == 0, temp_ref[0], 0.0)
    for h in range(1, HEADS):
        row = row + jnp.where(head == h, temp_ref[h], 0.0)
    return row


def project_kernel(tall_ref, x_ref, w_ref, tab_ref, q_ref, k_ref, v_ref, sums_ref, wcat, cross):
    step = pl.program_id(0)
    core = lax.axis_index("rows")
    rows_all = 2 * pl.num_programs(0) * TILE // COLS
    spans = slots(tall_ref, core, core * (rows_all // 2), rows_all)
    start = step * TILE

    @pl.when(step == 0)
    def _():
        def part(o):
            h, l = halves(w_ref[pl.ds(o, 64)])
            wcat[pl.ds(o, 64)] = h
            wcat[pl.ds(D + o, 64)] = h
            wcat[pl.ds(2 * D + o, 64)] = l

        sweep(D, 64, part)
        cross[...] = jnp.zeros_like(cross)
        sums_ref[...] = jnp.zeros_like(sums_ref)

    xhat, _ = normalize(x_ref[...])
    lhs = side(xhat * tab_ref[N1G : N1G + 1] + tab_ref[N1S : N1S + 1])
    qkv = dot_nn(lhs, wcat[...])
    q = qkv[:, 0:D] + tab_ref[QB : QB + 1]
    q_ref[...] = q
    k = qkv[:, D : 2 * D] + tab_ref[KB : KB + 1]
    k_ref[...] = k
    v_ref[...] = qkv[:, 2 * D : 3 * D] + tab_ref[VB : VB + 1]
    cross[...] += dot_nn(side(q.T), slots_below(k, slot_masks(start, TILE, spans)))
    for s, (lo, hi) in enumerate(spans):
        mask = span_mask(start, TILE, lo, hi)
        for n, v in enumerate((q, k)):
            row = HD + n
            sums_ref[s, row : row + 1] += jnp.sum(jnp.where(mask, v * v, 0.0), axis=0, keepdims=True)

    @pl.when(step == pl.num_programs(0) - 1)
    def _():
        for s in range(3):
            sums_ref[s, 0:HD] = fold(cross[:, s * D : s * D + D])


def project(tall, x, w, tab):
    tokens = x.shape[0]
    row = pl.BlockSpec((TILE, D), lambda i: (i, 0))
    return pl.pallas_call(
        project_kernel,
        grid=(tokens // TILE,),
        out_shape=[jax.ShapeDtypeStruct((tokens, D), F32)] * 3
        + [jax.ShapeDtypeStruct((3, HD + 8, D), F32)],
        in_specs=[
            pl.BlockSpec(memory_space=pltpu.SMEM),
            row,
            pl.BlockSpec((D, 3 * D), lambda i: (0, 0)),
            pl.BlockSpec((SMALL, D), lambda i: (0, 0)),
        ],
        out_specs=[row, row, row, pl.BlockSpec((3, HD + 8, D), lambda i: (0, 0, 0))],
        scratch_shapes=[pltpu.VMEM((3 * D, 3 * D), BF), pltpu.VMEM((D, 3 * D), F32)],
        compiler_params=pltpu.CompilerParams(vmem_limit_bytes=60 << 20),
    )(tall, x, w, tab)


ORDERS = ((0, 1, 2, 3), (1, 2, 0, 3), (2, 0, 1, 3))
EARLY, LATE = range(0, 3), range(3, 6)
PIECE = 256
GROUP = 1536
SHARD = D // 16
DMA = pltpu.SemaphoreType.DMA


class Links:
    def __init__(self):
        self.core = lax.axis_index("rows")
        chip = lax.axis_index("canvas")
        self.bits = (lax.axis_size("canvas") - 1).bit_length()
        self.mine = [lax.rem(lax.div(chip, 1 << b), 2) for b in range(self.bits)]
        self.there = [{"canvas": chip + (1 - 2 * m) * (1 << b)} for b, m in enumerate(self.mine)]
        self.twin = {"rows": 1 - self.core}

    def call(self):
        barrier = pltpu.get_barrier_semaphore()
        for other in [self.twin] + self.there:
            pl.semaphore_signal(barrier, inc=1, device_id=other, device_id_type=MESH_ID)

    def answer(self):
        pl.semaphore_wait(pltpu.get_barrier_semaphore(), self.bits + 1)

    def greet(self):
        self.call()
        self.answer()


def remote(src, dst, send, recv, other):
    return pltpu.make_async_remote_copy(
        src_ref=src,
        dst_ref=dst,
        send_sem=send,
        recv_sem=recv,
        device_id=other,
        device_id_type=MESH_ID,
    )


class Pieces:
    count = 6

    def __init__(self, links, lanes):
        self.links = links
        self.width = lanes // self.count

    def lanes(self, p):
        return slice(p * self.width, p * self.width + self.width)

    def bit(self, p, s):
        return ORDERS[p % 3][s]

    def start(self, p, s):
        at = 0
        for t in range(s):
            at = at + self.links.mine[self.bit(p, t)] * (D >> (t + 1))
        return at

    def held(self, p, s):
        return pl.ds(pl.multiple_of(self.start(p, s), 8), D >> s)


class Reduce(Pieces):
    def __init__(self, links, src, buf, work):
        super().__init__(links, src.shape[-1])
        self.src, self.buf = src, buf
        self.first, self.land, self.pair_sem, self.send_sem, self.recv_sem = work

    @classmethod
    def scratch(cls, lanes, bits):
        steps = max(bits, 4)
        return [
            pltpu.VMEM((D, lanes), F32),
            pltpu.VMEM((D - SHARD + (steps - 4) * SHARD, lanes), F32),
            DMA((2, cls.count)),
            DMA((cls.count, steps)),
            DMA((cls.count, steps)),
        ]

    def add(self, p, rows, src, src_rows):
        lanes = self.lanes(p)
        self.buf[rows, lanes] += src[src_rows, lanes]

    def pair(self, p):
        lanes = self.lanes(p)
        return remote(
            self.src.at[1 - self.links.core, :, lanes],
            self.first.at[:, lanes],
            self.pair_sem.at[0, p],
            self.pair_sem.at[1, p],
            self.links.twin,
        )

    def move(self, p, s):
        b = self.bit(p, s)
        half = D >> (s + 1)
        away = pl.multiple_of(self.start(p, s) + (1 - self.links.mine[b]) * half, 8)
        lanes = self.lanes(p)
        return remote(
            self.buf.at[pl.ds(away, half), lanes],
            self.land.at[pl.ds(D - (D >> s), half), lanes],
            self.send_sem.at[p, s],
            self.recv_sem.at[p, s],
            self.links.there[b],
        )

    def begin(self):
        for p in range(self.count):
            self.pair(p).start()

    def join(self, some):
        for p in some:
            self.pair(p).wait()
            self.add(p, pl.ds(0, D), self.first, pl.ds(0, D))
            self.move(p, 0).start()

    def launch(self):
        for p in range(self.count):
            self.move(p, 0).start()

    def down(self, s, some, last=3):
        for p in some:
            self.move(p, s).wait()
            self.add(p, self.held(p, s + 1), self.land, pl.ds(D - (D >> s), D >> (s + 1)))
            if s < last:
                self.move(p, s + 1).start()
        if s == 3:
            for b in range(4, self.links.bits):
                self.swap(b, some)

    def swap(self, b, some):
        at = pl.ds(D - SHARD + (b - 4) * SHARD, SHARD)
        copies = {}
        for p in some:
            lanes = self.lanes(p)
            copies[p] = remote(
                self.buf.at[self.held(p, 4), lanes],
                self.land.at[at, lanes],
                self.send_sem.at[p, b],
                self.recv_sem.at[p, b],
                self.links.there[b],
            )
            copies[p].start()
        for p in some:
            copies[p].wait()
            self.add(p, self.held(p, 4), self.land, at)


class Gather(Pieces):
    def __init__(self, links, whole, dst, work):
        super().__init__(links, whole.shape[1])
        self.whole, self.dst = whole, dst
        self.send_sem, self.recv_sem, self.out_sem = work

    @classmethod
    def scratch(cls, lanes):
        return [DMA((cls.count, 4)), DMA((cls.count, 4)), DMA((2, 3, cls.count))]

    def back(self, p, s):
        view = self.whole.at[self.held(p, s + 1), self.lanes(p)]
        return remote(
            view,
            view,
            self.send_sem.at[p, s],
            self.recv_sem.at[p, s],
            self.links.there[self.bit(p, s)],
        )

    def outs(self, p, n):
        mine = self.links.mine[self.bit(p, 0)]
        half = D // 2
        at = pl.multiple_of(half * (mine if n == 0 else 1 - mine), 8)
        rows = pl.ds(at, half)
        src = self.whole.at[rows, self.lanes(p)]
        dst = self.dst.at[self.links.core, rows, self.lanes(p)]
        sem = self.out_sem.at[n]
        return (
            pltpu.make_async_copy(src, dst, sem.at[0, p]),
            remote(src, dst, sem.at[1, p], sem.at[2, p], self.links.twin),
        )

    def begin(self, some):
        for p in some:
            self.back(p, 3).start()

    def up(self, s, some):
        for p in some:
            self.back(p, s).wait()
            if s > 0:
                self.back(p, s - 1).start()
            if s < 2:
                for copy in self.outs(p, 1 - s):
                    copy.start()

    def end(self):
        for n in range(2):
            for p in range(self.count):
                for copy in self.outs(p, n):
                    copy.wait()


class Turn(Pieces):
    def __init__(self, links, rest, whole, work):
        super().__init__(links, whole.shape[1])
        self.rest, self.whole = rest, whole
        self.land, self.send_sem, self.recv_sem = work

    @classmethod
    def scratch(cls, lanes, bits):
        steps = max(bits, 4) - 3
        return [
            pltpu.VMEM((steps * SHARD, lanes), F32),
            DMA((cls.count, steps)),
            DMA((cls.count, steps)),
        ]

    def move(self, p, n):
        lanes = self.lanes(p)
        if n == 0:
            b = self.bit(p, 3)
            at = pl.multiple_of((1 - self.links.mine[b]) * SHARD, 8)
            src = self.rest.at[pl.ds(at, SHARD), lanes]
        else:
            b = 3 + n
            src = self.whole.at[self.held(p, 4), lanes]
        return remote(
            src,
            self.land.at[n * SHARD : n * SHARD + SHARD, lanes],
            self.send_sem.at[p, n],
            self.recv_sem.at[p, n],
            self.links.there[b],
        )

    def begin(self):
        for p in range(self.count):
            self.move(p, 0).start()

    def end(self, some):
        for p in some:
            lanes = self.lanes(p)
            at = pl.multiple_of(self.links.mine[self.bit(p, 3)] * SHARD, 8)
            self.move(p, 0).wait()
            self.whole[self.held(p, 4), lanes] = (
                self.rest[pl.ds(at, SHARD), lanes] + self.land[0:SHARD, lanes]
            )
        for n in range(1, self.links.bits - 3):
            for p in some:
                self.move(p, n).start()
            for p in some:
                lanes = self.lanes(p)
                self.move(p, n).wait()
                self.whole[self.held(p, 4), lanes] += self.land[n * SHARD : n * SHARD + SHARD, lanes]


def row_flags(tall_ref, rows_all):
    ends = image_ends(tall_ref)

    def above(row):
        first = (row == 0) | (row == ends[0]) | (row == ends[1]) | (row == ends[2])
        return jnp.where(first, 0.0, 1.0)

    def below(row):
        return jnp.where(row + 1 == rows_all, 0.0, above(row + 1))

    return above, below


def middle_kernel(
    tall_ref,
    temp_ref,
    x_hbm,
    dy_hbm,
    v_hbm,
    sums_ref,
    wp_ref,
    w1_hbm,
    w2_ref,
    tab_ref,
    out_hbm,
    ds1_hbm,
    dmx_hbm,
    dwp_ref,
    shard_ref,
    gtab_ref,
    probs_ref,
    unit_ref,
    gprob_ref,
    joint_ref,
    wpv,
    wph,
    w1c,
    w2c,
    pcat,
    mixed,
    s1,
    li,
    act,
    slope,
    mid,
    s2,
    ds2,
    gp,
    n2c,
    dzc,
    b1_ref,
    b1g_ref,
    acc,
    cross,
    x_ref,
    dy_ref,
    v_ref,
    flags,
    nt,
    dt,
    peer_ref,
    dw_ref,
    load_sem,
    store_sem,
    edge_sem,
    *work,
):
    links = Links()
    core = links.core
    wide = x_ref.shape[0]
    tokens = wide - HALO
    dw1_ref, dw2_ref = dw_ref.at[0], dw_ref.at[1]
    reduce = Reduce(links, dw_ref, dw_ref.at[core], work)
    w1_ref = work[0]
    lo_ = x_ref
    own = pl.ds(pl.multiple_of(core * HALO, HALO), tokens)
    pairs = ((w1_hbm, w1_ref), (v_hbm, v_ref.at[own]), (x_hbm, x_ref.at[own]), (dy_hbm, dy_ref.at[own]))
    loads = [pltpu.make_async_copy(a, b, load_sem.at[i]) for i, (a, b) in enumerate(pairs)]
    for load in loads:
        load.start()
    links.call()
    edge = pl.ds(pl.multiple_of((1 - core) * (tokens - HALO), HALO), HALO)
    far = pl.ds(pl.multiple_of(core * tokens, HALO), HALO)
    pairs = (
        (sums_ref.at[2], peer_ref),
        (v_hbm.at[edge], v_ref.at[far]),
        (x_hbm.at[edge], x_ref.at[far]),
        (dy_hbm.at[edge], dy_ref.at[far]),
    )
    edges = [
        remote(a, b, edge_sem.at[0, i], edge_sem.at[1, i], links.twin)
        for i, (a, b) in enumerate(pairs)
    ]
    own_rows = tokens // COLS
    rows_wide = wide // COLS
    rows_all = 2 * own_rows
    first_row = core * (own_rows - HALO // COLS)
    own_off = pl.multiple_of(core * HALO, HALO)
    mlp = w1_hbm.shape[1]
    spans = slots(tall_ref, core, first_row, rows_all)
    above, below = row_flags(tall_ref, rows_all)

    def tab(r):
        return tab_ref[r : r + 1]

    def is_own(row):
        return (row >= core * (HALO // COLS)) & (row < core * (HALO // COLS) + own_rows)

    loads[0].wait()

    def part_1(o):
        rows = pl.ds(o, 64)
        h, l = halves(w1_ref[rows])
        w1c[rows] = h
        w1c[pl.ds(D + o, 64)] = h
        w1c[pl.ds(2 * D + o, 64)] = l

    sweep(D, 64, part_1)
    links.answer()
    for copy in edges:
        copy.start()

    def part_p(o):
        rows = pl.ds(o, 192)
        h, l = halves(wp_ref[rows])
        wpv[rows] = h
        wpv[pl.ds(D + o, 192)] = h
        wpv[pl.ds(2 * D + o, 192)] = l
        wph[rows, 0:D] = h
        wph[rows, D : 2 * D] = h
        wph[rows, 2 * D : 3 * D] = l

    sweep(D, 192, part_p)

    def part_2(o):
        rows = pl.ds(o, 256)
        h, l = halves(w2_ref[rows])
        w2c[rows, 0:D] = h
        w2c[rows, D : 2 * D] = h
        w2c[rows, 2 * D : 3 * D] = l

    sweep(mlp, 256, part_2)

    edges[0].wait()
    ones = group_ones()
    temp = head_row(temp_ref)
    joint_ref[...] = sums_ref[2] + peer_ref[...]

    def probabilities(s, carry):
        sums = jnp.where(s == 2, joint_ref[...], sums_ref[s])
        inv_q = lax.rsqrt(sums[HD : HD + 1] + EPS)
        inv_k = lax.rsqrt(sums[HD + 1 : HD + 2] + EPS)
        unit = sums[0:HD] * row_to_fold(inv_q, ones) * inv_k
        unit_ref[s] = unit
        weight = jnp.exp(temp * unit)
        probs = weight / group_sum(weight, ones)
        probs_ref[s] = probs
        h, l = halves(unfold(probs))
        lanes = pl.ds(pl.multiple_of(3 * D * s, 128), 3 * D)
        pcat[:, lanes] = jnp.concatenate([h, h, l], axis=1)
        return carry

    lax.fori_loop(0, 3, probabilities, 0)

    acc[...] = jnp.zeros_like(acc)
    gtab_ref[...] = jnp.zeros_like(gtab_ref)

    def add(r, v):
        acc[8 * r : 8 * r + 8] += v

    for copy in loads[1:] + edges[1:]:
        copy.wait()

    def own_part(o, size):
        token = o + lax.broadcasted_iota(jnp.int32, (size, D), 0)
        return jnp.where((token >= own_off) & (token < own_off + tokens), 1.0, 0.0)

    def attend(o):
        size = wide // 3
        mix = mix_nt(by_slot(v_ref[pl.ds(o, size)], slot_masks(o, size, spans)), pcat)
        mixed[pl.ds(o, size)] = mix
        z = dot_nn(side(mix), wpv[...]) + tab(PB)
        rows = pl.ds(o, size)
        branch = tab(SA) * z
        stream = x_ref[rows] + branch
        s1[rows] = stream
        xhat, _ = normalize(stream)
        li[pl.ds(pl.multiple_of(o + COLS, COLS), size)] = xhat * tab(N3G) + tab(N3S)
        add(41, eights(own_part(o, size) * branch * branch))

    sweep(wide, wide // 3, attend)

    pad = jnp.zeros((COLS, D), F32)
    for buf in (li, mid, gp, ds2):
        buf[0:COLS] = pad
        buf[wide + COLS : wide + 2 * COLS] = pad

    for r in range(rows_wide):
        row = first_row + r
        mine = jnp.where(is_own(r), 1.0, 0.0)
        for n, flag in enumerate((above(row), below(row), mine)):
            flags[n, r * COLS : r * COLS + COLS] = jnp.full((COLS, 128), flag, F32)

    block = 12 * COLS
    col = lax.rem(lax.broadcasted_iota(jnp.int32, (block + 2 * COLS, 128), 0), COLS)

    def convolve(src, base, flip, scale, visit, other=None, events=()):
        def one(n, carry):
            for when, event in events:
                pl.when(n == when)(event)
            lanes = pl.ds(pl.multiple_of(lax.rem(n, 3) * 128, 128), 128)
            m = lax.div(n, 3)
            place = lax.div((m - 1) * (m - 2), 2) + 2 * core * m * (2 - m) + (1 - core) * m * (m - 1)
            o = pl.multiple_of(place * block, block)
            rows = pl.ds(o, block)
            taps = [tab_ref[base + t : base + t + 1, lanes] for t in range(9)]
            if flip:
                taps = taps[::-1]
            if scale is not None:
                taps = [t * tab_ref[scale : scale + 1, lanes] for t in taps]
            u = src[pl.ds(o, block + 2 * COLS), lanes]
            left = jnp.where(col == 0, 0.0, pltpu.roll(u, 1, 0))
            right = jnp.where(col == COLS - 1, 0.0, pltpu.roll(u, block + 2 * COLS - 1, 0))
            up, down = flags[0, rows], flags[1, rows]

            def line(a):
                cut = slice(a * COLS, a * COLS + block)
                return left[cut] * taps[3 * a] + u[cut] * taps[3 * a + 1] + right[cut] * taps[3 * a + 2]

            visit(o, rows, lanes, line(1) + up * line(0) + down * line(2))
            if other is not None:
                near = other[pl.ds(o, block + 2 * COLS), lanes]
                mine = flags[2, rows]
                held = (
                    mine * up * near[0:block],
                    mine * near[COLS : COLS + block],
                    mine * down * near[2 * COLS : 2 * COLS + block],
                )
                inner = slice(COLS, COLS + block)
                for a in range(3):
                    for b, view in enumerate((right, u, left)):
                        t = 8 * (base + 3 * a + b)
                        acc[t : t + 8, lanes] += eights(view[inner] * held[a])
            return carry

        lax.fori_loop(0, 3 * (wide // block), one, 0)

    def first(o, rows, lanes, value):
        at = pl.ds(o + COLS, block)
        a, s = gelu_parts(value + tab_ref[C1B : C1B + 1, lanes])
        act[rows, lanes] = a
        slope[rows, lanes] = s
        mid[at, lanes] = a * tab_ref[BG : BG + 1, lanes] + tab_ref[BS : BS + 1, lanes]

    convolve(li, K1R, False, None, first)

    def second(o, rows, lanes, value):
        value = value + tab_ref[C2B : C2B + 1, lanes]
        lo_[rows, lanes] = value
        branch = tab_ref[SL : SL + 1, lanes] * value
        s2[rows, lanes] = s1[rows, lanes] + branch
        acc[8 * 42 : 8 * 42 + 8, lanes] += eights(flags[2, rows] * branch * branch)

    convolve(mid, K2R, False, None, second)

    dw1_ref[...] = jnp.zeros_like(dw1_ref)
    dw2_ref[...] = jnp.zeros_like(dw2_ref)
    b1g_ref[...] = jnp.zeros_like(b1g_ref)
    for i in range(mlp // D):
        b1_ref[0:1, i * D : i * D + D] = tab(F1B + i)

    def feed(o):
        here = pl.ds(o, TILE)
        xhat, _ = normalize(s2[here])
        n2 = xhat * tab(N2G) + tab(N2S)
        n2c[...] = side(n2)
        dz = tab(SM) * dy_ref[here]
        dzc[...] = side(dz)
        nt[...] = side(n2.T)
        dt[...] = side(dz.T)
        add(F2B, eights(dz))

        padded = pl.ds(pl.multiple_of(o + COLS, COLS), TILE)
        gp[COLS : COLS + TILE] = jnp.broadcast_to(tab(F2B), (TILE, D))
        ds2[padded] = jnp.zeros((TILE, D), F32)

        def chunk(j):
            return pl.ds(pl.multiple_of(j, PIECE), PIECE)

        def enter(j):
            return dot_nn(n2c[...], w1c[:, chunk(j)]), dot_nt(dzc[...], w2c[chunk(j)])

        def chunks(first):
            raw = dn = 0.0
            ready = enter(first)
            for j in range(0, GROUP, PIECE):
                lanes = chunk(first + j)
                pre, dh = ready
                if j + PIECE < GROUP:
                    ready = enter(first + j + PIECE)
                a, slope_j = gelu_parts(pre + b1_ref[0:1, lanes])
                dp = dh * slope_j
                ah, al = halves(a)
                ph, pl_ = halves(dp)
                w2h, w2l = w2c[lanes, 0:D], w2c[lanes, 2 * D : 3 * D]
                raw = raw + (dot_nn(ah, w2h) + (dot_nn(al, w2h) + dot_nn(ah, w2l)))
                w1h, w1l = w1c[0:D, lanes], w1c[2 * D : 3 * D, lanes]
                dn = dn + (dot_nt(ph, w1h) + (dot_nt(pl_, w1h) + dot_nt(ph, w1l)))
                b1g_ref[:, lanes] += eights(dp)
                dw1_ref[:, lanes] += dot_nn(nt[...], jnp.concatenate([ph, ph, pl_], axis=0))
                dw2_ref[:, lanes] += dot_nn(dt[...], jnp.concatenate([ah, ah, al], axis=0))
            gp[COLS : COLS + TILE] += raw
            ds2[padded] += dn

        sweep(mlp, GROUP, chunks)
        raw, dn = gp[COLS : COLS + TILE], ds2[padded]
        dy = dy_ref[here]
        xhat, r = normalize(s2[here])
        ds2[pl.ds(pl.multiple_of(o + COLS, COLS), TILE)] = dy + normalize_back(dn * tab(N2G), xhat, r)
        branch = tab(SM) * raw
        result = s2[here] + branch
        s2[here] = result
        add(40, eights(result * result))
        add(43, eights(branch * branch))
        add(SM, eights(dy * raw))
        add(N2G, eights(dn * xhat))
        add(N2S, eights(dn))

    def feed_one(i, carry):
        feed(pl.multiple_of(own_off + i * TILE, 128))
        return carry

    lax.fori_loop(0, tokens // TILE, feed_one, 0)
    reduce.begin()
    stores = [pltpu.make_async_copy(s2.at[own], out_hbm, store_sem.at[0])]
    stores[0].start()
    edge = HALO // 2
    rest = pl.multiple_of(COLS + (1 - core) * (tokens + edge), COLS)
    ds2[pl.ds(rest, edge)] = jnp.zeros((edge, D), F32)
    rows_out = pl.multiple_of(COLS + own_off + (1 - core) * (tokens - edge), COLS)
    rows_in = pl.multiple_of(COLS + edge + core * (tokens - edge), COLS)
    turned = remote(
        ds2.at[pl.ds(rows_out, edge)],
        ds2.at[pl.ds(rows_in, edge)],
        edge_sem.at[0, 4],
        edge_sem.at[1, 4],
        links.twin,
    )
    turned.start()

    def third(o, rows, lanes, value):
        grad = value * tab_ref[BG : BG + 1, lanes] * slope[rows, lanes]
        gp[pl.ds(o + COLS, block), lanes] = grad
        held = flags[2, rows] * value
        acc[8 * BG : 8 * BG + 8, lanes] += eights(held * act[rows, lanes])
        acc[8 * BS : 8 * BS + 8, lanes] += eights(held)
        acc[8 * C1B : 8 * C1B + 8, lanes] += eights(flags[2, rows] * grad)

    convolve(
        ds2,
        K2R,
        True,
        SL,
        third,
        mid,
        ((5, lambda: reduce.join(EARLY)), (6, turned.wait), (8, lambda: reduce.join(LATE))),
    )

    def fourth(o, rows, lanes, value):
        slope[rows, lanes] = value

    convolve(gp, K1R, True, None, fourth, li, ((6, lambda: reduce.down(0, EARLY, 2)),))

    dwp_ref[...] = jnp.zeros_like(dwp_ref)
    cross[...] = jnp.zeros_like(cross)

    def back(step):
        o = pl.multiple_of(own_off + step * TILE, 128)

        here_wide = pl.ds(o, TILE)
        xhat, r = normalize(s1[here_wide])
        grad = slope[here_wide]
        grad_two = ds2[pl.ds(pl.multiple_of(o + COLS, COLS), TILE)]
        result = grad_two + normalize_back(grad * tab(N3G), xhat, r)
        slope[here_wide] = result
        add(N3G, eights(grad * xhat))
        add(N3S, eights(grad))
        add(SL, eights(grad_two * lo_[here_wide]))
        add(C2B, eights(grad_two))
        add(PB, eights(result))
        dmx = dot_nt(side(tab(SA) * result), wph[...])
        act[here_wide] = dmx
        h, l = halves(result)
        dwp_ref[...] += dot_nn(side(mixed[pl.ds(o, TILE)].T), jnp.concatenate([h, h, l], axis=0))
        cross[...] += dot_nn(side(dmx.T), slots_below(v_ref[pl.ds(o, TILE)], slot_masks(o, TILE, spans)))

    def back_two(step, carry):
        back(2 * step)
        back(2 * step + 1)
        pl.when(step == 0)(lambda: reduce.down(0, LATE, 2))
        pl.when(step == 0)(lambda: reduce.down(1, EARLY, 2))
        return carry

    lax.fori_loop(0, tokens // TILE // 2, back_two, 0)
    reduce.down(1, LATE, 2)
    for src, dst in ((slope, ds1_hbm), (act, dmx_hbm)):
        stores.append(pltpu.make_async_copy(src.at[own], dst, store_sem.at[len(stores)]))
        stores[-1].start()
    for s in range(3):
        gprob_ref[s] = fold(cross[:, s * D : s * D + D])

    def total(r):
        return jnp.sum(acc[8 * r : 8 * r + 8], axis=0, keepdims=True)

    for r in (N3G, N3S, N2G, N2S, SL, SM, C1B, BG, BS, F2B, 40, 41, 42, 43):
        gtab_ref[r : r + 1] = total(r)
    for t in range(9):
        gtab_ref[K1R + t : K1R + t + 1] = total(K1R + t)
        gtab_ref[K2R + t : K2R + t + 1] = total(K2R + t) * tab(SL)
    gtab_ref[C2B : C2B + 1] = total(C2B) * tab(SL)
    gtab_ref[PB : PB + 1] = total(PB) * tab(SA)
    raw = dwp_ref[...]
    gtab_ref[SA : SA + 1] = jnp.sum(raw * wp_ref[...], axis=0, keepdims=True) + total(PB) * tab(PB)
    dwp_ref[...] = raw * tab(SA)
    for i in range(mlp // D):
        gtab_ref[F1B + i : F1B + i + 1] = jnp.sum(b1g_ref[:, i * D : i * D + D], axis=0, keepdims=True)
    reduce.down(2, EARLY, 2)
    reduce.down(2, LATE, 2)
    for p in range(reduce.count):
        lanes = reduce.lanes(p)
        shard_ref[:, lanes] = reduce.buf[reduce.held(p, 3), lanes]
    for copy in stores:
        copy.wait()


def middle(tall, temp, x, dy, v, sums, wp, w1, w2, tab):
    tokens = x.shape[0]
    wide = tokens + HALO
    mlp = w1.shape[1]
    smem = pl.BlockSpec(memory_space=pltpu.SMEM)
    vmem = pl.BlockSpec(memory_space=pltpu.VMEM)
    anywhere = pl.BlockSpec(memory_space=pl.ANY)

    def f(*shape):
        return jax.ShapeDtypeStruct(shape, F32)

    def s(*shape):
        return pltpu.VMEM(shape, F32)

    def b(*shape):
        return pltpu.VMEM(shape, BF)

    padded = s(wide + 2 * COLS, D)
    return pl.pallas_call(
        middle_kernel,
        out_shape=[
            f(tokens, D),
            f(tokens, D),
            f(tokens, D),
            f(D, D),
            f(2 * SHARD, mlp),
            f(TABLE, D),
            f(3, HD, D),
            f(3, HD, D),
            f(3, HD, D),
            f(*sums.shape[1:]),
        ],
        in_specs=[smem, smem] + [anywhere] * 3 + [vmem, vmem, anywhere, vmem, vmem],
        out_specs=[anywhere] * 3 + [vmem] * 7,
        scratch_shapes=[
            b(3 * D, D),
            b(D, 3 * D),
            b(3 * D, mlp),
            b(mlp, 3 * D),
            b(D, 9 * D),
            s(wide, D),
            s(wide, D),
            padded,
            s(wide, D),
            s(wide, D),
            padded,
            s(wide, D),
            padded,
            padded,
            b(TILE, 3 * D),
            b(TILE, 3 * D),
            s(8, mlp),
            s(8, mlp),
            s(8 * TABLE, D),
            s(D, 3 * D),
            s(wide, D),
            s(wide, D),
            s(wide, D),
            s(3, wide, 128),
            b(D, 3 * TILE),
            b(D, 3 * TILE),
            s(*sums.shape[1:]),
            s(2, D, mlp),
            DMA((4,)),
            DMA((3,)),
            DMA((2, 5)),
        ]
        + Reduce.scratch(mlp, (lax.axis_size("canvas") - 1).bit_length()),
        compiler_params=pltpu.CompilerParams(
            collective_id=0, has_side_effects=True, vmem_limit_bytes=60 << 20
        ),
    )(tall, temp, x, dy, v, sums, wp, w1, w2, tab)


def finish_kernel(
    tall_ref,
    temp_ref,
    x_ref,
    q_ref,
    k_ref,
    ds1_ref,
    dmx_ref,
    sums_ref,
    peer_ref,
    probs_ref,
    unit_ref,
    gprob_ref,
    w_ref,
    tab_ref,
    gtab_ref,
    dwp_ref,
    shard_ref,
    dx_ref,
    end_ref,
    town_ref,
    sum_hbm,
    wh,
    wl,
    pv,
    cv,
    ch,
    side_rows,
    acc,
    gpeer_ref,
    whole,
    dw_ref,
    otab_ref,
    end_first,
    tab_first,
    gsend,
    grecv,
    pair_sem,
    *work,
):
    step = pl.program_id(0)
    last = pl.num_programs(0) - 1
    links = Links()
    core = links.core
    turn = Turn(links, shard_ref, whole, work[:3])
    gather = Gather(links, whole, sum_hbm, work[3:])
    rows_all = 2 * pl.num_programs(0) * TILE // COLS
    spans = slots(tall_ref, core, core * (rows_all // 2), rows_all)
    start = step * TILE

    def tab(r):
        return tab_ref[r : r + 1]

    @pl.when(step == 0)
    def _():
        links.greet()
        swap = remote(gprob_ref.at[2], gpeer_ref, gsend, grecv, links.twin)
        swap.start()
        turn.begin()

        def part(o):
            h, l = halves(w_ref[pl.ds(o, 64)])
            wh[pl.ds(o, 64)] = h
            wl[pl.ds(o, 64)] = l

        sweep(D, 64, part)
        dw_ref[...] = jnp.zeros_like(dw_ref)
        dw_ref[1, :, D : 2 * D] = dwp_ref[...]
        acc[...] = jnp.zeros_like(acc)
        ones = group_ones()
        temp = head_row(temp_ref)
        swap.wait()

        def slot(s, heat):
            sums = jnp.where(s == 2, peer_ref[...], sums_ref[s])
            grad = gprob_ref[s] + jnp.where(s == 2, gpeer_ref[...], 0.0)
            inv_q = lax.rsqrt(sums[HD : HD + 1] + EPS)
            inv_k = lax.rsqrt(sums[HD + 1 : HD + 2] + EPS)
            probs = probs_ref[s]
            unit = unit_ref[s]
            scores = probs * (grad - group_sum(probs * grad, ones))
            part_heat = jnp.sum(scores * unit, axis=0, keepdims=True)
            heat = heat + jnp.where((s < 2) | (core == 0), part_heat, 0.0)
            pull = temp * scores
            both = pull * unit
            query = fold_to_row(group_sum(both, ones)) * inv_q * inv_q
            key = jnp.sum(both, axis=0, keepdims=True) * inv_k * inv_k
            side_rows[pl.ds(pl.multiple_of(8 * s, 8), 8)] = jnp.concatenate(
                [query, key, jnp.zeros((6, D), F32)], axis=0
            )
            across = pl.ds(pl.multiple_of(3 * D * s, 128), 3 * D)
            h, l = halves(unfold(pull * row_to_fold(inv_q, ones) * inv_k))
            cv[across] = jnp.concatenate([h, h, l], axis=0)
            ch[:, across] = jnp.concatenate([h, h, l], axis=1)
            h, l = halves(unfold(probs))
            pv[across] = jnp.concatenate([h, h, l], axis=0)
            return heat

        heat = lax.fori_loop(0, 3, slot, jnp.zeros((1, D), F32))
        otab_ref[...] = gtab_ref[...]
        otab_ref[44:45] = heat

    masks = [span_mask(start, TILE, lo, hi) for lo, hi in spans]
    factors = slot_masks(start, TILE, spans)

    def rows_of(r):
        return sum(jnp.where(mask, side_rows[8 * s + r : 8 * s + r + 1], 0.0) for s, mask in enumerate(masks))

    def at(n, *events):
        @pl.when(step == n)
        def _():
            for event, *args in events:
                event(*args)

    q, k = q_ref[...], k_ref[...]
    dq = mix_nt(by_slot(k, factors), ch) - q * rows_of(0)
    dk = mix_nn(by_slot(q, factors), cv) - k * rows_of(1)
    dv = mix_nn(by_slot(dmx_ref[...], factors), pv)
    dqkv = jnp.concatenate([dq, dk, dv], axis=1)
    at(0, (turn.end, EARLY), (gather.begin, EARLY))
    at(1, (gather.up, 3, EARLY))
    at(2, (gather.up, 2, LATE))
    at(3, (gather.up, 1, LATE))

    h, l = halves(dqkv)
    dn = dot_nt(h, wh[...]) + (dot_nt(l, wh[...]) + dot_nt(h, wl[...]))
    xhat, r = normalize(x_ref[...])
    nt = side((xhat * tab(N1G) + tab(N1S)).T)
    grads = dot_nn(nt, jnp.concatenate([h, h, l], axis=0))
    dw_ref[0] += grads[:, 0 : 2 * D]
    dw_ref[1, :, 0:D] += grads[:, 2 * D : 3 * D]
    dx_ref[...] = ds1_ref[...] + normalize_back(dn * tab(N1G), xhat, r)
    acc[0:8] += eights(dn * xhat)
    acc[8:16] += eights(dn)
    for i, v in enumerate((dq, dk, dv)):
        acc[16 + 8 * i : 24 + 8 * i] += eights(v)

    at(0, (turn.end, LATE), (gather.begin, LATE))
    at(1, (gather.up, 3, LATE), (gather.up, 2, EARLY))
    at(2, (gather.up, 1, EARLY))

    @pl.when(step == last)
    def _():
        for i, r in enumerate((N1G, N1S, QB, KB, VB)):
            otab_ref[r : r + 1] = jnp.sum(acc[8 * i : 8 * i + 8], axis=0, keepdims=True)
        trows = tab_first.shape[0]
        near = pl.ds(pl.multiple_of(core * trows, 8), trows)
        far = pl.ds(pl.multiple_of((1 - core) * trows, 8), trows)
        pairs = [(otab_ref.at[far], tab_first)]
        for p in range(end_first.shape[1] // 128):
            lanes = slice(p * 128, p * 128 + 128)
            pairs.append((dw_ref.at[1 - core, :, lanes], end_first.at[:, lanes]))
        copies = [
            remote(a, b, pair_sem.at[0, i], pair_sem.at[1, i], links.twin)
            for i, (a, b) in enumerate(pairs)
        ]
        for copy in copies:
            copy.start()
        gather.up(0, EARLY)
        gather.up(0, LATE)
        for copy in copies:
            copy.wait()
        town_ref[...] = otab_ref[near] + tab_first[...]
        end_ref[...] = dw_ref[core] + end_first[...]
        gather.end()


def finish(tall, temp, x, q, k, ds1, dmx, sums, peer, probs, unit, gprob, w, tab, gtab, dwp, shard):
    tokens = x.shape[0]
    smem = pl.BlockSpec(memory_space=pltpu.SMEM)
    anywhere = pl.BlockSpec(memory_space=pl.ANY)
    row = pl.BlockSpec((TILE, D), lambda i: (i, 0))
    bits = (lax.axis_size("canvas") - 1).bit_length()

    def whole(v):
        return pl.BlockSpec(v.shape, lambda i: (0,) * v.ndim)

    fixed = (sums, peer, probs, unit, gprob, w, tab, gtab, dwp, shard)
    return pl.pallas_call(
        finish_kernel,
        grid=(tokens // TILE,),
        out_shape=[
            jax.ShapeDtypeStruct((tokens, D), F32),
            jax.ShapeDtypeStruct((D, 2 * D), F32),
            jax.ShapeDtypeStruct((TABLE // 2, D), F32),
            jax.ShapeDtypeStruct((2, D, shard.shape[1]), F32),
        ],
        in_specs=[smem, smem] + [row] * 5 + [whole(v) for v in fixed],
        out_specs=[
            row,
            pl.BlockSpec((D, 2 * D), lambda i: (0, 0)),
            pl.BlockSpec((TABLE // 2, D), lambda i: (0, 0)),
            anywhere,
        ],
        scratch_shapes=[
            pltpu.VMEM((D, 3 * D), BF),
            pltpu.VMEM((D, 3 * D), BF),
            pltpu.VMEM((9 * D, D), BF),
            pltpu.VMEM((9 * D, D), BF),
            pltpu.VMEM((D, 9 * D), BF),
            pltpu.VMEM((24, D), F32),
            pltpu.VMEM((40, D), F32),
            pltpu.VMEM(gprob.shape[1:], F32),
            pltpu.VMEM((D, shard.shape[1]), F32),
            pltpu.VMEM((2, D, 2 * D), F32),
            pltpu.VMEM((TABLE, D), F32),
            pltpu.VMEM((D, 2 * D), F32),
            pltpu.VMEM((TABLE // 2, D), F32),
            DMA,
            DMA,
            DMA((2, 1 + 2 * D // 128)),
        ]
        + Turn.scratch(shard.shape[1], bits)
        + Gather.scratch(shard.shape[1]),
        compiler_params=pltpu.CompilerParams(
            collective_id=1, has_side_effects=True, vmem_limit_bytes=60 << 20
        ),
    )(tall, temp, x, q, k, ds1, dmx, *fixed)


NS_A, NS_B, NS_C = 3.4445, -4.7750, 2.0315


def times(a, b):
    return dot_nn(
        jnp.concatenate([a[0], a[1], a[0]], axis=1), jnp.concatenate([b[0], b[0], b[1]], axis=0)
    )


def mirrored(left, corner):
    edge = left.shape[1]
    return jnp.concatenate([left, jnp.concatenate([left[edge:].T, corner], axis=0)], axis=1)


EDGE = 2 * 128


def times_symmetric(a, b):
    lhs = jnp.concatenate([a[0], a[1], a[0]], axis=1)
    rhs = jnp.concatenate([b[0], b[0], b[1]], axis=0)
    return mirrored(dot_nn(lhs, rhs[:, :EDGE]), dot_nn(lhs[EDGE:], rhs[:, EDGE:]))


def gram_of(h, l):
    left = dot_nt(h, h[:EDGE]) + (dot_nt(l, h[:EDGE]) + dot_nt(h, l[:EDGE]))
    he, le = h[EDGE:], l[EDGE:]
    return mirrored(left, dot_nt(he, he) + (dot_nt(le, he) + dot_nt(he, le)))


def inverse_norm(v):
    total = jnp.sum(jnp.sum(v * v, axis=0, keepdims=True), axis=1, keepdims=True)
    return 1.0 / (jnp.sqrt(total) + 1e-07)


def wide_kernel(
    end_hbm,
    tab_hbm,
    mid_hbm,
    m1_hbm,
    m2_hbm,
    sum_hbm,
    otab_hbm,
    orth_hbm,
    xs,
    x,
    m1,
    m2,
    xc,
    poly,
    tbuf,
    tland,
    load_sem,
    tsend,
    trecv,
    tout,
    buf,
    own_sem,
    *work,
):
    links = Links()
    core = links.core
    reduce = Reduce(links, buf, buf, work[:5])
    gather = Gather(links, work[0], sum_hbm, work[5:])
    own = pltpu.make_async_copy(end_hbm, buf, own_sem)
    own.start()
    wide = m1.shape[1]
    blocks = wide // D
    trows = tbuf.shape[0]
    near = pl.ds(pl.multiple_of(core * trows, 8), trows)
    pairs = ((mid_hbm.at[core], x), (m1_hbm, m1), (m2_hbm, m2), (tab_hbm, tbuf))
    loads = [pltpu.make_async_copy(a, b, load_sem.at[i]) for i, (a, b) in enumerate(pairs)]
    for load in loads:
        load.start()
    links.greet()
    own.wait()
    reduce.launch()

    def table(n):
        return remote(tbuf, tland.at[n], tsend.at[n], trecv.at[n], links.there[n])

    def table_land(n):
        table(n).wait()
        tbuf[...] += tland[n]

    def down(s, some):
        reduce.down(s, some)
        if some is EARLY:
            table_land(s)
            if s < 3:
                table(s + 1).start()
        elif s == 3:
            for b in range(4, links.bits):
                table(b).start()
                table_land(b)
            for copy in touts:
                copy.start()
        if s == 3:
            for p in some:
                lanes = gather.lanes(p)
                gather.whole[gather.held(p, 4), lanes] = buf[gather.held(p, 4), lanes]
            gather.begin(some)

    touts = [
        pltpu.make_async_copy(tbuf, otab_hbm.at[near], tout.at[0]),
        remote(tbuf, otab_hbm.at[near], tout.at[1], tout.at[2], links.twin),
    ]

    for load in loads:
        load.wait()
    table(0).start()

    @pl.when(core == 0)
    def _():
        x[...] = MUON_KEEP * m1[...] + x[...]

    @pl.when(core == 1)
    def _():
        def flat(o):
            lanes = pl.ds(o, D)
            x[:, lanes] = MUON_KEEP * m2[lanes].T + x[:, lanes]

        sweep(wide, D, flat)

    inv = inverse_norm(x[...])
    chunks = [slice(o, o + 2 * PIECE) for o in range(0, wide, 2 * PIECE)]

    def keep(lanes, v):
        h, l = halves(v)
        xc[0:D, lanes] = h
        xc[D : 2 * D, lanes] = h
        xc[2 * D : 3 * D, lanes] = l

    def kept(lanes):
        return xc[0:D, lanes].astype(F32) + xc[2 * D : 3 * D, lanes].astype(F32)

    for lanes in chunks:
        keep(lanes, x[:, lanes] * inv)

    def gram():
        return gram_of(xc[0:D], xc[2 * D : 3 * D])

    schedule = {
        (0, 0): ((down, 0, LATE),),
        (0, 2): ((down, 1, EARLY),),
        (1, 0): ((down, 1, LATE),),
        (1, 1): ((down, 2, EARLY),),
        (1, 2): ((down, 2, LATE), (down, 3, EARLY)),
        (2, 0): ((down, 3, LATE),),
        (2, 1): ((gather.up, 3, EARLY),),
        (2, 2): ((gather.up, 3, LATE),),
        (3, 0): ((gather.up, 2, EARLY),),
        (3, 1): ((gather.up, 2, LATE),),
        (3, 2): ((gather.up, 1, EARLY),),
        (4, 0): ((gather.up, 1, LATE),),
    }

    def step(i, carry):
        def events(n):
            for turn in range(5):
                if (turn, n) in schedule:

                    @pl.when(i == turn)
                    def _():
                        for event, *args in schedule[turn, n]:
                            event(*args)

        g0 = gram()
        g = halves(g0)
        events(0)
        poly[...] = side(NS_B * g0 + NS_C * times_symmetric(g, g))
        events(1)

        def apply_to(o):
            lanes = pl.ds(pl.multiple_of(o, 2 * PIECE), 2 * PIECE)
            keep(lanes, NS_A * kept(lanes) + dot_nn(poly[...], xc[:, lanes]))

        sweep(wide, 2 * PIECE, apply_to)
        events(2)
        return carry

    down(0, EARLY)
    lax.fori_loop(0, 5, step, 0)
    for lanes in chunks:
        x[:, lanes] = kept(lanes)

    @pl.when(core == 0)
    def _():
        for b in range(blocks):
            xs[b] = x[:, b * D : b * D + D]

    @pl.when(core == 1)
    def _():
        def tall(o):
            xs[lax.div(o, D)] = x[:, pl.ds(o, D)].T

        sweep(wide, D, tall)

    orth = [
        pltpu.make_async_copy(xs, orth_hbm.at[core], tout.at[3]),
        remote(xs, orth_hbm.at[core], tout.at[4], tout.at[5], links.twin),
    ]
    for copy in orth:
        copy.start()
    gather.up(0, EARLY)
    gather.up(0, LATE)
    gather.end()
    for copy in touts + orth:
        copy.wait()


def wide_blocks(end, tab, mid, m1, m2):
    bits = (lax.axis_size("canvas") - 1).bit_length()
    anywhere = pl.BlockSpec(memory_space=pl.ANY)
    blocks = m1.shape[1] // D
    return pl.pallas_call(
        wide_kernel,
        out_shape=[
            jax.ShapeDtypeStruct((2,) + end.shape, F32),
            jax.ShapeDtypeStruct((TABLE, D), F32),
            jax.ShapeDtypeStruct((2, blocks, D, D), F32),
        ],
        in_specs=[anywhere] * 5,
        out_specs=[anywhere] * 3,
        scratch_shapes=[
            pltpu.VMEM((blocks, D, D), F32),
            pltpu.VMEM(m1.shape, F32),
            pltpu.VMEM(m1.shape, F32),
            pltpu.VMEM(m2.shape, F32),
            pltpu.VMEM((3 * D, m1.shape[1]), BF),
            pltpu.VMEM((D, 3 * D), BF),
            pltpu.VMEM((TABLE // 2, D), F32),
            pltpu.VMEM((bits, TABLE // 2, D), F32),
            DMA((4,)),
            DMA((bits,)),
            DMA((bits,)),
            DMA((6,)),
            pltpu.VMEM(end.shape, F32),
            DMA,
        ]
        + Reduce.scratch(end.shape[1], bits)
        + Gather.scratch(end.shape[1]),
        compiler_params=pltpu.CompilerParams(
            collective_id=2, has_side_effects=True, vmem_limit_bytes=60 << 20
        ),
    )(end, tab, mid, m1, m2)


def muon(w, orth, large):
    return w * (1.0 - MUON_RATE * DECAY) - MUON_RATE * 0.2 * math.sqrt(large) * orth


def square_kernel(
    end_hbm,
    mid_hbm,
    wide_hbm,
    mq_hbm,
    mp_hbm,
    m1_hbm,
    m2_hbm,
    w1_hbm,
    w2_hbm,
    out_hbm,
    dx_hbm,
    gq_out,
    gp_out,
    g1_out,
    g2_out,
    nq_out,
    np_out,
    n1_out,
    n2_out,
    w1_out,
    w2_out,
    c1_out,
    c2_out,
    out_out,
    dx_out,
    orth_hbm,
    end,
    mid,
    nat,
    mq,
    mp,
    m1,
    m2,
    w1,
    w2,
    c1,
    c2,
    wide,
    out,
    dx,
    xh,
    xl,
    xs,
    in_sem,
    out_sem,
):
    core = lax.axis_index("rows")
    mlp = m1.shape[1]
    blocks = mlp // D
    pairs = (
        (end_hbm, end),
        (mq_hbm, mq),
        (mp_hbm, mp),
        (mid_hbm, mid),
        (m1_hbm, m1),
        (m2_hbm, m2),
        (w1_hbm, w1),
        (w2_hbm, w2),
        (wide_hbm, wide),
        (out_hbm, out),
        (dx_hbm, dx),
    )
    loads = [pltpu.make_async_copy(a, b, in_sem.at[i]) for i, (a, b) in enumerate(pairs)]
    for load in loads:
        load.start()
    for load in loads[0:3]:
        load.wait()
    outs = (
        (end.at[0], gq_out.at[:, 0 : 2 * D]),
        (end.at[1, :, 0:D], gq_out.at[:, 2 * D : 3 * D]),
        (end.at[1, :, D : 2 * D], gp_out),
        (mq, nq_out),
        (mp, np_out),
        (mid.at[0], g1_out),
        (nat, g2_out),
        (m1, n1_out),
        (m2, n2_out),
        (out, out_out),
        (dx, dx_out),
        (w1, w1_out),
        (w2, w2_out),
        (c1, c1_out),
        (c2, c2_out),
        (xs, orth_hbm),
    )

    def store(*which):
        return [pltpu.make_async_copy(*outs[n], out_sem.at[n]) for n in which]

    def send(*which):
        for copy in store(*which):
            copy.start()

    send(0, 1, 2)

    def small(o):
        rows = pl.ds(o, 128)
        mq[rows, 0 : 2 * D] = MUON_KEEP * mq[rows, 0 : 2 * D] + end[0, rows]
        mq[rows, 2 * D : 3 * D] = MUON_KEEP * mq[rows, 2 * D : 3 * D] + end[1, rows, 0:D]
        mp[rows] = MUON_KEEP * mp[rows] + end[1, rows, D : 2 * D]

    sweep(D, 128, small)
    send(3, 4)

    def keep(b, v):
        xh[b], xl[b] = halves(v)

    @pl.when(core == 0)
    def _():
        xs[0] = mq[:, 0:D]
        xs[1] = mq[:, D : 2 * D]

    @pl.when(core == 1)
    def _():
        xs[0] = mq[:, 2 * D : 3 * D]
        xs[1] = mp[...]

    for b in range(2):
        keep(b, xs[b] * inverse_norm(xs[b]))

    def step(i, carry):
        x = [(xh[b], xl[b]) for b in range(2)]
        g = [gram_of(h, l) for h, l in x]
        pairs = [halves(v) for v in g]
        p = [NS_B * v + NS_C * times_symmetric(w, w) for v, w in zip(g, pairs)]
        pairs = [halves(v) for v in p]
        for b in range(2):
            h, l = x[b]
            keep(b, NS_A * (h.astype(F32) + l.astype(F32)) + times(pairs[b], x[b]))
        pl.when(i == 1)(moments)
        pl.when(i == 2)(weights)
        return carry

    def moments():
        for load in loads[3:6]:
            load.wait()
        send(5)

        def natural(o):
            nat[pl.ds(o, D)] = mid[1, :, pl.ds(o, D)].T

        sweep(mlp, D, natural)
        send(6)

        def large(o):
            rows = pl.ds(o, 64)
            m1[rows] = MUON_KEEP * m1[rows] + mid[0, rows]

        sweep(D, 64, large)
        send(7)

        def larger(o):
            rows = pl.ds(o, 256)
            m2[rows] = MUON_KEEP * m2[rows] + nat[rows]

        sweep(mlp, 256, larger)
        send(8)

    def weights():
        for load in loads[6:]:
            load.wait()
        send(9, 10)

        def block(o):
            at = pl.ds(o, D)
            b = lax.div(o, D)
            new = muon(w1[:, at], wide[0, b], mlp)
            w1[:, at] = new
            c1[:, at] = new.astype(BF)
            new = muon(w2[at], wide[1, b], mlp)
            w2[at] = new
            c2[at] = new.astype(BF)

        sweep(mlp, D, block)
        send(11, 12, 13, 14)

    lax.fori_loop(0, 5, step, 0)
    for b in range(2):
        xs[b] = xh[b].astype(F32) + xl[b].astype(F32)
    send(15)
    for copy in store(*range(len(outs))):
        copy.wait()


def square_blocks(end, mid, wide, mq, mp, m1, m2, w1, w2, out, dx):
    anywhere = pl.BlockSpec(memory_space=pl.ANY)

    def like(v, kind=F32):
        return jax.ShapeDtypeStruct(v.shape, kind)

    def room(v, kind=F32):
        return pltpu.VMEM(v.shape, kind)

    return pl.pallas_call(
        square_kernel,
        out_shape=[like(v) for v in (mq, mp, m1, m2, mq, mp, m1, m2, w1, w2)]
        + [like(w1, BF), like(w2, BF), like(out), like(dx), jax.ShapeDtypeStruct((2, D, D), F32)],
        in_specs=[anywhere] * 11,
        out_specs=[anywhere] * 15,
        scratch_shapes=[room(v) for v in (end, mid, m2, mq, mp, m1, m2, w1, w2)]
        + [room(w1, BF), room(w2, BF), room(wide), room(out), room(dx)]
        + [
            pltpu.VMEM((2, D, D), BF),
            pltpu.VMEM((2, D, D), BF),
            pltpu.VMEM((2, D, D), F32),
            DMA((11,)),
            DMA((16,)),
        ],
        compiler_params=pltpu.CompilerParams(vmem_limit_bytes=60 << 20),
    )(end, mid, wide, mq, mp, m1, m2, w1, w2, out, dx)


def trade_kernel(own_ref, peer_ref, send_sem, recv_sem):
    core = lax.axis_index("rows")
    twin = {"rows": 1 - core}
    barrier = pltpu.get_barrier_semaphore()
    pl.semaphore_signal(barrier, inc=1, device_id=twin, device_id_type=MESH_ID)
    pl.semaphore_wait(barrier, 1)
    copy = remote(own_ref, peer_ref, send_sem, recv_sem, twin)
    copy.start()
    copy.wait()


def trade(own):
    anywhere = pl.BlockSpec(memory_space=pl.ANY)
    return pl.pallas_call(
        trade_kernel,
        out_shape=jax.ShapeDtypeStruct(own.shape, F32),
        in_specs=[anywhere],
        out_specs=anywhere,
        scratch_shapes=[DMA, DMA],
        compiler_params=pltpu.CompilerParams(collective_id=3, has_side_effects=True),
    )(own)


def moment_step(current, one, two, gradient):
    first = BETA1 * one + (1.0 - BETA1) * gradient
    second = BETA2 * two + (1.0 - BETA2) * gradient * gradient
    fix_one = 1.0 - BETA1**STEP
    fix_two = 1.0 - BETA2**STEP
    updated = current - ADAM_RATE * (first / fix_one) / (jnp.sqrt(second / fix_two) + ADAM_FLOOR)
    return first, second, updated


def update_kernel(
    count,
    temp_ref,
    heat_one_ref,
    heat_two_ref,
    own_ref,
    peer_ref,
    wq_ref,
    wp_ref,
    tab_ref,
    one_ref,
    two_ref,
    gtab_ref,
    nq_ref,
    np_ref,
    cq_ref,
    cp_ref,
    first_ref,
    second_ref,
    small_ref,
    heat_first_ref,
    heat_second_ref,
    heat_ref,
    rms_ref,
):
    lower = lax.axis_index("rows") == 0
    own, peer = own_ref[...], peer_ref[...]
    low, high = jnp.where(lower, own, peer), jnp.where(lower, peer, own)
    for i, orth in enumerate((low[0], low[1], high[0])):
        lanes = slice(i * D, i * D + D)
        new = muon(wq_ref[:, lanes], orth, D)
        nq_ref[:, lanes] = new
        cq_ref[:, lanes] = new.astype(BF)
    new = muon(wp_ref[...], high[1], D)
    np_ref[...] = new
    cp_ref[...] = new.astype(BF)
    first, second, small = moment_step(tab_ref[...], one_ref[...], two_ref[...], gtab_ref[0:SMALL])
    first_ref[...] = first
    second_ref[...] = second
    small_ref[...] = small

    @pl.when(pl.program_id(0) == 0)
    def _():
        head = lax.broadcasted_iota(jnp.int32, (HEADS, D), 0)
        lane = lax.broadcasted_iota(jnp.int32, (HEADS, D), 1) // HD
        heat = jnp.sum(jnp.where(head == lane, gtab_ref[44:45], 0.0), axis=1, keepdims=True)
        head = lax.broadcasted_iota(jnp.int32, (HEADS, 1), 0)

        def column(ref):
            v = jnp.where(head == 0, ref[0], 0.0)
            for h in range(1, HEADS):
                v = jnp.where(head == h, ref[h], v)
            return v

        results = moment_step(column(temp_ref), column(heat_one_ref), column(heat_two_ref), heat)
        for ref, v in zip((heat_first_ref, heat_second_ref, heat_ref), results):
            for h in range(HEADS):
                ref[h] = v[h, 0]
        rms = jnp.sqrt(jnp.sum(gtab_ref[40:44], axis=1, keepdims=True) / count)
        for n in range(4):
            rms_ref[n] = rms[n, 0]


def update(count, temp, heat_one, heat_two, own, peer, wq, wp, tab, one, two, gtab):
    steps = 3
    piece = D // steps

    def rows(v):
        return pl.BlockSpec((piece, v.shape[1]), lambda i: (i, 0))

    def whole(v):
        return pl.BlockSpec(v.shape, lambda i: (0, 0))

    square = pl.BlockSpec((2, piece, D), lambda i: (0, i, 0))
    weights = (wq, wp)
    smem = pl.BlockSpec(memory_space=pltpu.SMEM)
    return pl.pallas_call(
        functools.partial(update_kernel, count),
        grid=(steps,),
        out_shape=[jax.ShapeDtypeStruct(w.shape, F32) for w in weights]
        + [jax.ShapeDtypeStruct(w.shape, BF) for w in weights]
        + [jax.ShapeDtypeStruct(tab.shape, F32)] * 3
        + [jax.ShapeDtypeStruct(temp.shape, F32)] * 3
        + [jax.ShapeDtypeStruct((4,), F32)],
        in_specs=[smem] * 3
        + [square, square]
        + [rows(w) for w in weights]
        + [whole(v) for v in (tab, one, two, gtab)],
        out_specs=[rows(w) for w in weights] * 2 + [whole(tab)] * 3 + [smem] * 4,
        compiler_params=pltpu.CompilerParams(vmem_limit_bytes=60 << 20),
    )(temp, heat_one, heat_two, own, peer, *weights, tab, one, two, gtab)


def on_device(
    x4, dy4, tall, wqkv, wp, w1, w2, mqkv, mp, m1, m2, tab, tab_one, tab_two, temp, temp_one, temp_two
):
    shape = x4.shape
    tokens = shape[1] * shape[2]
    x = x4.reshape(tokens, D)
    dy = dy4.reshape(tokens, D)
    q, k, v, sums = project(tall, x, wqkv, tab)
    out, ds1, dmx, dwp, shard, gtab, probs, unit, gprob, joint = middle(
        tall, temp, x, dy, v, sums, wp, w1, w2, tab
    )
    dx, end, gtab, mid = finish(
        tall, temp, x, q, k, ds1, dmx, sums, joint, probs, unit, gprob, wqkv, tab, gtab, dwp, shard
    )
    end, gtab, wide = wide_blocks(end, gtab, mid, m1, m2)
    *grads, new_1, new_2, copy_1, copy_2, out, dx, square = square_blocks(
        end, mid, wide, mqkv, mp, m1, m2, w1, w2, out, dx
    )
    count = tokens * D * lax.axis_size("rows") * lax.axis_size("canvas")
    new_q, new_p, copy_q, copy_p, *small = update(
        count, temp, temp_one, temp_two, square, trade(square), wqkv, wp, tab, tab_one, tab_two, gtab
    )
    new = (new_q, new_p, new_1, new_2, copy_q, copy_p, copy_1, copy_2)
    return (out.reshape(shape), dx.reshape(shape), *grads, *new, *small)


def solution(mesh):
    split = P("canvas", "rows", None, None)
    return jax.shard_map(
        on_device,
        mesh=mesh,
        in_specs=(split, split, P("canvas", None)) + (P(),) * 14,
        out_specs=(split, split) + (P(),) * 23,
        check_vma=False,
    )
```

```python
import functools
import math

import jax
import jax.numpy as jnp
from jax import lax
from jax.experimental import pallas as pl
from jax.experimental.pallas import tpu as pltpu
from jax.sharding import PartitionSpec as P

BF = jnp.bfloat16
F32 = jnp.float32
MESH_ID = pl.DeviceIdType.MESH

EPS = 1e-06
ROOT_HALF = 1.0 / math.sqrt(2.0)
ROOT_TWOPI = 1.0 / math.sqrt(2.0 * math.pi)
STEP = 10
MUON_RATE = 0.2
MUON_KEEP = 0.95
DECAY = 0.01
ADAM_RATE = 0.2
BETA1 = 0.9
BETA2 = 0.95
ADAM_FLOOR = 1e-08

HEADS = 8
HD = 48
D = HEADS * HD
COLS = 32
HALO = 4 * COLS
TILE = 256

N1G, N1S, N3G, N3S, N2G, N2S, SA, SL, SM, QB, KB, VB, PB, C1B, BG, BS, C2B, F2B = range(18)
F1B, K1R, K2R = 18, 22, 31
SMALL = 40
TABLE = 48


def halves(v):
    hi = v.astype(BF)
    return hi, (v - hi.astype(F32)).astype(BF)


def side(v):
    h, l = halves(v)
    return jnp.concatenate([h, l, h], axis=1)


def dot_nn(a, b):
    return lax.dot_general(a, b, (((1,), (0,)), ((), ())), preferred_element_type=F32)


def dot_nt(a, b):
    return lax.dot_general(a, b, (((1,), (1,)), ((), ())), preferred_element_type=F32)


def normalize(v):
    mean = jnp.mean(v, axis=1, keepdims=True)
    c = v - mean
    r = lax.rsqrt(jnp.mean(c * c, axis=1, keepdims=True) + EPS)
    return c * r, r


def normalize_back(e, xhat, r):
    return r * (
        e - jnp.mean(e, axis=1, keepdims=True) - xhat * jnp.mean(e * xhat, axis=1, keepdims=True)
    )


def gelu_parts(v):
    phi = 0.5 * (1.0 + lax.erf(v * ROOT_HALF))
    return v * phi, phi + v * jnp.exp(-0.5 * v * v) * ROOT_TWOPI


def eights(v):
    total = v[0:8]
    for i in range(8, v.shape[0], 8):
        total = total + v[i : i + 8]
    return total


def sweep(count, size, body):
    def one(i, carry):
        body(pl.multiple_of(i * size, size))
        return carry

    lax.fori_loop(0, count // size, one, 0)


def image_ends(tall_ref):
    e0 = tall_ref[0, 0]
    e1 = e0 + tall_ref[0, 1]
    return e0, e1, e1 + tall_ref[0, 2]


def slots(tall_ref, core, first_row, rows_all):
    e0, e1, e2 = image_ends(tall_ref)
    low = (jnp.where(core == 0, 0, e2), jnp.where(core == 0, e0, 0), e1)
    high = (jnp.where(core == 0, e0, rows_all), jnp.where(core == 0, e1, 0), e2)
    return [((a - first_row) * COLS, (b - first_row) * COLS) for a, b in zip(low, high)]


def span_mask(start, rows, lo, hi):
    token = start + lax.broadcasted_iota(jnp.int32, (rows, D), 0)
    return (token >= lo) & (token < hi)


def slot_masks(start, rows, spans):
    return [jnp.where(span_mask(start, rows, lo, hi), 1.0, 0.0).astype(BF) for lo, hi in spans]


def by_slot(v, masks):
    h, l = halves(v)
    parts = []
    for mask in masks:
        hm = h * mask
        parts += [hm, l * mask, hm]
    return parts


def whole_and_far(parts):
    return jnp.concatenate(parts, axis=1), jnp.concatenate([p[:, 128:] for p in parts], axis=1)


def mix_nt(parts, ref):
    every, far = whole_and_far(parts)
    corner = [ref[256:D, n * D + 128 : n * D + D] for n in range(len(parts))]
    return jnp.concatenate(
        [dot_nt(every, ref[0:256]), dot_nt(far, jnp.concatenate(corner, axis=1))], axis=1
    )


def mix_nn(parts, ref):
    every, far = whole_and_far(parts)
    corner = [ref[n * D + 128 : n * D + D, 256:D] for n in range(len(parts))]
    return jnp.concatenate(
        [dot_nn(every, ref[:, 0:256]), dot_nn(far, jnp.concatenate(corner, axis=0))], axis=1
    )


def slots_below(v, masks):
    h, l = halves(v)
    high = jnp.concatenate([h * mask for mask in masks], axis=1)
    return jnp.concatenate([high, high, jnp.concatenate([l * mask for mask in masks], axis=1)], axis=0)


def lane_head():
    return lax.broadcasted_iota(jnp.int32, (HD, D), 1) // HD


def lane_slot():
    return lax.broadcasted_iota(jnp.int32, (HD, D), 1) % HD


def fold(full):
    head = lane_head()
    total = jnp.where(head == 0, full[0:HD], 0.0)
    for h in range(1, HEADS):
        total = total + jnp.where(head == h, full[h * HD : h * HD + HD], 0.0)
    return total


def unfold(small):
    head = lane_head()
    return jnp.concatenate([jnp.where(head == h, small, 0.0) for h in range(HEADS)], axis=0)


def group_ones():
    a = lax.broadcasted_iota(jnp.int32, (D, D), 0) // HD
    b = lax.broadcasted_iota(jnp.int32, (D, D), 1) // HD
    return jnp.where(a == b, 1.0, 0.0).astype(BF)


def group_sum(v, ones):
    h = v.astype(BF)
    rest = v - h.astype(F32)
    m = rest.astype(BF)
    l = (rest - m.astype(F32)).astype(BF)
    return dot_nn(h, ones) + (dot_nn(m, ones) + dot_nn(l, ones))


def row_to_fold(row, ones):
    slot = lax.broadcasted_iota(jnp.int32, (HD, D), 0)
    return group_sum(jnp.where(lane_slot() == slot, jnp.broadcast_to(row, (HD, D)), 0.0), ones)


def fold_to_row(small):
    slot = lax.broadcasted_iota(jnp.int32, (HD, D), 0)
    return jnp.sum(jnp.where(lane_slot() == slot, small, 0.0), axis=0, keepdims=True)


def head_row(temp_ref):
    head = lax.broadcasted_iota(jnp.int32, (1, D), 1) // HD
    row = jnp.where(head == 0, temp_ref[0], 0.0)
    for h in range(1, HEADS):
        row = row + jnp.where(head == h, temp_ref[h], 0.0)
    return row


def project_kernel(tall_ref, x_ref, w_ref, tab_ref, q_ref, k_ref, v_ref, sums_ref, wcat, cross):
    step = pl.program_id(0)
    core = lax.axis_index("rows")
    rows_all = 2 * pl.num_programs(0) * TILE // COLS
    spans = slots(tall_ref, core, core * (rows_all // 2), rows_all)
    start = step * TILE

    @pl.when(step == 0)
    def _():
        def part(o):
            h, l = halves(w_ref[pl.ds(o, 64)])
            wcat[pl.ds(o, 64)] = h
            wcat[pl.ds(D + o, 64)] = h
            wcat[pl.ds(2 * D + o, 64)] = l

        sweep(D, 64, part)
        cross[...] = jnp.zeros_like(cross)
        sums_ref[...] = jnp.zeros_like(sums_ref)

    xhat, _ = normalize(x_ref[...])
    lhs = side(xhat * tab_ref[N1G : N1G + 1] + tab_ref[N1S : N1S + 1])
    qkv = dot_nn(lhs, wcat[...])
    q = qkv[:, 0:D] + tab_ref[QB : QB + 1]
    q_ref[...] = q
    k = qkv[:, D : 2 * D] + tab_ref[KB : KB + 1]
    k_ref[...] = k
    v_ref[...] = qkv[:, 2 * D : 3 * D] + tab_ref[VB : VB + 1]
    cross[...] += dot_nn(side(q.T), slots_below(k, slot_masks(start, TILE, spans)))
    for s, (lo, hi) in enumerate(spans):
        mask = span_mask(start, TILE, lo, hi)
        for n, v in enumerate((q, k)):
            row = HD + n
            sums_ref[s, row : row + 1] += jnp.sum(jnp.where(mask, v * v, 0.0), axis=0, keepdims=True)

    @pl.when(step == pl.num_programs(0) - 1)
    def _():
        for s in range(3):
            sums_ref[s, 0:HD] = fold(cross[:, s * D : s * D + D])


def project(tall, x, w, tab):
    tokens = x.shape[0]
    row = pl.BlockSpec((TILE, D), lambda i: (i, 0))
    return pl.pallas_call(
        project_kernel,
        grid=(tokens // TILE,),
        out_shape=[jax.ShapeDtypeStruct((tokens, D), F32)] * 3
        + [jax.ShapeDtypeStruct((3, HD + 8, D), F32)],
        in_specs=[
            pl.BlockSpec(memory_space=pltpu.SMEM),
            row,
            pl.BlockSpec((D, 3 * D), lambda i: (0, 0)),
            pl.BlockSpec((SMALL, D), lambda i: (0, 0)),
        ],
        out_specs=[row, row, row, pl.BlockSpec((3, HD + 8, D), lambda i: (0, 0, 0))],
        scratch_shapes=[pltpu.VMEM((3 * D, 3 * D), BF), pltpu.VMEM((D, 3 * D), F32)],
        compiler_params=pltpu.CompilerParams(vmem_limit_bytes=60 << 20),
    )(tall, x, w, tab)


ORDERS = ((0, 1, 2, 3), (1, 2, 0, 3), (2, 0, 1, 3))
EARLY, LATE = range(0, 3), range(3, 6)
PIECE = 256
GROUP = 1536
SHARD = D // 16
DMA = pltpu.SemaphoreType.DMA


class Links:
    def __init__(self):
        self.core = lax.axis_index("rows")
        chip = lax.axis_index("canvas")
        self.bits = (lax.axis_size("canvas") - 1).bit_length()
        self.mine = [lax.rem(lax.div(chip, 1 << b), 2) for b in range(self.bits)]
        self.there = [{"canvas": chip + (1 - 2 * m) * (1 << b)} for b, m in enumerate(self.mine)]
        self.twin = {"rows": 1 - self.core}

    def call(self):
        barrier = pltpu.get_barrier_semaphore()
        for other in [self.twin] + self.there:
            pl.semaphore_signal(barrier, inc=1, device_id=other, device_id_type=MESH_ID)

    def answer(self):
        pl.semaphore_wait(pltpu.get_barrier_semaphore(), self.bits + 1)

    def greet(self):
        self.call()
        self.answer()


def remote(src, dst, send, recv, other):
    return pltpu.make_async_remote_copy(
        src_ref=src,
        dst_ref=dst,
        send_sem=send,
        recv_sem=recv,
        device_id=other,
        device_id_type=MESH_ID,
    )


class Pieces:
    count = 6

    def __init__(self, links, lanes):
        self.links = links
        self.width = lanes // self.count

    def lanes(self, p):
        return slice(p * self.width, p * self.width + self.width)

    def bit(self, p, s):
        return ORDERS[p % 3][s]

    def start(self, p, s):
        at = 0
        for t in range(s):
            at = at + self.links.mine[self.bit(p, t)] * (D >> (t + 1))
        return at

    def held(self, p, s):
        return pl.ds(pl.multiple_of(self.start(p, s), 8), D >> s)


class Reduce(Pieces):
    def __init__(self, links, src, buf, work):
        super().__init__(links, src.shape[-1])
        self.src, self.buf = src, buf
        self.first, self.land, self.pair_sem, self.send_sem, self.recv_sem = work

    @classmethod
    def scratch(cls, lanes, bits):
        steps = max(bits, 4)
        return [
            pltpu.VMEM((D, lanes), F32),
            pltpu.VMEM((D - SHARD + (steps - 4) * SHARD, lanes), F32),
            DMA((2, cls.count)),
            DMA((cls.count, steps)),
            DMA((cls.count, steps)),
        ]

    def add(self, p, rows, src, src_rows):
        lanes = self.lanes(p)
        self.buf[rows, lanes] += src[src_rows, lanes]

    def pair(self, p):
        lanes = self.lanes(p)
        return remote(
            self.src.at[1 - self.links.core, :, lanes],
            self.first.at[:, lanes],
            self.pair_sem.at[0, p],
            self.pair_sem.at[1, p],
            self.links.twin,
        )

    def move(self, p, s):
        b = self.bit(p, s)
        half = D >> (s + 1)
        away = pl.multiple_of(self.start(p, s) + (1 - self.links.mine[b]) * half, 8)
        lanes = self.lanes(p)
        return remote(
            self.buf.at[pl.ds(away, half), lanes],
            self.land.at[pl.ds(D - (D >> s), half), lanes],
            self.send_sem.at[p, s],
            self.recv_sem.at[p, s],
            self.links.there[b],
        )

    def begin(self):
        for p in range(self.count):
            self.pair(p).start()

    def join(self, some):
        for p in some:
            self.pair(p).wait()
            self.add(p, pl.ds(0, D), self.first, pl.ds(0, D))
            self.move(p, 0).start()

    def launch(self):
        for p in range(self.count):
            self.move(p, 0).start()

    def down(self, s, some, last=3):
        for p in some:
            self.move(p, s).wait()
            self.add(p, self.held(p, s + 1), self.land, pl.ds(D - (D >> s), D >> (s + 1)))
            if s < last:
                self.move(p, s + 1).start()
        if s == 3:
            for b in range(4, self.links.bits):
                self.swap(b, some)

    def swap(self, b, some):
        at = pl.ds(D - SHARD + (b - 4) * SHARD, SHARD)
        copies = {}
        for p in some:
            lanes = self.lanes(p)
            copies[p] = remote(
                self.buf.at[self.held(p, 4), lanes],
                self.land.at[at, lanes],
                self.send_sem.at[p, b],
                self.recv_sem.at[p, b],
                self.links.there[b],
            )
            copies[p].start()
        for p in some:
            copies[p].wait()
            self.add(p, self.held(p, 4), self.land, at)


class Gather(Pieces):
    def __init__(self, links, whole, dst, work):
        super().__init__(links, whole.shape[1])
        self.whole, self.dst = whole, dst
        self.send_sem, self.recv_sem, self.out_sem = work

    @classmethod
    def scratch(cls, lanes):
        return [DMA((cls.count, 4)), DMA((cls.count, 4)), DMA((2, 3, cls.count))]

    def back(self, p, s):
        view = self.whole.at[self.held(p, s + 1), self.lanes(p)]
        return remote(
            view,
            view,
            self.send_sem.at[p, s],
            self.recv_sem.at[p, s],
            self.links.there[self.bit(p, s)],
        )

    def outs(self, p, n):
        mine = self.links.mine[self.bit(p, 0)]
        half = D // 2
        at = pl.multiple_of(half * (mine if n == 0 else 1 - mine), 8)
        rows = pl.ds(at, half)
        src = self.whole.at[rows, self.lanes(p)]
        dst = self.dst.at[self.links.core, rows, self.lanes(p)]
        sem = self.out_sem.at[n]
        return (
            pltpu.make_async_copy(src, dst, sem.at[0, p]),
            remote(src, dst, sem.at[1, p], sem.at[2, p], self.links.twin),
        )

    def begin(self, some):
        for p in some:
            self.back(p, 3).start()

    def up(self, s, some):
        for p in some:
            self.back(p, s).wait()
            if s > 0:
                self.back(p, s - 1).start()
            if s < 2:
                for copy in self.outs(p, 1 - s):
                    copy.start()

    def end(self):
        for n in range(2):
            for p in range(self.count):
                for copy in self.outs(p, n):
                    copy.wait()


class Turn(Pieces):
    def __init__(self, links, rest, whole, work):
        super().__init__(links, whole.shape[1])
        self.rest, self.whole = rest, whole
        self.land, self.send_sem, self.recv_sem = work

    @classmethod
    def scratch(cls, lanes, bits):
        steps = max(bits, 4) - 3
        return [
            pltpu.VMEM((steps * SHARD, lanes), F32),
            DMA((cls.count, steps)),
            DMA((cls.count, steps)),
        ]

    def move(self, p, n):
        lanes = self.lanes(p)
        if n == 0:
            b = self.bit(p, 3)
            at = pl.multiple_of((1 - self.links.mine[b]) * SHARD, 8)
            src = self.rest.at[pl.ds(at, SHARD), lanes]
        else:
            b = 3 + n
            src = self.whole.at[self.held(p, 4), lanes]
        return remote(
            src,
            self.land.at[n * SHARD : n * SHARD + SHARD, lanes],
            self.send_sem.at[p, n],
            self.recv_sem.at[p, n],
            self.links.there[b],
        )

    def begin(self):
        for p in range(self.count):
            self.move(p, 0).start()

    def end(self, some):
        for p in some:
            lanes = self.lanes(p)
            at = pl.multiple_of(self.links.mine[self.bit(p, 3)] * SHARD, 8)
            self.move(p, 0).wait()
            self.whole[self.held(p, 4), lanes] = (
                self.rest[pl.ds(at, SHARD), lanes] + self.land[0:SHARD, lanes]
            )
        for n in range(1, self.links.bits - 3):
            for p in some:
                self.move(p, n).start()
            for p in some:
                lanes = self.lanes(p)
                self.move(p, n).wait()
                self.whole[self.held(p, 4), lanes] += self.land[n * SHARD : n * SHARD + SHARD, lanes]


def row_flags(tall_ref, rows_all):
    ends = image_ends(tall_ref)

    def above(row):
        first = (row == 0) | (row == ends[0]) | (row == ends[1]) | (row == ends[2])
        return jnp.where(first, 0.0, 1.0)

    def below(row):
        return jnp.where(row + 1 == rows_all, 0.0, above(row + 1))

    return above, below


def middle_kernel(
    tall_ref,
    temp_ref,
    x_hbm,
    dy_hbm,
    v_hbm,
    sums_ref,
    wp_ref,
    w1_hbm,
    w2_ref,
    tab_ref,
    out_hbm,
    ds1_hbm,
    dmx_hbm,
    dwp_ref,
    shard_ref,
    gtab_ref,
    probs_ref,
    unit_ref,
    gprob_ref,
    joint_ref,
    wpv,
    wph,
    w1c,
    w2c,
    pcat,
    mixed,
    s1,
    li,
    act,
    slope,
    mid,
    s2,
    ds2,
    gp,
    n2c,
    dzc,
    b1_ref,
    b1g_ref,
    acc,
    cross,
    x_ref,
    dy_ref,
    v_ref,
    flags,
    nt,
    dt,
    peer_ref,
    dw_ref,
    load_sem,
    store_sem,
    edge_sem,
    *work,
):
    links = Links()
    core = links.core
    wide = x_ref.shape[0]
    tokens = wide - HALO
    dw1_ref, dw2_ref = dw_ref.at[0], dw_ref.at[1]
    reduce = Reduce(links, dw_ref, dw_ref.at[core], work)
    w1_ref = work[0]
    lo_ = x_ref
    own = pl.ds(pl.multiple_of(core * HALO, HALO), tokens)
    pairs = ((w1_hbm, w1_ref), (v_hbm, v_ref.at[own]), (x_hbm, x_ref.at[own]), (dy_hbm, dy_ref.at[own]))
    loads = [pltpu.make_async_copy(a, b, load_sem.at[i]) for i, (a, b) in enumerate(pairs)]
    for load in loads:
        load.start()
    links.call()
    edge = pl.ds(pl.multiple_of((1 - core) * (tokens - HALO), HALO), HALO)
    far = pl.ds(pl.multiple_of(core * tokens, HALO), HALO)
    pairs = (
        (sums_ref.at[2], peer_ref),
        (v_hbm.at[edge], v_ref.at[far]),
        (x_hbm.at[edge], x_ref.at[far]),
        (dy_hbm.at[edge], dy_ref.at[far]),
    )
    edges = [
        remote(a, b, edge_sem.at[0, i], edge_sem.at[1, i], links.twin)
        for i, (a, b) in enumerate(pairs)
    ]
    own_rows = tokens // COLS
    rows_wide = wide // COLS
    rows_all = 2 * own_rows
    first_row = core * (own_rows - HALO // COLS)
    own_off = pl.multiple_of(core * HALO, HALO)
    mlp = w1_hbm.shape[1]
    spans = slots(tall_ref, core, first_row, rows_all)
    above, below = row_flags(tall_ref, rows_all)

    def tab(r):
        return tab_ref[r : r + 1]

    def is_own(row):
        return (row >= core * (HALO // COLS)) & (row < core * (HALO // COLS) + own_rows)

    loads[0].wait()

    def part_1(o):
        rows = pl.ds(o, 64)
        h, l = halves(w1_ref[rows])
        w1c[rows] = h
        w1c[pl.ds(D + o, 64)] = h
        w1c[pl.ds(2 * D + o, 64)] = l

    sweep(D, 64, part_1)
    links.answer()
    for copy in edges:
        copy.start()

    def part_p(o):
        rows = pl.ds(o, 192)
        h, l = halves(wp_ref[rows])
        wpv[rows] = h
        wpv[pl.ds(D + o, 192)] = h
        wpv[pl.ds(2 * D + o, 192)] = l
        wph[rows, 0:D] = h
        wph[rows, D : 2 * D] = h
        wph[rows, 2 * D : 3 * D] = l

    sweep(D, 192, part_p)

    def part_2(o):
        rows = pl.ds(o, 256)
        h, l = halves(w2_ref[rows])
        w2c[rows, 0:D] = h
        w2c[rows, D : 2 * D] = h
        w2c[rows, 2 * D : 3 * D] = l

    sweep(mlp, 256, part_2)

    edges[0].wait()
    ones = group_ones()
    temp = head_row(temp_ref)
    for s in range(3):
        sums = sums_ref[s]
        if s == 2:
            sums = sums + peer_ref[...]
            joint_ref[...] = sums
        inv_q = lax.rsqrt(sums[HD : HD + 1] + EPS)
        inv_k = lax.rsqrt(sums[HD + 1 : HD + 2] + EPS)
        unit = sums[0:HD] * row_to_fold(inv_q, ones) * inv_k
        unit_ref[s] = unit
        weight = jnp.exp(temp * unit)
        probs = weight / group_sum(weight, ones)
        probs_ref[s] = probs
        h, l = halves(unfold(probs))
        pcat[:, 3 * s * D : 3 * s * D + 3 * D] = jnp.concatenate([h, h, l], axis=1)

    acc[...] = jnp.zeros_like(acc)
    gtab_ref[...] = jnp.zeros_like(gtab_ref)

    def add(r, v):
        acc[8 * r : 8 * r + 8] += v

    for copy in loads[1:] + edges[1:]:
        copy.wait()

    def own_part(o, size):
        token = o + lax.broadcasted_iota(jnp.int32, (size, D), 0)
        return jnp.where((token >= own_off) & (token < own_off + tokens), 1.0, 0.0)

    def attend(o):
        size = wide // 3
        mix = mix_nt(by_slot(v_ref[pl.ds(o, size)], slot_masks(o, size, spans)), pcat)
        mixed[pl.ds(o, size)] = mix
        z = dot_nn(side(mix), wpv[...]) + tab(PB)
        rows = pl.ds(o, size)
        branch = tab(SA) * z
        stream = x_ref[rows] + branch
        s1[rows] = stream
        xhat, _ = normalize(stream)
        li[pl.ds(pl.multiple_of(o + COLS, COLS), size)] = xhat * tab(N3G) + tab(N3S)
        add(41, eights(own_part(o, size) * branch * branch))

    sweep(wide, wide // 3, attend)

    pad = jnp.zeros((COLS, D), F32)
    for buf in (li, mid, gp, ds2):
        buf[0:COLS] = pad
        buf[wide + COLS : wide + 2 * COLS] = pad

    for r in range(rows_wide):
        row = first_row + r
        mine = jnp.where(is_own(r), 1.0, 0.0)
        for n, flag in enumerate((above(row), below(row), mine)):
            flags[n, r * COLS : r * COLS + COLS] = jnp.full((COLS, 128), flag, F32)

    block = 12 * COLS
    col = lax.rem(lax.broadcasted_iota(jnp.int32, (block + 2 * COLS, 128), 0), COLS)

    def convolve(src, base, flip, scale, visit, other=None, events=()):
        def one(n, carry):
            for when, event in events:
                pl.when(n == when)(event)
            lanes = pl.ds(pl.multiple_of(lax.rem(n, 3) * 128, 128), 128)
            m = lax.div(n, 3)
            place = lax.div((m - 1) * (m - 2), 2) + 2 * core * m * (2 - m) + (1 - core) * m * (m - 1)
            o = pl.multiple_of(place * block, block)
            rows = pl.ds(o, block)
            taps = [tab_ref[base + t : base + t + 1, lanes] for t in range(9)]
            if flip:
                taps = taps[::-1]
            if scale is not None:
                taps = [t * tab_ref[scale : scale + 1, lanes] for t in taps]
            u = src[pl.ds(o, block + 2 * COLS), lanes]
            left = jnp.where(col == 0, 0.0, pltpu.roll(u, 1, 0))
            right = jnp.where(col == COLS - 1, 0.0, pltpu.roll(u, block + 2 * COLS - 1, 0))
            up, down = flags[0, rows], flags[1, rows]

            def line(a):
                cut = slice(a * COLS, a * COLS + block)
                return left[cut] * taps[3 * a] + u[cut] * taps[3 * a + 1] + right[cut] * taps[3 * a + 2]

            visit(o, rows, lanes, line(1) + up * line(0) + down * line(2))
            if other is not None:
                near = other[pl.ds(o, block + 2 * COLS), lanes]
                mine = flags[2, rows]
                held = (
                    mine * up * near[0:block],
                    mine * near[COLS : COLS + block],
                    mine * down * near[2 * COLS : 2 * COLS + block],
                )
                inner = slice(COLS, COLS + block)
                for a in range(3):
                    for b, view in enumerate((right, u, left)):
                        t = 8 * (base + 3 * a + b)
                        acc[t : t + 8, lanes] += eights(view[inner] * held[a])
            return carry

        lax.fori_loop(0, 3 * (wide // block), one, 0)

    def first(o, rows, lanes, value):
        at = pl.ds(o + COLS, block)
        a, s = gelu_parts(value + tab_ref[C1B : C1B + 1, lanes])
        act[rows, lanes] = a
        slope[rows, lanes] = s
        mid[at, lanes] = a * tab_ref[BG : BG + 1, lanes] + tab_ref[BS : BS + 1, lanes]

    convolve(li, K1R, False, None, first)

    def second(o, rows, lanes, value):
        value = value + tab_ref[C2B : C2B + 1, lanes]
        lo_[rows, lanes] = value
        branch = tab_ref[SL : SL + 1, lanes] * value
        s2[rows, lanes] = s1[rows, lanes] + branch
        acc[8 * 42 : 8 * 42 + 8, lanes] += eights(flags[2, rows] * branch * branch)

    convolve(mid, K2R, False, None, second)

    dw1_ref[...] = jnp.zeros_like(dw1_ref)
    dw2_ref[...] = jnp.zeros_like(dw2_ref)
    b1g_ref[...] = jnp.zeros_like(b1g_ref)
    for i in range(mlp // D):
        b1_ref[0:1, i * D : i * D + D] = tab(F1B + i)

    def feed(o):
        here = pl.ds(o, TILE)
        xhat, _ = normalize(s2[here])
        n2 = xhat * tab(N2G) + tab(N2S)
        n2c[...] = side(n2)
        dz = tab(SM) * dy_ref[here]
        dzc[...] = side(dz)
        nt[...] = side(n2.T)
        dt[...] = side(dz.T)
        add(F2B, eights(dz))

        padded = pl.ds(pl.multiple_of(o + COLS, COLS), TILE)
        gp[COLS : COLS + TILE] = jnp.broadcast_to(tab(F2B), (TILE, D))
        ds2[padded] = jnp.zeros((TILE, D), F32)

        def chunk(j):
            return pl.ds(pl.multiple_of(j, PIECE), PIECE)

        def enter(j):
            return dot_nn(n2c[...], w1c[:, chunk(j)]), dot_nt(dzc[...], w2c[chunk(j)])

        def chunks(first):
            raw = dn = 0.0
            ready = enter(first)
            for j in range(0, GROUP, PIECE):
                lanes = chunk(first + j)
                pre, dh = ready
                if j + PIECE < GROUP:
                    ready = enter(first + j + PIECE)
                a, slope_j = gelu_parts(pre + b1_ref[0:1, lanes])
                dp = dh * slope_j
                ah, al = halves(a)
                ph, pl_ = halves(dp)
                w2h, w2l = w2c[lanes, 0:D], w2c[lanes, 2 * D : 3 * D]
                raw = raw + (dot_nn(ah, w2h) + (dot_nn(al, w2h) + dot_nn(ah, w2l)))
                w1h, w1l = w1c[0:D, lanes], w1c[2 * D : 3 * D, lanes]
                dn = dn + (dot_nt(ph, w1h) + (dot_nt(pl_, w1h) + dot_nt(ph, w1l)))
                b1g_ref[:, lanes] += eights(dp)
                dw1_ref[:, lanes] += dot_nn(nt[...], jnp.concatenate([ph, ph, pl_], axis=0))
                dw2_ref[:, lanes] += dot_nn(dt[...], jnp.concatenate([ah, ah, al], axis=0))
            gp[COLS : COLS + TILE] += raw
            ds2[padded] += dn

        sweep(mlp, GROUP, chunks)
        raw, dn = gp[COLS : COLS + TILE], ds2[padded]
        dy = dy_ref[here]
        xhat, r = normalize(s2[here])
        ds2[pl.ds(pl.multiple_of(o + COLS, COLS), TILE)] = dy + normalize_back(dn * tab(N2G), xhat, r)
        branch = tab(SM) * raw
        result = s2[here] + branch
        s2[here] = result
        add(40, eights(result * result))
        add(43, eights(branch * branch))
        add(SM, eights(dy * raw))
        add(N2G, eights(dn * xhat))
        add(N2S, eights(dn))

    def feed_one(i, carry):
        feed(pl.multiple_of(own_off + i * TILE, 128))
        return carry

    lax.fori_loop(0, tokens // TILE, feed_one, 0)
    reduce.begin()
    stores = [pltpu.make_async_copy(s2.at[own], out_hbm, store_sem.at[0])]
    stores[0].start()
    edge = HALO // 2
    rest = pl.multiple_of(COLS + (1 - core) * (tokens + edge), COLS)
    ds2[pl.ds(rest, edge)] = jnp.zeros((edge, D), F32)
    rows_out = pl.multiple_of(COLS + own_off + (1 - core) * (tokens - edge), COLS)
    rows_in = pl.multiple_of(COLS + edge + core * (tokens - edge), COLS)
    turned = remote(
        ds2.at[pl.ds(rows_out, edge)],
        ds2.at[pl.ds(rows_in, edge)],
        edge_sem.at[0, 4],
        edge_sem.at[1, 4],
        links.twin,
    )
    turned.start()

    def third(o, rows, lanes, value):
        grad = value * tab_ref[BG : BG + 1, lanes] * slope[rows, lanes]
        gp[pl.ds(o + COLS, block), lanes] = grad
        held = flags[2, rows] * value
        acc[8 * BG : 8 * BG + 8, lanes] += eights(held * act[rows, lanes])
        acc[8 * BS : 8 * BS + 8, lanes] += eights(held)
        acc[8 * C1B : 8 * C1B + 8, lanes] += eights(flags[2, rows] * grad)

    convolve(
        ds2,
        K2R,
        True,
        SL,
        third,
        mid,
        ((5, lambda: reduce.join(EARLY)), (6, turned.wait), (8, lambda: reduce.join(LATE))),
    )

    def fourth(o, rows, lanes, value):
        slope[rows, lanes] = value

    convolve(gp, K1R, True, None, fourth, li, ((6, lambda: reduce.down(0, EARLY, 2)),))

    dwp_ref[...] = jnp.zeros_like(dwp_ref)
    cross[...] = jnp.zeros_like(cross)

    def back(step):
        o = pl.multiple_of(own_off + step * TILE, 128)

        here_wide = pl.ds(o, TILE)
        xhat, r = normalize(s1[here_wide])
        grad = slope[here_wide]
        grad_two = ds2[pl.ds(pl.multiple_of(o + COLS, COLS), TILE)]
        result = grad_two + normalize_back(grad * tab(N3G), xhat, r)
        slope[here_wide] = result
        add(N3G, eights(grad * xhat))
        add(N3S, eights(grad))
        add(SL, eights(grad_two * lo_[here_wide]))
        add(C2B, eights(grad_two))
        add(PB, eights(result))
        dmx = dot_nt(side(tab(SA) * result), wph[...])
        act[here_wide] = dmx
        h, l = halves(result)
        dwp_ref[...] += dot_nn(side(mixed[pl.ds(o, TILE)].T), jnp.concatenate([h, h, l], axis=0))
        cross[...] += dot_nn(side(dmx.T), slots_below(v_ref[pl.ds(o, TILE)], slot_masks(o, TILE, spans)))

    def back_one(step, carry):
        back(step)
        pl.when(step == 0)(lambda: reduce.down(0, LATE, 2))
        pl.when(step == 1)(lambda: reduce.down(1, EARLY, 2))
        pl.when(step == 2)(lambda: reduce.down(1, LATE, 2))
        return carry

    lax.fori_loop(0, tokens // TILE, back_one, 0)
    for src, dst in ((slope, ds1_hbm), (act, dmx_hbm)):
        stores.append(pltpu.make_async_copy(src.at[own], dst, store_sem.at[len(stores)]))
        stores[-1].start()
    for s in range(3):
        gprob_ref[s] = fold(cross[:, s * D : s * D + D])

    def total(r):
        return jnp.sum(acc[8 * r : 8 * r + 8], axis=0, keepdims=True)

    for r in (N3G, N3S, N2G, N2S, SL, SM, C1B, BG, BS, F2B, 40, 41, 42, 43):
        gtab_ref[r : r + 1] = total(r)
    for t in range(9):
        gtab_ref[K1R + t : K1R + t + 1] = total(K1R + t)
        gtab_ref[K2R + t : K2R + t + 1] = total(K2R + t) * tab(SL)
    gtab_ref[C2B : C2B + 1] = total(C2B) * tab(SL)
    gtab_ref[PB : PB + 1] = total(PB) * tab(SA)
    raw = dwp_ref[...]
    gtab_ref[SA : SA + 1] = jnp.sum(raw * wp_ref[...], axis=0, keepdims=True) + total(PB) * tab(PB)
    dwp_ref[...] = raw * tab(SA)
    for i in range(mlp // D):
        gtab_ref[F1B + i : F1B + i + 1] = jnp.sum(b1g_ref[:, i * D : i * D + D], axis=0, keepdims=True)
    reduce.down(2, EARLY, 2)
    reduce.down(2, LATE, 2)
    for p in range(reduce.count):
        lanes = reduce.lanes(p)
        shard_ref[:, lanes] = reduce.buf[reduce.held(p, 3), lanes]
    for copy in stores:
        copy.wait()


def middle(tall, temp, x, dy, v, sums, wp, w1, w2, tab):
    tokens = x.shape[0]
    wide = tokens + HALO
    mlp = w1.shape[1]
    smem = pl.BlockSpec(memory_space=pltpu.SMEM)
    vmem = pl.BlockSpec(memory_space=pltpu.VMEM)
    anywhere = pl.BlockSpec(memory_space=pl.ANY)

    def f(*shape):
        return jax.ShapeDtypeStruct(shape, F32)

    def s(*shape):
        return pltpu.VMEM(shape, F32)

    def b(*shape):
        return pltpu.VMEM(shape, BF)

    padded = s(wide + 2 * COLS, D)
    return pl.pallas_call(
        middle_kernel,
        out_shape=[
            f(tokens, D),
            f(tokens, D),
            f(tokens, D),
            f(D, D),
            f(2 * SHARD, mlp),
            f(TABLE, D),
            f(3, HD, D),
            f(3, HD, D),
            f(3, HD, D),
            f(*sums.shape[1:]),
        ],
        in_specs=[smem, smem] + [anywhere] * 3 + [vmem, vmem, anywhere, vmem, vmem],
        out_specs=[anywhere] * 3 + [vmem] * 7,
        scratch_shapes=[
            b(3 * D, D),
            b(D, 3 * D),
            b(3 * D, mlp),
            b(mlp, 3 * D),
            b(D, 9 * D),
            s(wide, D),
            s(wide, D),
            padded,
            s(wide, D),
            s(wide, D),
            padded,
            s(wide, D),
            padded,
            padded,
            b(TILE, 3 * D),
            b(TILE, 3 * D),
            s(8, mlp),
            s(8, mlp),
            s(8 * TABLE, D),
            s(D, 3 * D),
            s(wide, D),
            s(wide, D),
            s(wide, D),
            s(3, wide, 128),
            b(D, 3 * TILE),
            b(D, 3 * TILE),
            s(*sums.shape[1:]),
            s(2, D, mlp),
            DMA((4,)),
            DMA((3,)),
            DMA((2, 5)),
        ]
        + Reduce.scratch(mlp, (lax.axis_size("canvas") - 1).bit_length()),
        compiler_params=pltpu.CompilerParams(
            collective_id=0, has_side_effects=True, vmem_limit_bytes=60 << 20
        ),
    )(tall, temp, x, dy, v, sums, wp, w1, w2, tab)


def finish_kernel(
    tall_ref,
    temp_ref,
    x_ref,
    q_ref,
    k_ref,
    ds1_ref,
    dmx_ref,
    sums_ref,
    peer_ref,
    probs_ref,
    unit_ref,
    gprob_ref,
    w_ref,
    tab_ref,
    gtab_ref,
    dwp_ref,
    shard_ref,
    dx_ref,
    end_ref,
    town_ref,
    sum_hbm,
    wh,
    wl,
    pv,
    cv,
    ch,
    side_rows,
    acc,
    gpeer_ref,
    whole,
    dw_ref,
    otab_ref,
    end_first,
    tab_first,
    gsend,
    grecv,
    pair_sem,
    *work,
):
    step = pl.program_id(0)
    last = pl.num_programs(0) - 1
    links = Links()
    core = links.core
    turn = Turn(links, shard_ref, whole, work[:3])
    gather = Gather(links, whole, sum_hbm, work[3:])
    rows_all = 2 * pl.num_programs(0) * TILE // COLS
    spans = slots(tall_ref, core, core * (rows_all // 2), rows_all)
    start = step * TILE

    def tab(r):
        return tab_ref[r : r + 1]

    @pl.when(step == 0)
    def _():
        links.greet()
        swap = remote(gprob_ref.at[2], gpeer_ref, gsend, grecv, links.twin)
        swap.start()
        turn.begin()

        def part(o):
            h, l = halves(w_ref[pl.ds(o, 64)])
            wh[pl.ds(o, 64)] = h
            wl[pl.ds(o, 64)] = l

        sweep(D, 64, part)
        dw_ref[...] = jnp.zeros_like(dw_ref)
        dw_ref[1, :, D : 2 * D] = dwp_ref[...]
        acc[...] = jnp.zeros_like(acc)
        ones = group_ones()
        temp = head_row(temp_ref)
        heat = jnp.zeros((1, D), F32)
        for s in range(3):
            sums = sums_ref[s]
            grad = gprob_ref[s]
            if s == 2:
                swap.wait()
                sums = peer_ref[...]
                grad = grad + gpeer_ref[...]
            inv_q = lax.rsqrt(sums[HD : HD + 1] + EPS)
            inv_k = lax.rsqrt(sums[HD + 1 : HD + 2] + EPS)
            probs = probs_ref[s]
            unit = unit_ref[s]
            scores = probs * (grad - group_sum(probs * grad, ones))
            part_heat = jnp.sum(scores * unit, axis=0, keepdims=True)
            heat = heat + (part_heat if s < 2 else jnp.where(core == 0, part_heat, 0.0))
            pull = temp * scores
            both = pull * unit
            side_rows[8 * s : 8 * s + 1] = fold_to_row(group_sum(both, ones)) * inv_q * inv_q
            side_rows[8 * s + 1 : 8 * s + 2] = jnp.sum(both, axis=0, keepdims=True) * inv_k * inv_k
            across = slice(3 * s * D, 3 * s * D + 3 * D)
            h, l = halves(unfold(pull * row_to_fold(inv_q, ones) * inv_k))
            cv[across] = jnp.concatenate([h, h, l], axis=0)
            ch[:, across] = jnp.concatenate([h, h, l], axis=1)
            h, l = halves(unfold(probs))
            pv[across] = jnp.concatenate([h, h, l], axis=0)
        otab_ref[...] = gtab_ref[...]
        otab_ref[44:45] = heat

    masks = [span_mask(start, TILE, lo, hi) for lo, hi in spans]
    factors = slot_masks(start, TILE, spans)

    def rows_of(r):
        return sum(jnp.where(mask, side_rows[8 * s + r : 8 * s + r + 1], 0.0) for s, mask in enumerate(masks))

    def at(n, *events):
        @pl.when(step == n)
        def _():
            for event, *args in events:
                event(*args)

    q, k = q_ref[...], k_ref[...]
    dq = mix_nt(by_slot(k, factors), ch) - q * rows_of(0)
    dk = mix_nn(by_slot(q, factors), cv) - k * rows_of(1)
    dv = mix_nn(by_slot(dmx_ref[...], factors), pv)
    dqkv = jnp.concatenate([dq, dk, dv], axis=1)
    at(0, (turn.end, EARLY), (gather.begin, EARLY))
    at(1, (gather.up, 3, EARLY))
    at(2, (gather.up, 2, LATE))
    at(3, (gather.up, 1, LATE))

    h, l = halves(dqkv)
    dn = dot_nt(h, wh[...]) + (dot_nt(l, wh[...]) + dot_nt(h, wl[...]))
    xhat, r = normalize(x_ref[...])
    nt = side((xhat * tab(N1G) + tab(N1S)).T)
    grads = dot_nn(nt, jnp.concatenate([h, h, l], axis=0))
    dw_ref[0] += grads[:, 0 : 2 * D]
    dw_ref[1, :, 0:D] += grads[:, 2 * D : 3 * D]
    dx_ref[...] = ds1_ref[...] + normalize_back(dn * tab(N1G), xhat, r)
    acc[0:8] += eights(dn * xhat)
    acc[8:16] += eights(dn)
    for i, v in enumerate((dq, dk, dv)):
        acc[16 + 8 * i : 24 + 8 * i] += eights(v)

    at(0, (turn.end, LATE), (gather.begin, LATE))
    at(1, (gather.up, 3, LATE), (gather.up, 2, EARLY))
    at(2, (gather.up, 1, EARLY))

    @pl.when(step == last)
    def _():
        for i, r in enumerate((N1G, N1S, QB, KB, VB)):
            otab_ref[r : r + 1] = jnp.sum(acc[8 * i : 8 * i + 8], axis=0, keepdims=True)
        trows = tab_first.shape[0]
        near = pl.ds(pl.multiple_of(core * trows, 8), trows)
        far = pl.ds(pl.multiple_of((1 - core) * trows, 8), trows)
        pairs = [(otab_ref.at[far], tab_first)]
        for p in range(end_first.shape[1] // 128):
            lanes = slice(p * 128, p * 128 + 128)
            pairs.append((dw_ref.at[1 - core, :, lanes], end_first.at[:, lanes]))
        copies = [
            remote(a, b, pair_sem.at[0, i], pair_sem.at[1, i], links.twin)
            for i, (a, b) in enumerate(pairs)
        ]
        for copy in copies:
            copy.start()
        gather.up(0, EARLY)
        gather.up(0, LATE)
        for copy in copies:
            copy.wait()
        town_ref[...] = otab_ref[near] + tab_first[...]
        end_ref[...] = dw_ref[core] + end_first[...]
        gather.end()


def finish(tall, temp, x, q, k, ds1, dmx, sums, peer, probs, unit, gprob, w, tab, gtab, dwp, shard):
    tokens = x.shape[0]
    smem = pl.BlockSpec(memory_space=pltpu.SMEM)
    anywhere = pl.BlockSpec(memory_space=pl.ANY)
    row = pl.BlockSpec((TILE, D), lambda i: (i, 0))
    bits = (lax.axis_size("canvas") - 1).bit_length()

    def whole(v):
        return pl.BlockSpec(v.shape, lambda i: (0,) * v.ndim)

    fixed = (sums, peer, probs, unit, gprob, w, tab, gtab, dwp, shard)
    return pl.pallas_call(
        finish_kernel,
        grid=(tokens // TILE,),
        out_shape=[
            jax.ShapeDtypeStruct((tokens, D), F32),
            jax.ShapeDtypeStruct((D, 2 * D), F32),
            jax.ShapeDtypeStruct((TABLE // 2, D), F32),
            jax.ShapeDtypeStruct((2, D, shard.shape[1]), F32),
        ],
        in_specs=[smem, smem] + [row] * 5 + [whole(v) for v in fixed],
        out_specs=[
            row,
            pl.BlockSpec((D, 2 * D), lambda i: (0, 0)),
            pl.BlockSpec((TABLE // 2, D), lambda i: (0, 0)),
            anywhere,
        ],
        scratch_shapes=[
            pltpu.VMEM((D, 3 * D), BF),
            pltpu.VMEM((D, 3 * D), BF),
            pltpu.VMEM((9 * D, D), BF),
            pltpu.VMEM((9 * D, D), BF),
            pltpu.VMEM((D, 9 * D), BF),
            pltpu.VMEM((24, D), F32),
            pltpu.VMEM((40, D), F32),
            pltpu.VMEM(gprob.shape[1:], F32),
            pltpu.VMEM((D, shard.shape[1]), F32),
            pltpu.VMEM((2, D, 2 * D), F32),
            pltpu.VMEM((TABLE, D), F32),
            pltpu.VMEM((D, 2 * D), F32),
            pltpu.VMEM((TABLE // 2, D), F32),
            DMA,
            DMA,
            DMA((2, 1 + 2 * D // 128)),
        ]
        + Turn.scratch(shard.shape[1], bits)
        + Gather.scratch(shard.shape[1]),
        compiler_params=pltpu.CompilerParams(
            collective_id=1, has_side_effects=True, vmem_limit_bytes=60 << 20
        ),
    )(tall, temp, x, q, k, ds1, dmx, *fixed)


NS_A, NS_B, NS_C = 3.4445, -4.7750, 2.0315


def times(a, b):
    return dot_nn(
        jnp.concatenate([a[0], a[1], a[0]], axis=1), jnp.concatenate([b[0], b[0], b[1]], axis=0)
    )


def mirrored(left, corner):
    edge = left.shape[1]
    return jnp.concatenate([left, jnp.concatenate([left[edge:].T, corner], axis=0)], axis=1)


EDGE = 2 * 128


def times_symmetric(a, b):
    lhs = jnp.concatenate([a[0], a[1], a[0]], axis=1)
    rhs = jnp.concatenate([b[0], b[0], b[1]], axis=0)
    return mirrored(dot_nn(lhs, rhs[:, :EDGE]), dot_nn(lhs[EDGE:], rhs[:, EDGE:]))


def gram_of(h, l):
    left = dot_nt(h, h[:EDGE]) + (dot_nt(l, h[:EDGE]) + dot_nt(h, l[:EDGE]))
    he, le = h[EDGE:], l[EDGE:]
    return mirrored(left, dot_nt(he, he) + (dot_nt(le, he) + dot_nt(he, le)))


def inverse_norm(v):
    total = jnp.sum(jnp.sum(v * v, axis=0, keepdims=True), axis=1, keepdims=True)
    return 1.0 / (jnp.sqrt(total) + 1e-07)


def wide_kernel(
    end_hbm,
    tab_hbm,
    mid_hbm,
    m1_hbm,
    m2_hbm,
    sum_hbm,
    otab_hbm,
    orth_hbm,
    xs,
    x,
    m1,
    m2,
    xc,
    poly,
    tbuf,
    tland,
    load_sem,
    tsend,
    trecv,
    tout,
    buf,
    own_sem,
    *work,
):
    links = Links()
    core = links.core
    reduce = Reduce(links, buf, buf, work[:5])
    gather = Gather(links, work[0], sum_hbm, work[5:])
    own = pltpu.make_async_copy(end_hbm, buf, own_sem)
    own.start()
    wide = m1.shape[1]
    blocks = wide // D
    trows = tbuf.shape[0]
    near = pl.ds(pl.multiple_of(core * trows, 8), trows)
    pairs = ((mid_hbm.at[core], x), (m1_hbm, m1), (m2_hbm, m2), (tab_hbm, tbuf))
    loads = [pltpu.make_async_copy(a, b, load_sem.at[i]) for i, (a, b) in enumerate(pairs)]
    for load in loads:
        load.start()
    links.greet()
    own.wait()
    reduce.launch()

    def table(n):
        return remote(tbuf, tland.at[n], tsend.at[n], trecv.at[n], links.there[n])

    def table_land(n):
        table(n).wait()
        tbuf[...] += tland[n]

    def down(s, some):
        reduce.down(s, some)
        if some is EARLY:
            table_land(s)
            if s < 3:
                table(s + 1).start()
        elif s == 3:
            for b in range(4, links.bits):
                table(b).start()
                table_land(b)
            for copy in touts:
                copy.start()
        if s == 3:
            for p in some:
                lanes = gather.lanes(p)
                gather.whole[gather.held(p, 4), lanes] = buf[gather.held(p, 4), lanes]
            gather.begin(some)

    touts = [
        pltpu.make_async_copy(tbuf, otab_hbm.at[near], tout.at[0]),
        remote(tbuf, otab_hbm.at[near], tout.at[1], tout.at[2], links.twin),
    ]

    for load in loads:
        load.wait()
    table(0).start()

    @pl.when(core == 0)
    def _():
        x[...] = MUON_KEEP * m1[...] + x[...]

    @pl.when(core == 1)
    def _():
        def flat(o):
            lanes = pl.ds(o, D)
            x[:, lanes] = MUON_KEEP * m2[lanes].T + x[:, lanes]

        sweep(wide, D, flat)

    inv = inverse_norm(x[...])
    chunks = [slice(o, o + 2 * PIECE) for o in range(0, wide, 2 * PIECE)]

    def keep(lanes, v):
        h, l = halves(v)
        xc[0:D, lanes] = h
        xc[D : 2 * D, lanes] = h
        xc[2 * D : 3 * D, lanes] = l

    def kept(lanes):
        return xc[0:D, lanes].astype(F32) + xc[2 * D : 3 * D, lanes].astype(F32)

    for lanes in chunks:
        keep(lanes, x[:, lanes] * inv)

    def gram():
        return gram_of(xc[0:D], xc[2 * D : 3 * D])

    schedule = {
        (0, 0): ((down, 0, LATE),),
        (0, 2): ((down, 1, EARLY),),
        (1, 0): ((down, 1, LATE),),
        (1, 1): ((down, 2, EARLY),),
        (1, 2): ((down, 2, LATE), (down, 3, EARLY)),
        (2, 0): ((down, 3, LATE),),
        (2, 1): ((gather.up, 3, EARLY),),
        (2, 2): ((gather.up, 3, LATE),),
        (3, 0): ((gather.up, 2, EARLY),),
        (3, 1): ((gather.up, 2, LATE),),
        (3, 2): ((gather.up, 1, EARLY),),
        (4, 0): ((gather.up, 1, LATE),),
    }

    def step(i, carry):
        def events(n):
            for turn in range(5):
                if (turn, n) in schedule:

                    @pl.when(i == turn)
                    def _():
                        for event, *args in schedule[turn, n]:
                            event(*args)

        g0 = gram()
        g = halves(g0)
        events(0)
        poly[...] = side(NS_B * g0 + NS_C * times_symmetric(g, g))
        events(1)

        def apply_to(o):
            lanes = pl.ds(pl.multiple_of(o, 2 * PIECE), 2 * PIECE)
            keep(lanes, NS_A * kept(lanes) + dot_nn(poly[...], xc[:, lanes]))

        sweep(wide, 2 * PIECE, apply_to)
        events(2)
        return carry

    down(0, EARLY)
    lax.fori_loop(0, 5, step, 0)
    for lanes in chunks:
        x[:, lanes] = kept(lanes)

    @pl.when(core == 0)
    def _():
        for b in range(blocks):
            xs[b] = x[:, b * D : b * D + D]

    @pl.when(core == 1)
    def _():
        def tall(o):
            xs[lax.div(o, D)] = x[:, pl.ds(o, D)].T

        sweep(wide, D, tall)

    orth = [
        pltpu.make_async_copy(xs, orth_hbm.at[core], tout.at[3]),
        remote(xs, orth_hbm.at[core], tout.at[4], tout.at[5], links.twin),
    ]
    for copy in orth:
        copy.start()
    gather.up(0, EARLY)
    gather.up(0, LATE)
    gather.end()
    for copy in touts + orth:
        copy.wait()


def wide_blocks(end, tab, mid, m1, m2):
    bits = (lax.axis_size("canvas") - 1).bit_length()
    anywhere = pl.BlockSpec(memory_space=pl.ANY)
    blocks = m1.shape[1] // D
    return pl.pallas_call(
        wide_kernel,
        out_shape=[
            jax.ShapeDtypeStruct((2,) + end.shape, F32),
            jax.ShapeDtypeStruct((TABLE, D), F32),
            jax.ShapeDtypeStruct((2, blocks, D, D), F32),
        ],
        in_specs=[anywhere] * 5,
        out_specs=[anywhere] * 3,
        scratch_shapes=[
            pltpu.VMEM((blocks, D, D), F32),
            pltpu.VMEM(m1.shape, F32),
            pltpu.VMEM(m1.shape, F32),
            pltpu.VMEM(m2.shape, F32),
            pltpu.VMEM((3 * D, m1.shape[1]), BF),
            pltpu.VMEM((D, 3 * D), BF),
            pltpu.VMEM((TABLE // 2, D), F32),
            pltpu.VMEM((bits, TABLE // 2, D), F32),
            DMA((4,)),
            DMA((bits,)),
            DMA((bits,)),
            DMA((6,)),
            pltpu.VMEM(end.shape, F32),
            DMA,
        ]
        + Reduce.scratch(end.shape[1], bits)
        + Gather.scratch(end.shape[1]),
        compiler_params=pltpu.CompilerParams(
            collective_id=2, has_side_effects=True, vmem_limit_bytes=60 << 20
        ),
    )(end, tab, mid, m1, m2)


def muon(w, orth, large):
    return w * (1.0 - MUON_RATE * DECAY) - MUON_RATE * 0.2 * math.sqrt(large) * orth


def square_kernel(
    end_hbm,
    mid_hbm,
    wide_hbm,
    mq_hbm,
    mp_hbm,
    m1_hbm,
    m2_hbm,
    w1_hbm,
    w2_hbm,
    out_hbm,
    dx_hbm,
    gq_out,
    gp_out,
    g1_out,
    g2_out,
    nq_out,
    np_out,
    n1_out,
    n2_out,
    w1_out,
    w2_out,
    c1_out,
    c2_out,
    out_out,
    dx_out,
    orth_hbm,
    end,
    mid,
    nat,
    mq,
    mp,
    m1,
    m2,
    w1,
    w2,
    c1,
    c2,
    wide,
    out,
    dx,
    xh,
    xl,
    xs,
    in_sem,
    out_sem,
):
    core = lax.axis_index("rows")
    mlp = m1.shape[1]
    blocks = mlp // D
    pairs = (
        (end_hbm, end),
        (mq_hbm, mq),
        (mp_hbm, mp),
        (mid_hbm, mid),
        (m1_hbm, m1),
        (m2_hbm, m2),
        (w1_hbm, w1),
        (w2_hbm, w2),
        (wide_hbm, wide),
        (out_hbm, out),
        (dx_hbm, dx),
    )
    loads = [pltpu.make_async_copy(a, b, in_sem.at[i]) for i, (a, b) in enumerate(pairs)]
    for load in loads:
        load.start()
    for load in loads[0:3]:
        load.wait()
    outs = (
        (end.at[0], gq_out.at[:, 0 : 2 * D]),
        (end.at[1, :, 0:D], gq_out.at[:, 2 * D : 3 * D]),
        (end.at[1, :, D : 2 * D], gp_out),
        (mq, nq_out),
        (mp, np_out),
        (mid.at[0], g1_out),
        (nat, g2_out),
        (m1, n1_out),
        (m2, n2_out),
        (out, out_out),
        (dx, dx_out),
        (w1, w1_out),
        (w2, w2_out),
        (c1, c1_out),
        (c2, c2_out),
        (xs, orth_hbm),
    )

    def store(*which):
        return [pltpu.make_async_copy(*outs[n], out_sem.at[n]) for n in which]

    def send(*which):
        for copy in store(*which):
            copy.start()

    send(0, 1, 2)

    def small(o):
        rows = pl.ds(o, 128)
        mq[rows, 0 : 2 * D] = MUON_KEEP * mq[rows, 0 : 2 * D] + end[0, rows]
        mq[rows, 2 * D : 3 * D] = MUON_KEEP * mq[rows, 2 * D : 3 * D] + end[1, rows, 0:D]
        mp[rows] = MUON_KEEP * mp[rows] + end[1, rows, D : 2 * D]

    sweep(D, 128, small)
    send(3, 4)

    def keep(b, v):
        xh[b], xl[b] = halves(v)

    @pl.when(core == 0)
    def _():
        xs[0] = mq[:, 0:D]
        xs[1] = mq[:, D : 2 * D]

    @pl.when(core == 1)
    def _():
        xs[0] = mq[:, 2 * D : 3 * D]
        xs[1] = mp[...]

    for b in range(2):
        keep(b, xs[b] * inverse_norm(xs[b]))

    def step(i, carry):
        x = [(xh[b], xl[b]) for b in range(2)]
        g = [gram_of(h, l) for h, l in x]
        pairs = [halves(v) for v in g]
        p = [NS_B * v + NS_C * times_symmetric(w, w) for v, w in zip(g, pairs)]
        pairs = [halves(v) for v in p]
        for b in range(2):
            h, l = x[b]
            keep(b, NS_A * (h.astype(F32) + l.astype(F32)) + times(pairs[b], x[b]))
        pl.when(i == 1)(moments)
        pl.when(i == 2)(weights)
        return carry

    def moments():
        for load in loads[3:6]:
            load.wait()
        send(5)

        def natural(o):
            nat[pl.ds(o, D)] = mid[1, :, pl.ds(o, D)].T

        sweep(mlp, D, natural)
        send(6)

        def large(o):
            rows = pl.ds(o, 64)
            m1[rows] = MUON_KEEP * m1[rows] + mid[0, rows]

        sweep(D, 64, large)
        send(7)

        def larger(o):
            rows = pl.ds(o, 256)
            m2[rows] = MUON_KEEP * m2[rows] + nat[rows]

        sweep(mlp, 256, larger)
        send(8)

    def weights():
        for load in loads[6:]:
            load.wait()
        send(9, 10)

        def block(o):
            at = pl.ds(o, D)
            b = lax.div(o, D)
            new = muon(w1[:, at], wide[0, b], mlp)
            w1[:, at] = new
            c1[:, at] = new.astype(BF)
            new = muon(w2[at], wide[1, b], mlp)
            w2[at] = new
            c2[at] = new.astype(BF)

        sweep(mlp, D, block)
        send(11, 12, 13, 14)

    lax.fori_loop(0, 5, step, 0)
    for b in range(2):
        xs[b] = xh[b].astype(F32) + xl[b].astype(F32)
    send(15)
    for copy in store(*range(len(outs))):
        copy.wait()


def square_blocks(end, mid, wide, mq, mp, m1, m2, w1, w2, out, dx):
    anywhere = pl.BlockSpec(memory_space=pl.ANY)

    def like(v, kind=F32):
        return jax.ShapeDtypeStruct(v.shape, kind)

    def room(v, kind=F32):
        return pltpu.VMEM(v.shape, kind)

    return pl.pallas_call(
        square_kernel,
        out_shape=[like(v) for v in (mq, mp, m1, m2, mq, mp, m1, m2, w1, w2)]
        + [like(w1, BF), like(w2, BF), like(out), like(dx), jax.ShapeDtypeStruct((2, D, D), F32)],
        in_specs=[anywhere] * 11,
        out_specs=[anywhere] * 15,
        scratch_shapes=[room(v) for v in (end, mid, m2, mq, mp, m1, m2, w1, w2)]
        + [room(w1, BF), room(w2, BF), room(wide), room(out), room(dx)]
        + [
            pltpu.VMEM((2, D, D), BF),
            pltpu.VMEM((2, D, D), BF),
            pltpu.VMEM((2, D, D), F32),
            DMA((11,)),
            DMA((16,)),
        ],
        compiler_params=pltpu.CompilerParams(vmem_limit_bytes=60 << 20),
    )(end, mid, wide, mq, mp, m1, m2, w1, w2, out, dx)


def trade_kernel(own_ref, peer_ref, send_sem, recv_sem):
    core = lax.axis_index("rows")
    twin = {"rows": 1 - core}
    barrier = pltpu.get_barrier_semaphore()
    pl.semaphore_signal(barrier, inc=1, device_id=twin, device_id_type=MESH_ID)
    pl.semaphore_wait(barrier, 1)
    copy = remote(own_ref, peer_ref, send_sem, recv_sem, twin)
    copy.start()
    copy.wait()


def trade(own):
    anywhere = pl.BlockSpec(memory_space=pl.ANY)
    return pl.pallas_call(
        trade_kernel,
        out_shape=jax.ShapeDtypeStruct(own.shape, F32),
        in_specs=[anywhere],
        out_specs=anywhere,
        scratch_shapes=[DMA, DMA],
        compiler_params=pltpu.CompilerParams(collective_id=3, has_side_effects=True),
    )(own)


def moment_step(current, one, two, gradient):
    first = BETA1 * one + (1.0 - BETA1) * gradient
    second = BETA2 * two + (1.0 - BETA2) * gradient * gradient
    fix_one = 1.0 - BETA1**STEP
    fix_two = 1.0 - BETA2**STEP
    updated = current - ADAM_RATE * (first / fix_one) / (jnp.sqrt(second / fix_two) + ADAM_FLOOR)
    return first, second, updated


def update_kernel(
    count,
    temp_ref,
    heat_one_ref,
    heat_two_ref,
    own_ref,
    peer_ref,
    wq_ref,
    wp_ref,
    tab_ref,
    one_ref,
    two_ref,
    gtab_ref,
    nq_ref,
    np_ref,
    cq_ref,
    cp_ref,
    first_ref,
    second_ref,
    small_ref,
    heat_first_ref,
    heat_second_ref,
    heat_ref,
    rms_ref,
):
    lower = lax.axis_index("rows") == 0
    own, peer = own_ref[...], peer_ref[...]
    low, high = jnp.where(lower, own, peer), jnp.where(lower, peer, own)
    for i, orth in enumerate((low[0], low[1], high[0])):
        lanes = slice(i * D, i * D + D)
        new = muon(wq_ref[:, lanes], orth, D)
        nq_ref[:, lanes] = new
        cq_ref[:, lanes] = new.astype(BF)
    new = muon(wp_ref[...], high[1], D)
    np_ref[...] = new
    cp_ref[...] = new.astype(BF)
    first, second, small = moment_step(tab_ref[...], one_ref[...], two_ref[...], gtab_ref[0:SMALL])
    first_ref[...] = first
    second_ref[...] = second
    small_ref[...] = small

    @pl.when(pl.program_id(0) == 0)
    def _():
        head = lax.broadcasted_iota(jnp.int32, (HEADS, D), 0)
        lane = lax.broadcasted_iota(jnp.int32, (HEADS, D), 1) // HD
        heat = jnp.sum(jnp.where(head == lane, gtab_ref[44:45], 0.0), axis=1, keepdims=True)
        head = lax.broadcasted_iota(jnp.int32, (HEADS, 1), 0)

        def column(ref):
            v = jnp.where(head == 0, ref[0], 0.0)
            for h in range(1, HEADS):
                v = jnp.where(head == h, ref[h], v)
            return v

        results = moment_step(column(temp_ref), column(heat_one_ref), column(heat_two_ref), heat)
        for ref, v in zip((heat_first_ref, heat_second_ref, heat_ref), results):
            for h in range(HEADS):
                ref[h] = v[h, 0]
        rms = jnp.sqrt(jnp.sum(gtab_ref[40:44], axis=1, keepdims=True) / count)
        for n in range(4):
            rms_ref[n] = rms[n, 0]


def update(count, temp, heat_one, heat_two, own, peer, wq, wp, tab, one, two, gtab):
    steps = 3
    piece = D // steps

    def rows(v):
        return pl.BlockSpec((piece, v.shape[1]), lambda i: (i, 0))

    def whole(v):
        return pl.BlockSpec(v.shape, lambda i: (0, 0))

    square = pl.BlockSpec((2, piece, D), lambda i: (0, i, 0))
    weights = (wq, wp)
    smem = pl.BlockSpec(memory_space=pltpu.SMEM)
    return pl.pallas_call(
        functools.partial(update_kernel, count),
        grid=(steps,),
        out_shape=[jax.ShapeDtypeStruct(w.shape, F32) for w in weights]
        + [jax.ShapeDtypeStruct(w.shape, BF) for w in weights]
        + [jax.ShapeDtypeStruct(tab.shape, F32)] * 3
        + [jax.ShapeDtypeStruct(temp.shape, F32)] * 3
        + [jax.ShapeDtypeStruct((4,), F32)],
        in_specs=[smem] * 3
        + [square, square]
        + [rows(w) for w in weights]
        + [whole(v) for v in (tab, one, two, gtab)],
        out_specs=[rows(w) for w in weights] * 2 + [whole(tab)] * 3 + [smem] * 4,
        compiler_params=pltpu.CompilerParams(vmem_limit_bytes=60 << 20),
    )(temp, heat_one, heat_two, own, peer, *weights, tab, one, two, gtab)


def on_device(
    x4, dy4, tall, wqkv, wp, w1, w2, mqkv, mp, m1, m2, tab, tab_one, tab_two, temp, temp_one, temp_two
):
    shape = x4.shape
    tokens = shape[1] * shape[2]
    x = x4.reshape(tokens, D)
    dy = dy4.reshape(tokens, D)
    q, k, v, sums = project(tall, x, wqkv, tab)
    out, ds1, dmx, dwp, shard, gtab, probs, unit, gprob, joint = middle(
        tall, temp, x, dy, v, sums, wp, w1, w2, tab
    )
    dx, end, gtab, mid = finish(
        tall, temp, x, q, k, ds1, dmx, sums, joint, probs, unit, gprob, wqkv, tab, gtab, dwp, shard
    )
    end, gtab, wide = wide_blocks(end, gtab, mid, m1, m2)
    *grads, new_1, new_2, copy_1, copy_2, out, dx, square = square_blocks(
        end, mid, wide, mqkv, mp, m1, m2, w1, w2, out, dx
    )
    count = tokens * D * lax.axis_size("rows") * lax.axis_size("canvas")
    new_q, new_p, copy_q, copy_p, *small = update(
        count, temp, temp_one, temp_two, square, trade(square), wqkv, wp, tab, tab_one, tab_two, gtab
    )
    new = (new_q, new_p, new_1, new_2, copy_q, copy_p, copy_1, copy_2)
    return (out.reshape(shape), dx.reshape(shape), *grads, *new, *small)


def solution(mesh):
    split = P("canvas", "rows", None, None)
    return jax.shard_map(
        on_device,
        mesh=mesh,
        in_specs=(split, split, P("canvas", None)) + (P(),) * 14,
        out_specs=(split, split) + (P(),) * 23,
        check_vma=False,
    )
```
